32 devices in a mesh: section: 4 (over y, x), dp: 8 (over z, core).
Axes of the slice: x: 2, y: 2, z: 4, core: 2. Of those that a mesh axis runs over, the one named last changes fastest.
Arguments:
- tokens: bfloat16 [8192, 512], P('dp'), may hold values from -6 to 6
- cotangent: bfloat16 [8192, 512], P('dp'), may hold values from -6 to 6
- lengths: int32 [32, 16], P('dp'), may hold values from 0 to 256, as said below
- mat_a: float32 [4, 512, 2048], P('section', 'dp'), may hold values from -3 to 3
- mat_b: float32 [2, 2048, 512], P(None, 'dp', 'section'), may hold values from -0.125 to 0.125
- norms: float32 [4, 512, 2], P('section', 'dp'), may hold values from -1 to 3
- first_a: float32 [4, 512, 2048], P('section', 'dp'), may hold values from -0.005859375 to 0.005859375
- second_a: float32 [4, 512, 2048], P('section', 'dp'), may hold values from 1.5884231e-07 to 6.3536925e-07
- first_b: float32 [2, 2048, 512], P(None, 'dp', 'section'), may hold values from -0.005859375 to 0.005859375
- second_b: float32 [2, 2048, 512], P(None, 'dp', 'section'), may hold values from 1.5884231e-07 to 6.3536925e-07
- first_n: float32 [4, 512, 2], P('section', 'dp'), may hold values from -0.015625 to 0.015625
- second_n: float32 [4, 512, 2], P('section', 'dp'), may hold values from 1.4295807e-06 to 5.718323e-06
Outputs:
- grad_norm: float32 [], replicated
- output: bfloat16 [4, 2048, 512], P('section', 'dp')
- input_grad: float32 [4, 2048, 512], P('section', 'dp')
- clip_a: float32 [4, 512, 2048], P('section', 'dp')
- moment_a: float32 [4, 512, 2048], P('section', 'dp')
- square_a: float32 [4, 512, 2048], P('section', 'dp')
- master_a: float32 [4, 512, 2048], P('section', 'dp')
- copy_a: bfloat16 [4, 512, 2048], P('section', 'dp')
- clip_b: float32 [2, 2048, 512], P(None, 'dp', 'section')
- moment_b: float32 [2, 2048, 512], P(None, 'dp', 'section')
- square_b: float32 [2, 2048, 512], P(None, 'dp', 'section')
- master_b: float32 [2, 2048, 512], P(None, 'dp', 'section')
- copy_b: bfloat16 [2, 2048, 512], P(None, 'dp', 'section')
- clip_n: float32 [4, 512, 2], P('section', 'dp')
- moment_n: float32 [4, 512, 2], P('section', 'dp')
- square_n: float32 [4, 512, 2], P('section', 'dp')
- master_n: float32 [4, 512, 2], P('section', 'dp')
- copy_n: bfloat16 [4, 512, 2], P('section', 'dp')
The draws below stay inside these ranges and needn't reach their ends.
Inputs may be any that keep to these rules, and one draw needn't show every extreme that they name: Each row packs sequences from the start of a micro-batch of 256 positions, the rest padding: either one sequence of 256 followed by zeros, or 16 lengths of 4 to 16. Some row is of the first kind in every draw.
All inputs are finite; a program needn't handle non-finite values.
Results may differ from the reference program's by a relative error of at most 0.022.
Values may be sent and summed in bfloat16 or wider, within the bound.
A program may use at most 256 MiB of HBM per device.

```python
import math
import jax
import jax.numpy as jnp
from jax import lax

D = 512
FF = 2048
HEADS = 8
DHEAD = 64
MB_TOK = 256
MICRO = 4
SEQ_MB = 16
STEP = 5
TOKENS = 8192
PARAMS = 6295552
N_DP = 8


def draw_lengths(key, part):
    key = jax.random.fold_in(key, 11)
    key_short, key_coin, key_forced = jax.random.split(key, 3)
    rows_all = TOKENS // MB_TOK
    short_rows = jax.random.randint(key_short, (rows_all, SEQ_MB), MB_TOK // 64, MB_TOK // 16 + 1)
    coin_flip = jax.random.randint(key_coin, (rows_all,), 0, 8)
    forced_row = jax.random.randint(key_forced, (), 0, rows_all)
    is_long = (coin_flip == 0) | (jnp.arange(rows_all) == forced_row)
    slot_index = jnp.arange(SEQ_MB)
    long_row = jnp.where(slot_index == 0, MB_TOK, 0)
    return jnp.where(is_long[:, None], long_row[None, :], short_rows).astype(jnp.int32)


def draw_mat_a(key, part):
    key = jax.random.fold_in(key, 21)
    base_draw = jax.random.truncated_normal(key, -6.0, 6.0, (4, D, FF), jnp.float32) * D ** (-0.5)
    columns = jnp.arange(FF)
    sections = jnp.arange(4)
    widen = (sections % 2 == 0)[:, None, None] & (columns >= 3 * D)[None, None, :]
    return base_draw * jnp.where(widen, 4.0, 1.0)


def draw_norms(key, part):
    key = jax.random.fold_in(key, 31)
    key_gain, key_bias = jax.random.split(key)
    features = jnp.arange(D).astype(jnp.float32) / D
    rising = 0.6 * jnp.exp(jnp.log(3.0) * features)
    gains = rising[None, :] * jax.random.uniform(key_gain, (4, D), jnp.float32, 0.85, 1.15)
    biases = jax.random.truncated_normal(key_bias, -3.0, 3.0, (4, D), jnp.float32) * 0.3
    return jnp.stack([gains, biases], axis=2)


def steps_of(rng, extent, cuts, low, high):
    gain = 1.0
    for axis_at, blocks in cuts:
        heights = jax.random.uniform(jax.random.fold_in(jax.random.fold_in(rng, 6), axis_at), (blocks,), jnp.float32, low / len(cuts), high / len(cuts))
        gain = gain * jnp.repeat(jnp.exp(heights), extent[axis_at] // blocks).reshape((-1,) + (1,) * (len(extent) - 1 - axis_at))
    return gain


def normal_values(own_key, dims, scale, limit, shards=(), kind=jnp.bfloat16):
    drawn = scale * jax.random.normal(own_key, dims, jnp.float32)
    if shards:
        drawn = drawn * steps_of(own_key, dims, shards, -0.22, 0.18)
    return jnp.clip(drawn, -limit, limit).astype(kind)


def setup_inputs(seed: int = 0) -> dict:
    splits = jax.random.split(jax.random.key(seed), 13)
    return {
        "tokens": normal_values(splits[0], (TOKENS, D), 1.0, 6.0, ((0, 8),)),
        "cotangent": normal_values(splits[1], (TOKENS, D), 1.0, 6.0, ((0, 8),)),
        "lengths": draw_lengths(jax.random.fold_in(splits[12], 71), 0),
        "mat_a": draw_mat_a(jax.random.fold_in(splits[12], 71), 0),
        "mat_b": normal_values(splits[4], (2, FF, D), FF ** -0.5, 0.125, ((1, 8), (2, 4)), jnp.float32),
        "norms": draw_norms(jax.random.fold_in(splits[12], 71), 0),
        "first_a": normal_values(splits[6], (4, D, FF), (PARAMS ** -0.5), 0.005859375, ((0, 4), (1, 8)), jnp.float32),
        "second_a": jnp.clip(jnp.exp(math.log(6.353692469929229e-07) - 1.3862944 * jax.random.uniform(splits[7], (4, D, FF), jnp.float32) ** steps_of(splits[7], (4, D, FF), ((0, 4), (1, 8)), -0.2, 0.2)), 1.5884231174823071e-07, 6.353692469929229e-07),
        "first_b": normal_values(splits[8], (2, FF, D), (PARAMS ** -0.5), 0.005859375, ((1, 8), (2, 4)), jnp.float32),
        "second_b": jnp.clip(jnp.exp(math.log(6.353692469929229e-07) - 1.3862944 * jax.random.uniform(splits[9], (2, FF, D), jnp.float32) ** steps_of(splits[9], (2, FF, D), ((1, 8), (2, 4)), -0.2, 0.2)), 1.5884231174823071e-07, 6.353692469929229e-07),
        "first_n": normal_values(splits[10], (4, D, 2), (3 * PARAMS ** -0.5), 0.015625, ((0, 4), (1, 8)), jnp.float32),
        "second_n": jnp.clip(jnp.exp(math.log(5.7183228818757925e-06) - 1.3862944 * jax.random.uniform(splits[11], (4, D, 2), jnp.float32) ** steps_of(splits[11], (4, D, 2), ((0, 4), (1, 8)), -0.2, 0.2)), 1.4295807204689481e-06, 5.7183228818757925e-06),
    }


@jax.custom_vjp
def low(v):
    return lax.optimization_barrier(v.astype(jnp.bfloat16)).astype(jnp.float32)

@jax.custom_vjp
def low_back(v):
    return v

def low_keep(v):
    return (low(v), None)

def low_pass(kept, grad):
    return (grad,)

def back_keep(v):
    return (v, None)

def back_low(kept, grad):
    return (low(grad),)
low.defvjp(low_keep, low_pass)
low_back.defvjp(back_keep, back_low)
EPSILON = 1e-05
NEGATIVE = -1e+30
CLIP_NORM = 1.0
BETA_ONE = 0.5
BETA_TWO = 0.5
ADAM_EPSILON = 1e-08
MATRIX_RATE = 0.05
NORM_RATE = 0.5
MATRIX_DECAY = 0.01
HIGHEST_PRECISION = lax.Precision.HIGHEST

def send_value(value):
    return low(low_back(value))

def product(left, right):
    return jnp.dot(left, right, precision=HIGHEST_PRECISION)

def normalized(value):
    centre = value - lax.optimization_barrier(jnp.mean(value, -1, keepdims=True))
    return centre * lax.rsqrt(lax.optimization_barrier(jnp.mean(centre * centre, -1, keepdims=True)) + EPSILON)

def attention(inputs, weight, segment):
    length = inputs.shape[0]
    width = inputs.shape[1]
    packed = send_value(product(inputs, weight[:, :3 * width]))
    queries = packed[:, :width].reshape(length, HEADS, DHEAD)
    key_heads = packed[:, width:2 * width].reshape(length, HEADS, DHEAD)
    value_heads = packed[:, 2 * width:].reshape(length, HEADS, DHEAD)
    block_rows = min(512, length)
    score_scale = DHEAD ** (-0.5)

    def one_block(block_id):
        row_start = block_id * block_rows
        query_block = lax.dynamic_slice_in_dim(queries, row_start, block_rows, 0)
        query_segment = lax.dynamic_slice_in_dim(segment, row_start, block_rows, 0)
        scores = jnp.einsum('qhd,khd->hqk', query_block, key_heads, precision=HIGHEST_PRECISION) * score_scale
        scores = low_back(scores)
        scores = jnp.where((query_segment[:, None] == segment[None, :])[None], scores, NEGATIVE)
        prob_low = low(jax.nn.softmax(scores, axis=-1))
        mixed = jnp.einsum('hqk,khd->qhd', prob_low, value_heads, precision=HIGHEST_PRECISION)
        return mixed.reshape(block_rows, width)
    mixed = lax.map(jax.checkpoint(one_block), jnp.arange(length // block_rows, dtype=jnp.int32))
    mixed = send_value(mixed.reshape(length, width))
    return low_back(product(mixed, weight[:, 3 * width:]))

def feed_forward(inputs, weight, down_mat):
    pre_act = low_back(product(inputs, weight))
    active = low(jax.nn.gelu(pre_act, approximate=True))
    return low_back(product(active, down_mat))

def micro_forward(weights_a, weights_b, weights_n, inputs, segment):
    first_mats = low(weights_a)
    down_mats = low(weights_b)
    scales = low(weights_n)
    stream = inputs
    dual_sum = jnp.zeros_like(inputs)
    for section_id in range(4):
        if section_id % 2 == 0:
            branch = attention(stream, first_mats[section_id], segment)
        else:
            branch = feed_forward(stream, first_mats[section_id], down_mats[section_id // 2])
        summed = stream + branch
        normal_out = normalized(summed) * scales[section_id, :, 0] + scales[section_id, :, 1]
        dual_sum = dual_sum + branch
        if section_id < 3:
            stream = send_value(normal_out)
            dual_sum = send_value(dual_sum)
        else:
            stream = normal_out
    return stream + normalized(dual_sum)

def adam_update(weight, moment_one, moment_two, gradient, step_rate, decay_rate):
    first_new = BETA_ONE * moment_one + (1.0 - BETA_ONE) * gradient
    second_new = BETA_TWO * moment_two + (1.0 - BETA_TWO) * gradient * gradient
    first_hat = first_new / (1.0 - BETA_ONE ** STEP)
    second_hat = second_new / (1.0 - BETA_TWO ** STEP)
    weight_new = weight - step_rate * (first_hat / (jnp.sqrt(second_hat) + ADAM_EPSILON) + decay_rate * weight)
    return (first_new, second_new, weight_new)

def segments_of(lengths, length):
    seq_ends = jnp.cumsum(lengths, axis=1, dtype=jnp.int32)
    places = jnp.arange(length, dtype=jnp.int32)
    segment = lax.optimization_barrier(jnp.sum((seq_ends[:, None, :] <= places[None, :, None]).astype(jnp.int32), axis=2, dtype=jnp.int32))
    live_rows = (places[None, :] < seq_ends[:, -1:]).astype(jnp.float32)
    return (segment, live_rows)

def reference(tokens, cotangent, lengths, mat_a, mat_b, norms, first_a, second_a, first_b, second_b, first_n, second_n):
    width = tokens.shape[1]
    length = MB_TOK
    micro_rows = tokens.shape[0] // length
    inputs = tokens.astype(jnp.float32).reshape(micro_rows, length, width)
    segment, live_rows = segments_of(lengths, length)
    pull_rows = cotangent.astype(jnp.float32).reshape(micro_rows, length, width) * live_rows[:, :, None]

    def one_micro(totals, micro_item):
        inputs_one, pull_one, segment_one = micro_item
        result, backward = jax.vjp(lambda weights_a, weights_b, weights_n, stream_in: micro_forward(weights_a, weights_b, weights_n, stream_in, segment_one), mat_a, mat_b, norms, inputs_one)
        grad_parts = backward(pull_one)
        return ((totals[0] + grad_parts[0], totals[1] + grad_parts[1], totals[2] + grad_parts[2]), (result, grad_parts[3]))
    start_totals = (jnp.zeros_like(mat_a), jnp.zeros_like(mat_b), jnp.zeros_like(norms))
    (grad_a, grad_b, grad_n), (results, input_grads) = lax.scan(one_micro, start_totals, (inputs, pull_rows, segment))
    total_square = jnp.sum(grad_a * grad_a) + jnp.sum(grad_b * grad_b) + jnp.sum(grad_n * grad_n)
    grad_norm = jnp.sqrt(total_square)
    factor = CLIP_NORM / jnp.maximum(grad_norm, CLIP_NORM)
    clip_a = grad_a * factor
    clip_b = grad_b * factor
    clip_n = grad_n * factor
    moment_a, square_a, master_a = adam_update(mat_a, first_a, second_a, clip_a, MATRIX_RATE, MATRIX_DECAY)
    moment_b, square_b, master_b = adam_update(mat_b, first_b, second_b, clip_b, MATRIX_RATE, MATRIX_DECAY)
    moment_n, square_n, master_n = adam_update(norms, first_n, second_n, clip_n, NORM_RATE, 0.0)

    def arrange(value):
        return value.reshape(N_DP, MICRO, length, width).transpose(1, 0, 2, 3).reshape(MICRO, N_DP * length, width)
    output = arrange(results).astype(jnp.bfloat16)
    input_grad = arrange(input_grads)
    return (grad_norm, output, input_grad, clip_a, moment_a, square_a, master_a, master_a.astype(jnp.bfloat16), clip_b, moment_b, square_b, master_b, master_b.astype(jnp.bfloat16), clip_n, moment_n, square_n, master_n, master_n.astype(jnp.bfloat16))
```

```python
import jax
import jax.numpy as jnp
from jax import lax
from jax.sharding import PartitionSpec as P

HEADS = 8
STEP = 5


EPSILON = 1e-05
NEGATIVE = -1e30
CLIP_NORM = 1.0
BETA_ONE = 0.5
BETA_TWO = 0.5
ADAM_EPSILON = 1e-08
MATRIX_RATE = 0.05
NORM_RATE = 0.5
MATRIX_DECAY = 0.01


def norm_stats(value):
    centre = value - jnp.mean(value, -1, keepdims=True)
    inverse = lax.rsqrt(jnp.mean(centre * centre, -1, keepdims=True) + EPSILON)
    return (centre * inverse, inverse)


def norm_back(normal, inverse, upstream):
    return inverse * (
        upstream
        - jnp.mean(upstream, -1, keepdims=True)
        - normal * jnp.mean(upstream * normal, -1, keepdims=True)
    )


def adam_update(weight, moment_one, moment_two, gradient, step_rate, decay_rate):
    first_new = BETA_ONE * moment_one + (1.0 - BETA_ONE) * gradient
    second_new = BETA_TWO * moment_two + (1.0 - BETA_TWO) * gradient * gradient
    first_hat = first_new / (1.0 - BETA_ONE**STEP)
    second_hat = second_new / (1.0 - BETA_TWO**STEP)
    weight_new = weight - step_rate * (
        first_hat / (jnp.sqrt(second_hat) + ADAM_EPSILON) + decay_rate * weight
    )
    return (first_new, second_new, weight_new)


def segments_of(lengths_row, length):
    ends = jnp.cumsum(lengths_row, dtype=jnp.int32)
    places = jnp.arange(length, dtype=jnp.int32)
    segment = jnp.sum((ends[None, :] <= places[:, None]).astype(jnp.int32), axis=1, dtype=jnp.int32)
    live = (places < ends[-1]).astype(jnp.float32)
    return segment, live


def matmul(left, right, dims):
    return lax.dot_general(left, right, (dims, ((), ())), preferred_element_type=jnp.float32)


NN = ((1,), (0,))
NT = ((1,), (1,))
TN = ((0,), (0,))


def attention_forward(stream, weight, mask):
    length, width = stream.shape
    size = width // HEADS
    packed = matmul(stream, weight[:, : 3 * width], NN).astype(jnp.bfloat16)
    heads = packed.reshape(length, 3, HEADS, size)
    scores = jnp.einsum("qhd,khd->hqk", heads[:, 0], heads[:, 1], preferred_element_type=jnp.float32)
    scores = jnp.where(mask[None], scores * size**-0.5, NEGATIVE)
    weights = jnp.exp(scores - jnp.max(scores, -1, keepdims=True))
    probs = weights / jnp.sum(weights, -1, keepdims=True)
    mixed = jnp.einsum("hqk,khd->qhd", probs.astype(jnp.bfloat16), heads[:, 2], preferred_element_type=jnp.float32)
    mixed = mixed.reshape(length, width).astype(jnp.bfloat16)
    branch = matmul(mixed, weight[:, 3 * width :], NN)
    return branch, (heads, probs, mixed)


def attention_backward(stream, weight, kept, grad_low):
    heads, probs, mixed = kept
    length, width = stream.shape
    size = width // HEADS
    grad_out = matmul(mixed, grad_low, TN)
    grad_mixed = matmul(grad_low, weight[:, 3 * width :], NT).astype(jnp.bfloat16)
    grad_mixed = grad_mixed.reshape(length, HEADS, size)
    grad_probs = jnp.einsum("qhd,khd->hqk", grad_mixed, heads[:, 2], preferred_element_type=jnp.float32)
    centre = jnp.sum(probs * grad_probs, -1, keepdims=True)
    grad_scores = (probs * (grad_probs - centre)).astype(jnp.bfloat16)
    low = probs.astype(jnp.bfloat16)
    scale = size**-0.5
    grad_q = jnp.einsum("hqk,khd->qhd", grad_scores, heads[:, 1], preferred_element_type=jnp.float32) * scale
    grad_k = jnp.einsum("hqk,qhd->khd", grad_scores, heads[:, 0], preferred_element_type=jnp.float32) * scale
    grad_v = jnp.einsum("hqk,qhd->khd", low, grad_mixed, preferred_element_type=jnp.float32)
    packed = jnp.concatenate([grad_q, grad_k, grad_v], axis=1).reshape(length, 3 * width)
    packed = packed.astype(jnp.bfloat16)
    grad_in = matmul(stream, packed, TN)
    grad_inputs = matmul(packed, weight[:, : 3 * width], NT)
    return grad_inputs, jnp.concatenate([grad_in, grad_out], axis=1)


def feed_forward(stream, weight, down):
    pre = matmul(stream, weight, NN)
    active = jax.nn.gelu(pre, approximate=True).astype(jnp.bfloat16)
    return matmul(active, down, NN), (pre, active)


def feed_backward(stream, weight, down, kept, grad_low):
    pre, active = kept
    grad_down = matmul(active, grad_low, TN)
    grad_active = matmul(grad_low, down, NT)
    pull = jax.vjp(lambda value: jax.nn.gelu(value, approximate=True), pre)[1]
    grad_pre = pull(grad_active)[0].astype(jnp.bfloat16)
    grad_up = matmul(stream, grad_pre, TN)
    return matmul(grad_pre, weight, NT), grad_up, grad_down


def micro_step(rows, pull, segment, mats, downs, gains, biases):
    low = jnp.bfloat16
    mask = segment[:, None] == segment[None, :]
    stream, dual = rows, jnp.zeros_like(rows)
    saved = []
    for sub in range(4):
        if sub % 2 == 0:
            branch, kept = attention_forward(stream, mats[sub], mask)
        else:
            branch, kept = feed_forward(stream, mats[sub], downs[sub // 2])
        normal, inverse = norm_stats(stream.astype(jnp.float32) + branch)
        out = normal * gains[sub] + biases[sub]
        total = dual.astype(jnp.float32) + branch
        saved.append((stream, kept, normal, inverse))
        if sub < 3:
            stream, dual = out.astype(low), total.astype(low)
    dual_normal, dual_inverse = norm_stats(total)
    output = (out + dual_normal).astype(low)
    grad_out, grad_dual = pull, norm_back(dual_normal, dual_inverse, pull)
    grads_a, grads_b, grads_n = [None] * 4, [None] * 2, [None] * 4
    for sub in (3, 2, 1, 0):
        stream, kept, normal, inverse = saved[sub]
        grads_n[sub] = jnp.stack([jnp.sum(grad_out * normal, 0), jnp.sum(grad_out, 0)], axis=1)
        summed = norm_back(normal, inverse, grad_out * gains[sub])
        branch_low = (summed + grad_dual).astype(low)
        if sub % 2 == 0:
            inner, grads_a[sub] = attention_backward(stream, mats[sub], kept, branch_low)
        else:
            inner, grads_a[sub], grads_b[sub // 2] = feed_backward(
                stream, mats[sub], downs[sub // 2], kept, branch_low
            )
        grad_in = summed + inner
        if sub > 0:
            grad_out = grad_in.astype(low).astype(jnp.float32)
            grad_dual = grad_dual.astype(low).astype(jnp.float32)
    return output, grad_in, jnp.stack(grads_a), jnp.stack(grads_b), jnp.stack(grads_n)


def body(
    tokens, cotangent, lengths, mat_a, mat_b, norms, first_a, second_a, first_b, second_b, first_n, second_n
):
    low = jnp.bfloat16
    own = lax.axis_index("section")
    length = tokens.shape[0] // lengths.shape[0]
    rows = lax.dynamic_slice_in_dim(tokens, own * length, length, 0)
    segment, live = segments_of(lax.dynamic_index_in_dim(lengths, own, 0, keepdims=False), length)
    pull = lax.dynamic_slice_in_dim(cotangent, own * length, length, 0).astype(jnp.float32) * live[:, None]

    def gathered(value):
        return lax.all_gather(lax.all_gather(value, "dp", axis=1, tiled=True), "section", axis=0, tiled=True)

    mats = gathered(mat_a.astype(low))
    scales = gathered(norms.astype(low)).astype(jnp.float32)
    downs = lax.all_gather(mat_b.astype(low), "section", axis=2, tiled=True)
    downs = lax.all_gather(downs, "dp", axis=1, tiled=True)
    output, input_grad, part_a, part_b, part_n = micro_step(
        rows, pull, segment, mats, downs, scales[:, :, 0], scales[:, :, 1]
    )

    def scattered(value, section_dim):
        value = lax.psum_scatter(value, "section", scatter_dimension=section_dim, tiled=True)
        return lax.psum_scatter(value, "dp", scatter_dimension=1, tiled=True).astype(jnp.float32)

    grad_a = scattered(part_a.astype(low), 0)
    grad_b = scattered(part_b.astype(low), 2)
    grad_n = scattered(part_n, 0)
    square = jnp.sum(grad_a * grad_a) + jnp.sum(grad_b * grad_b) + jnp.sum(grad_n * grad_n)
    grad_norm = jnp.sqrt(lax.psum(square, ("section", "dp")))
    factor = CLIP_NORM / jnp.maximum(grad_norm, CLIP_NORM)
    results = [grad_norm, output[None], input_grad[None]]
    for weight, one, two, grad, rate, decay in (
        (mat_a, first_a, second_a, grad_a, MATRIX_RATE, MATRIX_DECAY),
        (mat_b, first_b, second_b, grad_b, MATRIX_RATE, MATRIX_DECAY),
        (norms, first_n, second_n, grad_n, NORM_RATE, 0.0),
    ):
        clip = grad * factor
        moment, square_new, master = adam_update(weight, one, two, clip, rate, decay)
        results += [clip, moment, square_new, master, master.astype(low)]
    return tuple(results)


def solution(mesh):
    placed = (
        P("dp", None),
        P("dp", None),
        P("dp", None),
        P("section", "dp", None),
        P(None, "dp", "section"),
        P("section", "dp", None),
        P("section", "dp", None),
        P("section", "dp", None),
        P(None, "dp", "section"),
        P(None, "dp", "section"),
        P("section", "dp", None),
        P("section", "dp", None),
    )
    return jax.shard_map(
        body,
        mesh=mesh,
        in_specs=placed,
        out_specs=(
            P(),
            P("section", "dp", None),
            P("section", "dp", None),
            P("section", "dp", None),
            P("section", "dp", None),
            P("section", "dp", None),
            P("section", "dp", None),
            P("section", "dp", None),
            P(None, "dp", "section"),
            P(None, "dp", "section"),
            P(None, "dp", "section"),
            P(None, "dp", "section"),
            P(None, "dp", "section"),
            P("section", "dp", None),
            P("section", "dp", None),
            P("section", "dp", None),
            P("section", "dp", None),
            P("section", "dp", None),
        ),
        check_vma=False,
    )
```

```python
import functools
import types

import jax
import jax.numpy as jnp
from jax import lax
from jax.experimental import pallas as pl
from jax.experimental.pallas import tpu as pltpu
from jax.sharding import PartitionSpec as P

HEADS = 8
STEP = 5


EPSILON = 1e-05
NEGATIVE = -1e30
CLIP_NORM = 1.0
BETA_ONE = 0.5
BETA_TWO = 0.5
ADAM_EPSILON = 1e-08
MATRIX_RATE = 0.05
NORM_RATE = 0.5
MATRIX_DECAY = 0.01


def norm_stats(value):
    centre = value - jnp.mean(value, -1, keepdims=True)
    inverse = lax.rsqrt(jnp.mean(centre * centre, -1, keepdims=True) + EPSILON)
    return (centre * inverse, inverse)


def norm_back(normal, inverse, upstream):
    return inverse * (
        upstream
        - jnp.mean(upstream, -1, keepdims=True)
        - normal * jnp.mean(upstream * normal, -1, keepdims=True)
    )


def adam_update(weight, moment_one, moment_two, gradient, step_rate, decay_rate):
    first_new = BETA_ONE * moment_one + (1.0 - BETA_ONE) * gradient
    second_new = BETA_TWO * moment_two + (1.0 - BETA_TWO) * gradient * gradient
    first_hat = first_new / (1.0 - BETA_ONE**STEP)
    second_hat = second_new / (1.0 - BETA_TWO**STEP)
    weight_new = weight - step_rate * (
        first_hat / (jnp.sqrt(second_hat) + ADAM_EPSILON) + decay_rate * weight
    )
    return (first_new, second_new, weight_new)


def segments_of(lengths_row, length):
    ends = jnp.cumsum(lengths_row, dtype=jnp.int32)
    places = jnp.arange(length, dtype=jnp.int32)
    segment = jnp.sum((ends[None, :] <= places[:, None]).astype(jnp.int32), axis=1, dtype=jnp.int32)
    live = (places < ends[-1]).astype(jnp.float32)
    return segment, live


def matmul(left, right, dims):
    return lax.dot_general(left, right, (dims, ((), ())), preferred_element_type=jnp.float32)


NN = ((1,), (0,))
NT = ((1,), (1,))
TN = ((0,), (0,))


def attention_forward(stream, weight, mask):
    length, width = stream.shape
    size = width // HEADS
    packed = matmul(stream, weight[:, : 3 * width], NN).astype(jnp.bfloat16)
    heads = packed.reshape(length, 3, HEADS, size)
    scores = jnp.einsum("qhd,khd->hqk", heads[:, 0], heads[:, 1], preferred_element_type=jnp.float32)
    scores = jnp.where(mask[None], scores * size**-0.5, NEGATIVE)
    weights = jnp.exp(scores - jnp.max(scores, -1, keepdims=True))
    probs = weights / jnp.sum(weights, -1, keepdims=True)
    mixed = jnp.einsum("hqk,khd->qhd", probs.astype(jnp.bfloat16), heads[:, 2], preferred_element_type=jnp.float32)
    mixed = mixed.reshape(length, width).astype(jnp.bfloat16)
    branch = matmul(mixed, weight[:, 3 * width :], NN)
    return branch, (heads, probs, mixed)


def attention_backward(stream, weight, kept, grad_low):
    heads, probs, mixed = kept
    length, width = stream.shape
    size = width // HEADS
    grad_out = matmul(mixed, grad_low, TN)
    grad_mixed = matmul(grad_low, weight[:, 3 * width :], NT).astype(jnp.bfloat16)
    grad_mixed = grad_mixed.reshape(length, HEADS, size)
    grad_probs = jnp.einsum("qhd,khd->hqk", grad_mixed, heads[:, 2], preferred_element_type=jnp.float32)
    centre = jnp.sum(probs * grad_probs, -1, keepdims=True)
    grad_scores = (probs * (grad_probs - centre)).astype(jnp.bfloat16)
    low = probs.astype(jnp.bfloat16)
    scale = size**-0.5
    grad_q = jnp.einsum("hqk,khd->qhd", grad_scores, heads[:, 1], preferred_element_type=jnp.float32) * scale
    grad_k = jnp.einsum("hqk,qhd->khd", grad_scores, heads[:, 0], preferred_element_type=jnp.float32) * scale
    grad_v = jnp.einsum("hqk,qhd->khd", low, grad_mixed, preferred_element_type=jnp.float32)
    packed = jnp.concatenate([grad_q, grad_k, grad_v], axis=1).reshape(length, 3 * width)
    packed = packed.astype(jnp.bfloat16)
    grad_in = matmul(stream, packed, TN)
    grad_inputs = matmul(packed, weight[:, : 3 * width], NT)
    return grad_inputs, jnp.concatenate([grad_in, grad_out], axis=1)


def feed_forward(stream, weight, down):
    pre = matmul(stream, weight, NN)
    active = jax.nn.gelu(pre, approximate=True).astype(jnp.bfloat16)
    return matmul(active, down, NN), (pre, active)


def feed_backward(stream, weight, down, kept, grad_low):
    pre, active = kept
    grad_down = matmul(active, grad_low, TN)
    grad_active = matmul(grad_low, down, NT)
    pull = jax.vjp(lambda value: jax.nn.gelu(value, approximate=True), pre)[1]
    grad_pre = pull(grad_active)[0].astype(jnp.bfloat16)
    grad_up = matmul(stream, grad_pre, TN)
    return matmul(grad_pre, weight, NT), grad_up, grad_down


def micro_step(rows, pull, segment, mats, downs, gains, biases):
    low = jnp.bfloat16
    mask = segment[:, None] == segment[None, :]
    stream, dual = rows, jnp.zeros_like(rows)
    saved = []
    for sub in range(4):
        if sub % 2 == 0:
            branch, kept = attention_forward(stream, mats[sub], mask)
        else:
            branch, kept = feed_forward(stream, mats[sub], downs[sub // 2])
        normal, inverse = norm_stats(stream.astype(jnp.float32) + branch)
        out = normal * gains[sub] + biases[sub]
        total = dual.astype(jnp.float32) + branch
        saved.append((stream, kept, normal, inverse))
        if sub < 3:
            stream, dual = out.astype(low), total.astype(low)
    dual_normal, dual_inverse = norm_stats(total)
    output = (out + dual_normal).astype(low)
    grad_out, grad_dual = pull, norm_back(dual_normal, dual_inverse, pull)
    grads_a, grads_b, grads_n = [None] * 4, [None] * 2, [None] * 4
    for sub in (3, 2, 1, 0):
        stream, kept, normal, inverse = saved[sub]
        grads_n[sub] = jnp.stack([jnp.sum(grad_out * normal, 0), jnp.sum(grad_out, 0)], axis=1)
        summed = norm_back(normal, inverse, grad_out * gains[sub])
        branch_low = (summed + grad_dual).astype(low)
        if sub % 2 == 0:
            inner, grads_a[sub] = attention_backward(stream, mats[sub], kept, branch_low)
        else:
            inner, grads_a[sub], grads_b[sub // 2] = feed_backward(
                stream, mats[sub], downs[sub // 2], kept, branch_low
            )
        grad_in = summed + inner
        if sub > 0:
            grad_out = grad_in.astype(low).astype(jnp.float32)
            grad_dual = grad_dual.astype(low).astype(jnp.float32)
    return output, grad_in, jnp.stack(grads_a), jnp.stack(grads_b), jnp.stack(grads_n)


def finish_step(grad_norm, output, input_grad, *groups):
    factor = CLIP_NORM / jnp.maximum(grad_norm, CLIP_NORM)
    results = [grad_norm, output[None], input_grad[None]]
    for weight, one, two, grad, rate, decay in groups:
        clip = grad * factor
        moment, square_new, master = adam_update(weight, one, two, clip, rate, decay)
        results += [clip, moment, square_new, master, master.astype(jnp.bfloat16)]
    return tuple(results)


def body(
    tokens, cotangent, lengths, mat_a, mat_b, norms, first_a, second_a, first_b, second_b, first_n, second_n
):
    low = jnp.bfloat16
    own = lax.axis_index("section")
    length = tokens.shape[0] // lengths.shape[0]
    rows = lax.dynamic_slice_in_dim(tokens, own * length, length, 0)
    segment, live = segments_of(lax.dynamic_index_in_dim(lengths, own, 0, keepdims=False), length)
    pull = lax.dynamic_slice_in_dim(cotangent, own * length, length, 0).astype(jnp.float32) * live[:, None]

    def gathered(value):
        return lax.all_gather(lax.all_gather(value, "dp", axis=1, tiled=True), "section", axis=0, tiled=True)

    mats = gathered(mat_a.astype(low))
    scales = gathered(norms.astype(low)).astype(jnp.float32)
    downs = lax.all_gather(mat_b.astype(low), "section", axis=2, tiled=True)
    downs = lax.all_gather(downs, "dp", axis=1, tiled=True)
    output, input_grad, part_a, part_b, part_n = micro_step(
        rows, pull, segment, mats, downs, scales[:, :, 0], scales[:, :, 1]
    )

    def scattered(value, section_dim):
        value = lax.psum_scatter(value, "section", scatter_dimension=section_dim, tiled=True)
        return lax.psum_scatter(value, "dp", scatter_dimension=1, tiled=True).astype(jnp.float32)

    grad_a = scattered(part_a.astype(low), 0)
    grad_b = scattered(part_b.astype(low), 2)
    grad_n = scattered(part_n, 0)
    square = jnp.sum(grad_a * grad_a) + jnp.sum(grad_b * grad_b) + jnp.sum(grad_n * grad_n)
    grad_norm = jnp.sqrt(lax.psum(square, ("section", "dp")))
    return finish_step(
        grad_norm, output, input_grad,
        (mat_a, first_a, second_a, grad_a, MATRIX_RATE, MATRIX_DECAY),
        (mat_b, first_b, second_b, grad_b, MATRIX_RATE, MATRIX_DECAY),
        (norms, first_n, second_n, grad_n, NORM_RATE, 0.0),
    )


LOW = jnp.bfloat16
WIDE = jnp.float32
MESH = pl.DeviceIdType.MESH
SECTIONS = 4
LANES = 128
BLOCK = 64


def kernel_scratch(chips, rows_a, rows_b, cols_b, length, width, hidden):
    devices = 2 * chips
    return (
        ("wa", (4, width, hidden), LOW),
        ("wb", (2, hidden, width), LOW),
        ("tiles", (devices, SECTIONS, 8, LANES), WIDE),
        ("x", (4, length, width), LOW),
        ("xt", (4, width, length), LOW),
        ("y", (length, width), LOW),
        ("cot", (length, width), LOW),
        ("bias", (length, length), WIDE),
        ("live", (length, 1), WIDE),
        ("f", (length, width), WIDE),
        ("n", (4, length, width), WIDE),
        ("inv", (4, length, 1), WIDE),
        ("q", (2, length, width), LOW),
        ("k", (2, length, width), LOW),
        ("v", (2, length, width), LOW),
        ("kt", (2, width, length), LOW),
        ("vt", (2, width, length), LOW),
        ("ot", (2, width, length), LOW),
        ("pt", (2, HEADS, length, length), LOW),
        ("g", (2, length, hidden), LOW),
        ("slope", (2, length, hidden), LOW),
        ("gx", (length, width), WIDE),
        ("gy", (length, width), WIDE),
        ("df", (length, width), LOW),
        ("dft", (width, length), LOW),
        ("dm", (length, width), LOW),
        ("dqt", (width, length), LOW),
        ("dp", (length, hidden), LOW),
        ("ga", (4, chips, 2, rows_a, hidden), LOW),
        ("gb", (2, chips, 2, SECTIONS, 2, cols_b // 2, rows_b), LOW),
        ("ng", (devices, 8, width), WIDE),
        ("ns", (SECTIONS, 8, width), WIDE),
        ("sq", (devices, 8, LANES), WIDE),
        ("sqs", (SECTIONS, 8, LANES), WIDE),
        ("sa", (4, chips, rows_a, hidden), LOW),
        ("sb", (2, chips, SECTIONS, 2, cols_b // 2, rows_b), LOW),
        ("xa", (chips, rows_a, hidden), LOW),
        ("ya", (chips, rows_a, hidden), LOW),
        ("xha", (chips, rows_a // 2, hidden), LOW),
        ("yha", (chips, rows_a // 2, hidden), LOW),
        ("za", (chips + 1, rows_a, hidden), LOW),
        ("xb", (2, 2, chips, cols_b // 2, rows_b), LOW),
        ("yb", (2, 2, chips, cols_b // 2, rows_b), LOW),
        ("xhb", (2, chips, cols_b // 2, rows_b), LOW),
        ("yhb", (2, chips, cols_b // 2, rows_b), LOW),
        ("zb", (2, chips + 1, 2, cols_b // 2, rows_b), LOW),
        ("in_s", (2,), None),
        ("gz_s", (3, 2, chips, 2), None),
        ("gz_r", (3, chips, 2), None),
        ("gx_s", (3, chips, 2), None),
        ("gx_r", (3, chips, 2), None),
        ("gy_s", (3, chips, 2), None),
        ("gy_r", (3, chips, 2), None),
        ("gxr_s", (3, chips), None),
        ("gxr_r", (3, chips), None),
        ("gyr_s", (3, chips), None),
        ("gyr_r", (3, chips), None),
        ("gs_s", (6,), None),
        ("gs_r", (6,), None),
        ("small_s", (3, 2), None),
        ("small_r", (3, 2), None),
        ("sa_s", (4, chips), None),
        ("sa_r", (4, chips), None),
        ("xa_s", (chips, 2), None),
        ("xa_r", (chips, 2), None),
        ("ya_s", (chips, 2), None),
        ("ya_r", (chips, 2), None),
        ("xha_s", (chips,), None),
        ("xha_r", (chips,), None),
        ("yha_s", (chips,), None),
        ("yha_r", (chips,), None),
        ("za_s", (chips,), None),
        ("za_r", (chips + 1,), None),
        ("sb_s", (2, chips), None),
        ("sb_r", (2, chips), None),
        ("xb_s", (2, 2), None),
        ("xb_r", (2, 2), None),
        ("yb_s", (2, 2), None),
        ("yb_r", (2, 2), None),
        ("xhb_s", (2,), None),
        ("xhb_r", (2,), None),
        ("yhb_s", (2,), None),
        ("yhb_r", (2,), None),
        ("zb_s", (2, chips), None),
        ("zb_r", (2, chips + 1), None),
    )


INPUTS = ("tokens", "cotangent", "lengths", "mat_a", "mat_b", "norms")
OUTPUTS = ("grad_a", "grad_b", "grad_n", "square", "output", "input_grad")


def step_kernel(names, *refs):
    r = types.SimpleNamespace(**dict(zip(names, refs)))
    width, hidden = r.wa.shape[1:]
    length = r.x.shape[1]
    chips, rows_a = r.sa.shape[1:3]
    devices = 2 * chips
    half_b, rows_b = r.sb.shape[4:]
    cols_b = 2 * half_b
    half_a = rows_a // 2
    head = width // HEADS
    scale = head**-0.5

    s, d = lax.axis_index("section"), lax.axis_index("dp")
    z, c = lax.div(d, 2), lax.rem(d, 2)
    sx = s + 1 - 2 * lax.rem(s, 2)
    sy = lax.rem(s + 2, SECTIONS)
    sd = SECTIONS - 1 - s
    to_sibling = {"dp": d + 1 - 2 * c}
    to_up, to_down = {"dp": d + 2}, {"dp": d - 2}
    to_x, to_y = {"section": sx}, {"section": sy}
    below, above = z > 0, z < chips - 1
    group = [{"dp": lax.rem(d + step, devices)} for step in range(1, devices)]
    plane = [{"section": lax.rem(s + step, SECTIONS)} for step in range(1, SECTIONS)]
    finish = []

    def when(condition, work):
        if condition is None:
            work()
        else:
            pl.when(condition)(work)

    def push(source, target, send_sem, recv_sem, device):
        pltpu.make_async_remote_copy(
            src_ref=source,
            dst_ref=target,
            send_sem=send_sem,
            recv_sem=recv_sem,
            device_id=device,
            device_id_type=MESH,
        ).start()

    def arrived(target, sem):
        pltpu.make_async_remote_copy(
            src_ref=target, dst_ref=target, send_sem=sem, recv_sem=sem, device_id=to_x, device_id_type=MESH
        ).wait_recv()

    def sent(source, sem):
        pltpu.make_async_remote_copy(
            src_ref=source, dst_ref=source, send_sem=sem, recv_sem=sem, device_id=to_x, device_id_type=MESH
        ).wait_send()

    def at_end(condition, source, sem):
        finish.append((condition, source, sem))

    def aligned(start, size):
        return pl.ds(pl.multiple_of(start, size), size)

    own_x = pltpu.make_async_copy(r.tokens.at[aligned(s * length, length)], r.x.at[0], r.in_s.at[0])
    own_cot = pltpu.make_async_copy(r.cotangent.at[aligned(s * length, length)], r.cot, r.in_s.at[1])
    own_x.start()
    own_cot.start()
    barrier = pltpu.get_barrier_semaphore()
    for peer in group + plane:
        pl.semaphore_signal(barrier, inc=1, device_id=peer, device_id_type=MESH)
    r.wa[s, aligned(d * rows_a, rows_a), :] = r.mat_a[0].astype(LOW)
    for layer in range(2):
        r.wb[layer, aligned(d * rows_b, rows_b), aligned(s * cols_b, cols_b)] = r.mat_b[layer].astype(LOW)
    norms = r.norms[0].astype(LOW).astype(WIDE)
    place = lax.broadcasted_iota(jnp.int32, (rows_a, LANES), 1) - lax.broadcasted_iota(
        jnp.int32, (rows_a, LANES), 0
    )
    here = place == c * rows_a
    tile_rows = [
        jnp.sum(jnp.where(here, norms[:, kind : kind + 1], 0.0), 0, keepdims=True) for kind in range(2)
    ]
    r.tiles[d, s] = jnp.concatenate(tile_rows + [jnp.zeros((6, LANES), WIDE)], axis=0)
    pl.semaphore_wait(barrier, len(group) + len(plane))

    def small_out(which, source):
        for peer in group:
            push(source, source, r.small_s.at[which, 0], r.small_r.at[which, 0], peer)

    def small_group(which, like):
        arrived(like, r.small_r.at[which, 0])
        sent(like, r.small_s.at[which, 0])

    def small_plane_out(which, source):
        for peer in plane:
            push(source, source, r.small_s.at[which, 1], r.small_r.at[which, 1], peer)

    def small_plane(which, like):
        arrived(like, r.small_r.at[which, 1])
        sent(like, r.small_s.at[which, 1])

    def block_a(section, chip, half):
        return r.wa.at[section, aligned((2 * chip + c) * rows_a + half * half_a, half_a), :]

    def block_b(layer):
        part = rows_b // 2

        def block(section, chip, half):
            return r.wb.at[
                layer,
                aligned((2 * chip + c) * rows_b + half * part, part),
                aligned(section * cols_b, cols_b),
            ]

        return block

    items = (block_a, block_b(0), block_b(1))

    def to_the_sibling(item, section, chip, half):
        block = items[item](section, chip, half)
        slot = section if item == 0 else 3 + item
        push(block, block, r.gs_s.at[slot], r.gs_r.at[slot], to_sibling)

    def spread_plane(item, chip):
        for half in range(2):
            block = items[item](s, chip, half)
            push(block, block, r.gx_s.at[item, chip, half], r.gx_r.at[item, chip, half], to_x)
            push(block, block, r.gy_s.at[item, chip, half], r.gy_r.at[item, chip, half], to_y)
            to_the_sibling(item, s, chip, half)

    def up(item, chip, half):
        block = items[item](s, chip, half)
        push(block, block, r.gz_s.at[item, 0, chip, half], r.gz_r.at[item, chip, half], to_up)

    def down(item, chip, half):
        block = items[item](s, chip, half)
        push(block, block, r.gz_s.at[item, 1, chip, half], r.gz_r.at[item, chip, half], to_down)

    def start_line(item):
        for half in range(2):
            when(above, lambda: up(item, z, half))
            when(below, lambda: down(item, z, half))

    def line_step(item, step):
        def from_below():
            for half in range(2):
                arrived(items[item](s, z - step, half), r.gz_r.at[item, z - step, half])
                when(above, lambda: up(item, z - step, half))
            spread_plane(item, z - step)

        def from_above():
            for half in range(2):
                arrived(items[item](s, z + step, half), r.gz_r.at[item, z + step, half])
                when(below, lambda: down(item, z + step, half))
            spread_plane(item, z + step)

        when(z >= step, from_below)
        when(z + step < chips, from_above)

    def plane_step(item):
        for chip in range(chips):
            for half in range(2):
                arrived(items[item](sx, chip, half), r.gx_r.at[item, chip, half])
                if half == 1:
                    block = items[item](sx, chip, half)
                    push(block, block, r.gyr_s.at[item, chip], r.gyr_r.at[item, chip], to_y)
                to_the_sibling(item, sx, chip, half)
                arrived(items[item](sy, chip, half), r.gy_r.at[item, chip, half])
                if half == 0:
                    block = items[item](sy, chip, half)
                    push(block, block, r.gxr_s.at[item, chip], r.gxr_r.at[item, chip], to_x)
                to_the_sibling(item, sy, chip, half)

    def relay_step(item):
        for chip in range(chips):
            arrived(items[item](sd, chip, 0), r.gxr_r.at[item, chip])
            to_the_sibling(item, sd, chip, 0)
            arrived(items[item](sd, chip, 1), r.gyr_r.at[item, chip])
            to_the_sibling(item, sd, chip, 1)

    whole_a = r.wa.at[0, pl.ds(0, chips * rows_a)]
    whole_b = r.wb.at[0, pl.ds(0, chips * rows_b)]
    for slot in range(6):
        at_end(None, whole_a if slot < 4 else whole_b, r.gs_s.at[slot])
    for item in range(3):
        for chip in range(chips):
            for half in range(2):
                block = items[item](0, chip, half)
                at_end(None, block, r.gx_s.at[item, chip, half])
                at_end(None, block, r.gy_s.at[item, chip, half])
                at_end(above & (z >= chip), block, r.gz_s.at[item, 0, chip, half])
                at_end(below & (z <= chip), block, r.gz_s.at[item, 1, chip, half])
            block = items[item](0, chip, 0)
            at_end(None, block, r.gxr_s.at[item, chip])
            at_end(None, block, r.gyr_s.at[item, chip])

    def product(left, right, dims):
        return lax.dot_general(left, right, (dims, ((), ())), preferred_element_type=WIDE)

    def loop(count, work):
        def one(index, carry):
            work(index)
            return carry

        lax.fori_loop(0, count, one, 0)

    def gain_row(layer, kind):
        parts = [
            r.tiles[2 * chip, layer, kind : kind + 1, :] + r.tiles[2 * chip + 1, layer, kind : kind + 1, :]
            for chip in range(chips)
        ]
        return jnp.concatenate(parts, axis=1)

    def stats(value):
        centre = value - jnp.mean(value, -1, keepdims=True)
        inverse = lax.rsqrt(jnp.mean(centre * centre, -1, keepdims=True) + EPSILON)
        return centre * inverse, inverse

    lane = lax.broadcasted_iota(jnp.int32, (1, 2 * head), 1)
    first_half = (lane < head).astype(WIDE)
    half_masks = (first_half.astype(LOW), (1.0 - first_half).astype(LOW))

    def prepare_masks():
        ends, total = [], jnp.int32(0)
        for slot in range(r.lengths.shape[1]):
            total = total + r.lengths[s, slot]
            ends.append(total)
        down_places = lax.broadcasted_iota(jnp.int32, (length, 1), 0)
        across_places = lax.broadcasted_iota(jnp.int32, (1, length), 1)
        down_segment = jnp.zeros((length, 1), jnp.int32)
        across_segment = jnp.zeros((1, length), jnp.int32)
        for end in ends:
            down_segment = down_segment + (end <= down_places).astype(jnp.int32)
            across_segment = across_segment + (end <= across_places).astype(jnp.int32)
        r.bias[...] = jnp.where(down_segment == across_segment, 0.0, NEGATIVE)
        r.live[...] = (down_places < total).astype(WIDE)

    def attention(layer):
        at = layer // 2
        rows = r.x[layer]
        r.xt[layer] = rows.T
        r.q[at] = product(rows, r.wa[layer, :, 0:width], NN).astype(LOW) * jnp.asarray(scale, LOW)
        keys = product(rows, r.wa[layer, :, width : 2 * width], NN).astype(LOW)
        r.k[at] = keys
        r.kt[at] = (keys * jnp.asarray(scale, LOW)).T
        values = product(rows, r.wa[layer, :, 2 * width : 3 * width], NN).astype(LOW)
        r.v[at] = values
        r.vt[at] = values.T

        def pair(index):
            lanes = aligned(index * 2 * head, 2 * head)
            for which in range(2):
                scores = product(r.k[at, :, lanes], r.q[at, :, lanes] * half_masks[which], NT) + r.bias[...]
                weights = jnp.exp(scores - jnp.max(scores, 0, keepdims=True))
                probs = (weights * (1.0 / jnp.sum(weights, 0, keepdims=True))).astype(LOW)
                r.pt[at, 2 * index + which] = probs
                place = aligned((2 * index + which) * head, head)
                r.ot[at, place, :] = product(r.vt[at, place, :], probs, NN).astype(LOW)

        loop(HEADS // 2, pair)
        r.f[...] = product(r.ot[at].T, r.wa[layer, :, 3 * width :], NN)

    def expand(layer):
        at = layer // 2
        r.xt[layer] = r.x[layer].T

        def columns(index):
            place = aligned(index * width, width)
            pre = product(r.x[layer], r.wa[layer, :, place], NN)
            squared = pre * pre
            slope = 0.7978845608 * (1.0 + 3 * 0.044715 * squared)
            bent = jnp.tanh(0.7978845608 * pre * (1.0 + 0.044715 * squared))
            r.g[at, :, place] = (0.5 * pre * (1.0 + bent)).astype(LOW)
            r.slope[at, :, place] = (0.5 * (1.0 + bent) + 0.5 * pre * (1.0 - bent * bent) * slope).astype(LOW)

        loop(hidden // width, columns)

    def contract(layer):
        r.f[...] = product(r.g[layer // 2], r.wb[layer // 2], NN)

    def by_rows(work):
        loop(length // BLOCK, lambda index: work(aligned(index * BLOCK, BLOCK)))

    def normalize(layer):
        gain, offset = gain_row(layer, 0), gain_row(layer, 1)

        def some(rows):
            branch = r.f[rows, :]
            normal, inverse = stats(r.x[layer, rows, :].astype(WIDE) + branch)
            r.n[layer, rows, :] = normal
            r.inv[layer, rows, :] = inverse
            out = normal * gain + offset
            dual = branch if layer == 0 else r.y[rows, :].astype(WIDE) + branch
            if layer < 3:
                r.x[layer + 1, rows, :] = out.astype(LOW)
                r.y[rows, :] = dual.astype(LOW)
            else:
                dual_normal, dual_inverse = stats(dual)
                r.output[rows, :] = (out + dual_normal).astype(LOW)
                pull = r.cot[rows, :].astype(WIDE) * r.live[rows, :]
                r.gx[rows, :] = pull
                r.gy[rows, :] = norm_back(dual_normal, dual_inverse, pull)

        by_rows(some)

    def back_normalize(layer):
        gain = gain_row(layer, 0)

        def some(index, sums):
            rows = aligned(index * BLOCK, BLOCK)
            upstream = r.gx[rows, :]
            normal = r.n[layer, rows, :]
            summed = norm_back(normal, r.inv[layer, rows, :], upstream * gain)
            dual = r.gy[rows, :]
            r.gx[rows, :] = summed
            r.df[rows, :] = (summed + dual).astype(LOW)
            if layer == 3:
                r.gy[rows, :] = dual.astype(LOW).astype(WIDE)
            return (
                sums[0] + jnp.sum(upstream * normal, 0, keepdims=True),
                sums[1] + jnp.sum(upstream, 0, keepdims=True),
            )

        zero = jnp.zeros((1, width), WIDE)
        gains, offsets = lax.fori_loop(0, length // BLOCK, some, (zero, zero))
        r.ng[d, 2 * layer : 2 * layer + 1, :] = gains
        r.ng[d, 2 * layer + 1 : 2 * layer + 2, :] = offsets

    def pass_down(layer, inner):
        total = r.gx[...] + inner
        if layer > 0:
            r.gx[...] = total.astype(LOW).astype(WIDE)
        else:
            r.input_grad[...] = total

    def keep_a(layer, place, value):
        r.ga[layer, :, :, :, place] = value.astype(LOW).reshape(chips, 2, rows_a, value.shape[1])

    def back_contract(layer):
        at = layer // 2
        r.dft[...] = r.df[...].T

        def owner(index):
            value = product(r.dft[...], r.g[at, :, aligned(index * rows_b, rows_b)], NN)
            r.gb[at, lax.div(index, 2), lax.rem(index, 2)] = value.astype(LOW).reshape(
                SECTIONS, 2, half_b, rows_b
            )

        loop(devices, owner)

    def back_expand(layer):
        at = layer // 2

        def columns(index):
            place = aligned(index * width, width)
            pulled = product(r.df[...], r.wb[at, place, :], NT)
            pulled = (pulled * r.slope[at, :, place].astype(WIDE)).astype(LOW)
            r.dp[:, place] = pulled
            keep_a(layer, place, product(r.xt[layer], pulled, NN))

        loop(hidden // width, columns)
        return lambda: pass_down(layer, product(r.dp[...], r.wa[layer], NT))

    def back_attention(layer):
        at = layer // 2
        keep_a(layer, pl.ds(3 * width, width), product(r.ot[at], r.df[...], NN))
        r.dm[...] = product(r.df[...], r.wa[layer, :, 3 * width :], NT).astype(LOW)

        def pair(index):
            lanes = aligned(index * 2 * head, 2 * head)
            pulled = r.dm[:, lanes]
            keys, values = [], []
            for which in range(2):
                probs = r.pt[at, 2 * index + which]
                grad = product(r.v[at, :, lanes], pulled * half_masks[which], NT)
                full = probs.astype(WIDE)
                centre = jnp.sum(full * grad, 0, keepdims=True)
                scores = (full * (grad - centre)).astype(LOW)
                keys.append(product(scores, r.q[at, :, lanes], NN))
                values.append(product(probs, pulled, NN))
                place = aligned((2 * index + which) * head, head)
                r.dqt[place, :] = product(r.kt[at, place, :], scores, NN).astype(LOW)
            r.dp[:, aligned(width + index * 2 * head, 2 * head)] = jnp.where(
                lane < head, keys[0], keys[1]
            ).astype(LOW)
            r.dp[:, aligned(2 * width + index * 2 * head, 2 * head)] = jnp.where(
                lane < head, values[0], values[1]
            ).astype(LOW)

        loop(HEADS // 2, pair)
        r.dp[:, 0:width] = r.dqt[...].T

        def columns(index):
            place = aligned(index * width, width)
            keep_a(layer, place, product(r.xt[layer], r.dp[:, place], NN))

        loop(3, columns)
        return lambda: pass_down(layer, product(r.dp[:, 0 : 3 * width], r.wa[layer, :, 0 : 3 * width], NT))

    order = [chips - 1, 0] + [chip for chip in range(chips - 2, 0, -1)]

    def add_into(target, others):
        target[...] = functools.reduce(
            lambda left, right: left + right, [ref[...].astype(WIDE) for ref in (target, *others)]
        ).astype(LOW)

    def a_sibling(layer):
        for chip in order:
            push(r.ga.at[layer, chip, 1 - c], r.sa.at[layer, chip], r.sa_s.at[layer, chip], r.sa_r.at[layer, chip], to_sibling)
            at_end(None, r.sa.at[layer, chip], r.sa_s.at[layer, chip])

    first, second = pl.ds(0, half_a), pl.ds(half_a, half_a)

    def a_first(layer):
        role = [s == layer ^ bits for bits in range(4)]
        for chip in order:
            arrived(r.sa.at[layer, chip], r.sa_r.at[layer, chip])
            own = r.ga.at[layer, chip, c]
            add_into(own, [r.sa.at[layer, chip]])

            def far():
                push(own.at[second], r.yha.at[chip], r.yha_s.at[chip], r.yha_r.at[chip], to_y)
                push(own.at[first], r.xha.at[chip], r.xha_s.at[chip], r.xha_r.at[chip], to_x)

            def beside_x():
                push(own.at[first], r.xa.at[chip, first], r.xa_s.at[chip, 0], r.xa_r.at[chip, 0], to_x)

            def beside_y():
                push(own.at[second], r.ya.at[chip, second], r.ya_s.at[chip, 1], r.ya_r.at[chip, 1], to_y)

            when(role[3], far)
            when(role[1], beside_x)
            when(role[2], beside_y)

    def a_second(layer):
        role = [s == layer ^ bits for bits in range(4)]

        def beside_x():
            for chip in order:
                own = r.ga.at[layer, chip, c, second]
                arrived(r.yha.at[chip], r.yha_r.at[chip])
                add_into(own, [r.yha.at[chip]])
                push(own, r.xa.at[chip, second], r.xa_s.at[chip, 1], r.xa_r.at[chip, 1], to_x)

        def beside_y():
            for chip in order:
                own = r.ga.at[layer, chip, c, first]
                arrived(r.xha.at[chip], r.xha_r.at[chip])
                add_into(own, [r.xha.at[chip]])
                push(own, r.ya.at[chip, first], r.ya_s.at[chip, 0], r.ya_r.at[chip, 0], to_y)

        when(role[1], beside_x)
        when(role[2], beside_y)

    for chip in range(chips):
        at_end(None, r.yha.at[chip], r.yha_s.at[chip])
        at_end(None, r.xha.at[chip], r.xha_s.at[chip])
        for half in range(2):
            at_end(None, r.xha.at[chip], r.xa_s.at[chip, half])
            at_end(None, r.xha.at[chip], r.ya_s.at[chip, half])
        at_end((z < chip) | (z > chip), r.za.at[0], r.za_s.at[chip])

    def a_line(layer):
        def work():
            for chip in order:
                own = r.ga.at[layer, chip, c]
                for half in range(2):
                    arrived(r.xha.at[chip], r.xa_r.at[chip, half])
                    arrived(r.xha.at[chip], r.ya_r.at[chip, half])
                add_into(own, [r.xa.at[chip], r.ya.at[chip]])

                def upwards():
                    def join():
                        arrived(r.za.at[chip + 1], r.za_r.at[chip + 1])
                        add_into(own, [r.za.at[chip + 1]])

                    when(below, join)
                    push(own, r.za.at[chip + 1], r.za_s.at[chip], r.za_r.at[chip + 1], to_up)

                def downwards():
                    def join():
                        arrived(r.za.at[chip], r.za_r.at[chip])
                        add_into(own, [r.za.at[chip]])

                    when(above, join)
                    push(own, r.za.at[chip], r.za_s.at[chip], r.za_r.at[chip], to_down)

                when(z < chip, upwards)
                when(z > chip, downwards)

        when(s == layer, work)

    def a_last():
        own = r.ga.at[s, z, c]

        def from_below():
            arrived(r.za.at[z + 1], r.za_r.at[z + 1])
            add_into(own, [r.za.at[z + 1]])

        def from_above():
            arrived(r.za.at[z], r.za_r.at[z])
            add_into(own, [r.za.at[z]])

        when(below, from_below)
        when(above, from_above)

    def b_sibling(layer):
        for chip in order:
            push(r.gb.at[layer, chip, 1 - c], r.sb.at[layer, chip], r.sb_s.at[layer, chip], r.sb_r.at[layer, chip], to_sibling)
            at_end(None, r.sb.at[layer, chip], r.sb_s.at[layer, chip])

    def b_first(layer):
        for chip in order:
            arrived(r.sb.at[layer, chip], r.sb_r.at[layer, chip])
            add_into(r.gb.at[layer, chip, c], [r.sb.at[layer, chip]])
        own = r.gb.at[layer, :, c]
        push(own.at[:, sd, 1], r.yhb.at[layer], r.yhb_s.at[layer], r.yhb_r.at[layer], to_y)
        push(own.at[:, sd, 0], r.xhb.at[layer], r.xhb_s.at[layer], r.xhb_r.at[layer], to_x)
        push(own.at[:, sx, 0], r.xb.at[layer, 0], r.xb_s.at[layer, 0], r.xb_r.at[layer, 0], to_x)
        push(own.at[:, sy, 1], r.yb.at[layer, 1], r.yb_s.at[layer, 1], r.yb_r.at[layer, 1], to_y)
        at_end(None, r.yhb.at[layer], r.yhb_s.at[layer])
        at_end(None, r.xhb.at[layer], r.xhb_s.at[layer])
        for half in range(2):
            at_end(None, r.xhb.at[layer], r.xb_s.at[layer, half])
            at_end(None, r.xhb.at[layer], r.yb_s.at[layer, half])

    def b_second(layer):
        own = r.gb.at[layer, :, c]
        arrived(r.yhb.at[layer], r.yhb_r.at[layer])
        add_into(own.at[:, sx, 1], [r.yhb.at[layer]])
        push(own.at[:, sx, 1], r.xb.at[layer, 1], r.xb_s.at[layer, 1], r.xb_r.at[layer, 1], to_x)
        arrived(r.xhb.at[layer], r.xhb_r.at[layer])
        add_into(own.at[:, sy, 0], [r.xhb.at[layer]])
        push(own.at[:, sy, 0], r.yb.at[layer, 0], r.yb_s.at[layer, 0], r.yb_r.at[layer, 0], to_y)

    def b_line(layer):
        for half in range(2):
            arrived(r.xhb.at[layer], r.xb_r.at[layer, half])
            arrived(r.xhb.at[layer], r.yb_r.at[layer, half])
            add_into(r.gb.at[layer, :, c, s, half], [r.xb.at[layer, half], r.yb.at[layer, half]])
        for chip in order:
            own = r.gb.at[layer, chip, c, s]

            def upwards():
                def join():
                    arrived(r.zb.at[layer, chip + 1], r.zb_r.at[layer, chip + 1])
                    add_into(own, [r.zb.at[layer, chip + 1]])

                when(below, join)
                push(own, r.zb.at[layer, chip + 1], r.zb_s.at[layer, chip], r.zb_r.at[layer, chip + 1], to_up)

            def downwards():
                def join():
                    arrived(r.zb.at[layer, chip], r.zb_r.at[layer, chip])
                    add_into(own, [r.zb.at[layer, chip]])

                when(above, join)
                push(own, r.zb.at[layer, chip], r.zb_s.at[layer, chip], r.zb_r.at[layer, chip], to_down)

            when(z < chip, upwards)
            when(z > chip, downwards)
            at_end((z < chip) | (z > chip), r.zb.at[layer, 0], r.zb_s.at[layer, chip])

    def b_last(layer):
        own = r.gb.at[layer, z, c, s]

        def from_below():
            arrived(r.zb.at[layer, z + 1], r.zb_r.at[layer, z + 1])
            add_into(own, [r.zb.at[layer, z + 1]])

        def from_above():
            arrived(r.zb.at[layer, z], r.zb_r.at[layer, z])
            add_into(own, [r.zb.at[layer, z]])

        when(below, from_below)
        when(above, from_above)

    small_out(0, r.tiles.at[d, s])
    start_line(0)
    spread_plane(0, z)
    line_step(0, 1)
    start_line(1)
    start_line(2)
    for step in range(2, chips):
        line_step(0, step)
    small_group(0, r.tiles.at[pl.ds(0, devices - 1), 0])
    for peer in plane:
        push(r.tiles.at[:, s], r.tiles.at[:, s], r.small_s.at[0, 1], r.small_r.at[0, 1], peer)
    prepare_masks()
    plane_step(0)
    for item in (1, 2):
        spread_plane(item, z)
        for step in range(1, chips):
            line_step(item, step)
    own_x.wait()
    own_cot.wait()
    relay_step(0)
    small_plane(0, r.tiles.at[:, pl.ds(0, SECTIONS - 1)])
    for slot in range(4):
        arrived(whole_a, r.gs_r.at[slot])
    attention(0)
    normalize(0)
    expand(1)
    plane_step(1)
    relay_step(1)
    arrived(whole_b, r.gs_r.at[4])
    contract(1)
    normalize(1)
    plane_step(2)
    attention(2)
    normalize(2)
    expand(3)
    relay_step(2)
    arrived(whole_b, r.gs_r.at[5])
    contract(3)
    normalize(3)

    back_normalize(3)
    back_contract(3)
    b_sibling(1)
    rest = back_expand(3)
    a_sibling(3)
    rest()
    b_first(1)
    a_first(3)
    back_normalize(2)
    rest = back_attention(2)
    a_sibling(2)
    b_second(1)
    a_second(3)
    rest()
    a_first(2)
    back_normalize(1)
    back_contract(1)
    b_sibling(0)
    rest = back_expand(1)
    a_sibling(1)
    b_line(1)
    a_second(2)
    rest()
    b_first(0)
    a_first(1)
    back_normalize(0)
    rest = back_attention(0)
    a_sibling(0)
    b_second(0)
    a_second(1)
    small_out(1, r.ng.at[d])
    rest()
    a_first(0)
    b_line(0)
    small_group(1, r.ng.at[pl.ds(0, devices - 1)])
    r.ns[s] = functools.reduce(lambda left, right: left + right, [r.ng[index] for index in range(devices)])
    small_plane_out(1, r.ns.at[s])
    a_second(0)
    small_plane(1, r.ns.at[pl.ds(0, SECTIONS - 1)])
    for layer in (3, 2, 1, 0):
        a_line(layer)
    b_last(1)
    b_last(0)
    a_last()

    grad_a = r.ga[s, z, c].astype(WIDE)
    r.grad_a[...] = grad_a
    total = jnp.sum(jnp.sum(grad_a * grad_a, 0, keepdims=True), 1, keepdims=True)
    for layer in range(2):
        grad_b = r.gb[layer, z, c, s].reshape(cols_b, rows_b).astype(WIDE)
        r.grad_b[layer] = grad_b.T
        total = total + jnp.sum(jnp.sum(grad_b * grad_b, 0, keepdims=True), 1, keepdims=True)
    r.sq[d] = jnp.broadcast_to(total, (8, LANES))
    small_out(2, r.sq.at[d])
    grads = functools.reduce(lambda left, right: left + right, [r.ns[index] for index in range(SECTIONS)])
    norm_square = jnp.sum(jnp.sum(grads * grads, 0, keepdims=True), 1, keepdims=True)
    chosen = jnp.zeros((2, width), WIDE)
    for layer in range(4):
        chosen = jnp.where(s == layer, grads[2 * layer : 2 * layer + 2, :], chosen)
    spread = lax.broadcasted_iota(jnp.int32, (rows_a, width), 1) - lax.broadcasted_iota(
        jnp.int32, (rows_a, width), 0
    )
    mine = spread == d * rows_a
    columns = [
        jnp.sum(jnp.where(mine, chosen[kind : kind + 1, :], 0.0), 1, keepdims=True) for kind in range(2)
    ]
    kinds = lax.broadcasted_iota(jnp.int32, (rows_a, 2), 1)
    r.grad_n[...] = jnp.where(kinds == 0, columns[0], columns[1])
    small_group(2, r.sq.at[pl.ds(0, devices - 1)])
    r.sqs[s] = functools.reduce(lambda left, right: left + right, [r.sq[index] for index in range(devices)])
    small_plane_out(2, r.sqs.at[s])
    small_plane(2, r.sqs.at[pl.ds(0, SECTIONS - 1)])
    squares = functools.reduce(lambda left, right: left + right, [r.sqs[index] for index in range(SECTIONS)])
    r.square[...] = squares + norm_square
    for condition, source, sem in finish:
        when(condition, functools.partial(sent, source, sem))


def step_call(tokens, cotangent, lengths, mat_a, mat_b, norms):
    rows_a, hidden = mat_a.shape[1:]
    rows_b, cols_b = mat_b.shape[1:]
    width = tokens.shape[1]
    length = tokens.shape[0] // lengths.shape[0]
    chips = width // rows_a // 2
    scratch = kernel_scratch(chips, rows_a, rows_b, cols_b, length, width, hidden)
    shapes = []
    for _, shape, kind in scratch:
        shapes.append(pltpu.SemaphoreType.DMA(shape) if kind is None else pltpu.VMEM(shape, kind))
    anywhere, vmem = pl.BlockSpec(memory_space=pl.ANY), pl.BlockSpec(memory_space=pltpu.VMEM)
    return pl.pallas_call(
        functools.partial(step_kernel, INPUTS + OUTPUTS + tuple(name for name, _, _ in scratch)),
        out_shape=(
            jax.ShapeDtypeStruct((rows_a, hidden), WIDE),
            jax.ShapeDtypeStruct(mat_b.shape, WIDE),
            jax.ShapeDtypeStruct((rows_a, 2), WIDE),
            jax.ShapeDtypeStruct((8, LANES), WIDE),
            jax.ShapeDtypeStruct((length, width), LOW),
            jax.ShapeDtypeStruct((length, width), WIDE),
        ),
        in_specs=[anywhere, anywhere, pl.BlockSpec(memory_space=pltpu.SMEM), vmem, vmem, vmem],
        out_specs=[vmem] * len(OUTPUTS),
        scratch_shapes=shapes,
        compiler_params=pltpu.CompilerParams(
            collective_id=0, has_side_effects=True, vmem_limit_bytes=64 * 1024 * 1024 - 256 * 1024
        ),
    )(tokens, cotangent, lengths, mat_a, mat_b, norms)


def kernel_body(
    tokens, cotangent, lengths, mat_a, mat_b, norms, first_a, second_a, first_b, second_b, first_n, second_n
):
    grad_a, grad_b, grad_n, square, output, input_grad = step_call(
        tokens, cotangent, lengths, mat_a, mat_b, norms
    )
    return finish_step(
        jnp.sqrt(square[0, 0]), output, input_grad,
        (mat_a, first_a, second_a, grad_a[None], MATRIX_RATE, MATRIX_DECAY),
        (mat_b, first_b, second_b, grad_b, MATRIX_RATE, MATRIX_DECAY),
        (norms, first_n, second_n, grad_n[None], NORM_RATE, 0.0),
    )


def chosen_body(*args):
    rows_a = args[3].shape[1]
    groups = lax.axis_size("dp")
    by_kernel = rows_a % 32 == 0 and 2 * rows_a == LANES and groups * rows_a == args[0].shape[1]
    return (kernel_body if by_kernel else body)(*args)


def solution(mesh):
    placed = (
        P("dp", None),
        P("dp", None),
        P("dp", None),
        P("section", "dp", None),
        P(None, "dp", "section"),
        P("section", "dp", None),
        P("section", "dp", None),
        P("section", "dp", None),
        P(None, "dp", "section"),
        P(None, "dp", "section"),
        P("section", "dp", None),
        P("section", "dp", None),
    )
    return jax.shard_map(
        chosen_body,
        mesh=mesh,
        in_specs=placed,
        out_specs=(
            P(),
            P("section", "dp", None),
            P("section", "dp", None),
            P("section", "dp", None),
            P("section", "dp", None),
            P("section", "dp", None),
            P("section", "dp", None),
            P("section", "dp", None),
            P(None, "dp", "section"),
            P(None, "dp", "section"),
            P(None, "dp", "section"),
            P(None, "dp", "section"),
            P(None, "dp", "section"),
            P("section", "dp", None),
            P("section", "dp", None),
            P("section", "dp", None),
            P("section", "dp", None),
            P("section", "dp", None),
        ),
        check_vma=False,
    )
```

```python
import functools
import types

import jax
import jax.numpy as jnp
from jax import lax
from jax.experimental import pallas as pl
from jax.experimental.pallas import tpu as pltpu
from jax.sharding import PartitionSpec as P

HEADS = 8
STEP = 5


EPSILON = 1e-05
NEGATIVE = -1e30
CLIP_NORM = 1.0
BETA_ONE = 0.5
BETA_TWO = 0.5
ADAM_EPSILON = 1e-08
MATRIX_RATE = 0.05
NORM_RATE = 0.5
MATRIX_DECAY = 0.01


def norm_stats(value):
    centre = value - jnp.mean(value, -1, keepdims=True)
    inverse = lax.rsqrt(jnp.mean(centre * centre, -1, keepdims=True) + EPSILON)
    return (centre * inverse, inverse)


def norm_back(normal, inverse, upstream):
    return inverse * (
        upstream
        - jnp.mean(upstream, -1, keepdims=True)
        - normal * jnp.mean(upstream * normal, -1, keepdims=True)
    )


def adam_update(weight, moment_one, moment_two, gradient, step_rate, decay_rate):
    first_new = BETA_ONE * moment_one + (1.0 - BETA_ONE) * gradient
    second_new = BETA_TWO * moment_two + (1.0 - BETA_TWO) * gradient * gradient
    first_hat = first_new / (1.0 - BETA_ONE**STEP)
    second_hat = second_new / (1.0 - BETA_TWO**STEP)
    weight_new = weight - step_rate * (
        first_hat / (jnp.sqrt(second_hat) + ADAM_EPSILON) + decay_rate * weight
    )
    return (first_new, second_new, weight_new)


def segments_of(lengths_row, length):
    ends = jnp.cumsum(lengths_row, dtype=jnp.int32)
    places = jnp.arange(length, dtype=jnp.int32)
    segment = jnp.sum((ends[None, :] <= places[:, None]).astype(jnp.int32), axis=1, dtype=jnp.int32)
    live = (places < ends[-1]).astype(jnp.float32)
    return segment, live


def matmul(left, right, dims):
    return lax.dot_general(left, right, (dims, ((), ())), preferred_element_type=jnp.float32)


NN = ((1,), (0,))
NT = ((1,), (1,))
TN = ((0,), (0,))


def attention_forward(stream, weight, mask):
    length, width = stream.shape
    size = width // HEADS
    packed = matmul(stream, weight[:, : 3 * width], NN).astype(jnp.bfloat16)
    heads = packed.reshape(length, 3, HEADS, size)
    scores = jnp.einsum("qhd,khd->hqk", heads[:, 0], heads[:, 1], preferred_element_type=jnp.float32)
    scores = jnp.where(mask[None], scores * size**-0.5, NEGATIVE)
    weights = jnp.exp(scores - jnp.max(scores, -1, keepdims=True))
    probs = weights / jnp.sum(weights, -1, keepdims=True)
    mixed = jnp.einsum("hqk,khd->qhd", probs.astype(jnp.bfloat16), heads[:, 2], preferred_element_type=jnp.float32)
    mixed = mixed.reshape(length, width).astype(jnp.bfloat16)
    branch = matmul(mixed, weight[:, 3 * width :], NN)
    return branch, (heads, probs, mixed)


def attention_backward(stream, weight, kept, grad_low):
    heads, probs, mixed = kept
    length, width = stream.shape
    size = width // HEADS
    grad_out = matmul(mixed, grad_low, TN)
    grad_mixed = matmul(grad_low, weight[:, 3 * width :], NT).astype(jnp.bfloat16)
    grad_mixed = grad_mixed.reshape(length, HEADS, size)
    grad_probs = jnp.einsum("qhd,khd->hqk", grad_mixed, heads[:, 2], preferred_element_type=jnp.float32)
    centre = jnp.sum(probs * grad_probs, -1, keepdims=True)
    grad_scores = (probs * (grad_probs - centre)).astype(jnp.bfloat16)
    low = probs.astype(jnp.bfloat16)
    scale = size**-0.5
    grad_q = jnp.einsum("hqk,khd->qhd", grad_scores, heads[:, 1], preferred_element_type=jnp.float32) * scale
    grad_k = jnp.einsum("hqk,qhd->khd", grad_scores, heads[:, 0], preferred_element_type=jnp.float32) * scale
    grad_v = jnp.einsum("hqk,qhd->khd", low, grad_mixed, preferred_element_type=jnp.float32)
    packed = jnp.concatenate([grad_q, grad_k, grad_v], axis=1).reshape(length, 3 * width)
    packed = packed.astype(jnp.bfloat16)
    grad_in = matmul(stream, packed, TN)
    grad_inputs = matmul(packed, weight[:, : 3 * width], NT)
    return grad_inputs, jnp.concatenate([grad_in, grad_out], axis=1)


def feed_forward(stream, weight, down):
    pre = matmul(stream, weight, NN)
    active = jax.nn.gelu(pre, approximate=True).astype(jnp.bfloat16)
    return matmul(active, down, NN), (pre, active)


def feed_backward(stream, weight, down, kept, grad_low):
    pre, active = kept
    grad_down = matmul(active, grad_low, TN)
    grad_active = matmul(grad_low, down, NT)
    pull = jax.vjp(lambda value: jax.nn.gelu(value, approximate=True), pre)[1]
    grad_pre = pull(grad_active)[0].astype(jnp.bfloat16)
    grad_up = matmul(stream, grad_pre, TN)
    return matmul(grad_pre, weight, NT), grad_up, grad_down


def micro_step(rows, pull, segment, mats, downs, gains, biases):
    low = jnp.bfloat16
    mask = segment[:, None] == segment[None, :]
    stream, dual = rows, jnp.zeros_like(rows)
    saved = []
    for sub in range(4):
        if sub % 2 == 0:
            branch, kept = attention_forward(stream, mats[sub], mask)
        else:
            branch, kept = feed_forward(stream, mats[sub], downs[sub // 2])
        normal, inverse = norm_stats(stream.astype(jnp.float32) + branch)
        out = normal * gains[sub] + biases[sub]
        total = dual.astype(jnp.float32) + branch
        saved.append((stream, kept, normal, inverse))
        if sub < 3:
            stream, dual = out.astype(low), total.astype(low)
    dual_normal, dual_inverse = norm_stats(total)
    output = (out + dual_normal).astype(low)
    grad_out, grad_dual = pull, norm_back(dual_normal, dual_inverse, pull)
    grads_a, grads_b, grads_n = [None] * 4, [None] * 2, [None] * 4
    for sub in (3, 2, 1, 0):
        stream, kept, normal, inverse = saved[sub]
        grads_n[sub] = jnp.stack([jnp.sum(grad_out * normal, 0), jnp.sum(grad_out, 0)], axis=1)
        summed = norm_back(normal, inverse, grad_out * gains[sub])
        branch_low = (summed + grad_dual).astype(low)
        if sub % 2 == 0:
            inner, grads_a[sub] = attention_backward(stream, mats[sub], kept, branch_low)
        else:
            inner, grads_a[sub], grads_b[sub // 2] = feed_backward(
                stream, mats[sub], downs[sub // 2], kept, branch_low
            )
        grad_in = summed + inner
        if sub > 0:
            grad_out = grad_in.astype(low).astype(jnp.float32)
            grad_dual = grad_dual.astype(low).astype(jnp.float32)
    return output, grad_in, jnp.stack(grads_a), jnp.stack(grads_b), jnp.stack(grads_n)


def finish_step(grad_norm, output, input_grad, *groups):
    factor = CLIP_NORM / jnp.maximum(grad_norm, CLIP_NORM)
    results = [grad_norm, output[None], input_grad[None]]
    for weight, one, two, grad, rate, decay in groups:
        clip = grad * factor
        moment, square_new, master = adam_update(weight, one, two, clip, rate, decay)
        results += [clip, moment, square_new, master, master.astype(jnp.bfloat16)]
    return tuple(results)


def body(
    tokens, cotangent, lengths, mat_a, mat_b, norms, first_a, second_a, first_b, second_b, first_n, second_n
):
    low = jnp.bfloat16
    own = lax.axis_index("section")
    length = tokens.shape[0] // lengths.shape[0]
    rows = lax.dynamic_slice_in_dim(tokens, own * length, length, 0)
    segment, live = segments_of(lax.dynamic_index_in_dim(lengths, own, 0, keepdims=False), length)
    pull = lax.dynamic_slice_in_dim(cotangent, own * length, length, 0).astype(jnp.float32) * live[:, None]

    def gathered(value):
        return lax.all_gather(lax.all_gather(value, "dp", axis=1, tiled=True), "section", axis=0, tiled=True)

    mats = gathered(mat_a.astype(low))
    scales = gathered(norms.astype(low)).astype(jnp.float32)
    downs = lax.all_gather(mat_b.astype(low), "section", axis=2, tiled=True)
    downs = lax.all_gather(downs, "dp", axis=1, tiled=True)
    output, input_grad, part_a, part_b, part_n = micro_step(
        rows, pull, segment, mats, downs, scales[:, :, 0], scales[:, :, 1]
    )

    def scattered(value, section_dim):
        value = lax.psum_scatter(value, "section", scatter_dimension=section_dim, tiled=True)
        return lax.psum_scatter(value, "dp", scatter_dimension=1, tiled=True).astype(jnp.float32)

    grad_a = scattered(part_a.astype(low), 0)
    grad_b = scattered(part_b.astype(low), 2)
    grad_n = scattered(part_n, 0)
    square = jnp.sum(grad_a * grad_a) + jnp.sum(grad_b * grad_b) + jnp.sum(grad_n * grad_n)
    grad_norm = jnp.sqrt(lax.psum(square, ("section", "dp")))
    return finish_step(
        grad_norm, output, input_grad,
        (mat_a, first_a, second_a, grad_a, MATRIX_RATE, MATRIX_DECAY),
        (mat_b, first_b, second_b, grad_b, MATRIX_RATE, MATRIX_DECAY),
        (norms, first_n, second_n, grad_n, NORM_RATE, 0.0),
    )


LOW = jnp.bfloat16
WIDE = jnp.float32
MESH = pl.DeviceIdType.MESH
SECTIONS = 4
LANES = 128
BLOCK = 64
KERNEL_VMEM = 64 * 1024 * 1024 - 256 * 1024


def gradient_items(rows_a, rows_b, cols_b, width, hidden):
    part = rows_a // SECTIONS
    return (
        ("B1", 3, cols_b // 2, rows_b),
        ("F3", 3, part, hidden // 2),
        ("O2", 2, part, width // 2),
        ("K2", 2, part, 3 * width // 2),
        ("B0", 1, cols_b // 2, rows_b),
        ("F1", 1, part, hidden // 2),
        ("O0", 0, part, width // 2),
        ("K0", 0, part, 3 * width // 2),
    )


def item_scratch(name, chips, rows, columns):
    piece = (rows, columns)
    return (
        ("own" + name, (chips, 2, SECTIONS, 2) + piece, LOW),
        ("sib" + name, (chips, SECTIONS, 2) + piece, LOW),
        ("farx" + name, (chips,) + piece, LOW),
        ("fary" + name, (chips,) + piece, LOW),
        ("nearx" + name, (2, chips) + piece, LOW),
        ("neary" + name, (2, chips) + piece, LOW),
        ("line" + name, (chips, 2) + piece, LOW),
        ("done" + name, (2,) + piece if name[0] == "B" else (SECTIONS, 2) + piece, WIDE if name[0] == "B" else LOW),
    )


def kernel_scratch(chips, rows_a, rows_b, cols_b, length, width, hidden):
    devices = 2 * chips
    items = gradient_items(rows_a, rows_b, cols_b, width, hidden)
    count = len(items)
    received = sum((item_scratch(name, chips, rows, columns) for name, _, rows, columns in items), ())
    return received + (
        ("sib_s", (count, SECTIONS), None),
        ("sib_r", (count, SECTIONS), None),
        ("px_s", (count, 3), None),
        ("px_r", (count, 3), None),
        ("py_s", (count, 3), None),
        ("py_r", (count, 3), None),
        ("line_s", (count, chips), None),
        ("line_r", (count, chips), None),
        ("done_s", (count,), None),
        ("done_r", (count, SECTIONS), None),
        ("wa", (4, width, hidden), LOW),
        ("wb", (2, hidden, width), LOW),
        ("tiles", (devices, SECTIONS, 8, LANES), WIDE),
        ("x", (4, length, width), LOW),
        ("xt", (4, width, length), LOW),
        ("y", (length, width), LOW),
        ("cot", (length, width), LOW),
        ("bias", (length, length), WIDE),
        ("live", (length, 1), WIDE),
        ("f", (length, width), WIDE),
        ("n", (4, length, width), WIDE),
        ("inv", (4, length, 1), WIDE),
        ("q", (2, length, width), LOW),
        ("k", (2, length, width), LOW),
        ("v", (2, length, width), LOW),
        ("kt", (2, width, length), LOW),
        ("vt", (2, width, length), LOW),
        ("ot", (2, width, length), LOW),
        ("pt", (2, HEADS, length, length), LOW),
        ("g", (2, length, hidden), LOW),
        ("slope", (2, length, hidden), LOW),
        ("gx", (length, width), WIDE),
        ("gy", (length, width), WIDE),
        ("df", (length, width), LOW),
        ("dft", (width, length), LOW),
        ("dm", (length, width), LOW),
        ("dqt", (width, length), LOW),
        ("dp", (length, hidden), LOW),
        ("ng", (devices, 8, width), WIDE),
        ("ns", (SECTIONS, 8, width), WIDE),
        ("sq", (devices, 8, LANES), WIDE),
        ("sqs", (SECTIONS, 8, LANES), WIDE),
        ("sum", (8, LANES), WIDE),
        ("in_s", (2,), None),
        ("gz_s", (3, 2, chips, 2), None),
        ("gz_r", (3, chips, 2), None),
        ("gx_s", (3, chips, 2), None),
        ("gx_r", (3, chips, 2), None),
        ("gy_s", (3, chips, 2), None),
        ("gy_r", (3, chips, 2), None),
        ("gxr_s", (3, chips), None),
        ("gxr_r", (3, chips), None),
        ("gyr_s", (3, chips), None),
        ("gyr_r", (3, chips), None),
        ("gs_s", (6,), None),
        ("gs_r", (6,), None),
        ("small_s", (3, 2), None),
        ("small_r", (3, 2), None),
    )


INPUTS = ("tokens", "cotangent", "lengths", "mat_a", "mat_b", "norms")
OUTPUTS = ("grad_a", "grad_b", "grad_n", "square", "output", "input_grad")


def step_kernel(names, *refs):
    r = types.SimpleNamespace(**dict(zip(names, refs)))
    width, hidden = r.wa.shape[1:]
    length = r.x.shape[1]
    rows_a, (rows_b, cols_b) = r.mat_a.shape[1], r.mat_b.shape[1:]
    devices = r.tiles.shape[0]
    chips = devices // 2
    half_a, half_b = rows_a // 2, cols_b // 2
    grad_items = gradient_items(rows_a, rows_b, cols_b, width, hidden)
    head = width // HEADS
    scale = head**-0.5

    s, d = lax.axis_index("section"), lax.axis_index("dp")
    z, c = lax.div(d, 2), lax.rem(d, 2)
    sx = s + 1 - 2 * lax.rem(s, 2)
    sy = lax.rem(s + 2, SECTIONS)
    sd = SECTIONS - 1 - s
    to_sibling = {"dp": d + 1 - 2 * c}
    to_up, to_down = {"dp": d + 2}, {"dp": d - 2}
    to_x, to_y = {"section": sx}, {"section": sy}
    below, above = z > 0, z < chips - 1
    group = [{"dp": lax.rem(d + step, devices)} for step in range(1, devices)]
    plane = [{"section": lax.rem(s + step, SECTIONS)} for step in range(1, SECTIONS)]
    finish = []

    def when(condition, work):
        if condition is None:
            work()
        else:
            pl.when(condition)(work)

    def push(source, target, send_sem, recv_sem, device):
        pltpu.make_async_remote_copy(
            src_ref=source,
            dst_ref=target,
            send_sem=send_sem,
            recv_sem=recv_sem,
            device_id=device,
            device_id_type=MESH,
        ).start()

    def arrived(target, sem):
        pltpu.make_async_remote_copy(
            src_ref=target, dst_ref=target, send_sem=sem, recv_sem=sem, device_id=to_x, device_id_type=MESH
        ).wait_recv()

    def sent(source, sem):
        pltpu.make_async_remote_copy(
            src_ref=source, dst_ref=source, send_sem=sem, recv_sem=sem, device_id=to_x, device_id_type=MESH
        ).wait_send()

    def at_end(condition, source, sem):
        finish.append((condition, source, sem))

    def aligned(start, size):
        return pl.ds(pl.multiple_of(start, size), size)

    own_x = pltpu.make_async_copy(r.tokens.at[aligned(s * length, length)], r.x.at[0], r.in_s.at[0])
    own_cot = pltpu.make_async_copy(r.cotangent.at[aligned(s * length, length)], r.cot, r.in_s.at[1])
    own_x.start()
    own_cot.start()
    barrier = pltpu.get_barrier_semaphore()
    for peer in group + plane:
        pl.semaphore_signal(barrier, inc=1, device_id=peer, device_id_type=MESH)
    r.wa[s, aligned(d * rows_a, rows_a), :] = r.mat_a[0].astype(LOW)
    for layer in range(2):
        r.wb[layer, aligned(d * rows_b, rows_b), aligned(s * cols_b, cols_b)] = r.mat_b[layer].astype(LOW)
    norms = r.norms[0].astype(LOW).astype(WIDE)
    nothing = jnp.zeros((2, rows_a), WIDE)
    even = jnp.concatenate([norms, nothing], axis=1)
    odd = jnp.concatenate([nothing, norms], axis=1)
    r.tiles[d, s, 0:2, :] = jnp.where(c == 0, even, odd)
    r.tiles[d, s, 2:8, :] = jnp.zeros((6, LANES), WIDE)
    pl.semaphore_wait(barrier, len(group) + len(plane))

    def small_out(which, source):
        for peer in group:
            push(source, source, r.small_s.at[which, 0], r.small_r.at[which, 0], peer)

    def small_group(which, like):
        arrived(like, r.small_r.at[which, 0])
        sent(like, r.small_s.at[which, 0])

    def small_plane_out(which, source):
        for peer in plane:
            push(source, source, r.small_s.at[which, 1], r.small_r.at[which, 1], peer)

    def small_plane(which, like):
        arrived(like, r.small_r.at[which, 1])
        sent(like, r.small_s.at[which, 1])

    def block_a(section, chip, half):
        return r.wa.at[section, aligned((2 * chip + c) * rows_a + half * half_a, half_a), :]

    def block_b(layer):
        part = rows_b // 2

        def block(section, chip, half):
            return r.wb.at[
                layer,
                aligned((2 * chip + c) * rows_b + half * part, part),
                aligned(section * cols_b, cols_b),
            ]

        return block

    items = (block_a, block_b(0), block_b(1))

    def to_the_sibling(item, section, chip, half):
        block = items[item](section, chip, half)
        slot = section if item == 0 else 3 + item
        push(block, block, r.gs_s.at[slot], r.gs_r.at[slot], to_sibling)

    def spread_plane(item, chip):
        for half in range(2):
            block = items[item](s, chip, half)
            push(block, block, r.gx_s.at[item, chip, half], r.gx_r.at[item, chip, half], to_x)
            push(block, block, r.gy_s.at[item, chip, half], r.gy_r.at[item, chip, half], to_y)
            to_the_sibling(item, s, chip, half)

    def up(item, chip, half):
        block = items[item](s, chip, half)
        push(block, block, r.gz_s.at[item, 0, chip, half], r.gz_r.at[item, chip, half], to_up)

    def down(item, chip, half):
        block = items[item](s, chip, half)
        push(block, block, r.gz_s.at[item, 1, chip, half], r.gz_r.at[item, chip, half], to_down)

    def start_line(item):
        for half in range(2):
            when(above, lambda: up(item, z, half))
            when(below, lambda: down(item, z, half))

    def line_step(item, step):
        def from_below():
            for half in range(2):
                arrived(items[item](s, z - step, half), r.gz_r.at[item, z - step, half])
                when(above, lambda: up(item, z - step, half))
            spread_plane(item, z - step)

        def from_above():
            for half in range(2):
                arrived(items[item](s, z + step, half), r.gz_r.at[item, z + step, half])
                when(below, lambda: down(item, z + step, half))
            spread_plane(item, z + step)

        when(z >= step, from_below)
        when(z + step < chips, from_above)

    def plane_step(item):
        for chip in range(chips):
            for half in range(2):
                arrived(items[item](sx, chip, half), r.gx_r.at[item, chip, half])
                if half == 1:
                    block = items[item](sx, chip, half)
                    push(block, block, r.gyr_s.at[item, chip], r.gyr_r.at[item, chip], to_y)
                to_the_sibling(item, sx, chip, half)
                arrived(items[item](sy, chip, half), r.gy_r.at[item, chip, half])
                if half == 0:
                    block = items[item](sy, chip, half)
                    push(block, block, r.gxr_s.at[item, chip], r.gxr_r.at[item, chip], to_x)
                to_the_sibling(item, sy, chip, half)

    def relay_step(item):
        for chip in range(chips):
            arrived(items[item](sd, chip, 0), r.gxr_r.at[item, chip])
            to_the_sibling(item, sd, chip, 0)
            arrived(items[item](sd, chip, 1), r.gyr_r.at[item, chip])
            to_the_sibling(item, sd, chip, 1)

    whole_a = r.wa.at[0, pl.ds(0, chips * rows_a)]
    whole_b = r.wb.at[0, pl.ds(0, chips * rows_b)]
    for slot in range(6):
        at_end(None, whole_a if slot < 4 else whole_b, r.gs_s.at[slot])
    for item in range(3):
        for chip in range(chips):
            for half in range(2):
                block = items[item](0, chip, half)
                at_end(None, block, r.gx_s.at[item, chip, half])
                at_end(None, block, r.gy_s.at[item, chip, half])
                at_end(above & (z >= chip), block, r.gz_s.at[item, 0, chip, half])
                at_end(below & (z <= chip), block, r.gz_s.at[item, 1, chip, half])
            block = items[item](0, chip, 0)
            at_end(None, block, r.gxr_s.at[item, chip])
            at_end(None, block, r.gyr_s.at[item, chip])

    def product(left, right, dims):
        return lax.dot_general(left, right, (dims, ((), ())), preferred_element_type=WIDE)

    def loop(count, work):
        def one(index, carry):
            work(index)
            return carry

        lax.fori_loop(0, count, one, 0)

    def gain_row(layer, kind):
        parts = [
            r.tiles[2 * chip, layer, kind : kind + 1, :] + r.tiles[2 * chip + 1, layer, kind : kind + 1, :]
            for chip in range(chips)
        ]
        return jnp.concatenate(parts, axis=1)

    def stats(value):
        centre = value - jnp.mean(value, -1, keepdims=True)
        inverse = lax.rsqrt(jnp.mean(centre * centre, -1, keepdims=True) + EPSILON)
        return centre * inverse, inverse

    lane = lax.broadcasted_iota(jnp.int32, (1, 2 * head), 1)
    first_half = (lane < head).astype(WIDE)
    half_masks = (first_half.astype(LOW), (1.0 - first_half).astype(LOW))

    def prepare_masks():
        ends, total = [], jnp.int32(0)
        for slot in range(r.lengths.shape[1]):
            total = total + r.lengths[s, slot]
            ends.append(total)
        down_places = lax.broadcasted_iota(jnp.int32, (length, 1), 0)
        across_places = lax.broadcasted_iota(jnp.int32, (1, length), 1)
        down_segment = jnp.zeros((length, 1), jnp.int32)
        across_segment = jnp.zeros((1, length), jnp.int32)
        for end in ends:
            down_segment = down_segment + (end <= down_places).astype(jnp.int32)
            across_segment = across_segment + (end <= across_places).astype(jnp.int32)
        r.bias[...] = jnp.where(down_segment == across_segment, 0.0, NEGATIVE)
        r.live[...] = (down_places < total).astype(WIDE)

    def attention(layer):
        at = layer // 2
        rows = r.x[layer]
        r.xt[layer] = rows.T
        r.q[at] = product(rows, r.wa[layer, :, 0:width], NN).astype(LOW) * jnp.asarray(scale, LOW)
        keys = product(rows, r.wa[layer, :, width : 2 * width], NN).astype(LOW)
        r.k[at] = keys
        r.kt[at] = (keys * jnp.asarray(scale, LOW)).T
        values = product(rows, r.wa[layer, :, 2 * width : 3 * width], NN).astype(LOW)
        r.v[at] = values
        r.vt[at] = values.T

        def pair(index):
            lanes = aligned(index * 2 * head, 2 * head)
            for which in range(2):
                scores = product(r.k[at, :, lanes], r.q[at, :, lanes] * half_masks[which], NT) + r.bias[...]
                weights = jnp.exp(scores - jnp.max(scores, 0, keepdims=True))
                probs = (weights * (1.0 / jnp.sum(weights, 0, keepdims=True))).astype(LOW)
                r.pt[at, 2 * index + which] = probs
                place = aligned((2 * index + which) * head, head)
                r.ot[at, place, :] = product(r.vt[at, place, :], probs, NN).astype(LOW)

        loop(HEADS // 2, pair)
        r.f[...] = product(r.ot[at].T, r.wa[layer, :, 3 * width :], NN)

    def expand(layer):
        at = layer // 2
        r.xt[layer] = r.x[layer].T

        def columns(index):
            place = aligned(index * width, width)
            pre = product(r.x[layer], r.wa[layer, :, place], NN)
            squared = pre * pre
            slope = 0.7978845608 * (1.0 + 3 * 0.044715 * squared)
            bent = jnp.tanh(0.7978845608 * pre * (1.0 + 0.044715 * squared))
            r.g[at, :, place] = (0.5 * pre * (1.0 + bent)).astype(LOW)
            r.slope[at, :, place] = (0.5 * (1.0 + bent) + 0.5 * pre * (1.0 - bent * bent) * slope).astype(LOW)

        loop(hidden // width, columns)

    def contract(layer):
        r.f[...] = product(r.g[layer // 2], r.wb[layer // 2], NN)

    def by_rows(work):
        loop(length // BLOCK, lambda index: work(aligned(index * BLOCK, BLOCK)))

    def normalize(layer):
        gain, offset = gain_row(layer, 0), gain_row(layer, 1)

        def some(rows):
            branch = r.f[rows, :]
            normal, inverse = stats(r.x[layer, rows, :].astype(WIDE) + branch)
            r.n[layer, rows, :] = normal
            r.inv[layer, rows, :] = inverse
            out = normal * gain + offset
            dual = branch if layer == 0 else r.y[rows, :].astype(WIDE) + branch
            if layer < 3:
                r.x[layer + 1, rows, :] = out.astype(LOW)
                r.y[rows, :] = dual.astype(LOW)
            else:
                dual_normal, dual_inverse = stats(dual)
                r.output[rows, :] = (out + dual_normal).astype(LOW)
                pull = r.cot[rows, :].astype(WIDE) * r.live[rows, :]
                r.gx[rows, :] = pull
                r.gy[rows, :] = norm_back(dual_normal, dual_inverse, pull)

        by_rows(some)

    def back_normalize(layer):
        gain = gain_row(layer, 0)

        def some(index, sums):
            rows = aligned(index * BLOCK, BLOCK)
            upstream = r.gx[rows, :]
            normal = r.n[layer, rows, :]
            summed = norm_back(normal, r.inv[layer, rows, :], upstream * gain)
            dual = r.gy[rows, :]
            r.gx[rows, :] = summed
            r.df[rows, :] = (summed + dual).astype(LOW)
            if layer == 3:
                r.gy[rows, :] = dual.astype(LOW).astype(WIDE)
            return (
                sums[0] + jnp.sum(upstream * normal, 0, keepdims=True),
                sums[1] + jnp.sum(upstream, 0, keepdims=True),
            )

        zero = jnp.zeros((1, width), WIDE)
        gains, offsets = lax.fori_loop(0, length // BLOCK, some, (zero, zero))
        r.ng[d, 2 * layer : 2 * layer + 1, :] = gains
        r.ng[d, 2 * layer + 1 : 2 * layer + 2, :] = offsets

    def pass_down(layer, inner):
        total = r.gx[...] + inner
        if layer > 0:
            r.gx[...] = total.astype(LOW).astype(WIDE)
        else:
            r.input_grad[...] = total

    def keep(name, half, place, value):
        own = getattr(r, "own" + name)
        own[:, :, :, half, :, place] = value.astype(LOW).reshape(
            chips, 2, SECTIONS, rows_a // SECTIONS, value.shape[1]
        )

    def back_contract(layer):
        own = getattr(r, "ownB%d" % (layer // 2))
        r.dft[...] = r.df[...].T

        def owner(index):
            value = product(r.dft[...], r.g[layer // 2, :, aligned(index * rows_b, rows_b)], NN)
            own[lax.div(index, 2), lax.rem(index, 2)] = value.astype(LOW).reshape(SECTIONS, 2, half_b, rows_b)

        loop(devices, owner)

    def back_expand(layer):
        at = layer // 2

        def columns(index):
            place = aligned(index * width, width)
            pulled = product(r.df[...], r.wb[at, place, :], NT)
            pulled = (pulled * r.slope[at, :, place].astype(WIDE)).astype(LOW)
            r.dp[:, place] = pulled
            inner = aligned(lax.rem(index, 2) * width, width)
            keep("F%d" % layer, lax.div(index, 2), inner, product(r.xt[layer], pulled, NN))

        loop(hidden // width, columns)

    def back_expand_end(layer):
        pass_down(layer, product(r.dp[...], r.wa[layer], NT))

    def back_output(layer):
        at = layer // 2
        for half in range(2):
            place = pl.ds(half * width // 2, width // 2)
            keep("O%d" % layer, half, pl.ds(0, width // 2), product(r.ot[at], r.df[:, place], NN))
        r.dm[...] = product(r.df[...], r.wa[layer, :, 3 * width :], NT).astype(LOW)

    def back_heads(layer, begin, count):
        at = layer // 2

        def pair(step):
            index = begin + step
            lanes = aligned(index * 2 * head, 2 * head)
            pulled = r.dm[:, lanes]
            keys, values = [], []
            for which in range(2):
                probs = r.pt[at, 2 * index + which]
                grad = product(r.v[at, :, lanes], pulled * half_masks[which], NT)
                full = probs.astype(WIDE)
                centre = jnp.sum(full * grad, 0, keepdims=True)
                scores = (full * (grad - centre)).astype(LOW)
                keys.append(product(scores, r.q[at, :, lanes], NN))
                values.append(product(probs, pulled, NN))
                place = aligned((2 * index + which) * head, head)
                r.dqt[place, :] = product(r.kt[at, place, :], scores, NN).astype(LOW)
            r.dp[:, aligned(width + index * 2 * head, 2 * head)] = jnp.where(
                lane < head, keys[0], keys[1]
            ).astype(LOW)
            r.dp[:, aligned(2 * width + index * 2 * head, 2 * head)] = jnp.where(
                lane < head, values[0], values[1]
            ).astype(LOW)

        loop(count, pair)

    def back_packed(layer):
        r.dp[:, 0:width] = r.dqt[...].T
        part = 3 * width // 2
        for half in range(2):
            value = product(r.xt[layer], r.dp[:, half * part : (half + 1) * part], NN)
            keep("K%d" % layer, half, pl.ds(0, part), value)

    def back_packed_end(layer):
        pass_down(layer, product(r.dp[:, 0 : 3 * width], r.wa[layer, :, 0 : 3 * width], NT))

    def joined(target, others):
        return functools.reduce(
            lambda left, right: left + right, [ref[...].astype(WIDE) for ref in (target, *others)]
        )

    def add_into(target, others):
        target[...] = joined(target, others).astype(LOW)

    places = {name: place for place, (name, _, _, _) in enumerate(grad_items)}
    by_turn = (sd, sx, sy, s)

    def buffers(name):
        parts = ("own", "sib", "farx", "fary", "nearx", "neary", "line", "done")
        return types.SimpleNamespace(**{part: getattr(r, part + name) for part in parts})

    def to_core(name):
        item, place = buffers(name), places[name]
        for turn, section in enumerate(by_turn):
            push(
                item.own.at[:, 1 - c, section],
                item.sib.at[:, section],
                r.sib_s.at[place, turn],
                r.sib_r.at[place, turn],
                to_sibling,
            )
            at_end(None, item.sib.at[:, 0], r.sib_s.at[place, turn])

    def to_plane(name):
        item, place = buffers(name), places[name]
        own = item.own.at[:, c]

        def over_x(section, half, target, slot):
            push(own.at[:, section, half], target, r.px_s.at[place, slot], r.px_r.at[place, slot], to_x)
            at_end(None, item.farx, r.px_s.at[place, slot])

        def over_y(section, half, target, slot):
            push(own.at[:, section, half], target, r.py_s.at[place, slot], r.py_r.at[place, slot], to_y)
            at_end(None, item.farx, r.py_s.at[place, slot])

        for turn, section in enumerate(by_turn):
            arrived(item.sib.at[:, section], r.sib_r.at[place, turn])
            add_into(own.at[:, section], [item.sib.at[:, section]])
            if turn == 0:
                over_x(sd, 0, item.farx, 2)
                over_y(sd, 1, item.fary, 2)
            elif turn == 1:
                over_x(sx, 0, item.nearx.at[0], 0)
            elif turn == 2:
                over_y(sy, 1, item.neary.at[1], 1)

    def through_plane(name):
        item, place = buffers(name), places[name]
        own = item.own.at[:, c]
        arrived(item.fary, r.py_r.at[place, 2])
        add_into(own.at[:, sx, 1], [item.fary])
        push(own.at[:, sx, 1], item.nearx.at[1], r.px_s.at[place, 1], r.px_r.at[place, 1], to_x)
        at_end(None, item.farx, r.px_s.at[place, 1])
        arrived(item.farx, r.px_r.at[place, 2])
        add_into(own.at[:, sy, 0], [item.farx])
        push(own.at[:, sy, 0], item.neary.at[0], r.py_s.at[place, 0], r.py_r.at[place, 0], to_y)
        at_end(None, item.farx, r.py_s.at[place, 0])

    def to_line(name):
        item, place = buffers(name), places[name]
        own = item.own.at[:, c, s]
        for half in range(2):
            arrived(item.nearx.at[half], r.px_r.at[place, half])
            arrived(item.neary.at[half], r.py_r.at[place, half])
            add_into(own.at[:, half], [item.nearx.at[half], item.neary.at[half]])
        for step in range(1, chips):
            chip = lax.rem(z + step, chips)
            push(
                own.at[chip],
                item.line.at[z],
                r.line_s.at[place, step],
                r.line_r.at[place, z],
                {"dp": 2 * chip + c},
            )
            at_end(None, item.line.at[0], r.line_s.at[place, step])

    def to_owner(name):
        item, place = buffers(name), places[name]
        others = [lax.rem(z + step, chips) for step in range(1, chips)]
        for chip in others:
            arrived(item.line.at[chip], r.line_r.at[place, chip])
        total = joined(item.own.at[z, c, s], [item.line.at[chip] for chip in others])
        square = total * total
        while square.ndim > 2:
            square = jnp.sum(square, 0)
        square = jnp.sum(jnp.sum(square, 0, keepdims=True), 1, keepdims=True)
        r.sum[...] = r.sum[...] + jnp.broadcast_to(square, (8, LANES))
        if name[0] == "B":
            item.done[...] = total
            return
        item.done[s] = total.astype(LOW)
        layer = grad_items[place][1]
        mine = item.done.at[s]
        away = s != layer
        when(
            away,
            lambda: push(mine, mine, r.done_s.at[place], r.done_r.at[place, s], {"section": jnp.int32(layer)}),
        )
        at_end(away, mine, r.done_s.at[place])

    def collect(name):
        item, place = buffers(name), places[name]
        layer = grad_items[place][1]

        def work():
            for section in range(SECTIONS):
                if section != layer:
                    arrived(item.done.at[section], r.done_r.at[place, section])
            columns = item.done.shape[-1]
            start = 3 * width if name[0] == "O" else 0
            for section in range(SECTIONS):
                for half in range(2):
                    rows = pl.ds(section * (rows_a // SECTIONS), rows_a // SECTIONS)
                    place_to = pl.ds(start + half * columns, columns)
                    r.grad_a[rows, place_to] = item.done[section, half].astype(WIDE)

        when(s == layer, work)

    def all_sent():
        for condition, source, sem in finish:
            when(condition, functools.partial(sent, source, sem))
        finish.clear()

    small_out(0, r.tiles.at[d, s])
    start_line(0)
    spread_plane(0, z)
    line_step(0, 1)
    start_line(1)
    start_line(2)
    for step in range(2, chips):
        line_step(0, step)
    small_group(0, r.tiles.at[pl.ds(0, devices - 1), 0])
    for peer in plane:
        push(r.tiles.at[:, s], r.tiles.at[:, s], r.small_s.at[0, 1], r.small_r.at[0, 1], peer)
    prepare_masks()
    plane_step(0)
    for item in (1, 2):
        spread_plane(item, z)
        for step in range(1, chips):
            line_step(item, step)
    own_x.wait()
    own_cot.wait()
    relay_step(0)
    small_plane(0, r.tiles.at[:, pl.ds(0, SECTIONS - 1)])
    for slot in range(4):
        arrived(whole_a, r.gs_r.at[slot])
    attention(0)
    normalize(0)
    expand(1)
    plane_step(1)
    relay_step(1)
    arrived(whole_b, r.gs_r.at[4])
    contract(1)
    normalize(1)
    plane_step(2)
    attention(2)
    normalize(2)
    expand(3)
    relay_step(2)
    arrived(whole_b, r.gs_r.at[5])
    contract(3)
    normalize(3)

    r.sum[...] = jnp.zeros((8, LANES), WIDE)
    back_normalize(3)
    back_contract(3)
    to_core("B1")
    back_expand(3)
    to_core("F3")
    to_plane("B1")
    back_expand_end(3)
    back_normalize(2)
    back_output(2)
    to_core("O2")
    to_plane("F3")
    back_heads(2, 0, 2)
    through_plane("B1")
    to_plane("O2")
    back_heads(2, 2, 2)
    through_plane("F3")
    to_line("B1")
    back_packed(2)
    to_core("K2")
    through_plane("O2")
    back_packed_end(2)
    to_line("F3")
    back_normalize(1)
    to_plane("K2")
    to_owner("B1")
    back_contract(1)
    to_core("B0")
    to_line("O2")
    back_expand(1)
    to_core("F1")
    through_plane("K2")
    to_plane("B0")
    to_owner("F3")
    back_expand_end(1)
    back_normalize(0)
    back_output(0)
    to_core("O0")
    to_plane("F1")
    to_owner("O2")
    to_line("K2")
    back_heads(0, 0, 2)
    through_plane("B0")
    to_plane("O0")
    back_heads(0, 2, 2)
    through_plane("F1")
    to_line("B0")
    to_owner("K2")
    back_packed(0)
    to_core("K0")
    small_out(1, r.ng.at[d])
    through_plane("O0")
    to_line("F1")
    back_packed_end(0)
    to_plane("K0")
    to_owner("B0")
    to_line("O0")
    all_sent()
    through_plane("K0")
    to_owner("F1")
    to_owner("O0")
    small_group(1, r.ng.at[pl.ds(0, devices - 1)])
    r.ns[s] = functools.reduce(lambda left, right: left + right, [r.ng[index] for index in range(devices)])
    small_plane_out(1, r.ns.at[s])
    for name in ("F3", "O2", "K2", "F1"):
        collect(name)
    to_line("K0")
    collect("O0")
    for layer in range(2):
        done = buffers("B%d" % layer).done
        r.grad_b[layer] = done[...].reshape(cols_b, rows_b).T
    small_plane(1, r.ns.at[pl.ds(0, SECTIONS - 1)])
    grads = functools.reduce(lambda left, right: left + right, [r.ns[index] for index in range(SECTIONS)])
    norm_square = jnp.sum(jnp.sum(grads * grads, 0, keepdims=True), 1, keepdims=True)
    chosen = jnp.zeros((2, width), WIDE)
    for layer in range(4):
        chosen = jnp.where(s == layer, grads[2 * layer : 2 * layer + 2, :], chosen)
    for chip in range(chips):
        pair_of = chosen[:, chip * LANES : (chip + 1) * LANES]
        r.grad_n[...] = jnp.where(
            z == chip, jnp.where(c == 0, pair_of[:, :rows_a], pair_of[:, rows_a:]), r.grad_n[...]
        )
    to_owner("K0")

    r.sq[d] = r.sum[...]
    small_out(2, r.sq.at[d])
    collect("K0")
    small_group(2, r.sq.at[pl.ds(0, devices - 1)])
    r.sqs[s] = functools.reduce(lambda left, right: left + right, [r.sq[index] for index in range(devices)])
    small_plane_out(2, r.sqs.at[s])
    all_sent()
    small_plane(2, r.sqs.at[pl.ds(0, SECTIONS - 1)])
    squares = functools.reduce(lambda left, right: left + right, [r.sqs[index] for index in range(SECTIONS)])
    r.square[...] = squares + norm_square


def step_call(tokens, cotangent, lengths, mat_a, mat_b, norms):
    rows_a, hidden = mat_a.shape[1:]
    rows_b, cols_b = mat_b.shape[1:]
    width = tokens.shape[1]
    length = tokens.shape[0] // lengths.shape[0]
    chips = width // rows_a // 2
    scratch = kernel_scratch(chips, rows_a, rows_b, cols_b, length, width, hidden)
    shapes = []
    for _, shape, kind in scratch:
        shapes.append(pltpu.SemaphoreType.DMA(shape) if kind is None else pltpu.VMEM(shape, kind))
    anywhere, vmem = pl.BlockSpec(memory_space=pl.ANY), pl.BlockSpec(memory_space=pltpu.VMEM)
    return pl.pallas_call(
        functools.partial(step_kernel, INPUTS + OUTPUTS + tuple(name for name, _, _ in scratch)),
        out_shape=(
            jax.ShapeDtypeStruct((rows_a, hidden), WIDE),
            jax.ShapeDtypeStruct(mat_b.shape, WIDE),
            jax.ShapeDtypeStruct((2, rows_a), WIDE),
            jax.ShapeDtypeStruct((8, LANES), WIDE),
            jax.ShapeDtypeStruct((length, width), LOW),
            jax.ShapeDtypeStruct((length, width), WIDE),
        ),
        in_specs=[anywhere, anywhere, pl.BlockSpec(memory_space=pltpu.SMEM), vmem, vmem, vmem],
        out_specs=[vmem] * len(OUTPUTS),
        scratch_shapes=shapes,
        compiler_params=pltpu.CompilerParams(
            collective_id=0, has_side_effects=True, vmem_limit_bytes=KERNEL_VMEM
        ),
    )(tokens, cotangent, lengths, mat_a, mat_b, norms)


def update_kernel(*refs):
    square, output, input_grad = (ref[...] for ref in refs[:3])
    grad_norm = jnp.sqrt(square[0:1, 0:1])
    factor = CLIP_NORM / jnp.maximum(grad_norm, CLIP_NORM)
    inputs, outputs = refs[3:15], refs[15:]
    outputs[0][...] = grad_norm
    outputs[1][0] = output
    outputs[2][0] = input_grad
    for group, (rate, decay) in enumerate(
        ((MATRIX_RATE, MATRIX_DECAY), (MATRIX_RATE, MATRIX_DECAY), (NORM_RATE, 0.0))
    ):
        grad, weight, one, two = inputs[4 * group : 4 * group + 4]
        clip = grad[...].reshape(weight.shape) * factor
        moment, square_new, master = adam_update(weight[...], one[...], two[...], clip, rate, decay)
        for ref, value in zip(
            outputs[3 + 5 * group : 8 + 5 * group], (clip, moment, square_new, master, master.astype(LOW))
        ):
            ref[...] = value


def kernel_body(
    tokens, cotangent, lengths, mat_a, mat_b, norms, first_a, second_a, first_b, second_b, first_n, second_n
):
    norms, first_n, second_n = (jnp.swapaxes(value, 1, 2) for value in (norms, first_n, second_n))
    grad_a, grad_b, grad_n, square, output, input_grad = step_call(
        tokens, cotangent, lengths, mat_a, mat_b, norms
    )
    steps = 4

    def cut(value, dim):
        shape = tuple(size // steps if at == dim else size for at, size in enumerate(value.shape))
        return pl.BlockSpec(shape, lambda step: tuple(step if at == dim else 0 for at in range(len(shape))))

    def whole(value):
        return pl.BlockSpec(value.shape, lambda step: (0,) * len(value.shape))

    def like(value, kind=WIDE):
        return jax.ShapeDtypeStruct(value.shape, kind)

    args = (square, output, input_grad, grad_a, mat_a, first_a, second_a, grad_b, mat_b, first_b, second_b)
    specs = [whole(square), cut(output, 0), cut(input_grad, 0)]
    specs += [cut(grad_a, 0)] + [cut(mat_a, 1)] * 3 + [cut(grad_b, 1)] * 4
    args += (grad_n, norms, first_n, second_n)
    specs += [whole(grad_n)] + [whole(norms)] * 3
    shapes = [jax.ShapeDtypeStruct((1, 1), WIDE), like(output[None], LOW), like(input_grad[None])]
    out_specs = [whole(shapes[0]), cut(shapes[1], 1), cut(shapes[2], 1)]
    for value, spec in ((mat_a, cut(mat_a, 1)), (mat_b, cut(mat_b, 1)), (norms, whole(norms))):
        shapes += [like(value)] * 4 + [like(value, LOW)]
        out_specs += [spec] * 5
    results = pl.pallas_call(
        update_kernel,
        grid=(steps,),
        out_shape=shapes,
        in_specs=specs,
        out_specs=out_specs,
        compiler_params=pltpu.CompilerParams(vmem_limit_bytes=KERNEL_VMEM),
    )(*args)
    results = [results[0][0, 0], *results[1:]]
    results[-5:] = [jnp.swapaxes(value, 1, 2) for value in results[-5:]]
    return tuple(results)


def chosen_body(*args):
    rows_a = args[3].shape[1]
    groups = lax.axis_size("dp")
    by_kernel = rows_a % 32 == 0 and 2 * rows_a == LANES and groups * rows_a == args[0].shape[1]
    return (kernel_body if by_kernel else body)(*args)


def solution(mesh):
    placed = (
        P("dp", None),
        P("dp", None),
        P("dp", None),
        P("section", "dp", None),
        P(None, "dp", "section"),
        P("section", "dp", None),
        P("section", "dp", None),
        P("section", "dp", None),
        P(None, "dp", "section"),
        P(None, "dp", "section"),
        P("section", "dp", None),
        P("section", "dp", None),
    )
    return jax.shard_map(
        chosen_body,
        mesh=mesh,
        in_specs=placed,
        out_specs=(
            P(),
            P("section", "dp", None),
            P("section", "dp", None),
            P("section", "dp", None),
            P("section", "dp", None),
            P("section", "dp", None),
            P("section", "dp", None),
            P("section", "dp", None),
            P(None, "dp", "section"),
            P(None, "dp", "section"),
            P(None, "dp", "section"),
            P(None, "dp", "section"),
            P(None, "dp", "section"),
            P("section", "dp", None),
            P("section", "dp", None),
            P("section", "dp", None),
            P("section", "dp", None),
            P("section", "dp", None),
        ),
        check_vma=False,
    )
```

```python
import functools
import types

import jax
import jax.numpy as jnp
from jax import lax
from jax.experimental import pallas as pl
from jax.experimental.pallas import tpu as pltpu
from jax.sharding import PartitionSpec as P

HEADS = 8
STEP = 5


EPSILON = 1e-05
NEGATIVE = -1e30
CLIP_NORM = 1.0
BETA_ONE = 0.5
BETA_TWO = 0.5
ADAM_EPSILON = 1e-08
MATRIX_RATE = 0.05
NORM_RATE = 0.5
MATRIX_DECAY = 0.01


def norm_stats(value):
    centre = value - jnp.mean(value, -1, keepdims=True)
    inverse = lax.rsqrt(jnp.mean(centre * centre, -1, keepdims=True) + EPSILON)
    return (centre * inverse, inverse)


def norm_back(normal, inverse, upstream):
    return inverse * (
        upstream
        - jnp.mean(upstream, -1, keepdims=True)
        - normal * jnp.mean(upstream * normal, -1, keepdims=True)
    )


def adam_update(weight, moment_one, moment_two, gradient, step_rate, decay_rate):
    first_new = BETA_ONE * moment_one + (1.0 - BETA_ONE) * gradient
    second_new = BETA_TWO * moment_two + (1.0 - BETA_TWO) * gradient * gradient
    first_hat = first_new / (1.0 - BETA_ONE**STEP)
    second_hat = second_new / (1.0 - BETA_TWO**STEP)
    weight_new = weight - step_rate * (
        first_hat / (jnp.sqrt(second_hat) + ADAM_EPSILON) + decay_rate * weight
    )
    return (first_new, second_new, weight_new)


def segments_of(lengths_row, length):
    ends = jnp.cumsum(lengths_row, dtype=jnp.int32)
    places = jnp.arange(length, dtype=jnp.int32)
    segment = jnp.sum((ends[None, :] <= places[:, None]).astype(jnp.int32), axis=1, dtype=jnp.int32)
    live = (places < ends[-1]).astype(jnp.float32)
    return segment, live


def matmul(left, right, dims):
    return lax.dot_general(left, right, (dims, ((), ())), preferred_element_type=jnp.float32)


NN = ((1,), (0,))
NT = ((1,), (1,))
TN = ((0,), (0,))


def attention_forward(stream, weight, mask):
    length, width = stream.shape
    size = width // HEADS
    packed = matmul(stream, weight[:, : 3 * width], NN).astype(jnp.bfloat16)
    heads = packed.reshape(length, 3, HEADS, size)
    scores = jnp.einsum("qhd,khd->hqk", heads[:, 0], heads[:, 1], preferred_element_type=jnp.float32)
    scores = jnp.where(mask[None], scores * size**-0.5, NEGATIVE)
    weights = jnp.exp(scores - jnp.max(scores, -1, keepdims=True))
    probs = weights / jnp.sum(weights, -1, keepdims=True)
    mixed = jnp.einsum("hqk,khd->qhd", probs.astype(jnp.bfloat16), heads[:, 2], preferred_element_type=jnp.float32)
    mixed = mixed.reshape(length, width).astype(jnp.bfloat16)
    branch = matmul(mixed, weight[:, 3 * width :], NN)
    return branch, (heads, probs, mixed)


def attention_backward(stream, weight, kept, grad_low):
    heads, probs, mixed = kept
    length, width = stream.shape
    size = width // HEADS
    grad_out = matmul(mixed, grad_low, TN)
    grad_mixed = matmul(grad_low, weight[:, 3 * width :], NT).astype(jnp.bfloat16)
    grad_mixed = grad_mixed.reshape(length, HEADS, size)
    grad_probs = jnp.einsum("qhd,khd->hqk", grad_mixed, heads[:, 2], preferred_element_type=jnp.float32)
    centre = jnp.sum(probs * grad_probs, -1, keepdims=True)
    grad_scores = (probs * (grad_probs - centre)).astype(jnp.bfloat16)
    low = probs.astype(jnp.bfloat16)
    scale = size**-0.5
    grad_q = jnp.einsum("hqk,khd->qhd", grad_scores, heads[:, 1], preferred_element_type=jnp.float32) * scale
    grad_k = jnp.einsum("hqk,qhd->khd", grad_scores, heads[:, 0], preferred_element_type=jnp.float32) * scale
    grad_v = jnp.einsum("hqk,qhd->khd", low, grad_mixed, preferred_element_type=jnp.float32)
    packed = jnp.concatenate([grad_q, grad_k, grad_v], axis=1).reshape(length, 3 * width)
    packed = packed.astype(jnp.bfloat16)
    grad_in = matmul(stream, packed, TN)
    grad_inputs = matmul(packed, weight[:, : 3 * width], NT)
    return grad_inputs, jnp.concatenate([grad_in, grad_out], axis=1)


def feed_forward(stream, weight, down):
    pre = matmul(stream, weight, NN)
    active = jax.nn.gelu(pre, approximate=True).astype(jnp.bfloat16)
    return matmul(active, down, NN), (pre, active)


def feed_backward(stream, weight, down, kept, grad_low):
    pre, active = kept
    grad_down = matmul(active, grad_low, TN)
    grad_active = matmul(grad_low, down, NT)
    pull = jax.vjp(lambda value: jax.nn.gelu(value, approximate=True), pre)[1]
    grad_pre = pull(grad_active)[0].astype(jnp.bfloat16)
    grad_up = matmul(stream, grad_pre, TN)
    return matmul(grad_pre, weight, NT), grad_up, grad_down


def micro_step(rows, pull, segment, mats, downs, gains, biases):
    low = jnp.bfloat16
    mask = segment[:, None] == segment[None, :]
    stream, dual = rows, jnp.zeros_like(rows)
    saved = []
    for sub in range(4):
        if sub % 2 == 0:
            branch, kept = attention_forward(stream, mats[sub], mask)
        else:
            branch, kept = feed_forward(stream, mats[sub], downs[sub // 2])
        normal, inverse = norm_stats(stream.astype(jnp.float32) + branch)
        out = normal * gains[sub] + biases[sub]
        total = dual.astype(jnp.float32) + branch
        saved.append((stream, kept, normal, inverse))
        if sub < 3:
            stream, dual = out.astype(low), total.astype(low)
    dual_normal, dual_inverse = norm_stats(total)
    output = (out + dual_normal).astype(low)
    grad_out, grad_dual = pull, norm_back(dual_normal, dual_inverse, pull)
    grads_a, grads_b, grads_n = [None] * 4, [None] * 2, [None] * 4
    for sub in (3, 2, 1, 0):
        stream, kept, normal, inverse = saved[sub]
        grads_n[sub] = jnp.stack([jnp.sum(grad_out * normal, 0), jnp.sum(grad_out, 0)], axis=1)
        summed = norm_back(normal, inverse, grad_out * gains[sub])
        branch_low = (summed + grad_dual).astype(low)
        if sub % 2 == 0:
            inner, grads_a[sub] = attention_backward(stream, mats[sub], kept, branch_low)
        else:
            inner, grads_a[sub], grads_b[sub // 2] = feed_backward(
                stream, mats[sub], downs[sub // 2], kept, branch_low
            )
        grad_in = summed + inner
        if sub > 0:
            grad_out = grad_in.astype(low).astype(jnp.float32)
            grad_dual = grad_dual.astype(low).astype(jnp.float32)
    return output, grad_in, jnp.stack(grads_a), jnp.stack(grads_b), jnp.stack(grads_n)


def finish_step(grad_norm, output, input_grad, *groups):
    factor = CLIP_NORM / jnp.maximum(grad_norm, CLIP_NORM)
    results = [grad_norm, output[None], input_grad[None]]
    for weight, one, two, grad, rate, decay in groups:
        clip = grad * factor
        moment, square_new, master = adam_update(weight, one, two, clip, rate, decay)
        results += [clip, moment, square_new, master, master.astype(jnp.bfloat16)]
    return tuple(results)


def body(
    tokens, cotangent, lengths, mat_a, mat_b, norms, first_a, second_a, first_b, second_b, first_n, second_n
):
    low = jnp.bfloat16
    own = lax.axis_index("section")
    length = tokens.shape[0] // lengths.shape[0]
    rows = lax.dynamic_slice_in_dim(tokens, own * length, length, 0)
    segment, live = segments_of(lax.dynamic_index_in_dim(lengths, own, 0, keepdims=False), length)
    pull = lax.dynamic_slice_in_dim(cotangent, own * length, length, 0).astype(jnp.float32) * live[:, None]

    def gathered(value):
        return lax.all_gather(lax.all_gather(value, "dp", axis=1, tiled=True), "section", axis=0, tiled=True)

    mats = gathered(mat_a.astype(low))
    scales = gathered(norms.astype(low)).astype(jnp.float32)
    downs = lax.all_gather(mat_b.astype(low), "section", axis=2, tiled=True)
    downs = lax.all_gather(downs, "dp", axis=1, tiled=True)
    output, input_grad, part_a, part_b, part_n = micro_step(
        rows, pull, segment, mats, downs, scales[:, :, 0], scales[:, :, 1]
    )

    def scattered(value, section_dim):
        value = lax.psum_scatter(value, "section", scatter_dimension=section_dim, tiled=True)
        return lax.psum_scatter(value, "dp", scatter_dimension=1, tiled=True).astype(jnp.float32)

    grad_a = scattered(part_a.astype(low), 0)
    grad_b = scattered(part_b.astype(low), 2)
    grad_n = scattered(part_n, 0)
    square = jnp.sum(grad_a * grad_a) + jnp.sum(grad_b * grad_b) + jnp.sum(grad_n * grad_n)
    grad_norm = jnp.sqrt(lax.psum(square, ("section", "dp")))
    return finish_step(
        grad_norm, output, input_grad,
        (mat_a, first_a, second_a, grad_a, MATRIX_RATE, MATRIX_DECAY),
        (mat_b, first_b, second_b, grad_b, MATRIX_RATE, MATRIX_DECAY),
        (norms, first_n, second_n, grad_n, NORM_RATE, 0.0),
    )


LOW = jnp.bfloat16
WIDE = jnp.float32
MESH = pl.DeviceIdType.MESH
SECTIONS = 4
LANES = 128
BLOCK = 64
KERNEL_VMEM = 64 * 1024 * 1024 - 256 * 1024


def gradient_items(rows_a, rows_b, cols_b, width, hidden):
    part = rows_a // SECTIONS
    return (
        ("B1", 3, cols_b // 2, rows_b),
        ("F3", 3, part, hidden // 2),
        ("O2", 2, part, width // 2),
        ("K2", 2, part, 3 * width // 2),
        ("B0", 1, cols_b // 2, rows_b),
        ("F1", 1, part, hidden // 2),
        ("O0", 0, part, width // 2),
        ("K0", 0, part, 3 * width // 2),
    )


def item_scratch(name, chips, rows, columns):
    piece = (rows, columns)
    return (
        ("own" + name, (chips, 2, SECTIONS, 2) + piece, LOW),
        ("sib" + name, (chips, SECTIONS, 2) + piece, LOW),
        ("farx" + name, (chips,) + piece, LOW),
        ("fary" + name, (chips,) + piece, LOW),
        ("nearx" + name, (2, chips) + piece, LOW),
        ("neary" + name, (2, chips) + piece, LOW),
        ("line" + name, (chips, 2) + piece, LOW),
        ("done" + name, (2,) + piece if name[0] == "B" else (SECTIONS, 2) + piece, WIDE if name[0] == "B" else LOW),
    )


def kernel_scratch(chips, rows_a, rows_b, cols_b, length, width, hidden):
    devices = 2 * chips
    items = gradient_items(rows_a, rows_b, cols_b, width, hidden)
    count = len(items)
    received = sum((item_scratch(name, chips, rows, columns) for name, _, rows, columns in items), ())
    return received + (
        ("sib_s", (count, SECTIONS), None),
        ("sib_r", (count, SECTIONS), None),
        ("px_s", (count, 3), None),
        ("px_r", (count, 3), None),
        ("py_s", (count, 3), None),
        ("py_r", (count, 3), None),
        ("line_s", (count, chips), None),
        ("line_r", (count, chips), None),
        ("done_s", (count,), None),
        ("done_r", (count, SECTIONS), None),
        ("wa", (4, width, hidden), LOW),
        ("wb", (2, hidden, width), LOW),
        ("tiles", (devices, SECTIONS, 8, LANES), WIDE),
        ("x", (4, length, width), LOW),
        ("xt", (4, width, length), LOW),
        ("y", (length, width), LOW),
        ("cot", (length, width), LOW),
        ("bias", (length, length), WIDE),
        ("live", (length, 1), WIDE),
        ("f", (length, width), WIDE),
        ("n", (4, length, width), WIDE),
        ("inv", (4, length, 1), WIDE),
        ("q", (2, length, width), LOW),
        ("k", (2, length, width), LOW),
        ("v", (2, length, width), LOW),
        ("kt", (2, width, length), LOW),
        ("vt", (2, width, length), LOW),
        ("ot", (2, width, length), LOW),
        ("pt", (2, HEADS, length, length), LOW),
        ("g", (2, length, hidden), LOW),
        ("slope", (2, length, hidden), LOW),
        ("gx", (length, width), WIDE),
        ("gy", (length, width), WIDE),
        ("df", (length, width), LOW),
        ("dft", (width, length), LOW),
        ("dm", (length, width), LOW),
        ("dqt", (width, length), LOW),
        ("dp", (length, hidden), LOW),
        ("ng", (devices, 8, width), WIDE),
        ("ns", (SECTIONS, 8, width), WIDE),
        ("sq", (devices, 8, LANES), WIDE),
        ("sqs", (SECTIONS, 8, LANES), WIDE),
        ("sum", (8, LANES), WIDE),
        ("in_s", (2,), None),
        ("gz_s", (3, 2, chips, 2), None),
        ("gz_r", (3, chips, 2), None),
        ("gx_s", (3, chips, 2), None),
        ("gx_r", (3, chips, 2), None),
        ("gy_s", (3, chips, 2), None),
        ("gy_r", (3, chips, 2), None),
        ("gxr_s", (3, chips), None),
        ("gxr_r", (3, chips), None),
        ("gyr_s", (3, chips), None),
        ("gyr_r", (3, chips), None),
        ("gs_s", (6,), None),
        ("gs_r", (6,), None),
        ("small_s", (3, 2), None),
        ("small_r", (3, 2), None),
    )


INPUTS = ("tokens", "cotangent", "lengths", "mat_a", "mat_b", "norms")
OUTPUTS = ("grad_a", "grad_b", "grad_n", "square", "output", "input_grad")


def step_kernel(names, *refs):
    r = types.SimpleNamespace(**dict(zip(names, refs)))
    width, hidden = r.wa.shape[1:]
    length = r.x.shape[1]
    rows_a, (rows_b, cols_b) = r.mat_a.shape[1], r.mat_b.shape[1:]
    devices = r.tiles.shape[0]
    chips = devices // 2
    half_a, half_b = rows_a // 2, cols_b // 2
    grad_items = gradient_items(rows_a, rows_b, cols_b, width, hidden)
    head = width // HEADS
    scale = head**-0.5

    s, d = lax.axis_index("section"), lax.axis_index("dp")
    z, c = lax.div(d, 2), lax.rem(d, 2)
    sx = s + 1 - 2 * lax.rem(s, 2)
    sy = lax.rem(s + 2, SECTIONS)
    sd = SECTIONS - 1 - s
    to_sibling = {"dp": d + 1 - 2 * c}
    to_up, to_down = {"dp": d + 2}, {"dp": d - 2}
    to_x, to_y = {"section": sx}, {"section": sy}
    below, above = z > 0, z < chips - 1
    group = [{"dp": lax.rem(d + step, devices)} for step in range(1, devices)]
    plane = [{"section": lax.rem(s + step, SECTIONS)} for step in range(1, SECTIONS)]
    finish = []

    def when(condition, work):
        if condition is None:
            work()
        else:
            pl.when(condition)(work)

    def push(source, target, send_sem, recv_sem, device):
        pltpu.make_async_remote_copy(
            src_ref=source,
            dst_ref=target,
            send_sem=send_sem,
            recv_sem=recv_sem,
            device_id=device,
            device_id_type=MESH,
        ).start()

    def arrived(target, sem):
        pltpu.make_async_remote_copy(
            src_ref=target, dst_ref=target, send_sem=sem, recv_sem=sem, device_id=to_x, device_id_type=MESH
        ).wait_recv()

    def sent(source, sem):
        pltpu.make_async_remote_copy(
            src_ref=source, dst_ref=source, send_sem=sem, recv_sem=sem, device_id=to_x, device_id_type=MESH
        ).wait_send()

    def at_end(condition, source, sem):
        finish.append((condition, source, sem))

    def aligned(start, size):
        return pl.ds(pl.multiple_of(start, size), size)

    own_x = pltpu.make_async_copy(r.tokens.at[aligned(s * length, length)], r.x.at[0], r.in_s.at[0])
    own_cot = pltpu.make_async_copy(r.cotangent.at[aligned(s * length, length)], r.cot, r.in_s.at[1])
    own_x.start()
    own_cot.start()
    barrier = pltpu.get_barrier_semaphore()
    for peer in group + plane:
        pl.semaphore_signal(barrier, inc=1, device_id=peer, device_id_type=MESH)
    r.wa[s, aligned(d * rows_a, rows_a), :] = r.mat_a[0].astype(LOW)
    for layer in range(2):
        r.wb[layer, aligned(d * rows_b, rows_b), aligned(s * cols_b, cols_b)] = r.mat_b[layer].astype(LOW)
    norms = r.norms[0].astype(LOW).astype(WIDE)
    nothing = jnp.zeros((2, rows_a), WIDE)
    even = jnp.concatenate([norms, nothing], axis=1)
    odd = jnp.concatenate([nothing, norms], axis=1)
    r.tiles[d, s, 0:2, :] = jnp.where(c == 0, even, odd)
    r.tiles[d, s, 2:8, :] = jnp.zeros((6, LANES), WIDE)
    pl.semaphore_wait(barrier, len(group) + len(plane))

    def small_out(which, source):
        for peer in group:
            push(source, source, r.small_s.at[which, 0], r.small_r.at[which, 0], peer)

    def small_group(which, like):
        arrived(like, r.small_r.at[which, 0])
        sent(like, r.small_s.at[which, 0])

    def small_plane_out(which, source):
        for peer in plane:
            push(source, source, r.small_s.at[which, 1], r.small_r.at[which, 1], peer)

    def small_plane(which, like):
        arrived(like, r.small_r.at[which, 1])
        sent(like, r.small_s.at[which, 1])

    def block_a(section, chip, half):
        return r.wa.at[section, aligned((2 * chip + c) * rows_a + half * half_a, half_a), :]

    def block_b(layer):
        part = rows_b // 2

        def block(section, chip, half):
            return r.wb.at[
                layer,
                aligned((2 * chip + c) * rows_b + half * part, part),
                aligned(section * cols_b, cols_b),
            ]

        return block

    items = (block_a, block_b(0), block_b(1))

    def to_the_sibling(item, section, chip, half):
        block = items[item](section, chip, half)
        slot = section if item == 0 else 3 + item
        push(block, block, r.gs_s.at[slot], r.gs_r.at[slot], to_sibling)

    def spread_plane(item, chip):
        for half in range(2):
            block = items[item](s, chip, half)
            push(block, block, r.gx_s.at[item, chip, half], r.gx_r.at[item, chip, half], to_x)
            push(block, block, r.gy_s.at[item, chip, half], r.gy_r.at[item, chip, half], to_y)
            to_the_sibling(item, s, chip, half)

    def up(item, chip, half):
        block = items[item](s, chip, half)
        push(block, block, r.gz_s.at[item, 0, chip, half], r.gz_r.at[item, chip, half], to_up)

    def down(item, chip, half):
        block = items[item](s, chip, half)
        push(block, block, r.gz_s.at[item, 1, chip, half], r.gz_r.at[item, chip, half], to_down)

    def start_line(item):
        for half in range(2):
            when(above, lambda: up(item, z, half))
            when(below, lambda: down(item, z, half))

    def line_step(item, step):
        def from_below():
            for half in range(2):
                arrived(items[item](s, z - step, half), r.gz_r.at[item, z - step, half])
                when(above, lambda: up(item, z - step, half))
            spread_plane(item, z - step)

        def from_above():
            for half in range(2):
                arrived(items[item](s, z + step, half), r.gz_r.at[item, z + step, half])
                when(below, lambda: down(item, z + step, half))
            spread_plane(item, z + step)

        when(z >= step, from_below)
        when(z + step < chips, from_above)

    def plane_step(item):
        for chip in range(chips):
            for half in range(2):
                arrived(items[item](sx, chip, half), r.gx_r.at[item, chip, half])
                if half == 1:
                    block = items[item](sx, chip, half)
                    push(block, block, r.gyr_s.at[item, chip], r.gyr_r.at[item, chip], to_y)
                to_the_sibling(item, sx, chip, half)
                arrived(items[item](sy, chip, half), r.gy_r.at[item, chip, half])
                if half == 0:
                    block = items[item](sy, chip, half)
                    push(block, block, r.gxr_s.at[item, chip], r.gxr_r.at[item, chip], to_x)
                to_the_sibling(item, sy, chip, half)

    def relay_step(item):
        for chip in range(chips):
            arrived(items[item](sd, chip, 0), r.gxr_r.at[item, chip])
            to_the_sibling(item, sd, chip, 0)
            arrived(items[item](sd, chip, 1), r.gyr_r.at[item, chip])
            to_the_sibling(item, sd, chip, 1)

    whole_a = r.wa.at[0, pl.ds(0, chips * rows_a)]
    whole_b = r.wb.at[0, pl.ds(0, chips * rows_b)]
    for slot in range(6):
        at_end(None, whole_a if slot < 4 else whole_b, r.gs_s.at[slot])
    for item in range(3):
        for chip in range(chips):
            for half in range(2):
                block = items[item](0, chip, half)
                at_end(None, block, r.gx_s.at[item, chip, half])
                at_end(None, block, r.gy_s.at[item, chip, half])
                at_end(above & (z >= chip), block, r.gz_s.at[item, 0, chip, half])
                at_end(below & (z <= chip), block, r.gz_s.at[item, 1, chip, half])
            block = items[item](0, chip, 0)
            at_end(None, block, r.gxr_s.at[item, chip])
            at_end(None, block, r.gyr_s.at[item, chip])

    def product(left, right, dims):
        return lax.dot_general(left, right, (dims, ((), ())), preferred_element_type=WIDE)

    def loop(count, work):
        def one(index, carry):
            work(index)
            return carry

        lax.fori_loop(0, count, one, 0)

    def gain_row(layer, kind):
        parts = [
            r.tiles[2 * chip, layer, kind : kind + 1, :] + r.tiles[2 * chip + 1, layer, kind : kind + 1, :]
            for chip in range(chips)
        ]
        return jnp.concatenate(parts, axis=1)

    def stats(value):
        centre = value - jnp.mean(value, -1, keepdims=True)
        inverse = lax.rsqrt(jnp.mean(centre * centre, -1, keepdims=True) + EPSILON)
        return centre * inverse, inverse

    lane = lax.broadcasted_iota(jnp.int32, (1, 2 * head), 1)
    first_half = (lane < head).astype(WIDE)
    half_masks = (first_half.astype(LOW), (1.0 - first_half).astype(LOW))

    def prepare_masks():
        ends, total = [], jnp.int32(0)
        for slot in range(r.lengths.shape[1]):
            total = total + r.lengths[s, slot]
            ends.append(total)
        down_places = lax.broadcasted_iota(jnp.int32, (length, 1), 0)
        across_places = lax.broadcasted_iota(jnp.int32, (1, length), 1)
        down_segment = jnp.zeros((length, 1), jnp.int32)
        across_segment = jnp.zeros((1, length), jnp.int32)
        for end in ends:
            down_segment = down_segment + (end <= down_places).astype(jnp.int32)
            across_segment = across_segment + (end <= across_places).astype(jnp.int32)
        r.bias[...] = jnp.where(down_segment == across_segment, 0.0, NEGATIVE)
        r.live[...] = (down_places < total).astype(WIDE)

    def attention(layer):
        at = layer // 2
        rows = r.x[layer]
        r.xt[layer] = rows.T
        r.q[at] = product(rows, r.wa[layer, :, 0:width], NN).astype(LOW) * jnp.asarray(scale, LOW)
        keys = product(rows, r.wa[layer, :, width : 2 * width], NN).astype(LOW)
        r.k[at] = keys
        r.kt[at] = (keys * jnp.asarray(scale, LOW)).T
        values = product(rows, r.wa[layer, :, 2 * width : 3 * width], NN).astype(LOW)
        r.v[at] = values
        r.vt[at] = values.T

        def pair(index):
            lanes = aligned(index * 2 * head, 2 * head)
            for which in range(2):
                scores = product(r.k[at, :, lanes], r.q[at, :, lanes] * half_masks[which], NT) + r.bias[...]
                weights = jnp.exp(scores - jnp.max(scores, 0, keepdims=True))
                probs = (weights * (1.0 / jnp.sum(weights, 0, keepdims=True))).astype(LOW)
                r.pt[at, 2 * index + which] = probs
                place = aligned((2 * index + which) * head, head)
                r.ot[at, place, :] = product(r.vt[at, place, :], probs, NN).astype(LOW)

        def pairs(step):
            pair(2 * step)
            pair(2 * step + 1)

        loop(HEADS // 4, pairs)
        r.f[...] = product(r.ot[at].T, r.wa[layer, :, 3 * width :], NN)

    def expand(layer):
        at = layer // 2
        r.xt[layer] = r.x[layer].T

        def columns(index):
            place = aligned(index * width, width)
            pre = product(r.x[layer], r.wa[layer, :, place], NN)
            squared = pre * pre
            slope = 0.7978845608 * (1.0 + 3 * 0.044715 * squared)
            bent = jnp.tanh(0.7978845608 * pre * (1.0 + 0.044715 * squared))
            r.g[at, :, place] = (0.5 * pre * (1.0 + bent)).astype(LOW)
            r.slope[at, :, place] = (0.5 * (1.0 + bent) + 0.5 * pre * (1.0 - bent * bent) * slope).astype(LOW)

        loop(hidden // width, columns)

    def contract(layer):
        r.f[...] = product(r.g[layer // 2], r.wb[layer // 2], NN)

    def by_rows(work):
        loop(length // BLOCK, lambda index: work(aligned(index * BLOCK, BLOCK)))

    def normalize(layer):
        gain, offset = gain_row(layer, 0), gain_row(layer, 1)

        def some(rows):
            branch = r.f[rows, :]
            normal, inverse = stats(r.x[layer, rows, :].astype(WIDE) + branch)
            r.n[layer, rows, :] = normal
            r.inv[layer, rows, :] = inverse
            out = normal * gain + offset
            dual = branch if layer == 0 else r.y[rows, :].astype(WIDE) + branch
            if layer < 3:
                r.x[layer + 1, rows, :] = out.astype(LOW)
                r.y[rows, :] = dual.astype(LOW)
            else:
                dual_normal, dual_inverse = stats(dual)
                r.output[rows, :] = (out + dual_normal).astype(LOW)
                pull = r.cot[rows, :].astype(WIDE) * r.live[rows, :]
                r.gx[rows, :] = pull
                r.gy[rows, :] = norm_back(dual_normal, dual_inverse, pull)

        by_rows(some)

    def back_normalize(layer):
        gain = gain_row(layer, 0)

        def some(index, sums):
            rows = aligned(index * BLOCK, BLOCK)
            upstream = r.gx[rows, :]
            normal = r.n[layer, rows, :]
            summed = norm_back(normal, r.inv[layer, rows, :], upstream * gain)
            dual = r.gy[rows, :]
            r.gx[rows, :] = summed
            r.df[rows, :] = (summed + dual).astype(LOW)
            if layer == 3:
                r.gy[rows, :] = dual.astype(LOW).astype(WIDE)
            return (
                sums[0] + jnp.sum(upstream * normal, 0, keepdims=True),
                sums[1] + jnp.sum(upstream, 0, keepdims=True),
            )

        zero = jnp.zeros((1, width), WIDE)
        gains, offsets = lax.fori_loop(0, length // BLOCK, some, (zero, zero))
        r.ng[d, 2 * layer : 2 * layer + 1, :] = gains
        r.ng[d, 2 * layer + 1 : 2 * layer + 2, :] = offsets

    def pass_down(layer, inner):
        total = r.gx[...] + inner
        if layer > 0:
            r.gx[...] = total.astype(LOW).astype(WIDE)
        else:
            r.input_grad[...] = total

    def keep(name, half, place, value):
        own = getattr(r, "own" + name)
        own[:, :, :, half, :, place] = value.astype(LOW).reshape(
            chips, 2, SECTIONS, rows_a // SECTIONS, value.shape[1]
        )

    def back_contract(layer):
        own = getattr(r, "ownB%d" % (layer // 2))
        r.dft[...] = r.df[...].T

        def owner(index):
            value = product(r.dft[...], r.g[layer // 2, :, aligned(index * rows_b, rows_b)], NN)
            own[lax.div(index, 2), lax.rem(index, 2)] = value.astype(LOW).reshape(SECTIONS, 2, half_b, rows_b)

        loop(devices, owner)

    def back_expand(layer):
        at = layer // 2

        def columns(index):
            place = aligned(index * width, width)
            pulled = product(r.df[...], r.wb[at, place, :], NT)
            pulled = (pulled * r.slope[at, :, place].astype(WIDE)).astype(LOW)
            r.dp[:, place] = pulled
            inner = aligned(lax.rem(index, 2) * width, width)
            keep("F%d" % layer, lax.div(index, 2), inner, product(r.xt[layer], pulled, NN))

        loop(hidden // width, columns)

    def back_expand_end(layer):
        pass_down(layer, product(r.dp[...], r.wa[layer], NT))

    def back_output(layer):
        at = layer // 2
        for half in range(2):
            place = pl.ds(half * width // 2, width // 2)
            keep("O%d" % layer, half, pl.ds(0, width // 2), product(r.ot[at], r.df[:, place], NN))
        r.dm[...] = product(r.df[...], r.wa[layer, :, 3 * width :], NT).astype(LOW)

    def back_heads(layer, begin, count):
        at = layer // 2

        def pair(index):
            lanes = aligned(index * 2 * head, 2 * head)
            pulled = r.dm[:, lanes]
            keys, values = [], []
            for which in range(2):
                probs = r.pt[at, 2 * index + which]
                grad = product(r.v[at, :, lanes], pulled * half_masks[which], NT)
                full = probs.astype(WIDE)
                centre = jnp.sum(full * grad, 0, keepdims=True)
                scores = (full * (grad - centre)).astype(LOW)
                keys.append(product(scores, r.q[at, :, lanes], NN))
                values.append(product(probs, pulled, NN))
                place = aligned((2 * index + which) * head, head)
                r.dqt[place, :] = product(r.kt[at, place, :], scores, NN).astype(LOW)
            r.dp[:, aligned(width + index * 2 * head, 2 * head)] = jnp.where(
                lane < head, keys[0], keys[1]
            ).astype(LOW)
            r.dp[:, aligned(2 * width + index * 2 * head, 2 * head)] = jnp.where(
                lane < head, values[0], values[1]
            ).astype(LOW)

        def pairs(step):
            pair(begin + 2 * step)
            pair(begin + 2 * step + 1)

        loop(count // 2, pairs)

    def back_packed(layer):
        r.dp[:, 0:width] = r.dqt[...].T
        part = 3 * width // 2
        for half in range(2):
            value = product(r.xt[layer], r.dp[:, half * part : (half + 1) * part], NN)
            keep("K%d" % layer, half, pl.ds(0, part), value)

    def back_packed_end(layer):
        pass_down(layer, product(r.dp[:, 0 : 3 * width], r.wa[layer, :, 0 : 3 * width], NT))

    def joined(target, others):
        return functools.reduce(
            lambda left, right: left + right, [ref[...].astype(WIDE) for ref in (target, *others)]
        )

    def add_into(target, others):
        target[...] = joined(target, others).astype(LOW)

    places = {name: place for place, (name, _, _, _) in enumerate(grad_items)}
    by_turn = (sd, sx, sy, s)

    def buffers(name):
        parts = ("own", "sib", "farx", "fary", "nearx", "neary", "line", "done")
        return types.SimpleNamespace(**{part: getattr(r, part + name) for part in parts})

    def to_core(name):
        item, place = buffers(name), places[name]
        for turn, section in enumerate(by_turn):
            push(
                item.own.at[:, 1 - c, section],
                item.sib.at[:, section],
                r.sib_s.at[place, turn],
                r.sib_r.at[place, turn],
                to_sibling,
            )
            at_end(None, item.sib.at[:, 0], r.sib_s.at[place, turn])

    def to_plane(name):
        item, place = buffers(name), places[name]
        own = item.own.at[:, c]

        def over_x(section, half, target, slot):
            push(own.at[:, section, half], target, r.px_s.at[place, slot], r.px_r.at[place, slot], to_x)
            at_end(None, item.farx, r.px_s.at[place, slot])

        def over_y(section, half, target, slot):
            push(own.at[:, section, half], target, r.py_s.at[place, slot], r.py_r.at[place, slot], to_y)
            at_end(None, item.farx, r.py_s.at[place, slot])

        for turn, section in enumerate(by_turn):
            arrived(item.sib.at[:, section], r.sib_r.at[place, turn])
            add_into(own.at[:, section], [item.sib.at[:, section]])
            if turn == 0:
                over_x(sd, 0, item.farx, 2)
                over_y(sd, 1, item.fary, 2)
            elif turn == 1:
                over_x(sx, 0, item.nearx.at[0], 0)
            elif turn == 2:
                over_y(sy, 1, item.neary.at[1], 1)

    def through_plane(name):
        item, place = buffers(name), places[name]
        own = item.own.at[:, c]
        arrived(item.fary, r.py_r.at[place, 2])
        add_into(own.at[:, sx, 1], [item.fary])
        push(own.at[:, sx, 1], item.nearx.at[1], r.px_s.at[place, 1], r.px_r.at[place, 1], to_x)
        at_end(None, item.farx, r.px_s.at[place, 1])
        arrived(item.farx, r.px_r.at[place, 2])
        add_into(own.at[:, sy, 0], [item.farx])
        push(own.at[:, sy, 0], item.neary.at[0], r.py_s.at[place, 0], r.py_r.at[place, 0], to_y)
        at_end(None, item.farx, r.py_s.at[place, 0])

    def to_line(name):
        item, place = buffers(name), places[name]
        own = item.own.at[:, c, s]
        for half in range(2):
            arrived(item.nearx.at[half], r.px_r.at[place, half])
            arrived(item.neary.at[half], r.py_r.at[place, half])
            add_into(own.at[:, half], [item.nearx.at[half], item.neary.at[half]])
        for step in range(1, chips):
            chip = lax.rem(z + step, chips)
            push(
                own.at[chip],
                item.line.at[z],
                r.line_s.at[place, step],
                r.line_r.at[place, z],
                {"dp": 2 * chip + c},
            )
            at_end(None, item.line.at[0], r.line_s.at[place, step])

    def to_owner(name):
        item, place = buffers(name), places[name]
        others = [lax.rem(z + step, chips) for step in range(1, chips)]
        for chip in others:
            arrived(item.line.at[chip], r.line_r.at[place, chip])
        total = joined(item.own.at[z, c, s], [item.line.at[chip] for chip in others])
        square = total * total
        while square.ndim > 2:
            square = jnp.sum(square, 0)
        square = jnp.sum(jnp.sum(square, 0, keepdims=True), 1, keepdims=True)
        r.sum[...] = r.sum[...] + jnp.broadcast_to(square, (8, LANES))
        if name[0] == "B":
            item.done[...] = total
            return
        item.done[s] = total.astype(LOW)
        layer = grad_items[place][1]
        mine = item.done.at[s]
        away = s != layer
        when(
            away,
            lambda: push(mine, mine, r.done_s.at[place], r.done_r.at[place, s], {"section": jnp.int32(layer)}),
        )
        at_end(away, mine, r.done_s.at[place])

    def collect(name):
        item, place = buffers(name), places[name]
        layer = grad_items[place][1]

        def work():
            for section in range(SECTIONS):
                if section != layer:
                    arrived(item.done.at[section], r.done_r.at[place, section])
            columns = item.done.shape[-1]
            start = 3 * width if name[0] == "O" else 0
            for section in range(SECTIONS):
                for half in range(2):
                    rows = pl.ds(section * (rows_a // SECTIONS), rows_a // SECTIONS)
                    place_to = pl.ds(start + half * columns, columns)
                    r.grad_a[rows, place_to] = item.done[section, half].astype(WIDE)

        when(s == layer, work)

    def all_sent():
        for condition, source, sem in finish:
            when(condition, functools.partial(sent, source, sem))
        finish.clear()

    small_out(0, r.tiles.at[d, s])
    start_line(0)
    spread_plane(0, z)
    line_step(0, 1)
    start_line(1)
    start_line(2)
    for step in range(2, chips):
        line_step(0, step)
    small_group(0, r.tiles.at[pl.ds(0, devices - 1), 0])
    for peer in plane:
        push(r.tiles.at[:, s], r.tiles.at[:, s], r.small_s.at[0, 1], r.small_r.at[0, 1], peer)
    prepare_masks()
    plane_step(0)
    for item in (1, 2):
        spread_plane(item, z)
        for step in range(1, chips):
            line_step(item, step)
    own_x.wait()
    own_cot.wait()
    relay_step(0)
    small_plane(0, r.tiles.at[:, pl.ds(0, SECTIONS - 1)])
    for slot in range(4):
        arrived(whole_a, r.gs_r.at[slot])
    attention(0)
    normalize(0)
    expand(1)
    plane_step(1)
    relay_step(1)
    arrived(whole_b, r.gs_r.at[4])
    contract(1)
    normalize(1)
    plane_step(2)
    attention(2)
    normalize(2)
    expand(3)
    relay_step(2)
    arrived(whole_b, r.gs_r.at[5])
    contract(3)
    normalize(3)

    r.sum[...] = jnp.zeros((8, LANES), WIDE)
    back_normalize(3)
    back_contract(3)
    to_core("B1")
    back_expand(3)
    to_core("F3")
    to_plane("B1")
    back_expand_end(3)
    back_normalize(2)
    back_output(2)
    to_core("O2")
    to_plane("F3")
    back_heads(2, 0, 2)
    through_plane("B1")
    to_plane("O2")
    back_heads(2, 2, 2)
    through_plane("F3")
    to_line("B1")
    back_packed(2)
    to_core("K2")
    through_plane("O2")
    back_packed_end(2)
    to_line("F3")
    back_normalize(1)
    to_plane("K2")
    to_owner("B1")
    back_contract(1)
    to_core("B0")
    to_line("O2")
    back_expand(1)
    to_core("F1")
    through_plane("K2")
    to_plane("B0")
    to_owner("F3")
    back_expand_end(1)
    back_normalize(0)
    back_output(0)
    to_core("O0")
    to_plane("F1")
    to_owner("O2")
    to_line("K2")
    back_heads(0, 0, 2)
    through_plane("B0")
    to_plane("O0")
    back_heads(0, 2, 2)
    through_plane("F1")
    to_line("B0")
    to_owner("K2")
    back_packed(0)
    to_core("K0")
    small_out(1, r.ng.at[d])
    through_plane("O0")
    to_line("F1")
    back_packed_end(0)
    to_plane("K0")
    to_owner("B0")
    to_line("O0")
    all_sent()
    through_plane("K0")
    to_owner("F1")
    to_owner("O0")
    small_group(1, r.ng.at[pl.ds(0, devices - 1)])
    r.ns[s] = functools.reduce(lambda left, right: left + right, [r.ng[index] for index in range(devices)])
    small_plane_out(1, r.ns.at[s])
    for name in ("F3", "O2", "K2", "F1"):
        collect(name)
    to_line("K0")
    collect("O0")
    for layer in range(2):
        done = buffers("B%d" % layer).done
        r.grad_b[layer] = done[...].reshape(cols_b, rows_b).T
    small_plane(1, r.ns.at[pl.ds(0, SECTIONS - 1)])
    grads = functools.reduce(lambda left, right: left + right, [r.ns[index] for index in range(SECTIONS)])
    norm_square = jnp.sum(jnp.sum(grads * grads, 0, keepdims=True), 1, keepdims=True)
    chosen = jnp.zeros((2, width), WIDE)
    for layer in range(4):
        chosen = jnp.where(s == layer, grads[2 * layer : 2 * layer + 2, :], chosen)
    for chip in range(chips):
        pair_of = chosen[:, chip * LANES : (chip + 1) * LANES]
        r.grad_n[...] = jnp.where(
            z == chip, jnp.where(c == 0, pair_of[:, :rows_a], pair_of[:, rows_a:]), r.grad_n[...]
        )
    to_owner("K0")

    r.sq[d] = r.sum[...]
    small_out(2, r.sq.at[d])
    collect("K0")
    small_group(2, r.sq.at[pl.ds(0, devices - 1)])
    r.sqs[s] = functools.reduce(lambda left, right: left + right, [r.sq[index] for index in range(devices)])
    small_plane_out(2, r.sqs.at[s])
    all_sent()
    small_plane(2, r.sqs.at[pl.ds(0, SECTIONS - 1)])
    squares = functools.reduce(lambda left, right: left + right, [r.sqs[index] for index in range(SECTIONS)])
    r.square[...] = squares + norm_square


def step_call(tokens, cotangent, lengths, mat_a, mat_b, norms):
    rows_a, hidden = mat_a.shape[1:]
    rows_b, cols_b = mat_b.shape[1:]
    width = tokens.shape[1]
    length = tokens.shape[0] // lengths.shape[0]
    chips = width // rows_a // 2
    scratch = kernel_scratch(chips, rows_a, rows_b, cols_b, length, width, hidden)
    shapes = []
    for _, shape, kind in scratch:
        shapes.append(pltpu.SemaphoreType.DMA(shape) if kind is None else pltpu.VMEM(shape, kind))
    anywhere, vmem = pl.BlockSpec(memory_space=pl.ANY), pl.BlockSpec(memory_space=pltpu.VMEM)
    return pl.pallas_call(
        functools.partial(step_kernel, INPUTS + OUTPUTS + tuple(name for name, _, _ in scratch)),
        out_shape=(
            jax.ShapeDtypeStruct((rows_a, hidden), WIDE),
            jax.ShapeDtypeStruct(mat_b.shape, WIDE),
            jax.ShapeDtypeStruct((2, rows_a), WIDE),
            jax.ShapeDtypeStruct((8, LANES), WIDE),
            jax.ShapeDtypeStruct((length, width), LOW),
            jax.ShapeDtypeStruct((length, width), WIDE),
        ),
        in_specs=[anywhere, anywhere, pl.BlockSpec(memory_space=pltpu.SMEM), vmem, vmem, vmem],
        out_specs=[vmem] * len(OUTPUTS),
        scratch_shapes=shapes,
        compiler_params=pltpu.CompilerParams(
            collective_id=0, has_side_effects=True, vmem_limit_bytes=KERNEL_VMEM
        ),
    )(tokens, cotangent, lengths, mat_a, mat_b, norms)


def update_kernel(*refs):
    square, output, input_grad = (ref[...] for ref in refs[:3])
    grad_norm = jnp.sqrt(square[0:1, 0:1])
    factor = CLIP_NORM / jnp.maximum(grad_norm, CLIP_NORM)
    inputs, outputs = refs[3:15], refs[15:]
    outputs[0][...] = grad_norm
    outputs[1][0] = output
    outputs[2][0] = input_grad
    for group, (rate, decay) in enumerate(
        ((MATRIX_RATE, MATRIX_DECAY), (MATRIX_RATE, MATRIX_DECAY), (NORM_RATE, 0.0))
    ):
        grad, weight, one, two = inputs[4 * group : 4 * group + 4]
        clip = grad[...].reshape(weight.shape) * factor
        moment, square_new, master = adam_update(weight[...], one[...], two[...], clip, rate, decay)
        for ref, value in zip(
            outputs[3 + 5 * group : 8 + 5 * group], (clip, moment, square_new, master, master.astype(LOW))
        ):
            ref[...] = value


def kernel_body(
    tokens, cotangent, lengths, mat_a, mat_b, norms, first_a, second_a, first_b, second_b, first_n, second_n
):
    norms, first_n, second_n = (jnp.swapaxes(value, 1, 2) for value in (norms, first_n, second_n))
    grad_a, grad_b, grad_n, square, output, input_grad = step_call(
        tokens, cotangent, lengths, mat_a, mat_b, norms
    )
    steps = 4

    def cut(value, dim):
        shape = tuple(size // steps if at == dim else size for at, size in enumerate(value.shape))
        return pl.BlockSpec(shape, lambda step: tuple(step if at == dim else 0 for at in range(len(shape))))

    def whole(value):
        return pl.BlockSpec(value.shape, lambda step: (0,) * len(value.shape))

    def like(value, kind=WIDE):
        return jax.ShapeDtypeStruct(value.shape, kind)

    args = (square, output, input_grad, grad_a, mat_a, first_a, second_a, grad_b, mat_b, first_b, second_b)
    specs = [whole(square), cut(output, 0), cut(input_grad, 0)]
    specs += [cut(grad_a, 0)] + [cut(mat_a, 1)] * 3 + [cut(grad_b, 1)] * 4
    args += (grad_n, norms, first_n, second_n)
    specs += [whole(grad_n)] + [whole(norms)] * 3
    shapes = [jax.ShapeDtypeStruct((1, 1), WIDE), like(output[None], LOW), like(input_grad[None])]
    out_specs = [whole(shapes[0]), cut(shapes[1], 1), cut(shapes[2], 1)]
    for value, spec in ((mat_a, cut(mat_a, 1)), (mat_b, cut(mat_b, 1)), (norms, whole(norms))):
        shapes += [like(value)] * 4 + [like(value, LOW)]
        out_specs += [spec] * 5
    results = pl.pallas_call(
        update_kernel,
        grid=(steps,),
        out_shape=shapes,
        in_specs=specs,
        out_specs=out_specs,
        compiler_params=pltpu.CompilerParams(vmem_limit_bytes=KERNEL_VMEM),
    )(*args)
    results = [results[0][0, 0], *results[1:]]
    results[-5:] = [jnp.swapaxes(value, 1, 2) for value in results[-5:]]
    return tuple(results)


def chosen_body(*args):
    rows_a = args[3].shape[1]
    groups = lax.axis_size("dp")
    by_kernel = rows_a % 32 == 0 and 2 * rows_a == LANES and groups * rows_a == args[0].shape[1]
    return (kernel_body if by_kernel else body)(*args)


def solution(mesh):
    placed = (
        P("dp", None),
        P("dp", None),
        P("dp", None),
        P("section", "dp", None),
        P(None, "dp", "section"),
        P("section", "dp", None),
        P("section", "dp", None),
        P("section", "dp", None),
        P(None, "dp", "section"),
        P(None, "dp", "section"),
        P("section", "dp", None),
        P("section", "dp", None),
    )
    return jax.shard_map(
        chosen_body,
        mesh=mesh,
        in_specs=placed,
        out_specs=(
            P(),
            P("section", "dp", None),
            P("section", "dp", None),
            P("section", "dp", None),
            P("section", "dp", None),
            P("section", "dp", None),
            P("section", "dp", None),
            P("section", "dp", None),
            P(None, "dp", "section"),
            P(None, "dp", "section"),
            P(None, "dp", "section"),
            P(None, "dp", "section"),
            P(None, "dp", "section"),
            P("section", "dp", None),
            P("section", "dp", None),
            P("section", "dp", None),
            P("section", "dp", None),
            P("section", "dp", None),
        ),
        check_vma=False,
    )
```

```python
import functools
import types

import jax
import jax.numpy as jnp
from jax import lax
from jax.experimental import pallas as pl
from jax.experimental.pallas import tpu as pltpu
from jax.sharding import PartitionSpec as P

HEADS = 8
STEP = 5


EPSILON = 1e-05
NEGATIVE = -1e30
CLIP_NORM = 1.0
BETA_ONE = 0.5
BETA_TWO = 0.5
ADAM_EPSILON = 1e-08
MATRIX_RATE = 0.05
NORM_RATE = 0.5
MATRIX_DECAY = 0.01


def norm_stats(value):
    centre = value - jnp.mean(value, -1, keepdims=True)
    inverse = lax.rsqrt(jnp.mean(centre * centre, -1, keepdims=True) + EPSILON)
    return (centre * inverse, inverse)


def norm_back(normal, inverse, upstream):
    return inverse * (
        upstream
        - jnp.mean(upstream, -1, keepdims=True)
        - normal * jnp.mean(upstream * normal, -1, keepdims=True)
    )


def adam_update(weight, moment_one, moment_two, gradient, step_rate, decay_rate):
    first_new = BETA_ONE * moment_one + (1.0 - BETA_ONE) * gradient
    second_new = BETA_TWO * moment_two + (1.0 - BETA_TWO) * gradient * gradient
    first_hat = first_new / (1.0 - BETA_ONE**STEP)
    second_hat = second_new / (1.0 - BETA_TWO**STEP)
    weight_new = weight - step_rate * (
        first_hat / (jnp.sqrt(second_hat) + ADAM_EPSILON) + decay_rate * weight
    )
    return (first_new, second_new, weight_new)


def segments_of(lengths_row, length):
    ends = jnp.cumsum(lengths_row, dtype=jnp.int32)
    places = jnp.arange(length, dtype=jnp.int32)
    segment = jnp.sum((ends[None, :] <= places[:, None]).astype(jnp.int32), axis=1, dtype=jnp.int32)
    live = (places < ends[-1]).astype(jnp.float32)
    return segment, live


def matmul(left, right, dims):
    return lax.dot_general(left, right, (dims, ((), ())), preferred_element_type=jnp.float32)


NN = ((1,), (0,))
NT = ((1,), (1,))
TN = ((0,), (0,))


def attention_forward(stream, weight, mask):
    length, width = stream.shape
    size = width // HEADS
    packed = matmul(stream, weight[:, : 3 * width], NN).astype(jnp.bfloat16)
    heads = packed.reshape(length, 3, HEADS, size)
    scores = jnp.einsum("qhd,khd->hqk", heads[:, 0], heads[:, 1], preferred_element_type=jnp.float32)
    scores = jnp.where(mask[None], scores * size**-0.5, NEGATIVE)
    weights = jnp.exp(scores - jnp.max(scores, -1, keepdims=True))
    probs = weights / jnp.sum(weights, -1, keepdims=True)
    mixed = jnp.einsum("hqk,khd->qhd", probs.astype(jnp.bfloat16), heads[:, 2], preferred_element_type=jnp.float32)
    mixed = mixed.reshape(length, width).astype(jnp.bfloat16)
    branch = matmul(mixed, weight[:, 3 * width :], NN)
    return branch, (heads, probs, mixed)


def attention_backward(stream, weight, kept, grad_low):
    heads, probs, mixed = kept
    length, width = stream.shape
    size = width // HEADS
    grad_out = matmul(mixed, grad_low, TN)
    grad_mixed = matmul(grad_low, weight[:, 3 * width :], NT).astype(jnp.bfloat16)
    grad_mixed = grad_mixed.reshape(length, HEADS, size)
    grad_probs = jnp.einsum("qhd,khd->hqk", grad_mixed, heads[:, 2], preferred_element_type=jnp.float32)
    centre = jnp.sum(probs * grad_probs, -1, keepdims=True)
    grad_scores = (probs * (grad_probs - centre)).astype(jnp.bfloat16)
    low = probs.astype(jnp.bfloat16)
    scale = size**-0.5
    grad_q = jnp.einsum("hqk,khd->qhd", grad_scores, heads[:, 1], preferred_element_type=jnp.float32) * scale
    grad_k = jnp.einsum("hqk,qhd->khd", grad_scores, heads[:, 0], preferred_element_type=jnp.float32) * scale
    grad_v = jnp.einsum("hqk,qhd->khd", low, grad_mixed, preferred_element_type=jnp.float32)
    packed = jnp.concatenate([grad_q, grad_k, grad_v], axis=1).reshape(length, 3 * width)
    packed = packed.astype(jnp.bfloat16)
    grad_in = matmul(stream, packed, TN)
    grad_inputs = matmul(packed, weight[:, : 3 * width], NT)
    return grad_inputs, jnp.concatenate([grad_in, grad_out], axis=1)


def feed_forward(stream, weight, down):
    pre = matmul(stream, weight, NN)
    active = jax.nn.gelu(pre, approximate=True).astype(jnp.bfloat16)
    return matmul(active, down, NN), (pre, active)


def feed_backward(stream, weight, down, kept, grad_low):
    pre, active = kept
    grad_down = matmul(active, grad_low, TN)
    grad_active = matmul(grad_low, down, NT)
    pull = jax.vjp(lambda value: jax.nn.gelu(value, approximate=True), pre)[1]
    grad_pre = pull(grad_active)[0].astype(jnp.bfloat16)
    grad_up = matmul(stream, grad_pre, TN)
    return matmul(grad_pre, weight, NT), grad_up, grad_down


def micro_step(rows, pull, segment, mats, downs, gains, biases):
    low = jnp.bfloat16
    mask = segment[:, None] == segment[None, :]
    stream, dual = rows, jnp.zeros_like(rows)
    saved = []
    for sub in range(4):
        if sub % 2 == 0:
            branch, kept = attention_forward(stream, mats[sub], mask)
        else:
            branch, kept = feed_forward(stream, mats[sub], downs[sub // 2])
        normal, inverse = norm_stats(stream.astype(jnp.float32) + branch)
        out = normal * gains[sub] + biases[sub]
        total = dual.astype(jnp.float32) + branch
        saved.append((stream, kept, normal, inverse))
        if sub < 3:
            stream, dual = out.astype(low), total.astype(low)
    dual_normal, dual_inverse = norm_stats(total)
    output = (out + dual_normal).astype(low)
    grad_out, grad_dual = pull, norm_back(dual_normal, dual_inverse, pull)
    grads_a, grads_b, grads_n = [None] * 4, [None] * 2, [None] * 4
    for sub in (3, 2, 1, 0):
        stream, kept, normal, inverse = saved[sub]
        grads_n[sub] = jnp.stack([jnp.sum(grad_out * normal, 0), jnp.sum(grad_out, 0)], axis=1)
        summed = norm_back(normal, inverse, grad_out * gains[sub])
        branch_low = (summed + grad_dual).astype(low)
        if sub % 2 == 0:
            inner, grads_a[sub] = attention_backward(stream, mats[sub], kept, branch_low)
        else:
            inner, grads_a[sub], grads_b[sub // 2] = feed_backward(
                stream, mats[sub], downs[sub // 2], kept, branch_low
            )
        grad_in = summed + inner
        if sub > 0:
            grad_out = grad_in.astype(low).astype(jnp.float32)
            grad_dual = grad_dual.astype(low).astype(jnp.float32)
    return output, grad_in, jnp.stack(grads_a), jnp.stack(grads_b), jnp.stack(grads_n)


def finish_step(grad_norm, output, input_grad, *groups):
    factor = CLIP_NORM / jnp.maximum(grad_norm, CLIP_NORM)
    results = [grad_norm, output[None], input_grad[None]]
    for weight, one, two, grad, rate, decay in groups:
        clip = grad * factor
        moment, square_new, master = adam_update(weight, one, two, clip, rate, decay)
        results += [clip, moment, square_new, master, master.astype(jnp.bfloat16)]
    return tuple(results)


def body(
    tokens, cotangent, lengths, mat_a, mat_b, norms, first_a, second_a, first_b, second_b, first_n, second_n
):
    low = jnp.bfloat16
    own = lax.axis_index("section")
    length = tokens.shape[0] // lengths.shape[0]
    rows = lax.dynamic_slice_in_dim(tokens, own * length, length, 0)
    segment, live = segments_of(lax.dynamic_index_in_dim(lengths, own, 0, keepdims=False), length)
    pull = lax.dynamic_slice_in_dim(cotangent, own * length, length, 0).astype(jnp.float32) * live[:, None]

    def gathered(value):
        return lax.all_gather(lax.all_gather(value, "dp", axis=1, tiled=True), "section", axis=0, tiled=True)

    mats = gathered(mat_a.astype(low))
    scales = gathered(norms.astype(low)).astype(jnp.float32)
    downs = lax.all_gather(mat_b.astype(low), "section", axis=2, tiled=True)
    downs = lax.all_gather(downs, "dp", axis=1, tiled=True)
    output, input_grad, part_a, part_b, part_n = micro_step(
        rows, pull, segment, mats, downs, scales[:, :, 0], scales[:, :, 1]
    )

    def scattered(value, section_dim):
        value = lax.psum_scatter(value, "section", scatter_dimension=section_dim, tiled=True)
        return lax.psum_scatter(value, "dp", scatter_dimension=1, tiled=True).astype(jnp.float32)

    grad_a = scattered(part_a.astype(low), 0)
    grad_b = scattered(part_b.astype(low), 2)
    grad_n = scattered(part_n, 0)
    square = jnp.sum(grad_a * grad_a) + jnp.sum(grad_b * grad_b) + jnp.sum(grad_n * grad_n)
    grad_norm = jnp.sqrt(lax.psum(square, ("section", "dp")))
    return finish_step(
        grad_norm, output, input_grad,
        (mat_a, first_a, second_a, grad_a, MATRIX_RATE, MATRIX_DECAY),
        (mat_b, first_b, second_b, grad_b, MATRIX_RATE, MATRIX_DECAY),
        (norms, first_n, second_n, grad_n, NORM_RATE, 0.0),
    )


LOW = jnp.bfloat16
WIDE = jnp.float32
MESH = pl.DeviceIdType.MESH
SECTIONS = 4
LANES = 128
BLOCK = 64
KERNEL_VMEM = 64 * 1024 * 1024 - 256 * 1024


def gradient_items(rows_a, rows_b, cols_b, width, hidden):
    part = rows_a // SECTIONS
    return (
        ("B1", 3, cols_b // 2, rows_b),
        ("F3", 3, part, hidden // 2),
        ("O2", 2, part, width // 2),
        ("K2", 2, part, 3 * width // 2),
        ("B0", 1, cols_b // 2, rows_b),
        ("F1", 1, part, hidden // 2),
        ("O0", 0, part, width // 2),
        ("K0", 0, part, 3 * width // 2),
    )


def item_scratch(name, chips, rows, columns):
    piece = (rows, columns)
    return (
        ("own" + name, (chips, 2, SECTIONS, 2) + piece, LOW),
        ("sib" + name, (chips, SECTIONS, 2) + piece, LOW),
        ("farx" + name, (chips,) + piece, LOW),
        ("fary" + name, (chips,) + piece, LOW),
        ("nearx" + name, (2, chips) + piece, LOW),
        ("neary" + name, (2, chips) + piece, LOW),
        ("line" + name, (chips, 2) + piece, LOW),
        ("done" + name, (2,) + piece if name[0] == "B" else (SECTIONS, 2) + piece, WIDE if name[0] == "B" else LOW),
    )


def kernel_scratch(chips, rows_a, rows_b, cols_b, length, width, hidden):
    devices = 2 * chips
    items = gradient_items(rows_a, rows_b, cols_b, width, hidden)
    count = len(items)
    received = sum((item_scratch(name, chips, rows, columns) for name, _, rows, columns in items), ())
    return received + (
        ("sib_s", (count, SECTIONS), None),
        ("sib_r", (count, SECTIONS), None),
        ("px_s", (count, 3), None),
        ("px_r", (count, 3), None),
        ("py_s", (count, 3), None),
        ("py_r", (count, 3), None),
        ("line_s", (count, chips), None),
        ("line_r", (count, chips), None),
        ("done_s", (count,), None),
        ("done_r", (count, SECTIONS), None),
        ("wa", (4, chips, 2, SECTIONS, rows_a // SECTIONS, hidden), LOW),
        ("wb", (2, chips, 2, rows_b, width), LOW),
        ("cut", (SECTIONS, rows_a // SECTIONS, hidden), LOW),
        ("tiles", (devices, SECTIONS, 8, LANES), WIDE),
        ("x", (4, length, width), LOW),
        ("xt", (4, width, length), LOW),
        ("y", (length, width), LOW),
        ("cot", (length, width), LOW),
        ("bias", (length, length), WIDE),
        ("live", (length, 1), WIDE),
        ("f", (length, width), WIDE),
        ("n", (4, length, width), WIDE),
        ("inv", (4, length, 1), WIDE),
        ("q", (2, length, width), LOW),
        ("k", (2, length, width), LOW),
        ("v", (2, length, width), LOW),
        ("kt", (2, width, length), LOW),
        ("vt", (2, width, length), LOW),
        ("ot", (2, width, length), LOW),
        ("pt", (2, HEADS, length, length), LOW),
        ("g", (2, length, hidden), LOW),
        ("slope", (2, length, hidden), LOW),
        ("gx", (length, width), WIDE),
        ("gy", (length, width), WIDE),
        ("df", (length, width), LOW),
        ("dft", (width, length), LOW),
        ("dm", (length, width), LOW),
        ("dqt", (width, length), LOW),
        ("dp", (length, hidden), LOW),
        ("ng", (devices, 8, width), WIDE),
        ("ns", (SECTIONS, 8, width), WIDE),
        ("sq", (devices, 8, LANES), WIDE),
        ("sqs", (SECTIONS, 8, LANES), WIDE),
        ("sum", (8, LANES), WIDE),
        ("in_s", (2,), None),
        ("cut_s", (1,), None),
        ("cut_r", (SECTIONS,), None),
        ("gz_s", (6,), None),
        ("gz_r", (6, chips), None),
        ("gx_s", (6,), None),
        ("gx_r", (6,), None),
        ("gy_s", (6,), None),
        ("gy_r", (6,), None),
        ("rx_s", (6,), None),
        ("rx_r", (6,), None),
        ("ry_s", (6,), None),
        ("ry_r", (6,), None),
        ("gs_s", (6,), None),
        ("gs_r", (6,), None),
        ("small_s", (3, 2), None),
        ("small_r", (3, 2), None),
    )


INPUTS = ("tokens", "cotangent", "lengths", "mat_a", "mat_b", "norms")
OUTPUTS = ("grad_a", "grad_b", "grad_n", "square", "output", "input_grad")


def step_kernel(names, *refs):
    r = types.SimpleNamespace(**dict(zip(names, refs)))
    length, width = r.x.shape[1:]
    hidden = r.wa.shape[-1]
    rows_a, (rows_b, cols_b) = r.mat_a.shape[1], r.mat_b.shape[1:]
    devices = r.tiles.shape[0]
    chips = devices // 2
    half_b = cols_b // 2
    grad_items = gradient_items(rows_a, rows_b, cols_b, width, hidden)
    head = width // HEADS
    scale = head**-0.5

    s, d = lax.axis_index("section"), lax.axis_index("dp")
    z, c = lax.div(d, 2), lax.rem(d, 2)
    sx = s + 1 - 2 * lax.rem(s, 2)
    sy = lax.rem(s + 2, SECTIONS)
    sd = SECTIONS - 1 - s
    to_sibling = {"dp": d + 1 - 2 * c}
    to_up, to_down = {"dp": d + 2}, {"dp": d - 2}
    to_x, to_y = {"section": sx}, {"section": sy}
    below, above = z > 0, z < chips - 1
    group = [{"dp": lax.rem(d + step, devices)} for step in range(1, devices)]
    plane = [{"section": lax.rem(s + step, SECTIONS)} for step in range(1, SECTIONS)]
    finish = []

    def when(condition, work):
        if condition is None:
            work()
        else:
            pl.when(condition)(work)

    def push(source, target, send_sem, recv_sem, device):
        pltpu.make_async_remote_copy(
            src_ref=source,
            dst_ref=target,
            send_sem=send_sem,
            recv_sem=recv_sem,
            device_id=device,
            device_id_type=MESH,
        ).start()

    def arrived(target, sem):
        pltpu.make_async_remote_copy(
            src_ref=target, dst_ref=target, send_sem=sem, recv_sem=sem, device_id=to_x, device_id_type=MESH
        ).wait_recv()

    def sent(source, sem):
        pltpu.make_async_remote_copy(
            src_ref=source, dst_ref=source, send_sem=sem, recv_sem=sem, device_id=to_x, device_id_type=MESH
        ).wait_send()

    def at_end(condition, source, sem):
        finish.append((condition, source, sem))

    def aligned(start, size):
        return pl.ds(pl.multiple_of(start, size), size)

    own_x = pltpu.make_async_copy(r.tokens.at[aligned(s * length, length)], r.x.at[0], r.in_s.at[0])
    own_cot = pltpu.make_async_copy(r.cotangent.at[aligned(s * length, length)], r.cot, r.in_s.at[1])
    own_x.start()
    own_cot.start()
    barrier = pltpu.get_barrier_semaphore()
    for peer in group + plane:
        pl.semaphore_signal(barrier, inc=1, device_id=peer, device_id_type=MESH)
    r.cut[...] = r.mat_a[0].astype(LOW).reshape(SECTIONS, rows_a // SECTIONS, hidden)
    r.wa[s, z, c, s] = r.cut[s]
    for layer in range(2):
        r.wb[layer, z, c, :, aligned(s * cols_b, cols_b)] = r.mat_b[layer].astype(LOW)
    norms = r.norms[0].astype(LOW).astype(WIDE)
    nothing = jnp.zeros((2, rows_a), WIDE)
    even = jnp.concatenate([norms, nothing], axis=1)
    odd = jnp.concatenate([nothing, norms], axis=1)
    r.tiles[d, s, 0:2, :] = jnp.where(c == 0, even, odd)
    r.tiles[d, s, 2:8, :] = jnp.zeros((6, LANES), WIDE)
    pl.semaphore_wait(barrier, len(group) + len(plane))

    def small_out(which, source):
        for peer in group:
            push(source, source, r.small_s.at[which, 0], r.small_r.at[which, 0], peer)

    def small_group(which, like):
        arrived(like, r.small_r.at[which, 0])
        sent(like, r.small_s.at[which, 0])

    def small_plane_out(which, source):
        for peer in plane:
            push(source, source, r.small_s.at[which, 1], r.small_r.at[which, 1], peer)

    def small_plane(which, like):
        arrived(like, r.small_r.at[which, 1])
        sent(like, r.small_s.at[which, 1])

    every = slice(None)

    def block(item, chip, section):
        if item < 4:
            return r.wa.at[item, chip, c, section]
        return r.wb.at[item - 4, chip, c, :, aligned(section * cols_b, cols_b)]

    def half_block(item, section, half):
        if item < 4:
            return r.wa.at[item, :, c, section, :, pl.ds(half * hidden // 2, hidden // 2)]
        rows = pl.ds(half * rows_b // 2, rows_b // 2)
        return r.wb.at[item - 4, :, c, rows, aligned(section * cols_b, cols_b)]

    def core_blocks(item, core):
        return r.wa.at[item, :, core] if item < 4 else r.wb.at[item - 4, :, core]

    def cut_out():
        for section, device in ((sd, {"section": sd}), (sx, to_x), (sy, to_y)):
            push(r.cut.at[section], r.wa.at[s, z, c, section], r.cut_s.at[0], r.cut_r.at[s], device)
        at_end(None, r.cut.at[pl.ds(0, SECTIONS - 1)], r.cut_s.at[0])

    def cut_in():
        for section in (sx, sy, sd):
            arrived(r.wa.at[section, z, c, s], r.cut_r.at[section])

    def line_out(item):
        own = block(item, z, s)
        for step in range(1, chips):
            push(own, own, r.gz_s.at[item], r.gz_r.at[item, z], {"dp": 2 * lax.rem(z + step, chips) + c})
        several = block(item, pl.ds(0, chips - 1), s)
        at_end(None, several, r.gz_s.at[item])

    def plane_out(item, chip):
        own = block(item, chip, s)
        push(own, own, r.gx_s.at[item], r.gx_r.at[item], to_x)
        push(own, own, r.gy_s.at[item], r.gy_r.at[item], to_y)

    def line_in(item):
        for step in range(1, chips):
            chip = lax.rem(z + step, chips)
            arrived(block(item, chip, s), r.gz_r.at[item, chip])
            plane_out(item, chip)
        core_out(item, s)
        at_end(None, block(item, every, s), r.gx_s.at[item])
        at_end(None, block(item, every, s), r.gy_s.at[item])

    def core_out(item, section):
        blocks = block(item, every, section)
        push(blocks, blocks, r.gs_s.at[item], r.gs_r.at[item], to_sibling)

    def plane_in(item):
        arrived(block(item, every, sx), r.gx_r.at[item])
        part = half_block(item, sx, 1)
        push(part, part, r.ry_s.at[item], r.ry_r.at[item], to_y)
        arrived(block(item, every, sy), r.gy_r.at[item])
        part = half_block(item, sy, 0)
        push(part, part, r.rx_s.at[item], r.rx_r.at[item], to_x)
        core_out(item, sx)
        core_out(item, sy)
        at_end(None, part, r.ry_s.at[item])
        at_end(None, part, r.rx_s.at[item])

    def far_in(item):
        arrived(half_block(item, sd, 0), r.rx_r.at[item])
        arrived(half_block(item, sd, 1), r.ry_r.at[item])
        core_out(item, sd)
        at_end(None, core_blocks(item, c), r.gs_s.at[item])

    def core_in(item):
        arrived(core_blocks(item, 1 - c), r.gs_r.at[item])

    def product(left, right, dims):
        return lax.dot_general(left, right, (dims, ((), ())), preferred_element_type=WIDE)

    def loop(count, work):
        def one(index, carry):
            work(index)
            return carry

        lax.fori_loop(0, count, one, 0)

    def gain_row(layer, kind):
        parts = [
            r.tiles[2 * chip, layer, kind : kind + 1, :] + r.tiles[2 * chip + 1, layer, kind : kind + 1, :]
            for chip in range(chips)
        ]
        return jnp.concatenate(parts, axis=1)

    def stats(value):
        centre = value - jnp.mean(value, -1, keepdims=True)
        inverse = lax.rsqrt(jnp.mean(centre * centre, -1, keepdims=True) + EPSILON)
        return centre * inverse, inverse

    lane = lax.broadcasted_iota(jnp.int32, (1, 2 * head), 1)
    first_half = (lane < head).astype(WIDE)
    half_masks = (first_half.astype(LOW), (1.0 - first_half).astype(LOW))

    def prepare_masks():
        ends, total = [], jnp.int32(0)
        for slot in range(r.lengths.shape[1]):
            total = total + r.lengths[s, slot]
            ends.append(total)
        down_places = lax.broadcasted_iota(jnp.int32, (length, 1), 0)
        across_places = lax.broadcasted_iota(jnp.int32, (1, length), 1)
        down_segment = jnp.zeros((length, 1), jnp.int32)
        across_segment = jnp.zeros((1, length), jnp.int32)
        for end in ends:
            down_segment = down_segment + (end <= down_places).astype(jnp.int32)
            across_segment = across_segment + (end <= across_places).astype(jnp.int32)
        r.bias[...] = jnp.where(down_segment == across_segment, 0.0, NEGATIVE)
        r.live[...] = (down_places < total).astype(WIDE)

    def matrix(layer, place):
        value = r.wa[layer, :, :, :, :, place]
        return value.reshape(width, value.shape[-1])

    def attention(layer):
        at = layer // 2
        rows = r.x[layer]
        r.xt[layer] = rows.T
        r.q[at] = product(rows, matrix(layer, pl.ds(0, width)), NN).astype(LOW) * jnp.asarray(scale, LOW)
        keys = product(rows, matrix(layer, pl.ds(width, width)), NN).astype(LOW)
        r.k[at] = keys
        r.kt[at] = (keys * jnp.asarray(scale, LOW)).T
        values = product(rows, matrix(layer, pl.ds(2 * width, width)), NN).astype(LOW)
        r.v[at] = values
        r.vt[at] = values.T

        def pair(index):
            lanes = aligned(index * 2 * head, 2 * head)
            for which in range(2):
                scores = product(r.k[at, :, lanes], r.q[at, :, lanes] * half_masks[which], NT) + r.bias[...]
                weights = jnp.exp(scores - jnp.max(scores, 0, keepdims=True))
                probs = (weights * (1.0 / jnp.sum(weights, 0, keepdims=True))).astype(LOW)
                r.pt[at, 2 * index + which] = probs
                place = aligned((2 * index + which) * head, head)
                r.ot[at, place, :] = product(r.vt[at, place, :], probs, NN).astype(LOW)

        def pairs(step):
            pair(2 * step)
            pair(2 * step + 1)

        loop(HEADS // 4, pairs)
        r.f[...] = product(r.ot[at].T, matrix(layer, pl.ds(3 * width, width)), NN)

    def expand(layer):
        at = layer // 2
        r.xt[layer] = r.x[layer].T

        def columns(index):
            place = aligned(index * width, width)
            pre = product(r.x[layer], matrix(layer, place), NN)
            squared = pre * pre
            slope = 0.7978845608 * (1.0 + 3 * 0.044715 * squared)
            bent = jnp.tanh(0.7978845608 * pre * (1.0 + 0.044715 * squared))
            r.g[at, :, place] = (0.5 * pre * (1.0 + bent)).astype(LOW)
            r.slope[at, :, place] = (0.5 * (1.0 + bent) + 0.5 * pre * (1.0 - bent * bent) * slope).astype(LOW)

        loop(hidden // width, columns)

    def contract(layer):
        r.f[...] = product(r.g[layer // 2], r.wb[layer // 2].reshape(hidden, width), NN)

    def by_rows(work):
        loop(length // BLOCK, lambda index: work(aligned(index * BLOCK, BLOCK)))

    def normalize(layer):
        gain, offset = gain_row(layer, 0), gain_row(layer, 1)

        def some(rows):
            branch = r.f[rows, :]
            normal, inverse = stats(r.x[layer, rows, :].astype(WIDE) + branch)
            r.n[layer, rows, :] = normal
            r.inv[layer, rows, :] = inverse
            out = normal * gain + offset
            dual = branch if layer == 0 else r.y[rows, :].astype(WIDE) + branch
            if layer < 3:
                r.x[layer + 1, rows, :] = out.astype(LOW)
                r.y[rows, :] = dual.astype(LOW)
            else:
                dual_normal, dual_inverse = stats(dual)
                r.output[rows, :] = (out + dual_normal).astype(LOW)
                pull = r.cot[rows, :].astype(WIDE) * r.live[rows, :]
                r.gx[rows, :] = pull
                r.gy[rows, :] = norm_back(dual_normal, dual_inverse, pull)

        by_rows(some)

    def back_normalize(layer):
        gain = gain_row(layer, 0)

        def some(index, sums):
            rows = aligned(index * BLOCK, BLOCK)
            upstream = r.gx[rows, :]
            normal = r.n[layer, rows, :]
            summed = norm_back(normal, r.inv[layer, rows, :], upstream * gain)
            dual = r.gy[rows, :]
            r.gx[rows, :] = summed
            r.df[rows, :] = (summed + dual).astype(LOW)
            if layer == 3:
                r.gy[rows, :] = dual.astype(LOW).astype(WIDE)
            return (
                sums[0] + jnp.sum(upstream * normal, 0, keepdims=True),
                sums[1] + jnp.sum(upstream, 0, keepdims=True),
            )

        zero = jnp.zeros((1, width), WIDE)
        gains, offsets = lax.fori_loop(0, length // BLOCK, some, (zero, zero))
        r.ng[d, 2 * layer : 2 * layer + 1, :] = gains
        r.ng[d, 2 * layer + 1 : 2 * layer + 2, :] = offsets

    def pass_down(layer, inner):
        total = r.gx[...] + inner
        if layer > 0:
            r.gx[...] = total.astype(LOW).astype(WIDE)
        else:
            r.input_grad[...] = total

    def keep(name, half, place, value):
        own = getattr(r, "own" + name)
        own[:, :, :, half, :, place] = value.astype(LOW).reshape(
            chips, 2, SECTIONS, rows_a // SECTIONS, value.shape[1]
        )

    def back_contract(layer):
        own = getattr(r, "ownB%d" % (layer // 2))
        r.dft[...] = r.df[...].T

        def owner(index):
            value = product(r.dft[...], r.g[layer // 2, :, aligned(index * rows_b, rows_b)], NN)
            own[lax.div(index, 2), lax.rem(index, 2)] = value.astype(LOW).reshape(SECTIONS, 2, half_b, rows_b)

        loop(devices, owner)

    def back_expand(layer):
        at = layer // 2

        def columns(index):
            place = aligned(index * width, width)
            pulled = product(r.df[...], r.wb[at, index].reshape(width, width), NT)
            pulled = (pulled * r.slope[at, :, place].astype(WIDE)).astype(LOW)
            r.dp[:, place] = pulled
            inner = aligned(lax.rem(index, 2) * width, width)
            keep("F%d" % layer, lax.div(index, 2), inner, product(r.xt[layer], pulled, NN))

        loop(hidden // width, columns)

    def back_expand_end(layer):
        pass_down(layer, product(r.dp[...], matrix(layer, pl.ds(0, hidden)), NT))

    def back_output(layer):
        at = layer // 2
        for half in range(2):
            place = pl.ds(half * width // 2, width // 2)
            keep("O%d" % layer, half, pl.ds(0, width // 2), product(r.ot[at], r.df[:, place], NN))
        r.dm[...] = product(r.df[...], matrix(layer, pl.ds(3 * width, width)), NT).astype(LOW)

    def back_heads(layer, begin, count):
        at = layer // 2

        def pair(index):
            lanes = aligned(index * 2 * head, 2 * head)
            pulled = r.dm[:, lanes]
            keys, values = [], []
            for which in range(2):
                probs = r.pt[at, 2 * index + which]
                grad = product(r.v[at, :, lanes], pulled * half_masks[which], NT)
                full = probs.astype(WIDE)
                centre = jnp.sum(full * grad, 0, keepdims=True)
                scores = (full * (grad - centre)).astype(LOW)
                keys.append(product(scores, r.q[at, :, lanes], NN))
                values.append(product(probs, pulled, NN))
                place = aligned((2 * index + which) * head, head)
                r.dqt[place, :] = product(r.kt[at, place, :], scores, NN).astype(LOW)
            r.dp[:, aligned(width + index * 2 * head, 2 * head)] = jnp.where(
                lane < head, keys[0], keys[1]
            ).astype(LOW)
            r.dp[:, aligned(2 * width + index * 2 * head, 2 * head)] = jnp.where(
                lane < head, values[0], values[1]
            ).astype(LOW)

        def pairs(step):
            pair(begin + 2 * step)
            pair(begin + 2 * step + 1)

        loop(count // 2, pairs)

    def back_packed(layer):
        r.dp[:, 0:width] = r.dqt[...].T
        part = 3 * width // 2
        for half in range(2):
            value = product(r.xt[layer], r.dp[:, half * part : (half + 1) * part], NN)
            keep("K%d" % layer, half, pl.ds(0, part), value)

    def back_packed_end(layer):
        pass_down(layer, product(r.dp[:, 0 : 3 * width], matrix(layer, pl.ds(0, 3 * width)), NT))

    def joined(target, others):
        return functools.reduce(
            lambda left, right: left + right, [ref[...].astype(WIDE) for ref in (target, *others)]
        )

    def add_into(target, others):
        target[...] = joined(target, others).astype(LOW)

    places = {name: place for place, (name, _, _, _) in enumerate(grad_items)}
    by_turn = (sd, sx, sy, s)

    def buffers(name):
        parts = ("own", "sib", "farx", "fary", "nearx", "neary", "line", "done")
        return types.SimpleNamespace(**{part: getattr(r, part + name) for part in parts})

    def to_core(name):
        item, place = buffers(name), places[name]
        for turn, section in enumerate(by_turn):
            push(
                item.own.at[:, 1 - c, section],
                item.sib.at[:, section],
                r.sib_s.at[place, turn],
                r.sib_r.at[place, turn],
                to_sibling,
            )
            at_end(None, item.sib.at[:, 0], r.sib_s.at[place, turn])

    def to_plane(name):
        item, place = buffers(name), places[name]
        own = item.own.at[:, c]

        def over_x(section, half, target, slot):
            push(own.at[:, section, half], target, r.px_s.at[place, slot], r.px_r.at[place, slot], to_x)
            at_end(None, item.farx, r.px_s.at[place, slot])

        def over_y(section, half, target, slot):
            push(own.at[:, section, half], target, r.py_s.at[place, slot], r.py_r.at[place, slot], to_y)
            at_end(None, item.farx, r.py_s.at[place, slot])

        for turn, section in enumerate(by_turn):
            arrived(item.sib.at[:, section], r.sib_r.at[place, turn])
            add_into(own.at[:, section], [item.sib.at[:, section]])
            if turn == 0:
                over_x(sd, 0, item.farx, 2)
                over_y(sd, 1, item.fary, 2)
            elif turn == 1:
                over_x(sx, 0, item.nearx.at[0], 0)
            elif turn == 2:
                over_y(sy, 1, item.neary.at[1], 1)

    def through_plane(name):
        item, place = buffers(name), places[name]
        own = item.own.at[:, c]
        arrived(item.fary, r.py_r.at[place, 2])
        add_into(own.at[:, sx, 1], [item.fary])
        push(own.at[:, sx, 1], item.nearx.at[1], r.px_s.at[place, 1], r.px_r.at[place, 1], to_x)
        at_end(None, item.farx, r.px_s.at[place, 1])
        arrived(item.farx, r.px_r.at[place, 2])
        add_into(own.at[:, sy, 0], [item.farx])
        push(own.at[:, sy, 0], item.neary.at[0], r.py_s.at[place, 0], r.py_r.at[place, 0], to_y)
        at_end(None, item.farx, r.py_s.at[place, 0])

    def to_line(name):
        item, place = buffers(name), places[name]
        own = item.own.at[:, c, s]
        for half in range(2):
            arrived(item.nearx.at[half], r.px_r.at[place, half])
            arrived(item.neary.at[half], r.py_r.at[place, half])
            add_into(own.at[:, half], [item.nearx.at[half], item.neary.at[half]])
        for step in range(1, chips):
            chip = lax.rem(z + step, chips)
            push(
                own.at[chip],
                item.line.at[z],
                r.line_s.at[place, step],
                r.line_r.at[place, z],
                {"dp": 2 * chip + c},
            )
            at_end(None, item.line.at[0], r.line_s.at[place, step])

    def to_owner(name):
        item, place = buffers(name), places[name]
        others = [lax.rem(z + step, chips) for step in range(1, chips)]
        for chip in others:
            arrived(item.line.at[chip], r.line_r.at[place, chip])
        total = joined(item.own.at[z, c, s], [item.line.at[chip] for chip in others])
        square = total * total
        while square.ndim > 2:
            square = jnp.sum(square, 0)
        square = jnp.sum(jnp.sum(square, 0, keepdims=True), 1, keepdims=True)
        r.sum[...] = r.sum[...] + jnp.broadcast_to(square, (8, LANES))
        if name[0] == "B":
            item.done[...] = total
            return
        item.done[s] = total.astype(LOW)
        layer = grad_items[place][1]
        mine = item.done.at[s]
        away = s != layer
        when(
            away,
            lambda: push(mine, mine, r.done_s.at[place], r.done_r.at[place, s], {"section": jnp.int32(layer)}),
        )
        at_end(away, mine, r.done_s.at[place])

    def collect(name):
        item, place = buffers(name), places[name]
        layer = grad_items[place][1]

        def work():
            for section in range(SECTIONS):
                if section != layer:
                    arrived(item.done.at[section], r.done_r.at[place, section])
            columns = item.done.shape[-1]
            start = 3 * width if name[0] == "O" else 0
            for section in range(SECTIONS):
                for half in range(2):
                    rows = pl.ds(section * (rows_a // SECTIONS), rows_a // SECTIONS)
                    place_to = pl.ds(start + half * columns, columns)
                    r.grad_a[rows, place_to] = item.done[section, half].astype(WIDE)

        when(s == layer, work)

    def all_sent():
        for condition, source, sem in finish:
            when(condition, functools.partial(sent, source, sem))
        finish.clear()

    cut_out()
    small_out(0, r.tiles.at[d, s])
    line_out(4)
    plane_out(4, z)
    cut_in()
    for item in (0, 1):
        line_out(item)
        plane_out(item, z)
    for item in (2, 3, 5):
        line_out(item)
    small_group(0, r.tiles.at[pl.ds(0, devices - 1), 0])
    for peer in plane:
        push(r.tiles.at[:, s], r.tiles.at[:, s], r.small_s.at[0, 1], r.small_r.at[0, 1], peer)
    prepare_masks()
    line_in(0)
    line_in(1)
    plane_in(0)
    line_in(4)
    plane_in(1)
    far_in(0)
    for item in (2, 3, 5):
        plane_out(item, z)
    line_in(2)
    own_x.wait()
    own_cot.wait()
    small_plane(0, r.tiles.at[:, pl.ds(0, SECTIONS - 1)])
    core_in(0)
    attention(0)
    far_in(1)
    plane_in(4)
    line_in(3)
    line_in(5)
    normalize(0)
    core_in(1)
    expand(1)
    far_in(4)
    plane_in(2)
    core_in(4)
    contract(1)
    normalize(1)
    far_in(2)
    plane_in(3)
    core_in(2)
    attention(2)
    far_in(3)
    plane_in(5)
    normalize(2)
    core_in(3)
    expand(3)
    far_in(5)
    core_in(5)
    contract(3)
    normalize(3)

    r.sum[...] = jnp.zeros((8, LANES), WIDE)
    back_normalize(3)
    back_contract(3)
    to_core("B1")
    back_expand(3)
    to_core("F3")
    to_plane("B1")
    back_expand_end(3)
    back_normalize(2)
    back_output(2)
    to_core("O2")
    to_plane("F3")
    back_heads(2, 0, 2)
    through_plane("B1")
    to_plane("O2")
    back_heads(2, 2, 2)
    through_plane("F3")
    to_line("B1")
    back_packed(2)
    to_core("K2")
    through_plane("O2")
    back_packed_end(2)
    to_line("F3")
    back_normalize(1)
    to_plane("K2")
    to_owner("B1")
    back_contract(1)
    to_core("B0")
    to_line("O2")
    back_expand(1)
    to_core("F1")
    through_plane("K2")
    to_plane("B0")
    to_owner("F3")
    back_expand_end(1)
    back_normalize(0)
    back_output(0)
    to_core("O0")
    to_plane("F1")
    to_owner("O2")
    to_line("K2")
    back_heads(0, 0, 2)
    through_plane("B0")
    to_plane("O0")
    back_heads(0, 2, 2)
    through_plane("F1")
    to_line("B0")
    to_owner("K2")
    back_packed(0)
    to_core("K0")
    small_out(1, r.ng.at[d])
    through_plane("O0")
    to_line("F1")
    back_packed_end(0)
    to_plane("K0")
    to_owner("B0")
    to_line("O0")
    all_sent()
    through_plane("K0")
    to_owner("F1")
    to_owner("O0")
    small_group(1, r.ng.at[pl.ds(0, devices - 1)])
    r.ns[s] = functools.reduce(lambda left, right: left + right, [r.ng[index] for index in range(devices)])
    small_plane_out(1, r.ns.at[s])
    for name in ("F3", "O2", "K2", "F1"):
        collect(name)
    to_line("K0")
    collect("O0")
    for layer in range(2):
        done = buffers("B%d" % layer).done
        r.grad_b[layer] = done[...].reshape(cols_b, rows_b).T
    small_plane(1, r.ns.at[pl.ds(0, SECTIONS - 1)])
    grads = functools.reduce(lambda left, right: left + right, [r.ns[index] for index in range(SECTIONS)])
    norm_square = jnp.sum(jnp.sum(grads * grads, 0, keepdims=True), 1, keepdims=True)
    chosen = jnp.zeros((2, width), WIDE)
    for layer in range(4):
        chosen = jnp.where(s == layer, grads[2 * layer : 2 * layer + 2, :], chosen)
    for chip in range(chips):
        pair_of = chosen[:, chip * LANES : (chip + 1) * LANES]
        r.grad_n[...] = jnp.where(
            z == chip, jnp.where(c == 0, pair_of[:, :rows_a], pair_of[:, rows_a:]), r.grad_n[...]
        )
    to_owner("K0")

    r.sq[d] = r.sum[...]
    small_out(2, r.sq.at[d])
    collect("K0")
    small_group(2, r.sq.at[pl.ds(0, devices - 1)])
    r.sqs[s] = functools.reduce(lambda left, right: left + right, [r.sq[index] for index in range(devices)])
    small_plane_out(2, r.sqs.at[s])
    all_sent()
    small_plane(2, r.sqs.at[pl.ds(0, SECTIONS - 1)])
    squares = functools.reduce(lambda left, right: left + right, [r.sqs[index] for index in range(SECTIONS)])
    r.square[...] = squares + norm_square


def step_call(tokens, cotangent, lengths, mat_a, mat_b, norms):
    rows_a, hidden = mat_a.shape[1:]
    rows_b, cols_b = mat_b.shape[1:]
    width = tokens.shape[1]
    length = tokens.shape[0] // lengths.shape[0]
    chips = width // rows_a // 2
    scratch = kernel_scratch(chips, rows_a, rows_b, cols_b, length, width, hidden)
    shapes = []
    for _, shape, kind in scratch:
        shapes.append(pltpu.SemaphoreType.DMA(shape) if kind is None else pltpu.VMEM(shape, kind))
    anywhere, vmem = pl.BlockSpec(memory_space=pl.ANY), pl.BlockSpec(memory_space=pltpu.VMEM)
    return pl.pallas_call(
        functools.partial(step_kernel, INPUTS + OUTPUTS + tuple(name for name, _, _ in scratch)),
        out_shape=(
            jax.ShapeDtypeStruct((rows_a, hidden), WIDE),
            jax.ShapeDtypeStruct(mat_b.shape, WIDE),
            jax.ShapeDtypeStruct((2, rows_a), WIDE),
            jax.ShapeDtypeStruct((8, LANES), WIDE),
            jax.ShapeDtypeStruct((length, width), LOW),
            jax.ShapeDtypeStruct((length, width), WIDE),
        ),
        in_specs=[anywhere, anywhere, pl.BlockSpec(memory_space=pltpu.SMEM), vmem, vmem, vmem],
        out_specs=[vmem] * len(OUTPUTS),
        scratch_shapes=shapes,
        compiler_params=pltpu.CompilerParams(
            collective_id=0, has_side_effects=True, vmem_limit_bytes=KERNEL_VMEM
        ),
    )(tokens, cotangent, lengths, mat_a, mat_b, norms)


def update_kernel(*refs):
    square, output, input_grad = (ref[...] for ref in refs[:3])
    grad_norm = jnp.sqrt(square[0:1, 0:1])
    factor = CLIP_NORM / jnp.maximum(grad_norm, CLIP_NORM)
    inputs, outputs = refs[3:15], refs[15:]
    outputs[0][...] = grad_norm
    outputs[1][0] = output
    outputs[2][0] = input_grad
    for group, (rate, decay) in enumerate(
        ((MATRIX_RATE, MATRIX_DECAY), (MATRIX_RATE, MATRIX_DECAY), (NORM_RATE, 0.0))
    ):
        grad, weight, one, two = inputs[4 * group : 4 * group + 4]
        clip = grad[...].reshape(weight.shape) * factor
        moment, square_new, master = adam_update(weight[...], one[...], two[...], clip, rate, decay)
        for ref, value in zip(
            outputs[3 + 5 * group : 8 + 5 * group], (clip, moment, square_new, master, master.astype(LOW))
        ):
            ref[...] = value


def kernel_body(
    tokens, cotangent, lengths, mat_a, mat_b, norms, first_a, second_a, first_b, second_b, first_n, second_n
):
    norms, first_n, second_n = (jnp.swapaxes(value, 1, 2) for value in (norms, first_n, second_n))
    grad_a, grad_b, grad_n, square, output, input_grad = step_call(
        tokens, cotangent, lengths, mat_a, mat_b, norms
    )
    steps = 4

    def cut(value, dim):
        shape = tuple(size // steps if at == dim else size for at, size in enumerate(value.shape))
        return pl.BlockSpec(shape, lambda step: tuple(step if at == dim else 0 for at in range(len(shape))))

    def whole(value):
        return pl.BlockSpec(value.shape, lambda step: (0,) * len(value.shape))

    def like(value, kind=WIDE):
        return jax.ShapeDtypeStruct(value.shape, kind)

    args = (square, output, input_grad, grad_a, mat_a, first_a, second_a, grad_b, mat_b, first_b, second_b)
    specs = [whole(square), cut(output, 0), cut(input_grad, 0)]
    specs += [cut(grad_a, 0)] + [cut(mat_a, 1)] * 3 + [cut(grad_b, 1)] * 4
    args += (grad_n, norms, first_n, second_n)
    specs += [whole(grad_n)] + [whole(norms)] * 3
    shapes = [jax.ShapeDtypeStruct((1, 1), WIDE), like(output[None], LOW), like(input_grad[None])]
    out_specs = [whole(shapes[0]), cut(shapes[1], 1), cut(shapes[2], 1)]
    for value, spec in ((mat_a, cut(mat_a, 1)), (mat_b, cut(mat_b, 1)), (norms, whole(norms))):
        shapes += [like(value)] * 4 + [like(value, LOW)]
        out_specs += [spec] * 5
    results = pl.pallas_call(
        update_kernel,
        grid=(steps,),
        out_shape=shapes,
        in_specs=specs,
        out_specs=out_specs,
        compiler_params=pltpu.CompilerParams(vmem_limit_bytes=KERNEL_VMEM),
    )(*args)
    results = [results[0][0, 0], *results[1:]]
    results[-5:] = [jnp.swapaxes(value, 1, 2) for value in results[-5:]]
    return tuple(results)


def chosen_body(*args):
    rows_a = args[3].shape[1]
    groups = lax.axis_size("dp")
    by_kernel = rows_a % 32 == 0 and 2 * rows_a == LANES and groups * rows_a == args[0].shape[1]
    return (kernel_body if by_kernel else body)(*args)


def solution(mesh):
    placed = (
        P("dp", None),
        P("dp", None),
        P("dp", None),
        P("section", "dp", None),
        P(None, "dp", "section"),
        P("section", "dp", None),
        P("section", "dp", None),
        P("section", "dp", None),
        P(None, "dp", "section"),
        P(None, "dp", "section"),
        P("section", "dp", None),
        P("section", "dp", None),
    )
    return jax.shard_map(
        chosen_body,
        mesh=mesh,
        in_specs=placed,
        out_specs=(
            P(),
            P("section", "dp", None),
            P("section", "dp", None),
            P("section", "dp", None),
            P("section", "dp", None),
            P("section", "dp", None),
            P("section", "dp", None),
            P("section", "dp", None),
            P(None, "dp", "section"),
            P(None, "dp", "section"),
            P(None, "dp", "section"),
            P(None, "dp", "section"),
            P(None, "dp", "section"),
            P("section", "dp", None),
            P("section", "dp", None),
            P("section", "dp", None),
            P("section", "dp", None),
            P("section", "dp", None),
        ),
        check_vma=False,
    )
```

```python
import functools
import types

import jax
import jax.numpy as jnp
from jax import lax
from jax.experimental import pallas as pl
from jax.experimental.pallas import tpu as pltpu
from jax.sharding import PartitionSpec as P

HEADS = 8
STEP = 5


EPSILON = 1e-05
NEGATIVE = -1e30
CLIP_NORM = 1.0
BETA_ONE = 0.5
BETA_TWO = 0.5
ADAM_EPSILON = 1e-08
MATRIX_RATE = 0.05
NORM_RATE = 0.5
MATRIX_DECAY = 0.01


def norm_stats(value):
    centre = value - jnp.mean(value, -1, keepdims=True)
    inverse = lax.rsqrt(jnp.mean(centre * centre, -1, keepdims=True) + EPSILON)
    return (centre * inverse, inverse)


def norm_back(normal, inverse, upstream):
    return inverse * (
        upstream
        - jnp.mean(upstream, -1, keepdims=True)
        - normal * jnp.mean(upstream * normal, -1, keepdims=True)
    )


def adam_update(weight, moment_one, moment_two, gradient, step_rate, decay_rate):
    first_new = BETA_ONE * moment_one + (1.0 - BETA_ONE) * gradient
    second_new = BETA_TWO * moment_two + (1.0 - BETA_TWO) * gradient * gradient
    first_hat = first_new / (1.0 - BETA_ONE**STEP)
    second_hat = second_new / (1.0 - BETA_TWO**STEP)
    weight_new = weight - step_rate * (
        first_hat / (jnp.sqrt(second_hat) + ADAM_EPSILON) + decay_rate * weight
    )
    return (first_new, second_new, weight_new)


def segments_of(lengths_row, length):
    ends = jnp.cumsum(lengths_row, dtype=jnp.int32)
    places = jnp.arange(length, dtype=jnp.int32)
    segment = jnp.sum((ends[None, :] <= places[:, None]).astype(jnp.int32), axis=1, dtype=jnp.int32)
    live = (places < ends[-1]).astype(jnp.float32)
    return segment, live


def matmul(left, right, dims):
    return lax.dot_general(left, right, (dims, ((), ())), preferred_element_type=jnp.float32)


NN = ((1,), (0,))
NT = ((1,), (1,))
TN = ((0,), (0,))


def attention_forward(stream, weight, mask):
    length, width = stream.shape
    size = width // HEADS
    packed = matmul(stream, weight[:, : 3 * width], NN).astype(jnp.bfloat16)
    heads = packed.reshape(length, 3, HEADS, size)
    scores = jnp.einsum("qhd,khd->hqk", heads[:, 0], heads[:, 1], preferred_element_type=jnp.float32)
    scores = jnp.where(mask[None], scores * size**-0.5, NEGATIVE)
    weights = jnp.exp(scores - jnp.max(scores, -1, keepdims=True))
    probs = weights / jnp.sum(weights, -1, keepdims=True)
    mixed = jnp.einsum("hqk,khd->qhd", probs.astype(jnp.bfloat16), heads[:, 2], preferred_element_type=jnp.float32)
    mixed = mixed.reshape(length, width).astype(jnp.bfloat16)
    branch = matmul(mixed, weight[:, 3 * width :], NN)
    return branch, (heads, probs, mixed)


def attention_backward(stream, weight, kept, grad_low):
    heads, probs, mixed = kept
    length, width = stream.shape
    size = width // HEADS
    grad_out = matmul(mixed, grad_low, TN)
    grad_mixed = matmul(grad_low, weight[:, 3 * width :], NT).astype(jnp.bfloat16)
    grad_mixed = grad_mixed.reshape(length, HEADS, size)
    grad_probs = jnp.einsum("qhd,khd->hqk", grad_mixed, heads[:, 2], preferred_element_type=jnp.float32)
    centre = jnp.sum(probs * grad_probs, -1, keepdims=True)
    grad_scores = (probs * (grad_probs - centre)).astype(jnp.bfloat16)
    low = probs.astype(jnp.bfloat16)
    scale = size**-0.5
    grad_q = jnp.einsum("hqk,khd->qhd", grad_scores, heads[:, 1], preferred_element_type=jnp.float32) * scale
    grad_k = jnp.einsum("hqk,qhd->khd", grad_scores, heads[:, 0], preferred_element_type=jnp.float32) * scale
    grad_v = jnp.einsum("hqk,qhd->khd", low, grad_mixed, preferred_element_type=jnp.float32)
    packed = jnp.concatenate([grad_q, grad_k, grad_v], axis=1).reshape(length, 3 * width)
    packed = packed.astype(jnp.bfloat16)
    grad_in = matmul(stream, packed, TN)
    grad_inputs = matmul(packed, weight[:, : 3 * width], NT)
    return grad_inputs, jnp.concatenate([grad_in, grad_out], axis=1)


def feed_forward(stream, weight, down):
    pre = matmul(stream, weight, NN)
    active = jax.nn.gelu(pre, approximate=True).astype(jnp.bfloat16)
    return matmul(active, down, NN), (pre, active)


def feed_backward(stream, weight, down, kept, grad_low):
    pre, active = kept
    grad_down = matmul(active, grad_low, TN)
    grad_active = matmul(grad_low, down, NT)
    pull = jax.vjp(lambda value: jax.nn.gelu(value, approximate=True), pre)[1]
    grad_pre = pull(grad_active)[0].astype(jnp.bfloat16)
    grad_up = matmul(stream, grad_pre, TN)
    return matmul(grad_pre, weight, NT), grad_up, grad_down


def micro_step(rows, pull, segment, mats, downs, gains, biases):
    low = jnp.bfloat16
    mask = segment[:, None] == segment[None, :]
    stream, dual = rows, jnp.zeros_like(rows)
    saved = []
    for sub in range(4):
        if sub % 2 == 0:
            branch, kept = attention_forward(stream, mats[sub], mask)
        else:
            branch, kept = feed_forward(stream, mats[sub], downs[sub // 2])
        normal, inverse = norm_stats(stream.astype(jnp.float32) + branch)
        out = normal * gains[sub] + biases[sub]
        total = dual.astype(jnp.float32) + branch
        saved.append((stream, kept, normal, inverse))
        if sub < 3:
            stream, dual = out.astype(low), total.astype(low)
    dual_normal, dual_inverse = norm_stats(total)
    output = (out + dual_normal).astype(low)
    grad_out, grad_dual = pull, norm_back(dual_normal, dual_inverse, pull)
    grads_a, grads_b, grads_n = [None] * 4, [None] * 2, [None] * 4
    for sub in (3, 2, 1, 0):
        stream, kept, normal, inverse = saved[sub]
        grads_n[sub] = jnp.stack([jnp.sum(grad_out * normal, 0), jnp.sum(grad_out, 0)], axis=1)
        summed = norm_back(normal, inverse, grad_out * gains[sub])
        branch_low = (summed + grad_dual).astype(low)
        if sub % 2 == 0:
            inner, grads_a[sub] = attention_backward(stream, mats[sub], kept, branch_low)
        else:
            inner, grads_a[sub], grads_b[sub // 2] = feed_backward(
                stream, mats[sub], downs[sub // 2], kept, branch_low
            )
        grad_in = summed + inner
        if sub > 0:
            grad_out = grad_in.astype(low).astype(jnp.float32)
            grad_dual = grad_dual.astype(low).astype(jnp.float32)
    return output, grad_in, jnp.stack(grads_a), jnp.stack(grads_b), jnp.stack(grads_n)


def finish_step(grad_norm, output, input_grad, *groups):
    factor = CLIP_NORM / jnp.maximum(grad_norm, CLIP_NORM)
    results = [grad_norm, output[None], input_grad[None]]
    for weight, one, two, grad, rate, decay in groups:
        clip = grad * factor
        moment, square_new, master = adam_update(weight, one, two, clip, rate, decay)
        results += [clip, moment, square_new, master, master.astype(jnp.bfloat16)]
    return tuple(results)


def body(
    tokens, cotangent, lengths, mat_a, mat_b, norms, first_a, second_a, first_b, second_b, first_n, second_n
):
    low = jnp.bfloat16
    own = lax.axis_index("section")
    length = tokens.shape[0] // lengths.shape[0]
    rows = lax.dynamic_slice_in_dim(tokens, own * length, length, 0)
    segment, live = segments_of(lax.dynamic_index_in_dim(lengths, own, 0, keepdims=False), length)
    pull = lax.dynamic_slice_in_dim(cotangent, own * length, length, 0).astype(jnp.float32) * live[:, None]

    def gathered(value):
        return lax.all_gather(lax.all_gather(value, "dp", axis=1, tiled=True), "section", axis=0, tiled=True)

    mats = gathered(mat_a.astype(low))
    scales = gathered(norms.astype(low)).astype(jnp.float32)
    downs = lax.all_gather(mat_b.astype(low), "section", axis=2, tiled=True)
    downs = lax.all_gather(downs, "dp", axis=1, tiled=True)
    output, input_grad, part_a, part_b, part_n = micro_step(
        rows, pull, segment, mats, downs, scales[:, :, 0], scales[:, :, 1]
    )

    def scattered(value, section_dim):
        value = lax.psum_scatter(value, "section", scatter_dimension=section_dim, tiled=True)
        return lax.psum_scatter(value, "dp", scatter_dimension=1, tiled=True).astype(jnp.float32)

    grad_a = scattered(part_a.astype(low), 0)
    grad_b = scattered(part_b.astype(low), 2)
    grad_n = scattered(part_n, 0)
    square = jnp.sum(grad_a * grad_a) + jnp.sum(grad_b * grad_b) + jnp.sum(grad_n * grad_n)
    grad_norm = jnp.sqrt(lax.psum(square, ("section", "dp")))
    return finish_step(
        grad_norm, output, input_grad,
        (mat_a, first_a, second_a, grad_a, MATRIX_RATE, MATRIX_DECAY),
        (mat_b, first_b, second_b, grad_b, MATRIX_RATE, MATRIX_DECAY),
        (norms, first_n, second_n, grad_n, NORM_RATE, 0.0),
    )


LOW = jnp.bfloat16
WIDE = jnp.float32
MESH = pl.DeviceIdType.MESH
SECTIONS = 4
LANES = 128
BLOCK = 64
KERNEL_VMEM = 64 * 1024 * 1024 - 256 * 1024


def gradient_items(rows_a, rows_b, cols_b, width, hidden):
    part = rows_a // SECTIONS
    return (
        ("B1", 3, cols_b // 2, rows_b),
        ("F3", 3, part, hidden // 2),
        ("O2", 2, part, width // 2),
        ("K2", 2, part, 3 * width // 2),
        ("B0", 1, cols_b // 2, rows_b),
        ("F1", 1, part, hidden // 2),
        ("O0", 0, part, width // 2),
        ("K0", 0, part, 3 * width // 2),
    )


def item_scratch(name, chips, rows, columns):
    piece = (rows, columns)
    return (
        ("own" + name, (chips, 2, SECTIONS, 2) + piece, LOW),
        ("sib" + name, (chips, SECTIONS, 2) + piece, LOW),
        ("farx" + name, (chips,) + piece, LOW),
        ("fary" + name, (chips,) + piece, LOW),
        ("nearx" + name, (2, chips) + piece, LOW),
        ("neary" + name, (2, chips) + piece, LOW),
        ("line" + name, (chips, 2) + piece, LOW),
        ("done" + name, (2,) + piece if name[0] == "B" else (SECTIONS, 2) + piece, WIDE if name[0] == "B" else LOW),
    )


def kernel_scratch(chips, rows_a, rows_b, cols_b, length, width, hidden):
    devices = 2 * chips
    items = gradient_items(rows_a, rows_b, cols_b, width, hidden)
    count = len(items)
    received = sum((item_scratch(name, chips, rows, columns) for name, _, rows, columns in items), ())
    return received + (
        ("sib_s", (count, SECTIONS), None),
        ("sib_r", (count, SECTIONS), None),
        ("px_s", (count, 3), None),
        ("px_r", (count, 3), None),
        ("py_s", (count, 3), None),
        ("py_r", (count, 3), None),
        ("line_s", (count, chips), None),
        ("line_r", (count, chips), None),
        ("done_s", (count,), None),
        ("done_r", (count, SECTIONS), None),
        ("wa", (4, width, hidden), LOW),
        ("wb", (2, hidden, width), LOW),
        ("tiles", (devices, SECTIONS, 8, LANES), WIDE),
        ("x", (4, length, width), LOW),
        ("xt", (4, width, length), LOW),
        ("y", (length, width), LOW),
        ("cot", (length, width), LOW),
        ("bias", (length, length), WIDE),
        ("live", (length, 1), WIDE),
        ("f", (length, width), WIDE),
        ("n", (4, length, width), WIDE),
        ("inv", (4, length, 1), WIDE),
        ("q", (2, length, width), LOW),
        ("k", (2, length, width), LOW),
        ("v", (2, length, width), LOW),
        ("kt", (2, width, length), LOW),
        ("vt", (2, width, length), LOW),
        ("ot", (2, width, length), LOW),
        ("pt", (2, HEADS, length, length), LOW),
        ("g", (2, length, hidden), LOW),
        ("slope", (2, length, hidden), LOW),
        ("gx", (length, width), WIDE),
        ("gy", (length, width), WIDE),
        ("df", (length, width), LOW),
        ("dft", (width, length), LOW),
        ("dm", (length, width), LOW),
        ("dqt", (width, length), LOW),
        ("dp", (length, hidden), LOW),
        ("ng", (devices, 8, width), WIDE),
        ("ns", (SECTIONS, 8, width), WIDE),
        ("sq", (devices, 8, LANES), WIDE),
        ("sqs", (SECTIONS, 8, LANES), WIDE),
        ("sum", (8, LANES), WIDE),
        ("in_s", (2,), None),
        ("gz_s", (3, 2, chips, 2), None),
        ("gz_r", (3, chips, 2), None),
        ("gx_s", (3, chips, 2), None),
        ("gx_r", (3, chips, 2), None),
        ("gy_s", (3, chips, 2), None),
        ("gy_r", (3, chips, 2), None),
        ("gxr_s", (3, chips), None),
        ("gxr_r", (3, chips), None),
        ("gyr_s", (3, chips), None),
        ("gyr_r", (3, chips), None),
        ("gs_s", (6,), None),
        ("gs_r", (6,), None),
        ("small_s", (3, 2), None),
        ("small_r", (3, 2), None),
    )


INPUTS = ("tokens", "cotangent", "lengths", "mat_a", "mat_b", "norms")
OUTPUTS = ("grad_a", "grad_b", "grad_n", "square", "output", "input_grad")


def step_kernel(names, *refs):
    r = types.SimpleNamespace(**dict(zip(names, refs)))
    width, hidden = r.wa.shape[1:]
    length = r.x.shape[1]
    rows_a, (rows_b, cols_b) = r.mat_a.shape[1], r.mat_b.shape[1:]
    devices = r.tiles.shape[0]
    chips = devices // 2
    half_a, half_b = rows_a // 2, cols_b // 2
    grad_items = gradient_items(rows_a, rows_b, cols_b, width, hidden)
    head = width // HEADS
    scale = head**-0.5

    s, d = lax.axis_index("section"), lax.axis_index("dp")
    z, c = lax.div(d, 2), lax.rem(d, 2)
    sx = s + 1 - 2 * lax.rem(s, 2)
    sy = lax.rem(s + 2, SECTIONS)
    sd = SECTIONS - 1 - s
    to_sibling = {"dp": d + 1 - 2 * c}
    to_up, to_down = {"dp": d + 2}, {"dp": d - 2}
    to_x, to_y = {"section": sx}, {"section": sy}
    below, above = z > 0, z < chips - 1
    group = [{"dp": lax.rem(d + step, devices)} for step in range(1, devices)]
    plane = [{"section": lax.rem(s + step, SECTIONS)} for step in range(1, SECTIONS)]
    finish = []

    def when(condition, work):
        if condition is None:
            work()
        else:
            pl.when(condition)(work)

    def push(source, target, send_sem, recv_sem, device):
        pltpu.make_async_remote_copy(
            src_ref=source,
            dst_ref=target,
            send_sem=send_sem,
            recv_sem=recv_sem,
            device_id=device,
            device_id_type=MESH,
        ).start()

    def arrived(target, sem):
        pltpu.make_async_remote_copy(
            src_ref=target, dst_ref=target, send_sem=sem, recv_sem=sem, device_id=to_x, device_id_type=MESH
        ).wait_recv()

    def sent(source, sem):
        pltpu.make_async_remote_copy(
            src_ref=source, dst_ref=source, send_sem=sem, recv_sem=sem, device_id=to_x, device_id_type=MESH
        ).wait_send()

    def at_end(condition, source, sem):
        finish.append((condition, source, sem))

    def aligned(start, size):
        return pl.ds(pl.multiple_of(start, size), size)

    own_x = pltpu.make_async_copy(r.tokens.at[aligned(s * length, length)], r.x.at[0], r.in_s.at[0])
    own_cot = pltpu.make_async_copy(r.cotangent.at[aligned(s * length, length)], r.cot, r.in_s.at[1])
    own_x.start()
    own_cot.start()
    barrier = pltpu.get_barrier_semaphore()
    for peer in group + plane:
        pl.semaphore_signal(barrier, inc=1, device_id=peer, device_id_type=MESH)
    r.wa[s, aligned(d * rows_a, rows_a), :] = r.mat_a[0].astype(LOW)
    for layer in range(2):
        r.wb[layer, aligned(d * rows_b, rows_b), aligned(s * cols_b, cols_b)] = r.mat_b[layer].astype(LOW)
    norms = r.norms[0].astype(LOW).astype(WIDE)
    nothing = jnp.zeros((2, rows_a), WIDE)
    even = jnp.concatenate([norms, nothing], axis=1)
    odd = jnp.concatenate([nothing, norms], axis=1)
    r.tiles[d, s, 0:2, :] = jnp.where(c == 0, even, odd)
    r.tiles[d, s, 2:8, :] = jnp.zeros((6, LANES), WIDE)
    pl.semaphore_wait(barrier, len(group) + len(plane))

    def small_out(which, source):
        for peer in group:
            push(source, source, r.small_s.at[which, 0], r.small_r.at[which, 0], peer)

    def small_group(which, like):
        arrived(like, r.small_r.at[which, 0])
        sent(like, r.small_s.at[which, 0])

    def small_plane_out(which, source):
        for peer in plane:
            push(source, source, r.small_s.at[which, 1], r.small_r.at[which, 1], peer)

    def small_plane(which, like):
        arrived(like, r.small_r.at[which, 1])
        sent(like, r.small_s.at[which, 1])

    def block_a(section, chip, half):
        return r.wa.at[section, aligned((2 * chip + c) * rows_a + half * half_a, half_a), :]

    def block_b(layer):
        part = rows_b // 2

        def block(section, chip, half):
            return r.wb.at[
                layer,
                aligned((2 * chip + c) * rows_b + half * part, part),
                aligned(section * cols_b, cols_b),
            ]

        return block

    items = (block_a, block_b(0), block_b(1))

    def to_the_sibling(item, section, chip, half):
        block = items[item](section, chip, half)
        slot = section if item == 0 else 3 + item
        push(block, block, r.gs_s.at[slot], r.gs_r.at[slot], to_sibling)

    def spread_plane(item, chip):
        for half in range(2):
            block = items[item](s, chip, half)
            push(block, block, r.gx_s.at[item, chip, half], r.gx_r.at[item, chip, half], to_x)
            push(block, block, r.gy_s.at[item, chip, half], r.gy_r.at[item, chip, half], to_y)
            to_the_sibling(item, s, chip, half)

    def up(item, chip, half):
        block = items[item](s, chip, half)
        push(block, block, r.gz_s.at[item, 0, chip, half], r.gz_r.at[item, chip, half], to_up)

    def down(item, chip, half):
        block = items[item](s, chip, half)
        push(block, block, r.gz_s.at[item, 1, chip, half], r.gz_r.at[item, chip, half], to_down)

    def start_line(item):
        for half in range(2):
            when(above, lambda: up(item, z, half))
            when(below, lambda: down(item, z, half))

    def line_step(item, step):
        def from_below():
            for half in range(2):
                arrived(items[item](s, z - step, half), r.gz_r.at[item, z - step, half])
                when(above, lambda: up(item, z - step, half))
            spread_plane(item, z - step)

        def from_above():
            for half in range(2):
                arrived(items[item](s, z + step, half), r.gz_r.at[item, z + step, half])
                when(below, lambda: down(item, z + step, half))
            spread_plane(item, z + step)

        when(z >= step, from_below)
        when(z + step < chips, from_above)

    def plane_step(item):
        for chip in range(chips):
            for half in range(2):
                arrived(items[item](sx, chip, half), r.gx_r.at[item, chip, half])
                if half == 1:
                    block = items[item](sx, chip, half)
                    push(block, block, r.gyr_s.at[item, chip], r.gyr_r.at[item, chip], to_y)
                to_the_sibling(item, sx, chip, half)
                arrived(items[item](sy, chip, half), r.gy_r.at[item, chip, half])
                if half == 0:
                    block = items[item](sy, chip, half)
                    push(block, block, r.gxr_s.at[item, chip], r.gxr_r.at[item, chip], to_x)
                to_the_sibling(item, sy, chip, half)

    def relay_step(item):
        for chip in range(chips):
            arrived(items[item](sd, chip, 0), r.gxr_r.at[item, chip])
            to_the_sibling(item, sd, chip, 0)
            arrived(items[item](sd, chip, 1), r.gyr_r.at[item, chip])
            to_the_sibling(item, sd, chip, 1)

    whole_a = r.wa.at[0, pl.ds(0, chips * rows_a)]
    whole_b = r.wb.at[0, pl.ds(0, chips * rows_b)]
    for slot in range(6):
        at_end(None, whole_a if slot < 4 else whole_b, r.gs_s.at[slot])
    for item in range(3):
        for chip in range(chips):
            for half in range(2):
                block = items[item](0, chip, half)
                at_end(None, block, r.gx_s.at[item, chip, half])
                at_end(None, block, r.gy_s.at[item, chip, half])
                at_end(above & (z >= chip), block, r.gz_s.at[item, 0, chip, half])
                at_end(below & (z <= chip), block, r.gz_s.at[item, 1, chip, half])
            block = items[item](0, chip, 0)
            at_end(None, block, r.gxr_s.at[item, chip])
            at_end(None, block, r.gyr_s.at[item, chip])

    def product(left, right, dims):
        return lax.dot_general(left, right, (dims, ((), ())), preferred_element_type=WIDE)

    def loop(count, work):
        def one(index, carry):
            work(index)
            return carry

        lax.fori_loop(0, count, one, 0)

    def gain_row(layer, kind):
        parts = [
            r.tiles[2 * chip, layer, kind : kind + 1, :] + r.tiles[2 * chip + 1, layer, kind : kind + 1, :]
            for chip in range(chips)
        ]
        return jnp.concatenate(parts, axis=1)

    def stats(value):
        centre = value - jnp.mean(value, -1, keepdims=True)
        inverse = lax.rsqrt(jnp.mean(centre * centre, -1, keepdims=True) + EPSILON)
        return centre * inverse, inverse

    lane = lax.broadcasted_iota(jnp.int32, (1, 2 * head), 1)
    first_half = (lane < head).astype(WIDE)
    half_masks = (first_half.astype(LOW), (1.0 - first_half).astype(LOW))

    def prepare_masks():
        ends, total = [], jnp.int32(0)
        for slot in range(r.lengths.shape[1]):
            total = total + r.lengths[s, slot]
            ends.append(total)
        down_places = lax.broadcasted_iota(jnp.int32, (length, 1), 0)
        across_places = lax.broadcasted_iota(jnp.int32, (1, length), 1)
        down_segment = jnp.zeros((length, 1), jnp.int32)
        across_segment = jnp.zeros((1, length), jnp.int32)
        for end in ends:
            down_segment = down_segment + (end <= down_places).astype(jnp.int32)
            across_segment = across_segment + (end <= across_places).astype(jnp.int32)
        r.bias[...] = jnp.where(down_segment == across_segment, 0.0, NEGATIVE)
        r.live[...] = (down_places < total).astype(WIDE)

    def attention(layer):
        at = layer // 2
        rows = r.x[layer]
        r.xt[layer] = rows.T
        r.q[at] = product(rows, r.wa[layer, :, 0:width], NN).astype(LOW) * jnp.asarray(scale, LOW)
        keys = product(rows, r.wa[layer, :, width : 2 * width], NN).astype(LOW)
        r.k[at] = keys
        r.kt[at] = (keys * jnp.asarray(scale, LOW)).T
        values = product(rows, r.wa[layer, :, 2 * width : 3 * width], NN).astype(LOW)
        r.v[at] = values
        r.vt[at] = values.T

        def pair(index):
            lanes = aligned(index * 2 * head, 2 * head)
            for which in range(2):
                scores = product(r.k[at, :, lanes], r.q[at, :, lanes] * half_masks[which], NT) + r.bias[...]
                weights = jnp.exp(scores - jnp.max(scores, 0, keepdims=True))
                probs = (weights * (1.0 / jnp.sum(weights, 0, keepdims=True))).astype(LOW)
                r.pt[at, 2 * index + which] = probs
                place = aligned((2 * index + which) * head, head)
                r.ot[at, place, :] = product(r.vt[at, place, :], probs, NN).astype(LOW)

        def pairs(step):
            pair(2 * step)
            pair(2 * step + 1)

        loop(HEADS // 4, pairs)
        r.f[...] = product(r.ot[at].T, r.wa[layer, :, 3 * width :], NN)

    def expand(layer):
        at = layer // 2
        r.xt[layer] = r.x[layer].T

        def columns(index):
            place = aligned(index * width, width)
            pre = product(r.x[layer], r.wa[layer, :, place], NN)
            squared = pre * pre
            slope = 0.7978845608 * (1.0 + 3 * 0.044715 * squared)
            bent = jnp.tanh(0.7978845608 * pre * (1.0 + 0.044715 * squared))
            r.g[at, :, place] = (0.5 * pre * (1.0 + bent)).astype(LOW)
            r.slope[at, :, place] = (0.5 * (1.0 + bent) + 0.5 * pre * (1.0 - bent * bent) * slope).astype(LOW)

        loop(hidden // width, columns)

    def contract(layer):
        r.f[...] = product(r.g[layer // 2], r.wb[layer // 2], NN)

    def by_rows(work):
        loop(length // BLOCK, lambda index: work(aligned(index * BLOCK, BLOCK)))

    def normalize(layer):
        gain, offset = gain_row(layer, 0), gain_row(layer, 1)

        def some(rows):
            branch = r.f[rows, :]
            normal, inverse = stats(r.x[layer, rows, :].astype(WIDE) + branch)
            r.n[layer, rows, :] = normal
            r.inv[layer, rows, :] = inverse
            out = normal * gain + offset
            dual = branch if layer == 0 else r.y[rows, :].astype(WIDE) + branch
            if layer < 3:
                r.x[layer + 1, rows, :] = out.astype(LOW)
                r.y[rows, :] = dual.astype(LOW)
            else:
                dual_normal, dual_inverse = stats(dual)
                r.output[rows, :] = (out + dual_normal).astype(LOW)
                pull = r.cot[rows, :].astype(WIDE) * r.live[rows, :]
                r.gx[rows, :] = pull
                r.gy[rows, :] = norm_back(dual_normal, dual_inverse, pull)

        by_rows(some)

    def back_normalize(layer):
        gain = gain_row(layer, 0)

        def some(index, sums):
            rows = aligned(index * BLOCK, BLOCK)
            upstream = r.gx[rows, :]
            normal = r.n[layer, rows, :]
            summed = norm_back(normal, r.inv[layer, rows, :], upstream * gain)
            dual = r.gy[rows, :]
            r.gx[rows, :] = summed
            r.df[rows, :] = (summed + dual).astype(LOW)
            if layer == 3:
                r.gy[rows, :] = dual.astype(LOW).astype(WIDE)
            return (
                sums[0] + jnp.sum(upstream * normal, 0, keepdims=True),
                sums[1] + jnp.sum(upstream, 0, keepdims=True),
            )

        zero = jnp.zeros((1, width), WIDE)
        gains, offsets = lax.fori_loop(0, length // BLOCK, some, (zero, zero))
        r.ng[d, 2 * layer : 2 * layer + 1, :] = gains
        r.ng[d, 2 * layer + 1 : 2 * layer + 2, :] = offsets

    def pass_down(layer, inner):
        total = r.gx[...] + inner
        if layer > 0:
            r.gx[...] = total.astype(LOW).astype(WIDE)
        else:
            r.input_grad[...] = total

    def keep(name, half, place, value):
        own = getattr(r, "own" + name)
        own[:, :, :, half, :, place] = value.astype(LOW).reshape(
            chips, 2, SECTIONS, rows_a // SECTIONS, value.shape[1]
        )

    def back_contract(layer):
        own = getattr(r, "ownB%d" % (layer // 2))
        r.dft[...] = r.df[...].T

        def owner(index):
            value = product(r.dft[...], r.g[layer // 2, :, aligned(index * rows_b, rows_b)], NN)
            own[lax.div(index, 2), lax.rem(index, 2)] = value.astype(LOW).reshape(SECTIONS, 2, half_b, rows_b)

        loop(devices, owner)

    def back_expand(layer):
        at = layer // 2

        def columns(index):
            place = aligned(index * width, width)
            pulled = product(r.df[...], r.wb[at, place, :], NT)
            pulled = (pulled * r.slope[at, :, place].astype(WIDE)).astype(LOW)
            r.dp[:, place] = pulled
            inner = aligned(lax.rem(index, 2) * width, width)
            keep("F%d" % layer, lax.div(index, 2), inner, product(r.xt[layer], pulled, NN))

        loop(hidden // width, columns)

    def back_expand_end(layer):
        pass_down(layer, product(r.dp[...], r.wa[layer], NT))

    def back_output(layer):
        at = layer // 2
        for half in range(2):
            place = pl.ds(half * width // 2, width // 2)
            keep("O%d" % layer, half, pl.ds(0, width // 2), product(r.ot[at], r.df[:, place], NN))
        r.dm[...] = product(r.df[...], r.wa[layer, :, 3 * width :], NT).astype(LOW)

    def back_heads(layer, begin, count):
        at = layer // 2

        def pair(index):
            lanes = aligned(index * 2 * head, 2 * head)
            pulled = r.dm[:, lanes]
            keys, values = [], []
            for which in range(2):
                probs = r.pt[at, 2 * index + which]
                grad = product(r.v[at, :, lanes], pulled * half_masks[which], NT)
                full = probs.astype(WIDE)
                centre = jnp.sum(full * grad, 0, keepdims=True)
                scores = (full * (grad - centre)).astype(LOW)
                keys.append(product(scores, r.q[at, :, lanes], NN))
                values.append(product(probs, pulled, NN))
                place = aligned((2 * index + which) * head, head)
                r.dqt[place, :] = product(r.kt[at, place, :], scores, NN).astype(LOW)
            r.dp[:, aligned(width + index * 2 * head, 2 * head)] = jnp.where(
                lane < head, keys[0], keys[1]
            ).astype(LOW)
            r.dp[:, aligned(2 * width + index * 2 * head, 2 * head)] = jnp.where(
                lane < head, values[0], values[1]
            ).astype(LOW)

        def pairs(step):
            pair(begin + 2 * step)
            pair(begin + 2 * step + 1)

        loop(count // 2, pairs)

    def back_packed(layer):
        r.dp[:, 0:width] = r.dqt[...].T
        part = 3 * width // 2
        for half in range(2):
            value = product(r.xt[layer], r.dp[:, half * part : (half + 1) * part], NN)
            keep("K%d" % layer, half, pl.ds(0, part), value)

    def back_packed_end(layer):
        pass_down(layer, product(r.dp[:, 0 : 3 * width], r.wa[layer, :, 0 : 3 * width], NT))

    def joined(target, others):
        return functools.reduce(
            lambda left, right: left + right, [ref[...].astype(WIDE) for ref in (target, *others)]
        )

    def add_into(target, others):
        if len(others) == 1:
            target[...] = target[...] + others[0][...]
        else:
            target[...] = joined(target, others).astype(LOW)

    places = {name: place for place, (name, _, _, _) in enumerate(grad_items)}
    by_turn = (sd, sx, sy, s)

    def buffers(name):
        parts = ("own", "sib", "farx", "fary", "nearx", "neary", "line", "done")
        return types.SimpleNamespace(**{part: getattr(r, part + name) for part in parts})

    def to_core(name):
        item, place = buffers(name), places[name]
        for turn, section in enumerate(by_turn):
            push(
                item.own.at[:, 1 - c, section],
                item.sib.at[:, section],
                r.sib_s.at[place, turn],
                r.sib_r.at[place, turn],
                to_sibling,
            )
            at_end(None, item.sib.at[:, 0], r.sib_s.at[place, turn])

    def to_plane(name):
        item, place = buffers(name), places[name]
        own = item.own.at[:, c]

        def over_x(section, half, target, slot):
            push(own.at[:, section, half], target, r.px_s.at[place, slot], r.px_r.at[place, slot], to_x)
            at_end(None, item.farx, r.px_s.at[place, slot])

        def over_y(section, half, target, slot):
            push(own.at[:, section, half], target, r.py_s.at[place, slot], r.py_r.at[place, slot], to_y)
            at_end(None, item.farx, r.py_s.at[place, slot])

        for turn, section in enumerate(by_turn):
            arrived(item.sib.at[:, section], r.sib_r.at[place, turn])
            add_into(own.at[:, section], [item.sib.at[:, section]])
            if turn == 0:
                over_x(sd, 0, item.farx, 2)
                over_y(sd, 1, item.fary, 2)
            elif turn == 1:
                over_x(sx, 0, item.nearx.at[0], 0)
            elif turn == 2:
                over_y(sy, 1, item.neary.at[1], 1)

    def through_plane(name):
        item, place = buffers(name), places[name]
        own = item.own.at[:, c]
        arrived(item.fary, r.py_r.at[place, 2])
        add_into(own.at[:, sx, 1], [item.fary])
        push(own.at[:, sx, 1], item.nearx.at[1], r.px_s.at[place, 1], r.px_r.at[place, 1], to_x)
        at_end(None, item.farx, r.px_s.at[place, 1])
        arrived(item.farx, r.px_r.at[place, 2])
        add_into(own.at[:, sy, 0], [item.farx])
        push(own.at[:, sy, 0], item.neary.at[0], r.py_s.at[place, 0], r.py_r.at[place, 0], to_y)
        at_end(None, item.farx, r.py_s.at[place, 0])

    def to_line(name):
        item, place = buffers(name), places[name]
        own = item.own.at[:, c, s]
        for half in range(2):
            arrived(item.nearx.at[half], r.px_r.at[place, half])
            arrived(item.neary.at[half], r.py_r.at[place, half])
            add_into(own.at[:, half], [item.nearx.at[half], item.neary.at[half]])
        for step in range(1, chips):
            chip = lax.rem(z + step, chips)
            push(
                own.at[chip],
                item.line.at[z],
                r.line_s.at[place, step],
                r.line_r.at[place, z],
                {"dp": 2 * chip + c},
            )
            at_end(None, item.line.at[0], r.line_s.at[place, step])

    def to_owner(name):
        item, place = buffers(name), places[name]
        others = [lax.rem(z + step, chips) for step in range(1, chips)]
        for chip in others:
            arrived(item.line.at[chip], r.line_r.at[place, chip])
        total = joined(item.own.at[z, c, s], [item.line.at[chip] for chip in others])
        square = total * total
        while square.ndim > 2:
            square = jnp.sum(square, 0)
        square = jnp.sum(jnp.sum(square, 0, keepdims=True), 1, keepdims=True)
        r.sum[...] = r.sum[...] + jnp.broadcast_to(square, (8, LANES))
        if name[0] == "B":
            item.done[...] = total
            return
        item.done[s] = total.astype(LOW)
        layer = grad_items[place][1]
        mine = item.done.at[s]
        away = s != layer
        when(
            away,
            lambda: push(mine, mine, r.done_s.at[place], r.done_r.at[place, s], {"section": jnp.int32(layer)}),
        )
        at_end(away, mine, r.done_s.at[place])

    def collect(name):
        item, place = buffers(name), places[name]
        layer = grad_items[place][1]

        def work():
            for section in range(SECTIONS):
                if section != layer:
                    arrived(item.done.at[section], r.done_r.at[place, section])
            columns = item.done.shape[-1]
            start = 3 * width if name[0] == "O" else 0
            for section in range(SECTIONS):
                for half in range(2):
                    rows = pl.ds(section * (rows_a // SECTIONS), rows_a // SECTIONS)
                    place_to = pl.ds(start + half * columns, columns)
                    r.grad_a[rows, place_to] = item.done[section, half].astype(WIDE)

        when(s == layer, work)

    def all_sent():
        for condition, source, sem in finish:
            when(condition, functools.partial(sent, source, sem))
        finish.clear()

    small_out(0, r.tiles.at[d, s])
    start_line(0)
    spread_plane(0, z)
    line_step(0, 1)
    start_line(1)
    start_line(2)
    for step in range(2, chips):
        line_step(0, step)
    small_group(0, r.tiles.at[pl.ds(0, devices - 1), 0])
    for peer in plane:
        push(r.tiles.at[:, s], r.tiles.at[:, s], r.small_s.at[0, 1], r.small_r.at[0, 1], peer)
    prepare_masks()
    plane_step(0)
    for item in (1, 2):
        spread_plane(item, z)
        for step in range(1, chips):
            line_step(item, step)
    own_x.wait()
    own_cot.wait()
    relay_step(0)
    small_plane(0, r.tiles.at[:, pl.ds(0, SECTIONS - 1)])
    for slot in range(4):
        arrived(whole_a, r.gs_r.at[slot])
    attention(0)
    normalize(0)
    expand(1)
    plane_step(1)
    relay_step(1)
    arrived(whole_b, r.gs_r.at[4])
    contract(1)
    normalize(1)
    plane_step(2)
    attention(2)
    normalize(2)
    expand(3)
    relay_step(2)
    arrived(whole_b, r.gs_r.at[5])
    contract(3)
    normalize(3)

    r.sum[...] = jnp.zeros((8, LANES), WIDE)
    back_normalize(3)
    back_contract(3)
    to_core("B1")
    back_expand(3)
    to_core("F3")
    to_plane("B1")
    back_expand_end(3)
    back_normalize(2)
    back_output(2)
    to_core("O2")
    to_plane("F3")
    back_heads(2, 0, 2)
    through_plane("B1")
    to_plane("O2")
    back_heads(2, 2, 2)
    through_plane("F3")
    to_line("B1")
    back_packed(2)
    to_core("K2")
    through_plane("O2")
    back_packed_end(2)
    to_line("F3")
    back_normalize(1)
    to_plane("K2")
    to_owner("B1")
    back_contract(1)
    to_core("B0")
    to_line("O2")
    back_expand(1)
    to_core("F1")
    through_plane("K2")
    to_plane("B0")
    to_owner("F3")
    back_expand_end(1)
    back_normalize(0)
    back_output(0)
    to_core("O0")
    to_plane("F1")
    to_owner("O2")
    to_line("K2")
    back_heads(0, 0, 2)
    through_plane("B0")
    to_plane("O0")
    back_heads(0, 2, 2)
    through_plane("F1")
    to_line("B0")
    to_owner("K2")
    back_packed(0)
    to_core("K0")
    small_out(1, r.ng.at[d])
    through_plane("O0")
    to_line("F1")
    back_packed_end(0)
    to_plane("K0")
    to_owner("B0")
    to_line("O0")
    all_sent()
    through_plane("K0")
    to_owner("F1")
    to_owner("O0")
    small_group(1, r.ng.at[pl.ds(0, devices - 1)])
    r.ns[s] = functools.reduce(lambda left, right: left + right, [r.ng[index] for index in range(devices)])
    small_plane_out(1, r.ns.at[s])
    for name in ("F3", "O2", "K2", "F1"):
        collect(name)
    to_line("K0")
    collect("O0")
    for layer in range(2):
        done = buffers("B%d" % layer).done
        r.grad_b[layer] = done[...].reshape(cols_b, rows_b).T
    small_plane(1, r.ns.at[pl.ds(0, SECTIONS - 1)])
    grads = functools.reduce(lambda left, right: left + right, [r.ns[index] for index in range(SECTIONS)])
    norm_square = jnp.sum(jnp.sum(grads * grads, 0, keepdims=True), 1, keepdims=True)
    chosen = jnp.zeros((2, width), WIDE)
    for layer in range(4):
        chosen = jnp.where(s == layer, grads[2 * layer : 2 * layer + 2, :], chosen)
    for chip in range(chips):
        pair_of = chosen[:, chip * LANES : (chip + 1) * LANES]
        r.grad_n[...] = jnp.where(
            z == chip, jnp.where(c == 0, pair_of[:, :rows_a], pair_of[:, rows_a:]), r.grad_n[...]
        )
    to_owner("K0")

    r.sq[d] = r.sum[...]
    small_out(2, r.sq.at[d])
    collect("K0")
    small_group(2, r.sq.at[pl.ds(0, devices - 1)])
    r.sqs[s] = functools.reduce(lambda left, right: left + right, [r.sq[index] for index in range(devices)])
    small_plane_out(2, r.sqs.at[s])
    all_sent()
    small_plane(2, r.sqs.at[pl.ds(0, SECTIONS - 1)])
    squares = functools.reduce(lambda left, right: left + right, [r.sqs[index] for index in range(SECTIONS)])
    r.square[...] = squares + norm_square


def step_call(tokens, cotangent, lengths, mat_a, mat_b, norms):
    rows_a, hidden = mat_a.shape[1:]
    rows_b, cols_b = mat_b.shape[1:]
    width = tokens.shape[1]
    length = tokens.shape[0] // lengths.shape[0]
    chips = width // rows_a // 2
    scratch = kernel_scratch(chips, rows_a, rows_b, cols_b, length, width, hidden)
    shapes = []
    for _, shape, kind in scratch:
        shapes.append(pltpu.SemaphoreType.DMA(shape) if kind is None else pltpu.VMEM(shape, kind))
    anywhere, vmem = pl.BlockSpec(memory_space=pl.ANY), pl.BlockSpec(memory_space=pltpu.VMEM)
    return pl.pallas_call(
        functools.partial(step_kernel, INPUTS + OUTPUTS + tuple(name for name, _, _ in scratch)),
        out_shape=(
            jax.ShapeDtypeStruct((rows_a, hidden), WIDE),
            jax.ShapeDtypeStruct(mat_b.shape, WIDE),
            jax.ShapeDtypeStruct((2, rows_a), WIDE),
            jax.ShapeDtypeStruct((8, LANES), WIDE),
            jax.ShapeDtypeStruct((length, width), LOW),
            jax.ShapeDtypeStruct((length, width), WIDE),
        ),
        in_specs=[anywhere, anywhere, pl.BlockSpec(memory_space=pltpu.SMEM), vmem, vmem, vmem],
        out_specs=[vmem] * len(OUTPUTS),
        scratch_shapes=shapes,
        compiler_params=pltpu.CompilerParams(
            collective_id=0, has_side_effects=True, vmem_limit_bytes=KERNEL_VMEM
        ),
    )(tokens, cotangent, lengths, mat_a, mat_b, norms)


def update_kernel(*refs):
    square, output, input_grad = (ref[...] for ref in refs[:3])
    grad_norm = jnp.sqrt(square[0:1, 0:1])
    factor = CLIP_NORM / jnp.maximum(grad_norm, CLIP_NORM)
    inputs, outputs = refs[3:15], refs[15:]
    outputs[0][...] = grad_norm
    outputs[1][0] = output
    outputs[2][0] = input_grad
    for group, (rate, decay) in enumerate(
        ((MATRIX_RATE, MATRIX_DECAY), (MATRIX_RATE, MATRIX_DECAY), (NORM_RATE, 0.0))
    ):
        grad, weight, one, two = inputs[4 * group : 4 * group + 4]
        clip = grad[...].reshape(weight.shape) * factor
        moment, square_new, master = adam_update(weight[...], one[...], two[...], clip, rate, decay)
        for ref, value in zip(
            outputs[3 + 5 * group : 8 + 5 * group], (clip, moment, square_new, master, master.astype(LOW))
        ):
            ref[...] = value


def kernel_body(
    tokens, cotangent, lengths, mat_a, mat_b, norms, first_a, second_a, first_b, second_b, first_n, second_n
):
    norms, first_n, second_n = (jnp.swapaxes(value, 1, 2) for value in (norms, first_n, second_n))
    grad_a, grad_b, grad_n, square, output, input_grad = step_call(
        tokens, cotangent, lengths, mat_a, mat_b, norms
    )
    steps = 4

    def cut(value, dim):
        shape = tuple(size // steps if at == dim else size for at, size in enumerate(value.shape))
        return pl.BlockSpec(shape, lambda step: tuple(step if at == dim else 0 for at in range(len(shape))))

    def whole(value):
        return pl.BlockSpec(value.shape, lambda step: (0,) * len(value.shape))

    def like(value, kind=WIDE):
        return jax.ShapeDtypeStruct(value.shape, kind)

    args = (square, output, input_grad, grad_a, mat_a, first_a, second_a, grad_b, mat_b, first_b, second_b)
    specs = [whole(square), cut(output, 0), cut(input_grad, 0)]
    specs += [cut(grad_a, 0)] + [cut(mat_a, 1)] * 3 + [cut(grad_b, 1)] * 4
    args += (grad_n, norms, first_n, second_n)
    specs += [whole(grad_n)] + [whole(norms)] * 3
    shapes = [jax.ShapeDtypeStruct((1, 1), WIDE), like(output[None], LOW), like(input_grad[None])]
    out_specs = [whole(shapes[0]), cut(shapes[1], 1), cut(shapes[2], 1)]
    for value, spec in ((mat_a, cut(mat_a, 1)), (mat_b, cut(mat_b, 1)), (norms, whole(norms))):
        shapes += [like(value)] * 4 + [like(value, LOW)]
        out_specs += [spec] * 5
    results = pl.pallas_call(
        update_kernel,
        grid=(steps,),
        out_shape=shapes,
        in_specs=specs,
        out_specs=out_specs,
        compiler_params=pltpu.CompilerParams(vmem_limit_bytes=KERNEL_VMEM),
    )(*args)
    results = [results[0][0, 0], *results[1:]]
    results[-5:] = [jnp.swapaxes(value, 1, 2) for value in results[-5:]]
    return tuple(results)


def chosen_body(*args):
    rows_a = args[3].shape[1]
    groups = lax.axis_size("dp")
    by_kernel = rows_a % 32 == 0 and 2 * rows_a == LANES and groups * rows_a == args[0].shape[1]
    return (kernel_body if by_kernel else body)(*args)


def solution(mesh):
    placed = (
        P("dp", None),
        P("dp", None),
        P("dp", None),
        P("section", "dp", None),
        P(None, "dp", "section"),
        P("section", "dp", None),
        P("section", "dp", None),
        P("section", "dp", None),
        P(None, "dp", "section"),
        P(None, "dp", "section"),
        P("section", "dp", None),
        P("section", "dp", None),
    )
    return jax.shard_map(
        chosen_body,
        mesh=mesh,
        in_specs=placed,
        out_specs=(
            P(),
            P("section", "dp", None),
            P("section", "dp", None),
            P("section", "dp", None),
            P("section", "dp", None),
            P("section", "dp", None),
            P("section", "dp", None),
            P("section", "dp", None),
            P(None, "dp", "section"),
            P(None, "dp", "section"),
            P(None, "dp", "section"),
            P(None, "dp", "section"),
            P(None, "dp", "section"),
            P("section", "dp", None),
            P("section", "dp", None),
            P("section", "dp", None),
            P("section", "dp", None),
            P("section", "dp", None),
        ),
        check_vma=False,
    )
```

```python
import functools
import types

import jax
import jax.numpy as jnp
from jax import lax
from jax.experimental import pallas as pl
from jax.experimental.pallas import tpu as pltpu
from jax.sharding import PartitionSpec as P

HEADS = 8
STEP = 5


EPSILON = 1e-05
NEGATIVE = -1e30
CLIP_NORM = 1.0
BETA_ONE = 0.5
BETA_TWO = 0.5
ADAM_EPSILON = 1e-08
MATRIX_RATE = 0.05
NORM_RATE = 0.5
MATRIX_DECAY = 0.01


def norm_stats(value):
    centre = value - jnp.mean(value, -1, keepdims=True)
    inverse = lax.rsqrt(jnp.mean(centre * centre, -1, keepdims=True) + EPSILON)
    return (centre * inverse, inverse)


def norm_back(normal, inverse, upstream):
    return inverse * (
        upstream
        - jnp.mean(upstream, -1, keepdims=True)
        - normal * jnp.mean(upstream * normal, -1, keepdims=True)
    )


def adam_update(weight, moment_one, moment_two, gradient, step_rate, decay_rate):
    first_new = BETA_ONE * moment_one + (1.0 - BETA_ONE) * gradient
    second_new = BETA_TWO * moment_two + (1.0 - BETA_TWO) * gradient * gradient
    first_hat = first_new / (1.0 - BETA_ONE**STEP)
    second_hat = second_new / (1.0 - BETA_TWO**STEP)
    weight_new = weight - step_rate * (
        first_hat / (jnp.sqrt(second_hat) + ADAM_EPSILON) + decay_rate * weight
    )
    return (first_new, second_new, weight_new)


def segments_of(lengths_row, length):
    ends = jnp.cumsum(lengths_row, dtype=jnp.int32)
    places = jnp.arange(length, dtype=jnp.int32)
    segment = jnp.sum((ends[None, :] <= places[:, None]).astype(jnp.int32), axis=1, dtype=jnp.int32)
    live = (places < ends[-1]).astype(jnp.float32)
    return segment, live


def matmul(left, right, dims):
    return lax.dot_general(left, right, (dims, ((), ())), preferred_element_type=jnp.float32)


NN = ((1,), (0,))
NT = ((1,), (1,))
TN = ((0,), (0,))


def attention_forward(stream, weight, mask):
    length, width = stream.shape
    size = width // HEADS
    packed = matmul(stream, weight[:, : 3 * width], NN).astype(jnp.bfloat16)
    heads = packed.reshape(length, 3, HEADS, size)
    scores = jnp.einsum("qhd,khd->hqk", heads[:, 0], heads[:, 1], preferred_element_type=jnp.float32)
    scores = jnp.where(mask[None], scores * size**-0.5, NEGATIVE)
    weights = jnp.exp(scores - jnp.max(scores, -1, keepdims=True))
    probs = weights / jnp.sum(weights, -1, keepdims=True)
    mixed = jnp.einsum("hqk,khd->qhd", probs.astype(jnp.bfloat16), heads[:, 2], preferred_element_type=jnp.float32)
    mixed = mixed.reshape(length, width).astype(jnp.bfloat16)
    branch = matmul(mixed, weight[:, 3 * width :], NN)
    return branch, (heads, probs, mixed)


def attention_backward(stream, weight, kept, grad_low):
    heads, probs, mixed = kept
    length, width = stream.shape
    size = width // HEADS
    grad_out = matmul(mixed, grad_low, TN)
    grad_mixed = matmul(grad_low, weight[:, 3 * width :], NT).astype(jnp.bfloat16)
    grad_mixed = grad_mixed.reshape(length, HEADS, size)
    grad_probs = jnp.einsum("qhd,khd->hqk", grad_mixed, heads[:, 2], preferred_element_type=jnp.float32)
    centre = jnp.sum(probs * grad_probs, -1, keepdims=True)
    grad_scores = (probs * (grad_probs - centre)).astype(jnp.bfloat16)
    low = probs.astype(jnp.bfloat16)
    scale = size**-0.5
    grad_q = jnp.einsum("hqk,khd->qhd", grad_scores, heads[:, 1], preferred_element_type=jnp.float32) * scale
    grad_k = jnp.einsum("hqk,qhd->khd", grad_scores, heads[:, 0], preferred_element_type=jnp.float32) * scale
    grad_v = jnp.einsum("hqk,qhd->khd", low, grad_mixed, preferred_element_type=jnp.float32)
    packed = jnp.concatenate([grad_q, grad_k, grad_v], axis=1).reshape(length, 3 * width)
    packed = packed.astype(jnp.bfloat16)
    grad_in = matmul(stream, packed, TN)
    grad_inputs = matmul(packed, weight[:, : 3 * width], NT)
    return grad_inputs, jnp.concatenate([grad_in, grad_out], axis=1)


def feed_forward(stream, weight, down):
    pre = matmul(stream, weight, NN)
    active = jax.nn.gelu(pre, approximate=True).astype(jnp.bfloat16)
    return matmul(active, down, NN), (pre, active)


def feed_backward(stream, weight, down, kept, grad_low):
    pre, active = kept
    grad_down = matmul(active, grad_low, TN)
    grad_active = matmul(grad_low, down, NT)
    pull = jax.vjp(lambda value: jax.nn.gelu(value, approximate=True), pre)[1]
    grad_pre = pull(grad_active)[0].astype(jnp.bfloat16)
    grad_up = matmul(stream, grad_pre, TN)
    return matmul(grad_pre, weight, NT), grad_up, grad_down


def micro_step(rows, pull, segment, mats, downs, gains, biases):
    low = jnp.bfloat16
    mask = segment[:, None] == segment[None, :]
    stream, dual = rows, jnp.zeros_like(rows)
    saved = []
    for sub in range(4):
        if sub % 2 == 0:
            branch, kept = attention_forward(stream, mats[sub], mask)
        else:
            branch, kept = feed_forward(stream, mats[sub], downs[sub // 2])
        normal, inverse = norm_stats(stream.astype(jnp.float32) + branch)
        out = normal * gains[sub] + biases[sub]
        total = dual.astype(jnp.float32) + branch
        saved.append((stream, kept, normal, inverse))
        if sub < 3:
            stream, dual = out.astype(low), total.astype(low)
    dual_normal, dual_inverse = norm_stats(total)
    output = (out + dual_normal).astype(low)
    grad_out, grad_dual = pull, norm_back(dual_normal, dual_inverse, pull)
    grads_a, grads_b, grads_n = [None] * 4, [None] * 2, [None] * 4
    for sub in (3, 2, 1, 0):
        stream, kept, normal, inverse = saved[sub]
        grads_n[sub] = jnp.stack([jnp.sum(grad_out * normal, 0), jnp.sum(grad_out, 0)], axis=1)
        summed = norm_back(normal, inverse, grad_out * gains[sub])
        branch_low = (summed + grad_dual).astype(low)
        if sub % 2 == 0:
            inner, grads_a[sub] = attention_backward(stream, mats[sub], kept, branch_low)
        else:
            inner, grads_a[sub], grads_b[sub // 2] = feed_backward(
                stream, mats[sub], downs[sub // 2], kept, branch_low
            )
        grad_in = summed + inner
        if sub > 0:
            grad_out = grad_in.astype(low).astype(jnp.float32)
            grad_dual = grad_dual.astype(low).astype(jnp.float32)
    return output, grad_in, jnp.stack(grads_a), jnp.stack(grads_b), jnp.stack(grads_n)


def finish_step(grad_norm, output, input_grad, *groups):
    factor = CLIP_NORM / jnp.maximum(grad_norm, CLIP_NORM)
    results = [grad_norm, output[None], input_grad[None]]
    for weight, one, two, grad, rate, decay in groups:
        clip = grad * factor
        moment, square_new, master = adam_update(weight, one, two, clip, rate, decay)
        results += [clip, moment, square_new, master, master.astype(jnp.bfloat16)]
    return tuple(results)


def body(
    tokens, cotangent, lengths, mat_a, mat_b, norms, first_a, second_a, first_b, second_b, first_n, second_n
):
    low = jnp.bfloat16
    own = lax.axis_index("section")
    length = tokens.shape[0] // lengths.shape[0]
    rows = lax.dynamic_slice_in_dim(tokens, own * length, length, 0)
    segment, live = segments_of(lax.dynamic_index_in_dim(lengths, own, 0, keepdims=False), length)
    pull = lax.dynamic_slice_in_dim(cotangent, own * length, length, 0).astype(jnp.float32) * live[:, None]

    def gathered(value):
        return lax.all_gather(lax.all_gather(value, "dp", axis=1, tiled=True), "section", axis=0, tiled=True)

    mats = gathered(mat_a.astype(low))
    scales = gathered(norms.astype(low)).astype(jnp.float32)
    downs = lax.all_gather(mat_b.astype(low), "section", axis=2, tiled=True)
    downs = lax.all_gather(downs, "dp", axis=1, tiled=True)
    output, input_grad, part_a, part_b, part_n = micro_step(
        rows, pull, segment, mats, downs, scales[:, :, 0], scales[:, :, 1]
    )

    def scattered(value, section_dim):
        value = lax.psum_scatter(value, "section", scatter_dimension=section_dim, tiled=True)
        return lax.psum_scatter(value, "dp", scatter_dimension=1, tiled=True).astype(jnp.float32)

    grad_a = scattered(part_a.astype(low), 0)
    grad_b = scattered(part_b.astype(low), 2)
    grad_n = scattered(part_n, 0)
    square = jnp.sum(grad_a * grad_a) + jnp.sum(grad_b * grad_b) + jnp.sum(grad_n * grad_n)
    grad_norm = jnp.sqrt(lax.psum(square, ("section", "dp")))
    return finish_step(
        grad_norm, output, input_grad,
        (mat_a, first_a, second_a, grad_a, MATRIX_RATE, MATRIX_DECAY),
        (mat_b, first_b, second_b, grad_b, MATRIX_RATE, MATRIX_DECAY),
        (norms, first_n, second_n, grad_n, NORM_RATE, 0.0),
    )


LOW = jnp.bfloat16
WIDE = jnp.float32
MESH = pl.DeviceIdType.MESH
SECTIONS = 4
LANES = 128
BLOCK = 64
KERNEL_VMEM = 64 * 1024 * 1024 - 256 * 1024


def gradient_items(rows_a, rows_b, cols_b, width, hidden):
    part = rows_a // SECTIONS
    return (
        ("B1", 3, cols_b // 2, rows_b),
        ("F3", 3, part, hidden // 2),
        ("O2", 2, part, width // 2),
        ("K2", 2, part, 3 * width // 2),
        ("B0", 1, cols_b // 2, rows_b),
        ("F1", 1, part, hidden // 2),
        ("O0", 0, part, width // 2),
        ("K0", 0, part, 3 * width // 2),
    )


def item_scratch(name, chips, rows, columns):
    piece = (rows, columns)
    return (
        ("own" + name, (chips, 2, SECTIONS, 2) + piece, LOW),
        ("sib" + name, (chips, SECTIONS, 2) + piece, LOW),
        ("farx" + name, (chips,) + piece, LOW),
        ("fary" + name, (chips,) + piece, LOW),
        ("nearx" + name, (2, chips) + piece, LOW),
        ("neary" + name, (2, chips) + piece, LOW),
        ("line" + name, (chips, 2) + piece, LOW),
        ("done" + name, (2,) + piece if name[0] == "B" else (SECTIONS, 2) + piece, WIDE if name[0] == "B" else LOW),
    )


def kernel_scratch(chips, rows_a, rows_b, cols_b, length, width, hidden):
    devices = 2 * chips
    items = gradient_items(rows_a, rows_b, cols_b, width, hidden)
    count = len(items)
    received = sum((item_scratch(name, chips, rows, columns) for name, _, rows, columns in items), ())
    return received + (
        ("sib_s", (count, SECTIONS), None),
        ("sib_r", (count, SECTIONS), None),
        ("px_s", (count, 3), None),
        ("px_r", (count, 3), None),
        ("py_s", (count, 3), None),
        ("py_r", (count, 3), None),
        ("line_s", (count, chips), None),
        ("line_r", (count, chips), None),
        ("done_s", (count,), None),
        ("done_r", (count, SECTIONS), None),
        ("wa", (4, width, hidden), LOW),
        ("wb", (2, hidden, width), LOW),
        ("tiles", (devices, SECTIONS, 8, LANES), WIDE),
        ("x", (4, length, width), LOW),
        ("xt", (4, width, length), LOW),
        ("y", (length, width), LOW),
        ("cot", (length, width), LOW),
        ("bias", (length, length), WIDE),
        ("live", (length, 1), WIDE),
        ("f", (length, width), WIDE),
        ("n", (4, length, width), WIDE),
        ("inv", (4, length, 1), WIDE),
        ("q", (2, length, width), LOW),
        ("k", (2, length, width), LOW),
        ("v", (2, length, width), LOW),
        ("kt", (2, width, length), LOW),
        ("vt", (2, width, length), LOW),
        ("ot", (2, width, length), LOW),
        ("pt", (2, HEADS, length, length), LOW),
        ("g", (2, length, hidden), LOW),
        ("slope", (2, length, hidden), LOW),
        ("gx", (length, width), WIDE),
        ("gy", (length, width), WIDE),
        ("df", (length, width), LOW),
        ("dft", (width, length), LOW),
        ("dm", (length, width), LOW),
        ("dqt", (width, length), LOW),
        ("dp", (length, hidden), LOW),
        ("ng", (devices, 8, width), WIDE),
        ("ns", (SECTIONS, 8, width), WIDE),
        ("sq", (devices, 8, LANES), WIDE),
        ("sqs", (SECTIONS, 8, LANES), WIDE),
        ("sum", (8, LANES), WIDE),
        ("in_s", (2,), None),
        ("gz_s", (3, 2, chips, 2), None),
        ("gz_r", (3, chips, 2), None),
        ("gx_s", (3, chips, 2), None),
        ("gx_r", (3, chips, 2), None),
        ("gy_s", (3, chips, 2), None),
        ("gy_r", (3, chips, 2), None),
        ("gxr_s", (3, chips), None),
        ("gxr_r", (3, chips), None),
        ("gyr_s", (3, chips), None),
        ("gyr_r", (3, chips), None),
        ("gs_s", (6,), None),
        ("gs_r", (6,), None),
        ("small_s", (3, 2), None),
        ("small_r", (3, 2), None),
    )


INPUTS = ("tokens", "cotangent", "lengths", "mat_a", "mat_b", "norms")
OUTPUTS = ("grad_a", "grad_b", "grad_n", "square", "output", "input_grad")


def step_kernel(names, *refs):
    r = types.SimpleNamespace(**dict(zip(names, refs)))
    width, hidden = r.wa.shape[1:]
    length = r.x.shape[1]
    rows_a, (rows_b, cols_b) = r.mat_a.shape[1], r.mat_b.shape[1:]
    devices = r.tiles.shape[0]
    chips = devices // 2
    half_a, half_b = rows_a // 2, cols_b // 2
    grad_items = gradient_items(rows_a, rows_b, cols_b, width, hidden)
    head = width // HEADS
    scale = head**-0.5

    s, d = lax.axis_index("section"), lax.axis_index("dp")
    z, c = lax.div(d, 2), lax.rem(d, 2)
    sx = s + 1 - 2 * lax.rem(s, 2)
    sy = lax.rem(s + 2, SECTIONS)
    sd = SECTIONS - 1 - s
    to_sibling = {"dp": d + 1 - 2 * c}
    to_up, to_down = {"dp": d + 2}, {"dp": d - 2}
    to_x, to_y = {"section": sx}, {"section": sy}
    below, above = z > 0, z < chips - 1
    group = [{"dp": lax.rem(d + step, devices)} for step in range(1, devices)]
    plane = [{"section": lax.rem(s + step, SECTIONS)} for step in range(1, SECTIONS)]
    finish = []

    def when(condition, work):
        if condition is None:
            work()
        else:
            pl.when(condition)(work)

    def push(source, target, send_sem, recv_sem, device):
        pltpu.make_async_remote_copy(
            src_ref=source,
            dst_ref=target,
            send_sem=send_sem,
            recv_sem=recv_sem,
            device_id=device,
            device_id_type=MESH,
        ).start()

    def arrived(target, sem):
        pltpu.make_async_remote_copy(
            src_ref=target, dst_ref=target, send_sem=sem, recv_sem=sem, device_id=to_x, device_id_type=MESH
        ).wait_recv()

    def sent(source, sem):
        pltpu.make_async_remote_copy(
            src_ref=source, dst_ref=source, send_sem=sem, recv_sem=sem, device_id=to_x, device_id_type=MESH
        ).wait_send()

    def at_end(condition, source, sem):
        finish.append((condition, source, sem))

    def aligned(start, size):
        return pl.ds(pl.multiple_of(start, size), size)

    own_x = pltpu.make_async_copy(r.tokens.at[aligned(s * length, length)], r.x.at[0], r.in_s.at[0])
    own_cot = pltpu.make_async_copy(r.cotangent.at[aligned(s * length, length)], r.cot, r.in_s.at[1])
    own_x.start()
    own_cot.start()
    barrier = pltpu.get_barrier_semaphore()
    for peer in group + plane:
        pl.semaphore_signal(barrier, inc=1, device_id=peer, device_id_type=MESH)
    r.wa[s, aligned(d * rows_a, rows_a), :] = r.mat_a[0].astype(LOW)
    for layer in range(2):
        r.wb[layer, aligned(d * rows_b, rows_b), aligned(s * cols_b, cols_b)] = r.mat_b[layer].astype(LOW)
    norms = r.norms[0].astype(LOW).astype(WIDE)
    nothing = jnp.zeros((2, rows_a), WIDE)
    even = jnp.concatenate([norms, nothing], axis=1)
    odd = jnp.concatenate([nothing, norms], axis=1)
    r.tiles[d, s, 0:2, :] = jnp.where(c == 0, even, odd)
    r.tiles[d, s, 2:8, :] = jnp.zeros((6, LANES), WIDE)
    pl.semaphore_wait(barrier, len(group) + len(plane))

    def small_out(which, source):
        for peer in group:
            push(source, source, r.small_s.at[which, 0], r.small_r.at[which, 0], peer)

    def small_group(which, like):
        arrived(like, r.small_r.at[which, 0])
        sent(like, r.small_s.at[which, 0])

    def small_plane_out(which, source):
        for peer in plane:
            push(source, source, r.small_s.at[which, 1], r.small_r.at[which, 1], peer)

    def small_plane(which, like):
        arrived(like, r.small_r.at[which, 1])
        sent(like, r.small_s.at[which, 1])

    def block_a(section, chip, half):
        return r.wa.at[section, aligned((2 * chip + c) * rows_a + half * half_a, half_a), :]

    def block_b(layer):
        part = rows_b // 2

        def block(section, chip, half):
            return r.wb.at[
                layer,
                aligned((2 * chip + c) * rows_b + half * part, part),
                aligned(section * cols_b, cols_b),
            ]

        return block

    items = (block_a, block_b(0), block_b(1))

    def to_the_sibling(item, section, chip, half):
        block = items[item](section, chip, half)
        slot = section if item == 0 else 3 + item
        push(block, block, r.gs_s.at[slot], r.gs_r.at[slot], to_sibling)

    def spread_plane(item, chip):
        for half in range(2):
            block = items[item](s, chip, half)
            push(block, block, r.gx_s.at[item, chip, half], r.gx_r.at[item, chip, half], to_x)
            push(block, block, r.gy_s.at[item, chip, half], r.gy_r.at[item, chip, half], to_y)
            to_the_sibling(item, s, chip, half)

    def up(item, chip, half):
        block = items[item](s, chip, half)
        push(block, block, r.gz_s.at[item, 0, chip, half], r.gz_r.at[item, chip, half], to_up)

    def down(item, chip, half):
        block = items[item](s, chip, half)
        push(block, block, r.gz_s.at[item, 1, chip, half], r.gz_r.at[item, chip, half], to_down)

    def start_line(item):
        for half in range(2):
            when(above, lambda: up(item, z, half))
            when(below, lambda: down(item, z, half))

    def line_step(item, step):
        def from_below():
            for half in range(2):
                arrived(items[item](s, z - step, half), r.gz_r.at[item, z - step, half])
                when(above, lambda: up(item, z - step, half))
            spread_plane(item, z - step)

        def from_above():
            for half in range(2):
                arrived(items[item](s, z + step, half), r.gz_r.at[item, z + step, half])
                when(below, lambda: down(item, z + step, half))
            spread_plane(item, z + step)

        when(z >= step, from_below)
        when(z + step < chips, from_above)

    def plane_step(item):
        for chip in range(chips):
            for half in range(2):
                arrived(items[item](sx, chip, half), r.gx_r.at[item, chip, half])
                if half == 1:
                    block = items[item](sx, chip, half)
                    push(block, block, r.gyr_s.at[item, chip], r.gyr_r.at[item, chip], to_y)
                to_the_sibling(item, sx, chip, half)
                arrived(items[item](sy, chip, half), r.gy_r.at[item, chip, half])
                if half == 0:
                    block = items[item](sy, chip, half)
                    push(block, block, r.gxr_s.at[item, chip], r.gxr_r.at[item, chip], to_x)
                to_the_sibling(item, sy, chip, half)

    def relay_step(item):
        for chip in range(chips):
            arrived(items[item](sd, chip, 0), r.gxr_r.at[item, chip])
            to_the_sibling(item, sd, chip, 0)
            arrived(items[item](sd, chip, 1), r.gyr_r.at[item, chip])
            to_the_sibling(item, sd, chip, 1)

    whole_a = r.wa.at[0, pl.ds(0, chips * rows_a)]
    whole_b = r.wb.at[0, pl.ds(0, chips * rows_b)]
    for slot in range(6):
        at_end(None, whole_a if slot < 4 else whole_b, r.gs_s.at[slot])
    for item in (0, 2):
        for chip in range(chips):
            for half in range(2):
                block = items[item](0, chip, half)
                at_end(None, block, r.gx_s.at[item, chip, half])
                at_end(None, block, r.gy_s.at[item, chip, half])
                at_end(above & (z >= chip), block, r.gz_s.at[item, 0, chip, half])
                at_end(below & (z <= chip), block, r.gz_s.at[item, 1, chip, half])
            block = items[item](0, chip, 0)
            at_end(None, block, r.gxr_s.at[item, chip])
            at_end(None, block, r.gyr_s.at[item, chip])

    def row_block(chip, half):
        part = rows_b // 2
        return r.wb.at[0, aligned((2 * chip + c) * rows_b + half * part, part), :]

    def rows_to_sibling(chip, half):
        push(row_block(chip, half), row_block(chip, half), r.gs_s.at[4], r.gs_r.at[4], to_sibling)

    def rows_up(chip, half):
        rows = row_block(chip, half)
        push(rows, rows, r.gz_s.at[1, 0, chip, half], r.gz_r.at[1, chip, half], to_up)

    def rows_down(chip, half):
        rows = row_block(chip, half)
        push(rows, rows, r.gz_s.at[1, 1, chip, half], r.gz_r.at[1, chip, half], to_down)

    def rows_plane():
        for half in range(2):
            block = items[1](s, z, half)
            push(block, block, r.gx_s.at[1, 0, half], r.gx_r.at[1, 0, half], to_x)
            push(block, block, r.gy_s.at[1, 0, half], r.gy_r.at[1, 0, half], to_y)
            at_end(None, block, r.gx_s.at[1, 0, half])
            at_end(None, block, r.gy_s.at[1, 0, half])

    def rows_relay():
        for half in range(2):
            arrived(items[1](sx, z, half), r.gx_r.at[1, 0, half])
            arrived(items[1](sy, z, half), r.gy_r.at[1, 0, half])
        block = items[1](sx, z, 1)
        push(block, block, r.gyr_s.at[1, 0], r.gyr_r.at[1, 0], to_y)
        block = items[1](sy, z, 0)
        push(block, block, r.gxr_s.at[1, 0], r.gxr_r.at[1, 0], to_x)
        at_end(None, block, r.gyr_s.at[1, 0])
        at_end(None, block, r.gxr_s.at[1, 0])

    def rows_line():
        for half, sem in ((0, r.gxr_r), (1, r.gyr_r)):
            arrived(items[1](sd, z, half), sem.at[1, 0])
            when(above, lambda: rows_up(z, half))
            when(below, lambda: rows_down(z, half))
            rows_to_sibling(z, half)
        for chip in range(chips):
            for half in range(2):
                at_end(above & (z >= chip), row_block(chip, half), r.gz_s.at[1, 0, chip, half])
                at_end(below & (z <= chip), row_block(chip, half), r.gz_s.at[1, 1, chip, half])

    def rows_step(step):
        def from_below():
            for half in range(2):
                arrived(row_block(z - step, half), r.gz_r.at[1, z - step, half])
                when(above, lambda: rows_up(z - step, half))
                rows_to_sibling(z - step, half)

        def from_above():
            for half in range(2):
                arrived(row_block(z + step, half), r.gz_r.at[1, z + step, half])
                when(below, lambda: rows_down(z + step, half))
                rows_to_sibling(z + step, half)

        when(z >= step, from_below)
        when(z + step < chips, from_above)

    def product(left, right, dims):
        return lax.dot_general(left, right, (dims, ((), ())), preferred_element_type=WIDE)

    def loop(count, work):
        def one(index, carry):
            work(index)
            return carry

        lax.fori_loop(0, count, one, 0)

    def gain_row(layer, kind):
        parts = [
            r.tiles[2 * chip, layer, kind : kind + 1, :] + r.tiles[2 * chip + 1, layer, kind : kind + 1, :]
            for chip in range(chips)
        ]
        return jnp.concatenate(parts, axis=1)

    def stats(value):
        centre = value - jnp.mean(value, -1, keepdims=True)
        inverse = lax.rsqrt(jnp.mean(centre * centre, -1, keepdims=True) + EPSILON)
        return centre * inverse, inverse

    lane = lax.broadcasted_iota(jnp.int32, (1, 2 * head), 1)
    first_half = (lane < head).astype(WIDE)
    half_masks = (first_half.astype(LOW), (1.0 - first_half).astype(LOW))

    def prepare_masks():
        ends, total = [], jnp.int32(0)
        for slot in range(r.lengths.shape[1]):
            total = total + r.lengths[s, slot]
            ends.append(total)
        down_places = lax.broadcasted_iota(jnp.int32, (length, 1), 0)
        across_places = lax.broadcasted_iota(jnp.int32, (1, length), 1)
        down_segment = jnp.zeros((length, 1), jnp.int32)
        across_segment = jnp.zeros((1, length), jnp.int32)
        for end in ends:
            down_segment = down_segment + (end <= down_places).astype(jnp.int32)
            across_segment = across_segment + (end <= across_places).astype(jnp.int32)
        r.bias[...] = jnp.where(down_segment == across_segment, 0.0, NEGATIVE)
        r.live[...] = (down_places < total).astype(WIDE)

    def attention(layer):
        at = layer // 2
        rows = r.x[layer]
        r.xt[layer] = rows.T
        r.q[at] = product(rows, r.wa[layer, :, 0:width], NN).astype(LOW) * jnp.asarray(scale, LOW)
        keys = product(rows, r.wa[layer, :, width : 2 * width], NN).astype(LOW)
        r.k[at] = keys
        r.kt[at] = (keys * jnp.asarray(scale, LOW)).T
        values = product(rows, r.wa[layer, :, 2 * width : 3 * width], NN).astype(LOW)
        r.v[at] = values
        r.vt[at] = values.T

        def pair(index):
            lanes = aligned(index * 2 * head, 2 * head)
            for which in range(2):
                scores = product(r.k[at, :, lanes], r.q[at, :, lanes] * half_masks[which], NT) + r.bias[...]
                weights = jnp.exp(scores - jnp.max(scores, 0, keepdims=True))
                probs = (weights * (1.0 / jnp.sum(weights, 0, keepdims=True))).astype(LOW)
                r.pt[at, 2 * index + which] = probs
                place = aligned((2 * index + which) * head, head)
                r.ot[at, place, :] = product(r.vt[at, place, :], probs, NN).astype(LOW)

        def pairs(step):
            pair(2 * step)
            pair(2 * step + 1)

        loop(HEADS // 4, pairs)
        r.f[...] = product(r.ot[at].T, r.wa[layer, :, 3 * width :], NN)

    def expand(layer):
        at = layer // 2
        r.xt[layer] = r.x[layer].T

        def columns(index):
            place = aligned(index * width, width)
            pre = product(r.x[layer], r.wa[layer, :, place], NN)
            squared = pre * pre
            slope = 0.7978845608 * (1.0 + 3 * 0.044715 * squared)
            bent = jnp.tanh(0.7978845608 * pre * (1.0 + 0.044715 * squared))
            r.g[at, :, place] = (0.5 * pre * (1.0 + bent)).astype(LOW)
            r.slope[at, :, place] = (0.5 * (1.0 + bent) + 0.5 * pre * (1.0 - bent * bent) * slope).astype(LOW)

        loop(hidden // width, columns)

    def contract(layer):
        r.f[...] = product(r.g[layer // 2], r.wb[layer // 2], NN)

    def by_rows(work):
        loop(length // BLOCK, lambda index: work(aligned(index * BLOCK, BLOCK)))

    def normalize(layer):
        gain, offset = gain_row(layer, 0), gain_row(layer, 1)

        def some(rows):
            branch = r.f[rows, :]
            normal, inverse = stats(r.x[layer, rows, :].astype(WIDE) + branch)
            r.n[layer, rows, :] = normal
            r.inv[layer, rows, :] = inverse
            out = normal * gain + offset
            dual = branch if layer == 0 else r.y[rows, :].astype(WIDE) + branch
            if layer < 3:
                r.x[layer + 1, rows, :] = out.astype(LOW)
                r.y[rows, :] = dual.astype(LOW)
            else:
                dual_normal, dual_inverse = stats(dual)
                r.output[rows, :] = (out + dual_normal).astype(LOW)
                pull = r.cot[rows, :].astype(WIDE) * r.live[rows, :]
                r.gx[rows, :] = pull
                r.gy[rows, :] = norm_back(dual_normal, dual_inverse, pull)

        by_rows(some)

    def back_normalize(layer):
        gain = gain_row(layer, 0)

        def some(index, sums):
            rows = aligned(index * BLOCK, BLOCK)
            upstream = r.gx[rows, :]
            normal = r.n[layer, rows, :]
            summed = norm_back(normal, r.inv[layer, rows, :], upstream * gain)
            dual = r.gy[rows, :]
            r.gx[rows, :] = summed
            r.df[rows, :] = (summed + dual).astype(LOW)
            if layer == 3:
                r.gy[rows, :] = dual.astype(LOW).astype(WIDE)
            return (
                sums[0] + jnp.sum(upstream * normal, 0, keepdims=True),
                sums[1] + jnp.sum(upstream, 0, keepdims=True),
            )

        zero = jnp.zeros((1, width), WIDE)
        gains, offsets = lax.fori_loop(0, length // BLOCK, some, (zero, zero))
        r.ng[d, 2 * layer : 2 * layer + 1, :] = gains
        r.ng[d, 2 * layer + 1 : 2 * layer + 2, :] = offsets

    def pass_down(layer, inner):
        total = r.gx[...] + inner
        if layer > 0:
            r.gx[...] = total.astype(LOW).astype(WIDE)
        else:
            r.input_grad[...] = total

    def keep(name, half, place, value):
        own = getattr(r, "own" + name)
        own[:, :, :, half, :, place] = value.astype(LOW).reshape(
            chips, 2, SECTIONS, rows_a // SECTIONS, value.shape[1]
        )

    def back_contract(layer):
        own = getattr(r, "ownB%d" % (layer // 2))
        r.dft[...] = r.df[...].T

        def owner(index):
            value = product(r.dft[...], r.g[layer // 2, :, aligned(index * rows_b, rows_b)], NN)
            own[lax.div(index, 2), lax.rem(index, 2)] = value.astype(LOW).reshape(SECTIONS, 2, half_b, rows_b)

        loop(devices, owner)

    def back_expand(layer):
        at = layer // 2

        def columns(index):
            place = aligned(index * width, width)
            pulled = product(r.df[...], r.wb[at, place, :], NT)
            pulled = (pulled * r.slope[at, :, place].astype(WIDE)).astype(LOW)
            r.dp[:, place] = pulled
            inner = aligned(lax.rem(index, 2) * width, width)
            keep("F%d" % layer, lax.div(index, 2), inner, product(r.xt[layer], pulled, NN))

        loop(hidden // width, columns)

    def back_expand_end(layer):
        pass_down(layer, product(r.dp[...], r.wa[layer], NT))

    def back_output(layer):
        at = layer // 2
        for half in range(2):
            place = pl.ds(half * width // 2, width // 2)
            keep("O%d" % layer, half, pl.ds(0, width // 2), product(r.ot[at], r.df[:, place], NN))
        r.dm[...] = product(r.df[...], r.wa[layer, :, 3 * width :], NT).astype(LOW)

    def back_heads(layer, begin, count):
        at = layer // 2

        def pair(index):
            lanes = aligned(index * 2 * head, 2 * head)
            pulled = r.dm[:, lanes]
            keys, values = [], []
            for which in range(2):
                probs = r.pt[at, 2 * index + which]
                grad = product(r.v[at, :, lanes], pulled * half_masks[which], NT)
                full = probs.astype(WIDE)
                centre = jnp.sum(full * grad, 0, keepdims=True)
                scores = (full * (grad - centre)).astype(LOW)
                keys.append(product(scores, r.q[at, :, lanes], NN))
                values.append(product(probs, pulled, NN))
                place = aligned((2 * index + which) * head, head)
                r.dqt[place, :] = product(r.kt[at, place, :], scores, NN).astype(LOW)
            r.dp[:, aligned(width + index * 2 * head, 2 * head)] = jnp.where(
                lane < head, keys[0], keys[1]
            ).astype(LOW)
            r.dp[:, aligned(2 * width + index * 2 * head, 2 * head)] = jnp.where(
                lane < head, values[0], values[1]
            ).astype(LOW)

        def pairs(step):
            pair(begin + 2 * step)
            pair(begin + 2 * step + 1)

        loop(count // 2, pairs)

    def back_packed(layer):
        r.dp[:, 0:width] = r.dqt[...].T
        part = 3 * width // 2
        for half in range(2):
            value = product(r.xt[layer], r.dp[:, half * part : (half + 1) * part], NN)
            keep("K%d" % layer, half, pl.ds(0, part), value)

    def back_packed_end(layer):
        pass_down(layer, product(r.dp[:, 0 : 3 * width], r.wa[layer, :, 0 : 3 * width], NT))

    def joined(target, others):
        return functools.reduce(
            lambda left, right: left + right, [ref[...].astype(WIDE) for ref in (target, *others)]
        )

    def add_into(target, others):
        if len(others) == 1:
            target[...] = target[...] + others[0][...]
        else:
            target[...] = joined(target, others).astype(LOW)

    places = {name: place for place, (name, _, _, _) in enumerate(grad_items)}
    by_turn = (sd, sx, sy, s)

    def buffers(name):
        parts = ("own", "sib", "farx", "fary", "nearx", "neary", "line", "done")
        return types.SimpleNamespace(**{part: getattr(r, part + name) for part in parts})

    def to_core(name):
        item, place = buffers(name), places[name]
        for turn, section in enumerate(by_turn):
            push(
                item.own.at[:, 1 - c, section],
                item.sib.at[:, section],
                r.sib_s.at[place, turn],
                r.sib_r.at[place, turn],
                to_sibling,
            )
            at_end(None, item.sib.at[:, 0], r.sib_s.at[place, turn])

    def to_plane(name):
        item, place = buffers(name), places[name]
        own = item.own.at[:, c]

        def over_x(section, half, target, slot):
            push(own.at[:, section, half], target, r.px_s.at[place, slot], r.px_r.at[place, slot], to_x)
            at_end(None, item.farx, r.px_s.at[place, slot])

        def over_y(section, half, target, slot):
            push(own.at[:, section, half], target, r.py_s.at[place, slot], r.py_r.at[place, slot], to_y)
            at_end(None, item.farx, r.py_s.at[place, slot])

        for turn, section in enumerate(by_turn):
            arrived(item.sib.at[:, section], r.sib_r.at[place, turn])
            add_into(own.at[:, section], [item.sib.at[:, section]])
            if turn == 0:
                over_x(sd, 0, item.farx, 2)
                over_y(sd, 1, item.fary, 2)
            elif turn == 1:
                over_x(sx, 0, item.nearx.at[0], 0)
            elif turn == 2:
                over_y(sy, 1, item.neary.at[1], 1)

    def through_plane(name):
        item, place = buffers(name), places[name]
        own = item.own.at[:, c]
        arrived(item.fary, r.py_r.at[place, 2])
        add_into(own.at[:, sx, 1], [item.fary])
        push(own.at[:, sx, 1], item.nearx.at[1], r.px_s.at[place, 1], r.px_r.at[place, 1], to_x)
        at_end(None, item.farx, r.px_s.at[place, 1])
        arrived(item.farx, r.px_r.at[place, 2])
        add_into(own.at[:, sy, 0], [item.farx])
        push(own.at[:, sy, 0], item.neary.at[0], r.py_s.at[place, 0], r.py_r.at[place, 0], to_y)
        at_end(None, item.farx, r.py_s.at[place, 0])

    def to_line(name):
        item, place = buffers(name), places[name]
        own = item.own.at[:, c, s]
        for half in range(2):
            arrived(item.nearx.at[half], r.px_r.at[place, half])
            arrived(item.neary.at[half], r.py_r.at[place, half])
            add_into(own.at[:, half], [item.nearx.at[half], item.neary.at[half]])
        for step in range(1, chips):
            chip = lax.rem(z + step, chips)
            push(
                own.at[chip],
                item.line.at[z],
                r.line_s.at[place, step],
                r.line_r.at[place, z],
                {"dp": 2 * chip + c},
            )
            at_end(None, item.line.at[0], r.line_s.at[place, step])

    def to_owner(name):
        item, place = buffers(name), places[name]
        others = [lax.rem(z + step, chips) for step in range(1, chips)]
        for chip in others:
            arrived(item.line.at[chip], r.line_r.at[place, chip])
        total = joined(item.own.at[z, c, s], [item.line.at[chip] for chip in others])
        square = total * total
        while square.ndim > 2:
            square = jnp.sum(square, 0)
        square = jnp.sum(jnp.sum(square, 0, keepdims=True), 1, keepdims=True)
        r.sum[...] = r.sum[...] + jnp.broadcast_to(square, (8, LANES))
        if name[0] == "B":
            item.done[...] = total
            return
        item.done[s] = total.astype(LOW)
        layer = grad_items[place][1]
        mine = item.done.at[s]
        away = s != layer
        when(
            away,
            lambda: push(mine, mine, r.done_s.at[place], r.done_r.at[place, s], {"section": jnp.int32(layer)}),
        )
        at_end(away, mine, r.done_s.at[place])

    def collect(name):
        item, place = buffers(name), places[name]
        layer = grad_items[place][1]

        def work():
            for section in range(SECTIONS):
                if section != layer:
                    arrived(item.done.at[section], r.done_r.at[place, section])
            columns = item.done.shape[-1]
            start = 3 * width if name[0] == "O" else 0
            for section in range(SECTIONS):
                for half in range(2):
                    rows = pl.ds(section * (rows_a // SECTIONS), rows_a // SECTIONS)
                    place_to = pl.ds(start + half * columns, columns)
                    r.grad_a[rows, place_to] = item.done[section, half].astype(WIDE)

        when(s == layer, work)

    def all_sent():
        for condition, source, sem in finish:
            when(condition, functools.partial(sent, source, sem))
        finish.clear()

    small_out(0, r.tiles.at[d, s])
    start_line(0)
    spread_plane(0, z)
    rows_plane()
    line_step(0, 1)
    rows_relay()
    line_step(0, 2)
    rows_line()
    start_line(2)
    for step in range(3, chips):
        line_step(0, step)
    small_group(0, r.tiles.at[pl.ds(0, devices - 1), 0])
    for peer in plane:
        push(r.tiles.at[:, s], r.tiles.at[:, s], r.small_s.at[0, 1], r.small_r.at[0, 1], peer)
    prepare_masks()
    rows_step(1)
    plane_step(0)
    for step in range(2, chips):
        rows_step(step)
    spread_plane(2, z)
    for step in range(1, chips):
        line_step(2, step)
    own_x.wait()
    own_cot.wait()
    relay_step(0)
    small_plane(0, r.tiles.at[:, pl.ds(0, SECTIONS - 1)])
    for slot in range(4):
        arrived(whole_a, r.gs_r.at[slot])
    attention(0)
    normalize(0)
    expand(1)
    arrived(whole_b, r.gs_r.at[4])
    contract(1)
    normalize(1)
    plane_step(2)
    attention(2)
    normalize(2)
    expand(3)
    relay_step(2)
    arrived(whole_b, r.gs_r.at[5])
    contract(3)
    normalize(3)

    r.sum[...] = jnp.zeros((8, LANES), WIDE)
    back_normalize(3)
    back_contract(3)
    to_core("B1")
    back_expand(3)
    to_core("F3")
    to_plane("B1")
    back_expand_end(3)
    back_normalize(2)
    back_output(2)
    to_core("O2")
    to_plane("F3")
    back_heads(2, 0, 2)
    through_plane("B1")
    to_plane("O2")
    back_heads(2, 2, 2)
    through_plane("F3")
    to_line("B1")
    back_packed(2)
    to_core("K2")
    through_plane("O2")
    back_packed_end(2)
    to_line("F3")
    back_normalize(1)
    to_plane("K2")
    to_owner("B1")
    back_contract(1)
    to_core("B0")
    to_line("O2")
    back_expand(1)
    to_core("F1")
    through_plane("K2")
    to_plane("B0")
    to_owner("F3")
    back_expand_end(1)
    back_normalize(0)
    back_output(0)
    to_core("O0")
    to_plane("F1")
    to_owner("O2")
    to_line("K2")
    back_heads(0, 0, 2)
    through_plane("B0")
    to_plane("O0")
    back_heads(0, 2, 2)
    through_plane("F1")
    to_line("B0")
    to_owner("K2")
    back_packed(0)
    to_core("K0")
    small_out(1, r.ng.at[d])
    through_plane("O0")
    to_line("F1")
    back_packed_end(0)
    to_plane("K0")
    to_owner("B0")
    to_line("O0")
    all_sent()
    through_plane("K0")
    to_owner("F1")
    to_owner("O0")
    small_group(1, r.ng.at[pl.ds(0, devices - 1)])
    r.ns[s] = functools.reduce(lambda left, right: left + right, [r.ng[index] for index in range(devices)])
    small_plane_out(1, r.ns.at[s])
    for name in ("F3", "O2", "K2", "F1"):
        collect(name)
    to_line("K0")
    collect("O0")
    for layer in range(2):
        done = buffers("B%d" % layer).done
        r.grad_b[layer] = done[...].reshape(cols_b, rows_b).T
    small_plane(1, r.ns.at[pl.ds(0, SECTIONS - 1)])
    grads = functools.reduce(lambda left, right: left + right, [r.ns[index] for index in range(SECTIONS)])
    norm_square = jnp.sum(jnp.sum(grads * grads, 0, keepdims=True), 1, keepdims=True)
    chosen = jnp.zeros((2, width), WIDE)
    for layer in range(4):
        chosen = jnp.where(s == layer, grads[2 * layer : 2 * layer + 2, :], chosen)
    for chip in range(chips):
        pair_of = chosen[:, chip * LANES : (chip + 1) * LANES]
        r.grad_n[...] = jnp.where(
            z == chip, jnp.where(c == 0, pair_of[:, :rows_a], pair_of[:, rows_a:]), r.grad_n[...]
        )
    to_owner("K0")

    r.sq[d] = r.sum[...]
    small_out(2, r.sq.at[d])
    collect("K0")
    small_group(2, r.sq.at[pl.ds(0, devices - 1)])
    r.sqs[s] = functools.reduce(lambda left, right: left + right, [r.sq[index] for index in range(devices)])
    small_plane_out(2, r.sqs.at[s])
    all_sent()
    small_plane(2, r.sqs.at[pl.ds(0, SECTIONS - 1)])
    squares = functools.reduce(lambda left, right: left + right, [r.sqs[index] for index in range(SECTIONS)])
    r.square[...] = squares + norm_square


def step_call(tokens, cotangent, lengths, mat_a, mat_b, norms):
    rows_a, hidden = mat_a.shape[1:]
    rows_b, cols_b = mat_b.shape[1:]
    width = tokens.shape[1]
    length = tokens.shape[0] // lengths.shape[0]
    chips = width // rows_a // 2
    scratch = kernel_scratch(chips, rows_a, rows_b, cols_b, length, width, hidden)
    shapes = []
    for _, shape, kind in scratch:
        shapes.append(pltpu.SemaphoreType.DMA(shape) if kind is None else pltpu.VMEM(shape, kind))
    anywhere, vmem = pl.BlockSpec(memory_space=pl.ANY), pl.BlockSpec(memory_space=pltpu.VMEM)
    return pl.pallas_call(
        functools.partial(step_kernel, INPUTS + OUTPUTS + tuple(name for name, _, _ in scratch)),
        out_shape=(
            jax.ShapeDtypeStruct((rows_a, hidden), WIDE),
            jax.ShapeDtypeStruct(mat_b.shape, WIDE),
            jax.ShapeDtypeStruct((2, rows_a), WIDE),
            jax.ShapeDtypeStruct((8, LANES), WIDE),
            jax.ShapeDtypeStruct((length, width), LOW),
            jax.ShapeDtypeStruct((length, width), WIDE),
        ),
        in_specs=[anywhere, anywhere, pl.BlockSpec(memory_space=pltpu.SMEM), vmem, vmem, vmem],
        out_specs=[vmem] * len(OUTPUTS),
        scratch_shapes=shapes,
        compiler_params=pltpu.CompilerParams(
            collective_id=0, has_side_effects=True, vmem_limit_bytes=KERNEL_VMEM
        ),
    )(tokens, cotangent, lengths, mat_a, mat_b, norms)


def update_kernel(*refs):
    square, output, input_grad = (ref[...] for ref in refs[:3])
    grad_norm = jnp.sqrt(square[0:1, 0:1])
    factor = CLIP_NORM / jnp.maximum(grad_norm, CLIP_NORM)
    inputs, outputs = refs[3:15], refs[15:]
    outputs[0][...] = grad_norm
    outputs[1][0] = output
    outputs[2][0] = input_grad
    for group, (rate, decay) in enumerate(
        ((MATRIX_RATE, MATRIX_DECAY), (MATRIX_RATE, MATRIX_DECAY), (NORM_RATE, 0.0))
    ):
        grad, weight, one, two = inputs[4 * group : 4 * group + 4]
        clip = grad[...].reshape(weight.shape) * factor
        moment, square_new, master = adam_update(weight[...], one[...], two[...], clip, rate, decay)
        for ref, value in zip(
            outputs[3 + 5 * group : 8 + 5 * group], (clip, moment, square_new, master, master.astype(LOW))
        ):
            ref[...] = value


def kernel_body(
    tokens, cotangent, lengths, mat_a, mat_b, norms, first_a, second_a, first_b, second_b, first_n, second_n
):
    norms, first_n, second_n = (jnp.swapaxes(value, 1, 2) for value in (norms, first_n, second_n))
    grad_a, grad_b, grad_n, square, output, input_grad = step_call(
        tokens, cotangent, lengths, mat_a, mat_b, norms
    )
    steps = 4

    def cut(value, dim):
        shape = tuple(size // steps if at == dim else size for at, size in enumerate(value.shape))
        return pl.BlockSpec(shape, lambda step: tuple(step if at == dim else 0 for at in range(len(shape))))

    def whole(value):
        return pl.BlockSpec(value.shape, lambda step: (0,) * len(value.shape))

    def like(value, kind=WIDE):
        return jax.ShapeDtypeStruct(value.shape, kind)

    args = (square, output, input_grad, grad_a, mat_a, first_a, second_a, grad_b, mat_b, first_b, second_b)
    specs = [whole(square), cut(output, 0), cut(input_grad, 0)]
    specs += [cut(grad_a, 0)] + [cut(mat_a, 1)] * 3 + [cut(grad_b, 1)] * 4
    args += (grad_n, norms, first_n, second_n)
    specs += [whole(grad_n)] + [whole(norms)] * 3
    shapes = [jax.ShapeDtypeStruct((1, 1), WIDE), like(output[None], LOW), like(input_grad[None])]
    out_specs = [whole(shapes[0]), cut(shapes[1], 1), cut(shapes[2], 1)]
    for value, spec in ((mat_a, cut(mat_a, 1)), (mat_b, cut(mat_b, 1)), (norms, whole(norms))):
        shapes += [like(value)] * 4 + [like(value, LOW)]
        out_specs += [spec] * 5
    results = pl.pallas_call(
        update_kernel,
        grid=(steps,),
        out_shape=shapes,
        in_specs=specs,
        out_specs=out_specs,
        compiler_params=pltpu.CompilerParams(vmem_limit_bytes=KERNEL_VMEM),
    )(*args)
    results = [results[0][0, 0], *results[1:]]
    results[-5:] = [jnp.swapaxes(value, 1, 2) for value in results[-5:]]
    return tuple(results)


def chosen_body(*args):
    rows_a = args[3].shape[1]
    groups = lax.axis_size("dp")
    by_kernel = rows_a % 32 == 0 and 2 * rows_a == LANES and groups * rows_a == args[0].shape[1]
    return (kernel_body if by_kernel else body)(*args)


def solution(mesh):
    placed = (
        P("dp", None),
        P("dp", None),
        P("dp", None),
        P("section", "dp", None),
        P(None, "dp", "section"),
        P("section", "dp", None),
        P("section", "dp", None),
        P("section", "dp", None),
        P(None, "dp", "section"),
        P(None, "dp", "section"),
        P("section", "dp", None),
        P("section", "dp", None),
    )
    return jax.shard_map(
        chosen_body,
        mesh=mesh,
        in_specs=placed,
        out_specs=(
            P(),
            P("section", "dp", None),
            P("section", "dp", None),
            P("section", "dp", None),
            P("section", "dp", None),
            P("section", "dp", None),
            P("section", "dp", None),
            P("section", "dp", None),
            P(None, "dp", "section"),
            P(None, "dp", "section"),
            P(None, "dp", "section"),
            P(None, "dp", "section"),
            P(None, "dp", "section"),
            P("section", "dp", None),
            P("section", "dp", None),
            P("section", "dp", None),
            P("section", "dp", None),
            P("section", "dp", None),
        ),
        check_vma=False,
    )
```

```python
import functools
import types

import jax
import jax.numpy as jnp
from jax import lax
from jax.experimental import pallas as pl
from jax.experimental.pallas import tpu as pltpu
from jax.sharding import PartitionSpec as P

HEADS = 8
STEP = 5


EPSILON = 1e-05
NEGATIVE = -1e30
CLIP_NORM = 1.0
BETA_ONE = 0.5
BETA_TWO = 0.5
ADAM_EPSILON = 1e-08
MATRIX_RATE = 0.05
NORM_RATE = 0.5
MATRIX_DECAY = 0.01


def norm_stats(value):
    centre = value - jnp.mean(value, -1, keepdims=True)
    inverse = lax.rsqrt(jnp.mean(centre * centre, -1, keepdims=True) + EPSILON)
    return (centre * inverse, inverse)


def norm_back(normal, inverse, upstream):
    return inverse * (
        upstream
        - jnp.mean(upstream, -1, keepdims=True)
        - normal * jnp.mean(upstream * normal, -1, keepdims=True)
    )


def adam_update(weight, moment_one, moment_two, gradient, step_rate, decay_rate):
    first_new = BETA_ONE * moment_one + (1.0 - BETA_ONE) * gradient
    second_new = BETA_TWO * moment_two + (1.0 - BETA_TWO) * gradient * gradient
    first_hat = first_new / (1.0 - BETA_ONE**STEP)
    second_hat = second_new / (1.0 - BETA_TWO**STEP)
    weight_new = weight - step_rate * (
        first_hat / (jnp.sqrt(second_hat) + ADAM_EPSILON) + decay_rate * weight
    )
    return (first_new, second_new, weight_new)


def segments_of(lengths_row, length):
    ends = jnp.cumsum(lengths_row, dtype=jnp.int32)
    places = jnp.arange(length, dtype=jnp.int32)
    segment = jnp.sum((ends[None, :] <= places[:, None]).astype(jnp.int32), axis=1, dtype=jnp.int32)
    live = (places < ends[-1]).astype(jnp.float32)
    return segment, live


def matmul(left, right, dims):
    return lax.dot_general(left, right, (dims, ((), ())), preferred_element_type=jnp.float32)


NN = ((1,), (0,))
NT = ((1,), (1,))
TN = ((0,), (0,))


def attention_forward(stream, weight, mask):
    length, width = stream.shape
    size = width // HEADS
    packed = matmul(stream, weight[:, : 3 * width], NN).astype(jnp.bfloat16)
    heads = packed.reshape(length, 3, HEADS, size)
    scores = jnp.einsum("qhd,khd->hqk", heads[:, 0], heads[:, 1], preferred_element_type=jnp.float32)
    scores = jnp.where(mask[None], scores * size**-0.5, NEGATIVE)
    weights = jnp.exp(scores - jnp.max(scores, -1, keepdims=True))
    probs = weights / jnp.sum(weights, -1, keepdims=True)
    mixed = jnp.einsum("hqk,khd->qhd", probs.astype(jnp.bfloat16), heads[:, 2], preferred_element_type=jnp.float32)
    mixed = mixed.reshape(length, width).astype(jnp.bfloat16)
    branch = matmul(mixed, weight[:, 3 * width :], NN)
    return branch, (heads, probs, mixed)


def attention_backward(stream, weight, kept, grad_low):
    heads, probs, mixed = kept
    length, width = stream.shape
    size = width // HEADS
    grad_out = matmul(mixed, grad_low, TN)
    grad_mixed = matmul(grad_low, weight[:, 3 * width :], NT).astype(jnp.bfloat16)
    grad_mixed = grad_mixed.reshape(length, HEADS, size)
    grad_probs = jnp.einsum("qhd,khd->hqk", grad_mixed, heads[:, 2], preferred_element_type=jnp.float32)
    centre = jnp.sum(probs * grad_probs, -1, keepdims=True)
    grad_scores = (probs * (grad_probs - centre)).astype(jnp.bfloat16)
    low = probs.astype(jnp.bfloat16)
    scale = size**-0.5
    grad_q = jnp.einsum("hqk,khd->qhd", grad_scores, heads[:, 1], preferred_element_type=jnp.float32) * scale
    grad_k = jnp.einsum("hqk,qhd->khd", grad_scores, heads[:, 0], preferred_element_type=jnp.float32) * scale
    grad_v = jnp.einsum("hqk,qhd->khd", low, grad_mixed, preferred_element_type=jnp.float32)
    packed = jnp.concatenate([grad_q, grad_k, grad_v], axis=1).reshape(length, 3 * width)
    packed = packed.astype(jnp.bfloat16)
    grad_in = matmul(stream, packed, TN)
    grad_inputs = matmul(packed, weight[:, : 3 * width], NT)
    return grad_inputs, jnp.concatenate([grad_in, grad_out], axis=1)


def feed_forward(stream, weight, down):
    pre = matmul(stream, weight, NN)
    active = jax.nn.gelu(pre, approximate=True).astype(jnp.bfloat16)
    return matmul(active, down, NN), (pre, active)


def feed_backward(stream, weight, down, kept, grad_low):
    pre, active = kept
    grad_down = matmul(active, grad_low, TN)
    grad_active = matmul(grad_low, down, NT)
    pull = jax.vjp(lambda value: jax.nn.gelu(value, approximate=True), pre)[1]
    grad_pre = pull(grad_active)[0].astype(jnp.bfloat16)
    grad_up = matmul(stream, grad_pre, TN)
    return matmul(grad_pre, weight, NT), grad_up, grad_down


def micro_step(rows, pull, segment, mats, downs, gains, biases):
    low = jnp.bfloat16
    mask = segment[:, None] == segment[None, :]
    stream, dual = rows, jnp.zeros_like(rows)
    saved = []
    for sub in range(4):
        if sub % 2 == 0:
            branch, kept = attention_forward(stream, mats[sub], mask)
        else:
            branch, kept = feed_forward(stream, mats[sub], downs[sub // 2])
        normal, inverse = norm_stats(stream.astype(jnp.float32) + branch)
        out = normal * gains[sub] + biases[sub]
        total = dual.astype(jnp.float32) + branch
        saved.append((stream, kept, normal, inverse))
        if sub < 3:
            stream, dual = out.astype(low), total.astype(low)
    dual_normal, dual_inverse = norm_stats(total)
    output = (out + dual_normal).astype(low)
    grad_out, grad_dual = pull, norm_back(dual_normal, dual_inverse, pull)
    grads_a, grads_b, grads_n = [None] * 4, [None] * 2, [None] * 4
    for sub in (3, 2, 1, 0):
        stream, kept, normal, inverse = saved[sub]
        grads_n[sub] = jnp.stack([jnp.sum(grad_out * normal, 0), jnp.sum(grad_out, 0)], axis=1)
        summed = norm_back(normal, inverse, grad_out * gains[sub])
        branch_low = (summed + grad_dual).astype(low)
        if sub % 2 == 0:
            inner, grads_a[sub] = attention_backward(stream, mats[sub], kept, branch_low)
        else:
            inner, grads_a[sub], grads_b[sub // 2] = feed_backward(
                stream, mats[sub], downs[sub // 2], kept, branch_low
            )
        grad_in = summed + inner
        if sub > 0:
            grad_out = grad_in.astype(low).astype(jnp.float32)
            grad_dual = grad_dual.astype(low).astype(jnp.float32)
    return output, grad_in, jnp.stack(grads_a), jnp.stack(grads_b), jnp.stack(grads_n)


def finish_step(grad_norm, output, input_grad, *groups):
    factor = CLIP_NORM / jnp.maximum(grad_norm, CLIP_NORM)
    results = [grad_norm, output[None], input_grad[None]]
    for weight, one, two, grad, rate, decay in groups:
        clip = grad * factor
        moment, square_new, master = adam_update(weight, one, two, clip, rate, decay)
        results += [clip, moment, square_new, master, master.astype(jnp.bfloat16)]
    return tuple(results)


def body(
    tokens, cotangent, lengths, mat_a, mat_b, norms, first_a, second_a, first_b, second_b, first_n, second_n
):
    low = jnp.bfloat16
    own = lax.axis_index("section")
    length = tokens.shape[0] // lengths.shape[0]
    rows = lax.dynamic_slice_in_dim(tokens, own * length, length, 0)
    segment, live = segments_of(lax.dynamic_index_in_dim(lengths, own, 0, keepdims=False), length)
    pull = lax.dynamic_slice_in_dim(cotangent, own * length, length, 0).astype(jnp.float32) * live[:, None]

    def gathered(value):
        return lax.all_gather(lax.all_gather(value, "dp", axis=1, tiled=True), "section", axis=0, tiled=True)

    mats = gathered(mat_a.astype(low))
    scales = gathered(norms.astype(low)).astype(jnp.float32)
    downs = lax.all_gather(mat_b.astype(low), "section", axis=2, tiled=True)
    downs = lax.all_gather(downs, "dp", axis=1, tiled=True)
    output, input_grad, part_a, part_b, part_n = micro_step(
        rows, pull, segment, mats, downs, scales[:, :, 0], scales[:, :, 1]
    )

    def scattered(value, section_dim):
        value = lax.psum_scatter(value, "section", scatter_dimension=section_dim, tiled=True)
        return lax.psum_scatter(value, "dp", scatter_dimension=1, tiled=True).astype(jnp.float32)

    grad_a = scattered(part_a.astype(low), 0)
    grad_b = scattered(part_b.astype(low), 2)
    grad_n = scattered(part_n, 0)
    square = jnp.sum(grad_a * grad_a) + jnp.sum(grad_b * grad_b) + jnp.sum(grad_n * grad_n)
    grad_norm = jnp.sqrt(lax.psum(square, ("section", "dp")))
    return finish_step(
        grad_norm, output, input_grad,
        (mat_a, first_a, second_a, grad_a, MATRIX_RATE, MATRIX_DECAY),
        (mat_b, first_b, second_b, grad_b, MATRIX_RATE, MATRIX_DECAY),
        (norms, first_n, second_n, grad_n, NORM_RATE, 0.0),
    )


LOW = jnp.bfloat16
WIDE = jnp.float32
MESH = pl.DeviceIdType.MESH
SECTIONS = 4
LANES = 128
BLOCK = 64
KERNEL_VMEM = 64 * 1024 * 1024 - 256 * 1024


def gradient_items(rows_a, rows_b, cols_b, width, hidden):
    part = rows_a // SECTIONS
    return (
        ("B1", 3, cols_b // 2, rows_b),
        ("F3", 3, part, hidden // 2),
        ("O2", 2, part, width // 2),
        ("K2", 2, part, 3 * width // 2),
        ("B0", 1, cols_b // 2, rows_b),
        ("F1", 1, part, hidden // 2),
        ("O0", 0, part, width // 2),
        ("K0", 0, part, 3 * width // 2),
    )


def item_scratch(name, chips, rows, columns):
    piece = (rows, columns)
    return (
        ("own" + name, (chips, 2, SECTIONS, 2) + piece, LOW),
        ("sib" + name, (chips, SECTIONS, 2) + piece, LOW),
        ("farx" + name, (chips,) + piece, LOW),
        ("fary" + name, (chips,) + piece, LOW),
        ("nearx" + name, (2, chips) + piece, LOW),
        ("neary" + name, (2, chips) + piece, LOW),
        ("line" + name, (chips, 2) + piece, LOW),
        ("done" + name, (2,) + piece if name[0] == "B" else (SECTIONS, 2) + piece, WIDE if name[0] == "B" else LOW),
    )


def kernel_scratch(chips, rows_a, rows_b, cols_b, length, width, hidden):
    devices = 2 * chips
    items = gradient_items(rows_a, rows_b, cols_b, width, hidden)
    count = len(items)
    received = sum((item_scratch(name, chips, rows, columns) for name, _, rows, columns in items), ())
    return received + (
        ("sib_s", (count, SECTIONS), None),
        ("sib_r", (count, SECTIONS), None),
        ("px_s", (count, 3), None),
        ("px_r", (count, 3), None),
        ("py_s", (count, 3), None),
        ("py_r", (count, 3), None),
        ("line_s", (count, chips), None),
        ("line_r", (count, chips), None),
        ("done_s", (count,), None),
        ("done_r", (count, SECTIONS), None),
        ("wa", (4, width, hidden), LOW),
        ("wb", (2, hidden, width), LOW),
        ("tiles", (devices, SECTIONS, 8, LANES), WIDE),
        ("x", (4, length, width), LOW),
        ("xt", (4, width, length), LOW),
        ("y", (length, width), LOW),
        ("cot", (length, width), LOW),
        ("bias", (length, length), WIDE),
        ("live", (length, 1), WIDE),
        ("f", (length, width), WIDE),
        ("n", (4, length, width), WIDE),
        ("inv", (4, length, 1), WIDE),
        ("q", (2, length, width), LOW),
        ("k", (2, length, width), LOW),
        ("v", (2, length, width), LOW),
        ("kt", (2, width, length), LOW),
        ("vt", (2, width, length), LOW),
        ("ot", (2, width, length), LOW),
        ("pt", (2, HEADS, length, length), LOW),
        ("g", (2, length, hidden), LOW),
        ("slope", (2, length, hidden), LOW),
        ("gx", (length, width), WIDE),
        ("gy", (length, width), WIDE),
        ("df", (length, width), LOW),
        ("dft", (width, length), LOW),
        ("dm", (length, width), LOW),
        ("dqt", (width, length), LOW),
        ("dp", (length, hidden), LOW),
        ("ng", (devices, 8, width), WIDE),
        ("ns", (SECTIONS, 8, width), WIDE),
        ("sq", (devices, 8, LANES), WIDE),
        ("sqs", (SECTIONS, 8, LANES), WIDE),
        ("sum", (8, LANES), WIDE),
        ("in_s", (2,), None),
        ("gz_s", (3, 2, chips, 2), None),
        ("gz_r", (3, chips, 2), None),
        ("gx_s", (3, chips, 2), None),
        ("gx_r", (3, chips, 2), None),
        ("gy_s", (3, chips, 2), None),
        ("gy_r", (3, chips, 2), None),
        ("gxr_s", (3, chips), None),
        ("gxr_r", (3, chips), None),
        ("gyr_s", (3, chips), None),
        ("gyr_r", (3, chips), None),
        ("gs_s", (6,), None),
        ("gs_r", (6,), None),
        ("small_s", (3, 2), None),
        ("small_r", (3, 2), None),
    )


INPUTS = ("tokens", "cotangent", "lengths", "mat_a", "mat_b", "norms")
OUTPUTS = ("grad_a", "grad_b", "grad_n", "square", "output", "input_grad")


def step_kernel(names, *refs):
    r = types.SimpleNamespace(**dict(zip(names, refs)))
    width, hidden = r.wa.shape[1:]
    length = r.x.shape[1]
    rows_a, (rows_b, cols_b) = r.mat_a.shape[1], r.mat_b.shape[1:]
    devices = r.tiles.shape[0]
    chips = devices // 2
    half_a, half_b = rows_a // 2, cols_b // 2
    grad_items = gradient_items(rows_a, rows_b, cols_b, width, hidden)
    head = width // HEADS
    scale = head**-0.5

    s, d = lax.axis_index("section"), lax.axis_index("dp")
    z, c = lax.div(d, 2), lax.rem(d, 2)
    sx = s + 1 - 2 * lax.rem(s, 2)
    sy = lax.rem(s + 2, SECTIONS)
    sd = SECTIONS - 1 - s
    to_sibling = {"dp": d + 1 - 2 * c}
    to_up, to_down = {"dp": d + 2}, {"dp": d - 2}
    to_x, to_y = {"section": sx}, {"section": sy}
    below, above = z > 0, z < chips - 1
    group = [{"dp": lax.rem(d + step, devices)} for step in range(1, devices)]
    plane = [{"section": lax.rem(s + step, SECTIONS)} for step in range(1, SECTIONS)]
    finish = []

    def when(condition, work):
        if condition is None:
            work()
        else:
            pl.when(condition)(work)

    def push(source, target, send_sem, recv_sem, device):
        pltpu.make_async_remote_copy(
            src_ref=source,
            dst_ref=target,
            send_sem=send_sem,
            recv_sem=recv_sem,
            device_id=device,
            device_id_type=MESH,
        ).start()

    def arrived(target, sem):
        pltpu.make_async_remote_copy(
            src_ref=target, dst_ref=target, send_sem=sem, recv_sem=sem, device_id=to_x, device_id_type=MESH
        ).wait_recv()

    def sent(source, sem):
        pltpu.make_async_remote_copy(
            src_ref=source, dst_ref=source, send_sem=sem, recv_sem=sem, device_id=to_x, device_id_type=MESH
        ).wait_send()

    def at_end(condition, source, sem):
        finish.append((condition, source, sem))

    def aligned(start, size):
        return pl.ds(pl.multiple_of(start, size), size)

    own_x = pltpu.make_async_copy(r.tokens.at[aligned(s * length, length)], r.x.at[0], r.in_s.at[0])
    own_cot = pltpu.make_async_copy(r.cotangent.at[aligned(s * length, length)], r.cot, r.in_s.at[1])
    own_x.start()
    own_cot.start()
    barrier = pltpu.get_barrier_semaphore()
    for peer in group + plane:
        pl.semaphore_signal(barrier, inc=1, device_id=peer, device_id_type=MESH)
    r.wa[s, aligned(d * rows_a, rows_a), :] = r.mat_a[0].astype(LOW)
    for layer in range(2):
        r.wb[layer, aligned(d * rows_b, rows_b), aligned(s * cols_b, cols_b)] = r.mat_b[layer].astype(LOW)
    norms = r.norms[0].astype(LOW).astype(WIDE)
    nothing = jnp.zeros((2, rows_a), WIDE)
    even = jnp.concatenate([norms, nothing], axis=1)
    odd = jnp.concatenate([nothing, norms], axis=1)
    r.tiles[d, s, 0:2, :] = jnp.where(c == 0, even, odd)
    r.tiles[d, s, 2:8, :] = jnp.zeros((6, LANES), WIDE)
    pl.semaphore_wait(barrier, len(group) + len(plane))

    def small_out(which, source):
        for peer in group:
            push(source, source, r.small_s.at[which, 0], r.small_r.at[which, 0], peer)

    def small_group(which, like):
        arrived(like, r.small_r.at[which, 0])
        sent(like, r.small_s.at[which, 0])

    def small_plane_out(which, source):
        for peer in plane:
            push(source, source, r.small_s.at[which, 1], r.small_r.at[which, 1], peer)

    def small_plane(which, like):
        arrived(like, r.small_r.at[which, 1])
        sent(like, r.small_s.at[which, 1])

    def block_a(section, chip, half):
        return r.wa.at[section, aligned((2 * chip + c) * rows_a + half * half_a, half_a), :]

    def block_b(layer):
        part = rows_b // 2

        def block(section, chip, half):
            return r.wb.at[
                layer,
                aligned((2 * chip + c) * rows_b + half * part, part),
                aligned(section * cols_b, cols_b),
            ]

        return block

    items = (block_a, block_b(0), block_b(1))

    def to_the_sibling(item, section, chip, half):
        block = items[item](section, chip, half)
        slot = section if item == 0 else 3 + item
        push(block, block, r.gs_s.at[slot], r.gs_r.at[slot], to_sibling)

    def spread_plane(item, chip):
        for half in range(2):
            block = items[item](s, chip, half)
            push(block, block, r.gx_s.at[item, chip, half], r.gx_r.at[item, chip, half], to_x)
            push(block, block, r.gy_s.at[item, chip, half], r.gy_r.at[item, chip, half], to_y)
            to_the_sibling(item, s, chip, half)

    def up(item, chip, half):
        block = items[item](s, chip, half)
        push(block, block, r.gz_s.at[item, 0, chip, half], r.gz_r.at[item, chip, half], to_up)

    def down(item, chip, half):
        block = items[item](s, chip, half)
        push(block, block, r.gz_s.at[item, 1, chip, half], r.gz_r.at[item, chip, half], to_down)

    def start_line(item):
        for half in range(2):
            when(above, lambda: up(item, z, half))
            when(below, lambda: down(item, z, half))

    def line_step(item, step):
        def from_below():
            for half in range(2):
                arrived(items[item](s, z - step, half), r.gz_r.at[item, z - step, half])
                when(above, lambda: up(item, z - step, half))
            spread_plane(item, z - step)

        def from_above():
            for half in range(2):
                arrived(items[item](s, z + step, half), r.gz_r.at[item, z + step, half])
                when(below, lambda: down(item, z + step, half))
            spread_plane(item, z + step)

        when(z >= step, from_below)
        when(z + step < chips, from_above)

    def plane_step(item):
        for chip in range(chips):
            for half in range(2):
                arrived(items[item](sx, chip, half), r.gx_r.at[item, chip, half])
                if half == 1:
                    block = items[item](sx, chip, half)
                    push(block, block, r.gyr_s.at[item, chip], r.gyr_r.at[item, chip], to_y)
                to_the_sibling(item, sx, chip, half)
                arrived(items[item](sy, chip, half), r.gy_r.at[item, chip, half])
                if half == 0:
                    block = items[item](sy, chip, half)
                    push(block, block, r.gxr_s.at[item, chip], r.gxr_r.at[item, chip], to_x)
                to_the_sibling(item, sy, chip, half)

    def relay_step(item):
        for chip in range(chips):
            arrived(items[item](sd, chip, 0), r.gxr_r.at[item, chip])
            to_the_sibling(item, sd, chip, 0)
            arrived(items[item](sd, chip, 1), r.gyr_r.at[item, chip])
            to_the_sibling(item, sd, chip, 1)

    whole_a = r.wa.at[0, pl.ds(0, chips * rows_a)]
    whole_b = r.wb.at[0, pl.ds(0, chips * rows_b)]
    for slot in range(6):
        at_end(None, whole_a if slot < 4 else whole_b, r.gs_s.at[slot])
    for item in (0, 2):
        for chip in range(chips):
            for half in range(2):
                block = items[item](0, chip, half)
                at_end(None, block, r.gx_s.at[item, chip, half])
                at_end(None, block, r.gy_s.at[item, chip, half])
                at_end(above & (z >= chip), block, r.gz_s.at[item, 0, chip, half])
                at_end(below & (z <= chip), block, r.gz_s.at[item, 1, chip, half])
            block = items[item](0, chip, 0)
            at_end(None, block, r.gxr_s.at[item, chip])
            at_end(None, block, r.gyr_s.at[item, chip])

    def row_block(chip, half):
        part = rows_b // 2
        return r.wb.at[0, aligned((2 * chip + c) * rows_b + half * part, part), :]

    def rows_to_sibling(chip, half):
        push(row_block(chip, half), row_block(chip, half), r.gs_s.at[4], r.gs_r.at[4], to_sibling)

    def rows_up(chip, half):
        rows = row_block(chip, half)
        push(rows, rows, r.gz_s.at[1, 0, chip, half], r.gz_r.at[1, chip, half], to_up)

    def rows_down(chip, half):
        rows = row_block(chip, half)
        push(rows, rows, r.gz_s.at[1, 1, chip, half], r.gz_r.at[1, chip, half], to_down)

    def rows_plane():
        for half in range(2):
            block = items[1](s, z, half)
            push(block, block, r.gx_s.at[1, 0, half], r.gx_r.at[1, 0, half], to_x)
            push(block, block, r.gy_s.at[1, 0, half], r.gy_r.at[1, 0, half], to_y)
            at_end(None, block, r.gx_s.at[1, 0, half])
            at_end(None, block, r.gy_s.at[1, 0, half])

    def rows_relay():
        for half in range(2):
            arrived(items[1](sx, z, half), r.gx_r.at[1, 0, half])
            arrived(items[1](sy, z, half), r.gy_r.at[1, 0, half])
        block = items[1](sx, z, 1)
        push(block, block, r.gyr_s.at[1, 0], r.gyr_r.at[1, 0], to_y)
        block = items[1](sy, z, 0)
        push(block, block, r.gxr_s.at[1, 0], r.gxr_r.at[1, 0], to_x)
        at_end(None, block, r.gyr_s.at[1, 0])
        at_end(None, block, r.gxr_s.at[1, 0])

    def rows_line():
        for half, sem in ((0, r.gxr_r), (1, r.gyr_r)):
            arrived(items[1](sd, z, half), sem.at[1, 0])
            when(above, lambda: rows_up(z, half))
            when(below, lambda: rows_down(z, half))
            rows_to_sibling(z, half)
        for chip in range(chips):
            for half in range(2):
                at_end(above & (z >= chip), row_block(chip, half), r.gz_s.at[1, 0, chip, half])
                at_end(below & (z <= chip), row_block(chip, half), r.gz_s.at[1, 1, chip, half])

    def rows_step(step):
        def from_below():
            for half in range(2):
                arrived(row_block(z - step, half), r.gz_r.at[1, z - step, half])
                when(above, lambda: rows_up(z - step, half))
                rows_to_sibling(z - step, half)

        def from_above():
            for half in range(2):
                arrived(row_block(z + step, half), r.gz_r.at[1, z + step, half])
                when(below, lambda: rows_down(z + step, half))
                rows_to_sibling(z + step, half)

        when(z >= step, from_below)
        when(z + step < chips, from_above)

    def product(left, right, dims):
        return lax.dot_general(left, right, (dims, ((), ())), preferred_element_type=WIDE)

    def loop(count, work):
        def one(index, carry):
            work(index)
            return carry

        lax.fori_loop(0, count, one, 0)

    def gain_row(layer, kind):
        parts = [
            r.tiles[2 * chip, layer, kind : kind + 1, :] + r.tiles[2 * chip + 1, layer, kind : kind + 1, :]
            for chip in range(chips)
        ]
        return jnp.concatenate(parts, axis=1)

    def stats(value):
        centre = value - jnp.mean(value, -1, keepdims=True)
        inverse = lax.rsqrt(jnp.mean(centre * centre, -1, keepdims=True) + EPSILON)
        return centre * inverse, inverse

    lane = lax.broadcasted_iota(jnp.int32, (1, 2 * head), 1)
    first_half = (lane < head).astype(WIDE)
    half_masks = (first_half.astype(LOW), (1.0 - first_half).astype(LOW))

    def prepare_masks():
        ends, total = [], jnp.int32(0)
        for slot in range(r.lengths.shape[1]):
            total = total + r.lengths[s, slot]
            ends.append(total)
        down_places = lax.broadcasted_iota(jnp.int32, (length, 1), 0)
        across_places = lax.broadcasted_iota(jnp.int32, (1, length), 1)
        down_segment = jnp.zeros((length, 1), jnp.int32)
        across_segment = jnp.zeros((1, length), jnp.int32)
        for end in ends:
            down_segment = down_segment + (end <= down_places).astype(jnp.int32)
            across_segment = across_segment + (end <= across_places).astype(jnp.int32)
        r.bias[...] = jnp.where(down_segment == across_segment, 0.0, NEGATIVE)
        r.live[...] = (down_places < total).astype(WIDE)

    def attention(layer):
        at = layer // 2
        rows = r.x[layer]
        r.xt[layer] = rows.T
        r.q[at] = product(rows, r.wa[layer, :, 0:width], NN).astype(LOW) * jnp.asarray(scale, LOW)
        keys = product(rows, r.wa[layer, :, width : 2 * width], NN).astype(LOW)
        r.k[at] = keys
        r.kt[at] = (keys * jnp.asarray(scale, LOW)).T
        values = product(rows, r.wa[layer, :, 2 * width : 3 * width], NN).astype(LOW)
        r.v[at] = values
        r.vt[at] = values.T

        def pair(index):
            lanes = aligned(index * 2 * head, 2 * head)
            for which in range(2):
                scores = product(r.k[at, :, lanes], r.q[at, :, lanes] * half_masks[which], NT) + r.bias[...]
                weights = jnp.exp(scores - jnp.max(scores, 0, keepdims=True))
                probs = (weights * (1.0 / jnp.sum(weights, 0, keepdims=True))).astype(LOW)
                r.pt[at, 2 * index + which] = probs
                place = aligned((2 * index + which) * head, head)
                r.ot[at, place, :] = product(r.vt[at, place, :], probs, NN).astype(LOW)

        def pairs(step):
            pair(2 * step)
            pair(2 * step + 1)

        loop(HEADS // 4, pairs)
        r.f[...] = product(r.ot[at].T, r.wa[layer, :, 3 * width :], NN)

    def expand(layer):
        at = layer // 2
        r.xt[layer] = r.x[layer].T

        def columns(index):
            place = pl.ds(index * width, width)
            pre = product(r.x[layer], r.wa[layer, :, place], NN)
            squared = pre * pre
            slope = 0.7978845608 * (1.0 + 3 * 0.044715 * squared)
            bent = jnp.tanh(0.7978845608 * pre * (1.0 + 0.044715 * squared))
            r.g[at, :, place] = (0.5 * pre * (1.0 + bent)).astype(LOW)
            r.slope[at, :, place] = (0.5 * (1.0 + bent) + 0.5 * pre * (1.0 - bent * bent) * slope).astype(LOW)

        for index in range(hidden // width):
            columns(index)

    def contract(layer):
        r.f[...] = product(r.g[layer // 2], r.wb[layer // 2], NN)

    def by_rows(work):
        for index in range(length // BLOCK):
            work(pl.ds(index * BLOCK, BLOCK))

    def normalize(layer):
        gain, offset = gain_row(layer, 0), gain_row(layer, 1)

        def some(rows):
            branch = r.f[rows, :]
            normal, inverse = stats(r.x[layer, rows, :].astype(WIDE) + branch)
            r.n[layer, rows, :] = normal
            r.inv[layer, rows, :] = inverse
            out = normal * gain + offset
            dual = branch if layer == 0 else r.y[rows, :].astype(WIDE) + branch
            if layer < 3:
                r.x[layer + 1, rows, :] = out.astype(LOW)
                r.y[rows, :] = dual.astype(LOW)
            else:
                dual_normal, dual_inverse = stats(dual)
                r.output[rows, :] = (out + dual_normal).astype(LOW)
                pull = r.cot[rows, :].astype(WIDE) * r.live[rows, :]
                r.gx[rows, :] = pull
                r.gy[rows, :] = norm_back(dual_normal, dual_inverse, pull)

        by_rows(some)

    def back_normalize(layer):
        gain = gain_row(layer, 0)

        def some(index, sums):
            rows = pl.ds(index * BLOCK, BLOCK)
            upstream = r.gx[rows, :]
            normal = r.n[layer, rows, :]
            summed = norm_back(normal, r.inv[layer, rows, :], upstream * gain)
            dual = r.gy[rows, :]
            r.gx[rows, :] = summed
            r.df[rows, :] = (summed + dual).astype(LOW)
            if layer == 3:
                r.gy[rows, :] = dual.astype(LOW).astype(WIDE)
            return (
                sums[0] + jnp.sum(upstream * normal, 0, keepdims=True),
                sums[1] + jnp.sum(upstream, 0, keepdims=True),
            )

        zero = jnp.zeros((1, width), WIDE)
        gains, offsets = zero, zero
        for index in range(length // BLOCK):
            gains, offsets = some(index, (gains, offsets))
        r.ng[d, 2 * layer : 2 * layer + 1, :] = gains
        r.ng[d, 2 * layer + 1 : 2 * layer + 2, :] = offsets

    def pass_down(layer, inner):
        total = r.gx[...] + inner
        if layer > 0:
            r.gx[...] = total.astype(LOW).astype(WIDE)
        else:
            r.input_grad[...] = total

    def keep(name, half, place, value):
        own = getattr(r, "own" + name)
        own[:, :, :, half, :, place] = value.astype(LOW).reshape(
            chips, 2, SECTIONS, rows_a // SECTIONS, value.shape[1]
        )

    def back_contract(layer):
        own = getattr(r, "ownB%d" % (layer // 2))
        r.dft[...] = r.df[...].T

        def owner(index):
            value = product(r.dft[...], r.g[layer // 2, :, pl.ds(index * rows_b, rows_b)], NN)
            own[index // 2, index % 2] = value.astype(LOW).reshape(SECTIONS, 2, half_b, rows_b)

        for index in range(devices):
            owner(index)

    def back_expand(layer):
        at = layer // 2

        def columns(index):
            place = pl.ds(index * width, width)
            pulled = product(r.df[...], r.wb[at, place, :], NT)
            pulled = (pulled * r.slope[at, :, place].astype(WIDE)).astype(LOW)
            r.dp[:, place] = pulled
            inner = pl.ds(index % 2 * width, width)
            keep("F%d" % layer, index // 2, inner, product(r.xt[layer], pulled, NN))

        for index in range(hidden // width):
            columns(index)

    def back_expand_end(layer):
        pass_down(layer, product(r.dp[...], r.wa[layer], NT))

    def back_output(layer):
        at = layer // 2
        for half in range(2):
            place = pl.ds(half * width // 2, width // 2)
            keep("O%d" % layer, half, pl.ds(0, width // 2), product(r.ot[at], r.df[:, place], NN))
        r.dm[...] = product(r.df[...], r.wa[layer, :, 3 * width :], NT).astype(LOW)

    def back_heads(layer, begin, count):
        at = layer // 2

        def pair(index):
            lanes = aligned(index * 2 * head, 2 * head)
            pulled = r.dm[:, lanes]
            keys, values = [], []
            for which in range(2):
                probs = r.pt[at, 2 * index + which]
                grad = product(r.v[at, :, lanes], pulled * half_masks[which], NT)
                full = probs.astype(WIDE)
                centre = jnp.sum(full * grad, 0, keepdims=True)
                scores = (full * (grad - centre)).astype(LOW)
                keys.append(product(scores, r.q[at, :, lanes], NN))
                values.append(product(probs, pulled, NN))
                place = aligned((2 * index + which) * head, head)
                r.dqt[place, :] = product(r.kt[at, place, :], scores, NN).astype(LOW)
            r.dp[:, aligned(width + index * 2 * head, 2 * head)] = jnp.where(
                lane < head, keys[0], keys[1]
            ).astype(LOW)
            r.dp[:, aligned(2 * width + index * 2 * head, 2 * head)] = jnp.where(
                lane < head, values[0], values[1]
            ).astype(LOW)

        def pairs(step):
            pair(begin + 2 * step)
            pair(begin + 2 * step + 1)

        loop(count // 2, pairs)

    def back_packed(layer):
        r.dp[:, 0:width] = r.dqt[...].T
        part = 3 * width // 2
        for half in range(2):
            value = product(r.xt[layer], r.dp[:, half * part : (half + 1) * part], NN)
            keep("K%d" % layer, half, pl.ds(0, part), value)

    def back_packed_end(layer):
        pass_down(layer, product(r.dp[:, 0 : 3 * width], r.wa[layer, :, 0 : 3 * width], NT))

    def joined(target, others):
        return functools.reduce(
            lambda left, right: left + right, [ref[...].astype(WIDE) for ref in (target, *others)]
        )

    def add_into(target, others):
        if len(others) == 1:
            target[...] = target[...] + others[0][...]
        else:
            target[...] = joined(target, others).astype(LOW)

    places = {name: place for place, (name, _, _, _) in enumerate(grad_items)}
    by_turn = (sd, sx, sy, s)

    def buffers(name):
        parts = ("own", "sib", "farx", "fary", "nearx", "neary", "line", "done")
        return types.SimpleNamespace(**{part: getattr(r, part + name) for part in parts})

    def to_core(name):
        item, place = buffers(name), places[name]
        for turn, section in enumerate(by_turn):
            push(
                item.own.at[:, 1 - c, section],
                item.sib.at[:, section],
                r.sib_s.at[place, turn],
                r.sib_r.at[place, turn],
                to_sibling,
            )
            at_end(None, item.sib.at[:, 0], r.sib_s.at[place, turn])

    def to_plane(name):
        item, place = buffers(name), places[name]
        own = item.own.at[:, c]

        def over_x(section, half, target, slot):
            push(own.at[:, section, half], target, r.px_s.at[place, slot], r.px_r.at[place, slot], to_x)
            at_end(None, item.farx, r.px_s.at[place, slot])

        def over_y(section, half, target, slot):
            push(own.at[:, section, half], target, r.py_s.at[place, slot], r.py_r.at[place, slot], to_y)
            at_end(None, item.farx, r.py_s.at[place, slot])

        for turn, section in enumerate(by_turn):
            arrived(item.sib.at[:, section], r.sib_r.at[place, turn])
            add_into(own.at[:, section], [item.sib.at[:, section]])
            if turn == 0:
                over_x(sd, 0, item.farx, 2)
                over_y(sd, 1, item.fary, 2)
            elif turn == 1:
                over_x(sx, 0, item.nearx.at[0], 0)
            elif turn == 2:
                over_y(sy, 1, item.neary.at[1], 1)

    def through_plane(name):
        item, place = buffers(name), places[name]
        own = item.own.at[:, c]
        arrived(item.fary, r.py_r.at[place, 2])
        add_into(own.at[:, sx, 1], [item.fary])
        push(own.at[:, sx, 1], item.nearx.at[1], r.px_s.at[place, 1], r.px_r.at[place, 1], to_x)
        at_end(None, item.farx, r.px_s.at[place, 1])
        arrived(item.farx, r.px_r.at[place, 2])
        add_into(own.at[:, sy, 0], [item.farx])
        push(own.at[:, sy, 0], item.neary.at[0], r.py_s.at[place, 0], r.py_r.at[place, 0], to_y)
        at_end(None, item.farx, r.py_s.at[place, 0])

    def to_line(name):
        item, place = buffers(name), places[name]
        own = item.own.at[:, c, s]
        for half in range(2):
            arrived(item.nearx.at[half], r.px_r.at[place, half])
            arrived(item.neary.at[half], r.py_r.at[place, half])
            add_into(own.at[:, half], [item.nearx.at[half], item.neary.at[half]])
        for step in range(1, chips):
            chip = lax.rem(z + step, chips)
            push(
                own.at[chip],
                item.line.at[z],
                r.line_s.at[place, step],
                r.line_r.at[place, z],
                {"dp": 2 * chip + c},
            )
            at_end(None, item.line.at[0], r.line_s.at[place, step])

    def to_owner(name):
        item, place = buffers(name), places[name]
        others = [lax.rem(z + step, chips) for step in range(1, chips)]
        for chip in others:
            arrived(item.line.at[chip], r.line_r.at[place, chip])
        total = joined(item.own.at[z, c, s], [item.line.at[chip] for chip in others])
        square = total * total
        while square.ndim > 2:
            square = jnp.sum(square, 0)
        square = jnp.sum(jnp.sum(square, 0, keepdims=True), 1, keepdims=True)
        r.sum[...] = r.sum[...] + jnp.broadcast_to(square, (8, LANES))
        if name[0] == "B":
            item.done[...] = total
            return
        item.done[s] = total.astype(LOW)
        layer = grad_items[place][1]
        mine = item.done.at[s]
        away = s != layer
        when(
            away,
            lambda: push(mine, mine, r.done_s.at[place], r.done_r.at[place, s], {"section": jnp.int32(layer)}),
        )
        at_end(away, mine, r.done_s.at[place])

    def collect(name):
        item, place = buffers(name), places[name]
        layer = grad_items[place][1]

        def work():
            for section in range(SECTIONS):
                if section != layer:
                    arrived(item.done.at[section], r.done_r.at[place, section])
            columns = item.done.shape[-1]
            start = 3 * width if name[0] == "O" else 0
            for section in range(SECTIONS):
                for half in range(2):
                    rows = pl.ds(section * (rows_a // SECTIONS), rows_a // SECTIONS)
                    place_to = pl.ds(start + half * columns, columns)
                    r.grad_a[rows, place_to] = item.done[section, half].astype(WIDE)

        when(s == layer, work)

    def all_sent():
        for condition, source, sem in finish:
            when(condition, functools.partial(sent, source, sem))
        finish.clear()

    small_out(0, r.tiles.at[d, s])
    start_line(0)
    spread_plane(0, z)
    rows_plane()
    line_step(0, 1)
    rows_relay()
    line_step(0, 2)
    rows_line()
    start_line(2)
    for step in range(3, chips):
        line_step(0, step)
    small_group(0, r.tiles.at[pl.ds(0, devices - 1), 0])
    for peer in plane:
        push(r.tiles.at[:, s], r.tiles.at[:, s], r.small_s.at[0, 1], r.small_r.at[0, 1], peer)
    prepare_masks()
    rows_step(1)
    plane_step(0)
    for step in range(2, chips):
        rows_step(step)
    spread_plane(2, z)
    for step in range(1, chips):
        line_step(2, step)
    own_x.wait()
    own_cot.wait()
    relay_step(0)
    small_plane(0, r.tiles.at[:, pl.ds(0, SECTIONS - 1)])
    for slot in range(4):
        arrived(whole_a, r.gs_r.at[slot])
    attention(0)
    normalize(0)
    expand(1)
    arrived(whole_b, r.gs_r.at[4])
    contract(1)
    normalize(1)
    plane_step(2)
    attention(2)
    normalize(2)
    expand(3)
    relay_step(2)
    arrived(whole_b, r.gs_r.at[5])
    contract(3)
    normalize(3)

    r.sum[...] = jnp.zeros((8, LANES), WIDE)
    back_normalize(3)
    back_contract(3)
    to_core("B1")
    back_expand(3)
    to_core("F3")
    to_plane("B1")
    back_expand_end(3)
    back_normalize(2)
    back_output(2)
    to_core("O2")
    to_plane("F3")
    back_heads(2, 0, 2)
    through_plane("B1")
    to_plane("O2")
    back_heads(2, 2, 2)
    through_plane("F3")
    to_line("B1")
    back_packed(2)
    to_core("K2")
    through_plane("O2")
    back_packed_end(2)
    to_line("F3")
    back_normalize(1)
    to_plane("K2")
    to_owner("B1")
    back_contract(1)
    to_core("B0")
    to_line("O2")
    back_expand(1)
    to_core("F1")
    through_plane("K2")
    to_plane("B0")
    to_owner("F3")
    back_expand_end(1)
    back_normalize(0)
    back_output(0)
    to_core("O0")
    to_plane("F1")
    to_owner("O2")
    to_line("K2")
    back_heads(0, 0, 2)
    through_plane("B0")
    to_plane("O0")
    back_heads(0, 2, 2)
    through_plane("F1")
    to_line("B0")
    to_owner("K2")
    back_packed(0)
    to_core("K0")
    small_out(1, r.ng.at[d])
    through_plane("O0")
    to_line("F1")
    back_packed_end(0)
    to_plane("K0")
    to_owner("B0")
    to_line("O0")
    all_sent()
    through_plane("K0")
    to_owner("F1")
    to_owner("O0")
    small_group(1, r.ng.at[pl.ds(0, devices - 1)])
    r.ns[s] = functools.reduce(lambda left, right: left + right, [r.ng[index] for index in range(devices)])
    small_plane_out(1, r.ns.at[s])
    for name in ("F3", "O2", "K2", "F1"):
        collect(name)
    to_line("K0")
    collect("O0")
    for layer in range(2):
        done = buffers("B%d" % layer).done
        r.grad_b[layer] = done[...].reshape(cols_b, rows_b).T
    small_plane(1, r.ns.at[pl.ds(0, SECTIONS - 1)])
    grads = functools.reduce(lambda left, right: left + right, [r.ns[index] for index in range(SECTIONS)])
    norm_square = jnp.sum(jnp.sum(grads * grads, 0, keepdims=True), 1, keepdims=True)
    chosen = jnp.zeros((2, width), WIDE)
    for layer in range(4):
        chosen = jnp.where(s == layer, grads[2 * layer : 2 * layer + 2, :], chosen)
    for chip in range(chips):
        pair_of = chosen[:, chip * LANES : (chip + 1) * LANES]
        r.grad_n[...] = jnp.where(
            z == chip, jnp.where(c == 0, pair_of[:, :rows_a], pair_of[:, rows_a:]), r.grad_n[...]
        )
    to_owner("K0")

    r.sq[d] = r.sum[...]
    small_out(2, r.sq.at[d])
    collect("K0")
    small_group(2, r.sq.at[pl.ds(0, devices - 1)])
    r.sqs[s] = functools.reduce(lambda left, right: left + right, [r.sq[index] for index in range(devices)])
    small_plane_out(2, r.sqs.at[s])
    all_sent()
    small_plane(2, r.sqs.at[pl.ds(0, SECTIONS - 1)])
    squares = functools.reduce(lambda left, right: left + right, [r.sqs[index] for index in range(SECTIONS)])
    r.square[...] = squares + norm_square


def step_call(tokens, cotangent, lengths, mat_a, mat_b, norms):
    rows_a, hidden = mat_a.shape[1:]
    rows_b, cols_b = mat_b.shape[1:]
    width = tokens.shape[1]
    length = tokens.shape[0] // lengths.shape[0]
    chips = width // rows_a // 2
    scratch = kernel_scratch(chips, rows_a, rows_b, cols_b, length, width, hidden)
    shapes = []
    for _, shape, kind in scratch:
        shapes.append(pltpu.SemaphoreType.DMA(shape) if kind is None else pltpu.VMEM(shape, kind))
    anywhere, vmem = pl.BlockSpec(memory_space=pl.ANY), pl.BlockSpec(memory_space=pltpu.VMEM)
    return pl.pallas_call(
        functools.partial(step_kernel, INPUTS + OUTPUTS + tuple(name for name, _, _ in scratch)),
        out_shape=(
            jax.ShapeDtypeStruct((rows_a, hidden), WIDE),
            jax.ShapeDtypeStruct(mat_b.shape, WIDE),
            jax.ShapeDtypeStruct((2, rows_a), WIDE),
            jax.ShapeDtypeStruct((8, LANES), WIDE),
            jax.ShapeDtypeStruct((length, width), LOW),
            jax.ShapeDtypeStruct((length, width), WIDE),
        ),
        in_specs=[anywhere, anywhere, pl.BlockSpec(memory_space=pltpu.SMEM), vmem, vmem, vmem],
        out_specs=[vmem] * len(OUTPUTS),
        scratch_shapes=shapes,
        compiler_params=pltpu.CompilerParams(
            collective_id=0, has_side_effects=True, vmem_limit_bytes=KERNEL_VMEM
        ),
    )(tokens, cotangent, lengths, mat_a, mat_b, norms)


def update_kernel(*refs):
    square, output, input_grad = (ref[...] for ref in refs[:3])
    grad_norm = jnp.sqrt(square[0:1, 0:1])
    factor = CLIP_NORM / jnp.maximum(grad_norm, CLIP_NORM)
    inputs, outputs = refs[3:15], refs[15:]
    outputs[0][...] = grad_norm
    outputs[1][0] = output
    outputs[2][0] = input_grad
    for group, (rate, decay) in enumerate(
        ((MATRIX_RATE, MATRIX_DECAY), (MATRIX_RATE, MATRIX_DECAY), (NORM_RATE, 0.0))
    ):
        grad, weight, one, two = inputs[4 * group : 4 * group + 4]
        clip = grad[...].reshape(weight.shape) * factor
        moment, square_new, master = adam_update(weight[...], one[...], two[...], clip, rate, decay)
        for ref, value in zip(
            outputs[3 + 5 * group : 8 + 5 * group], (clip, moment, square_new, master, master.astype(LOW))
        ):
            ref[...] = value


def kernel_body(
    tokens, cotangent, lengths, mat_a, mat_b, norms, first_a, second_a, first_b, second_b, first_n, second_n
):
    norms, first_n, second_n = (jnp.swapaxes(value, 1, 2) for value in (norms, first_n, second_n))
    grad_a, grad_b, grad_n, square, output, input_grad = step_call(
        tokens, cotangent, lengths, mat_a, mat_b, norms
    )
    steps = 4

    def cut(value, dim):
        shape = tuple(size // steps if at == dim else size for at, size in enumerate(value.shape))
        return pl.BlockSpec(shape, lambda step: tuple(step if at == dim else 0 for at in range(len(shape))))

    def whole(value):
        return pl.BlockSpec(value.shape, lambda step: (0,) * len(value.shape))

    def like(value, kind=WIDE):
        return jax.ShapeDtypeStruct(value.shape, kind)

    args = (square, output, input_grad, grad_a, mat_a, first_a, second_a, grad_b, mat_b, first_b, second_b)
    specs = [whole(square), cut(output, 0), cut(input_grad, 0)]
    specs += [cut(grad_a, 0)] + [cut(mat_a, 1)] * 3 + [cut(grad_b, 1)] * 4
    args += (grad_n, norms, first_n, second_n)
    specs += [whole(grad_n)] + [whole(norms)] * 3
    shapes = [jax.ShapeDtypeStruct((1, 1), WIDE), like(output[None], LOW), like(input_grad[None])]
    out_specs = [whole(shapes[0]), cut(shapes[1], 1), cut(shapes[2], 1)]
    for value, spec in ((mat_a, cut(mat_a, 1)), (mat_b, cut(mat_b, 1)), (norms, whole(norms))):
        shapes += [like(value)] * 4 + [like(value, LOW)]
        out_specs += [spec] * 5
    results = pl.pallas_call(
        update_kernel,
        grid=(steps,),
        out_shape=shapes,
        in_specs=specs,
        out_specs=out_specs,
        compiler_params=pltpu.CompilerParams(vmem_limit_bytes=KERNEL_VMEM),
    )(*args)
    results = [results[0][0, 0], *results[1:]]
    results[-5:] = [jnp.swapaxes(value, 1, 2) for value in results[-5:]]
    return tuple(results)


def chosen_body(*args):
    rows_a = args[3].shape[1]
    groups = lax.axis_size("dp")
    by_kernel = rows_a % 32 == 0 and 2 * rows_a == LANES and groups * rows_a == args[0].shape[1]
    return (kernel_body if by_kernel else body)(*args)


def solution(mesh):
    placed = (
        P("dp", None),
        P("dp", None),
        P("dp", None),
        P("section", "dp", None),
        P(None, "dp", "section"),
        P("section", "dp", None),
        P("section", "dp", None),
        P("section", "dp", None),
        P(None, "dp", "section"),
        P(None, "dp", "section"),
        P("section", "dp", None),
        P("section", "dp", None),
    )
    return jax.shard_map(
        chosen_body,
        mesh=mesh,
        in_specs=placed,
        out_specs=(
            P(),
            P("section", "dp", None),
            P("section", "dp", None),
            P("section", "dp", None),
            P("section", "dp", None),
            P("section", "dp", None),
            P("section", "dp", None),
            P("section", "dp", None),
            P(None, "dp", "section"),
            P(None, "dp", "section"),
            P(None, "dp", "section"),
            P(None, "dp", "section"),
            P(None, "dp", "section"),
            P("section", "dp", None),
            P("section", "dp", None),
            P("section", "dp", None),
            P("section", "dp", None),
            P("section", "dp", None),
        ),
        check_vma=False,
    )
```

```python
import functools
import types

import jax
import jax.numpy as jnp
from jax import lax
from jax.experimental import pallas as pl
from jax.experimental.pallas import tpu as pltpu
from jax.sharding import PartitionSpec as P

HEADS = 8
STEP = 5


EPSILON = 1e-05
NEGATIVE = -1e30
CLIP_NORM = 1.0
BETA_ONE = 0.5
BETA_TWO = 0.5
ADAM_EPSILON = 1e-08
MATRIX_RATE = 0.05
NORM_RATE = 0.5
MATRIX_DECAY = 0.01


def norm_stats(value):
    centre = value - jnp.mean(value, -1, keepdims=True)
    inverse = lax.rsqrt(jnp.mean(centre * centre, -1, keepdims=True) + EPSILON)
    return (centre * inverse, inverse)


def norm_back(normal, inverse, upstream):
    return inverse * (
        upstream
        - jnp.mean(upstream, -1, keepdims=True)
        - normal * jnp.mean(upstream * normal, -1, keepdims=True)
    )


def adam_update(weight, moment_one, moment_two, gradient, step_rate, decay_rate):
    first_new = BETA_ONE * moment_one + (1.0 - BETA_ONE) * gradient
    second_new = BETA_TWO * moment_two + (1.0 - BETA_TWO) * gradient * gradient
    first_hat = first_new / (1.0 - BETA_ONE**STEP)
    second_hat = second_new / (1.0 - BETA_TWO**STEP)
    weight_new = weight - step_rate * (
        first_hat / (jnp.sqrt(second_hat) + ADAM_EPSILON) + decay_rate * weight
    )
    return (first_new, second_new, weight_new)


def segments_of(lengths_row, length):
    ends = jnp.cumsum(lengths_row, dtype=jnp.int32)
    places = jnp.arange(length, dtype=jnp.int32)
    segment = jnp.sum((ends[None, :] <= places[:, None]).astype(jnp.int32), axis=1, dtype=jnp.int32)
    live = (places < ends[-1]).astype(jnp.float32)
    return segment, live


def matmul(left, right, dims):
    return lax.dot_general(left, right, (dims, ((), ())), preferred_element_type=jnp.float32)


NN = ((1,), (0,))
NT = ((1,), (1,))
TN = ((0,), (0,))


def attention_forward(stream, weight, mask):
    length, width = stream.shape
    size = width // HEADS
    packed = matmul(stream, weight[:, : 3 * width], NN).astype(jnp.bfloat16)
    heads = packed.reshape(length, 3, HEADS, size)
    scores = jnp.einsum("qhd,khd->hqk", heads[:, 0], heads[:, 1], preferred_element_type=jnp.float32)
    scores = jnp.where(mask[None], scores * size**-0.5, NEGATIVE)
    weights = jnp.exp(scores - jnp.max(scores, -1, keepdims=True))
    probs = weights / jnp.sum(weights, -1, keepdims=True)
    mixed = jnp.einsum("hqk,khd->qhd", probs.astype(jnp.bfloat16), heads[:, 2], preferred_element_type=jnp.float32)
    mixed = mixed.reshape(length, width).astype(jnp.bfloat16)
    branch = matmul(mixed, weight[:, 3 * width :], NN)
    return branch, (heads, probs, mixed)


def attention_backward(stream, weight, kept, grad_low):
    heads, probs, mixed = kept
    length, width = stream.shape
    size = width // HEADS
    grad_out = matmul(mixed, grad_low, TN)
    grad_mixed = matmul(grad_low, weight[:, 3 * width :], NT).astype(jnp.bfloat16)
    grad_mixed = grad_mixed.reshape(length, HEADS, size)
    grad_probs = jnp.einsum("qhd,khd->hqk", grad_mixed, heads[:, 2], preferred_element_type=jnp.float32)
    centre = jnp.sum(probs * grad_probs, -1, keepdims=True)
    grad_scores = (probs * (grad_probs - centre)).astype(jnp.bfloat16)
    low = probs.astype(jnp.bfloat16)
    scale = size**-0.5
    grad_q = jnp.einsum("hqk,khd->qhd", grad_scores, heads[:, 1], preferred_element_type=jnp.float32) * scale
    grad_k = jnp.einsum("hqk,qhd->khd", grad_scores, heads[:, 0], preferred_element_type=jnp.float32) * scale
    grad_v = jnp.einsum("hqk,qhd->khd", low, grad_mixed, preferred_element_type=jnp.float32)
    packed = jnp.concatenate([grad_q, grad_k, grad_v], axis=1).reshape(length, 3 * width)
    packed = packed.astype(jnp.bfloat16)
    grad_in = matmul(stream, packed, TN)
    grad_inputs = matmul(packed, weight[:, : 3 * width], NT)
    return grad_inputs, jnp.concatenate([grad_in, grad_out], axis=1)


def feed_forward(stream, weight, down):
    pre = matmul(stream, weight, NN)
    active = jax.nn.gelu(pre, approximate=True).astype(jnp.bfloat16)
    return matmul(active, down, NN), (pre, active)


def feed_backward(stream, weight, down, kept, grad_low):
    pre, active = kept
    grad_down = matmul(active, grad_low, TN)
    grad_active = matmul(grad_low, down, NT)
    pull = jax.vjp(lambda value: jax.nn.gelu(value, approximate=True), pre)[1]
    grad_pre = pull(grad_active)[0].astype(jnp.bfloat16)
    grad_up = matmul(stream, grad_pre, TN)
    return matmul(grad_pre, weight, NT), grad_up, grad_down


def micro_step(rows, pull, segment, mats, downs, gains, biases):
    low = jnp.bfloat16
    mask = segment[:, None] == segment[None, :]
    stream, dual = rows, jnp.zeros_like(rows)
    saved = []
    for sub in range(4):
        if sub % 2 == 0:
            branch, kept = attention_forward(stream, mats[sub], mask)
        else:
            branch, kept = feed_forward(stream, mats[sub], downs[sub // 2])
        normal, inverse = norm_stats(stream.astype(jnp.float32) + branch)
        out = normal * gains[sub] + biases[sub]
        total = dual.astype(jnp.float32) + branch
        saved.append((stream, kept, normal, inverse))
        if sub < 3:
            stream, dual = out.astype(low), total.astype(low)
    dual_normal, dual_inverse = norm_stats(total)
    output = (out + dual_normal).astype(low)
    grad_out, grad_dual = pull, norm_back(dual_normal, dual_inverse, pull)
    grads_a, grads_b, grads_n = [None] * 4, [None] * 2, [None] * 4
    for sub in (3, 2, 1, 0):
        stream, kept, normal, inverse = saved[sub]
        grads_n[sub] = jnp.stack([jnp.sum(grad_out * normal, 0), jnp.sum(grad_out, 0)], axis=1)
        summed = norm_back(normal, inverse, grad_out * gains[sub])
        branch_low = (summed + grad_dual).astype(low)
        if sub % 2 == 0:
            inner, grads_a[sub] = attention_backward(stream, mats[sub], kept, branch_low)
        else:
            inner, grads_a[sub], grads_b[sub // 2] = feed_backward(
                stream, mats[sub], downs[sub // 2], kept, branch_low
            )
        grad_in = summed + inner
        if sub > 0:
            grad_out = grad_in.astype(low).astype(jnp.float32)
            grad_dual = grad_dual.astype(low).astype(jnp.float32)
    return output, grad_in, jnp.stack(grads_a), jnp.stack(grads_b), jnp.stack(grads_n)


def finish_step(grad_norm, output, input_grad, *groups):
    factor = CLIP_NORM / jnp.maximum(grad_norm, CLIP_NORM)
    results = [grad_norm, output[None], input_grad[None]]
    for weight, one, two, grad, rate, decay in groups:
        clip = grad * factor
        moment, square_new, master = adam_update(weight, one, two, clip, rate, decay)
        results += [clip, moment, square_new, master, master.astype(jnp.bfloat16)]
    return tuple(results)


def body(
    tokens, cotangent, lengths, mat_a, mat_b, norms, first_a, second_a, first_b, second_b, first_n, second_n
):
    low = jnp.bfloat16
    own = lax.axis_index("section")
    length = tokens.shape[0] // lengths.shape[0]
    rows = lax.dynamic_slice_in_dim(tokens, own * length, length, 0)
    segment, live = segments_of(lax.dynamic_index_in_dim(lengths, own, 0, keepdims=False), length)
    pull = lax.dynamic_slice_in_dim(cotangent, own * length, length, 0).astype(jnp.float32) * live[:, None]

    def gathered(value):
        return lax.all_gather(lax.all_gather(value, "dp", axis=1, tiled=True), "section", axis=0, tiled=True)

    mats = gathered(mat_a.astype(low))
    scales = gathered(norms.astype(low)).astype(jnp.float32)
    downs = lax.all_gather(mat_b.astype(low), "section", axis=2, tiled=True)
    downs = lax.all_gather(downs, "dp", axis=1, tiled=True)
    output, input_grad, part_a, part_b, part_n = micro_step(
        rows, pull, segment, mats, downs, scales[:, :, 0], scales[:, :, 1]
    )

    def scattered(value, section_dim):
        value = lax.psum_scatter(value, "section", scatter_dimension=section_dim, tiled=True)
        return lax.psum_scatter(value, "dp", scatter_dimension=1, tiled=True).astype(jnp.float32)

    grad_a = scattered(part_a.astype(low), 0)
    grad_b = scattered(part_b.astype(low), 2)
    grad_n = scattered(part_n, 0)
    square = jnp.sum(grad_a * grad_a) + jnp.sum(grad_b * grad_b) + jnp.sum(grad_n * grad_n)
    grad_norm = jnp.sqrt(lax.psum(square, ("section", "dp")))
    return finish_step(
        grad_norm, output, input_grad,
        (mat_a, first_a, second_a, grad_a, MATRIX_RATE, MATRIX_DECAY),
        (mat_b, first_b, second_b, grad_b, MATRIX_RATE, MATRIX_DECAY),
        (norms, first_n, second_n, grad_n, NORM_RATE, 0.0),
    )


LOW = jnp.bfloat16
WIDE = jnp.float32
MESH = pl.DeviceIdType.MESH
SECTIONS = 4
LANES = 128
BLOCK = 64
KERNEL_VMEM = 64 * 1024 * 1024 - 256 * 1024


def gradient_items(rows_a, rows_b, cols_b, width, hidden):
    part = rows_a // SECTIONS
    return (
        ("B1", 3, cols_b // 2, rows_b),
        ("F3", 3, part, hidden // 2),
        ("O2", 2, part, width // 2),
        ("K2", 2, part, 3 * width // 2),
        ("B0", 1, cols_b // 2, rows_b),
        ("F1", 1, part, hidden // 2),
        ("O0", 0, part, width // 2),
        ("K0", 0, part, 3 * width // 2),
    )


def item_scratch(name, chips, rows, columns):
    piece = (rows, columns)
    return (
        ("own" + name, (chips, SECTIONS, 2) + piece, LOW),
        ("farx" + name, (chips,) + piece, LOW),
        ("fary" + name, (chips,) + piece, LOW),
        ("nearx" + name, (2, chips) + piece, LOW),
        ("neary" + name, (2, chips) + piece, LOW),
        ("line" + name, (chips, 2) + piece, LOW),
        ("done" + name, (2,) + piece if name[0] == "B" else (SECTIONS, 2) + piece, WIDE if name[0] == "B" else LOW),
    )


def kernel_scratch(chips, rows_a, rows_b, cols_b, length, width, hidden):
    devices = 2 * chips
    items = gradient_items(rows_a, rows_b, cols_b, width, hidden)
    count = len(items)
    received = sum((item_scratch(name, chips, rows, columns) for name, _, rows, columns in items), ())
    return received + (
        ("fac_s", (32,), None),
        ("fac_r", (32,), None),
        ("px_s", (count, 3), None),
        ("px_r", (count, 3), None),
        ("py_s", (count, 3), None),
        ("py_r", (count, 3), None),
        ("line_s", (count, chips), None),
        ("line_r", (count, chips), None),
        ("done_s", (count,), None),
        ("done_r", (count, SECTIONS), None),
        ("wa", (4, width, hidden), LOW),
        ("wb", (2, hidden, width), LOW),
        ("tiles", (devices, SECTIONS, 8, LANES), WIDE),
        ("x", (4, length, width), LOW),
        ("xt", (4, chips, 2, rows_a, length), LOW),
        ("xtc", (4, chips, rows_a, 2 * length), LOW),
        ("y", (length, width), LOW),
        ("cot", (length, width), LOW),
        ("bias", (length, length), WIDE),
        ("live", (length, 1), WIDE),
        ("f", (length, width), WIDE),
        ("n", (4, length, width), WIDE),
        ("inv", (4, length, 1), WIDE),
        ("q", (2, length, width), LOW),
        ("k", (2, length, width), LOW),
        ("v", (2, length, width), LOW),
        ("kt", (2, width, length), LOW),
        ("vt", (2, width, length), LOW),
        ("ot", (2, chips, 2, rows_a, length), LOW),
        ("otc", (2, chips, rows_a, 2 * length), LOW),
        ("pt", (2, HEADS, length, length), LOW),
        ("g", (2, length, hidden), LOW),
        ("gc", (2, chips, 2 * length, rows_b), LOW),
        ("slope", (2, length, hidden), LOW),
        ("gx", (length, width), WIDE),
        ("gy", (length, width), WIDE),
        ("df", (2, 2 * length, width), LOW),
        ("dft", (2, width, 2 * length), LOW),
        ("dm", (length, width), LOW),
        ("dqt", (width, length), LOW),
        ("dh", (2, 2 * length, hidden), LOW),
        ("dp", (2, 2 * length, 3 * width), LOW),
        ("ng", (devices, 8, width), WIDE),
        ("ns", (SECTIONS, 8, width), WIDE),
        ("sq", (devices, 8, LANES), WIDE),
        ("sqs", (SECTIONS, 8, LANES), WIDE),
        ("sum", (8, LANES), WIDE),
        ("in_s", (2,), None),
        ("gz_s", (3, 2, chips, 2), None),
        ("gz_r", (3, chips, 2), None),
        ("gx_s", (3, chips, 2), None),
        ("gx_r", (3, chips, 2), None),
        ("gy_s", (3, chips, 2), None),
        ("gy_r", (3, chips, 2), None),
        ("gxr_s", (3, chips), None),
        ("gxr_r", (3, chips), None),
        ("gyr_s", (3, chips), None),
        ("gyr_r", (3, chips), None),
        ("gs_s", (6,), None),
        ("gs_r", (6,), None),
        ("small_s", (3, 2), None),
        ("small_r", (3, 2), None),
    )


INPUTS = ("tokens", "cotangent", "lengths", "mat_a", "mat_b", "norms")
OUTPUTS = ("grad_a", "grad_b", "grad_n", "square", "output", "input_grad")


def step_kernel(names, *refs):
    r = types.SimpleNamespace(**dict(zip(names, refs)))
    width, hidden = r.wa.shape[1:]
    length = r.x.shape[1]
    rows_a, (rows_b, cols_b) = r.mat_a.shape[1], r.mat_b.shape[1:]
    devices = r.tiles.shape[0]
    chips = devices // 2
    half_a, half_b = rows_a // 2, cols_b // 2
    grad_items = gradient_items(rows_a, rows_b, cols_b, width, hidden)
    head = width // HEADS
    scale = head**-0.5

    s, d = lax.axis_index("section"), lax.axis_index("dp")
    z, c = lax.div(d, 2), lax.rem(d, 2)
    sx = s + 1 - 2 * lax.rem(s, 2)
    sy = lax.rem(s + 2, SECTIONS)
    sd = SECTIONS - 1 - s
    to_sibling = {"dp": d + 1 - 2 * c}
    to_up, to_down = {"dp": d + 2}, {"dp": d - 2}
    to_x, to_y = {"section": sx}, {"section": sy}
    below, above = z > 0, z < chips - 1
    group = [{"dp": lax.rem(d + step, devices)} for step in range(1, devices)]
    plane = [{"section": lax.rem(s + step, SECTIONS)} for step in range(1, SECTIONS)]
    finish = []

    def when(condition, work):
        if condition is None:
            work()
        else:
            pl.when(condition)(work)

    def push(source, target, send_sem, recv_sem, device):
        pltpu.make_async_remote_copy(
            src_ref=source,
            dst_ref=target,
            send_sem=send_sem,
            recv_sem=recv_sem,
            device_id=device,
            device_id_type=MESH,
        ).start()

    def arrived(target, sem):
        pltpu.make_async_remote_copy(
            src_ref=target, dst_ref=target, send_sem=sem, recv_sem=sem, device_id=to_x, device_id_type=MESH
        ).wait_recv()

    def sent(source, sem):
        pltpu.make_async_remote_copy(
            src_ref=source, dst_ref=source, send_sem=sem, recv_sem=sem, device_id=to_x, device_id_type=MESH
        ).wait_send()

    def at_end(condition, source, sem):
        finish.append((condition, source, sem))

    def aligned(start, size):
        return pl.ds(pl.multiple_of(start, size), size)

    own_x = pltpu.make_async_copy(r.tokens.at[aligned(s * length, length)], r.x.at[0], r.in_s.at[0])
    own_cot = pltpu.make_async_copy(r.cotangent.at[aligned(s * length, length)], r.cot, r.in_s.at[1])
    own_x.start()
    own_cot.start()
    barrier = pltpu.get_barrier_semaphore()
    for peer in group + plane:
        pl.semaphore_signal(barrier, inc=1, device_id=peer, device_id_type=MESH)
    r.wa[s, aligned(d * rows_a, rows_a), :] = r.mat_a[0].astype(LOW)
    for layer in range(2):
        r.wb[layer, aligned(d * rows_b, rows_b), aligned(s * cols_b, cols_b)] = r.mat_b[layer].astype(LOW)
    norms = r.norms[0].astype(LOW).astype(WIDE)
    nothing = jnp.zeros((2, rows_a), WIDE)
    even = jnp.concatenate([norms, nothing], axis=1)
    odd = jnp.concatenate([nothing, norms], axis=1)
    r.tiles[d, s, 0:2, :] = jnp.where(c == 0, even, odd)
    r.tiles[d, s, 2:8, :] = jnp.zeros((6, LANES), WIDE)
    pl.semaphore_wait(barrier, len(group) + len(plane))

    def small_out(which, source):
        for peer in group:
            push(source, source, r.small_s.at[which, 0], r.small_r.at[which, 0], peer)

    def small_group(which, like):
        arrived(like, r.small_r.at[which, 0])
        sent(like, r.small_s.at[which, 0])

    def small_plane_out(which, source):
        for peer in plane:
            push(source, source, r.small_s.at[which, 1], r.small_r.at[which, 1], peer)

    def small_plane(which, like):
        arrived(like, r.small_r.at[which, 1])
        sent(like, r.small_s.at[which, 1])

    def block_a(section, chip, half):
        return r.wa.at[section, aligned((2 * chip + c) * rows_a + half * half_a, half_a), :]

    def block_b(layer):
        part = rows_b // 2

        def block(section, chip, half):
            return r.wb.at[
                layer,
                aligned((2 * chip + c) * rows_b + half * part, part),
                aligned(section * cols_b, cols_b),
            ]

        return block

    items = (block_a, block_b(0), block_b(1))

    def to_the_sibling(item, section, chip, half):
        block = items[item](section, chip, half)
        slot = section if item == 0 else 3 + item
        push(block, block, r.gs_s.at[slot], r.gs_r.at[slot], to_sibling)

    def spread_plane(item, chip):
        for half in range(2):
            block = items[item](s, chip, half)
            push(block, block, r.gx_s.at[item, chip, half], r.gx_r.at[item, chip, half], to_x)
            push(block, block, r.gy_s.at[item, chip, half], r.gy_r.at[item, chip, half], to_y)
            to_the_sibling(item, s, chip, half)

    def up(item, chip, half):
        block = items[item](s, chip, half)
        push(block, block, r.gz_s.at[item, 0, chip, half], r.gz_r.at[item, chip, half], to_up)

    def down(item, chip, half):
        block = items[item](s, chip, half)
        push(block, block, r.gz_s.at[item, 1, chip, half], r.gz_r.at[item, chip, half], to_down)

    def start_line(item):
        for half in range(2):
            when(above, lambda: up(item, z, half))
            when(below, lambda: down(item, z, half))

    def line_step(item, step):
        def from_below():
            for half in range(2):
                arrived(items[item](s, z - step, half), r.gz_r.at[item, z - step, half])
                when(above, lambda: up(item, z - step, half))
            spread_plane(item, z - step)

        def from_above():
            for half in range(2):
                arrived(items[item](s, z + step, half), r.gz_r.at[item, z + step, half])
                when(below, lambda: down(item, z + step, half))
            spread_plane(item, z + step)

        when(z >= step, from_below)
        when(z + step < chips, from_above)

    def plane_step(item):
        for chip in range(chips):
            for half in range(2):
                arrived(items[item](sx, chip, half), r.gx_r.at[item, chip, half])
                if half == 1:
                    block = items[item](sx, chip, half)
                    push(block, block, r.gyr_s.at[item, chip], r.gyr_r.at[item, chip], to_y)
                to_the_sibling(item, sx, chip, half)
                arrived(items[item](sy, chip, half), r.gy_r.at[item, chip, half])
                if half == 0:
                    block = items[item](sy, chip, half)
                    push(block, block, r.gxr_s.at[item, chip], r.gxr_r.at[item, chip], to_x)
                to_the_sibling(item, sy, chip, half)

    def relay_step(item):
        for chip in range(chips):
            arrived(items[item](sd, chip, 0), r.gxr_r.at[item, chip])
            to_the_sibling(item, sd, chip, 0)
            arrived(items[item](sd, chip, 1), r.gyr_r.at[item, chip])
            to_the_sibling(item, sd, chip, 1)

    whole_a = r.wa.at[0, pl.ds(0, chips * rows_a)]
    whole_b = r.wb.at[0, pl.ds(0, chips * rows_b)]
    def gather_sends(item):
        for chip in range(chips):
            for half in range(2):
                block = items[item](0, chip, half)
                at_end(None, block, r.gx_s.at[item, chip, half])
                at_end(None, block, r.gy_s.at[item, chip, half])
                at_end(above & (z >= chip), block, r.gz_s.at[item, 0, chip, half])
                at_end(below & (z <= chip), block, r.gz_s.at[item, 1, chip, half])
            block = items[item](0, chip, 0)
            at_end(None, block, r.gxr_s.at[item, chip])
            at_end(None, block, r.gyr_s.at[item, chip])

    def row_block(chip, half):
        part = rows_b // 2
        return r.wb.at[0, aligned((2 * chip + c) * rows_b + half * part, part), :]

    def rows_to_sibling(chip, half):
        push(row_block(chip, half), row_block(chip, half), r.gs_s.at[4], r.gs_r.at[4], to_sibling)

    def rows_up(chip, half):
        rows = row_block(chip, half)
        push(rows, rows, r.gz_s.at[1, 0, chip, half], r.gz_r.at[1, chip, half], to_up)

    def rows_down(chip, half):
        rows = row_block(chip, half)
        push(rows, rows, r.gz_s.at[1, 1, chip, half], r.gz_r.at[1, chip, half], to_down)

    def rows_plane():
        for half in range(2):
            block = items[1](s, z, half)
            push(block, block, r.gx_s.at[1, 0, half], r.gx_r.at[1, 0, half], to_x)
            push(block, block, r.gy_s.at[1, 0, half], r.gy_r.at[1, 0, half], to_y)
            at_end(None, block, r.gx_s.at[1, 0, half])
            at_end(None, block, r.gy_s.at[1, 0, half])

    def rows_relay():
        for half in range(2):
            arrived(items[1](sx, z, half), r.gx_r.at[1, 0, half])
            arrived(items[1](sy, z, half), r.gy_r.at[1, 0, half])
        block = items[1](sx, z, 1)
        push(block, block, r.gyr_s.at[1, 0], r.gyr_r.at[1, 0], to_y)
        block = items[1](sy, z, 0)
        push(block, block, r.gxr_s.at[1, 0], r.gxr_r.at[1, 0], to_x)
        at_end(None, block, r.gyr_s.at[1, 0])
        at_end(None, block, r.gxr_s.at[1, 0])

    def rows_line():
        for half, sem in ((0, r.gxr_r), (1, r.gyr_r)):
            arrived(items[1](sd, z, half), sem.at[1, 0])
            when(above, lambda: rows_up(z, half))
            when(below, lambda: rows_down(z, half))
            rows_to_sibling(z, half)
        for chip in range(chips):
            for half in range(2):
                at_end(above & (z >= chip), row_block(chip, half), r.gz_s.at[1, 0, chip, half])
                at_end(below & (z <= chip), row_block(chip, half), r.gz_s.at[1, 1, chip, half])

    def rows_step(step):
        def from_below():
            for half in range(2):
                arrived(row_block(z - step, half), r.gz_r.at[1, z - step, half])
                when(above, lambda: rows_up(z - step, half))
                rows_to_sibling(z - step, half)

        def from_above():
            for half in range(2):
                arrived(row_block(z + step, half), r.gz_r.at[1, z + step, half])
                when(below, lambda: rows_down(z + step, half))
                rows_to_sibling(z + step, half)

        when(z >= step, from_below)
        when(z + step < chips, from_above)

    mine, other = pl.ds(0, length), pl.ds(length, length)

    def give(slot, source, target):
        push(source, target, r.fac_s.at[slot], r.fac_r.at[slot], to_sibling)
        at_end(None, target, r.fac_s.at[slot])

    def taken(slot, target):
        arrived(target, r.fac_r.at[slot])

    def give_rows(layer):
        r.xtc[layer, :, :, 0:length] = r.xt[layer, :, c]
        give(layer, r.xt.at[layer, :, 1 - c], r.xtc.at[layer, :, :, other])

    def product(left, right, dims):
        return lax.dot_general(left, right, (dims, ((), ())), preferred_element_type=WIDE)

    def loop(count, work):
        def one(index, carry):
            work(index)
            return carry

        lax.fori_loop(0, count, one, 0)

    def gain_row(layer, kind):
        parts = [
            r.tiles[2 * chip, layer, kind : kind + 1, :] + r.tiles[2 * chip + 1, layer, kind : kind + 1, :]
            for chip in range(chips)
        ]
        return jnp.concatenate(parts, axis=1)

    def stats(value):
        centre = value - jnp.mean(value, -1, keepdims=True)
        inverse = lax.rsqrt(jnp.mean(centre * centre, -1, keepdims=True) + EPSILON)
        return centre * inverse, inverse

    lane = lax.broadcasted_iota(jnp.int32, (1, 2 * head), 1)
    first_half = (lane < head).astype(WIDE)
    half_masks = (first_half.astype(LOW), (1.0 - first_half).astype(LOW))

    def prepare_masks():
        ends, total = [], jnp.int32(0)
        for slot in range(r.lengths.shape[1]):
            total = total + r.lengths[s, slot]
            ends.append(total)
        down_places = lax.broadcasted_iota(jnp.int32, (length, 1), 0)
        across_places = lax.broadcasted_iota(jnp.int32, (1, length), 1)
        down_segment = jnp.zeros((length, 1), jnp.int32)
        across_segment = jnp.zeros((1, length), jnp.int32)
        for end in ends:
            down_segment = down_segment + (end <= down_places).astype(jnp.int32)
            across_segment = across_segment + (end <= across_places).astype(jnp.int32)
        r.bias[...] = jnp.where(down_segment == across_segment, 0.0, NEGATIVE)
        r.live[...] = (down_places < total).astype(WIDE)

    def attention(layer):
        at = layer // 2
        rows = r.x[layer]
        r.xt[layer] = rows.T.reshape(chips, 2, rows_a, length)
        give_rows(layer)
        r.q[at] = product(rows, r.wa[layer, :, 0:width], NN).astype(LOW) * jnp.asarray(scale, LOW)
        keys = product(rows, r.wa[layer, :, width : 2 * width], NN).astype(LOW)
        r.k[at] = keys
        r.kt[at] = (keys * jnp.asarray(scale, LOW)).T
        values = product(rows, r.wa[layer, :, 2 * width : 3 * width], NN).astype(LOW)
        r.v[at] = values
        r.vt[at] = values.T

        def pair(index):
            lanes = aligned(index * 2 * head, 2 * head)
            for which in range(2):
                scores = product(r.k[at, :, lanes], r.q[at, :, lanes] * half_masks[which], NT) + r.bias[...]
                weights = jnp.exp(scores - jnp.max(scores, 0, keepdims=True))
                probs = (weights * (1.0 / jnp.sum(weights, 0, keepdims=True))).astype(LOW)
                r.pt[at, 2 * index + which] = probs
                place = aligned((2 * index + which) * head, head)
                r.ot[at, index, which] = product(r.vt[at, place, :], probs, NN).astype(LOW)

        def pairs(step):
            pair(2 * step)
            pair(2 * step + 1)

        loop(HEADS // 4, pairs)
        r.otc[at, :, :, 0:length] = r.ot[at, :, c]
        give(4 + at, r.ot.at[at, :, 1 - c], r.otc.at[at, :, :, other])
        r.f[...] = product(r.ot[at].reshape(width, length).T, r.wa[layer, :, 3 * width :], NN)

    def expand(layer):
        at = layer // 2
        r.xt[layer] = r.x[layer].T.reshape(chips, 2, rows_a, length)
        give_rows(layer)

        def columns(index):
            place = pl.ds(index * width, width)
            pre = product(r.x[layer], r.wa[layer, :, place], NN)
            squared = pre * pre
            slope = 0.7978845608 * (1.0 + 3 * 0.044715 * squared)
            bent = jnp.tanh(0.7978845608 * pre * (1.0 + 0.044715 * squared))
            r.g[at, :, place] = (0.5 * pre * (1.0 + bent)).astype(LOW)
            r.slope[at, :, place] = (0.5 * (1.0 + bent) + 0.5 * pre * (1.0 - bent * bent) * slope).astype(LOW)
            block = aligned((2 * index + c) * rows_b, rows_b)
            r.gc[at, index, 0:length, :] = r.g[at, :, block]
            block = aligned((2 * index + 1 - c) * rows_b, rows_b)
            give(6 + chips * at + index, r.g.at[at, :, block], r.gc.at[at, index, other, :])

        for index in range(hidden // width):
            columns(index)

    def contract(layer):
        r.f[...] = product(r.g[layer // 2], r.wb[layer // 2], NN)

    def by_rows(work):
        for index in range(length // BLOCK):
            work(pl.ds(index * BLOCK, BLOCK))

    def normalize(layer):
        gain, offset = gain_row(layer, 0), gain_row(layer, 1)

        def some(rows):
            branch = r.f[rows, :]
            normal, inverse = stats(r.x[layer, rows, :].astype(WIDE) + branch)
            r.n[layer, rows, :] = normal
            r.inv[layer, rows, :] = inverse
            out = normal * gain + offset
            dual = branch if layer == 0 else r.y[rows, :].astype(WIDE) + branch
            if layer < 3:
                r.x[layer + 1, rows, :] = out.astype(LOW)
                r.y[rows, :] = dual.astype(LOW)
            else:
                dual_normal, dual_inverse = stats(dual)
                r.output[rows, :] = (out + dual_normal).astype(LOW)
                pull = r.cot[rows, :].astype(WIDE) * r.live[rows, :]
                r.gx[rows, :] = pull
                r.gy[rows, :] = norm_back(dual_normal, dual_inverse, pull)

        by_rows(some)

    def back_normalize(layer):
        gain = gain_row(layer, 0)

        def some(index, sums):
            rows = pl.ds(index * BLOCK, BLOCK)
            upstream = r.gx[rows, :]
            normal = r.n[layer, rows, :]
            summed = norm_back(normal, r.inv[layer, rows, :], upstream * gain)
            dual = r.gy[rows, :]
            r.gx[rows, :] = summed
            r.df[layer // 2, rows, :] = (summed + dual).astype(LOW)
            if layer == 3:
                r.gy[rows, :] = dual.astype(LOW).astype(WIDE)
            return (
                sums[0] + jnp.sum(upstream * normal, 0, keepdims=True),
                sums[1] + jnp.sum(upstream, 0, keepdims=True),
            )

        zero = jnp.zeros((1, width), WIDE)
        gains, offsets = zero, zero
        for index in range(length // BLOCK):
            gains, offsets = some(index, (gains, offsets))
        r.ng[d, 2 * layer : 2 * layer + 1, :] = gains
        r.ng[d, 2 * layer + 1 : 2 * layer + 2, :] = offsets

    def pass_down(layer, inner):
        total = r.gx[...] + inner
        if layer > 0:
            r.gx[...] = total.astype(LOW).astype(WIDE)
        else:
            r.input_grad[...] = total

    base = 6 + 2 * chips

    def back_hidden(layer):
        at = layer // 2
        r.dft[at, :, 0:length] = r.df[at, 0:length, :].T
        give(base + at, r.dft.at[at, :, mine], r.dft.at[at, :, other])
        for index in range(hidden // width):
            place = pl.ds(index * width, width)
            pulled = product(r.df[at, 0:length, :], r.wb[at, pl.ds(index * width, width), :], NT)
            r.dh[at, 0:length, place] = (pulled * r.slope[at, :, place].astype(WIDE)).astype(LOW)
            give(base + 2 + chips * at + index, r.dh.at[at, mine, place], r.dh.at[at, other, place])

    def back_expand_end(layer):
        pass_down(layer, product(r.dh[layer // 2, 0:length, :], r.wa[layer], NT))

    def back_output(layer):
        at = layer // 2
        give(base + 2 + 2 * chips + at, r.df.at[at, mine], r.df.at[at, other])
        r.dm[...] = product(r.df[at, 0:length, :], r.wa[layer, :, 3 * width :], NT).astype(LOW)

    def back_heads(layer, begin, count):
        at = layer // 2

        def pair(index):
            lanes = aligned(index * 2 * head, 2 * head)
            pulled = r.dm[:, lanes]
            keys, values = [], []
            for which in range(2):
                probs = r.pt[at, 2 * index + which]
                grad = product(r.v[at, :, lanes], pulled * half_masks[which], NT)
                full = probs.astype(WIDE)
                centre = jnp.sum(full * grad, 0, keepdims=True)
                scores = (full * (grad - centre)).astype(LOW)
                keys.append(product(scores, r.q[at, :, lanes], NN))
                values.append(product(probs, pulled, NN))
                place = aligned((2 * index + which) * head, head)
                r.dqt[place, :] = product(r.kt[at, place, :], scores, NN).astype(LOW)
            r.dp[at, 0:length, aligned(width + index * 2 * head, 2 * head)] = jnp.where(
                lane < head, keys[0], keys[1]
            ).astype(LOW)
            r.dp[at, 0:length, aligned(2 * width + index * 2 * head, 2 * head)] = jnp.where(
                lane < head, values[0], values[1]
            ).astype(LOW)

        def pairs(step):
            pair(begin + 2 * step)
            pair(begin + 2 * step + 1)

        loop(count // 2, pairs)

    def back_packed(layer):
        at = layer // 2
        slot = base + 4 + 2 * chips + 2 * at
        place = pl.ds(width, 2 * width)
        give(slot, r.dp.at[at, mine, place], r.dp.at[at, other, place])
        r.dp[at, 0:length, 0:width] = r.dqt[...].T
        place = pl.ds(0, width)
        give(slot + 1, r.dp.at[at, mine, place], r.dp.at[at, other, place])

    def back_packed_end(layer):
        pass_down(layer, product(r.dp[layer // 2, 0:length, :], r.wa[layer, :, 0 : 3 * width], NT))

    def keep(name, half, place, value):
        own = getattr(r, "own" + name)
        own[:, :, half, :, place] = value.astype(LOW).reshape(chips, SECTIONS, rows_a // SECTIONS, value.shape[1])

    def chip_rows(value):
        return value.reshape(chips * rows_a, 2 * length)

    def grad_down(at):
        own = getattr(r, "ownB%d" % at)
        taken(base + at, r.dft.at[at, :, other])
        for chip in range(chips):
            taken(6 + chips * at + chip, r.gc.at[at, chip, other, :])
            value = product(r.dft[at], r.gc[at, chip], NN)
            own[chip] = value.astype(LOW).reshape(SECTIONS, 2, half_b, rows_b)

    def grad_up(layer):
        at = layer // 2
        taken(layer, r.xtc.at[layer, :, :, other])
        for index in range(hidden // width):
            place = pl.ds(index * width, width)
            taken(base + 2 + chips * at + index, r.dh.at[at, other, place])
            value = product(chip_rows(r.xtc[layer]), r.dh[at, :, place], NN)
            keep("F%d" % layer, index // 2, pl.ds(index % 2 * width, width), value)

    def grad_output(layer):
        at = layer // 2
        taken(4 + at, r.otc.at[at, :, :, other])
        taken(base + 2 + 2 * chips + at, r.df.at[at, other])
        for half in range(2):
            place = pl.ds(half * width // 2, width // 2)
            value = product(chip_rows(r.otc[at]), r.df[at, :, place], NN)
            keep("O%d" % layer, half, pl.ds(0, width // 2), value)

    def grad_packed(layer):
        at = layer // 2
        slot = base + 4 + 2 * chips + 2 * at
        taken(layer, r.xtc.at[layer, :, :, other])
        taken(slot, r.dp.at[at, other, pl.ds(width, 2 * width)])
        taken(slot + 1, r.dp.at[at, other, pl.ds(0, width)])
        part = 3 * width // 2
        for half in range(2):
            value = product(chip_rows(r.xtc[layer]), r.dp[at, :, half * part : (half + 1) * part], NN)
            keep("K%d" % layer, half, pl.ds(0, part), value)

    def joined(target, others):
        return functools.reduce(
            lambda left, right: left + right, [ref[...].astype(WIDE) for ref in (target, *others)]
        )

    def add_into(target, others):
        if len(others) == 1:
            target[...] = target[...] + others[0][...]
        else:
            target[...] = joined(target, others).astype(LOW)

    places = {name: place for place, (name, _, _, _) in enumerate(grad_items)}

    def buffers(name):
        parts = ("own", "farx", "fary", "nearx", "neary", "line", "done")
        return types.SimpleNamespace(**{part: getattr(r, part + name) for part in parts})

    def to_plane(name):
        item, place = buffers(name), places[name]

        def over_x(section, half, target, slot):
            push(item.own.at[:, section, half], target, r.px_s.at[place, slot], r.px_r.at[place, slot], to_x)
            at_end(None, item.farx, r.px_s.at[place, slot])

        def over_y(section, half, target, slot):
            push(item.own.at[:, section, half], target, r.py_s.at[place, slot], r.py_r.at[place, slot], to_y)
            at_end(None, item.farx, r.py_s.at[place, slot])

        over_x(sd, 0, item.farx, 2)
        over_y(sd, 1, item.fary, 2)
        over_x(sx, 0, item.nearx.at[0], 0)
        over_y(sy, 1, item.neary.at[1], 1)

    def through_plane(name):
        item, place = buffers(name), places[name]
        own = item.own
        arrived(item.fary, r.py_r.at[place, 2])
        add_into(own.at[:, sx, 1], [item.fary])
        push(own.at[:, sx, 1], item.nearx.at[1], r.px_s.at[place, 1], r.px_r.at[place, 1], to_x)
        at_end(None, item.farx, r.px_s.at[place, 1])
        arrived(item.farx, r.px_r.at[place, 2])
        add_into(own.at[:, sy, 0], [item.farx])
        push(own.at[:, sy, 0], item.neary.at[0], r.py_s.at[place, 0], r.py_r.at[place, 0], to_y)
        at_end(None, item.farx, r.py_s.at[place, 0])

    def to_line(name):
        item, place = buffers(name), places[name]
        own = item.own.at[:, s]
        for half in range(2):
            arrived(item.nearx.at[half], r.px_r.at[place, half])
            arrived(item.neary.at[half], r.py_r.at[place, half])
            add_into(own.at[:, half], [item.nearx.at[half], item.neary.at[half]])
        for step in range(1, chips):
            chip = lax.rem(z + step, chips)
            push(
                own.at[chip],
                item.line.at[z],
                r.line_s.at[place, step],
                r.line_r.at[place, z],
                {"dp": 2 * chip + c},
            )
            at_end(None, item.line.at[0], r.line_s.at[place, step])

    def to_owner(name):
        item, place = buffers(name), places[name]
        others = [lax.rem(z + step, chips) for step in range(1, chips)]
        for chip in others:
            arrived(item.line.at[chip], r.line_r.at[place, chip])
        total = joined(item.own.at[z, s], [item.line.at[chip] for chip in others])
        square = total * total
        while square.ndim > 2:
            square = jnp.sum(square, 0)
        square = jnp.sum(jnp.sum(square, 0, keepdims=True), 1, keepdims=True)
        r.sum[...] = r.sum[...] + jnp.broadcast_to(square, (8, LANES))
        if name[0] == "B":
            item.done[...] = total
            return
        item.done[s] = total.astype(LOW)
        layer = grad_items[place][1]
        mine = item.done.at[s]
        away = s != layer
        when(
            away,
            lambda: push(mine, mine, r.done_s.at[place], r.done_r.at[place, s], {"section": jnp.int32(layer)}),
        )
        at_end(away, mine, r.done_s.at[place])

    def collect(name):
        item, place = buffers(name), places[name]
        layer = grad_items[place][1]

        def work():
            for section in range(SECTIONS):
                if section != layer:
                    arrived(item.done.at[section], r.done_r.at[place, section])
            columns = item.done.shape[-1]
            start = 3 * width if name[0] == "O" else 0
            for section in range(SECTIONS):
                for half in range(2):
                    rows = pl.ds(section * (rows_a // SECTIONS), rows_a // SECTIONS)
                    place_to = pl.ds(start + half * columns, columns)
                    r.grad_a[rows, place_to] = item.done[section, half].astype(WIDE)

        when(s == layer, work)

    def all_sent():
        for condition, source, sem in finish:
            when(condition, functools.partial(sent, source, sem))
        finish.clear()

    small_out(0, r.tiles.at[d, s])
    start_line(0)
    spread_plane(0, z)
    rows_plane()
    line_step(0, 1)
    rows_relay()
    line_step(0, 2)
    rows_line()
    start_line(2)
    for step in range(3, chips):
        line_step(0, step)
    small_group(0, r.tiles.at[pl.ds(0, devices - 1), 0])
    for peer in plane:
        push(r.tiles.at[:, s], r.tiles.at[:, s], r.small_s.at[0, 1], r.small_r.at[0, 1], peer)
    prepare_masks()
    rows_step(1)
    plane_step(0)
    for step in range(2, chips):
        rows_step(step)
    spread_plane(2, z)
    for step in range(1, chips):
        line_step(2, step)
    own_x.wait()
    own_cot.wait()
    relay_step(0)
    small_plane(0, r.tiles.at[:, pl.ds(0, SECTIONS - 1)])
    for slot in range(4):
        arrived(whole_a, r.gs_r.at[slot])
    attention(0)
    normalize(0)
    expand(1)
    arrived(whole_b, r.gs_r.at[4])
    contract(1)
    normalize(1)
    plane_step(2)
    attention(2)
    normalize(2)
    expand(3)
    gather_sends(0)
    for slot in range(5):
        at_end(None, whole_a if slot < 4 else whole_b, r.gs_s.at[slot])
    all_sent()
    relay_step(2)
    arrived(whole_b, r.gs_r.at[5])
    contract(3)
    normalize(3)

    r.sum[...] = jnp.zeros((8, LANES), WIDE)
    back_normalize(3)
    back_hidden(3)
    back_expand_end(3)
    grad_down(1)
    to_plane("B1")
    back_normalize(2)
    grad_up(3)
    to_plane("F3")
    back_output(2)
    back_heads(2, 0, 2)
    through_plane("B1")
    grad_output(2)
    to_plane("O2")
    back_heads(2, 2, 2)
    back_packed(2)
    through_plane("F3")
    back_packed_end(2)
    to_line("B1")
    through_plane("O2")
    back_normalize(1)
    grad_packed(2)
    to_plane("K2")
    back_hidden(1)
    to_line("F3")
    to_line("O2")
    back_expand_end(1)
    grad_down(0)
    to_plane("B0")
    through_plane("K2")
    to_owner("B1")
    back_normalize(0)
    small_out(1, r.ng.at[d])
    grad_up(1)
    to_plane("F1")
    back_output(0)
    to_owner("F3")
    to_owner("O2")
    back_heads(0, 0, 2)
    through_plane("B0")
    to_line("K2")
    grad_output(0)
    to_plane("O0")
    back_heads(0, 2, 2)
    back_packed(0)
    through_plane("F1")
    to_owner("K2")
    grad_packed(0)
    to_plane("K0")
    through_plane("O0")
    to_line("B0")
    back_packed_end(0)
    to_line("F1")
    to_line("O0")
    gather_sends(2)
    at_end(None, whole_b, r.gs_s.at[5])
    all_sent()
    through_plane("K0")
    to_owner("B0")
    to_owner("F1")
    to_owner("O0")
    small_group(1, r.ng.at[pl.ds(0, devices - 1)])
    r.ns[s] = functools.reduce(lambda left, right: left + right, [r.ng[index] for index in range(devices)])
    small_plane_out(1, r.ns.at[s])
    for name in ("F3", "O2", "K2", "F1"):
        collect(name)
    to_line("K0")
    collect("O0")
    for layer in range(2):
        done = buffers("B%d" % layer).done
        r.grad_b[layer] = done[...].reshape(cols_b, rows_b).T
    small_plane(1, r.ns.at[pl.ds(0, SECTIONS - 1)])
    grads = functools.reduce(lambda left, right: left + right, [r.ns[index] for index in range(SECTIONS)])
    norm_square = jnp.sum(jnp.sum(grads * grads, 0, keepdims=True), 1, keepdims=True)
    chosen = jnp.zeros((2, width), WIDE)
    for layer in range(4):
        chosen = jnp.where(s == layer, grads[2 * layer : 2 * layer + 2, :], chosen)
    for chip in range(chips):
        pair_of = chosen[:, chip * LANES : (chip + 1) * LANES]
        r.grad_n[...] = jnp.where(
            z == chip, jnp.where(c == 0, pair_of[:, :rows_a], pair_of[:, rows_a:]), r.grad_n[...]
        )
    to_owner("K0")

    r.sq[d] = r.sum[...]
    small_out(2, r.sq.at[d])
    collect("K0")
    small_group(2, r.sq.at[pl.ds(0, devices - 1)])
    r.sqs[s] = functools.reduce(lambda left, right: left + right, [r.sq[index] for index in range(devices)])
    small_plane_out(2, r.sqs.at[s])
    all_sent()
    small_plane(2, r.sqs.at[pl.ds(0, SECTIONS - 1)])
    squares = functools.reduce(lambda left, right: left + right, [r.sqs[index] for index in range(SECTIONS)])
    r.square[...] = squares + norm_square


def step_call(tokens, cotangent, lengths, mat_a, mat_b, norms):
    rows_a, hidden = mat_a.shape[1:]
    rows_b, cols_b = mat_b.shape[1:]
    width = tokens.shape[1]
    length = tokens.shape[0] // lengths.shape[0]
    chips = width // rows_a // 2
    scratch = kernel_scratch(chips, rows_a, rows_b, cols_b, length, width, hidden)
    shapes = []
    for _, shape, kind in scratch:
        shapes.append(pltpu.SemaphoreType.DMA(shape) if kind is None else pltpu.VMEM(shape, kind))
    anywhere, vmem = pl.BlockSpec(memory_space=pl.ANY), pl.BlockSpec(memory_space=pltpu.VMEM)
    return pl.pallas_call(
        functools.partial(step_kernel, INPUTS + OUTPUTS + tuple(name for name, _, _ in scratch)),
        out_shape=(
            jax.ShapeDtypeStruct((rows_a, hidden), WIDE),
            jax.ShapeDtypeStruct(mat_b.shape, WIDE),
            jax.ShapeDtypeStruct((2, rows_a), WIDE),
            jax.ShapeDtypeStruct((8, LANES), WIDE),
            jax.ShapeDtypeStruct((length, width), LOW),
            jax.ShapeDtypeStruct((length, width), WIDE),
        ),
        in_specs=[anywhere, anywhere, pl.BlockSpec(memory_space=pltpu.SMEM), vmem, vmem, vmem],
        out_specs=[vmem] * len(OUTPUTS),
        scratch_shapes=shapes,
        compiler_params=pltpu.CompilerParams(
            collective_id=0, has_side_effects=True, vmem_limit_bytes=KERNEL_VMEM
        ),
    )(tokens, cotangent, lengths, mat_a, mat_b, norms)


def update_kernel(*refs):
    square, output, input_grad = (ref[...] for ref in refs[:3])
    grad_norm = jnp.sqrt(square[0:1, 0:1])
    factor = CLIP_NORM / jnp.maximum(grad_norm, CLIP_NORM)
    inputs, outputs = refs[3:15], refs[15:]
    outputs[0][...] = grad_norm
    outputs[1][0] = output
    outputs[2][0] = input_grad
    for group, (rate, decay) in enumerate(
        ((MATRIX_RATE, MATRIX_DECAY), (MATRIX_RATE, MATRIX_DECAY), (NORM_RATE, 0.0))
    ):
        grad, weight, one, two = inputs[4 * group : 4 * group + 4]
        clip = grad[...].reshape(weight.shape) * factor
        moment, square_new, master = adam_update(weight[...], one[...], two[...], clip, rate, decay)
        for ref, value in zip(
            outputs[3 + 5 * group : 8 + 5 * group], (clip, moment, square_new, master, master.astype(LOW))
        ):
            ref[...] = value


def kernel_body(
    tokens, cotangent, lengths, mat_a, mat_b, norms, first_a, second_a, first_b, second_b, first_n, second_n
):
    norms, first_n, second_n = (jnp.swapaxes(value, 1, 2) for value in (norms, first_n, second_n))
    grad_a, grad_b, grad_n, square, output, input_grad = step_call(
        tokens, cotangent, lengths, mat_a, mat_b, norms
    )
    steps = 4

    def cut(value, dim):
        shape = tuple(size // steps if at == dim else size for at, size in enumerate(value.shape))
        return pl.BlockSpec(shape, lambda step: tuple(step if at == dim else 0 for at in range(len(shape))))

    def whole(value):
        return pl.BlockSpec(value.shape, lambda step: (0,) * len(value.shape))

    def like(value, kind=WIDE):
        return jax.ShapeDtypeStruct(value.shape, kind)

    args = (square, output, input_grad, grad_a, mat_a, first_a, second_a, grad_b, mat_b, first_b, second_b)
    specs = [whole(square), cut(output, 0), cut(input_grad, 0)]
    specs += [cut(grad_a, 0)] + [cut(mat_a, 1)] * 3 + [cut(grad_b, 1)] * 4
    args += (grad_n, norms, first_n, second_n)
    specs += [whole(grad_n)] + [whole(norms)] * 3
    shapes = [jax.ShapeDtypeStruct((1, 1), WIDE), like(output[None], LOW), like(input_grad[None])]
    out_specs = [whole(shapes[0]), cut(shapes[1], 1), cut(shapes[2], 1)]
    for value, spec in ((mat_a, cut(mat_a, 1)), (mat_b, cut(mat_b, 1)), (norms, whole(norms))):
        shapes += [like(value)] * 4 + [like(value, LOW)]
        out_specs += [spec] * 5
    results = pl.pallas_call(
        update_kernel,
        grid=(steps,),
        out_shape=shapes,
        in_specs=specs,
        out_specs=out_specs,
        compiler_params=pltpu.CompilerParams(vmem_limit_bytes=KERNEL_VMEM),
    )(*args)
    results = [results[0][0, 0], *results[1:]]
    results[-5:] = [jnp.swapaxes(value, 1, 2) for value in results[-5:]]
    return tuple(results)


def chosen_body(*args):
    rows_a = args[3].shape[1]
    groups = lax.axis_size("dp")
    by_kernel = rows_a % 32 == 0 and 2 * rows_a == LANES and groups * rows_a == args[0].shape[1]
    return (kernel_body if by_kernel else body)(*args)


def solution(mesh):
    placed = (
        P("dp", None),
        P("dp", None),
        P("dp", None),
        P("section", "dp", None),
        P(None, "dp", "section"),
        P("section", "dp", None),
        P("section", "dp", None),
        P("section", "dp", None),
        P(None, "dp", "section"),
        P(None, "dp", "section"),
        P("section", "dp", None),
        P("section", "dp", None),
    )
    return jax.shard_map(
        chosen_body,
        mesh=mesh,
        in_specs=placed,
        out_specs=(
            P(),
            P("section", "dp", None),
            P("section", "dp", None),
            P("section", "dp", None),
            P("section", "dp", None),
            P("section", "dp", None),
            P("section", "dp", None),
            P("section", "dp", None),
            P(None, "dp", "section"),
            P(None, "dp", "section"),
            P(None, "dp", "section"),
            P(None, "dp", "section"),
            P(None, "dp", "section"),
            P("section", "dp", None),
            P("section", "dp", None),
            P("section", "dp", None),
            P("section", "dp", None),
            P("section", "dp", None),
        ),
        check_vma=False,
    )
```

```python
import functools
import types

import jax
import jax.numpy as jnp
from jax import lax
from jax.experimental import pallas as pl
from jax.experimental.pallas import tpu as pltpu
from jax.sharding import PartitionSpec as P

HEADS = 8
STEP = 5


EPSILON = 1e-05
NEGATIVE = -1e30
CLIP_NORM = 1.0
BETA_ONE = 0.5
BETA_TWO = 0.5
ADAM_EPSILON = 1e-08
MATRIX_RATE = 0.05
NORM_RATE = 0.5
MATRIX_DECAY = 0.01


def norm_stats(value):
    centre = value - jnp.mean(value, -1, keepdims=True)
    inverse = lax.rsqrt(jnp.mean(centre * centre, -1, keepdims=True) + EPSILON)
    return (centre * inverse, inverse)


def norm_back(normal, inverse, upstream):
    return inverse * (
        upstream
        - jnp.mean(upstream, -1, keepdims=True)
        - normal * jnp.mean(upstream * normal, -1, keepdims=True)
    )


def adam_update(weight, moment_one, moment_two, gradient, step_rate, decay_rate):
    first_new = BETA_ONE * moment_one + (1.0 - BETA_ONE) * gradient
    second_new = BETA_TWO * moment_two + (1.0 - BETA_TWO) * gradient * gradient
    first_hat = first_new / (1.0 - BETA_ONE**STEP)
    second_hat = second_new / (1.0 - BETA_TWO**STEP)
    weight_new = weight - step_rate * (
        first_hat / (jnp.sqrt(second_hat) + ADAM_EPSILON) + decay_rate * weight
    )
    return (first_new, second_new, weight_new)


def segments_of(lengths_row, length):
    ends = jnp.cumsum(lengths_row, dtype=jnp.int32)
    places = jnp.arange(length, dtype=jnp.int32)
    segment = jnp.sum((ends[None, :] <= places[:, None]).astype(jnp.int32), axis=1, dtype=jnp.int32)
    live = (places < ends[-1]).astype(jnp.float32)
    return segment, live


def matmul(left, right, dims):
    return lax.dot_general(left, right, (dims, ((), ())), preferred_element_type=jnp.float32)


NN = ((1,), (0,))
NT = ((1,), (1,))
TN = ((0,), (0,))


def attention_forward(stream, weight, mask):
    length, width = stream.shape
    size = width // HEADS
    packed = matmul(stream, weight[:, : 3 * width], NN).astype(jnp.bfloat16)
    heads = packed.reshape(length, 3, HEADS, size)
    scores = jnp.einsum("qhd,khd->hqk", heads[:, 0], heads[:, 1], preferred_element_type=jnp.float32)
    scores = jnp.where(mask[None], scores * size**-0.5, NEGATIVE)
    weights = jnp.exp(scores - jnp.max(scores, -1, keepdims=True))
    probs = weights / jnp.sum(weights, -1, keepdims=True)
    mixed = jnp.einsum("hqk,khd->qhd", probs.astype(jnp.bfloat16), heads[:, 2], preferred_element_type=jnp.float32)
    mixed = mixed.reshape(length, width).astype(jnp.bfloat16)
    branch = matmul(mixed, weight[:, 3 * width :], NN)
    return branch, (heads, probs, mixed)


def attention_backward(stream, weight, kept, grad_low):
    heads, probs, mixed = kept
    length, width = stream.shape
    size = width // HEADS
    grad_out = matmul(mixed, grad_low, TN)
    grad_mixed = matmul(grad_low, weight[:, 3 * width :], NT).astype(jnp.bfloat16)
    grad_mixed = grad_mixed.reshape(length, HEADS, size)
    grad_probs = jnp.einsum("qhd,khd->hqk", grad_mixed, heads[:, 2], preferred_element_type=jnp.float32)
    centre = jnp.sum(probs * grad_probs, -1, keepdims=True)
    grad_scores = (probs * (grad_probs - centre)).astype(jnp.bfloat16)
    low = probs.astype(jnp.bfloat16)
    scale = size**-0.5
    grad_q = jnp.einsum("hqk,khd->qhd", grad_scores, heads[:, 1], preferred_element_type=jnp.float32) * scale
    grad_k = jnp.einsum("hqk,qhd->khd", grad_scores, heads[:, 0], preferred_element_type=jnp.float32) * scale
    grad_v = jnp.einsum("hqk,qhd->khd", low, grad_mixed, preferred_element_type=jnp.float32)
    packed = jnp.concatenate([grad_q, grad_k, grad_v], axis=1).reshape(length, 3 * width)
    packed = packed.astype(jnp.bfloat16)
    grad_in = matmul(stream, packed, TN)
    grad_inputs = matmul(packed, weight[:, : 3 * width], NT)
    return grad_inputs, jnp.concatenate([grad_in, grad_out], axis=1)


def feed_forward(stream, weight, down):
    pre = matmul(stream, weight, NN)
    active = jax.nn.gelu(pre, approximate=True).astype(jnp.bfloat16)
    return matmul(active, down, NN), (pre, active)


def feed_backward(stream, weight, down, kept, grad_low):
    pre, active = kept
    grad_down = matmul(active, grad_low, TN)
    grad_active = matmul(grad_low, down, NT)
    pull = jax.vjp(lambda value: jax.nn.gelu(value, approximate=True), pre)[1]
    grad_pre = pull(grad_active)[0].astype(jnp.bfloat16)
    grad_up = matmul(stream, grad_pre, TN)
    return matmul(grad_pre, weight, NT), grad_up, grad_down


def micro_step(rows, pull, segment, mats, downs, gains, biases):
    low = jnp.bfloat16
    mask = segment[:, None] == segment[None, :]
    stream, dual = rows, jnp.zeros_like(rows)
    saved = []
    for sub in range(4):
        if sub % 2 == 0:
            branch, kept = attention_forward(stream, mats[sub], mask)
        else:
            branch, kept = feed_forward(stream, mats[sub], downs[sub // 2])
        normal, inverse = norm_stats(stream.astype(jnp.float32) + branch)
        out = normal * gains[sub] + biases[sub]
        total = dual.astype(jnp.float32) + branch
        saved.append((stream, kept, normal, inverse))
        if sub < 3:
            stream, dual = out.astype(low), total.astype(low)
    dual_normal, dual_inverse = norm_stats(total)
    output = (out + dual_normal).astype(low)
    grad_out, grad_dual = pull, norm_back(dual_normal, dual_inverse, pull)
    grads_a, grads_b, grads_n = [None] * 4, [None] * 2, [None] * 4
    for sub in (3, 2, 1, 0):
        stream, kept, normal, inverse = saved[sub]
        grads_n[sub] = jnp.stack([jnp.sum(grad_out * normal, 0), jnp.sum(grad_out, 0)], axis=1)
        summed = norm_back(normal, inverse, grad_out * gains[sub])
        branch_low = (summed + grad_dual).astype(low)
        if sub % 2 == 0:
            inner, grads_a[sub] = attention_backward(stream, mats[sub], kept, branch_low)
        else:
            inner, grads_a[sub], grads_b[sub // 2] = feed_backward(
                stream, mats[sub], downs[sub // 2], kept, branch_low
            )
        grad_in = summed + inner
        if sub > 0:
            grad_out = grad_in.astype(low).astype(jnp.float32)
            grad_dual = grad_dual.astype(low).astype(jnp.float32)
    return output, grad_in, jnp.stack(grads_a), jnp.stack(grads_b), jnp.stack(grads_n)


def finish_step(grad_norm, output, input_grad, *groups):
    factor = CLIP_NORM / jnp.maximum(grad_norm, CLIP_NORM)
    results = [grad_norm, output[None], input_grad[None]]
    for weight, one, two, grad, rate, decay in groups:
        clip = grad * factor
        moment, square_new, master = adam_update(weight, one, two, clip, rate, decay)
        results += [clip, moment, square_new, master, master.astype(jnp.bfloat16)]
    return tuple(results)


def body(
    tokens, cotangent, lengths, mat_a, mat_b, norms, first_a, second_a, first_b, second_b, first_n, second_n
):
    low = jnp.bfloat16
    own = lax.axis_index("section")
    length = tokens.shape[0] // lengths.shape[0]
    rows = lax.dynamic_slice_in_dim(tokens, own * length, length, 0)
    segment, live = segments_of(lax.dynamic_index_in_dim(lengths, own, 0, keepdims=False), length)
    pull = lax.dynamic_slice_in_dim(cotangent, own * length, length, 0).astype(jnp.float32) * live[:, None]

    def gathered(value):
        return lax.all_gather(lax.all_gather(value, "dp", axis=1, tiled=True), "section", axis=0, tiled=True)

    mats = gathered(mat_a.astype(low))
    scales = gathered(norms.astype(low)).astype(jnp.float32)
    downs = lax.all_gather(mat_b.astype(low), "section", axis=2, tiled=True)
    downs = lax.all_gather(downs, "dp", axis=1, tiled=True)
    output, input_grad, part_a, part_b, part_n = micro_step(
        rows, pull, segment, mats, downs, scales[:, :, 0], scales[:, :, 1]
    )

    def scattered(value, section_dim):
        value = lax.psum_scatter(value, "section", scatter_dimension=section_dim, tiled=True)
        return lax.psum_scatter(value, "dp", scatter_dimension=1, tiled=True).astype(jnp.float32)

    grad_a = scattered(part_a.astype(low), 0)
    grad_b = scattered(part_b.astype(low), 2)
    grad_n = scattered(part_n, 0)
    square = jnp.sum(grad_a * grad_a) + jnp.sum(grad_b * grad_b) + jnp.sum(grad_n * grad_n)
    grad_norm = jnp.sqrt(lax.psum(square, ("section", "dp")))
    return finish_step(
        grad_norm, output, input_grad,
        (mat_a, first_a, second_a, grad_a, MATRIX_RATE, MATRIX_DECAY),
        (mat_b, first_b, second_b, grad_b, MATRIX_RATE, MATRIX_DECAY),
        (norms, first_n, second_n, grad_n, NORM_RATE, 0.0),
    )


LOW = jnp.bfloat16
WIDE = jnp.float32
MESH = pl.DeviceIdType.MESH
SECTIONS = 4
LANES = 128
BLOCK = 64
KERNEL_VMEM = 64 * 1024 * 1024 - 256 * 1024


def gradient_items(rows_a, rows_b, cols_b, width, hidden):
    part = rows_a // SECTIONS
    return (
        ("B1", 3, cols_b // 2, rows_b),
        ("F3", 3, part, hidden // 2),
        ("O2", 2, part, width // 2),
        ("K2", 2, part, 3 * width // 2),
        ("B0", 1, cols_b // 2, rows_b),
        ("F1", 1, part, hidden // 2),
        ("O0", 0, part, width // 2),
        ("K0", 0, part, 3 * width // 2),
    )


def item_scratch(name, chips, rows, columns):
    piece = (rows, columns)
    return (
        ("own" + name, (chips, SECTIONS, 2) + piece, LOW),
        ("farx" + name, (chips,) + piece, LOW),
        ("fary" + name, (chips,) + piece, LOW),
        ("nearx" + name, (2, chips) + piece, LOW),
        ("neary" + name, (2, chips) + piece, LOW),
        ("line" + name, (chips, 2) + piece, LOW),
        ("done" + name, (2,) + piece if name[0] == "B" else (SECTIONS, 2) + piece, WIDE if name[0] == "B" else LOW),
    )


def kernel_scratch(chips, rows_a, rows_b, cols_b, length, width, hidden):
    devices = 2 * chips
    items = gradient_items(rows_a, rows_b, cols_b, width, hidden)
    count = len(items)
    received = sum((item_scratch(name, chips, rows, columns) for name, _, rows, columns in items), ())
    return received + (
        ("fac_s", (32,), None),
        ("fac_r", (32,), None),
        ("px_s", (count, 3), None),
        ("px_r", (count, 3), None),
        ("py_s", (count, 3), None),
        ("py_r", (count, 3), None),
        ("line_s", (count, chips), None),
        ("line_r", (count, chips), None),
        ("done_s", (count,), None),
        ("done_r", (count, SECTIONS), None),
        ("wa", (4, width, hidden), LOW),
        ("wb", (2, hidden, width), LOW),
        ("tiles", (devices, SECTIONS, 8, LANES), WIDE),
        ("x", (4, length, width), LOW),
        ("xt", (4, chips, 2, rows_a, length), LOW),
        ("xtc", (4, chips, rows_a, 2 * length), LOW),
        ("y", (length, width), LOW),
        ("cot", (length, width), LOW),
        ("bias", (length, length), WIDE),
        ("live", (length, 1), WIDE),
        ("f", (length, width), WIDE),
        ("n", (4, length, width), WIDE),
        ("inv", (4, length, 1), WIDE),
        ("q", (2, length, width), LOW),
        ("k", (2, length, width), LOW),
        ("v", (2, length, width), LOW),
        ("kt", (2, width, length), LOW),
        ("vt", (2, width, length), LOW),
        ("ot", (2, chips, 2, rows_a, length), LOW),
        ("otc", (2, chips, rows_a, 2 * length), LOW),
        ("pt", (2, HEADS, length, length), LOW),
        ("g", (2, length, hidden), LOW),
        ("gc", (2, chips, 2 * length, rows_b), LOW),
        ("slope", (2, length, hidden), LOW),
        ("gx", (length, width), WIDE),
        ("gy", (length, width), WIDE),
        ("df", (2, 2 * length, width), LOW),
        ("dft", (2, width, 2 * length), LOW),
        ("dm", (length, width), LOW),
        ("dqt", (width, length), LOW),
        ("dh", (2, 2 * length, hidden), LOW),
        ("dp", (2, 2 * length, 3 * width), LOW),
        ("ng", (devices, 8, width), WIDE),
        ("ns", (SECTIONS, 8, width), WIDE),
        ("sq", (devices, 8, LANES), WIDE),
        ("sqs", (SECTIONS, 8, LANES), WIDE),
        ("sum", (8, LANES), WIDE),
        ("in_s", (2,), None),
        ("gz_s", (3, 2, chips, 2), None),
        ("gz_r", (3, chips, 2), None),
        ("gx_s", (3, chips, 2), None),
        ("gx_r", (3, chips, 2), None),
        ("gy_s", (3, chips, 2), None),
        ("gy_r", (3, chips, 2), None),
        ("gxr_s", (3, chips), None),
        ("gxr_r", (3, chips), None),
        ("gyr_s", (3, chips), None),
        ("gyr_r", (3, chips), None),
        ("gs_s", (6,), None),
        ("gs_r", (6,), None),
        ("small_s", (3, 2), None),
        ("small_r", (3, 2), None),
    )


INPUTS = ("tokens", "cotangent", "lengths", "mat_a", "mat_b", "norms")
OUTPUTS = ("grad_a", "grad_b", "grad_n", "square", "output", "input_grad")


def step_kernel(names, *refs):
    r = types.SimpleNamespace(**dict(zip(names, refs)))
    width, hidden = r.wa.shape[1:]
    length = r.x.shape[1]
    rows_a, (rows_b, cols_b) = r.mat_a.shape[1], r.mat_b.shape[1:]
    devices = r.tiles.shape[0]
    chips = devices // 2
    half_a, half_b = rows_a // 2, cols_b // 2
    grad_items = gradient_items(rows_a, rows_b, cols_b, width, hidden)
    head = width // HEADS
    scale = head**-0.5

    s, d = lax.axis_index("section"), lax.axis_index("dp")
    z, c = lax.div(d, 2), lax.rem(d, 2)
    sx = s + 1 - 2 * lax.rem(s, 2)
    sy = lax.rem(s + 2, SECTIONS)
    sd = SECTIONS - 1 - s
    to_sibling = {"dp": d + 1 - 2 * c}
    to_up, to_down = {"dp": d + 2}, {"dp": d - 2}
    to_x, to_y = {"section": sx}, {"section": sy}
    below, above = z > 0, z < chips - 1
    group = [{"dp": lax.rem(d + step, devices)} for step in range(1, devices)]
    plane = [{"section": lax.rem(s + step, SECTIONS)} for step in range(1, SECTIONS)]
    finish = []

    def when(condition, work):
        if condition is None:
            work()
        else:
            pl.when(condition)(work)

    def push(source, target, send_sem, recv_sem, device):
        pltpu.make_async_remote_copy(
            src_ref=source,
            dst_ref=target,
            send_sem=send_sem,
            recv_sem=recv_sem,
            device_id=device,
            device_id_type=MESH,
        ).start()

    def arrived(target, sem):
        pltpu.make_async_remote_copy(
            src_ref=target, dst_ref=target, send_sem=sem, recv_sem=sem, device_id=to_x, device_id_type=MESH
        ).wait_recv()

    def sent(source, sem):
        pltpu.make_async_remote_copy(
            src_ref=source, dst_ref=source, send_sem=sem, recv_sem=sem, device_id=to_x, device_id_type=MESH
        ).wait_send()

    def at_end(condition, source, sem):
        finish.append((condition, source, sem))

    def aligned(start, size):
        return pl.ds(pl.multiple_of(start, size), size)

    own_x = pltpu.make_async_copy(r.tokens.at[aligned(s * length, length)], r.x.at[0], r.in_s.at[0])
    own_cot = pltpu.make_async_copy(r.cotangent.at[aligned(s * length, length)], r.cot, r.in_s.at[1])
    own_x.start()
    own_cot.start()
    barrier = pltpu.get_barrier_semaphore()
    for peer in group + plane:
        pl.semaphore_signal(barrier, inc=1, device_id=peer, device_id_type=MESH)
    r.wa[s, aligned(d * rows_a, rows_a), :] = r.mat_a[0].astype(LOW)
    for layer in range(2):
        r.wb[layer, aligned(d * rows_b, rows_b), aligned(s * cols_b, cols_b)] = r.mat_b[layer].astype(LOW)
    norms = r.norms[0].astype(LOW).astype(WIDE)
    nothing = jnp.zeros((2, rows_a), WIDE)
    even = jnp.concatenate([norms, nothing], axis=1)
    odd = jnp.concatenate([nothing, norms], axis=1)
    r.tiles[d, s, 0:2, :] = jnp.where(c == 0, even, odd)
    r.tiles[d, s, 2:8, :] = jnp.zeros((6, LANES), WIDE)
    pl.semaphore_wait(barrier, len(group) + len(plane))

    def small_out(which, source):
        for peer in group:
            push(source, source, r.small_s.at[which, 0], r.small_r.at[which, 0], peer)

    def small_group(which, like):
        arrived(like, r.small_r.at[which, 0])
        sent(like, r.small_s.at[which, 0])

    def small_plane_out(which, source):
        for peer in plane:
            push(source, source, r.small_s.at[which, 1], r.small_r.at[which, 1], peer)

    def small_plane(which, like):
        arrived(like, r.small_r.at[which, 1])
        sent(like, r.small_s.at[which, 1])

    def block_a(section, chip, half):
        return r.wa.at[section, aligned((2 * chip + c) * rows_a + half * half_a, half_a), :]

    def block_b(layer):
        part = rows_b // 2

        def block(section, chip, half):
            return r.wb.at[
                layer,
                aligned((2 * chip + c) * rows_b + half * part, part),
                aligned(section * cols_b, cols_b),
            ]

        return block

    items = (block_a, block_b(0), block_b(1))

    def to_the_sibling(item, section, chip, half):
        block = items[item](section, chip, half)
        slot = section if item == 0 else 3 + item
        push(block, block, r.gs_s.at[slot], r.gs_r.at[slot], to_sibling)

    def spread_plane(item, chip):
        for half in range(2):
            block = items[item](s, chip, half)
            push(block, block, r.gx_s.at[item, chip, half], r.gx_r.at[item, chip, half], to_x)
            push(block, block, r.gy_s.at[item, chip, half], r.gy_r.at[item, chip, half], to_y)
            to_the_sibling(item, s, chip, half)

    def up(item, chip, half):
        block = items[item](s, chip, half)
        push(block, block, r.gz_s.at[item, 0, chip, half], r.gz_r.at[item, chip, half], to_up)

    def down(item, chip, half):
        block = items[item](s, chip, half)
        push(block, block, r.gz_s.at[item, 1, chip, half], r.gz_r.at[item, chip, half], to_down)

    def start_line(item):
        for half in range(2):
            when(above, lambda: up(item, z, half))
            when(below, lambda: down(item, z, half))

    def line_step(item, step):
        def from_below():
            for half in range(2):
                arrived(items[item](s, z - step, half), r.gz_r.at[item, z - step, half])
                when(above, lambda: up(item, z - step, half))
            spread_plane(item, z - step)

        def from_above():
            for half in range(2):
                arrived(items[item](s, z + step, half), r.gz_r.at[item, z + step, half])
                when(below, lambda: down(item, z + step, half))
            spread_plane(item, z + step)

        when(z >= step, from_below)
        when(z + step < chips, from_above)

    def plane_step(item):
        for chip in range(chips):
            for half in range(2):
                arrived(items[item](sx, chip, half), r.gx_r.at[item, chip, half])
                if half == 1:
                    block = items[item](sx, chip, half)
                    push(block, block, r.gyr_s.at[item, chip], r.gyr_r.at[item, chip], to_y)
                to_the_sibling(item, sx, chip, half)
                arrived(items[item](sy, chip, half), r.gy_r.at[item, chip, half])
                if half == 0:
                    block = items[item](sy, chip, half)
                    push(block, block, r.gxr_s.at[item, chip], r.gxr_r.at[item, chip], to_x)
                to_the_sibling(item, sy, chip, half)

    def relay_step(item):
        for chip in range(chips):
            arrived(items[item](sd, chip, 0), r.gxr_r.at[item, chip])
            to_the_sibling(item, sd, chip, 0)
            arrived(items[item](sd, chip, 1), r.gyr_r.at[item, chip])
            to_the_sibling(item, sd, chip, 1)

    whole_a = r.wa.at[0, pl.ds(0, chips * rows_a)]
    whole_b = r.wb.at[0, pl.ds(0, chips * rows_b)]
    def gather_sends(item):
        for chip in range(chips):
            for half in range(2):
                block = items[item](0, chip, half)
                at_end(None, block, r.gx_s.at[item, chip, half])
                at_end(None, block, r.gy_s.at[item, chip, half])
                at_end(above & (z >= chip), block, r.gz_s.at[item, 0, chip, half])
                at_end(below & (z <= chip), block, r.gz_s.at[item, 1, chip, half])
            block = items[item](0, chip, 0)
            at_end(None, block, r.gxr_s.at[item, chip])
            at_end(None, block, r.gyr_s.at[item, chip])

    def row_block(chip, half):
        part = rows_b // 2
        return r.wb.at[0, aligned((2 * chip + c) * rows_b + half * part, part), :]

    def rows_to_sibling(chip, half):
        push(row_block(chip, half), row_block(chip, half), r.gs_s.at[4], r.gs_r.at[4], to_sibling)

    def rows_up(chip, half):
        rows = row_block(chip, half)
        push(rows, rows, r.gz_s.at[1, 0, chip, half], r.gz_r.at[1, chip, half], to_up)

    def rows_down(chip, half):
        rows = row_block(chip, half)
        push(rows, rows, r.gz_s.at[1, 1, chip, half], r.gz_r.at[1, chip, half], to_down)

    def rows_plane():
        for half in range(2):
            block = items[1](s, z, half)
            push(block, block, r.gx_s.at[1, 0, half], r.gx_r.at[1, 0, half], to_x)
            push(block, block, r.gy_s.at[1, 0, half], r.gy_r.at[1, 0, half], to_y)
            at_end(None, block, r.gx_s.at[1, 0, half])
            at_end(None, block, r.gy_s.at[1, 0, half])

    def rows_relay():
        for half in range(2):
            arrived(items[1](sx, z, half), r.gx_r.at[1, 0, half])
            arrived(items[1](sy, z, half), r.gy_r.at[1, 0, half])
        block = items[1](sx, z, 1)
        push(block, block, r.gyr_s.at[1, 0], r.gyr_r.at[1, 0], to_y)
        block = items[1](sy, z, 0)
        push(block, block, r.gxr_s.at[1, 0], r.gxr_r.at[1, 0], to_x)
        at_end(None, block, r.gyr_s.at[1, 0])
        at_end(None, block, r.gxr_s.at[1, 0])

    def rows_line():
        for half, sem in ((0, r.gxr_r), (1, r.gyr_r)):
            arrived(items[1](sd, z, half), sem.at[1, 0])
            when(above, lambda: rows_up(z, half))
            when(below, lambda: rows_down(z, half))
            rows_to_sibling(z, half)
        for chip in range(chips):
            for half in range(2):
                at_end(above & (z >= chip), row_block(chip, half), r.gz_s.at[1, 0, chip, half])
                at_end(below & (z <= chip), row_block(chip, half), r.gz_s.at[1, 1, chip, half])

    def rows_step(step):
        def from_below():
            for half in range(2):
                arrived(row_block(z - step, half), r.gz_r.at[1, z - step, half])
                when(above, lambda: rows_up(z - step, half))
                rows_to_sibling(z - step, half)

        def from_above():
            for half in range(2):
                arrived(row_block(z + step, half), r.gz_r.at[1, z + step, half])
                when(below, lambda: rows_down(z + step, half))
                rows_to_sibling(z + step, half)

        when(z >= step, from_below)
        when(z + step < chips, from_above)

    mine, other = pl.ds(0, length), pl.ds(length, length)

    def give(slot, source, target):
        push(source, target, r.fac_s.at[slot], r.fac_r.at[slot], to_sibling)
        at_end(None, target, r.fac_s.at[slot])

    def taken(slot, target):
        arrived(target, r.fac_r.at[slot])

    def give_rows(layer):
        r.xt[layer] = r.x[layer].T.reshape(chips, 2, rows_a, length)
        r.xtc[layer, :, :, 0:length] = r.xt[layer, :, c]
        give(layer, r.xt.at[layer, :, 1 - c], r.xtc.at[layer, :, :, other])

    def product(left, right, dims):
        return lax.dot_general(left, right, (dims, ((), ())), preferred_element_type=WIDE)

    def loop(count, work):
        def one(index, carry):
            work(index)
            return carry

        lax.fori_loop(0, count, one, 0)

    def gain_row(layer, kind):
        parts = [
            r.tiles[2 * chip, layer, kind : kind + 1, :] + r.tiles[2 * chip + 1, layer, kind : kind + 1, :]
            for chip in range(chips)
        ]
        return jnp.concatenate(parts, axis=1)

    def stats(value):
        centre = value - jnp.mean(value, -1, keepdims=True)
        inverse = lax.rsqrt(jnp.mean(centre * centre, -1, keepdims=True) + EPSILON)
        return centre * inverse, inverse

    lane = lax.broadcasted_iota(jnp.int32, (1, 2 * head), 1)
    first_half = (lane < head).astype(WIDE)
    half_masks = (first_half.astype(LOW), (1.0 - first_half).astype(LOW))

    def prepare_masks():
        ends, total = [], jnp.int32(0)
        for slot in range(r.lengths.shape[1]):
            total = total + r.lengths[s, slot]
            ends.append(total)
        down_places = lax.broadcasted_iota(jnp.int32, (length, 1), 0)
        across_places = lax.broadcasted_iota(jnp.int32, (1, length), 1)
        down_segment = jnp.zeros((length, 1), jnp.int32)
        across_segment = jnp.zeros((1, length), jnp.int32)
        for end in ends:
            down_segment = down_segment + (end <= down_places).astype(jnp.int32)
            across_segment = across_segment + (end <= across_places).astype(jnp.int32)
        r.bias[...] = jnp.where(down_segment == across_segment, 0.0, NEGATIVE)
        r.live[...] = (down_places < total).astype(WIDE)

    def attention(layer):
        at = layer // 2
        rows = r.x[layer]
        r.q[at] = product(rows, r.wa[layer, :, 0:width], NN).astype(LOW) * jnp.asarray(scale, LOW)
        keys = product(rows, r.wa[layer, :, width : 2 * width], NN).astype(LOW)
        r.k[at] = keys
        values = product(rows, r.wa[layer, :, 2 * width : 3 * width], NN).astype(LOW)
        r.v[at] = values
        r.vt[at] = values.T

        def pair(index):
            lanes = aligned(index * 2 * head, 2 * head)
            for which in range(2):
                scores = product(r.k[at, :, lanes], r.q[at, :, lanes] * half_masks[which], NT) + r.bias[...]
                weights = jnp.exp(scores - jnp.max(scores, 0, keepdims=True))
                probs = (weights * (1.0 / jnp.sum(weights, 0, keepdims=True))).astype(LOW)
                r.pt[at, 2 * index + which] = probs
                place = aligned((2 * index + which) * head, head)
                r.ot[at, index, which] = product(r.vt[at, place, :], probs, NN).astype(LOW)

        def pairs(step):
            pair(2 * step)
            pair(2 * step + 1)

        loop(HEADS // 4, pairs)
        r.otc[at, :, :, 0:length] = r.ot[at, :, c]
        give(4 + at, r.ot.at[at, :, 1 - c], r.otc.at[at, :, :, other])
        r.f[...] = product(r.ot[at].reshape(width, length).T, r.wa[layer, :, 3 * width :], NN)

    def expand(layer):
        at = layer // 2
        def columns(index):
            place = pl.ds(index * width, width)
            pre = product(r.x[layer], r.wa[layer, :, place], NN)
            squared = pre * pre
            slope = 0.7978845608 * (1.0 + 3 * 0.044715 * squared)
            bent = jnp.tanh(0.7978845608 * pre * (1.0 + 0.044715 * squared))
            r.g[at, :, place] = (0.5 * pre * (1.0 + bent)).astype(LOW)
            r.slope[at, :, place] = (0.5 * (1.0 + bent) + 0.5 * pre * (1.0 - bent * bent) * slope).astype(LOW)
            block = aligned((2 * index + c) * rows_b, rows_b)
            r.gc[at, index, 0:length, :] = r.g[at, :, block]
            block = aligned((2 * index + 1 - c) * rows_b, rows_b)
            give(6 + chips * at + index, r.g.at[at, :, block], r.gc.at[at, index, other, :])

        for index in range(hidden // width):
            columns(index)

    def contract(layer):
        r.f[...] = product(r.g[layer // 2], r.wb[layer // 2], NN)

    def by_rows(work):
        for index in range(length // BLOCK):
            work(pl.ds(index * BLOCK, BLOCK))

    def normalize(layer):
        gain, offset = gain_row(layer, 0), gain_row(layer, 1)

        def some(rows):
            branch = r.f[rows, :]
            normal, inverse = stats(r.x[layer, rows, :].astype(WIDE) + branch)
            r.n[layer, rows, :] = normal
            r.inv[layer, rows, :] = inverse
            out = normal * gain + offset
            dual = branch if layer == 0 else r.y[rows, :].astype(WIDE) + branch
            if layer < 3:
                r.x[layer + 1, rows, :] = out.astype(LOW)
                r.y[rows, :] = dual.astype(LOW)
            else:
                dual_normal, dual_inverse = stats(dual)
                r.output[rows, :] = (out + dual_normal).astype(LOW)
                pull = r.cot[rows, :].astype(WIDE) * r.live[rows, :]
                r.gx[rows, :] = pull
                r.gy[rows, :] = norm_back(dual_normal, dual_inverse, pull)

        by_rows(some)

    def back_normalize(layer):
        gain = gain_row(layer, 0)

        def some(index, sums):
            rows = pl.ds(index * BLOCK, BLOCK)
            upstream = r.gx[rows, :]
            normal = r.n[layer, rows, :]
            summed = norm_back(normal, r.inv[layer, rows, :], upstream * gain)
            dual = r.gy[rows, :]
            r.gx[rows, :] = summed
            r.df[layer // 2, rows, :] = (summed + dual).astype(LOW)
            if layer == 3:
                r.gy[rows, :] = dual.astype(LOW).astype(WIDE)
            return (
                sums[0] + jnp.sum(upstream * normal, 0, keepdims=True),
                sums[1] + jnp.sum(upstream, 0, keepdims=True),
            )

        zero = jnp.zeros((1, width), WIDE)
        gains, offsets = zero, zero
        for index in range(length // BLOCK):
            gains, offsets = some(index, (gains, offsets))
        r.ng[d, 2 * layer : 2 * layer + 1, :] = gains
        r.ng[d, 2 * layer + 1 : 2 * layer + 2, :] = offsets

    def pass_down(layer, inner):
        total = r.gx[...] + inner
        if layer > 0:
            r.gx[...] = total.astype(LOW).astype(WIDE)
        else:
            r.input_grad[...] = total

    base = 6 + 2 * chips

    def back_hidden(layer):
        at = layer // 2
        r.dft[at, :, 0:length] = r.df[at, 0:length, :].T
        give(base + at, r.dft.at[at, :, mine], r.dft.at[at, :, other])
        for index in range(hidden // width):
            place = pl.ds(index * width, width)
            pulled = product(r.df[at, 0:length, :], r.wb[at, pl.ds(index * width, width), :], NT)
            r.dh[at, 0:length, place] = (pulled * r.slope[at, :, place].astype(WIDE)).astype(LOW)
            give(base + 2 + chips * at + index, r.dh.at[at, mine, place], r.dh.at[at, other, place])

    def back_expand_end(layer):
        pass_down(layer, product(r.dh[layer // 2, 0:length, :], r.wa[layer], NT))

    def back_output(layer):
        at = layer // 2
        give(base + 2 + 2 * chips + at, r.df.at[at, mine], r.df.at[at, other])
        r.dm[...] = product(r.df[at, 0:length, :], r.wa[layer, :, 3 * width :], NT).astype(LOW)
        r.kt[at] = (r.k[at] * jnp.asarray(scale, LOW)).T

    def back_heads(layer, begin, count):
        at = layer // 2

        def pair(index):
            lanes = aligned(index * 2 * head, 2 * head)
            pulled = r.dm[:, lanes]
            keys, values = [], []
            for which in range(2):
                probs = r.pt[at, 2 * index + which]
                grad = product(r.v[at, :, lanes], pulled * half_masks[which], NT)
                full = probs.astype(WIDE)
                centre = jnp.sum(full * grad, 0, keepdims=True)
                scores = (full * (grad - centre)).astype(LOW)
                keys.append(product(scores, r.q[at, :, lanes], NN))
                values.append(product(probs, pulled, NN))
                place = aligned((2 * index + which) * head, head)
                r.dqt[place, :] = product(r.kt[at, place, :], scores, NN).astype(LOW)
            r.dp[at, 0:length, aligned(width + index * 2 * head, 2 * head)] = jnp.where(
                lane < head, keys[0], keys[1]
            ).astype(LOW)
            r.dp[at, 0:length, aligned(2 * width + index * 2 * head, 2 * head)] = jnp.where(
                lane < head, values[0], values[1]
            ).astype(LOW)

        def pairs(step):
            pair(begin + 2 * step)
            pair(begin + 2 * step + 1)

        loop(count // 2, pairs)

    def back_packed(layer):
        at = layer // 2
        slot = base + 4 + 2 * chips + 2 * at
        place = pl.ds(width, 2 * width)
        give(slot, r.dp.at[at, mine, place], r.dp.at[at, other, place])
        r.dp[at, 0:length, 0:width] = r.dqt[...].T
        place = pl.ds(0, width)
        give(slot + 1, r.dp.at[at, mine, place], r.dp.at[at, other, place])

    def back_packed_end(layer):
        pass_down(layer, product(r.dp[layer // 2, 0:length, :], r.wa[layer, :, 0 : 3 * width], NT))

    def keep(name, half, place, value):
        own = getattr(r, "own" + name)
        own[:, :, half, :, place] = value.astype(LOW).reshape(chips, SECTIONS, rows_a // SECTIONS, value.shape[1])

    def chip_rows(value):
        return value.reshape(chips * rows_a, 2 * length)

    def grad_down(at):
        own = getattr(r, "ownB%d" % at)
        taken(base + at, r.dft.at[at, :, other])
        for chip in range(chips):
            taken(6 + chips * at + chip, r.gc.at[at, chip, other, :])
            value = product(r.dft[at], r.gc[at, chip], NN)
            own[chip] = value.astype(LOW).reshape(SECTIONS, 2, half_b, rows_b)

    def grad_up(layer):
        at = layer // 2
        taken(layer, r.xtc.at[layer, :, :, other])
        for index in range(hidden // width):
            place = pl.ds(index * width, width)
            taken(base + 2 + chips * at + index, r.dh.at[at, other, place])
            value = product(chip_rows(r.xtc[layer]), r.dh[at, :, place], NN)
            keep("F%d" % layer, index // 2, pl.ds(index % 2 * width, width), value)

    def grad_output(layer):
        at = layer // 2
        taken(4 + at, r.otc.at[at, :, :, other])
        taken(base + 2 + 2 * chips + at, r.df.at[at, other])
        for half in range(2):
            place = pl.ds(half * width // 2, width // 2)
            value = product(chip_rows(r.otc[at]), r.df[at, :, place], NN)
            keep("O%d" % layer, half, pl.ds(0, width // 2), value)

    def grad_packed(layer):
        at = layer // 2
        slot = base + 4 + 2 * chips + 2 * at
        taken(layer, r.xtc.at[layer, :, :, other])
        taken(slot, r.dp.at[at, other, pl.ds(width, 2 * width)])
        taken(slot + 1, r.dp.at[at, other, pl.ds(0, width)])
        part = 3 * width // 2
        for half in range(2):
            value = product(chip_rows(r.xtc[layer]), r.dp[at, :, half * part : (half + 1) * part], NN)
            keep("K%d" % layer, half, pl.ds(0, part), value)

    def joined(target, others):
        return functools.reduce(
            lambda left, right: left + right, [ref[...].astype(WIDE) for ref in (target, *others)]
        )

    def add_into(target, others):
        if len(others) == 1:
            target[...] = target[...] + others[0][...]
        else:
            target[...] = joined(target, others).astype(LOW)

    places = {name: place for place, (name, _, _, _) in enumerate(grad_items)}

    def buffers(name):
        parts = ("own", "farx", "fary", "nearx", "neary", "line", "done")
        return types.SimpleNamespace(**{part: getattr(r, part + name) for part in parts})

    def to_plane(name):
        item, place = buffers(name), places[name]

        def over_x(section, half, target, slot):
            push(item.own.at[:, section, half], target, r.px_s.at[place, slot], r.px_r.at[place, slot], to_x)
            at_end(None, item.farx, r.px_s.at[place, slot])

        def over_y(section, half, target, slot):
            push(item.own.at[:, section, half], target, r.py_s.at[place, slot], r.py_r.at[place, slot], to_y)
            at_end(None, item.farx, r.py_s.at[place, slot])

        over_x(sd, 0, item.farx, 2)
        over_y(sd, 1, item.fary, 2)
        over_x(sx, 0, item.nearx.at[0], 0)
        over_y(sy, 1, item.neary.at[1], 1)

    def through_plane(name):
        item, place = buffers(name), places[name]
        own = item.own
        arrived(item.fary, r.py_r.at[place, 2])
        add_into(own.at[:, sx, 1], [item.fary])
        push(own.at[:, sx, 1], item.nearx.at[1], r.px_s.at[place, 1], r.px_r.at[place, 1], to_x)
        at_end(None, item.farx, r.px_s.at[place, 1])
        arrived(item.farx, r.px_r.at[place, 2])
        add_into(own.at[:, sy, 0], [item.farx])
        push(own.at[:, sy, 0], item.neary.at[0], r.py_s.at[place, 0], r.py_r.at[place, 0], to_y)
        at_end(None, item.farx, r.py_s.at[place, 0])

    def to_line(name):
        item, place = buffers(name), places[name]
        own = item.own.at[:, s]
        for half in range(2):
            arrived(item.nearx.at[half], r.px_r.at[place, half])
            arrived(item.neary.at[half], r.py_r.at[place, half])
            add_into(own.at[:, half], [item.nearx.at[half], item.neary.at[half]])
        for step in range(1, chips):
            chip = lax.rem(z + step, chips)
            push(
                own.at[chip],
                item.line.at[z],
                r.line_s.at[place, step],
                r.line_r.at[place, z],
                {"dp": 2 * chip + c},
            )
            at_end(None, item.line.at[0], r.line_s.at[place, step])

    def to_owner(name):
        item, place = buffers(name), places[name]
        others = [lax.rem(z + step, chips) for step in range(1, chips)]
        for chip in others:
            arrived(item.line.at[chip], r.line_r.at[place, chip])
        total = joined(item.own.at[z, s], [item.line.at[chip] for chip in others])
        square = total * total
        while square.ndim > 2:
            square = jnp.sum(square, 0)
        square = jnp.sum(jnp.sum(square, 0, keepdims=True), 1, keepdims=True)
        r.sum[...] = r.sum[...] + jnp.broadcast_to(square, (8, LANES))
        if name[0] == "B":
            item.done[...] = total
            return
        item.done[s] = total.astype(LOW)
        layer = grad_items[place][1]
        mine = item.done.at[s]
        away = s != layer
        when(
            away,
            lambda: push(mine, mine, r.done_s.at[place], r.done_r.at[place, s], {"section": jnp.int32(layer)}),
        )
        at_end(away, mine, r.done_s.at[place])

    def collect(name):
        item, place = buffers(name), places[name]
        layer = grad_items[place][1]

        def work():
            for section in range(SECTIONS):
                if section != layer:
                    arrived(item.done.at[section], r.done_r.at[place, section])
            columns = item.done.shape[-1]
            start = 3 * width if name[0] == "O" else 0
            for section in range(SECTIONS):
                for half in range(2):
                    rows = pl.ds(section * (rows_a // SECTIONS), rows_a // SECTIONS)
                    place_to = pl.ds(start + half * columns, columns)
                    r.grad_a[rows, place_to] = item.done[section, half].astype(WIDE)

        when(s == layer, work)

    def all_sent():
        for condition, source, sem in finish:
            when(condition, functools.partial(sent, source, sem))
        finish.clear()

    small_out(0, r.tiles.at[d, s])
    start_line(0)
    spread_plane(0, z)
    rows_plane()
    line_step(0, 1)
    rows_relay()
    line_step(0, 2)
    rows_line()
    start_line(2)
    for step in range(3, chips):
        line_step(0, step)
    small_group(0, r.tiles.at[pl.ds(0, devices - 1), 0])
    for peer in plane:
        push(r.tiles.at[:, s], r.tiles.at[:, s], r.small_s.at[0, 1], r.small_r.at[0, 1], peer)
    prepare_masks()
    rows_step(1)
    plane_step(0)
    for step in range(2, chips):
        rows_step(step)
    spread_plane(2, z)
    for step in range(1, chips):
        line_step(2, step)
    own_x.wait()
    own_cot.wait()
    relay_step(0)
    small_plane(0, r.tiles.at[:, pl.ds(0, SECTIONS - 1)])
    for slot in range(4):
        arrived(whole_a, r.gs_r.at[slot])
    attention(0)
    normalize(0)
    expand(1)
    arrived(whole_b, r.gs_r.at[4])
    contract(1)
    normalize(1)
    plane_step(2)
    attention(2)
    normalize(2)
    expand(3)
    gather_sends(0)
    for slot in range(5):
        at_end(None, whole_a if slot < 4 else whole_b, r.gs_s.at[slot])
    all_sent()
    relay_step(2)
    arrived(whole_b, r.gs_r.at[5])
    contract(3)
    normalize(3)

    r.sum[...] = jnp.zeros((8, LANES), WIDE)
    back_normalize(3)
    back_hidden(3)
    back_expand_end(3)
    give_rows(3)
    grad_down(1)
    to_plane("B1")
    back_normalize(2)
    grad_up(3)
    to_plane("F3")
    back_output(2)
    back_heads(2, 0, 2)
    through_plane("B1")
    grad_output(2)
    to_plane("O2")
    back_heads(2, 2, 2)
    back_packed(2)
    give_rows(2)
    through_plane("F3")
    back_packed_end(2)
    to_line("B1")
    through_plane("O2")
    back_normalize(1)
    grad_packed(2)
    to_plane("K2")
    back_hidden(1)
    give_rows(1)
    to_line("F3")
    to_line("O2")
    back_expand_end(1)
    grad_down(0)
    to_plane("B0")
    through_plane("K2")
    to_owner("B1")
    back_normalize(0)
    small_out(1, r.ng.at[d])
    grad_up(1)
    to_plane("F1")
    back_output(0)
    give_rows(0)
    to_owner("F3")
    to_owner("O2")
    back_heads(0, 0, 2)
    through_plane("B0")
    to_line("K2")
    grad_output(0)
    to_plane("O0")
    back_heads(0, 2, 2)
    back_packed(0)
    through_plane("F1")
    to_owner("K2")
    grad_packed(0)
    to_plane("K0")
    through_plane("O0")
    to_line("B0")
    back_packed_end(0)
    to_line("F1")
    to_line("O0")
    gather_sends(2)
    at_end(None, whole_b, r.gs_s.at[5])
    all_sent()
    through_plane("K0")
    to_owner("B0")
    to_owner("F1")
    to_owner("O0")
    small_group(1, r.ng.at[pl.ds(0, devices - 1)])
    r.ns[s] = functools.reduce(lambda left, right: left + right, [r.ng[index] for index in range(devices)])
    small_plane_out(1, r.ns.at[s])
    for name in ("F3", "O2", "K2", "F1"):
        collect(name)
    to_line("K0")
    collect("O0")
    for layer in range(2):
        done = buffers("B%d" % layer).done
        r.grad_b[layer] = done[...].reshape(cols_b, rows_b).T
    small_plane(1, r.ns.at[pl.ds(0, SECTIONS - 1)])
    grads = functools.reduce(lambda left, right: left + right, [r.ns[index] for index in range(SECTIONS)])
    norm_square = jnp.sum(jnp.sum(grads * grads, 0, keepdims=True), 1, keepdims=True)
    chosen = jnp.zeros((2, width), WIDE)
    for layer in range(4):
        chosen = jnp.where(s == layer, grads[2 * layer : 2 * layer + 2, :], chosen)
    for chip in range(chips):
        pair_of = chosen[:, chip * LANES : (chip + 1) * LANES]
        r.grad_n[...] = jnp.where(
            z == chip, jnp.where(c == 0, pair_of[:, :rows_a], pair_of[:, rows_a:]), r.grad_n[...]
        )
    to_owner("K0")

    r.sq[d] = r.sum[...]
    small_out(2, r.sq.at[d])
    collect("K0")
    small_group(2, r.sq.at[pl.ds(0, devices - 1)])
    r.sqs[s] = functools.reduce(lambda left, right: left + right, [r.sq[index] for index in range(devices)])
    small_plane_out(2, r.sqs.at[s])
    all_sent()
    small_plane(2, r.sqs.at[pl.ds(0, SECTIONS - 1)])
    squares = functools.reduce(lambda left, right: left + right, [r.sqs[index] for index in range(SECTIONS)])
    r.square[...] = squares + norm_square


def step_call(tokens, cotangent, lengths, mat_a, mat_b, norms):
    rows_a, hidden = mat_a.shape[1:]
    rows_b, cols_b = mat_b.shape[1:]
    width = tokens.shape[1]
    length = tokens.shape[0] // lengths.shape[0]
    chips = width // rows_a // 2
    scratch = kernel_scratch(chips, rows_a, rows_b, cols_b, length, width, hidden)
    shapes = []
    for _, shape, kind in scratch:
        shapes.append(pltpu.SemaphoreType.DMA(shape) if kind is None else pltpu.VMEM(shape, kind))
    anywhere, vmem = pl.BlockSpec(memory_space=pl.ANY), pl.BlockSpec(memory_space=pltpu.VMEM)
    return pl.pallas_call(
        functools.partial(step_kernel, INPUTS + OUTPUTS + tuple(name for name, _, _ in scratch)),
        out_shape=(
            jax.ShapeDtypeStruct((rows_a, hidden), WIDE),
            jax.ShapeDtypeStruct(mat_b.shape, WIDE),
            jax.ShapeDtypeStruct((2, rows_a), WIDE),
            jax.ShapeDtypeStruct((8, LANES), WIDE),
            jax.ShapeDtypeStruct((length, width), LOW),
            jax.ShapeDtypeStruct((length, width), WIDE),
        ),
        in_specs=[anywhere, anywhere, pl.BlockSpec(memory_space=pltpu.SMEM), vmem, vmem, vmem],
        out_specs=[vmem] * len(OUTPUTS),
        scratch_shapes=shapes,
        compiler_params=pltpu.CompilerParams(
            collective_id=0, has_side_effects=True, vmem_limit_bytes=KERNEL_VMEM
        ),
    )(tokens, cotangent, lengths, mat_a, mat_b, norms)


def update_kernel(*refs):
    square, output, input_grad = (ref[...] for ref in refs[:3])
    grad_norm = jnp.sqrt(square[0:1, 0:1])
    factor = CLIP_NORM / jnp.maximum(grad_norm, CLIP_NORM)
    inputs, outputs = refs[3:15], refs[15:]
    outputs[0][...] = grad_norm
    outputs[1][0] = output
    outputs[2][0] = input_grad
    for group, (rate, decay) in enumerate(
        ((MATRIX_RATE, MATRIX_DECAY), (MATRIX_RATE, MATRIX_DECAY), (NORM_RATE, 0.0))
    ):
        grad, weight, one, two = inputs[4 * group : 4 * group + 4]
        clip = grad[...].reshape(weight.shape) * factor
        moment, square_new, master = adam_update(weight[...], one[...], two[...], clip, rate, decay)
        for ref, value in zip(
            outputs[3 + 5 * group : 8 + 5 * group], (clip, moment, square_new, master, master.astype(LOW))
        ):
            ref[...] = value


def kernel_body(
    tokens, cotangent, lengths, mat_a, mat_b, norms, first_a, second_a, first_b, second_b, first_n, second_n
):
    norms, first_n, second_n = (jnp.swapaxes(value, 1, 2) for value in (norms, first_n, second_n))
    grad_a, grad_b, grad_n, square, output, input_grad = step_call(
        tokens, cotangent, lengths, mat_a, mat_b, norms
    )
    steps = 4

    def cut(value, dim):
        shape = tuple(size // steps if at == dim else size for at, size in enumerate(value.shape))
        return pl.BlockSpec(shape, lambda step: tuple(step if at == dim else 0 for at in range(len(shape))))

    def whole(value):
        return pl.BlockSpec(value.shape, lambda step: (0,) * len(value.shape))

    def like(value, kind=WIDE):
        return jax.ShapeDtypeStruct(value.shape, kind)

    args = (square, output, input_grad, grad_a, mat_a, first_a, second_a, grad_b, mat_b, first_b, second_b)
    specs = [whole(square), cut(output, 0), cut(input_grad, 0)]
    specs += [cut(grad_a, 0)] + [cut(mat_a, 1)] * 3 + [cut(grad_b, 1)] * 4
    args += (grad_n, norms, first_n, second_n)
    specs += [whole(grad_n)] + [whole(norms)] * 3
    shapes = [jax.ShapeDtypeStruct((1, 1), WIDE), like(output[None], LOW), like(input_grad[None])]
    out_specs = [whole(shapes[0]), cut(shapes[1], 1), cut(shapes[2], 1)]
    for value, spec in ((mat_a, cut(mat_a, 1)), (mat_b, cut(mat_b, 1)), (norms, whole(norms))):
        shapes += [like(value)] * 4 + [like(value, LOW)]
        out_specs += [spec] * 5
    results = pl.pallas_call(
        update_kernel,
        grid=(steps,),
        out_shape=shapes,
        in_specs=specs,
        out_specs=out_specs,
        compiler_params=pltpu.CompilerParams(vmem_limit_bytes=KERNEL_VMEM),
    )(*args)
    results = [results[0][0, 0], *results[1:]]
    results[-5:] = [jnp.swapaxes(value, 1, 2) for value in results[-5:]]
    return tuple(results)


def chosen_body(*args):
    rows_a = args[3].shape[1]
    groups = lax.axis_size("dp")
    by_kernel = rows_a % 32 == 0 and 2 * rows_a == LANES and groups * rows_a == args[0].shape[1]
    return (kernel_body if by_kernel else body)(*args)


def solution(mesh):
    placed = (
        P("dp", None),
        P("dp", None),
        P("dp", None),
        P("section", "dp", None),
        P(None, "dp", "section"),
        P("section", "dp", None),
        P("section", "dp", None),
        P("section", "dp", None),
        P(None, "dp", "section"),
        P(None, "dp", "section"),
        P("section", "dp", None),
        P("section", "dp", None),
    )
    return jax.shard_map(
        chosen_body,
        mesh=mesh,
        in_specs=placed,
        out_specs=(
            P(),
            P("section", "dp", None),
            P("section", "dp", None),
            P("section", "dp", None),
            P("section", "dp", None),
            P("section", "dp", None),
            P("section", "dp", None),
            P("section", "dp", None),
            P(None, "dp", "section"),
            P(None, "dp", "section"),
            P(None, "dp", "section"),
            P(None, "dp", "section"),
            P(None, "dp", "section"),
            P("section", "dp", None),
            P("section", "dp", None),
            P("section", "dp", None),
            P("section", "dp", None),
            P("section", "dp", None),
        ),
        check_vma=False,
    )
```

```python
import functools
import types

import jax
import jax.numpy as jnp
from jax import lax
from jax.experimental import pallas as pl
from jax.experimental.pallas import tpu as pltpu
from jax.sharding import PartitionSpec as P

HEADS = 8
STEP = 5


EPSILON = 1e-05
NEGATIVE = -1e30
CLIP_NORM = 1.0
BETA_ONE = 0.5
BETA_TWO = 0.5
ADAM_EPSILON = 1e-08
MATRIX_RATE = 0.05
NORM_RATE = 0.5
MATRIX_DECAY = 0.01


def norm_stats(value):
    centre = value - jnp.mean(value, -1, keepdims=True)
    inverse = lax.rsqrt(jnp.mean(centre * centre, -1, keepdims=True) + EPSILON)
    return (centre * inverse, inverse)


def norm_back(normal, inverse, upstream):
    return inverse * (
        upstream
        - jnp.mean(upstream, -1, keepdims=True)
        - normal * jnp.mean(upstream * normal, -1, keepdims=True)
    )


def adam_update(weight, moment_one, moment_two, gradient, step_rate, decay_rate):
    first_new = BETA_ONE * moment_one + (1.0 - BETA_ONE) * gradient
    second_new = BETA_TWO * moment_two + (1.0 - BETA_TWO) * gradient * gradient
    first_hat = first_new / (1.0 - BETA_ONE**STEP)
    second_hat = second_new / (1.0 - BETA_TWO**STEP)
    weight_new = weight - step_rate * (
        first_hat / (jnp.sqrt(second_hat) + ADAM_EPSILON) + decay_rate * weight
    )
    return (first_new, second_new, weight_new)


def segments_of(lengths_row, length):
    ends = jnp.cumsum(lengths_row, dtype=jnp.int32)
    places = jnp.arange(length, dtype=jnp.int32)
    segment = jnp.sum((ends[None, :] <= places[:, None]).astype(jnp.int32), axis=1, dtype=jnp.int32)
    live = (places < ends[-1]).astype(jnp.float32)
    return segment, live


def matmul(left, right, dims):
    return lax.dot_general(left, right, (dims, ((), ())), preferred_element_type=jnp.float32)


NN = ((1,), (0,))
NT = ((1,), (1,))
TN = ((0,), (0,))


def attention_forward(stream, weight, mask):
    length, width = stream.shape
    size = width // HEADS
    packed = matmul(stream, weight[:, : 3 * width], NN).astype(jnp.bfloat16)
    heads = packed.reshape(length, 3, HEADS, size)
    scores = jnp.einsum("qhd,khd->hqk", heads[:, 0], heads[:, 1], preferred_element_type=jnp.float32)
    scores = jnp.where(mask[None], scores * size**-0.5, NEGATIVE)
    weights = jnp.exp(scores - jnp.max(scores, -1, keepdims=True))
    probs = weights / jnp.sum(weights, -1, keepdims=True)
    mixed = jnp.einsum("hqk,khd->qhd", probs.astype(jnp.bfloat16), heads[:, 2], preferred_element_type=jnp.float32)
    mixed = mixed.reshape(length, width).astype(jnp.bfloat16)
    branch = matmul(mixed, weight[:, 3 * width :], NN)
    return branch, (heads, probs, mixed)


def attention_backward(stream, weight, kept, grad_low):
    heads, probs, mixed = kept
    length, width = stream.shape
    size = width // HEADS
    grad_out = matmul(mixed, grad_low, TN)
    grad_mixed = matmul(grad_low, weight[:, 3 * width :], NT).astype(jnp.bfloat16)
    grad_mixed = grad_mixed.reshape(length, HEADS, size)
    grad_probs = jnp.einsum("qhd,khd->hqk", grad_mixed, heads[:, 2], preferred_element_type=jnp.float32)
    centre = jnp.sum(probs * grad_probs, -1, keepdims=True)
    grad_scores = (probs * (grad_probs - centre)).astype(jnp.bfloat16)
    low = probs.astype(jnp.bfloat16)
    scale = size**-0.5
    grad_q = jnp.einsum("hqk,khd->qhd", grad_scores, heads[:, 1], preferred_element_type=jnp.float32) * scale
    grad_k = jnp.einsum("hqk,qhd->khd", grad_scores, heads[:, 0], preferred_element_type=jnp.float32) * scale
    grad_v = jnp.einsum("hqk,qhd->khd", low, grad_mixed, preferred_element_type=jnp.float32)
    packed = jnp.concatenate([grad_q, grad_k, grad_v], axis=1).reshape(length, 3 * width)
    packed = packed.astype(jnp.bfloat16)
    grad_in = matmul(stream, packed, TN)
    grad_inputs = matmul(packed, weight[:, : 3 * width], NT)
    return grad_inputs, jnp.concatenate([grad_in, grad_out], axis=1)


def feed_forward(stream, weight, down):
    pre = matmul(stream, weight, NN)
    active = jax.nn.gelu(pre, approximate=True).astype(jnp.bfloat16)
    return matmul(active, down, NN), (pre, active)


def feed_backward(stream, weight, down, kept, grad_low):
    pre, active = kept
    grad_down = matmul(active, grad_low, TN)
    grad_active = matmul(grad_low, down, NT)
    pull = jax.vjp(lambda value: jax.nn.gelu(value, approximate=True), pre)[1]
    grad_pre = pull(grad_active)[0].astype(jnp.bfloat16)
    grad_up = matmul(stream, grad_pre, TN)
    return matmul(grad_pre, weight, NT), grad_up, grad_down


def micro_step(rows, pull, segment, mats, downs, gains, biases):
    low = jnp.bfloat16
    mask = segment[:, None] == segment[None, :]
    stream, dual = rows, jnp.zeros_like(rows)
    saved = []
    for sub in range(4):
        if sub % 2 == 0:
            branch, kept = attention_forward(stream, mats[sub], mask)
        else:
            branch, kept = feed_forward(stream, mats[sub], downs[sub // 2])
        normal, inverse = norm_stats(stream.astype(jnp.float32) + branch)
        out = normal * gains[sub] + biases[sub]
        total = dual.astype(jnp.float32) + branch
        saved.append((stream, kept, normal, inverse))
        if sub < 3:
            stream, dual = out.astype(low), total.astype(low)
    dual_normal, dual_inverse = norm_stats(total)
    output = (out + dual_normal).astype(low)
    grad_out, grad_dual = pull, norm_back(dual_normal, dual_inverse, pull)
    grads_a, grads_b, grads_n = [None] * 4, [None] * 2, [None] * 4
    for sub in (3, 2, 1, 0):
        stream, kept, normal, inverse = saved[sub]
        grads_n[sub] = jnp.stack([jnp.sum(grad_out * normal, 0), jnp.sum(grad_out, 0)], axis=1)
        summed = norm_back(normal, inverse, grad_out * gains[sub])
        branch_low = (summed + grad_dual).astype(low)
        if sub % 2 == 0:
            inner, grads_a[sub] = attention_backward(stream, mats[sub], kept, branch_low)
        else:
            inner, grads_a[sub], grads_b[sub // 2] = feed_backward(
                stream, mats[sub], downs[sub // 2], kept, branch_low
            )
        grad_in = summed + inner
        if sub > 0:
            grad_out = grad_in.astype(low).astype(jnp.float32)
            grad_dual = grad_dual.astype(low).astype(jnp.float32)
    return output, grad_in, jnp.stack(grads_a), jnp.stack(grads_b), jnp.stack(grads_n)


def finish_step(grad_norm, output, input_grad, *groups):
    factor = CLIP_NORM / jnp.maximum(grad_norm, CLIP_NORM)
    results = [grad_norm, output[None], input_grad[None]]
    for weight, one, two, grad, rate, decay in groups:
        clip = grad * factor
        moment, square_new, master = adam_update(weight, one, two, clip, rate, decay)
        results += [clip, moment, square_new, master, master.astype(jnp.bfloat16)]
    return tuple(results)


def body(
    tokens, cotangent, lengths, mat_a, mat_b, norms, first_a, second_a, first_b, second_b, first_n, second_n
):
    low = jnp.bfloat16
    own = lax.axis_index("section")
    length = tokens.shape[0] // lengths.shape[0]
    rows = lax.dynamic_slice_in_dim(tokens, own * length, length, 0)
    segment, live = segments_of(lax.dynamic_index_in_dim(lengths, own, 0, keepdims=False), length)
    pull = lax.dynamic_slice_in_dim(cotangent, own * length, length, 0).astype(jnp.float32) * live[:, None]

    def gathered(value):
        return lax.all_gather(lax.all_gather(value, "dp", axis=1, tiled=True), "section", axis=0, tiled=True)

    mats = gathered(mat_a.astype(low))
    scales = gathered(norms.astype(low)).astype(jnp.float32)
    downs = lax.all_gather(mat_b.astype(low), "section", axis=2, tiled=True)
    downs = lax.all_gather(downs, "dp", axis=1, tiled=True)
    output, input_grad, part_a, part_b, part_n = micro_step(
        rows, pull, segment, mats, downs, scales[:, :, 0], scales[:, :, 1]
    )

    def scattered(value, section_dim):
        value = lax.psum_scatter(value, "section", scatter_dimension=section_dim, tiled=True)
        return lax.psum_scatter(value, "dp", scatter_dimension=1, tiled=True).astype(jnp.float32)

    grad_a = scattered(part_a.astype(low), 0)
    grad_b = scattered(part_b.astype(low), 2)
    grad_n = scattered(part_n, 0)
    square = jnp.sum(grad_a * grad_a) + jnp.sum(grad_b * grad_b) + jnp.sum(grad_n * grad_n)
    grad_norm = jnp.sqrt(lax.psum(square, ("section", "dp")))
    return finish_step(
        grad_norm, output, input_grad,
        (mat_a, first_a, second_a, grad_a, MATRIX_RATE, MATRIX_DECAY),
        (mat_b, first_b, second_b, grad_b, MATRIX_RATE, MATRIX_DECAY),
        (norms, first_n, second_n, grad_n, NORM_RATE, 0.0),
    )


LOW = jnp.bfloat16
WIDE = jnp.float32
MESH = pl.DeviceIdType.MESH
SECTIONS = 4
LANES = 128
BLOCK = 64
KERNEL_VMEM = 64 * 1024 * 1024 - 256 * 1024


def gradient_items(rows_a, rows_b, cols_b, width, hidden):
    part = rows_a // SECTIONS
    return (
        ("B1", 3, cols_b // 2, rows_b),
        ("F3", 3, part, hidden // 2),
        ("O2", 2, part, width // 2),
        ("K2", 2, part, 3 * width // 2),
        ("B0", 1, cols_b // 2, rows_b),
        ("F1", 1, part, hidden // 2),
        ("O0", 0, part, width // 2),
        ("K0", 0, part, 3 * width // 2),
    )


def item_scratch(name, chips, rows, columns):
    piece = (rows, columns)
    return (
        ("own" + name, (chips, SECTIONS, 2) + piece, LOW),
        ("farx" + name, (chips,) + piece, LOW),
        ("fary" + name, (chips,) + piece, LOW),
        ("nearx" + name, (2, chips) + piece, LOW),
        ("neary" + name, (2, chips) + piece, LOW),
        ("line" + name, (chips, 2) + piece, LOW),
        ("done" + name, (2,) + piece if name[0] == "B" else (SECTIONS, 2) + piece, WIDE if name[0] == "B" else LOW),
    )


def kernel_scratch(chips, rows_a, rows_b, cols_b, length, width, hidden):
    devices = 2 * chips
    items = gradient_items(rows_a, rows_b, cols_b, width, hidden)
    count = len(items)
    received = sum((item_scratch(name, chips, rows, columns) for name, _, rows, columns in items), ())
    return received + (
        ("fac_s", (32,), None),
        ("fac_r", (32,), None),
        ("px_s", (count, 3), None),
        ("px_r", (count, 3), None),
        ("py_s", (count, 3), None),
        ("py_r", (count, 3), None),
        ("line_s", (count, chips), None),
        ("line_r", (count, chips), None),
        ("done_s", (count,), None),
        ("done_r", (count, SECTIONS), None),
        ("wa", (4, width, hidden), LOW),
        ("wb", (2, hidden, width), LOW),
        ("tiles", (devices, SECTIONS, 8, LANES), WIDE),
        ("x", (4, length, width), LOW),
        ("xt", (4, chips, 2, rows_a, length), LOW),
        ("xtc", (4, chips, rows_a, 2 * length), LOW),
        ("y", (length, width), LOW),
        ("cot", (length, width), LOW),
        ("bias", (length, length), WIDE),
        ("live", (length, 1), WIDE),
        ("f", (length, width), WIDE),
        ("n", (4, length, width), WIDE),
        ("inv", (4, length, 1), WIDE),
        ("q", (2, length, width), LOW),
        ("k", (2, length, width), LOW),
        ("v", (2, length, width), LOW),
        ("kt", (2, width, length), LOW),
        ("vt", (2, width, length), LOW),
        ("ot", (2, chips, 2, rows_a, length), LOW),
        ("otc", (2, chips, rows_a, 2 * length), LOW),
        ("pt", (2, HEADS, length, length), LOW),
        ("g", (2, length, hidden), LOW),
        ("gc", (2, chips, 2 * length, rows_b), LOW),
        ("slope", (2, length, hidden), LOW),
        ("gx", (length, width), WIDE),
        ("gy", (length, width), WIDE),
        ("df", (2, 2 * length, width), LOW),
        ("dft", (2, width, 2 * length), LOW),
        ("dm", (length, width), LOW),
        ("dqt", (width, length), LOW),
        ("dh", (2, 2 * length, hidden), LOW),
        ("dp", (2, 2 * length, 3 * width), LOW),
        ("ng", (devices, 8, width), WIDE),
        ("ns", (SECTIONS, 8, width), WIDE),
        ("sq", (devices, 8, LANES), WIDE),
        ("sqs", (SECTIONS, 8, LANES), WIDE),
        ("sum", (8, LANES), WIDE),
        ("in_s", (2,), None),
        ("gz_s", (3, 2, chips, 2), None),
        ("gz_r", (3, chips, 2), None),
        ("gx_s", (3, chips, 2), None),
        ("gx_r", (3, chips, 2), None),
        ("gy_s", (3, chips, 2), None),
        ("gy_r", (3, chips, 2), None),
        ("gxr_s", (3, chips), None),
        ("gxr_r", (3, chips), None),
        ("gyr_s", (3, chips), None),
        ("gyr_r", (3, chips), None),
        ("gs_s", (6,), None),
        ("gs_r", (6,), None),
        ("small_s", (3, 2), None),
        ("small_r", (3, 2), None),
    )


INPUTS = ("tokens", "cotangent", "lengths", "mat_a", "mat_b", "norms")
OUTPUTS = ("grad_a", "grad_b", "grad_n", "square", "output", "input_grad")


def step_kernel(names, *refs):
    r = types.SimpleNamespace(**dict(zip(names, refs)))
    width, hidden = r.wa.shape[1:]
    length = r.x.shape[1]
    rows_a, (rows_b, cols_b) = r.mat_a.shape[1], r.mat_b.shape[1:]
    devices = r.tiles.shape[0]
    chips = devices // 2
    half_a, half_b = rows_a // 2, cols_b // 2
    grad_items = gradient_items(rows_a, rows_b, cols_b, width, hidden)
    head = width // HEADS
    scale = head**-0.5

    s, d = lax.axis_index("section"), lax.axis_index("dp")
    z, c = lax.div(d, 2), lax.rem(d, 2)
    sx = s + 1 - 2 * lax.rem(s, 2)
    sy = lax.rem(s + 2, SECTIONS)
    sd = SECTIONS - 1 - s
    to_sibling = {"dp": d + 1 - 2 * c}
    to_up, to_down = {"dp": d + 2}, {"dp": d - 2}
    to_x, to_y = {"section": sx}, {"section": sy}
    below, above = z > 0, z < chips - 1
    group = [{"dp": lax.rem(d + step, devices)} for step in range(1, devices)]
    plane = [{"section": lax.rem(s + step, SECTIONS)} for step in range(1, SECTIONS)]
    finish = []

    def when(condition, work):
        if condition is None:
            work()
        else:
            pl.when(condition)(work)

    def push(source, target, send_sem, recv_sem, device):
        pltpu.make_async_remote_copy(
            src_ref=source,
            dst_ref=target,
            send_sem=send_sem,
            recv_sem=recv_sem,
            device_id=device,
            device_id_type=MESH,
        ).start()

    def arrived(target, sem):
        pltpu.make_async_remote_copy(
            src_ref=target, dst_ref=target, send_sem=sem, recv_sem=sem, device_id=to_x, device_id_type=MESH
        ).wait_recv()

    def sent(source, sem):
        pltpu.make_async_remote_copy(
            src_ref=source, dst_ref=source, send_sem=sem, recv_sem=sem, device_id=to_x, device_id_type=MESH
        ).wait_send()

    def at_end(condition, source, sem):
        finish.append((condition, source, sem))

    def aligned(start, size):
        return pl.ds(pl.multiple_of(start, size), size)

    own_x = pltpu.make_async_copy(r.tokens.at[aligned(s * length, length)], r.x.at[0], r.in_s.at[0])
    own_cot = pltpu.make_async_copy(r.cotangent.at[aligned(s * length, length)], r.cot, r.in_s.at[1])
    own_x.start()
    own_cot.start()
    barrier = pltpu.get_barrier_semaphore()
    for peer in group + plane:
        pl.semaphore_signal(barrier, inc=1, device_id=peer, device_id_type=MESH)
    r.wa[s, aligned(d * rows_a, rows_a), :] = r.mat_a[0].astype(LOW)
    for layer in range(2):
        r.wb[layer, aligned(d * rows_b, rows_b), aligned(s * cols_b, cols_b)] = r.mat_b[layer].astype(LOW)
    norms = r.norms[0].astype(LOW).astype(WIDE)
    nothing = jnp.zeros((2, rows_a), WIDE)
    even = jnp.concatenate([norms, nothing], axis=1)
    odd = jnp.concatenate([nothing, norms], axis=1)
    r.tiles[d, s, 0:2, :] = jnp.where(c == 0, even, odd)
    r.tiles[d, s, 2:8, :] = jnp.zeros((6, LANES), WIDE)
    pl.semaphore_wait(barrier, len(group) + len(plane))

    def small_out(which, source):
        for peer in group:
            push(source, source, r.small_s.at[which, 0], r.small_r.at[which, 0], peer)

    def small_group(which, like):
        arrived(like, r.small_r.at[which, 0])
        sent(like, r.small_s.at[which, 0])

    def small_plane_out(which, source):
        for peer in plane:
            push(source, source, r.small_s.at[which, 1], r.small_r.at[which, 1], peer)

    def small_plane(which, like):
        arrived(like, r.small_r.at[which, 1])
        sent(like, r.small_s.at[which, 1])

    def block_a(section, chip, half):
        return r.wa.at[section, aligned((2 * chip + c) * rows_a + half * half_a, half_a), :]

    def block_b(layer):
        part = rows_b // 2

        def block(section, chip, half):
            return r.wb.at[
                layer,
                aligned((2 * chip + c) * rows_b + half * part, part),
                aligned(section * cols_b, cols_b),
            ]

        return block

    items = (block_a, block_b(0), block_b(1))

    def to_the_sibling(item, section, chip, half):
        block = items[item](section, chip, half)
        slot = section if item == 0 else 3 + item
        push(block, block, r.gs_s.at[slot], r.gs_r.at[slot], to_sibling)

    def spread_plane(item, chip):
        for half in range(2):
            block = items[item](s, chip, half)
            push(block, block, r.gx_s.at[item, chip, half], r.gx_r.at[item, chip, half], to_x)
            push(block, block, r.gy_s.at[item, chip, half], r.gy_r.at[item, chip, half], to_y)
            to_the_sibling(item, s, chip, half)

    def up(item, chip, half):
        block = items[item](s, chip, half)
        push(block, block, r.gz_s.at[item, 0, chip, half], r.gz_r.at[item, chip, half], to_up)

    def down(item, chip, half):
        block = items[item](s, chip, half)
        push(block, block, r.gz_s.at[item, 1, chip, half], r.gz_r.at[item, chip, half], to_down)

    def start_line(item):
        for half in range(2):
            when(above, lambda: up(item, z, half))
            when(below, lambda: down(item, z, half))

    def line_step(item, step):
        def from_below():
            for half in range(2):
                arrived(items[item](s, z - step, half), r.gz_r.at[item, z - step, half])
                when(above, lambda: up(item, z - step, half))
            spread_plane(item, z - step)

        def from_above():
            for half in range(2):
                arrived(items[item](s, z + step, half), r.gz_r.at[item, z + step, half])
                when(below, lambda: down(item, z + step, half))
            spread_plane(item, z + step)

        when(z >= step, from_below)
        when(z + step < chips, from_above)

    def plane_step(item):
        for chip in range(chips):
            for half in range(2):
                arrived(items[item](sx, chip, half), r.gx_r.at[item, chip, half])
                if half == 1:
                    block = items[item](sx, chip, half)
                    push(block, block, r.gyr_s.at[item, chip], r.gyr_r.at[item, chip], to_y)
                to_the_sibling(item, sx, chip, half)
                arrived(items[item](sy, chip, half), r.gy_r.at[item, chip, half])
                if half == 0:
                    block = items[item](sy, chip, half)
                    push(block, block, r.gxr_s.at[item, chip], r.gxr_r.at[item, chip], to_x)
                to_the_sibling(item, sy, chip, half)

    def relay_step(item):
        for chip in range(chips):
            arrived(items[item](sd, chip, 0), r.gxr_r.at[item, chip])
            to_the_sibling(item, sd, chip, 0)
            arrived(items[item](sd, chip, 1), r.gyr_r.at[item, chip])
            to_the_sibling(item, sd, chip, 1)

    whole_a = r.wa.at[0, pl.ds(0, chips * rows_a)]
    whole_b = r.wb.at[0, pl.ds(0, chips * rows_b)]
    def gather_sends(item):
        for chip in range(chips):
            for half in range(2):
                block = items[item](0, chip, half)
                at_end(None, block, r.gx_s.at[item, chip, half])
                at_end(None, block, r.gy_s.at[item, chip, half])
                at_end(above & (z >= chip), block, r.gz_s.at[item, 0, chip, half])
                at_end(below & (z <= chip), block, r.gz_s.at[item, 1, chip, half])
            block = items[item](0, chip, 0)
            at_end(None, block, r.gxr_s.at[item, chip])
            at_end(None, block, r.gyr_s.at[item, chip])

    def row_block(chip, half):
        part = rows_b // 2
        return r.wb.at[0, aligned((2 * chip + c) * rows_b + half * part, part), :]

    def rows_to_sibling(chip, half):
        push(row_block(chip, half), row_block(chip, half), r.gs_s.at[4], r.gs_r.at[4], to_sibling)

    def rows_up(chip, half):
        rows = row_block(chip, half)
        push(rows, rows, r.gz_s.at[1, 0, chip, half], r.gz_r.at[1, chip, half], to_up)

    def rows_down(chip, half):
        rows = row_block(chip, half)
        push(rows, rows, r.gz_s.at[1, 1, chip, half], r.gz_r.at[1, chip, half], to_down)

    def rows_plane():
        for half in range(2):
            block = items[1](s, z, half)
            push(block, block, r.gx_s.at[1, 0, half], r.gx_r.at[1, 0, half], to_x)
            push(block, block, r.gy_s.at[1, 0, half], r.gy_r.at[1, 0, half], to_y)
            at_end(None, block, r.gx_s.at[1, 0, half])
            at_end(None, block, r.gy_s.at[1, 0, half])

    def rows_relay():
        for half in range(2):
            arrived(items[1](sx, z, half), r.gx_r.at[1, 0, half])
            arrived(items[1](sy, z, half), r.gy_r.at[1, 0, half])
        block = items[1](sx, z, 1)
        push(block, block, r.gyr_s.at[1, 0], r.gyr_r.at[1, 0], to_y)
        block = items[1](sy, z, 0)
        push(block, block, r.gxr_s.at[1, 0], r.gxr_r.at[1, 0], to_x)
        at_end(None, block, r.gyr_s.at[1, 0])
        at_end(None, block, r.gxr_s.at[1, 0])

    def rows_line():
        for half, sem in ((0, r.gxr_r), (1, r.gyr_r)):
            arrived(items[1](sd, z, half), sem.at[1, 0])
            when(above, lambda: rows_up(z, half))
            when(below, lambda: rows_down(z, half))
            rows_to_sibling(z, half)
        for chip in range(chips):
            for half in range(2):
                at_end(above & (z >= chip), row_block(chip, half), r.gz_s.at[1, 0, chip, half])
                at_end(below & (z <= chip), row_block(chip, half), r.gz_s.at[1, 1, chip, half])

    def rows_step(step):
        def from_below():
            for half in range(2):
                arrived(row_block(z - step, half), r.gz_r.at[1, z - step, half])
                when(above, lambda: rows_up(z - step, half))
                rows_to_sibling(z - step, half)

        def from_above():
            for half in range(2):
                arrived(row_block(z + step, half), r.gz_r.at[1, z + step, half])
                when(below, lambda: rows_down(z + step, half))
                rows_to_sibling(z + step, half)

        when(z >= step, from_below)
        when(z + step < chips, from_above)

    mine, other = pl.ds(0, length), pl.ds(length, length)

    def give(slot, source, target):
        push(source, target, r.fac_s.at[slot], r.fac_r.at[slot], to_sibling)
        at_end(None, target, r.fac_s.at[slot])

    def taken(slot, target):
        arrived(target, r.fac_r.at[slot])

    def give_rows(layer):
        r.xt[layer] = r.x[layer].T.reshape(chips, 2, rows_a, length)
        r.xtc[layer, :, :, 0:length] = r.xt[layer, :, c]
        give(layer, r.xt.at[layer, :, 1 - c], r.xtc.at[layer, :, :, other])

    def product(left, right, dims):
        return lax.dot_general(left, right, (dims, ((), ())), preferred_element_type=WIDE)

    def loop(count, work):
        def one(index, carry):
            work(index)
            return carry

        lax.fori_loop(0, count, one, 0)

    def gain_row(layer, kind):
        parts = [
            r.tiles[2 * chip, layer, kind : kind + 1, :] + r.tiles[2 * chip + 1, layer, kind : kind + 1, :]
            for chip in range(chips)
        ]
        return jnp.concatenate(parts, axis=1)

    def stats(value):
        centre = value - jnp.mean(value, -1, keepdims=True)
        inverse = lax.rsqrt(jnp.mean(centre * centre, -1, keepdims=True) + EPSILON)
        return centre * inverse, inverse

    lane = lax.broadcasted_iota(jnp.int32, (1, 2 * head), 1)
    first_half = (lane < head).astype(WIDE)
    half_masks = (first_half.astype(LOW), (1.0 - first_half).astype(LOW))

    def prepare_masks():
        ends, total = [], jnp.int32(0)
        for slot in range(r.lengths.shape[1]):
            total = total + r.lengths[s, slot]
            ends.append(total)
        down_places = lax.broadcasted_iota(jnp.int32, (length, 1), 0)
        across_places = lax.broadcasted_iota(jnp.int32, (1, length), 1)
        down_segment = jnp.zeros((length, 1), jnp.int32)
        across_segment = jnp.zeros((1, length), jnp.int32)
        for end in ends:
            down_segment = down_segment + (end <= down_places).astype(jnp.int32)
            across_segment = across_segment + (end <= across_places).astype(jnp.int32)
        r.bias[...] = jnp.where(down_segment == across_segment, 0.0, NEGATIVE)
        r.live[...] = (down_places < total).astype(WIDE)

    def attention(layer):
        at = layer // 2
        rows = r.x[layer]
        r.q[at] = product(rows, r.wa[layer, :, 0:width], NN).astype(LOW) * jnp.asarray(scale, LOW)
        keys = product(rows, r.wa[layer, :, width : 2 * width], NN).astype(LOW)
        r.k[at] = keys
        values = product(rows, r.wa[layer, :, 2 * width : 3 * width], NN).astype(LOW)
        r.v[at] = values
        r.vt[at] = values.T

        def pair(index):
            lanes = aligned(index * 2 * head, 2 * head)
            for which in range(2):
                scores = product(r.k[at, :, lanes], r.q[at, :, lanes] * half_masks[which], NT) + r.bias[...]
                weights = jnp.exp(scores - jnp.max(scores, 0, keepdims=True))
                probs = (weights * (1.0 / jnp.sum(weights, 0, keepdims=True))).astype(LOW)
                r.pt[at, 2 * index + which] = probs
                place = aligned((2 * index + which) * head, head)
                r.ot[at, index, which] = product(r.vt[at, place, :], probs, NN).astype(LOW)

        def pairs(step):
            pair(2 * step)
            pair(2 * step + 1)

        loop(HEADS // 4, pairs)
        r.otc[at, :, :, 0:length] = r.ot[at, :, c]
        give(4 + at, r.ot.at[at, :, 1 - c], r.otc.at[at, :, :, other])
        r.f[...] = product(r.ot[at].reshape(width, length).T, r.wa[layer, :, 3 * width :], NN)

    def expand(layer):
        at = layer // 2
        def columns(index):
            place = pl.ds(index * width, width)
            pre = product(r.x[layer], r.wa[layer, :, place], NN)
            squared = pre * pre
            slope = 0.7978845608 * (1.0 + 3 * 0.044715 * squared)
            bent = jnp.tanh(0.7978845608 * pre * (1.0 + 0.044715 * squared))
            r.g[at, :, place] = (0.5 * pre * (1.0 + bent)).astype(LOW)
            r.slope[at, :, place] = (0.5 * (1.0 + bent) + 0.5 * pre * (1.0 - bent * bent) * slope).astype(LOW)
            block = aligned((2 * index + c) * rows_b, rows_b)
            r.gc[at, index, 0:length, :] = r.g[at, :, block]
            block = aligned((2 * index + 1 - c) * rows_b, rows_b)
            give(6 + chips * at + index, r.g.at[at, :, block], r.gc.at[at, index, other, :])

        for index in range(hidden // width):
            columns(index)

    def contract(layer):
        r.f[...] = product(r.g[layer // 2], r.wb[layer // 2], NN)

    def by_rows(work):
        for index in range(length // BLOCK):
            work(pl.ds(index * BLOCK, BLOCK))

    def normalize(layer):
        gain, offset = gain_row(layer, 0), gain_row(layer, 1)

        def some(rows):
            branch = r.f[rows, :]
            normal, inverse = stats(r.x[layer, rows, :].astype(WIDE) + branch)
            r.n[layer, rows, :] = normal
            r.inv[layer, rows, :] = inverse
            out = normal * gain + offset
            dual = branch if layer == 0 else r.y[rows, :].astype(WIDE) + branch
            if layer < 3:
                r.x[layer + 1, rows, :] = out.astype(LOW)
                r.y[rows, :] = dual.astype(LOW)
            else:
                dual_normal, dual_inverse = stats(dual)
                r.output[rows, :] = (out + dual_normal).astype(LOW)
                pull = r.cot[rows, :].astype(WIDE) * r.live[rows, :]
                r.gx[rows, :] = pull
                r.gy[rows, :] = norm_back(dual_normal, dual_inverse, pull)

        by_rows(some)

    def back_normalize(layer):
        gain = gain_row(layer, 0)

        def some(index, sums):
            rows = pl.ds(index * BLOCK, BLOCK)
            upstream = r.gx[rows, :]
            normal = r.n[layer, rows, :]
            summed = norm_back(normal, r.inv[layer, rows, :], upstream * gain)
            dual = r.gy[rows, :]
            r.gx[rows, :] = summed
            r.df[layer // 2, rows, :] = (summed + dual).astype(LOW)
            if layer == 3:
                r.gy[rows, :] = dual.astype(LOW).astype(WIDE)
            return (
                sums[0] + jnp.sum(upstream * normal, 0, keepdims=True),
                sums[1] + jnp.sum(upstream, 0, keepdims=True),
            )

        zero = jnp.zeros((1, width), WIDE)
        gains, offsets = zero, zero
        for index in range(length // BLOCK):
            gains, offsets = some(index, (gains, offsets))
        r.ng[d, 2 * layer : 2 * layer + 1, :] = gains
        r.ng[d, 2 * layer + 1 : 2 * layer + 2, :] = offsets

    def pass_down(layer, inner):
        total = r.gx[...] + inner
        if layer > 0:
            r.gx[...] = total.astype(LOW).astype(WIDE)
        else:
            r.input_grad[...] = total

    base = 6 + 2 * chips

    def back_hidden(layer):
        at = layer // 2
        r.dft[at, :, 0:length] = r.df[at, 0:length, :].T
        give(base + at, r.dft.at[at, :, mine], r.dft.at[at, :, other])
        for index in range(hidden // width):
            place = pl.ds(index * width, width)
            pulled = product(r.df[at, 0:length, :], r.wb[at, pl.ds(index * width, width), :], NT)
            r.dh[at, 0:length, place] = (pulled * r.slope[at, :, place].astype(WIDE)).astype(LOW)
            give(base + 2 + chips * at + index, r.dh.at[at, mine, place], r.dh.at[at, other, place])

    def back_expand_end(layer):
        pass_down(layer, product(r.dh[layer // 2, 0:length, :], r.wa[layer], NT))

    def back_output(layer):
        at = layer // 2
        give(base + 2 + 2 * chips + at, r.df.at[at, mine], r.df.at[at, other])
        r.dm[...] = product(r.df[at, 0:length, :], r.wa[layer, :, 3 * width :], NT).astype(LOW)
        r.kt[at] = (r.k[at] * jnp.asarray(scale, LOW)).T

    def back_heads(layer, begin, count):
        at = layer // 2

        def pair(index):
            lanes = aligned(index * 2 * head, 2 * head)
            pulled = r.dm[:, lanes]
            keys, values = [], []
            for which in range(2):
                probs = r.pt[at, 2 * index + which]
                grad = product(r.v[at, :, lanes], pulled * half_masks[which], NT)
                full = probs.astype(WIDE)
                centre = jnp.sum(full * grad, 0, keepdims=True)
                scores = (full * (grad - centre)).astype(LOW)
                keys.append(product(scores, r.q[at, :, lanes], NN))
                values.append(product(probs, pulled, NN))
                place = aligned((2 * index + which) * head, head)
                r.dqt[place, :] = product(r.kt[at, place, :], scores, NN).astype(LOW)
            r.dp[at, 0:length, aligned(width + index * 2 * head, 2 * head)] = jnp.where(
                lane < head, keys[0], keys[1]
            ).astype(LOW)
            r.dp[at, 0:length, aligned(2 * width + index * 2 * head, 2 * head)] = jnp.where(
                lane < head, values[0], values[1]
            ).astype(LOW)

        def pairs(step):
            pair(begin + 2 * step)
            pair(begin + 2 * step + 1)

        loop(count // 2, pairs)

    def back_packed(layer):
        at = layer // 2
        slot = base + 4 + 2 * chips + 2 * at
        place = pl.ds(width, 2 * width)
        give(slot, r.dp.at[at, mine, place], r.dp.at[at, other, place])
        r.dp[at, 0:length, 0:width] = r.dqt[...].T
        place = pl.ds(0, width)
        give(slot + 1, r.dp.at[at, mine, place], r.dp.at[at, other, place])

    def back_packed_end(layer):
        pass_down(layer, product(r.dp[layer // 2, 0:length, :], r.wa[layer, :, 0 : 3 * width], NT))

    def keep(name, half, place, value):
        own = getattr(r, "own" + name)
        own[:, :, half, :, place] = value.astype(LOW).reshape(chips, SECTIONS, rows_a // SECTIONS, value.shape[1])

    def chip_rows(value):
        return value.reshape(chips * rows_a, 2 * length)

    def grad_down(at):
        own = getattr(r, "ownB%d" % at)
        taken(base + at, r.dft.at[at, :, other])
        for chip in range(chips):
            taken(6 + chips * at + chip, r.gc.at[at, chip, other, :])
            value = product(r.dft[at], r.gc[at, chip], NN)
            own[chip] = value.astype(LOW).reshape(SECTIONS, 2, half_b, rows_b)

    def grad_up(layer):
        at = layer // 2
        taken(layer, r.xtc.at[layer, :, :, other])
        for index in range(hidden // width):
            place = pl.ds(index * width, width)
            taken(base + 2 + chips * at + index, r.dh.at[at, other, place])
            value = product(chip_rows(r.xtc[layer]), r.dh[at, :, place], NN)
            keep("F%d" % layer, index // 2, pl.ds(index % 2 * width, width), value)

    def grad_output(layer):
        at = layer // 2
        taken(4 + at, r.otc.at[at, :, :, other])
        taken(base + 2 + 2 * chips + at, r.df.at[at, other])
        for half in range(2):
            place = pl.ds(half * width // 2, width // 2)
            value = product(chip_rows(r.otc[at]), r.df[at, :, place], NN)
            keep("O%d" % layer, half, pl.ds(0, width // 2), value)

    def grad_packed(layer):
        at = layer // 2
        slot = base + 4 + 2 * chips + 2 * at
        taken(layer, r.xtc.at[layer, :, :, other])
        taken(slot, r.dp.at[at, other, pl.ds(width, 2 * width)])
        taken(slot + 1, r.dp.at[at, other, pl.ds(0, width)])
        part = 3 * width // 2
        for half in range(2):
            value = product(chip_rows(r.xtc[layer]), r.dp[at, :, half * part : (half + 1) * part], NN)
            keep("K%d" % layer, half, pl.ds(0, part), value)

    def joined(target, others):
        return functools.reduce(
            lambda left, right: left + right, [ref[...].astype(WIDE) for ref in (target, *others)]
        )

    def add_into(target, others):
        if len(others) == 1:
            target[...] = target[...] + others[0][...]
        else:
            target[...] = joined(target, others).astype(LOW)

    places = {name: place for place, (name, _, _, _) in enumerate(grad_items)}

    def buffers(name):
        parts = ("own", "farx", "fary", "nearx", "neary", "line", "done")
        return types.SimpleNamespace(**{part: getattr(r, part + name) for part in parts})

    def to_plane(name):
        item, place = buffers(name), places[name]

        def over_x(section, half, target, slot):
            push(item.own.at[:, section, half], target, r.px_s.at[place, slot], r.px_r.at[place, slot], to_x)
            at_end(None, item.farx, r.px_s.at[place, slot])

        def over_y(section, half, target, slot):
            push(item.own.at[:, section, half], target, r.py_s.at[place, slot], r.py_r.at[place, slot], to_y)
            at_end(None, item.farx, r.py_s.at[place, slot])

        over_x(sd, 0, item.farx, 2)
        over_y(sd, 1, item.fary, 2)
        over_x(sx, 0, item.nearx.at[0], 0)
        over_y(sy, 1, item.neary.at[1], 1)

    def through_plane(name):
        item, place = buffers(name), places[name]
        own = item.own
        arrived(item.fary, r.py_r.at[place, 2])
        add_into(own.at[:, sx, 1], [item.fary])
        push(own.at[:, sx, 1], item.nearx.at[1], r.px_s.at[place, 1], r.px_r.at[place, 1], to_x)
        at_end(None, item.farx, r.px_s.at[place, 1])
        arrived(item.farx, r.px_r.at[place, 2])
        add_into(own.at[:, sy, 0], [item.farx])
        push(own.at[:, sy, 0], item.neary.at[0], r.py_s.at[place, 0], r.py_r.at[place, 0], to_y)
        at_end(None, item.farx, r.py_s.at[place, 0])

    def to_line(name):
        item, place = buffers(name), places[name]
        own = item.own.at[:, s]
        for half in range(2):
            arrived(item.nearx.at[half], r.px_r.at[place, half])
            arrived(item.neary.at[half], r.py_r.at[place, half])
            add_into(own.at[:, half], [item.nearx.at[half], item.neary.at[half]])
        for step in range(1, chips):
            chip = lax.rem(z + step, chips)
            push(
                own.at[chip],
                item.line.at[z],
                r.line_s.at[place, step],
                r.line_r.at[place, z],
                {"dp": 2 * chip + c},
            )
            at_end(None, item.line.at[0], r.line_s.at[place, step])

    def to_owner(name):
        item, place = buffers(name), places[name]
        others = [lax.rem(z + step, chips) for step in range(1, chips)]
        for chip in others:
            arrived(item.line.at[chip], r.line_r.at[place, chip])
        total = joined(item.own.at[z, s], [item.line.at[chip] for chip in others])
        square = total * total
        while square.ndim > 2:
            square = jnp.sum(square, 0)
        square = jnp.sum(jnp.sum(square, 0, keepdims=True), 1, keepdims=True)
        r.sum[...] = r.sum[...] + jnp.broadcast_to(square, (8, LANES))
        if name[0] == "B":
            item.done[...] = total
            return
        item.done[s] = total.astype(LOW)
        layer = grad_items[place][1]
        mine = item.done.at[s]
        away = s != layer
        when(
            away,
            lambda: push(mine, mine, r.done_s.at[place], r.done_r.at[place, s], {"section": jnp.int32(layer)}),
        )
        at_end(away, mine, r.done_s.at[place])

    def collect(name):
        item, place = buffers(name), places[name]
        layer = grad_items[place][1]

        def work():
            for section in range(SECTIONS):
                if section != layer:
                    arrived(item.done.at[section], r.done_r.at[place, section])
            columns = item.done.shape[-1]
            start = 3 * width if name[0] == "O" else 0
            for section in range(SECTIONS):
                for half in range(2):
                    rows = pl.ds(section * (rows_a // SECTIONS), rows_a // SECTIONS)
                    place_to = pl.ds(start + half * columns, columns)
                    r.grad_a[rows, place_to] = item.done[section, half].astype(WIDE)

        when(s == layer, work)

    def all_sent():
        for condition, source, sem in finish:
            when(condition, functools.partial(sent, source, sem))
        finish.clear()

    small_out(0, r.tiles.at[d, s])
    start_line(0)
    spread_plane(0, z)
    rows_plane()
    line_step(0, 1)
    rows_relay()
    line_step(0, 2)
    rows_line()
    start_line(2)
    for step in range(3, chips):
        line_step(0, step)
    small_group(0, r.tiles.at[pl.ds(0, devices - 1), 0])
    for peer in plane:
        push(r.tiles.at[:, s], r.tiles.at[:, s], r.small_s.at[0, 1], r.small_r.at[0, 1], peer)
    prepare_masks()
    rows_step(1)
    plane_step(0)
    for step in range(2, chips):
        rows_step(step)
    spread_plane(2, z)
    for step in range(1, chips):
        line_step(2, step)
    own_x.wait()
    own_cot.wait()
    relay_step(0)
    small_plane(0, r.tiles.at[:, pl.ds(0, SECTIONS - 1)])
    for slot in range(4):
        arrived(whole_a, r.gs_r.at[slot])
    attention(0)
    normalize(0)
    expand(1)
    arrived(whole_b, r.gs_r.at[4])
    contract(1)
    normalize(1)
    plane_step(2)
    attention(2)
    normalize(2)
    expand(3)
    gather_sends(0)
    for slot in range(5):
        at_end(None, whole_a if slot < 4 else whole_b, r.gs_s.at[slot])
    all_sent()
    relay_step(2)
    arrived(whole_b, r.gs_r.at[5])
    contract(3)
    normalize(3)

    r.sum[...] = jnp.zeros((8, LANES), WIDE)
    back_normalize(3)
    back_hidden(3)
    back_expand_end(3)
    give_rows(3)
    grad_down(1)
    to_plane("B1")
    back_normalize(2)
    back_output(2)
    grad_up(3)
    to_plane("F3")
    back_heads(2, 0, 2)
    grad_output(2)
    to_plane("O2")
    back_heads(2, 2, 2)
    back_packed(2)
    give_rows(2)
    back_packed_end(2)
    back_normalize(1)
    through_plane("B1")
    grad_packed(2)
    to_plane("K2")
    back_hidden(1)
    give_rows(1)
    through_plane("F3")
    back_expand_end(1)
    back_normalize(0)
    small_out(1, r.ng.at[d])
    through_plane("O2")
    grad_down(0)
    to_plane("B0")
    back_output(0)
    give_rows(0)
    to_line("B1")
    grad_up(1)
    to_plane("F1")
    back_heads(0, 0, 2)
    grad_output(0)
    to_plane("O0")
    through_plane("K2")
    back_heads(0, 2, 2)
    back_packed(0)
    to_line("F3")
    to_line("O2")
    through_plane("B0")
    grad_packed(0)
    to_plane("K0")
    to_owner("B1")
    to_line("K2")
    through_plane("F1")
    through_plane("O0")
    back_packed_end(0)
    to_owner("F3")
    to_owner("O2")
    to_line("B0")
    to_owner("K2")
    to_line("F1")
    to_line("O0")
    gather_sends(2)
    at_end(None, whole_b, r.gs_s.at[5])
    all_sent()
    through_plane("K0")
    to_owner("B0")
    to_owner("F1")
    to_owner("O0")
    small_group(1, r.ng.at[pl.ds(0, devices - 1)])
    r.ns[s] = functools.reduce(lambda left, right: left + right, [r.ng[index] for index in range(devices)])
    small_plane_out(1, r.ns.at[s])
    for name in ("F3", "O2", "K2", "F1"):
        collect(name)
    to_line("K0")
    collect("O0")
    for layer in range(2):
        done = buffers("B%d" % layer).done
        r.grad_b[layer] = done[...].reshape(cols_b, rows_b).T
    small_plane(1, r.ns.at[pl.ds(0, SECTIONS - 1)])
    grads = functools.reduce(lambda left, right: left + right, [r.ns[index] for index in range(SECTIONS)])
    norm_square = jnp.sum(jnp.sum(grads * grads, 0, keepdims=True), 1, keepdims=True)
    chosen = jnp.zeros((2, width), WIDE)
    for layer in range(4):
        chosen = jnp.where(s == layer, grads[2 * layer : 2 * layer + 2, :], chosen)
    for chip in range(chips):
        pair_of = chosen[:, chip * LANES : (chip + 1) * LANES]
        r.grad_n[...] = jnp.where(
            z == chip, jnp.where(c == 0, pair_of[:, :rows_a], pair_of[:, rows_a:]), r.grad_n[...]
        )
    to_owner("K0")

    r.sq[d] = r.sum[...]
    small_out(2, r.sq.at[d])
    collect("K0")
    small_group(2, r.sq.at[pl.ds(0, devices - 1)])
    r.sqs[s] = functools.reduce(lambda left, right: left + right, [r.sq[index] for index in range(devices)])
    small_plane_out(2, r.sqs.at[s])
    all_sent()
    small_plane(2, r.sqs.at[pl.ds(0, SECTIONS - 1)])
    squares = functools.reduce(lambda left, right: left + right, [r.sqs[index] for index in range(SECTIONS)])
    r.square[...] = squares + norm_square


def step_call(tokens, cotangent, lengths, mat_a, mat_b, norms):
    rows_a, hidden = mat_a.shape[1:]
    rows_b, cols_b = mat_b.shape[1:]
    width = tokens.shape[1]
    length = tokens.shape[0] // lengths.shape[0]
    chips = width // rows_a // 2
    scratch = kernel_scratch(chips, rows_a, rows_b, cols_b, length, width, hidden)
    shapes = []
    for _, shape, kind in scratch:
        shapes.append(pltpu.SemaphoreType.DMA(shape) if kind is None else pltpu.VMEM(shape, kind))
    anywhere, vmem = pl.BlockSpec(memory_space=pl.ANY), pl.BlockSpec(memory_space=pltpu.VMEM)
    return pl.pallas_call(
        functools.partial(step_kernel, INPUTS + OUTPUTS + tuple(name for name, _, _ in scratch)),
        out_shape=(
            jax.ShapeDtypeStruct((rows_a, hidden), WIDE),
            jax.ShapeDtypeStruct(mat_b.shape, WIDE),
            jax.ShapeDtypeStruct((2, rows_a), WIDE),
            jax.ShapeDtypeStruct((8, LANES), WIDE),
            jax.ShapeDtypeStruct((length, width), LOW),
            jax.ShapeDtypeStruct((length, width), WIDE),
        ),
        in_specs=[anywhere, anywhere, pl.BlockSpec(memory_space=pltpu.SMEM), vmem, vmem, vmem],
        out_specs=[vmem] * len(OUTPUTS),
        scratch_shapes=shapes,
        compiler_params=pltpu.CompilerParams(
            collective_id=0, has_side_effects=True, vmem_limit_bytes=KERNEL_VMEM
        ),
    )(tokens, cotangent, lengths, mat_a, mat_b, norms)


def update_kernel(*refs):
    square, output, input_grad = (ref[...] for ref in refs[:3])
    grad_norm = jnp.sqrt(square[0:1, 0:1])
    factor = CLIP_NORM / jnp.maximum(grad_norm, CLIP_NORM)
    inputs, outputs = refs[3:15], refs[15:]
    outputs[0][...] = grad_norm
    outputs[1][0] = output
    outputs[2][0] = input_grad
    for group, (rate, decay) in enumerate(
        ((MATRIX_RATE, MATRIX_DECAY), (MATRIX_RATE, MATRIX_DECAY), (NORM_RATE, 0.0))
    ):
        grad, weight, one, two = inputs[4 * group : 4 * group + 4]
        clip = grad[...].reshape(weight.shape) * factor
        moment, square_new, master = adam_update(weight[...], one[...], two[...], clip, rate, decay)
        for ref, value in zip(
            outputs[3 + 5 * group : 8 + 5 * group], (clip, moment, square_new, master, master.astype(LOW))
        ):
            ref[...] = value


def kernel_body(
    tokens, cotangent, lengths, mat_a, mat_b, norms, first_a, second_a, first_b, second_b, first_n, second_n
):
    norms, first_n, second_n = (jnp.swapaxes(value, 1, 2) for value in (norms, first_n, second_n))
    grad_a, grad_b, grad_n, square, output, input_grad = step_call(
        tokens, cotangent, lengths, mat_a, mat_b, norms
    )
    steps = 4

    def cut(value, dim):
        shape = tuple(size // steps if at == dim else size for at, size in enumerate(value.shape))
        return pl.BlockSpec(shape, lambda step: tuple(step if at == dim else 0 for at in range(len(shape))))

    def whole(value):
        return pl.BlockSpec(value.shape, lambda step: (0,) * len(value.shape))

    def like(value, kind=WIDE):
        return jax.ShapeDtypeStruct(value.shape, kind)

    args = (square, output, input_grad, grad_a, mat_a, first_a, second_a, grad_b, mat_b, first_b, second_b)
    specs = [whole(square), cut(output, 0), cut(input_grad, 0)]
    specs += [cut(grad_a, 0)] + [cut(mat_a, 1)] * 3 + [cut(grad_b, 1)] * 4
    args += (grad_n, norms, first_n, second_n)
    specs += [whole(grad_n)] + [whole(norms)] * 3
    shapes = [jax.ShapeDtypeStruct((1, 1), WIDE), like(output[None], LOW), like(input_grad[None])]
    out_specs = [whole(shapes[0]), cut(shapes[1], 1), cut(shapes[2], 1)]
    for value, spec in ((mat_a, cut(mat_a, 1)), (mat_b, cut(mat_b, 1)), (norms, whole(norms))):
        shapes += [like(value)] * 4 + [like(value, LOW)]
        out_specs += [spec] * 5
    results = pl.pallas_call(
        update_kernel,
        grid=(steps,),
        out_shape=shapes,
        in_specs=specs,
        out_specs=out_specs,
        compiler_params=pltpu.CompilerParams(vmem_limit_bytes=KERNEL_VMEM),
    )(*args)
    results = [results[0][0, 0], *results[1:]]
    results[-5:] = [jnp.swapaxes(value, 1, 2) for value in results[-5:]]
    return tuple(results)


def chosen_body(*args):
    rows_a = args[3].shape[1]
    groups = lax.axis_size("dp")
    by_kernel = rows_a % 32 == 0 and 2 * rows_a == LANES and groups * rows_a == args[0].shape[1]
    return (kernel_body if by_kernel else body)(*args)


def solution(mesh):
    placed = (
        P("dp", None),
        P("dp", None),
        P("dp", None),
        P("section", "dp", None),
        P(None, "dp", "section"),
        P("section", "dp", None),
        P("section", "dp", None),
        P("section", "dp", None),
        P(None, "dp", "section"),
        P(None, "dp", "section"),
        P("section", "dp", None),
        P("section", "dp", None),
    )
    return jax.shard_map(
        chosen_body,
        mesh=mesh,
        in_specs=placed,
        out_specs=(
            P(),
            P("section", "dp", None),
            P("section", "dp", None),
            P("section", "dp", None),
            P("section", "dp", None),
            P("section", "dp", None),
            P("section", "dp", None),
            P("section", "dp", None),
            P(None, "dp", "section"),
            P(None, "dp", "section"),
            P(None, "dp", "section"),
            P(None, "dp", "section"),
            P(None, "dp", "section"),
            P("section", "dp", None),
            P("section", "dp", None),
            P("section", "dp", None),
            P("section", "dp", None),
            P("section", "dp", None),
        ),
        check_vma=False,
    )
```

```python
import functools
import types

import jax
import jax.numpy as jnp
from jax import lax
from jax.experimental import pallas as pl
from jax.experimental.pallas import tpu as pltpu
from jax.sharding import PartitionSpec as P

HEADS = 8
STEP = 5


EPSILON = 1e-05
NEGATIVE = -1e30
CLIP_NORM = 1.0
BETA_ONE = 0.5
BETA_TWO = 0.5
ADAM_EPSILON = 1e-08
MATRIX_RATE = 0.05
NORM_RATE = 0.5
MATRIX_DECAY = 0.01


def norm_stats(value):
    centre = value - jnp.mean(value, -1, keepdims=True)
    inverse = lax.rsqrt(jnp.mean(centre * centre, -1, keepdims=True) + EPSILON)
    return (centre * inverse, inverse)


def norm_back(normal, inverse, upstream):
    return inverse * (
        upstream
        - jnp.mean(upstream, -1, keepdims=True)
        - normal * jnp.mean(upstream * normal, -1, keepdims=True)
    )


def adam_update(weight, moment_one, moment_two, gradient, step_rate, decay_rate):
    first_new = BETA_ONE * moment_one + (1.0 - BETA_ONE) * gradient
    second_new = BETA_TWO * moment_two + (1.0 - BETA_TWO) * gradient * gradient
    first_hat = first_new / (1.0 - BETA_ONE**STEP)
    second_hat = second_new / (1.0 - BETA_TWO**STEP)
    weight_new = weight - step_rate * (
        first_hat / (jnp.sqrt(second_hat) + ADAM_EPSILON) + decay_rate * weight
    )
    return (first_new, second_new, weight_new)


def segments_of(lengths_row, length):
    ends = jnp.cumsum(lengths_row, dtype=jnp.int32)
    places = jnp.arange(length, dtype=jnp.int32)
    segment = jnp.sum((ends[None, :] <= places[:, None]).astype(jnp.int32), axis=1, dtype=jnp.int32)
    live = (places < ends[-1]).astype(jnp.float32)
    return segment, live


def matmul(left, right, dims):
    return lax.dot_general(left, right, (dims, ((), ())), preferred_element_type=jnp.float32)


NN = ((1,), (0,))
NT = ((1,), (1,))
TN = ((0,), (0,))


def attention_forward(stream, weight, mask):
    length, width = stream.shape
    size = width // HEADS
    packed = matmul(stream, weight[:, : 3 * width], NN).astype(jnp.bfloat16)
    heads = packed.reshape(length, 3, HEADS, size)
    scores = jnp.einsum("qhd,khd->hqk", heads[:, 0], heads[:, 1], preferred_element_type=jnp.float32)
    scores = jnp.where(mask[None], scores * size**-0.5, NEGATIVE)
    weights = jnp.exp(scores - jnp.max(scores, -1, keepdims=True))
    probs = weights / jnp.sum(weights, -1, keepdims=True)
    mixed = jnp.einsum("hqk,khd->qhd", probs.astype(jnp.bfloat16), heads[:, 2], preferred_element_type=jnp.float32)
    mixed = mixed.reshape(length, width).astype(jnp.bfloat16)
    branch = matmul(mixed, weight[:, 3 * width :], NN)
    return branch, (heads, probs, mixed)


def attention_backward(stream, weight, kept, grad_low):
    heads, probs, mixed = kept
    length, width = stream.shape
    size = width // HEADS
    grad_out = matmul(mixed, grad_low, TN)
    grad_mixed = matmul(grad_low, weight[:, 3 * width :], NT).astype(jnp.bfloat16)
    grad_mixed = grad_mixed.reshape(length, HEADS, size)
    grad_probs = jnp.einsum("qhd,khd->hqk", grad_mixed, heads[:, 2], preferred_element_type=jnp.float32)
    centre = jnp.sum(probs * grad_probs, -1, keepdims=True)
    grad_scores = (probs * (grad_probs - centre)).astype(jnp.bfloat16)
    low = probs.astype(jnp.bfloat16)
    scale = size**-0.5
    grad_q = jnp.einsum("hqk,khd->qhd", grad_scores, heads[:, 1], preferred_element_type=jnp.float32) * scale
    grad_k = jnp.einsum("hqk,qhd->khd", grad_scores, heads[:, 0], preferred_element_type=jnp.float32) * scale
    grad_v = jnp.einsum("hqk,qhd->khd", low, grad_mixed, preferred_element_type=jnp.float32)
    packed = jnp.concatenate([grad_q, grad_k, grad_v], axis=1).reshape(length, 3 * width)
    packed = packed.astype(jnp.bfloat16)
    grad_in = matmul(stream, packed, TN)
    grad_inputs = matmul(packed, weight[:, : 3 * width], NT)
    return grad_inputs, jnp.concatenate([grad_in, grad_out], axis=1)


def feed_forward(stream, weight, down):
    pre = matmul(stream, weight, NN)
    active = jax.nn.gelu(pre, approximate=True).astype(jnp.bfloat16)
    return matmul(active, down, NN), (pre, active)


def feed_backward(stream, weight, down, kept, grad_low):
    pre, active = kept
    grad_down = matmul(active, grad_low, TN)
    grad_active = matmul(grad_low, down, NT)
    pull = jax.vjp(lambda value: jax.nn.gelu(value, approximate=True), pre)[1]
    grad_pre = pull(grad_active)[0].astype(jnp.bfloat16)
    grad_up = matmul(stream, grad_pre, TN)
    return matmul(grad_pre, weight, NT), grad_up, grad_down


def micro_step(rows, pull, segment, mats, downs, gains, biases):
    low = jnp.bfloat16
    mask = segment[:, None] == segment[None, :]
    stream, dual = rows, jnp.zeros_like(rows)
    saved = []
    for sub in range(4):
        if sub % 2 == 0:
            branch, kept = attention_forward(stream, mats[sub], mask)
        else:
            branch, kept = feed_forward(stream, mats[sub], downs[sub // 2])
        normal, inverse = norm_stats(stream.astype(jnp.float32) + branch)
        out = normal * gains[sub] + biases[sub]
        total = dual.astype(jnp.float32) + branch
        saved.append((stream, kept, normal, inverse))
        if sub < 3:
            stream, dual = out.astype(low), total.astype(low)
    dual_normal, dual_inverse = norm_stats(total)
    output = (out + dual_normal).astype(low)
    grad_out, grad_dual = pull, norm_back(dual_normal, dual_inverse, pull)
    grads_a, grads_b, grads_n = [None] * 4, [None] * 2, [None] * 4
    for sub in (3, 2, 1, 0):
        stream, kept, normal, inverse = saved[sub]
        grads_n[sub] = jnp.stack([jnp.sum(grad_out * normal, 0), jnp.sum(grad_out, 0)], axis=1)
        summed = norm_back(normal, inverse, grad_out * gains[sub])
        branch_low = (summed + grad_dual).astype(low)
        if sub % 2 == 0:
            inner, grads_a[sub] = attention_backward(stream, mats[sub], kept, branch_low)
        else:
            inner, grads_a[sub], grads_b[sub // 2] = feed_backward(
                stream, mats[sub], downs[sub // 2], kept, branch_low
            )
        grad_in = summed + inner
        if sub > 0:
            grad_out = grad_in.astype(low).astype(jnp.float32)
            grad_dual = grad_dual.astype(low).astype(jnp.float32)
    return output, grad_in, jnp.stack(grads_a), jnp.stack(grads_b), jnp.stack(grads_n)


def finish_step(grad_norm, output, input_grad, *groups):
    factor = CLIP_NORM / jnp.maximum(grad_norm, CLIP_NORM)
    results = [grad_norm, output[None], input_grad[None]]
    for weight, one, two, grad, rate, decay in groups:
        clip = grad * factor
        moment, square_new, master = adam_update(weight, one, two, clip, rate, decay)
        results += [clip, moment, square_new, master, master.astype(jnp.bfloat16)]
    return tuple(results)


def body(
    tokens, cotangent, lengths, mat_a, mat_b, norms, first_a, second_a, first_b, second_b, first_n, second_n
):
    low = jnp.bfloat16
    own = lax.axis_index("section")
    length = tokens.shape[0] // lengths.shape[0]
    rows = lax.dynamic_slice_in_dim(tokens, own * length, length, 0)
    segment, live = segments_of(lax.dynamic_index_in_dim(lengths, own, 0, keepdims=False), length)
    pull = lax.dynamic_slice_in_dim(cotangent, own * length, length, 0).astype(jnp.float32) * live[:, None]

    def gathered(value):
        return lax.all_gather(lax.all_gather(value, "dp", axis=1, tiled=True), "section", axis=0, tiled=True)

    mats = gathered(mat_a.astype(low))
    scales = gathered(norms.astype(low)).astype(jnp.float32)
    downs = lax.all_gather(mat_b.astype(low), "section", axis=2, tiled=True)
    downs = lax.all_gather(downs, "dp", axis=1, tiled=True)
    output, input_grad, part_a, part_b, part_n = micro_step(
        rows, pull, segment, mats, downs, scales[:, :, 0], scales[:, :, 1]
    )

    def scattered(value, section_dim):
        value = lax.psum_scatter(value, "section", scatter_dimension=section_dim, tiled=True)
        return lax.psum_scatter(value, "dp", scatter_dimension=1, tiled=True).astype(jnp.float32)

    grad_a = scattered(part_a.astype(low), 0)
    grad_b = scattered(part_b.astype(low), 2)
    grad_n = scattered(part_n, 0)
    square = jnp.sum(grad_a * grad_a) + jnp.sum(grad_b * grad_b) + jnp.sum(grad_n * grad_n)
    grad_norm = jnp.sqrt(lax.psum(square, ("section", "dp")))
    return finish_step(
        grad_norm, output, input_grad,
        (mat_a, first_a, second_a, grad_a, MATRIX_RATE, MATRIX_DECAY),
        (mat_b, first_b, second_b, grad_b, MATRIX_RATE, MATRIX_DECAY),
        (norms, first_n, second_n, grad_n, NORM_RATE, 0.0),
    )


LOW = jnp.bfloat16
WIDE = jnp.float32
MESH = pl.DeviceIdType.MESH
SECTIONS = 4
LANES = 128
BLOCK = 64
KERNEL_VMEM = 64 * 1024 * 1024 - 256 * 1024


def gradient_items(rows_a, rows_b, cols_b, width, hidden):
    part = rows_a // SECTIONS
    return (
        ("B1", 3, cols_b // 2, rows_b),
        ("F3", 3, part, hidden // 2),
        ("O2", 2, part, width // 2),
        ("K2", 2, part, 3 * width // 2),
        ("B0", 1, cols_b // 2, rows_b),
        ("F1", 1, part, hidden // 2),
        ("O0", 0, part, width // 2),
        ("K0", 0, part, 3 * width // 2),
    )


LINE_FIRST = ("K2",)


def item_scratch(name, chips, rows, columns):
    piece = (rows, columns)
    if name in LINE_FIRST:
        return (
            ("own" + name, (chips, SECTIONS, 2) + piece, LOW),
            ("farx" + name, piece, LOW),
            ("fary" + name, piece, LOW),
            ("nearx" + name, (2,) + piece, LOW),
            ("neary" + name, (2,) + piece, LOW),
            ("line" + name, (chips, SECTIONS, 2) + piece, LOW),
            ("done" + name, (SECTIONS, 2) + piece, LOW),
        )
    return (
        ("own" + name, (chips, SECTIONS, 2) + piece, LOW),
        ("farx" + name, (chips,) + piece, LOW),
        ("fary" + name, (chips,) + piece, LOW),
        ("nearx" + name, (2, chips) + piece, LOW),
        ("neary" + name, (2, chips) + piece, LOW),
        ("line" + name, (chips, 2) + piece, LOW),
        ("done" + name, (2,) + piece if name[0] == "B" else (SECTIONS, 2) + piece, WIDE if name[0] == "B" else LOW),
    )


def kernel_scratch(chips, rows_a, rows_b, cols_b, length, width, hidden):
    devices = 2 * chips
    items = gradient_items(rows_a, rows_b, cols_b, width, hidden)
    count = len(items)
    received = sum((item_scratch(name, chips, rows, columns) for name, _, rows, columns in items), ())
    return received + (
        ("fac_s", (32,), None),
        ("fac_r", (32,), None),
        ("px_s", (count, 3), None),
        ("px_r", (count, 3), None),
        ("py_s", (count, 3), None),
        ("py_r", (count, 3), None),
        ("line_s", (count, chips), None),
        ("line_r", (count, chips), None),
        ("done_s", (count,), None),
        ("done_r", (count, SECTIONS), None),
        ("wa", (4, width, hidden), LOW),
        ("wb", (2, hidden, width), LOW),
        ("tiles", (devices, SECTIONS, 8, LANES), WIDE),
        ("x", (4, length, width), LOW),
        ("xt", (4, chips, 2, rows_a, length), LOW),
        ("xtc", (4, chips, rows_a, 2 * length), LOW),
        ("y", (length, width), LOW),
        ("cot", (length, width), LOW),
        ("bias", (length, length), WIDE),
        ("live", (length, 1), WIDE),
        ("f", (length, width), WIDE),
        ("n", (4, length, width), WIDE),
        ("inv", (4, length, 1), WIDE),
        ("q", (2, length, width), LOW),
        ("k", (2, length, width), LOW),
        ("v", (2, length, width), LOW),
        ("kt", (2, width, length), LOW),
        ("vt", (2, width, length), LOW),
        ("ot", (2, chips, 2, rows_a, length), LOW),
        ("otc", (2, chips, rows_a, 2 * length), LOW),
        ("pt", (2, HEADS, length, length), LOW),
        ("g", (2, length, hidden), LOW),
        ("gc", (2, chips, 2 * length, rows_b), LOW),
        ("slope", (2, length, hidden), LOW),
        ("gx", (length, width), WIDE),
        ("gy", (length, width), WIDE),
        ("df", (2, 2 * length, width), LOW),
        ("dft", (2, width, 2 * length), LOW),
        ("dm", (length, width), LOW),
        ("dqt", (width, length), LOW),
        ("dh", (2, 2 * length, hidden), LOW),
        ("dp", (2, 2 * length, 3 * width), LOW),
        ("ng", (devices, 8, width), WIDE),
        ("ns", (SECTIONS, 8, width), WIDE),
        ("sq", (devices, 8, LANES), WIDE),
        ("sqs", (SECTIONS, 8, LANES), WIDE),
        ("sum", (8, LANES), WIDE),
        ("in_s", (2,), None),
        ("gz_s", (3, 2, chips, 2), None),
        ("gz_r", (3, chips, 2), None),
        ("gx_s", (3, chips, 2), None),
        ("gx_r", (3, chips, 2), None),
        ("gy_s", (3, chips, 2), None),
        ("gy_r", (3, chips, 2), None),
        ("gxr_s", (3, chips), None),
        ("gxr_r", (3, chips), None),
        ("gyr_s", (3, chips), None),
        ("gyr_r", (3, chips), None),
        ("gs_s", (6,), None),
        ("gs_r", (6,), None),
        ("small_s", (3, 2), None),
        ("small_r", (3, 2), None),
    )


INPUTS = ("tokens", "cotangent", "lengths", "mat_a", "mat_b", "norms")
OUTPUTS = ("grad_a", "grad_b", "grad_n", "square", "output", "input_grad")


def step_kernel(names, *refs):
    r = types.SimpleNamespace(**dict(zip(names, refs)))
    width, hidden = r.wa.shape[1:]
    length = r.x.shape[1]
    rows_a, (rows_b, cols_b) = r.mat_a.shape[1], r.mat_b.shape[1:]
    devices = r.tiles.shape[0]
    chips = devices // 2
    half_a, half_b = rows_a // 2, cols_b // 2
    grad_items = gradient_items(rows_a, rows_b, cols_b, width, hidden)
    head = width // HEADS
    scale = head**-0.5

    s, d = lax.axis_index("section"), lax.axis_index("dp")
    z, c = lax.div(d, 2), lax.rem(d, 2)
    sx = s + 1 - 2 * lax.rem(s, 2)
    sy = lax.rem(s + 2, SECTIONS)
    sd = SECTIONS - 1 - s
    to_sibling = {"dp": d + 1 - 2 * c}
    to_up, to_down = {"dp": d + 2}, {"dp": d - 2}
    to_x, to_y = {"section": sx}, {"section": sy}
    below, above = z > 0, z < chips - 1
    group = [{"dp": lax.rem(d + step, devices)} for step in range(1, devices)]
    plane = [{"section": lax.rem(s + step, SECTIONS)} for step in range(1, SECTIONS)]
    finish = []

    def when(condition, work):
        if condition is None:
            work()
        else:
            pl.when(condition)(work)

    def push(source, target, send_sem, recv_sem, device):
        pltpu.make_async_remote_copy(
            src_ref=source,
            dst_ref=target,
            send_sem=send_sem,
            recv_sem=recv_sem,
            device_id=device,
            device_id_type=MESH,
        ).start()

    def arrived(target, sem):
        pltpu.make_async_remote_copy(
            src_ref=target, dst_ref=target, send_sem=sem, recv_sem=sem, device_id=to_x, device_id_type=MESH
        ).wait_recv()

    def sent(source, sem):
        pltpu.make_async_remote_copy(
            src_ref=source, dst_ref=source, send_sem=sem, recv_sem=sem, device_id=to_x, device_id_type=MESH
        ).wait_send()

    def at_end(condition, source, sem):
        finish.append((condition, source, sem))

    def aligned(start, size):
        return pl.ds(pl.multiple_of(start, size), size)

    own_x = pltpu.make_async_copy(r.tokens.at[aligned(s * length, length)], r.x.at[0], r.in_s.at[0])
    own_cot = pltpu.make_async_copy(r.cotangent.at[aligned(s * length, length)], r.cot, r.in_s.at[1])
    own_x.start()
    own_cot.start()
    barrier = pltpu.get_barrier_semaphore()
    for peer in group + plane:
        pl.semaphore_signal(barrier, inc=1, device_id=peer, device_id_type=MESH)
    r.wa[s, aligned(d * rows_a, rows_a), :] = r.mat_a[0].astype(LOW)
    for layer in range(2):
        r.wb[layer, aligned(d * rows_b, rows_b), aligned(s * cols_b, cols_b)] = r.mat_b[layer].astype(LOW)
    norms = r.norms[0].astype(LOW).astype(WIDE)
    nothing = jnp.zeros((2, rows_a), WIDE)
    even = jnp.concatenate([norms, nothing], axis=1)
    odd = jnp.concatenate([nothing, norms], axis=1)
    r.tiles[d, s, 0:2, :] = jnp.where(c == 0, even, odd)
    r.tiles[d, s, 2:8, :] = jnp.zeros((6, LANES), WIDE)
    pl.semaphore_wait(barrier, len(group) + len(plane))

    def small_out(which, source):
        for peer in group:
            push(source, source, r.small_s.at[which, 0], r.small_r.at[which, 0], peer)

    def small_group(which, like):
        arrived(like, r.small_r.at[which, 0])
        sent(like, r.small_s.at[which, 0])

    def small_plane_out(which, source):
        for peer in plane:
            push(source, source, r.small_s.at[which, 1], r.small_r.at[which, 1], peer)

    def small_plane(which, like):
        arrived(like, r.small_r.at[which, 1])
        sent(like, r.small_s.at[which, 1])

    def block_a(section, chip, half):
        return r.wa.at[section, aligned((2 * chip + c) * rows_a + half * half_a, half_a), :]

    def block_b(layer):
        part = rows_b // 2

        def block(section, chip, half):
            return r.wb.at[
                layer,
                aligned((2 * chip + c) * rows_b + half * part, part),
                aligned(section * cols_b, cols_b),
            ]

        return block

    items = (block_a, block_b(0), block_b(1))

    def to_the_sibling(item, section, chip, half):
        block = items[item](section, chip, half)
        slot = section if item == 0 else 3 + item
        push(block, block, r.gs_s.at[slot], r.gs_r.at[slot], to_sibling)

    def spread_plane(item, chip):
        for half in range(2):
            block = items[item](s, chip, half)
            push(block, block, r.gx_s.at[item, chip, half], r.gx_r.at[item, chip, half], to_x)
            push(block, block, r.gy_s.at[item, chip, half], r.gy_r.at[item, chip, half], to_y)
            to_the_sibling(item, s, chip, half)

    def up(item, chip, half):
        block = items[item](s, chip, half)
        push(block, block, r.gz_s.at[item, 0, chip, half], r.gz_r.at[item, chip, half], to_up)

    def down(item, chip, half):
        block = items[item](s, chip, half)
        push(block, block, r.gz_s.at[item, 1, chip, half], r.gz_r.at[item, chip, half], to_down)

    def start_line(item):
        for half in range(2):
            when(above, lambda: up(item, z, half))
            when(below, lambda: down(item, z, half))

    def line_step(item, step):
        def from_below():
            for half in range(2):
                arrived(items[item](s, z - step, half), r.gz_r.at[item, z - step, half])
                when(above, lambda: up(item, z - step, half))
            spread_plane(item, z - step)

        def from_above():
            for half in range(2):
                arrived(items[item](s, z + step, half), r.gz_r.at[item, z + step, half])
                when(below, lambda: down(item, z + step, half))
            spread_plane(item, z + step)

        when(z >= step, from_below)
        when(z + step < chips, from_above)

    def plane_step(item):
        for chip in range(chips):
            for half in range(2):
                arrived(items[item](sx, chip, half), r.gx_r.at[item, chip, half])
                if half == 1:
                    block = items[item](sx, chip, half)
                    push(block, block, r.gyr_s.at[item, chip], r.gyr_r.at[item, chip], to_y)
                to_the_sibling(item, sx, chip, half)
                arrived(items[item](sy, chip, half), r.gy_r.at[item, chip, half])
                if half == 0:
                    block = items[item](sy, chip, half)
                    push(block, block, r.gxr_s.at[item, chip], r.gxr_r.at[item, chip], to_x)
                to_the_sibling(item, sy, chip, half)

    def relay_step(item):
        for chip in range(chips):
            arrived(items[item](sd, chip, 0), r.gxr_r.at[item, chip])
            to_the_sibling(item, sd, chip, 0)
            arrived(items[item](sd, chip, 1), r.gyr_r.at[item, chip])
            to_the_sibling(item, sd, chip, 1)

    whole_a = r.wa.at[0, pl.ds(0, chips * rows_a)]
    whole_b = r.wb.at[0, pl.ds(0, chips * rows_b)]
    def gather_sends(item):
        for chip in range(chips):
            for half in range(2):
                block = items[item](0, chip, half)
                at_end(None, block, r.gx_s.at[item, chip, half])
                at_end(None, block, r.gy_s.at[item, chip, half])
                at_end(above & (z >= chip), block, r.gz_s.at[item, 0, chip, half])
                at_end(below & (z <= chip), block, r.gz_s.at[item, 1, chip, half])
            block = items[item](0, chip, 0)
            at_end(None, block, r.gxr_s.at[item, chip])
            at_end(None, block, r.gyr_s.at[item, chip])

    def row_block(chip, half):
        part = rows_b // 2
        return r.wb.at[0, aligned((2 * chip + c) * rows_b + half * part, part), :]

    def rows_to_sibling(chip, half):
        push(row_block(chip, half), row_block(chip, half), r.gs_s.at[4], r.gs_r.at[4], to_sibling)

    def rows_up(chip, half):
        rows = row_block(chip, half)
        push(rows, rows, r.gz_s.at[1, 0, chip, half], r.gz_r.at[1, chip, half], to_up)

    def rows_down(chip, half):
        rows = row_block(chip, half)
        push(rows, rows, r.gz_s.at[1, 1, chip, half], r.gz_r.at[1, chip, half], to_down)

    def rows_plane():
        for half in range(2):
            block = items[1](s, z, half)
            push(block, block, r.gx_s.at[1, 0, half], r.gx_r.at[1, 0, half], to_x)
            push(block, block, r.gy_s.at[1, 0, half], r.gy_r.at[1, 0, half], to_y)
            at_end(None, block, r.gx_s.at[1, 0, half])
            at_end(None, block, r.gy_s.at[1, 0, half])

    def rows_relay():
        for half in range(2):
            arrived(items[1](sx, z, half), r.gx_r.at[1, 0, half])
            arrived(items[1](sy, z, half), r.gy_r.at[1, 0, half])
        block = items[1](sx, z, 1)
        push(block, block, r.gyr_s.at[1, 0], r.gyr_r.at[1, 0], to_y)
        block = items[1](sy, z, 0)
        push(block, block, r.gxr_s.at[1, 0], r.gxr_r.at[1, 0], to_x)
        at_end(None, block, r.gyr_s.at[1, 0])
        at_end(None, block, r.gxr_s.at[1, 0])

    def rows_line():
        for half, sem in ((0, r.gxr_r), (1, r.gyr_r)):
            arrived(items[1](sd, z, half), sem.at[1, 0])
            when(above, lambda: rows_up(z, half))
            when(below, lambda: rows_down(z, half))
            rows_to_sibling(z, half)
        for chip in range(chips):
            for half in range(2):
                at_end(above & (z >= chip), row_block(chip, half), r.gz_s.at[1, 0, chip, half])
                at_end(below & (z <= chip), row_block(chip, half), r.gz_s.at[1, 1, chip, half])

    def rows_step(step):
        def from_below():
            for half in range(2):
                arrived(row_block(z - step, half), r.gz_r.at[1, z - step, half])
                when(above, lambda: rows_up(z - step, half))
                rows_to_sibling(z - step, half)

        def from_above():
            for half in range(2):
                arrived(row_block(z + step, half), r.gz_r.at[1, z + step, half])
                when(below, lambda: rows_down(z + step, half))
                rows_to_sibling(z + step, half)

        when(z >= step, from_below)
        when(z + step < chips, from_above)

    mine, other = pl.ds(0, length), pl.ds(length, length)

    def give(slot, source, target):
        push(source, target, r.fac_s.at[slot], r.fac_r.at[slot], to_sibling)
        at_end(None, target, r.fac_s.at[slot])

    def taken(slot, target):
        arrived(target, r.fac_r.at[slot])

    def give_rows(layer):
        r.xt[layer] = r.x[layer].T.reshape(chips, 2, rows_a, length)
        r.xtc[layer, :, :, 0:length] = r.xt[layer, :, c]
        give(layer, r.xt.at[layer, :, 1 - c], r.xtc.at[layer, :, :, other])

    def product(left, right, dims):
        return lax.dot_general(left, right, (dims, ((), ())), preferred_element_type=WIDE)

    def loop(count, work):
        def one(index, carry):
            work(index)
            return carry

        lax.fori_loop(0, count, one, 0)

    def gain_row(layer, kind):
        parts = [
            r.tiles[2 * chip, layer, kind : kind + 1, :] + r.tiles[2 * chip + 1, layer, kind : kind + 1, :]
            for chip in range(chips)
        ]
        return jnp.concatenate(parts, axis=1)

    def stats(value):
        centre = value - jnp.mean(value, -1, keepdims=True)
        inverse = lax.rsqrt(jnp.mean(centre * centre, -1, keepdims=True) + EPSILON)
        return centre * inverse, inverse

    lane = lax.broadcasted_iota(jnp.int32, (1, 2 * head), 1)
    first_half = (lane < head).astype(WIDE)
    half_masks = (first_half.astype(LOW), (1.0 - first_half).astype(LOW))

    def prepare_masks():
        ends, total = [], jnp.int32(0)
        for slot in range(r.lengths.shape[1]):
            total = total + r.lengths[s, slot]
            ends.append(total)
        down_places = lax.broadcasted_iota(jnp.int32, (length, 1), 0)
        across_places = lax.broadcasted_iota(jnp.int32, (1, length), 1)
        down_segment = jnp.zeros((length, 1), jnp.int32)
        across_segment = jnp.zeros((1, length), jnp.int32)
        for end in ends:
            down_segment = down_segment + (end <= down_places).astype(jnp.int32)
            across_segment = across_segment + (end <= across_places).astype(jnp.int32)
        r.bias[...] = jnp.where(down_segment == across_segment, 0.0, NEGATIVE)
        r.live[...] = (down_places < total).astype(WIDE)

    def attention(layer):
        at = layer // 2
        rows = r.x[layer]
        r.q[at] = product(rows, r.wa[layer, :, 0:width], NN).astype(LOW) * jnp.asarray(scale, LOW)
        keys = product(rows, r.wa[layer, :, width : 2 * width], NN).astype(LOW)
        r.k[at] = keys
        values = product(rows, r.wa[layer, :, 2 * width : 3 * width], NN).astype(LOW)
        r.v[at] = values
        r.vt[at] = values.T

        def pair(index):
            lanes = aligned(index * 2 * head, 2 * head)
            for which in range(2):
                scores = product(r.k[at, :, lanes], r.q[at, :, lanes] * half_masks[which], NT) + r.bias[...]
                weights = jnp.exp(scores - jnp.max(scores, 0, keepdims=True))
                probs = (weights * (1.0 / jnp.sum(weights, 0, keepdims=True))).astype(LOW)
                r.pt[at, 2 * index + which] = probs
                place = aligned((2 * index + which) * head, head)
                r.ot[at, index, which] = product(r.vt[at, place, :], probs, NN).astype(LOW)

        def pairs(step):
            pair(2 * step)
            pair(2 * step + 1)

        loop(HEADS // 4, pairs)
        r.otc[at, :, :, 0:length] = r.ot[at, :, c]
        give(4 + at, r.ot.at[at, :, 1 - c], r.otc.at[at, :, :, other])
        r.f[...] = product(r.ot[at].reshape(width, length).T, r.wa[layer, :, 3 * width :], NN)

    def expand(layer):
        at = layer // 2
        def columns(index):
            place = pl.ds(index * width, width)
            pre = product(r.x[layer], r.wa[layer, :, place], NN)
            squared = pre * pre
            slope = 0.7978845608 * (1.0 + 3 * 0.044715 * squared)
            bent = jnp.tanh(0.7978845608 * pre * (1.0 + 0.044715 * squared))
            r.g[at, :, place] = (0.5 * pre * (1.0 + bent)).astype(LOW)
            r.slope[at, :, place] = (0.5 * (1.0 + bent) + 0.5 * pre * (1.0 - bent * bent) * slope).astype(LOW)
            block = aligned((2 * index + c) * rows_b, rows_b)
            r.gc[at, index, 0:length, :] = r.g[at, :, block]
            block = aligned((2 * index + 1 - c) * rows_b, rows_b)
            give(6 + chips * at + index, r.g.at[at, :, block], r.gc.at[at, index, other, :])

        for index in range(hidden // width):
            columns(index)

    def contract(layer):
        r.f[...] = product(r.g[layer // 2], r.wb[layer // 2], NN)

    def by_rows(work):
        for index in range(length // BLOCK):
            work(pl.ds(index * BLOCK, BLOCK))

    def normalize(layer):
        gain, offset = gain_row(layer, 0), gain_row(layer, 1)

        def some(rows):
            branch = r.f[rows, :]
            normal, inverse = stats(r.x[layer, rows, :].astype(WIDE) + branch)
            r.n[layer, rows, :] = normal
            r.inv[layer, rows, :] = inverse
            out = normal * gain + offset
            dual = branch if layer == 0 else r.y[rows, :].astype(WIDE) + branch
            if layer < 3:
                r.x[layer + 1, rows, :] = out.astype(LOW)
                r.y[rows, :] = dual.astype(LOW)
            else:
                dual_normal, dual_inverse = stats(dual)
                r.output[rows, :] = (out + dual_normal).astype(LOW)
                pull = r.cot[rows, :].astype(WIDE) * r.live[rows, :]
                r.gx[rows, :] = pull
                r.gy[rows, :] = norm_back(dual_normal, dual_inverse, pull)

        by_rows(some)

    def back_normalize(layer):
        gain = gain_row(layer, 0)

        def some(index, sums):
            rows = pl.ds(index * BLOCK, BLOCK)
            upstream = r.gx[rows, :]
            normal = r.n[layer, rows, :]
            summed = norm_back(normal, r.inv[layer, rows, :], upstream * gain)
            dual = r.gy[rows, :]
            r.gx[rows, :] = summed
            r.df[layer // 2, rows, :] = (summed + dual).astype(LOW)
            if layer == 3:
                r.gy[rows, :] = dual.astype(LOW).astype(WIDE)
            return (
                sums[0] + jnp.sum(upstream * normal, 0, keepdims=True),
                sums[1] + jnp.sum(upstream, 0, keepdims=True),
            )

        zero = jnp.zeros((1, width), WIDE)
        gains, offsets = zero, zero
        for index in range(length // BLOCK):
            gains, offsets = some(index, (gains, offsets))
        r.ng[d, 2 * layer : 2 * layer + 1, :] = gains
        r.ng[d, 2 * layer + 1 : 2 * layer + 2, :] = offsets

    def pass_down(layer, inner):
        total = r.gx[...] + inner
        if layer > 0:
            r.gx[...] = total.astype(LOW).astype(WIDE)
        else:
            r.input_grad[...] = total

    base = 6 + 2 * chips

    def back_hidden(layer):
        at = layer // 2
        r.dft[at, :, 0:length] = r.df[at, 0:length, :].T
        give(base + at, r.dft.at[at, :, mine], r.dft.at[at, :, other])
        for index in range(hidden // width):
            place = pl.ds(index * width, width)
            pulled = product(r.df[at, 0:length, :], r.wb[at, pl.ds(index * width, width), :], NT)
            r.dh[at, 0:length, place] = (pulled * r.slope[at, :, place].astype(WIDE)).astype(LOW)
            give(base + 2 + chips * at + index, r.dh.at[at, mine, place], r.dh.at[at, other, place])

    def back_expand_end(layer):
        pass_down(layer, product(r.dh[layer // 2, 0:length, :], r.wa[layer], NT))

    def back_output(layer):
        at = layer // 2
        give(base + 2 + 2 * chips + at, r.df.at[at, mine], r.df.at[at, other])
        r.dm[...] = product(r.df[at, 0:length, :], r.wa[layer, :, 3 * width :], NT).astype(LOW)
        r.kt[at] = (r.k[at] * jnp.asarray(scale, LOW)).T

    def back_heads(layer, begin, count):
        at = layer // 2

        def pair(index):
            lanes = aligned(index * 2 * head, 2 * head)
            pulled = r.dm[:, lanes]
            keys, values = [], []
            for which in range(2):
                probs = r.pt[at, 2 * index + which]
                grad = product(r.v[at, :, lanes], pulled * half_masks[which], NT)
                full = probs.astype(WIDE)
                centre = jnp.sum(full * grad, 0, keepdims=True)
                scores = (full * (grad - centre)).astype(LOW)
                keys.append(product(scores, r.q[at, :, lanes], NN))
                values.append(product(probs, pulled, NN))
                place = aligned((2 * index + which) * head, head)
                r.dqt[place, :] = product(r.kt[at, place, :], scores, NN).astype(LOW)
            r.dp[at, 0:length, aligned(width + index * 2 * head, 2 * head)] = jnp.where(
                lane < head, keys[0], keys[1]
            ).astype(LOW)
            r.dp[at, 0:length, aligned(2 * width + index * 2 * head, 2 * head)] = jnp.where(
                lane < head, values[0], values[1]
            ).astype(LOW)

        def pairs(step):
            pair(begin + 2 * step)
            pair(begin + 2 * step + 1)

        loop(count // 2, pairs)

    def back_packed(layer):
        at = layer // 2
        slot = base + 4 + 2 * chips + 2 * at
        place = pl.ds(width, 2 * width)
        give(slot, r.dp.at[at, mine, place], r.dp.at[at, other, place])
        r.dp[at, 0:length, 0:width] = r.dqt[...].T
        place = pl.ds(0, width)
        give(slot + 1, r.dp.at[at, mine, place], r.dp.at[at, other, place])

    def back_packed_end(layer):
        pass_down(layer, product(r.dp[layer // 2, 0:length, :], r.wa[layer, :, 0 : 3 * width], NT))

    def keep(name, half, place, value):
        own = getattr(r, "own" + name)
        own[:, :, half, :, place] = value.astype(LOW).reshape(chips, SECTIONS, rows_a // SECTIONS, value.shape[1])

    def chip_rows(value):
        return value.reshape(chips * rows_a, 2 * length)

    def grad_down(at):
        own = getattr(r, "ownB%d" % at)
        taken(base + at, r.dft.at[at, :, other])
        for chip in range(chips):
            taken(6 + chips * at + chip, r.gc.at[at, chip, other, :])
            value = product(r.dft[at], r.gc[at, chip], NN)
            own[chip] = value.astype(LOW).reshape(SECTIONS, 2, half_b, rows_b)

    def grad_up(layer):
        at = layer // 2
        taken(layer, r.xtc.at[layer, :, :, other])
        for index in range(hidden // width):
            place = pl.ds(index * width, width)
            taken(base + 2 + chips * at + index, r.dh.at[at, other, place])
            value = product(chip_rows(r.xtc[layer]), r.dh[at, :, place], NN)
            keep("F%d" % layer, index // 2, pl.ds(index % 2 * width, width), value)

    def grad_output(layer):
        at = layer // 2
        taken(4 + at, r.otc.at[at, :, :, other])
        taken(base + 2 + 2 * chips + at, r.df.at[at, other])
        for half in range(2):
            place = pl.ds(half * width // 2, width // 2)
            value = product(chip_rows(r.otc[at]), r.df[at, :, place], NN)
            keep("O%d" % layer, half, pl.ds(0, width // 2), value)

    def grad_packed(layer):
        at = layer // 2
        slot = base + 4 + 2 * chips + 2 * at
        taken(layer, r.xtc.at[layer, :, :, other])
        taken(slot, r.dp.at[at, other, pl.ds(width, 2 * width)])
        taken(slot + 1, r.dp.at[at, other, pl.ds(0, width)])
        part = 3 * width // 2
        for half in range(2):
            value = product(chip_rows(r.xtc[layer]), r.dp[at, :, half * part : (half + 1) * part], NN)
            keep("K%d" % layer, half, pl.ds(0, part), value)

    def joined(target, others):
        return functools.reduce(
            lambda left, right: left + right, [ref[...].astype(WIDE) for ref in (target, *others)]
        )

    def add_into(target, others):
        if len(others) == 1:
            target[...] = target[...] + others[0][...]
        else:
            target[...] = joined(target, others).astype(LOW)

    places = {name: place for place, (name, _, _, _) in enumerate(grad_items)}

    def buffers(name):
        parts = ("own", "farx", "fary", "nearx", "neary", "line", "done")
        return types.SimpleNamespace(**{part: getattr(r, part + name) for part in parts})

    def plane_first_sends(name, own):
        item, place = buffers(name), places[name]

        def over_x(section, half, target, slot):
            push(own(section, half), target, r.px_s.at[place, slot], r.px_r.at[place, slot], to_x)
            at_end(None, item.farx, r.px_s.at[place, slot])

        def over_y(section, half, target, slot):
            push(own(section, half), target, r.py_s.at[place, slot], r.py_r.at[place, slot], to_y)
            at_end(None, item.farx, r.py_s.at[place, slot])

        over_x(sd, 0, item.farx, 2)
        over_y(sd, 1, item.fary, 2)
        over_x(sx, 0, item.nearx.at[0], 0)
        over_y(sy, 1, item.neary.at[1], 1)

    def plane_second_sends(name, own):
        item, place = buffers(name), places[name]
        arrived(item.fary, r.py_r.at[place, 2])
        add_into(own(sx, 1), [item.fary])
        push(own(sx, 1), item.nearx.at[1], r.px_s.at[place, 1], r.px_r.at[place, 1], to_x)
        at_end(None, item.farx, r.px_s.at[place, 1])
        arrived(item.farx, r.px_r.at[place, 2])
        add_into(own(sy, 0), [item.farx])
        push(own(sy, 0), item.neary.at[0], r.py_s.at[place, 0], r.py_r.at[place, 0], to_y)
        at_end(None, item.farx, r.py_s.at[place, 0])

    def near_arrived(name):
        item, place = buffers(name), places[name]
        for half in range(2):
            arrived(item.nearx.at[half], r.px_r.at[place, half])
            arrived(item.neary.at[half], r.py_r.at[place, half])

    def line_sends(name, own):
        item, place = buffers(name), places[name]
        for step in range(1, chips):
            chip = lax.rem(z + step, chips)
            push(
                own.at[chip],
                item.line.at[z],
                r.line_s.at[place, step],
                r.line_r.at[place, z],
                {"dp": 2 * chip + c},
            )
            at_end(None, item.line.at[0], r.line_s.at[place, step])

    def line_arrived(name):
        item, place = buffers(name), places[name]
        others = [lax.rem(z + step, chips) for step in range(1, chips)]
        for chip in others:
            arrived(item.line.at[chip], r.line_r.at[place, chip])
        return [item.line.at[chip] for chip in others]

    def by_section(name):
        own = buffers(name).own
        if name in LINE_FIRST:
            return lambda section, half: own.at[z, section, half]
        return lambda section, half: own.at[:, section, half]

    def to_plane(name):
        if name in LINE_FIRST:
            line_sends(name, buffers(name).own)
        else:
            plane_first_sends(name, by_section(name))

    def through_plane(name):
        if name in LINE_FIRST:
            add_into(buffers(name).own.at[z], line_arrived(name))
            plane_first_sends(name, by_section(name))
        else:
            plane_second_sends(name, by_section(name))

    def to_line(name):
        if name in LINE_FIRST:
            plane_second_sends(name, by_section(name))
            return
        item = buffers(name)
        own = item.own.at[:, s]
        near_arrived(name)
        for half in range(2):
            add_into(own.at[:, half], [item.nearx.at[half], item.neary.at[half]])
        line_sends(name, own)

    def to_owner(name):
        item, place = buffers(name), places[name]
        if name in LINE_FIRST:
            near_arrived(name)
            terms = [item.nearx, item.neary]
        else:
            terms = line_arrived(name)
        total = joined(item.own.at[z, s], terms)
        square = total * total
        while square.ndim > 2:
            square = jnp.sum(square, 0)
        square = jnp.sum(jnp.sum(square, 0, keepdims=True), 1, keepdims=True)
        r.sum[...] = r.sum[...] + jnp.broadcast_to(square, (8, LANES))
        if name[0] == "B":
            item.done[...] = total
            return
        item.done[s] = total.astype(LOW)
        layer = grad_items[place][1]
        mine = item.done.at[s]
        away = s != layer
        when(
            away,
            lambda: push(mine, mine, r.done_s.at[place], r.done_r.at[place, s], {"section": jnp.int32(layer)}),
        )
        at_end(away, mine, r.done_s.at[place])

    def collect(name):
        item, place = buffers(name), places[name]
        layer = grad_items[place][1]

        def work():
            for section in range(SECTIONS):
                if section != layer:
                    arrived(item.done.at[section], r.done_r.at[place, section])
            columns = item.done.shape[-1]
            start = 3 * width if name[0] == "O" else 0
            for section in range(SECTIONS):
                for half in range(2):
                    rows = pl.ds(section * (rows_a // SECTIONS), rows_a // SECTIONS)
                    place_to = pl.ds(start + half * columns, columns)
                    r.grad_a[rows, place_to] = item.done[section, half].astype(WIDE)

        when(s == layer, work)

    def all_sent():
        for condition, source, sem in finish:
            when(condition, functools.partial(sent, source, sem))
        finish.clear()

    small_out(0, r.tiles.at[d, s])
    start_line(0)
    spread_plane(0, z)
    rows_plane()
    line_step(0, 1)
    rows_relay()
    line_step(0, 2)
    rows_line()
    start_line(2)
    for step in range(3, chips):
        line_step(0, step)
    small_group(0, r.tiles.at[pl.ds(0, devices - 1), 0])
    for peer in plane:
        push(r.tiles.at[:, s], r.tiles.at[:, s], r.small_s.at[0, 1], r.small_r.at[0, 1], peer)
    prepare_masks()
    rows_step(1)
    plane_step(0)
    for step in range(2, chips):
        rows_step(step)
    spread_plane(2, z)
    for step in range(1, chips):
        line_step(2, step)
    own_x.wait()
    own_cot.wait()
    relay_step(0)
    small_plane(0, r.tiles.at[:, pl.ds(0, SECTIONS - 1)])
    for slot in range(4):
        arrived(whole_a, r.gs_r.at[slot])
    attention(0)
    normalize(0)
    expand(1)
    arrived(whole_b, r.gs_r.at[4])
    contract(1)
    normalize(1)
    plane_step(2)
    attention(2)
    normalize(2)
    expand(3)
    gather_sends(0)
    for slot in range(5):
        at_end(None, whole_a if slot < 4 else whole_b, r.gs_s.at[slot])
    all_sent()
    relay_step(2)
    arrived(whole_b, r.gs_r.at[5])
    contract(3)
    normalize(3)

    r.sum[...] = jnp.zeros((8, LANES), WIDE)
    back_normalize(3)
    back_hidden(3)
    back_expand_end(3)
    give_rows(3)
    grad_down(1)
    to_plane("B1")
    back_normalize(2)
    grad_up(3)
    to_plane("F3")
    back_output(2)
    back_heads(2, 0, 2)
    through_plane("B1")
    grad_output(2)
    to_plane("O2")
    back_heads(2, 2, 2)
    back_packed(2)
    give_rows(2)
    through_plane("F3")
    back_packed_end(2)
    to_line("B1")
    through_plane("O2")
    back_normalize(1)
    grad_packed(2)
    to_plane("K2")
    back_hidden(1)
    give_rows(1)
    to_line("F3")
    to_line("O2")
    back_expand_end(1)
    grad_down(0)
    to_plane("B0")
    through_plane("K2")
    to_owner("B1")
    back_normalize(0)
    small_out(1, r.ng.at[d])
    grad_up(1)
    to_plane("F1")
    back_output(0)
    give_rows(0)
    to_owner("F3")
    to_owner("O2")
    back_heads(0, 0, 2)
    through_plane("B0")
    to_line("K2")
    grad_output(0)
    to_plane("O0")
    back_heads(0, 2, 2)
    back_packed(0)
    through_plane("F1")
    to_owner("K2")
    grad_packed(0)
    to_plane("K0")
    through_plane("O0")
    to_line("B0")
    back_packed_end(0)
    to_line("F1")
    to_line("O0")
    gather_sends(2)
    at_end(None, whole_b, r.gs_s.at[5])
    all_sent()
    through_plane("K0")
    to_owner("B0")
    to_owner("F1")
    to_owner("O0")
    small_group(1, r.ng.at[pl.ds(0, devices - 1)])
    r.ns[s] = functools.reduce(lambda left, right: left + right, [r.ng[index] for index in range(devices)])
    small_plane_out(1, r.ns.at[s])
    for name in ("F3", "O2", "K2", "F1"):
        collect(name)
    to_line("K0")
    collect("O0")
    for layer in range(2):
        done = buffers("B%d" % layer).done
        r.grad_b[layer] = done[...].reshape(cols_b, rows_b).T
    small_plane(1, r.ns.at[pl.ds(0, SECTIONS - 1)])
    grads = functools.reduce(lambda left, right: left + right, [r.ns[index] for index in range(SECTIONS)])
    norm_square = jnp.sum(jnp.sum(grads * grads, 0, keepdims=True), 1, keepdims=True)
    chosen = jnp.zeros((2, width), WIDE)
    for layer in range(4):
        chosen = jnp.where(s == layer, grads[2 * layer : 2 * layer + 2, :], chosen)
    for chip in range(chips):
        pair_of = chosen[:, chip * LANES : (chip + 1) * LANES]
        r.grad_n[...] = jnp.where(
            z == chip, jnp.where(c == 0, pair_of[:, :rows_a], pair_of[:, rows_a:]), r.grad_n[...]
        )
    to_owner("K0")

    r.sq[d] = r.sum[...]
    small_out(2, r.sq.at[d])
    collect("K0")
    small_group(2, r.sq.at[pl.ds(0, devices - 1)])
    r.sqs[s] = functools.reduce(lambda left, right: left + right, [r.sq[index] for index in range(devices)])
    small_plane_out(2, r.sqs.at[s])
    all_sent()
    small_plane(2, r.sqs.at[pl.ds(0, SECTIONS - 1)])
    squares = functools.reduce(lambda left, right: left + right, [r.sqs[index] for index in range(SECTIONS)])
    r.square[...] = squares + norm_square


def step_call(tokens, cotangent, lengths, mat_a, mat_b, norms):
    rows_a, hidden = mat_a.shape[1:]
    rows_b, cols_b = mat_b.shape[1:]
    width = tokens.shape[1]
    length = tokens.shape[0] // lengths.shape[0]
    chips = width // rows_a // 2
    scratch = kernel_scratch(chips, rows_a, rows_b, cols_b, length, width, hidden)
    shapes = []
    for _, shape, kind in scratch:
        shapes.append(pltpu.SemaphoreType.DMA(shape) if kind is None else pltpu.VMEM(shape, kind))
    anywhere, vmem = pl.BlockSpec(memory_space=pl.ANY), pl.BlockSpec(memory_space=pltpu.VMEM)
    return pl.pallas_call(
        functools.partial(step_kernel, INPUTS + OUTPUTS + tuple(name for name, _, _ in scratch)),
        out_shape=(
            jax.ShapeDtypeStruct((rows_a, hidden), WIDE),
            jax.ShapeDtypeStruct(mat_b.shape, WIDE),
            jax.ShapeDtypeStruct((2, rows_a), WIDE),
            jax.ShapeDtypeStruct((8, LANES), WIDE),
            jax.ShapeDtypeStruct((length, width), LOW),
            jax.ShapeDtypeStruct((length, width), WIDE),
        ),
        in_specs=[anywhere, anywhere, pl.BlockSpec(memory_space=pltpu.SMEM), vmem, vmem, vmem],
        out_specs=[vmem] * len(OUTPUTS),
        scratch_shapes=shapes,
        compiler_params=pltpu.CompilerParams(
            collective_id=0, has_side_effects=True, vmem_limit_bytes=KERNEL_VMEM
        ),
    )(tokens, cotangent, lengths, mat_a, mat_b, norms)


def update_kernel(*refs):
    square, output, input_grad = (ref[...] for ref in refs[:3])
    grad_norm = jnp.sqrt(square[0:1, 0:1])
    factor = CLIP_NORM / jnp.maximum(grad_norm, CLIP_NORM)
    inputs, outputs = refs[3:15], refs[15:]
    outputs[0][...] = grad_norm
    outputs[1][0] = output
    outputs[2][0] = input_grad
    for group, (rate, decay) in enumerate(
        ((MATRIX_RATE, MATRIX_DECAY), (MATRIX_RATE, MATRIX_DECAY), (NORM_RATE, 0.0))
    ):
        grad, weight, one, two = inputs[4 * group : 4 * group + 4]
        clip = grad[...].reshape(weight.shape) * factor
        moment, square_new, master = adam_update(weight[...], one[...], two[...], clip, rate, decay)
        for ref, value in zip(
            outputs[3 + 5 * group : 8 + 5 * group], (clip, moment, square_new, master, master.astype(LOW))
        ):
            ref[...] = value


def kernel_body(
    tokens, cotangent, lengths, mat_a, mat_b, norms, first_a, second_a, first_b, second_b, first_n, second_n
):
    norms, first_n, second_n = (jnp.swapaxes(value, 1, 2) for value in (norms, first_n, second_n))
    grad_a, grad_b, grad_n, square, output, input_grad = step_call(
        tokens, cotangent, lengths, mat_a, mat_b, norms
    )
    steps = 4

    def cut(value, dim):
        shape = tuple(size // steps if at == dim else size for at, size in enumerate(value.shape))
        return pl.BlockSpec(shape, lambda step: tuple(step if at == dim else 0 for at in range(len(shape))))

    def whole(value):
        return pl.BlockSpec(value.shape, lambda step: (0,) * len(value.shape))

    def like(value, kind=WIDE):
        return jax.ShapeDtypeStruct(value.shape, kind)

    args = (square, output, input_grad, grad_a, mat_a, first_a, second_a, grad_b, mat_b, first_b, second_b)
    specs = [whole(square), cut(output, 0), cut(input_grad, 0)]
    specs += [cut(grad_a, 0)] + [cut(mat_a, 1)] * 3 + [cut(grad_b, 1)] * 4
    args += (grad_n, norms, first_n, second_n)
    specs += [whole(grad_n)] + [whole(norms)] * 3
    shapes = [jax.ShapeDtypeStruct((1, 1), WIDE), like(output[None], LOW), like(input_grad[None])]
    out_specs = [whole(shapes[0]), cut(shapes[1], 1), cut(shapes[2], 1)]
    for value, spec in ((mat_a, cut(mat_a, 1)), (mat_b, cut(mat_b, 1)), (norms, whole(norms))):
        shapes += [like(value)] * 4 + [like(value, LOW)]
        out_specs += [spec] * 5
    results = pl.pallas_call(
        update_kernel,
        grid=(steps,),
        out_shape=shapes,
        in_specs=specs,
        out_specs=out_specs,
        compiler_params=pltpu.CompilerParams(vmem_limit_bytes=KERNEL_VMEM),
    )(*args)
    results = [results[0][0, 0], *results[1:]]
    results[-5:] = [jnp.swapaxes(value, 1, 2) for value in results[-5:]]
    return tuple(results)


def chosen_body(*args):
    rows_a = args[3].shape[1]
    groups = lax.axis_size("dp")
    by_kernel = rows_a % 32 == 0 and 2 * rows_a == LANES and groups * rows_a == args[0].shape[1]
    return (kernel_body if by_kernel else body)(*args)


def solution(mesh):
    placed = (
        P("dp", None),
        P("dp", None),
        P("dp", None),
        P("section", "dp", None),
        P(None, "dp", "section"),
        P("section", "dp", None),
        P("section", "dp", None),
        P("section", "dp", None),
        P(None, "dp", "section"),
        P(None, "dp", "section"),
        P("section", "dp", None),
        P("section", "dp", None),
    )
    return jax.shard_map(
        chosen_body,
        mesh=mesh,
        in_specs=placed,
        out_specs=(
            P(),
            P("section", "dp", None),
            P("section", "dp", None),
            P("section", "dp", None),
            P("section", "dp", None),
            P("section", "dp", None),
            P("section", "dp", None),
            P("section", "dp", None),
            P(None, "dp", "section"),
            P(None, "dp", "section"),
            P(None, "dp", "section"),
            P(None, "dp", "section"),
            P(None, "dp", "section"),
            P("section", "dp", None),
            P("section", "dp", None),
            P("section", "dp", None),
            P("section", "dp", None),
            P("section", "dp", None),
        ),
        check_vma=False,
    )
```

```python
import functools
import types

import jax
import jax.numpy as jnp
from jax import lax
from jax.experimental import pallas as pl
from jax.experimental.pallas import tpu as pltpu
from jax.sharding import PartitionSpec as P

HEADS = 8
STEP = 5


EPSILON = 1e-05
NEGATIVE = -1e30
CLIP_NORM = 1.0
BETA_ONE = 0.5
BETA_TWO = 0.5
ADAM_EPSILON = 1e-08
MATRIX_RATE = 0.05
NORM_RATE = 0.5
MATRIX_DECAY = 0.01


def norm_stats(value):
    centre = value - jnp.mean(value, -1, keepdims=True)
    inverse = lax.rsqrt(jnp.mean(centre * centre, -1, keepdims=True) + EPSILON)
    return (centre * inverse, inverse)


def norm_back(normal, inverse, upstream):
    return inverse * (
        upstream
        - jnp.mean(upstream, -1, keepdims=True)
        - normal * jnp.mean(upstream * normal, -1, keepdims=True)
    )


def adam_update(weight, moment_one, moment_two, gradient, step_rate, decay_rate):
    first_new = BETA_ONE * moment_one + (1.0 - BETA_ONE) * gradient
    second_new = BETA_TWO * moment_two + (1.0 - BETA_TWO) * gradient * gradient
    first_hat = first_new / (1.0 - BETA_ONE**STEP)
    second_hat = second_new / (1.0 - BETA_TWO**STEP)
    weight_new = weight - step_rate * (
        first_hat / (jnp.sqrt(second_hat) + ADAM_EPSILON) + decay_rate * weight
    )
    return (first_new, second_new, weight_new)


def segments_of(lengths_row, length):
    ends = jnp.cumsum(lengths_row, dtype=jnp.int32)
    places = jnp.arange(length, dtype=jnp.int32)
    segment = jnp.sum((ends[None, :] <= places[:, None]).astype(jnp.int32), axis=1, dtype=jnp.int32)
    live = (places < ends[-1]).astype(jnp.float32)
    return segment, live


def matmul(left, right, dims):
    return lax.dot_general(left, right, (dims, ((), ())), preferred_element_type=jnp.float32)


NN = ((1,), (0,))
NT = ((1,), (1,))
TN = ((0,), (0,))


def attention_forward(stream, weight, mask):
    length, width = stream.shape
    size = width // HEADS
    packed = matmul(stream, weight[:, : 3 * width], NN).astype(jnp.bfloat16)
    heads = packed.reshape(length, 3, HEADS, size)
    scores = jnp.einsum("qhd,khd->hqk", heads[:, 0], heads[:, 1], preferred_element_type=jnp.float32)
    scores = jnp.where(mask[None], scores * size**-0.5, NEGATIVE)
    weights = jnp.exp(scores - jnp.max(scores, -1, keepdims=True))
    probs = weights / jnp.sum(weights, -1, keepdims=True)
    mixed = jnp.einsum("hqk,khd->qhd", probs.astype(jnp.bfloat16), heads[:, 2], preferred_element_type=jnp.float32)
    mixed = mixed.reshape(length, width).astype(jnp.bfloat16)
    branch = matmul(mixed, weight[:, 3 * width :], NN)
    return branch, (heads, probs, mixed)


def attention_backward(stream, weight, kept, grad_low):
    heads, probs, mixed = kept
    length, width = stream.shape
    size = width // HEADS
    grad_out = matmul(mixed, grad_low, TN)
    grad_mixed = matmul(grad_low, weight[:, 3 * width :], NT).astype(jnp.bfloat16)
    grad_mixed = grad_mixed.reshape(length, HEADS, size)
    grad_probs = jnp.einsum("qhd,khd->hqk", grad_mixed, heads[:, 2], preferred_element_type=jnp.float32)
    centre = jnp.sum(probs * grad_probs, -1, keepdims=True)
    grad_scores = (probs * (grad_probs - centre)).astype(jnp.bfloat16)
    low = probs.astype(jnp.bfloat16)
    scale = size**-0.5
    grad_q = jnp.einsum("hqk,khd->qhd", grad_scores, heads[:, 1], preferred_element_type=jnp.float32) * scale
    grad_k = jnp.einsum("hqk,qhd->khd", grad_scores, heads[:, 0], preferred_element_type=jnp.float32) * scale
    grad_v = jnp.einsum("hqk,qhd->khd", low, grad_mixed, preferred_element_type=jnp.float32)
    packed = jnp.concatenate([grad_q, grad_k, grad_v], axis=1).reshape(length, 3 * width)
    packed = packed.astype(jnp.bfloat16)
    grad_in = matmul(stream, packed, TN)
    grad_inputs = matmul(packed, weight[:, : 3 * width], NT)
    return grad_inputs, jnp.concatenate([grad_in, grad_out], axis=1)


def feed_forward(stream, weight, down):
    pre = matmul(stream, weight, NN)
    active = jax.nn.gelu(pre, approximate=True).astype(jnp.bfloat16)
    return matmul(active, down, NN), (pre, active)


def feed_backward(stream, weight, down, kept, grad_low):
    pre, active = kept
    grad_down = matmul(active, grad_low, TN)
    grad_active = matmul(grad_low, down, NT)
    pull = jax.vjp(lambda value: jax.nn.gelu(value, approximate=True), pre)[1]
    grad_pre = pull(grad_active)[0].astype(jnp.bfloat16)
    grad_up = matmul(stream, grad_pre, TN)
    return matmul(grad_pre, weight, NT), grad_up, grad_down


def micro_step(rows, pull, segment, mats, downs, gains, biases):
    low = jnp.bfloat16
    mask = segment[:, None] == segment[None, :]
    stream, dual = rows, jnp.zeros_like(rows)
    saved = []
    for sub in range(4):
        if sub % 2 == 0:
            branch, kept = attention_forward(stream, mats[sub], mask)
        else:
            branch, kept = feed_forward(stream, mats[sub], downs[sub // 2])
        normal, inverse = norm_stats(stream.astype(jnp.float32) + branch)
        out = normal * gains[sub] + biases[sub]
        total = dual.astype(jnp.float32) + branch
        saved.append((stream, kept, normal, inverse))
        if sub < 3:
            stream, dual = out.astype(low), total.astype(low)
    dual_normal, dual_inverse = norm_stats(total)
    output = (out + dual_normal).astype(low)
    grad_out, grad_dual = pull, norm_back(dual_normal, dual_inverse, pull)
    grads_a, grads_b, grads_n = [None] * 4, [None] * 2, [None] * 4
    for sub in (3, 2, 1, 0):
        stream, kept, normal, inverse = saved[sub]
        grads_n[sub] = jnp.stack([jnp.sum(grad_out * normal, 0), jnp.sum(grad_out, 0)], axis=1)
        summed = norm_back(normal, inverse, grad_out * gains[sub])
        branch_low = (summed + grad_dual).astype(low)
        if sub % 2 == 0:
            inner, grads_a[sub] = attention_backward(stream, mats[sub], kept, branch_low)
        else:
            inner, grads_a[sub], grads_b[sub // 2] = feed_backward(
                stream, mats[sub], downs[sub // 2], kept, branch_low
            )
        grad_in = summed + inner
        if sub > 0:
            grad_out = grad_in.astype(low).astype(jnp.float32)
            grad_dual = grad_dual.astype(low).astype(jnp.float32)
    return output, grad_in, jnp.stack(grads_a), jnp.stack(grads_b), jnp.stack(grads_n)


def finish_step(grad_norm, output, input_grad, *groups):
    factor = CLIP_NORM / jnp.maximum(grad_norm, CLIP_NORM)
    results = [grad_norm, output[None], input_grad[None]]
    for weight, one, two, grad, rate, decay in groups:
        clip = grad * factor
        moment, square_new, master = adam_update(weight, one, two, clip, rate, decay)
        results += [clip, moment, square_new, master, master.astype(jnp.bfloat16)]
    return tuple(results)


def body(
    tokens, cotangent, lengths, mat_a, mat_b, norms, first_a, second_a, first_b, second_b, first_n, second_n
):
    low = jnp.bfloat16
    own = lax.axis_index("section")
    length = tokens.shape[0] // lengths.shape[0]
    rows = lax.dynamic_slice_in_dim(tokens, own * length, length, 0)
    segment, live = segments_of(lax.dynamic_index_in_dim(lengths, own, 0, keepdims=False), length)
    pull = lax.dynamic_slice_in_dim(cotangent, own * length, length, 0).astype(jnp.float32) * live[:, None]

    def gathered(value):
        return lax.all_gather(lax.all_gather(value, "dp", axis=1, tiled=True), "section", axis=0, tiled=True)

    mats = gathered(mat_a.astype(low))
    scales = gathered(norms.astype(low)).astype(jnp.float32)
    downs = lax.all_gather(mat_b.astype(low), "section", axis=2, tiled=True)
    downs = lax.all_gather(downs, "dp", axis=1, tiled=True)
    output, input_grad, part_a, part_b, part_n = micro_step(
        rows, pull, segment, mats, downs, scales[:, :, 0], scales[:, :, 1]
    )

    def scattered(value, section_dim):
        value = lax.psum_scatter(value, "section", scatter_dimension=section_dim, tiled=True)
        return lax.psum_scatter(value, "dp", scatter_dimension=1, tiled=True).astype(jnp.float32)

    grad_a = scattered(part_a.astype(low), 0)
    grad_b = scattered(part_b.astype(low), 2)
    grad_n = scattered(part_n, 0)
    square = jnp.sum(grad_a * grad_a) + jnp.sum(grad_b * grad_b) + jnp.sum(grad_n * grad_n)
    grad_norm = jnp.sqrt(lax.psum(square, ("section", "dp")))
    return finish_step(
        grad_norm, output, input_grad,
        (mat_a, first_a, second_a, grad_a, MATRIX_RATE, MATRIX_DECAY),
        (mat_b, first_b, second_b, grad_b, MATRIX_RATE, MATRIX_DECAY),
        (norms, first_n, second_n, grad_n, NORM_RATE, 0.0),
    )


LOW = jnp.bfloat16
WIDE = jnp.float32
MESH = pl.DeviceIdType.MESH
SECTIONS = 4
LANES = 128
BLOCK = 64
KERNEL_VMEM = 64 * 1024 * 1024 - 256 * 1024


def gradient_items(rows_a, rows_b, cols_b, width, hidden):
    part = rows_a // SECTIONS
    return (
        ("B1", 3, cols_b // 2, rows_b),
        ("F3", 3, part, hidden // 2),
        ("O2", 2, part, width // 2),
        ("K2", 2, part, 3 * width // 2),
        ("B0", 1, cols_b // 2, rows_b),
        ("F1", 1, part, hidden // 2),
        ("O0", 0, part, width // 2),
        ("K0", 0, part, 3 * width // 2),
    )


def item_scratch(name, chips, rows, columns):
    piece = (rows, columns)
    return (
        ("own" + name, (chips, SECTIONS, 2) + piece, LOW),
        ("farx" + name, (chips,) + piece, LOW),
        ("fary" + name, (chips,) + piece, LOW),
        ("nearx" + name, (2, chips) + piece, LOW),
        ("neary" + name, (2, chips) + piece, LOW),
        ("line" + name, (chips, 2) + piece, LOW),
        ("done" + name, (2,) + piece if name[0] == "B" else (SECTIONS, 2) + piece, WIDE if name[0] == "B" else LOW),
    )


def kernel_scratch(chips, rows_a, rows_b, cols_b, length, width, hidden):
    devices = 2 * chips
    items = gradient_items(rows_a, rows_b, cols_b, width, hidden)
    count = len(items)
    received = sum((item_scratch(name, chips, rows, columns) for name, _, rows, columns in items), ())
    return received + (
        ("fac_s", (32,), None),
        ("fac_r", (32,), None),
        ("px_s", (count, 3), None),
        ("px_r", (count, 3), None),
        ("py_s", (count, 3), None),
        ("py_r", (count, 3), None),
        ("line_s", (count, chips), None),
        ("line_r", (count, chips), None),
        ("done_s", (count,), None),
        ("done_r", (count, SECTIONS), None),
        ("wa", (4, width, hidden), LOW),
        ("wb", (2, hidden, width), LOW),
        ("tiles", (devices, SECTIONS, 8, LANES), WIDE),
        ("x", (4, length, width), LOW),
        ("xt", (4, chips, 2, rows_a, length), LOW),
        ("xtc", (4, chips, rows_a, 2 * length), LOW),
        ("y", (length, width), LOW),
        ("cot", (length, width), LOW),
        ("bias", (length, length), WIDE),
        ("live", (length, 1), WIDE),
        ("f", (length, width), WIDE),
        ("n", (4, length, width), WIDE),
        ("inv", (4, length, 1), WIDE),
        ("q", (2, length, width), LOW),
        ("k", (2, length, width), LOW),
        ("v", (2, length, width), LOW),
        ("kt", (2, width, length), LOW),
        ("vt", (2, width, length), LOW),
        ("ot", (2, chips, 2, rows_a, length), LOW),
        ("otc", (2, chips, rows_a, 2 * length), LOW),
        ("pt", (2, HEADS, length, length), LOW),
        ("g", (2, length, hidden), LOW),
        ("gc", (2, chips, 2 * length, rows_b), LOW),
        ("slope", (2, length, hidden), LOW),
        ("gx", (length, width), WIDE),
        ("gy", (length, width), WIDE),
        ("df", (2, 2 * length, width), LOW),
        ("dft", (2, width, 2 * length), LOW),
        ("dm", (length, width), LOW),
        ("dqt", (width, length), LOW),
        ("dh", (2, 2 * length, hidden), LOW),
        ("dp", (2, 2 * length, 3 * width), LOW),
        ("ng", (devices, 8, width), WIDE),
        ("ns", (SECTIONS, 8, width), WIDE),
        ("sq", (devices, 8, LANES), WIDE),
        ("sqs", (SECTIONS, 8, LANES), WIDE),
        ("sum", (8, LANES), WIDE),
        ("in_s", (2,), None),
        ("gz_s", (3, 2, chips, 2), None),
        ("gz_r", (3, chips, 2), None),
        ("gx_s", (3, chips, 2), None),
        ("gx_r", (3, chips, 2), None),
        ("gy_s", (3, chips, 2), None),
        ("gy_r", (3, chips, 2), None),
        ("gxr_s", (3, chips), None),
        ("gxr_r", (3, chips), None),
        ("gyr_s", (3, chips), None),
        ("gyr_r", (3, chips), None),
        ("gs_s", (6,), None),
        ("gs_r", (6,), None),
        ("small_s", (3, 2), None),
        ("small_r", (3, 2), None),
    )


INPUTS = ("tokens", "cotangent", "lengths", "mat_a", "mat_b", "norms")
OUTPUTS = ("grad_a", "grad_b", "grad_n", "square", "output", "input_grad")


def step_kernel(names, *refs):
    r = types.SimpleNamespace(**dict(zip(names, refs)))
    width, hidden = r.wa.shape[1:]
    length = r.x.shape[1]
    rows_a, (rows_b, cols_b) = r.mat_a.shape[1], r.mat_b.shape[1:]
    devices = r.tiles.shape[0]
    chips = devices // 2
    half_a, half_b = rows_a // 2, cols_b // 2
    grad_items = gradient_items(rows_a, rows_b, cols_b, width, hidden)
    head = width // HEADS
    scale = head**-0.5

    s, d = lax.axis_index("section"), lax.axis_index("dp")
    z, c = lax.div(d, 2), lax.rem(d, 2)
    sx = s + 1 - 2 * lax.rem(s, 2)
    sy = lax.rem(s + 2, SECTIONS)
    sd = SECTIONS - 1 - s
    to_sibling = {"dp": d + 1 - 2 * c}
    to_up, to_down = {"dp": d + 2}, {"dp": d - 2}
    to_x, to_y = {"section": sx}, {"section": sy}
    below, above = z > 0, z < chips - 1
    group = [{"dp": lax.rem(d + step, devices)} for step in range(1, devices)]
    plane = [{"section": lax.rem(s + step, SECTIONS)} for step in range(1, SECTIONS)]
    finish = []

    def when(condition, work):
        if condition is None:
            work()
        else:
            pl.when(condition)(work)

    def push(source, target, send_sem, recv_sem, device):
        pltpu.make_async_remote_copy(
            src_ref=source,
            dst_ref=target,
            send_sem=send_sem,
            recv_sem=recv_sem,
            device_id=device,
            device_id_type=MESH,
        ).start()

    def arrived(target, sem):
        pltpu.make_async_remote_copy(
            src_ref=target, dst_ref=target, send_sem=sem, recv_sem=sem, device_id=to_x, device_id_type=MESH
        ).wait_recv()

    def sent(source, sem):
        pltpu.make_async_remote_copy(
            src_ref=source, dst_ref=source, send_sem=sem, recv_sem=sem, device_id=to_x, device_id_type=MESH
        ).wait_send()

    def at_end(condition, source, sem):
        finish.append((condition, source, sem))

    def aligned(start, size):
        return pl.ds(pl.multiple_of(start, size), size)

    own_x = pltpu.make_async_copy(r.tokens.at[aligned(s * length, length)], r.x.at[0], r.in_s.at[0])
    own_cot = pltpu.make_async_copy(r.cotangent.at[aligned(s * length, length)], r.cot, r.in_s.at[1])
    own_x.start()
    own_cot.start()
    barrier = pltpu.get_barrier_semaphore()
    for peer in group + plane:
        pl.semaphore_signal(barrier, inc=1, device_id=peer, device_id_type=MESH)
    r.wa[s, aligned(d * rows_a, rows_a), :] = r.mat_a[0].astype(LOW)
    for layer in range(2):
        r.wb[layer, aligned(d * rows_b, rows_b), aligned(s * cols_b, cols_b)] = r.mat_b[layer].astype(LOW)
    norms = r.norms[0].astype(LOW).astype(WIDE)
    nothing = jnp.zeros((2, rows_a), WIDE)
    even = jnp.concatenate([norms, nothing], axis=1)
    odd = jnp.concatenate([nothing, norms], axis=1)
    r.tiles[d, s, 0:2, :] = jnp.where(c == 0, even, odd)
    r.tiles[d, s, 2:8, :] = jnp.zeros((6, LANES), WIDE)
    pl.semaphore_wait(barrier, len(group) + len(plane))

    def small_out(which, source):
        for peer in group:
            push(source, source, r.small_s.at[which, 0], r.small_r.at[which, 0], peer)

    def small_group(which, like):
        arrived(like, r.small_r.at[which, 0])
        sent(like, r.small_s.at[which, 0])

    def small_plane_out(which, source):
        for peer in plane:
            push(source, source, r.small_s.at[which, 1], r.small_r.at[which, 1], peer)

    def small_plane(which, like):
        arrived(like, r.small_r.at[which, 1])
        sent(like, r.small_s.at[which, 1])

    def block_a(section, chip, half):
        return r.wa.at[section, aligned((2 * chip + c) * rows_a + half * half_a, half_a), :]

    def block_b(layer):
        part = rows_b // 2

        def block(section, chip, half):
            return r.wb.at[
                layer,
                aligned((2 * chip + c) * rows_b + half * part, part),
                aligned(section * cols_b, cols_b),
            ]

        return block

    items = (block_a, block_b(0), block_b(1))

    def to_the_sibling(item, section, chip, half):
        block = items[item](section, chip, half)
        slot = section if item == 0 else 3 + item
        push(block, block, r.gs_s.at[slot], r.gs_r.at[slot], to_sibling)

    def spread_plane(item, chip):
        for half in range(2):
            block = items[item](s, chip, half)
            push(block, block, r.gx_s.at[item, chip, half], r.gx_r.at[item, chip, half], to_x)
            push(block, block, r.gy_s.at[item, chip, half], r.gy_r.at[item, chip, half], to_y)
            to_the_sibling(item, s, chip, half)

    def up(item, chip, half):
        block = items[item](s, chip, half)
        push(block, block, r.gz_s.at[item, 0, chip, half], r.gz_r.at[item, chip, half], to_up)

    def down(item, chip, half):
        block = items[item](s, chip, half)
        push(block, block, r.gz_s.at[item, 1, chip, half], r.gz_r.at[item, chip, half], to_down)

    def start_line(item):
        for half in range(2):
            when(above, lambda: up(item, z, half))
            when(below, lambda: down(item, z, half))

    def line_step(item, step):
        def from_below():
            for half in range(2):
                arrived(items[item](s, z - step, half), r.gz_r.at[item, z - step, half])
                when(above, lambda: up(item, z - step, half))
            spread_plane(item, z - step)

        def from_above():
            for half in range(2):
                arrived(items[item](s, z + step, half), r.gz_r.at[item, z + step, half])
                when(below, lambda: down(item, z + step, half))
            spread_plane(item, z + step)

        when(z >= step, from_below)
        when(z + step < chips, from_above)

    def plane_step(item):
        for chip in range(chips):
            for half in range(2):
                arrived(items[item](sx, chip, half), r.gx_r.at[item, chip, half])
                if half == 1:
                    block = items[item](sx, chip, half)
                    push(block, block, r.gyr_s.at[item, chip], r.gyr_r.at[item, chip], to_y)
                to_the_sibling(item, sx, chip, half)
                arrived(items[item](sy, chip, half), r.gy_r.at[item, chip, half])
                if half == 0:
                    block = items[item](sy, chip, half)
                    push(block, block, r.gxr_s.at[item, chip], r.gxr_r.at[item, chip], to_x)
                to_the_sibling(item, sy, chip, half)

    def relay_step(item):
        for chip in range(chips):
            arrived(items[item](sd, chip, 0), r.gxr_r.at[item, chip])
            to_the_sibling(item, sd, chip, 0)
            arrived(items[item](sd, chip, 1), r.gyr_r.at[item, chip])
            to_the_sibling(item, sd, chip, 1)

    whole_a = r.wa.at[0, pl.ds(0, chips * rows_a)]
    whole_b = r.wb.at[0, pl.ds(0, chips * rows_b)]
    def gather_sends(item):
        for chip in range(chips):
            for half in range(2):
                block = items[item](0, chip, half)
                at_end(None, block, r.gx_s.at[item, chip, half])
                at_end(None, block, r.gy_s.at[item, chip, half])
                at_end(above & (z >= chip), block, r.gz_s.at[item, 0, chip, half])
                at_end(below & (z <= chip), block, r.gz_s.at[item, 1, chip, half])
            block = items[item](0, chip, 0)
            at_end(None, block, r.gxr_s.at[item, chip])
            at_end(None, block, r.gyr_s.at[item, chip])

    def row_block(chip, half):
        part = rows_b // 2
        return r.wb.at[0, aligned((2 * chip + c) * rows_b + half * part, part), :]

    def rows_to_sibling(chip, half):
        push(row_block(chip, half), row_block(chip, half), r.gs_s.at[4], r.gs_r.at[4], to_sibling)

    def rows_up(chip, half):
        rows = row_block(chip, half)
        push(rows, rows, r.gz_s.at[1, 0, chip, half], r.gz_r.at[1, chip, half], to_up)

    def rows_down(chip, half):
        rows = row_block(chip, half)
        push(rows, rows, r.gz_s.at[1, 1, chip, half], r.gz_r.at[1, chip, half], to_down)

    def rows_plane():
        for half in range(2):
            block = items[1](s, z, half)
            push(block, block, r.gx_s.at[1, 0, half], r.gx_r.at[1, 0, half], to_x)
            push(block, block, r.gy_s.at[1, 0, half], r.gy_r.at[1, 0, half], to_y)
            at_end(None, block, r.gx_s.at[1, 0, half])
            at_end(None, block, r.gy_s.at[1, 0, half])

    def rows_relay():
        for half in range(2):
            arrived(items[1](sx, z, half), r.gx_r.at[1, 0, half])
            arrived(items[1](sy, z, half), r.gy_r.at[1, 0, half])
        block = items[1](sx, z, 1)
        push(block, block, r.gyr_s.at[1, 0], r.gyr_r.at[1, 0], to_y)
        block = items[1](sy, z, 0)
        push(block, block, r.gxr_s.at[1, 0], r.gxr_r.at[1, 0], to_x)
        at_end(None, block, r.gyr_s.at[1, 0])
        at_end(None, block, r.gxr_s.at[1, 0])

    def rows_line():
        for half, sem in ((0, r.gxr_r), (1, r.gyr_r)):
            arrived(items[1](sd, z, half), sem.at[1, 0])
            when(above, lambda: rows_up(z, half))
            when(below, lambda: rows_down(z, half))
            rows_to_sibling(z, half)
        for chip in range(chips):
            for half in range(2):
                at_end(above & (z >= chip), row_block(chip, half), r.gz_s.at[1, 0, chip, half])
                at_end(below & (z <= chip), row_block(chip, half), r.gz_s.at[1, 1, chip, half])

    def rows_step(step):
        def from_below():
            for half in range(2):
                arrived(row_block(z - step, half), r.gz_r.at[1, z - step, half])
                when(above, lambda: rows_up(z - step, half))
                rows_to_sibling(z - step, half)

        def from_above():
            for half in range(2):
                arrived(row_block(z + step, half), r.gz_r.at[1, z + step, half])
                when(below, lambda: rows_down(z + step, half))
                rows_to_sibling(z + step, half)

        when(z >= step, from_below)
        when(z + step < chips, from_above)

    mine, other = pl.ds(0, length), pl.ds(length, length)

    def give(slot, source, target):
        push(source, target, r.fac_s.at[slot], r.fac_r.at[slot], to_sibling)
        at_end(None, target, r.fac_s.at[slot])

    def taken(slot, target):
        arrived(target, r.fac_r.at[slot])

    def give_rows(layer):
        r.xt[layer] = r.x[layer].T.reshape(chips, 2, rows_a, length)
        r.xtc[layer, :, :, 0:length] = r.xt[layer, :, c]
        give(layer, r.xt.at[layer, :, 1 - c], r.xtc.at[layer, :, :, other])

    def product(left, right, dims):
        return lax.dot_general(left, right, (dims, ((), ())), preferred_element_type=WIDE)

    def loop(count, work):
        def one(index, carry):
            work(index)
            return carry

        lax.fori_loop(0, count, one, 0)

    def gain_row(layer, kind):
        parts = [
            r.tiles[2 * chip, layer, kind : kind + 1, :] + r.tiles[2 * chip + 1, layer, kind : kind + 1, :]
            for chip in range(chips)
        ]
        return jnp.concatenate(parts, axis=1)

    def stats(value):
        centre = value - jnp.mean(value, -1, keepdims=True)
        inverse = lax.rsqrt(jnp.mean(centre * centre, -1, keepdims=True) + EPSILON)
        return centre * inverse, inverse

    lane = lax.broadcasted_iota(jnp.int32, (1, 2 * head), 1)
    first_half = (lane < head).astype(WIDE)
    half_masks = (first_half.astype(LOW), (1.0 - first_half).astype(LOW))

    def prepare_masks():
        ends, total = [], jnp.int32(0)
        for slot in range(r.lengths.shape[1]):
            total = total + r.lengths[s, slot]
            ends.append(total)
        down_places = lax.broadcasted_iota(jnp.int32, (length, 1), 0)
        across_places = lax.broadcasted_iota(jnp.int32, (1, length), 1)
        down_segment = jnp.zeros((length, 1), jnp.int32)
        across_segment = jnp.zeros((1, length), jnp.int32)
        for end in ends:
            down_segment = down_segment + (end <= down_places).astype(jnp.int32)
            across_segment = across_segment + (end <= across_places).astype(jnp.int32)
        r.bias[...] = jnp.where(down_segment == across_segment, 0.0, NEGATIVE)
        r.live[...] = (down_places < total).astype(WIDE)

    def attention(layer):
        at = layer // 2
        rows = r.x[layer]
        r.q[at] = product(rows, r.wa[layer, :, 0:width], NN).astype(LOW) * jnp.asarray(scale, LOW)
        keys = product(rows, r.wa[layer, :, width : 2 * width], NN).astype(LOW)
        r.k[at] = keys
        values = product(rows, r.wa[layer, :, 2 * width : 3 * width], NN).astype(LOW)
        r.v[at] = values
        r.vt[at] = values.T

        def pair(index):
            lanes = aligned(index * 2 * head, 2 * head)
            for which in range(2):
                scores = product(r.k[at, :, lanes], r.q[at, :, lanes] * half_masks[which], NT) + r.bias[...]
                weights = jnp.exp(scores - jnp.max(scores, 0, keepdims=True))
                probs = (weights * (1.0 / jnp.sum(weights, 0, keepdims=True))).astype(LOW)
                r.pt[at, 2 * index + which] = probs
                place = aligned((2 * index + which) * head, head)
                r.ot[at, index, which] = product(r.vt[at, place, :], probs, NN).astype(LOW)

        def pairs(step):
            pair(2 * step)
            pair(2 * step + 1)

        loop(HEADS // 4, pairs)
        r.otc[at, :, :, 0:length] = r.ot[at, :, c]
        give(4 + at, r.ot.at[at, :, 1 - c], r.otc.at[at, :, :, other])
        r.f[...] = product(r.ot[at].reshape(width, length).T, r.wa[layer, :, 3 * width :], NN)

    def expand(layer):
        at = layer // 2
        def columns(index):
            place = pl.ds(index * width, width)
            pre = product(r.x[layer], r.wa[layer, :, place], NN)
            squared = pre * pre
            slope = 0.7978845608 * (1.0 + 3 * 0.044715 * squared)
            bent = jnp.tanh(0.7978845608 * pre * (1.0 + 0.044715 * squared))
            r.g[at, :, place] = (0.5 * pre * (1.0 + bent)).astype(LOW)
            r.slope[at, :, place] = (0.5 * (1.0 + bent) + 0.5 * pre * (1.0 - bent * bent) * slope).astype(LOW)
            block = aligned((2 * index + c) * rows_b, rows_b)
            r.gc[at, index, 0:length, :] = r.g[at, :, block]
            block = aligned((2 * index + 1 - c) * rows_b, rows_b)
            give(6 + chips * at + index, r.g.at[at, :, block], r.gc.at[at, index, other, :])

        for index in range(hidden // width):
            columns(index)

    def contract(layer):
        r.f[...] = product(r.g[layer // 2], r.wb[layer // 2], NN)

    def by_rows(work):
        for index in range(length // BLOCK):
            work(pl.ds(index * BLOCK, BLOCK))

    def normalize(layer):
        gain, offset = gain_row(layer, 0), gain_row(layer, 1)

        def some(rows):
            branch = r.f[rows, :]
            normal, inverse = stats(r.x[layer, rows, :].astype(WIDE) + branch)
            r.n[layer, rows, :] = normal
            r.inv[layer, rows, :] = inverse
            out = normal * gain + offset
            dual = branch if layer == 0 else r.y[rows, :].astype(WIDE) + branch
            if layer < 3:
                r.x[layer + 1, rows, :] = out.astype(LOW)
                r.y[rows, :] = dual.astype(LOW)
            else:
                dual_normal, dual_inverse = stats(dual)
                r.output[rows, :] = (out + dual_normal).astype(LOW)
                pull = r.cot[rows, :].astype(WIDE) * r.live[rows, :]
                r.gx[rows, :] = pull
                r.gy[rows, :] = norm_back(dual_normal, dual_inverse, pull)

        by_rows(some)

    def back_normalize(layer):
        gain = gain_row(layer, 0)

        def some(index, sums):
            rows = pl.ds(index * BLOCK, BLOCK)
            upstream = r.gx[rows, :]
            normal = r.n[layer, rows, :]
            summed = norm_back(normal, r.inv[layer, rows, :], upstream * gain)
            dual = r.gy[rows, :]
            r.gx[rows, :] = summed
            r.df[layer // 2, rows, :] = (summed + dual).astype(LOW)
            if layer == 3:
                r.gy[rows, :] = dual.astype(LOW).astype(WIDE)
            return (
                sums[0] + jnp.sum(upstream * normal, 0, keepdims=True),
                sums[1] + jnp.sum(upstream, 0, keepdims=True),
            )

        zero = jnp.zeros((1, width), WIDE)
        gains, offsets = zero, zero
        for index in range(length // BLOCK):
            gains, offsets = some(index, (gains, offsets))
        r.ng[d, 2 * layer : 2 * layer + 1, :] = gains
        r.ng[d, 2 * layer + 1 : 2 * layer + 2, :] = offsets

    def pass_down(layer, inner):
        total = r.gx[...] + inner
        if layer > 0:
            r.gx[...] = total.astype(LOW).astype(WIDE)
        else:
            r.input_grad[...] = total

    base = 6 + 2 * chips

    def back_hidden(layer):
        at = layer // 2
        r.dft[at, :, 0:length] = r.df[at, 0:length, :].T
        give(base + at, r.dft.at[at, :, mine], r.dft.at[at, :, other])
        for index in range(hidden // width):
            place = pl.ds(index * width, width)
            pulled = product(r.df[at, 0:length, :], r.wb[at, pl.ds(index * width, width), :], NT)
            r.dh[at, 0:length, place] = (pulled * r.slope[at, :, place].astype(WIDE)).astype(LOW)
            give(base + 2 + chips * at + index, r.dh.at[at, mine, place], r.dh.at[at, other, place])

    def back_expand_end(layer):
        pass_down(layer, product(r.dh[layer // 2, 0:length, :], r.wa[layer], NT))

    def back_output(layer):
        at = layer // 2
        give(base + 2 + 2 * chips + at, r.df.at[at, mine], r.df.at[at, other])
        r.dm[...] = product(r.df[at, 0:length, :], r.wa[layer, :, 3 * width :], NT).astype(LOW)
        r.kt[at] = (r.k[at] * jnp.asarray(scale, LOW)).T

    def back_heads(layer, begin, count):
        at = layer // 2

        def pair(index):
            lanes = aligned(index * 2 * head, 2 * head)
            pulled = r.dm[:, lanes]
            keys, values = [], []
            for which in range(2):
                probs = r.pt[at, 2 * index + which]
                grad = product(r.v[at, :, lanes], pulled * half_masks[which], NT)
                full = probs.astype(WIDE)
                centre = jnp.sum(full * grad, 0, keepdims=True)
                scores = (full * (grad - centre)).astype(LOW)
                keys.append(product(scores, r.q[at, :, lanes], NN))
                values.append(product(probs, pulled, NN))
                place = aligned((2 * index + which) * head, head)
                r.dqt[place, :] = product(r.kt[at, place, :], scores, NN).astype(LOW)
            r.dp[at, 0:length, aligned(width + index * 2 * head, 2 * head)] = jnp.where(
                lane < head, keys[0], keys[1]
            ).astype(LOW)
            r.dp[at, 0:length, aligned(2 * width + index * 2 * head, 2 * head)] = jnp.where(
                lane < head, values[0], values[1]
            ).astype(LOW)

        def pairs(step):
            pair(begin + 2 * step)
            pair(begin + 2 * step + 1)

        loop(count // 2, pairs)

    def back_packed(layer):
        at = layer // 2
        slot = base + 4 + 2 * chips + 2 * at
        place = pl.ds(width, 2 * width)
        give(slot, r.dp.at[at, mine, place], r.dp.at[at, other, place])
        r.dp[at, 0:length, 0:width] = r.dqt[...].T
        place = pl.ds(0, width)
        give(slot + 1, r.dp.at[at, mine, place], r.dp.at[at, other, place])

    def back_packed_end(layer):
        pass_down(layer, product(r.dp[layer // 2, 0:length, :], r.wa[layer, :, 0 : 3 * width], NT))

    def keep(name, half, place, value):
        own = getattr(r, "own" + name)
        own[:, :, half, :, place] = value.astype(LOW).reshape(chips, SECTIONS, rows_a // SECTIONS, value.shape[1])

    def chip_rows(value):
        return value.reshape(chips * rows_a, 2 * length)

    def grad_down(at):
        own = getattr(r, "ownB%d" % at)
        taken(base + at, r.dft.at[at, :, other])
        for chip in range(chips):
            taken(6 + chips * at + chip, r.gc.at[at, chip, other, :])
            value = product(r.dft[at], r.gc[at, chip], NN)
            own[chip] = value.astype(LOW).reshape(SECTIONS, 2, half_b, rows_b)

    def grad_up(layer):
        at = layer // 2
        taken(layer, r.xtc.at[layer, :, :, other])
        for index in range(hidden // width):
            place = pl.ds(index * width, width)
            taken(base + 2 + chips * at + index, r.dh.at[at, other, place])
            value = product(chip_rows(r.xtc[layer]), r.dh[at, :, place], NN)
            keep("F%d" % layer, index // 2, pl.ds(index % 2 * width, width), value)

    def grad_output(layer):
        at = layer // 2
        taken(4 + at, r.otc.at[at, :, :, other])
        taken(base + 2 + 2 * chips + at, r.df.at[at, other])
        for half in range(2):
            place = pl.ds(half * width // 2, width // 2)
            value = product(chip_rows(r.otc[at]), r.df[at, :, place], NN)
            keep("O%d" % layer, half, pl.ds(0, width // 2), value)

    def grad_packed(layer):
        at = layer // 2
        slot = base + 4 + 2 * chips + 2 * at
        taken(layer, r.xtc.at[layer, :, :, other])
        taken(slot, r.dp.at[at, other, pl.ds(width, 2 * width)])
        taken(slot + 1, r.dp.at[at, other, pl.ds(0, width)])
        part = 3 * width // 2
        for half in range(2):
            value = product(chip_rows(r.xtc[layer]), r.dp[at, :, half * part : (half + 1) * part], NN)
            keep("K%d" % layer, half, pl.ds(0, part), value)

    def joined(target, others):
        return functools.reduce(
            lambda left, right: left + right, [ref[...].astype(WIDE) for ref in (target, *others)]
        )

    def add_into(target, others):
        if len(others) == 1:
            target[...] = target[...] + others[0][...]
        else:
            target[...] = joined(target, others).astype(LOW)

    places = {name: place for place, (name, _, _, _) in enumerate(grad_items)}

    def buffers(name):
        parts = ("own", "farx", "fary", "nearx", "neary", "line", "done")
        return types.SimpleNamespace(**{part: getattr(r, part + name) for part in parts})

    def to_plane(name):
        item, place = buffers(name), places[name]

        def over_x(section, half, target, slot):
            push(item.own.at[:, section, half], target, r.px_s.at[place, slot], r.px_r.at[place, slot], to_x)
            at_end(None, item.farx, r.px_s.at[place, slot])

        def over_y(section, half, target, slot):
            push(item.own.at[:, section, half], target, r.py_s.at[place, slot], r.py_r.at[place, slot], to_y)
            at_end(None, item.farx, r.py_s.at[place, slot])

        over_x(sd, 0, item.farx, 2)
        over_y(sd, 1, item.fary, 2)
        over_x(sx, 0, item.nearx.at[0], 0)
        over_y(sy, 1, item.neary.at[1], 1)

    def through_plane(name):
        item, place = buffers(name), places[name]
        own = item.own
        arrived(item.fary, r.py_r.at[place, 2])
        add_into(own.at[:, sx, 1], [item.fary])
        push(own.at[:, sx, 1], item.nearx.at[1], r.px_s.at[place, 1], r.px_r.at[place, 1], to_x)
        at_end(None, item.farx, r.px_s.at[place, 1])
        arrived(item.farx, r.px_r.at[place, 2])
        add_into(own.at[:, sy, 0], [item.farx])
        push(own.at[:, sy, 0], item.neary.at[0], r.py_s.at[place, 0], r.py_r.at[place, 0], to_y)
        at_end(None, item.farx, r.py_s.at[place, 0])

    def to_line(name):
        item, place = buffers(name), places[name]
        own = item.own.at[:, s]
        for half in range(2):
            arrived(item.nearx.at[half], r.px_r.at[place, half])
            arrived(item.neary.at[half], r.py_r.at[place, half])
            add_into(own.at[:, half], [item.nearx.at[half], item.neary.at[half]])
        for step in range(1, chips):
            chip = lax.rem(z + step, chips)
            push(
                own.at[chip],
                item.line.at[z],
                r.line_s.at[place, step],
                r.line_r.at[place, z],
                {"dp": 2 * chip + c},
            )
            at_end(None, item.line.at[0], r.line_s.at[place, step])

    def to_owner(name):
        item, place = buffers(name), places[name]
        others = [lax.rem(z + step, chips) for step in range(1, chips)]
        for chip in others:
            arrived(item.line.at[chip], r.line_r.at[place, chip])
        total = joined(item.own.at[z, s], [item.line.at[chip] for chip in others])
        square = total * total
        while square.ndim > 2:
            square = jnp.sum(square, 0)
        square = jnp.sum(jnp.sum(square, 0, keepdims=True), 1, keepdims=True)
        r.sum[...] = r.sum[...] + jnp.broadcast_to(square, (8, LANES))
        if name[0] == "B":
            item.done[...] = total
            return
        item.done[s] = total.astype(LOW)
        layer = grad_items[place][1]
        mine = item.done.at[s]
        away = s != layer
        when(
            away,
            lambda: push(mine, mine, r.done_s.at[place], r.done_r.at[place, s], {"section": jnp.int32(layer)}),
        )
        at_end(away, mine, r.done_s.at[place])

    def collect(name):
        item, place = buffers(name), places[name]
        layer = grad_items[place][1]

        def work():
            for section in range(SECTIONS):
                if section != layer:
                    arrived(item.done.at[section], r.done_r.at[place, section])
            columns = item.done.shape[-1]
            start = 3 * width if name[0] == "O" else 0
            for section in range(SECTIONS):
                for half in range(2):
                    rows = pl.ds(section * (rows_a // SECTIONS), rows_a // SECTIONS)
                    place_to = pl.ds(start + half * columns, columns)
                    r.grad_a[rows, place_to] = item.done[section, half].astype(WIDE)

        when(s == layer, work)

    def all_sent():
        for condition, source, sem in finish:
            when(condition, functools.partial(sent, source, sem))
        finish.clear()

    small_out(0, r.tiles.at[d, s])
    start_line(0)
    spread_plane(0, z)
    rows_plane()
    line_step(0, 1)
    rows_relay()
    line_step(0, 2)
    rows_line()
    start_line(2)
    for step in range(3, chips):
        line_step(0, step)
    small_group(0, r.tiles.at[pl.ds(0, devices - 1), 0])
    for peer in plane:
        push(r.tiles.at[:, s], r.tiles.at[:, s], r.small_s.at[0, 1], r.small_r.at[0, 1], peer)
    prepare_masks()
    rows_step(1)
    plane_step(0)
    for step in range(2, chips):
        rows_step(step)
    spread_plane(2, z)
    for step in range(1, chips):
        line_step(2, step)
    own_x.wait()
    own_cot.wait()
    relay_step(0)
    small_plane(0, r.tiles.at[:, pl.ds(0, SECTIONS - 1)])
    for slot in range(4):
        arrived(whole_a, r.gs_r.at[slot])
    attention(0)
    normalize(0)
    expand(1)
    arrived(whole_b, r.gs_r.at[4])
    contract(1)
    normalize(1)
    plane_step(2)
    attention(2)
    normalize(2)
    expand(3)
    gather_sends(0)
    for slot in range(5):
        at_end(None, whole_a if slot < 4 else whole_b, r.gs_s.at[slot])
    all_sent()
    relay_step(2)
    arrived(whole_b, r.gs_r.at[5])
    contract(3)
    normalize(3)

    r.sum[...] = jnp.zeros((8, LANES), WIDE)
    back_normalize(3)
    back_hidden(3)
    back_expand_end(3)
    give_rows(3)
    grad_down(1)
    to_plane("B1")
    back_normalize(2)
    back_output(2)
    grad_up(3)
    to_plane("F3")
    back_heads(2, 0, 2)
    through_plane("B1")
    back_heads(2, 2, 2)
    give_rows(2)
    through_plane("F3")
    back_packed(2)
    grad_output(2)
    to_plane("O2")
    back_packed_end(2)
    back_normalize(1)
    back_hidden(1)
    give_rows(1)
    to_line("B1")
    through_plane("O2")
    to_line("F3")
    grad_packed(2)
    to_plane("K2")
    grad_down(0)
    to_plane("B0")
    to_line("O2")
    back_expand_end(1)
    back_normalize(0)
    small_out(1, r.ng.at[d])
    back_output(0)
    give_rows(0)
    through_plane("K2")
    back_heads(0, 0, 2)
    through_plane("B0")
    grad_up(1)
    to_plane("F1")
    back_heads(0, 2, 2)
    to_line("K2")
    grad_output(0)
    to_plane("O0")
    back_packed(0)
    to_line("B0")
    to_owner("B1")
    to_owner("F3")
    to_owner("O2")
    through_plane("F1")
    grad_packed(0)
    to_plane("K0")
    through_plane("O0")
    back_packed_end(0)
    to_owner("K2")
    to_line("F1")
    to_owner("B0")
    gather_sends(2)
    at_end(None, whole_b, r.gs_s.at[5])
    all_sent()
    through_plane("K0")
    to_line("O0")
    small_group(1, r.ng.at[pl.ds(0, devices - 1)])
    r.ns[s] = functools.reduce(lambda left, right: left + right, [r.ng[index] for index in range(devices)])
    small_plane_out(1, r.ns.at[s])
    to_line("K0")
    to_owner("F1")
    to_owner("O0")
    for name in ("F3", "O2", "K2", "F1"):
        collect(name)
    collect("O0")
    for layer in range(2):
        done = buffers("B%d" % layer).done
        r.grad_b[layer] = done[...].reshape(cols_b, rows_b).T
    small_plane(1, r.ns.at[pl.ds(0, SECTIONS - 1)])
    grads = functools.reduce(lambda left, right: left + right, [r.ns[index] for index in range(SECTIONS)])
    norm_square = jnp.sum(jnp.sum(grads * grads, 0, keepdims=True), 1, keepdims=True)
    chosen = jnp.zeros((2, width), WIDE)
    for layer in range(4):
        chosen = jnp.where(s == layer, grads[2 * layer : 2 * layer + 2, :], chosen)
    for chip in range(chips):
        pair_of = chosen[:, chip * LANES : (chip + 1) * LANES]
        r.grad_n[...] = jnp.where(
            z == chip, jnp.where(c == 0, pair_of[:, :rows_a], pair_of[:, rows_a:]), r.grad_n[...]
        )
    to_owner("K0")

    r.sq[d] = r.sum[...]
    small_out(2, r.sq.at[d])
    collect("K0")
    small_group(2, r.sq.at[pl.ds(0, devices - 1)])
    r.sqs[s] = functools.reduce(lambda left, right: left + right, [r.sq[index] for index in range(devices)])
    small_plane_out(2, r.sqs.at[s])
    all_sent()
    small_plane(2, r.sqs.at[pl.ds(0, SECTIONS - 1)])
    squares = functools.reduce(lambda left, right: left + right, [r.sqs[index] for index in range(SECTIONS)])
    r.square[...] = squares + norm_square


def step_call(tokens, cotangent, lengths, mat_a, mat_b, norms):
    rows_a, hidden = mat_a.shape[1:]
    rows_b, cols_b = mat_b.shape[1:]
    width = tokens.shape[1]
    length = tokens.shape[0] // lengths.shape[0]
    chips = width // rows_a // 2
    scratch = kernel_scratch(chips, rows_a, rows_b, cols_b, length, width, hidden)
    shapes = []
    for _, shape, kind in scratch:
        shapes.append(pltpu.SemaphoreType.DMA(shape) if kind is None else pltpu.VMEM(shape, kind))
    anywhere, vmem = pl.BlockSpec(memory_space=pl.ANY), pl.BlockSpec(memory_space=pltpu.VMEM)
    return pl.pallas_call(
        functools.partial(step_kernel, INPUTS + OUTPUTS + tuple(name for name, _, _ in scratch)),
        out_shape=(
            jax.ShapeDtypeStruct((rows_a, hidden), WIDE),
            jax.ShapeDtypeStruct(mat_b.shape, WIDE),
            jax.ShapeDtypeStruct((2, rows_a), WIDE),
            jax.ShapeDtypeStruct((8, LANES), WIDE),
            jax.ShapeDtypeStruct((length, width), LOW),
            jax.ShapeDtypeStruct((length, width), WIDE),
        ),
        in_specs=[anywhere, anywhere, pl.BlockSpec(memory_space=pltpu.SMEM), vmem, vmem, vmem],
        out_specs=[vmem] * len(OUTPUTS),
        scratch_shapes=shapes,
        compiler_params=pltpu.CompilerParams(
            collective_id=0, has_side_effects=True, vmem_limit_bytes=KERNEL_VMEM
        ),
    )(tokens, cotangent, lengths, mat_a, mat_b, norms)


def update_kernel(*refs):
    square, output, input_grad = (ref[...] for ref in refs[:3])
    grad_norm = jnp.sqrt(square[0:1, 0:1])
    factor = CLIP_NORM / jnp.maximum(grad_norm, CLIP_NORM)
    inputs, outputs = refs[3:15], refs[15:]
    outputs[0][...] = grad_norm
    outputs[1][0] = output
    outputs[2][0] = input_grad
    for group, (rate, decay) in enumerate(
        ((MATRIX_RATE, MATRIX_DECAY), (MATRIX_RATE, MATRIX_DECAY), (NORM_RATE, 0.0))
    ):
        grad, weight, one, two = inputs[4 * group : 4 * group + 4]
        clip = grad[...].reshape(weight.shape) * factor
        moment, square_new, master = adam_update(weight[...], one[...], two[...], clip, rate, decay)
        for ref, value in zip(
            outputs[3 + 5 * group : 8 + 5 * group], (clip, moment, square_new, master, master.astype(LOW))
        ):
            ref[...] = value


def kernel_body(
    tokens, cotangent, lengths, mat_a, mat_b, norms, first_a, second_a, first_b, second_b, first_n, second_n
):
    norms, first_n, second_n = (jnp.swapaxes(value, 1, 2) for value in (norms, first_n, second_n))
    grad_a, grad_b, grad_n, square, output, input_grad = step_call(
        tokens, cotangent, lengths, mat_a, mat_b, norms
    )
    steps = 4

    def cut(value, dim):
        shape = tuple(size // steps if at == dim else size for at, size in enumerate(value.shape))
        return pl.BlockSpec(shape, lambda step: tuple(step if at == dim else 0 for at in range(len(shape))))

    def whole(value):
        return pl.BlockSpec(value.shape, lambda step: (0,) * len(value.shape))

    def like(value, kind=WIDE):
        return jax.ShapeDtypeStruct(value.shape, kind)

    args = (square, output, input_grad, grad_a, mat_a, first_a, second_a, grad_b, mat_b, first_b, second_b)
    specs = [whole(square), cut(output, 0), cut(input_grad, 0)]
    specs += [cut(grad_a, 0)] + [cut(mat_a, 1)] * 3 + [cut(grad_b, 1)] * 4
    args += (grad_n, norms, first_n, second_n)
    specs += [whole(grad_n)] + [whole(norms)] * 3
    shapes = [jax.ShapeDtypeStruct((1, 1), WIDE), like(output[None], LOW), like(input_grad[None])]
    out_specs = [whole(shapes[0]), cut(shapes[1], 1), cut(shapes[2], 1)]
    for value, spec in ((mat_a, cut(mat_a, 1)), (mat_b, cut(mat_b, 1)), (norms, whole(norms))):
        shapes += [like(value)] * 4 + [like(value, LOW)]
        out_specs += [spec] * 5
    results = pl.pallas_call(
        update_kernel,
        grid=(steps,),
        out_shape=shapes,
        in_specs=specs,
        out_specs=out_specs,
        compiler_params=pltpu.CompilerParams(vmem_limit_bytes=KERNEL_VMEM),
    )(*args)
    results = [results[0][0, 0], *results[1:]]
    results[-5:] = [jnp.swapaxes(value, 1, 2) for value in results[-5:]]
    return tuple(results)


def chosen_body(*args):
    rows_a = args[3].shape[1]
    groups = lax.axis_size("dp")
    by_kernel = rows_a % 32 == 0 and 2 * rows_a == LANES and groups * rows_a == args[0].shape[1]
    return (kernel_body if by_kernel else body)(*args)


def solution(mesh):
    placed = (
        P("dp", None),
        P("dp", None),
        P("dp", None),
        P("section", "dp", None),
        P(None, "dp", "section"),
        P("section", "dp", None),
        P("section", "dp", None),
        P("section", "dp", None),
        P(None, "dp", "section"),
        P(None, "dp", "section"),
        P("section", "dp", None),
        P("section", "dp", None),
    )
    return jax.shard_map(
        chosen_body,
        mesh=mesh,
        in_specs=placed,
        out_specs=(
            P(),
            P("section", "dp", None),
            P("section", "dp", None),
            P("section", "dp", None),
            P("section", "dp", None),
            P("section", "dp", None),
            P("section", "dp", None),
            P("section", "dp", None),
            P(None, "dp", "section"),
            P(None, "dp", "section"),
            P(None, "dp", "section"),
            P(None, "dp", "section"),
            P(None, "dp", "section"),
            P("section", "dp", None),
            P("section", "dp", None),
            P("section", "dp", None),
            P("section", "dp", None),
            P("section", "dp", None),
        ),
        check_vma=False,
    )
```

```python
import functools
import types

import jax
import jax.numpy as jnp
from jax import lax
from jax.experimental import pallas as pl
from jax.experimental.pallas import tpu as pltpu
from jax.sharding import PartitionSpec as P

HEADS = 8
STEP = 5


EPSILON = 1e-05
NEGATIVE = -1e30
CLIP_NORM = 1.0
BETA_ONE = 0.5
BETA_TWO = 0.5
ADAM_EPSILON = 1e-08
MATRIX_RATE = 0.05
NORM_RATE = 0.5
MATRIX_DECAY = 0.01


def norm_stats(value):
    centre = value - jnp.mean(value, -1, keepdims=True)
    inverse = lax.rsqrt(jnp.mean(centre * centre, -1, keepdims=True) + EPSILON)
    return (centre * inverse, inverse)


def norm_back(normal, inverse, upstream):
    return inverse * (
        upstream
        - jnp.mean(upstream, -1, keepdims=True)
        - normal * jnp.mean(upstream * normal, -1, keepdims=True)
    )


def adam_update(weight, moment_one, moment_two, gradient, step_rate, decay_rate):
    first_new = BETA_ONE * moment_one + (1.0 - BETA_ONE) * gradient
    second_new = BETA_TWO * moment_two + (1.0 - BETA_TWO) * gradient * gradient
    first_hat = first_new / (1.0 - BETA_ONE**STEP)
    second_hat = second_new / (1.0 - BETA_TWO**STEP)
    weight_new = weight - step_rate * (
        first_hat / (jnp.sqrt(second_hat) + ADAM_EPSILON) + decay_rate * weight
    )
    return (first_new, second_new, weight_new)


def segments_of(lengths_row, length):
    ends = jnp.cumsum(lengths_row, dtype=jnp.int32)
    places = jnp.arange(length, dtype=jnp.int32)
    segment = jnp.sum((ends[None, :] <= places[:, None]).astype(jnp.int32), axis=1, dtype=jnp.int32)
    live = (places < ends[-1]).astype(jnp.float32)
    return segment, live


def matmul(left, right, dims):
    return lax.dot_general(left, right, (dims, ((), ())), preferred_element_type=jnp.float32)


NN = ((1,), (0,))
NT = ((1,), (1,))
TN = ((0,), (0,))


def attention_forward(stream, weight, mask):
    length, width = stream.shape
    size = width // HEADS
    packed = matmul(stream, weight[:, : 3 * width], NN).astype(jnp.bfloat16)
    heads = packed.reshape(length, 3, HEADS, size)
    scores = jnp.einsum("qhd,khd->hqk", heads[:, 0], heads[:, 1], preferred_element_type=jnp.float32)
    scores = jnp.where(mask[None], scores * size**-0.5, NEGATIVE)
    weights = jnp.exp(scores - jnp.max(scores, -1, keepdims=True))
    probs = weights / jnp.sum(weights, -1, keepdims=True)
    mixed = jnp.einsum("hqk,khd->qhd", probs.astype(jnp.bfloat16), heads[:, 2], preferred_element_type=jnp.float32)
    mixed = mixed.reshape(length, width).astype(jnp.bfloat16)
    branch = matmul(mixed, weight[:, 3 * width :], NN)
    return branch, (heads, probs, mixed)


def attention_backward(stream, weight, kept, grad_low):
    heads, probs, mixed = kept
    length, width = stream.shape
    size = width // HEADS
    grad_out = matmul(mixed, grad_low, TN)
    grad_mixed = matmul(grad_low, weight[:, 3 * width :], NT).astype(jnp.bfloat16)
    grad_mixed = grad_mixed.reshape(length, HEADS, size)
    grad_probs = jnp.einsum("qhd,khd->hqk", grad_mixed, heads[:, 2], preferred_element_type=jnp.float32)
    centre = jnp.sum(probs * grad_probs, -1, keepdims=True)
    grad_scores = (probs * (grad_probs - centre)).astype(jnp.bfloat16)
    low = probs.astype(jnp.bfloat16)
    scale = size**-0.5
    grad_q = jnp.einsum("hqk,khd->qhd", grad_scores, heads[:, 1], preferred_element_type=jnp.float32) * scale
    grad_k = jnp.einsum("hqk,qhd->khd", grad_scores, heads[:, 0], preferred_element_type=jnp.float32) * scale
    grad_v = jnp.einsum("hqk,qhd->khd", low, grad_mixed, preferred_element_type=jnp.float32)
    packed = jnp.concatenate([grad_q, grad_k, grad_v], axis=1).reshape(length, 3 * width)
    packed = packed.astype(jnp.bfloat16)
    grad_in = matmul(stream, packed, TN)
    grad_inputs = matmul(packed, weight[:, : 3 * width], NT)
    return grad_inputs, jnp.concatenate([grad_in, grad_out], axis=1)


def feed_forward(stream, weight, down):
    pre = matmul(stream, weight, NN)
    active = jax.nn.gelu(pre, approximate=True).astype(jnp.bfloat16)
    return matmul(active, down, NN), (pre, active)


def feed_backward(stream, weight, down, kept, grad_low):
    pre, active = kept
    grad_down = matmul(active, grad_low, TN)
    grad_active = matmul(grad_low, down, NT)
    pull = jax.vjp(lambda value: jax.nn.gelu(value, approximate=True), pre)[1]
    grad_pre = pull(grad_active)[0].astype(jnp.bfloat16)
    grad_up = matmul(stream, grad_pre, TN)
    return matmul(grad_pre, weight, NT), grad_up, grad_down


def micro_step(rows, pull, segment, mats, downs, gains, biases):
    low = jnp.bfloat16
    mask = segment[:, None] == segment[None, :]
    stream, dual = rows, jnp.zeros_like(rows)
    saved = []
    for sub in range(4):
        if sub % 2 == 0:
            branch, kept = attention_forward(stream, mats[sub], mask)
        else:
            branch, kept = feed_forward(stream, mats[sub], downs[sub // 2])
        normal, inverse = norm_stats(stream.astype(jnp.float32) + branch)
        out = normal * gains[sub] + biases[sub]
        total = dual.astype(jnp.float32) + branch
        saved.append((stream, kept, normal, inverse))
        if sub < 3:
            stream, dual = out.astype(low), total.astype(low)
    dual_normal, dual_inverse = norm_stats(total)
    output = (out + dual_normal).astype(low)
    grad_out, grad_dual = pull, norm_back(dual_normal, dual_inverse, pull)
    grads_a, grads_b, grads_n = [None] * 4, [None] * 2, [None] * 4
    for sub in (3, 2, 1, 0):
        stream, kept, normal, inverse = saved[sub]
        grads_n[sub] = jnp.stack([jnp.sum(grad_out * normal, 0), jnp.sum(grad_out, 0)], axis=1)
        summed = norm_back(normal, inverse, grad_out * gains[sub])
        branch_low = (summed + grad_dual).astype(low)
        if sub % 2 == 0:
            inner, grads_a[sub] = attention_backward(stream, mats[sub], kept, branch_low)
        else:
            inner, grads_a[sub], grads_b[sub // 2] = feed_backward(
                stream, mats[sub], downs[sub // 2], kept, branch_low
            )
        grad_in = summed + inner
        if sub > 0:
            grad_out = grad_in.astype(low).astype(jnp.float32)
            grad_dual = grad_dual.astype(low).astype(jnp.float32)
    return output, grad_in, jnp.stack(grads_a), jnp.stack(grads_b), jnp.stack(grads_n)


def finish_step(grad_norm, output, input_grad, *groups):
    factor = CLIP_NORM / jnp.maximum(grad_norm, CLIP_NORM)
    results = [grad_norm, output[None], input_grad[None]]
    for weight, one, two, grad, rate, decay in groups:
        clip = grad * factor
        moment, square_new, master = adam_update(weight, one, two, clip, rate, decay)
        results += [clip, moment, square_new, master, master.astype(jnp.bfloat16)]
    return tuple(results)


def body(
    tokens, cotangent, lengths, mat_a, mat_b, norms, first_a, second_a, first_b, second_b, first_n, second_n
):
    low = jnp.bfloat16
    own = lax.axis_index("section")
    length = tokens.shape[0] // lengths.shape[0]
    rows = lax.dynamic_slice_in_dim(tokens, own * length, length, 0)
    segment, live = segments_of(lax.dynamic_index_in_dim(lengths, own, 0, keepdims=False), length)
    pull = lax.dynamic_slice_in_dim(cotangent, own * length, length, 0).astype(jnp.float32) * live[:, None]

    def gathered(value):
        return lax.all_gather(lax.all_gather(value, "dp", axis=1, tiled=True), "section", axis=0, tiled=True)

    mats = gathered(mat_a.astype(low))
    scales = gathered(norms.astype(low)).astype(jnp.float32)
    downs = lax.all_gather(mat_b.astype(low), "section", axis=2, tiled=True)
    downs = lax.all_gather(downs, "dp", axis=1, tiled=True)
    output, input_grad, part_a, part_b, part_n = micro_step(
        rows, pull, segment, mats, downs, scales[:, :, 0], scales[:, :, 1]
    )

    def scattered(value, section_dim):
        value = lax.psum_scatter(value, "section", scatter_dimension=section_dim, tiled=True)
        return lax.psum_scatter(value, "dp", scatter_dimension=1, tiled=True).astype(jnp.float32)

    grad_a = scattered(part_a.astype(low), 0)
    grad_b = scattered(part_b.astype(low), 2)
    grad_n = scattered(part_n, 0)
    square = jnp.sum(grad_a * grad_a) + jnp.sum(grad_b * grad_b) + jnp.sum(grad_n * grad_n)
    grad_norm = jnp.sqrt(lax.psum(square, ("section", "dp")))
    return finish_step(
        grad_norm, output, input_grad,
        (mat_a, first_a, second_a, grad_a, MATRIX_RATE, MATRIX_DECAY),
        (mat_b, first_b, second_b, grad_b, MATRIX_RATE, MATRIX_DECAY),
        (norms, first_n, second_n, grad_n, NORM_RATE, 0.0),
    )


LOW = jnp.bfloat16
WIDE = jnp.float32
MESH = pl.DeviceIdType.MESH
SECTIONS = 4
LANES = 128
BLOCK = 64
ROWS_FIRST = (5,)
KERNEL_VMEM = 64 * 1024 * 1024 - 256 * 1024


def gradient_items(rows_a, rows_b, cols_b, width, hidden):
    part = rows_a // SECTIONS
    return (
        ("B1", 3, cols_b // 2, rows_b),
        ("F3", 3, part, hidden // 2),
        ("O2", 2, part, width // 2),
        ("K2", 2, part, 3 * width // 2),
        ("B0", 1, cols_b // 2, rows_b),
        ("F1", 1, part, hidden // 2),
        ("O0", 0, part, width // 2),
        ("K0", 0, part, 3 * width // 2),
    )


def item_scratch(name, chips, rows, columns):
    piece = (rows, columns)
    return (
        ("own" + name, (chips, SECTIONS, 2) + piece, LOW),
        ("farx" + name, (chips,) + piece, LOW),
        ("fary" + name, (chips,) + piece, LOW),
        ("nearx" + name, (2, chips) + piece, LOW),
        ("neary" + name, (2, chips) + piece, LOW),
        ("line" + name, (chips, 2) + piece, LOW),
        ("done" + name, (2,) + piece if name[0] == "B" else (SECTIONS, 2) + piece, WIDE if name[0] == "B" else LOW),
    )


def kernel_scratch(chips, rows_a, rows_b, cols_b, length, width, hidden):
    devices = 2 * chips
    items = gradient_items(rows_a, rows_b, cols_b, width, hidden)
    count = len(items)
    received = sum((item_scratch(name, chips, rows, columns) for name, _, rows, columns in items), ())
    return received + (
        ("fac_s", (32,), None),
        ("fac_r", (32,), None),
        ("px_s", (count, 3), None),
        ("px_r", (count, 3), None),
        ("py_s", (count, 3), None),
        ("py_r", (count, 3), None),
        ("line_s", (count, chips), None),
        ("line_r", (count, chips), None),
        ("done_s", (count,), None),
        ("done_r", (count, SECTIONS), None),
        ("wa", (4, chips, 2, SECTIONS, rows_a // SECTIONS, hidden), LOW),
        ("wb", (2, chips, 2, rows_b, width), LOW),
        ("cut", (SECTIONS, rows_a // SECTIONS, hidden), LOW),
        ("tiles", (devices, SECTIONS, 8, LANES), WIDE),
        ("x", (4, length, width), LOW),
        ("xt", (4, chips, 2, rows_a, length), LOW),
        ("xtc", (4, chips, rows_a, 2 * length), LOW),
        ("y", (length, width), LOW),
        ("cot", (length, width), LOW),
        ("bias", (length, length), WIDE),
        ("live", (length, 1), WIDE),
        ("f", (length, width), WIDE),
        ("n", (4, length, width), WIDE),
        ("inv", (4, length, 1), WIDE),
        ("q", (2, length, width), LOW),
        ("k", (2, length, width), LOW),
        ("v", (2, length, width), LOW),
        ("kt", (2, width, length), LOW),
        ("vt", (2, width, length), LOW),
        ("ot", (2, chips, 2, rows_a, length), LOW),
        ("otc", (2, chips, rows_a, 2 * length), LOW),
        ("pt", (2, HEADS, length, length), LOW),
        ("g", (2, length, hidden), LOW),
        ("gc", (2, chips, 2 * length, rows_b), LOW),
        ("slope", (2, length, hidden), LOW),
        ("gx", (length, width), WIDE),
        ("gy", (length, width), WIDE),
        ("df", (2, 2 * length, width), LOW),
        ("dft", (2, width, 2 * length), LOW),
        ("dm", (length, width), LOW),
        ("dqt", (width, length), LOW),
        ("dh", (2, 2 * length, hidden), LOW),
        ("dp", (2, 2 * length, 3 * width), LOW),
        ("ng", (devices, 8, width), WIDE),
        ("ns", (SECTIONS, 8, width), WIDE),
        ("sq", (devices, 8, LANES), WIDE),
        ("sqs", (SECTIONS, 8, LANES), WIDE),
        ("sum", (8, LANES), WIDE),
        ("in_s", (2,), None),
        ("cut_s", (1,), None),
        ("cut_r", (SECTIONS,), None),
        ("gz_s", (6,), None),
        ("gz_r", (6, chips), None),
        ("gx_s", (6,), None),
        ("gx_r", (6,), None),
        ("gy_s", (6,), None),
        ("gy_r", (6,), None),
        ("rx_s", (6,), None),
        ("rx_r", (6,), None),
        ("ry_s", (6,), None),
        ("ry_r", (6,), None),
        ("gs_s", (6,), None),
        ("gs_r", (6,), None),
        ("small_s", (3, 2), None),
        ("small_r", (3, 2), None),
    )


INPUTS = ("tokens", "cotangent", "lengths", "mat_a", "mat_b", "norms")
OUTPUTS = ("grad_a", "grad_b", "grad_n", "square", "output", "input_grad")


def step_kernel(names, *refs):
    r = types.SimpleNamespace(**dict(zip(names, refs)))
    length, width = r.x.shape[1:]
    hidden = r.wa.shape[-1]
    rows_a, (rows_b, cols_b) = r.mat_a.shape[1], r.mat_b.shape[1:]
    devices = r.tiles.shape[0]
    chips = devices // 2
    half_b = cols_b // 2
    grad_items = gradient_items(rows_a, rows_b, cols_b, width, hidden)
    head = width // HEADS
    scale = head**-0.5

    s, d = lax.axis_index("section"), lax.axis_index("dp")
    z, c = lax.div(d, 2), lax.rem(d, 2)
    sx = s + 1 - 2 * lax.rem(s, 2)
    sy = lax.rem(s + 2, SECTIONS)
    sd = SECTIONS - 1 - s
    to_sibling = {"dp": d + 1 - 2 * c}
    to_up, to_down = {"dp": d + 2}, {"dp": d - 2}
    to_x, to_y = {"section": sx}, {"section": sy}
    below, above = z > 0, z < chips - 1
    group = [{"dp": lax.rem(d + step, devices)} for step in range(1, devices)]
    plane = [{"section": lax.rem(s + step, SECTIONS)} for step in range(1, SECTIONS)]
    finish = []

    def when(condition, work):
        if condition is None:
            work()
        else:
            pl.when(condition)(work)

    def push(source, target, send_sem, recv_sem, device):
        pltpu.make_async_remote_copy(
            src_ref=source,
            dst_ref=target,
            send_sem=send_sem,
            recv_sem=recv_sem,
            device_id=device,
            device_id_type=MESH,
        ).start()

    def arrived(target, sem):
        pltpu.make_async_remote_copy(
            src_ref=target, dst_ref=target, send_sem=sem, recv_sem=sem, device_id=to_x, device_id_type=MESH
        ).wait_recv()

    def sent(source, sem):
        pltpu.make_async_remote_copy(
            src_ref=source, dst_ref=source, send_sem=sem, recv_sem=sem, device_id=to_x, device_id_type=MESH
        ).wait_send()

    def at_end(condition, source, sem):
        finish.append((condition, source, sem))

    def aligned(start, size):
        return pl.ds(pl.multiple_of(start, size), size)

    own_x = pltpu.make_async_copy(r.tokens.at[aligned(s * length, length)], r.x.at[0], r.in_s.at[0])
    own_cot = pltpu.make_async_copy(r.cotangent.at[aligned(s * length, length)], r.cot, r.in_s.at[1])
    own_x.start()
    own_cot.start()
    barrier = pltpu.get_barrier_semaphore()
    for peer in group + plane:
        pl.semaphore_signal(barrier, inc=1, device_id=peer, device_id_type=MESH)
    r.cut[...] = r.mat_a[0].astype(LOW).reshape(SECTIONS, rows_a // SECTIONS, hidden)
    r.wa[s, z, c, s] = r.cut[s]
    for layer in range(2):
        r.wb[layer, z, c, :, aligned(s * cols_b, cols_b)] = r.mat_b[layer].astype(LOW)
    norms = r.norms[0].astype(LOW).astype(WIDE)
    nothing = jnp.zeros((2, rows_a), WIDE)
    even = jnp.concatenate([norms, nothing], axis=1)
    odd = jnp.concatenate([nothing, norms], axis=1)
    r.tiles[d, s, 0:2, :] = jnp.where(c == 0, even, odd)
    r.tiles[d, s, 2:8, :] = jnp.zeros((6, LANES), WIDE)
    pl.semaphore_wait(barrier, len(group) + len(plane))

    def small_out(which, source):
        for peer in group:
            push(source, source, r.small_s.at[which, 0], r.small_r.at[which, 0], peer)

    def small_group(which, like):
        arrived(like, r.small_r.at[which, 0])
        sent(like, r.small_s.at[which, 0])

    def small_plane_out(which, source):
        for peer in plane:
            push(source, source, r.small_s.at[which, 1], r.small_r.at[which, 1], peer)

    def small_plane(which, like):
        arrived(like, r.small_r.at[which, 1])
        sent(like, r.small_s.at[which, 1])

    every = slice(None)

    def block(item, chip, section):
        if item < 4:
            return r.wa.at[item, chip, c, section]
        return r.wb.at[item - 4, chip, c, :, aligned(section * cols_b, cols_b)]

    def half_block(item, section, half):
        if item < 4:
            return r.wa.at[item, :, c, section, :, pl.ds(half * hidden // 2, hidden // 2)]
        rows = pl.ds(half * rows_b // 2, rows_b // 2)
        return r.wb.at[item - 4, :, c, rows, aligned(section * cols_b, cols_b)]

    def half_piece(item, section, half):
        rows = pl.ds(half * rows_b // 2, rows_b // 2)
        return r.wb.at[item - 4, z, c, rows, aligned(section * cols_b, cols_b)]

    def core_blocks(item, core):
        return r.wa.at[item, :, core] if item < 4 else r.wb.at[item - 4, :, core]

    def cut_out():
        for section, device in ((sd, {"section": sd}), (sx, to_x), (sy, to_y)):
            push(r.cut.at[section], r.wa.at[s, z, c, section], r.cut_s.at[0], r.cut_r.at[s], device)
        at_end(None, r.cut.at[pl.ds(0, SECTIONS - 1)], r.cut_s.at[0])

    def cut_in():
        for section in (sx, sy, sd):
            arrived(r.wa.at[section, z, c, s], r.cut_r.at[section])

    def line_out(item):
        if item in ROWS_FIRST:
            rows_out(item)
            return
        own = block(item, z, s)
        for step in range(1, chips):
            push(own, own, r.gz_s.at[item], r.gz_r.at[item, z], {"dp": 2 * lax.rem(z + step, chips) + c})
        several = block(item, pl.ds(0, chips - 1), s)
        at_end(None, several, r.gz_s.at[item])

    def plane_out(item, chip):
        own = block(item, chip, s)
        push(own, own, r.gx_s.at[item], r.gx_r.at[item], to_x)
        push(own, own, r.gy_s.at[item], r.gy_r.at[item], to_y)

    def rows_out(item):
        arrived(half_piece(item, sd, 0), r.rx_r.at[item])
        arrived(half_piece(item, sd, 1), r.ry_r.at[item])
        rows = r.wb.at[item - 4, z, c]
        for step in range(1, chips):
            push(rows, rows, r.gz_s.at[item], r.gz_r.at[item, z], {"dp": 2 * lax.rem(z + step, chips) + c})
        push(rows, rows, r.gs_s.at[item], r.gs_r.at[item], to_sibling)
        at_end(None, r.wb.at[item - 4, pl.ds(0, chips - 1), c], r.gz_s.at[item])

    def rows_in(item):
        for step in range(1, chips):
            chip = lax.rem(z + step, chips)
            rows = r.wb.at[item - 4, chip, c]
            arrived(rows, r.gz_r.at[item, chip])
            push(rows, rows, r.gs_s.at[item], r.gs_r.at[item], to_sibling)
        at_end(None, core_blocks(item, c), r.gs_s.at[item])

    def line_in(item):
        if item in ROWS_FIRST:
            rows_in(item)
            return
        for step in range(1, chips):
            chip = lax.rem(z + step, chips)
            arrived(block(item, chip, s), r.gz_r.at[item, chip])
            plane_out(item, chip)
        core_out(item, s)
        at_end(None, block(item, every, s), r.gx_s.at[item])
        at_end(None, block(item, every, s), r.gy_s.at[item])

    def core_out(item, section):
        blocks = block(item, every, section)
        push(blocks, blocks, r.gs_s.at[item], r.gs_r.at[item], to_sibling)

    def plane_in(item):
        over = z if item in ROWS_FIRST else every
        piece = half_piece if item in ROWS_FIRST else half_block
        arrived(block(item, over, sx), r.gx_r.at[item])
        part = piece(item, sx, 1)
        push(part, part, r.ry_s.at[item], r.ry_r.at[item], to_y)
        arrived(block(item, over, sy), r.gy_r.at[item])
        part = piece(item, sy, 0)
        push(part, part, r.rx_s.at[item], r.rx_r.at[item], to_x)
        if item in ROWS_FIRST:
            at_end(None, block(item, z, sx), r.gx_s.at[item])
            at_end(None, block(item, z, sx), r.gy_s.at[item])
        else:
            core_out(item, sx)
            core_out(item, sy)
        at_end(None, part, r.ry_s.at[item])
        at_end(None, part, r.rx_s.at[item])

    def far_in(item):
        arrived(half_block(item, sd, 0), r.rx_r.at[item])
        arrived(half_block(item, sd, 1), r.ry_r.at[item])
        core_out(item, sd)
        at_end(None, core_blocks(item, c), r.gs_s.at[item])

    def core_in(item):
        arrived(core_blocks(item, 1 - c), r.gs_r.at[item])

    mine, other = pl.ds(0, length), pl.ds(length, length)

    def give(slot, source, target):
        push(source, target, r.fac_s.at[slot], r.fac_r.at[slot], to_sibling)
        at_end(None, target, r.fac_s.at[slot])

    def taken(slot, target):
        arrived(target, r.fac_r.at[slot])

    def give_rows(layer):
        r.xt[layer] = r.x[layer].T.reshape(chips, 2, rows_a, length)
        r.xtc[layer, :, :, 0:length] = r.xt[layer, :, c]
        give(layer, r.xt.at[layer, :, 1 - c], r.xtc.at[layer, :, :, other])

    def product(left, right, dims):
        return lax.dot_general(left, right, (dims, ((), ())), preferred_element_type=WIDE)

    def loop(count, work):
        def one(index, carry):
            work(index)
            return carry

        lax.fori_loop(0, count, one, 0)

    def gain_row(layer, kind):
        parts = [
            r.tiles[2 * chip, layer, kind : kind + 1, :] + r.tiles[2 * chip + 1, layer, kind : kind + 1, :]
            for chip in range(chips)
        ]
        return jnp.concatenate(parts, axis=1)

    def stats(value):
        centre = value - jnp.mean(value, -1, keepdims=True)
        inverse = lax.rsqrt(jnp.mean(centre * centre, -1, keepdims=True) + EPSILON)
        return centre * inverse, inverse

    lane = lax.broadcasted_iota(jnp.int32, (1, 2 * head), 1)
    first_half = (lane < head).astype(WIDE)
    half_masks = (first_half.astype(LOW), (1.0 - first_half).astype(LOW))

    def prepare_masks():
        ends, total = [], jnp.int32(0)
        for slot in range(r.lengths.shape[1]):
            total = total + r.lengths[s, slot]
            ends.append(total)
        down_places = lax.broadcasted_iota(jnp.int32, (length, 1), 0)
        across_places = lax.broadcasted_iota(jnp.int32, (1, length), 1)
        down_segment = jnp.zeros((length, 1), jnp.int32)
        across_segment = jnp.zeros((1, length), jnp.int32)
        for end in ends:
            down_segment = down_segment + (end <= down_places).astype(jnp.int32)
            across_segment = across_segment + (end <= across_places).astype(jnp.int32)
        r.bias[...] = jnp.where(down_segment == across_segment, 0.0, NEGATIVE)
        r.live[...] = (down_places < total).astype(WIDE)

    def matrix(layer, place):
        value = r.wa[layer, :, :, :, :, place]
        return value.reshape(width, value.shape[-1])

    def attention_in(layer):
        at = layer // 2
        rows = r.x[layer]
        r.q[at] = product(rows, matrix(layer, pl.ds(0, width)), NN).astype(LOW) * jnp.asarray(scale, LOW)
        keys = product(rows, matrix(layer, pl.ds(width, width)), NN).astype(LOW)
        r.k[at] = keys
        values = product(rows, matrix(layer, pl.ds(2 * width, width)), NN).astype(LOW)
        r.v[at] = values
        r.vt[at] = values.T

    def attention_heads(layer, begin, count):
        at = layer // 2

        def pair(index):
            lanes = aligned(index * 2 * head, 2 * head)
            for which in range(2):
                scores = product(r.k[at, :, lanes], r.q[at, :, lanes] * half_masks[which], NT) + r.bias[...]
                weights = jnp.exp(scores - jnp.max(scores, 0, keepdims=True))
                probs = (weights * (1.0 / jnp.sum(weights, 0, keepdims=True))).astype(LOW)
                r.pt[at, 2 * index + which] = probs
                place = aligned((2 * index + which) * head, head)
                r.ot[at, index, which] = product(r.vt[at, place, :], probs, NN).astype(LOW)

        for index in range(begin, begin + count):
            pair(index)

    def attention_out(layer):
        at = layer // 2
        r.otc[at, :, :, 0:length] = r.ot[at, :, c]
        give(4 + at, r.ot.at[at, :, 1 - c], r.otc.at[at, :, :, other])
        r.f[...] = product(r.ot[at].reshape(width, length).T, matrix(layer, pl.ds(3 * width, width)), NN)

    def expand(layer, index):
        at = layer // 2
        place = pl.ds(index * width, width)
        pre = product(r.x[layer], matrix(layer, place), NN)
        squared = pre * pre
        slope = 0.7978845608 * (1.0 + 3 * 0.044715 * squared)
        bent = jnp.tanh(0.7978845608 * pre * (1.0 + 0.044715 * squared))
        r.g[at, :, place] = (0.5 * pre * (1.0 + bent)).astype(LOW)
        r.slope[at, :, place] = (0.5 * (1.0 + bent) + 0.5 * pre * (1.0 - bent * bent) * slope).astype(LOW)
        block = aligned((2 * index + c) * rows_b, rows_b)
        r.gc[at, index, 0:length, :] = r.g[at, :, block]
        block = aligned((2 * index + 1 - c) * rows_b, rows_b)
        give(6 + chips * at + index, r.g.at[at, :, block], r.gc.at[at, index, other, :])

    def contract(layer):
        r.f[...] = product(r.g[layer // 2], r.wb[layer // 2].reshape(hidden, width), NN)

    def by_rows(work):
        for index in range(length // BLOCK):
            work(pl.ds(index * BLOCK, BLOCK))

    def normalize(layer):
        gain, offset = gain_row(layer, 0), gain_row(layer, 1)

        def some(rows):
            branch = r.f[rows, :]
            normal, inverse = stats(r.x[layer, rows, :].astype(WIDE) + branch)
            r.n[layer, rows, :] = normal
            r.inv[layer, rows, :] = inverse
            out = normal * gain + offset
            dual = branch if layer == 0 else r.y[rows, :].astype(WIDE) + branch
            if layer < 3:
                r.x[layer + 1, rows, :] = out.astype(LOW)
                r.y[rows, :] = dual.astype(LOW)
            else:
                dual_normal, dual_inverse = stats(dual)
                r.output[rows, :] = (out + dual_normal).astype(LOW)
                pull = r.cot[rows, :].astype(WIDE) * r.live[rows, :]
                r.gx[rows, :] = pull
                r.gy[rows, :] = norm_back(dual_normal, dual_inverse, pull)

        by_rows(some)

    def back_normalize(layer):
        gain = gain_row(layer, 0)

        def some(index, sums):
            rows = pl.ds(index * BLOCK, BLOCK)
            upstream = r.gx[rows, :]
            normal = r.n[layer, rows, :]
            summed = norm_back(normal, r.inv[layer, rows, :], upstream * gain)
            dual = r.gy[rows, :]
            r.gx[rows, :] = summed
            r.df[layer // 2, rows, :] = (summed + dual).astype(LOW)
            if layer == 3:
                r.gy[rows, :] = dual.astype(LOW).astype(WIDE)
            return (
                sums[0] + jnp.sum(upstream * normal, 0, keepdims=True),
                sums[1] + jnp.sum(upstream, 0, keepdims=True),
            )

        zero = jnp.zeros((1, width), WIDE)
        gains, offsets = zero, zero
        for index in range(length // BLOCK):
            gains, offsets = some(index, (gains, offsets))
        r.ng[d, 2 * layer : 2 * layer + 1, :] = gains
        r.ng[d, 2 * layer + 1 : 2 * layer + 2, :] = offsets

    def pass_down(layer, inner):
        total = r.gx[...] + inner
        if layer > 0:
            r.gx[...] = total.astype(LOW).astype(WIDE)
        else:
            r.input_grad[...] = total

    base = 6 + 2 * chips

    def back_hidden(layer):
        at = layer // 2
        r.dft[at, :, 0:length] = r.df[at, 0:length, :].T
        give(base + at, r.dft.at[at, :, mine], r.dft.at[at, :, other])
        for index in range(hidden // width):
            place = pl.ds(index * width, width)
            pulled = product(r.df[at, 0:length, :], r.wb[at, index].reshape(width, width), NT)
            r.dh[at, 0:length, place] = (pulled * r.slope[at, :, place].astype(WIDE)).astype(LOW)
            give(base + 2 + chips * at + index, r.dh.at[at, mine, place], r.dh.at[at, other, place])

    def back_expand_end(layer):
        pass_down(layer, product(r.dh[layer // 2, 0:length, :], matrix(layer, pl.ds(0, hidden)), NT))

    def back_output(layer):
        at = layer // 2
        give(base + 2 + 2 * chips + at, r.df.at[at, mine], r.df.at[at, other])
        r.dm[...] = product(r.df[at, 0:length, :], matrix(layer, pl.ds(3 * width, width)), NT).astype(LOW)
        r.kt[at] = (r.k[at] * jnp.asarray(scale, LOW)).T

    def back_heads(layer, begin, count):
        at = layer // 2

        def pair(index):
            lanes = aligned(index * 2 * head, 2 * head)
            pulled = r.dm[:, lanes]
            keys, values = [], []
            for which in range(2):
                probs = r.pt[at, 2 * index + which]
                grad = product(r.v[at, :, lanes], pulled * half_masks[which], NT)
                full = probs.astype(WIDE)
                centre = jnp.sum(full * grad, 0, keepdims=True)
                scores = (full * (grad - centre)).astype(LOW)
                keys.append(product(scores, r.q[at, :, lanes], NN))
                values.append(product(probs, pulled, NN))
                place = aligned((2 * index + which) * head, head)
                r.dqt[place, :] = product(r.kt[at, place, :], scores, NN).astype(LOW)
            r.dp[at, 0:length, aligned(width + index * 2 * head, 2 * head)] = jnp.where(
                lane < head, keys[0], keys[1]
            ).astype(LOW)
            r.dp[at, 0:length, aligned(2 * width + index * 2 * head, 2 * head)] = jnp.where(
                lane < head, values[0], values[1]
            ).astype(LOW)

        def pairs(step):
            pair(begin + 2 * step)
            pair(begin + 2 * step + 1)

        loop(count // 2, pairs)

    def back_packed(layer):
        at = layer // 2
        slot = base + 4 + 2 * chips + 2 * at
        place = pl.ds(width, 2 * width)
        give(slot, r.dp.at[at, mine, place], r.dp.at[at, other, place])
        r.dp[at, 0:length, 0:width] = r.dqt[...].T
        place = pl.ds(0, width)
        give(slot + 1, r.dp.at[at, mine, place], r.dp.at[at, other, place])

    def back_packed_end(layer):
        pass_down(layer, product(r.dp[layer // 2, 0:length, :], matrix(layer, pl.ds(0, 3 * width)), NT))

    def keep(name, half, place, value):
        own = getattr(r, "own" + name)
        own[:, :, half, :, place] = value.astype(LOW).reshape(chips, SECTIONS, rows_a // SECTIONS, value.shape[1])

    def chip_rows(value):
        return value.reshape(chips * rows_a, 2 * length)

    def grad_down(at):
        own = getattr(r, "ownB%d" % at)
        taken(base + at, r.dft.at[at, :, other])
        for chip in range(chips):
            taken(6 + chips * at + chip, r.gc.at[at, chip, other, :])
            value = product(r.dft[at], r.gc[at, chip], NN)
            own[chip] = value.astype(LOW).reshape(SECTIONS, 2, half_b, rows_b)

    def grad_up(layer):
        at = layer // 2
        taken(layer, r.xtc.at[layer, :, :, other])
        for index in range(hidden // width):
            place = pl.ds(index * width, width)
            taken(base + 2 + chips * at + index, r.dh.at[at, other, place])
            value = product(chip_rows(r.xtc[layer]), r.dh[at, :, place], NN)
            keep("F%d" % layer, index // 2, pl.ds(index % 2 * width, width), value)

    def grad_output(layer):
        at = layer // 2
        taken(4 + at, r.otc.at[at, :, :, other])
        taken(base + 2 + 2 * chips + at, r.df.at[at, other])
        for half in range(2):
            place = pl.ds(half * width // 2, width // 2)
            value = product(chip_rows(r.otc[at]), r.df[at, :, place], NN)
            keep("O%d" % layer, half, pl.ds(0, width // 2), value)

    def grad_packed(layer):
        at = layer // 2
        slot = base + 4 + 2 * chips + 2 * at
        taken(layer, r.xtc.at[layer, :, :, other])
        taken(slot, r.dp.at[at, other, pl.ds(width, 2 * width)])
        taken(slot + 1, r.dp.at[at, other, pl.ds(0, width)])
        part = 3 * width // 2
        for half in range(2):
            value = product(chip_rows(r.xtc[layer]), r.dp[at, :, half * part : (half + 1) * part], NN)
            keep("K%d" % layer, half, pl.ds(0, part), value)

    def joined(target, others):
        return functools.reduce(
            lambda left, right: left + right, [ref[...].astype(WIDE) for ref in (target, *others)]
        )

    def add_into(target, others):
        if len(others) == 1:
            target[...] = target[...] + others[0][...]
        else:
            target[...] = joined(target, others).astype(LOW)

    places = {name: place for place, (name, _, _, _) in enumerate(grad_items)}

    def buffers(name):
        parts = ("own", "farx", "fary", "nearx", "neary", "line", "done")
        return types.SimpleNamespace(**{part: getattr(r, part + name) for part in parts})

    def to_plane(name):
        item, place = buffers(name), places[name]

        def over_x(section, half, target, slot):
            push(item.own.at[:, section, half], target, r.px_s.at[place, slot], r.px_r.at[place, slot], to_x)
            at_end(None, item.farx, r.px_s.at[place, slot])

        def over_y(section, half, target, slot):
            push(item.own.at[:, section, half], target, r.py_s.at[place, slot], r.py_r.at[place, slot], to_y)
            at_end(None, item.farx, r.py_s.at[place, slot])

        over_x(sd, 0, item.farx, 2)
        over_y(sd, 1, item.fary, 2)
        over_x(sx, 0, item.nearx.at[0], 0)
        over_y(sy, 1, item.neary.at[1], 1)

    def through_plane(name):
        item, place = buffers(name), places[name]
        own = item.own
        arrived(item.fary, r.py_r.at[place, 2])
        add_into(own.at[:, sx, 1], [item.fary])
        push(own.at[:, sx, 1], item.nearx.at[1], r.px_s.at[place, 1], r.px_r.at[place, 1], to_x)
        at_end(None, item.farx, r.px_s.at[place, 1])
        arrived(item.farx, r.px_r.at[place, 2])
        add_into(own.at[:, sy, 0], [item.farx])
        push(own.at[:, sy, 0], item.neary.at[0], r.py_s.at[place, 0], r.py_r.at[place, 0], to_y)
        at_end(None, item.farx, r.py_s.at[place, 0])

    def to_line(name):
        item, place = buffers(name), places[name]
        own = item.own.at[:, s]
        for half in range(2):
            arrived(item.nearx.at[half], r.px_r.at[place, half])
            arrived(item.neary.at[half], r.py_r.at[place, half])
            add_into(own.at[:, half], [item.nearx.at[half], item.neary.at[half]])
        for step in range(1, chips):
            chip = lax.rem(z + step, chips)
            push(
                own.at[chip],
                item.line.at[z],
                r.line_s.at[place, step],
                r.line_r.at[place, z],
                {"dp": 2 * chip + c},
            )
            at_end(None, item.line.at[0], r.line_s.at[place, step])

    def to_owner(name):
        item, place = buffers(name), places[name]
        others = [lax.rem(z + step, chips) for step in range(1, chips)]
        for chip in others:
            arrived(item.line.at[chip], r.line_r.at[place, chip])
        total = joined(item.own.at[z, s], [item.line.at[chip] for chip in others])
        square = total * total
        while square.ndim > 2:
            square = jnp.sum(square, 0)
        square = jnp.sum(jnp.sum(square, 0, keepdims=True), 1, keepdims=True)
        r.sum[...] = r.sum[...] + jnp.broadcast_to(square, (8, LANES))
        if name[0] == "B":
            item.done[...] = total
            return
        item.done[s] = total.astype(LOW)
        layer = grad_items[place][1]
        mine = item.done.at[s]
        away = s != layer
        when(
            away,
            lambda: push(mine, mine, r.done_s.at[place], r.done_r.at[place, s], {"section": jnp.int32(layer)}),
        )
        at_end(away, mine, r.done_s.at[place])

    def collect(name):
        item, place = buffers(name), places[name]
        layer = grad_items[place][1]

        def work():
            for section in range(SECTIONS):
                if section != layer:
                    arrived(item.done.at[section], r.done_r.at[place, section])
            columns = item.done.shape[-1]
            start = 3 * width if name[0] == "O" else 0
            for section in range(SECTIONS):
                for half in range(2):
                    rows = pl.ds(section * (rows_a // SECTIONS), rows_a // SECTIONS)
                    place_to = pl.ds(start + half * columns, columns)
                    r.grad_a[rows, place_to] = item.done[section, half].astype(WIDE)

        when(s == layer, work)

    def all_sent(count=None):
        for condition, source, sem in finish[:count]:
            when(condition, functools.partial(sent, source, sem))
        del finish[:count]

    cut_out()
    small_out(0, r.tiles.at[d, s])
    plane_out(5, z)
    line_out(4)
    plane_out(4, z)
    cut_in()
    plane_out(1, z)
    line_out(0)
    plane_out(0, z)
    line_out(1)
    line_out(2)
    plane_out(3, z)
    line_out(3)
    line_in(4)
    small_group(0, r.tiles.at[pl.ds(0, devices - 1), 0])
    for peer in plane:
        push(r.tiles.at[:, s], r.tiles.at[:, s], r.small_s.at[0, 1], r.small_r.at[0, 1], peer)
    line_in(0)
    plane_in(5)
    line_in(1)
    plane_in(0)
    plane_out(2, z)
    plane_in(1)
    far_in(0)
    line_in(2)
    plane_in(4)
    line_out(5)
    own_x.wait()
    own_cot.wait()
    prepare_masks()
    core_in(0)
    attention_in(0)
    far_in(1)
    attention_heads(0, 0, 2)
    attention_heads(0, 2, 2)
    plane_in(2)
    attention_out(0)
    small_plane(0, r.tiles.at[:, pl.ds(0, SECTIONS - 1)])
    normalize(0)
    far_in(4)
    core_in(1)
    line_in(3)
    expand(1, 0)
    expand(1, 1)
    early = len(finish)
    far_in(2)
    expand(1, 2)
    expand(1, 3)
    core_in(4)
    contract(1)
    normalize(1)
    core_in(2)
    plane_in(3)
    attention_in(2)
    attention_heads(2, 0, 2)
    attention_heads(2, 2, 2)
    far_in(3)
    attention_out(2)
    line_in(5)
    normalize(2)
    core_in(3)
    expand(3, 0)
    expand(3, 1)
    expand(3, 2)
    expand(3, 3)
    all_sent(early)
    core_in(5)
    contract(3)
    normalize(3)

    r.sum[...] = jnp.zeros((8, LANES), WIDE)
    back_normalize(3)
    back_hidden(3)
    back_expand_end(3)
    give_rows(3)
    grad_down(1)
    to_plane("B1")
    back_normalize(2)
    back_output(2)
    grad_up(3)
    to_plane("F3")
    back_heads(2, 0, 2)
    through_plane("B1")
    back_heads(2, 2, 2)
    give_rows(2)
    through_plane("F3")
    back_packed(2)
    grad_output(2)
    to_plane("O2")
    back_packed_end(2)
    back_normalize(1)
    back_hidden(1)
    give_rows(1)
    to_line("B1")
    through_plane("O2")
    to_line("F3")
    grad_packed(2)
    to_plane("K2")
    grad_down(0)
    to_plane("B0")
    to_line("O2")
    back_expand_end(1)
    back_normalize(0)
    small_out(1, r.ng.at[d])
    back_output(0)
    give_rows(0)
    through_plane("K2")
    back_heads(0, 0, 2)
    through_plane("B0")
    grad_up(1)
    to_plane("F1")
    back_heads(0, 2, 2)
    to_line("K2")
    grad_output(0)
    to_plane("O0")
    back_packed(0)
    to_line("B0")
    to_owner("B1")
    to_owner("F3")
    to_owner("O2")
    through_plane("F1")
    grad_packed(0)
    to_plane("K0")
    through_plane("O0")
    back_packed_end(0)
    to_owner("K2")
    to_line("F1")
    to_owner("B0")
    all_sent()
    through_plane("K0")
    to_line("O0")
    small_group(1, r.ng.at[pl.ds(0, devices - 1)])
    r.ns[s] = functools.reduce(lambda left, right: left + right, [r.ng[index] for index in range(devices)])
    small_plane_out(1, r.ns.at[s])
    to_line("K0")
    to_owner("F1")
    to_owner("O0")
    for name in ("F3", "O2", "K2", "F1"):
        collect(name)
    collect("O0")
    for layer in range(2):
        done = buffers("B%d" % layer).done
        r.grad_b[layer] = done[...].reshape(cols_b, rows_b).T
    small_plane(1, r.ns.at[pl.ds(0, SECTIONS - 1)])
    grads = functools.reduce(lambda left, right: left + right, [r.ns[index] for index in range(SECTIONS)])
    norm_square = jnp.sum(jnp.sum(grads * grads, 0, keepdims=True), 1, keepdims=True)
    chosen = jnp.zeros((2, width), WIDE)
    for layer in range(4):
        chosen = jnp.where(s == layer, grads[2 * layer : 2 * layer + 2, :], chosen)
    for chip in range(chips):
        pair_of = chosen[:, chip * LANES : (chip + 1) * LANES]
        r.grad_n[...] = jnp.where(
            z == chip, jnp.where(c == 0, pair_of[:, :rows_a], pair_of[:, rows_a:]), r.grad_n[...]
        )
    to_owner("K0")

    r.sq[d] = r.sum[...]
    small_out(2, r.sq.at[d])
    collect("K0")
    small_group(2, r.sq.at[pl.ds(0, devices - 1)])
    r.sqs[s] = functools.reduce(lambda left, right: left + right, [r.sq[index] for index in range(devices)])
    small_plane_out(2, r.sqs.at[s])
    all_sent()
    small_plane(2, r.sqs.at[pl.ds(0, SECTIONS - 1)])
    squares = functools.reduce(lambda left, right: left + right, [r.sqs[index] for index in range(SECTIONS)])
    r.square[...] = squares + norm_square


def step_call(tokens, cotangent, lengths, mat_a, mat_b, norms):
    rows_a, hidden = mat_a.shape[1:]
    rows_b, cols_b = mat_b.shape[1:]
    width = tokens.shape[1]
    length = tokens.shape[0] // lengths.shape[0]
    chips = width // rows_a // 2
    scratch = kernel_scratch(chips, rows_a, rows_b, cols_b, length, width, hidden)
    shapes = []
    for _, shape, kind in scratch:
        shapes.append(pltpu.SemaphoreType.DMA(shape) if kind is None else pltpu.VMEM(shape, kind))
    anywhere, vmem = pl.BlockSpec(memory_space=pl.ANY), pl.BlockSpec(memory_space=pltpu.VMEM)
    return pl.pallas_call(
        functools.partial(step_kernel, INPUTS + OUTPUTS + tuple(name for name, _, _ in scratch)),
        out_shape=(
            jax.ShapeDtypeStruct((rows_a, hidden), WIDE),
            jax.ShapeDtypeStruct(mat_b.shape, WIDE),
            jax.ShapeDtypeStruct((2, rows_a), WIDE),
            jax.ShapeDtypeStruct((8, LANES), WIDE),
            jax.ShapeDtypeStruct((length, width), LOW),
            jax.ShapeDtypeStruct((length, width), WIDE),
        ),
        in_specs=[anywhere, anywhere, pl.BlockSpec(memory_space=pltpu.SMEM), vmem, vmem, vmem],
        out_specs=[vmem] * len(OUTPUTS),
        scratch_shapes=shapes,
        compiler_params=pltpu.CompilerParams(
            collective_id=0, has_side_effects=True, vmem_limit_bytes=KERNEL_VMEM
        ),
    )(tokens, cotangent, lengths, mat_a, mat_b, norms)


def update_kernel(*refs):
    square, output, input_grad = (ref[...] for ref in refs[:3])
    grad_norm = jnp.sqrt(square[0:1, 0:1])
    factor = CLIP_NORM / jnp.maximum(grad_norm, CLIP_NORM)
    inputs, outputs = refs[3:15], refs[15:]
    outputs[0][...] = grad_norm
    outputs[1][0] = output
    outputs[2][0] = input_grad
    for group, (rate, decay) in enumerate(
        ((MATRIX_RATE, MATRIX_DECAY), (MATRIX_RATE, MATRIX_DECAY), (NORM_RATE, 0.0))
    ):
        grad, weight, one, two = inputs[4 * group : 4 * group + 4]
        clip = grad[...].reshape(weight.shape) * factor
        moment, square_new, master = adam_update(weight[...], one[...], two[...], clip, rate, decay)
        for ref, value in zip(
            outputs[3 + 5 * group : 8 + 5 * group], (clip, moment, square_new, master, master.astype(LOW))
        ):
            ref[...] = value


def kernel_body(
    tokens, cotangent, lengths, mat_a, mat_b, norms, first_a, second_a, first_b, second_b, first_n, second_n
):
    norms, first_n, second_n = (jnp.swapaxes(value, 1, 2) for value in (norms, first_n, second_n))
    grad_a, grad_b, grad_n, square, output, input_grad = step_call(
        tokens, cotangent, lengths, mat_a, mat_b, norms
    )
    steps = 4

    def cut(value, dim):
        shape = tuple(size // steps if at == dim else size for at, size in enumerate(value.shape))
        return pl.BlockSpec(shape, lambda step: tuple(step if at == dim else 0 for at in range(len(shape))))

    def whole(value):
        return pl.BlockSpec(value.shape, lambda step: (0,) * len(value.shape))

    def like(value, kind=WIDE):
        return jax.ShapeDtypeStruct(value.shape, kind)

    args = (square, output, input_grad, grad_a, mat_a, first_a, second_a, grad_b, mat_b, first_b, second_b)
    specs = [whole(square), cut(output, 0), cut(input_grad, 0)]
    specs += [cut(grad_a, 0)] + [cut(mat_a, 1)] * 3 + [cut(grad_b, 1)] * 4
    args += (grad_n, norms, first_n, second_n)
    specs += [whole(grad_n)] + [whole(norms)] * 3
    shapes = [jax.ShapeDtypeStruct((1, 1), WIDE), like(output[None], LOW), like(input_grad[None])]
    out_specs = [whole(shapes[0]), cut(shapes[1], 1), cut(shapes[2], 1)]
    for value, spec in ((mat_a, cut(mat_a, 1)), (mat_b, cut(mat_b, 1)), (norms, whole(norms))):
        shapes += [like(value)] * 4 + [like(value, LOW)]
        out_specs += [spec] * 5
    results = pl.pallas_call(
        update_kernel,
        grid=(steps,),
        out_shape=shapes,
        in_specs=specs,
        out_specs=out_specs,
        compiler_params=pltpu.CompilerParams(vmem_limit_bytes=KERNEL_VMEM),
    )(*args)
    results = [results[0][0, 0], *results[1:]]
    results[-5:] = [jnp.swapaxes(value, 1, 2) for value in results[-5:]]
    return tuple(results)


def chosen_body(*args):
    rows_a = args[3].shape[1]
    groups = lax.axis_size("dp")
    by_kernel = rows_a % 32 == 0 and 2 * rows_a == LANES and groups * rows_a == args[0].shape[1]
    return (kernel_body if by_kernel else body)(*args)


def solution(mesh):
    placed = (
        P("dp", None),
        P("dp", None),
        P("dp", None),
        P("section", "dp", None),
        P(None, "dp", "section"),
        P("section", "dp", None),
        P("section", "dp", None),
        P("section", "dp", None),
        P(None, "dp", "section"),
        P(None, "dp", "section"),
        P("section", "dp", None),
        P("section", "dp", None),
    )
    return jax.shard_map(
        chosen_body,
        mesh=mesh,
        in_specs=placed,
        out_specs=(
            P(),
            P("section", "dp", None),
            P("section", "dp", None),
            P("section", "dp", None),
            P("section", "dp", None),
            P("section", "dp", None),
            P("section", "dp", None),
            P("section", "dp", None),
            P(None, "dp", "section"),
            P(None, "dp", "section"),
            P(None, "dp", "section"),
            P(None, "dp", "section"),
            P(None, "dp", "section"),
            P("section", "dp", None),
            P("section", "dp", None),
            P("section", "dp", None),
            P("section", "dp", None),
            P("section", "dp", None),
        ),
        check_vma=False,
    )
```

```python
import functools
import types

import jax
import jax.numpy as jnp
from jax import lax
from jax.experimental import pallas as pl
from jax.experimental.pallas import tpu as pltpu
from jax.sharding import PartitionSpec as P

HEADS = 8
STEP = 5


EPSILON = 1e-05
NEGATIVE = -1e30
CLIP_NORM = 1.0
BETA_ONE = 0.5
BETA_TWO = 0.5
ADAM_EPSILON = 1e-08
MATRIX_RATE = 0.05
NORM_RATE = 0.5
MATRIX_DECAY = 0.01


def norm_stats(value):
    centre = value - jnp.mean(value, -1, keepdims=True)
    inverse = lax.rsqrt(jnp.mean(centre * centre, -1, keepdims=True) + EPSILON)
    return (centre * inverse, inverse)


def norm_back(normal, inverse, upstream):
    return inverse * (
        upstream
        - jnp.mean(upstream, -1, keepdims=True)
        - normal * jnp.mean(upstream * normal, -1, keepdims=True)
    )


def adam_update(weight, moment_one, moment_two, gradient, step_rate, decay_rate):
    first_new = BETA_ONE * moment_one + (1.0 - BETA_ONE) * gradient
    second_new = BETA_TWO * moment_two + (1.0 - BETA_TWO) * gradient * gradient
    first_hat = first_new / (1.0 - BETA_ONE**STEP)
    second_hat = second_new / (1.0 - BETA_TWO**STEP)
    weight_new = weight - step_rate * (
        first_hat / (jnp.sqrt(second_hat) + ADAM_EPSILON) + decay_rate * weight
    )
    return (first_new, second_new, weight_new)


def segments_of(lengths_row, length):
    ends = jnp.cumsum(lengths_row, dtype=jnp.int32)
    places = jnp.arange(length, dtype=jnp.int32)
    segment = jnp.sum((ends[None, :] <= places[:, None]).astype(jnp.int32), axis=1, dtype=jnp.int32)
    live = (places < ends[-1]).astype(jnp.float32)
    return segment, live


def matmul(left, right, dims):
    return lax.dot_general(left, right, (dims, ((), ())), preferred_element_type=jnp.float32)


NN = ((1,), (0,))
NT = ((1,), (1,))
TN = ((0,), (0,))


def attention_forward(stream, weight, mask):
    length, width = stream.shape
    size = width // HEADS
    packed = matmul(stream, weight[:, : 3 * width], NN).astype(jnp.bfloat16)
    heads = packed.reshape(length, 3, HEADS, size)
    scores = jnp.einsum("qhd,khd->hqk", heads[:, 0], heads[:, 1], preferred_element_type=jnp.float32)
    scores = jnp.where(mask[None], scores * size**-0.5, NEGATIVE)
    weights = jnp.exp(scores - jnp.max(scores, -1, keepdims=True))
    probs = weights / jnp.sum(weights, -1, keepdims=True)
    mixed = jnp.einsum("hqk,khd->qhd", probs.astype(jnp.bfloat16), heads[:, 2], preferred_element_type=jnp.float32)
    mixed = mixed.reshape(length, width).astype(jnp.bfloat16)
    branch = matmul(mixed, weight[:, 3 * width :], NN)
    return branch, (heads, probs, mixed)


def attention_backward(stream, weight, kept, grad_low):
    heads, probs, mixed = kept
    length, width = stream.shape
    size = width // HEADS
    grad_out = matmul(mixed, grad_low, TN)
    grad_mixed = matmul(grad_low, weight[:, 3 * width :], NT).astype(jnp.bfloat16)
    grad_mixed = grad_mixed.reshape(length, HEADS, size)
    grad_probs = jnp.einsum("qhd,khd->hqk", grad_mixed, heads[:, 2], preferred_element_type=jnp.float32)
    centre = jnp.sum(probs * grad_probs, -1, keepdims=True)
    grad_scores = (probs * (grad_probs - centre)).astype(jnp.bfloat16)
    low = probs.astype(jnp.bfloat16)
    scale = size**-0.5
    grad_q = jnp.einsum("hqk,khd->qhd", grad_scores, heads[:, 1], preferred_element_type=jnp.float32) * scale
    grad_k = jnp.einsum("hqk,qhd->khd", grad_scores, heads[:, 0], preferred_element_type=jnp.float32) * scale
    grad_v = jnp.einsum("hqk,qhd->khd", low, grad_mixed, preferred_element_type=jnp.float32)
    packed = jnp.concatenate([grad_q, grad_k, grad_v], axis=1).reshape(length, 3 * width)
    packed = packed.astype(jnp.bfloat16)
    grad_in = matmul(stream, packed, TN)
    grad_inputs = matmul(packed, weight[:, : 3 * width], NT)
    return grad_inputs, jnp.concatenate([grad_in, grad_out], axis=1)


def feed_forward(stream, weight, down):
    pre = matmul(stream, weight, NN)
    active = jax.nn.gelu(pre, approximate=True).astype(jnp.bfloat16)
    return matmul(active, down, NN), (pre, active)


def feed_backward(stream, weight, down, kept, grad_low):
    pre, active = kept
    grad_down = matmul(active, grad_low, TN)
    grad_active = matmul(grad_low, down, NT)
    pull = jax.vjp(lambda value: jax.nn.gelu(value, approximate=True), pre)[1]
    grad_pre = pull(grad_active)[0].astype(jnp.bfloat16)
    grad_up = matmul(stream, grad_pre, TN)
    return matmul(grad_pre, weight, NT), grad_up, grad_down


def micro_step(rows, pull, segment, mats, downs, gains, biases):
    low = jnp.bfloat16
    mask = segment[:, None] == segment[None, :]
    stream, dual = rows, jnp.zeros_like(rows)
    saved = []
    for sub in range(4):
        if sub % 2 == 0:
            branch, kept = attention_forward(stream, mats[sub], mask)
        else:
            branch, kept = feed_forward(stream, mats[sub], downs[sub // 2])
        normal, inverse = norm_stats(stream.astype(jnp.float32) + branch)
        out = normal * gains[sub] + biases[sub]
        total = dual.astype(jnp.float32) + branch
        saved.append((stream, kept, normal, inverse))
        if sub < 3:
            stream, dual = out.astype(low), total.astype(low)
    dual_normal, dual_inverse = norm_stats(total)
    output = (out + dual_normal).astype(low)
    grad_out, grad_dual = pull, norm_back(dual_normal, dual_inverse, pull)
    grads_a, grads_b, grads_n = [None] * 4, [None] * 2, [None] * 4
    for sub in (3, 2, 1, 0):
        stream, kept, normal, inverse = saved[sub]
        grads_n[sub] = jnp.stack([jnp.sum(grad_out * normal, 0), jnp.sum(grad_out, 0)], axis=1)
        summed = norm_back(normal, inverse, grad_out * gains[sub])
        branch_low = (summed + grad_dual).astype(low)
        if sub % 2 == 0:
            inner, grads_a[sub] = attention_backward(stream, mats[sub], kept, branch_low)
        else:
            inner, grads_a[sub], grads_b[sub // 2] = feed_backward(
                stream, mats[sub], downs[sub // 2], kept, branch_low
            )
        grad_in = summed + inner
        if sub > 0:
            grad_out = grad_in.astype(low).astype(jnp.float32)
            grad_dual = grad_dual.astype(low).astype(jnp.float32)
    return output, grad_in, jnp.stack(grads_a), jnp.stack(grads_b), jnp.stack(grads_n)


def finish_step(grad_norm, output, input_grad, *groups):
    factor = CLIP_NORM / jnp.maximum(grad_norm, CLIP_NORM)
    results = [grad_norm, output[None], input_grad[None]]
    for weight, one, two, grad, rate, decay in groups:
        clip = grad * factor
        moment, square_new, master = adam_update(weight, one, two, clip, rate, decay)
        results += [clip, moment, square_new, master, master.astype(jnp.bfloat16)]
    return tuple(results)


def body(
    tokens, cotangent, lengths, mat_a, mat_b, norms, first_a, second_a, first_b, second_b, first_n, second_n
):
    low = jnp.bfloat16
    own = lax.axis_index("section")
    length = tokens.shape[0] // lengths.shape[0]
    rows = lax.dynamic_slice_in_dim(tokens, own * length, length, 0)
    segment, live = segments_of(lax.dynamic_index_in_dim(lengths, own, 0, keepdims=False), length)
    pull = lax.dynamic_slice_in_dim(cotangent, own * length, length, 0).astype(jnp.float32) * live[:, None]

    def gathered(value):
        return lax.all_gather(lax.all_gather(value, "dp", axis=1, tiled=True), "section", axis=0, tiled=True)

    mats = gathered(mat_a.astype(low))
    scales = gathered(norms.astype(low)).astype(jnp.float32)
    downs = lax.all_gather(mat_b.astype(low), "section", axis=2, tiled=True)
    downs = lax.all_gather(downs, "dp", axis=1, tiled=True)
    output, input_grad, part_a, part_b, part_n = micro_step(
        rows, pull, segment, mats, downs, scales[:, :, 0], scales[:, :, 1]
    )

    def scattered(value, section_dim):
        value = lax.psum_scatter(value, "section", scatter_dimension=section_dim, tiled=True)
        return lax.psum_scatter(value, "dp", scatter_dimension=1, tiled=True).astype(jnp.float32)

    grad_a = scattered(part_a.astype(low), 0)
    grad_b = scattered(part_b.astype(low), 2)
    grad_n = scattered(part_n, 0)
    square = jnp.sum(grad_a * grad_a) + jnp.sum(grad_b * grad_b) + jnp.sum(grad_n * grad_n)
    grad_norm = jnp.sqrt(lax.psum(square, ("section", "dp")))
    return finish_step(
        grad_norm, output, input_grad,
        (mat_a, first_a, second_a, grad_a, MATRIX_RATE, MATRIX_DECAY),
        (mat_b, first_b, second_b, grad_b, MATRIX_RATE, MATRIX_DECAY),
        (norms, first_n, second_n, grad_n, NORM_RATE, 0.0),
    )


LOW = jnp.bfloat16
WIDE = jnp.float32
MESH = pl.DeviceIdType.MESH
SECTIONS = 4
LANES = 128
BLOCK = 64
ROWS_FIRST = (5,)
KERNEL_VMEM = 64 * 1024 * 1024 - 256 * 1024


def gradient_items(rows_a, rows_b, cols_b, width, hidden):
    part = rows_a // SECTIONS
    return (
        ("B1", 3, cols_b // 2, rows_b),
        ("F3", 3, part, hidden // 2),
        ("O2", 2, part, width // 2),
        ("K2", 2, part, 3 * width // 2),
        ("B0", 1, cols_b // 2, rows_b),
        ("F1", 1, part, hidden // 2),
        ("O0", 0, part, width // 2),
        ("K0", 0, part, 3 * width // 2),
    )


def item_scratch(name, chips, rows, columns):
    piece = (rows, columns)
    return (
        ("own" + name, (chips, SECTIONS, 2) + piece, LOW),
        ("farx" + name, (chips,) + piece, LOW),
        ("fary" + name, (chips,) + piece, LOW),
        ("nearx" + name, (2, chips) + piece, LOW),
        ("neary" + name, (2, chips) + piece, LOW),
        ("line" + name, (chips, 2) + piece, LOW),
        ("done" + name, (2,) + piece if name[0] == "B" else (SECTIONS, 2) + piece, WIDE if name[0] == "B" else LOW),
    )


def kernel_scratch(chips, rows_a, rows_b, cols_b, length, width, hidden):
    devices = 2 * chips
    items = gradient_items(rows_a, rows_b, cols_b, width, hidden)
    count = len(items)
    received = sum((item_scratch(name, chips, rows, columns) for name, _, rows, columns in items), ())
    return received + (
        ("fac_s", (32,), None),
        ("fac_r", (32,), None),
        ("px_s", (count, 3), None),
        ("px_r", (count, 3), None),
        ("py_s", (count, 3), None),
        ("py_r", (count, 3), None),
        ("line_s", (count, chips), None),
        ("line_r", (count, chips), None),
        ("done_s", (count,), None),
        ("done_r", (count, SECTIONS), None),
        ("wa", (4, chips, 2, SECTIONS, rows_a // SECTIONS, hidden), LOW),
        ("wb", (2, chips, 2, rows_b, width), LOW),
        ("cut", (SECTIONS, rows_a // SECTIONS, hidden), LOW),
        ("tiles", (devices, SECTIONS, 8, LANES), WIDE),
        ("x", (4, length, width), LOW),
        ("xt", (4, chips, 2, rows_a, length), LOW),
        ("xtc", (4, chips, rows_a, 2 * length), LOW),
        ("y", (length, width), LOW),
        ("cot", (length, width), LOW),
        ("bias", (length, length), WIDE),
        ("live", (length, 1), WIDE),
        ("f", (length, width), WIDE),
        ("n", (4, length, width), WIDE),
        ("inv", (4, length, 1), WIDE),
        ("q", (2, length, width), LOW),
        ("k", (2, length, width), LOW),
        ("v", (2, length, width), LOW),
        ("kt", (2, width, length), LOW),
        ("vt", (2, width, length), LOW),
        ("ot", (2, chips, 2, rows_a, length), LOW),
        ("otc", (2, chips, rows_a, 2 * length), LOW),
        ("pt", (2, HEADS, length, length), LOW),
        ("g", (2, length, hidden), LOW),
        ("gc", (2, chips, 2 * length, rows_b), LOW),
        ("slope", (2, length, hidden), LOW),
        ("gx", (length, width), WIDE),
        ("gy", (length, width), WIDE),
        ("df", (2, 2 * length, width), LOW),
        ("dft", (2, width, 2 * length), LOW),
        ("dm", (length, width), LOW),
        ("dqt", (width, length), LOW),
        ("dh", (2, 2 * length, hidden), LOW),
        ("dp", (2, 2 * length, 3 * width), LOW),
        ("ng", (devices, 8, width), WIDE),
        ("ns", (SECTIONS, 8, width), WIDE),
        ("sq", (devices, 8, LANES), WIDE),
        ("sqs", (SECTIONS, 8, LANES), WIDE),
        ("sum", (8, LANES), WIDE),
        ("in_s", (2,), None),
        ("cut_s", (1,), None),
        ("cut_r", (SECTIONS,), None),
        ("gz_s", (6,), None),
        ("gz_r", (6, chips), None),
        ("gx_s", (6,), None),
        ("gx_r", (6,), None),
        ("gy_s", (6,), None),
        ("gy_r", (6,), None),
        ("rx_s", (6,), None),
        ("rx_r", (6,), None),
        ("ry_s", (6,), None),
        ("ry_r", (6,), None),
        ("gs_s", (6,), None),
        ("gs_r", (6,), None),
        ("small_s", (3, 2), None),
        ("small_r", (3, 2), None),
    )


INPUTS = ("tokens", "cotangent", "lengths", "mat_a", "mat_b", "norms")
OUTPUTS = ("grad_a", "grad_b", "grad_n", "square", "output", "input_grad")


def step_kernel(names, *refs):
    r = types.SimpleNamespace(**dict(zip(names, refs)))
    length, width = r.x.shape[1:]
    hidden = r.wa.shape[-1]
    rows_a, (rows_b, cols_b) = r.mat_a.shape[1], r.mat_b.shape[1:]
    devices = r.tiles.shape[0]
    chips = devices // 2
    half_b = cols_b // 2
    grad_items = gradient_items(rows_a, rows_b, cols_b, width, hidden)
    head = width // HEADS
    scale = head**-0.5

    s, d = lax.axis_index("section"), lax.axis_index("dp")
    z, c = lax.div(d, 2), lax.rem(d, 2)
    sx = s + 1 - 2 * lax.rem(s, 2)
    sy = lax.rem(s + 2, SECTIONS)
    sd = SECTIONS - 1 - s
    to_sibling = {"dp": d + 1 - 2 * c}
    to_up, to_down = {"dp": d + 2}, {"dp": d - 2}
    to_x, to_y = {"section": sx}, {"section": sy}
    below, above = z > 0, z < chips - 1
    group = [{"dp": lax.rem(d + step, devices)} for step in range(1, devices)]
    plane = [{"section": lax.rem(s + step, SECTIONS)} for step in range(1, SECTIONS)]
    finish = []

    def when(condition, work):
        if condition is None:
            work()
        else:
            pl.when(condition)(work)

    def push(source, target, send_sem, recv_sem, device):
        pltpu.make_async_remote_copy(
            src_ref=source,
            dst_ref=target,
            send_sem=send_sem,
            recv_sem=recv_sem,
            device_id=device,
            device_id_type=MESH,
        ).start()

    def arrived(target, sem):
        pltpu.make_async_remote_copy(
            src_ref=target, dst_ref=target, send_sem=sem, recv_sem=sem, device_id=to_x, device_id_type=MESH
        ).wait_recv()

    def sent(source, sem):
        pltpu.make_async_remote_copy(
            src_ref=source, dst_ref=source, send_sem=sem, recv_sem=sem, device_id=to_x, device_id_type=MESH
        ).wait_send()

    def at_end(condition, source, sem):
        finish.append((condition, source, sem))

    def aligned(start, size):
        return pl.ds(pl.multiple_of(start, size), size)

    own_x = pltpu.make_async_copy(r.tokens.at[aligned(s * length, length)], r.x.at[0], r.in_s.at[0])
    own_cot = pltpu.make_async_copy(r.cotangent.at[aligned(s * length, length)], r.cot, r.in_s.at[1])
    own_x.start()
    own_cot.start()
    barrier = pltpu.get_barrier_semaphore()
    for peer in group + plane:
        pl.semaphore_signal(barrier, inc=1, device_id=peer, device_id_type=MESH)
    r.cut[...] = r.mat_a[0].astype(LOW).reshape(SECTIONS, rows_a // SECTIONS, hidden)
    r.wa[s, z, c, s] = r.cut[s]
    for layer in range(2):
        r.wb[layer, z, c, :, aligned(s * cols_b, cols_b)] = r.mat_b[layer].astype(LOW)
    norms = r.norms[0].astype(LOW).astype(WIDE)
    nothing = jnp.zeros((2, rows_a), WIDE)
    even = jnp.concatenate([norms, nothing], axis=1)
    odd = jnp.concatenate([nothing, norms], axis=1)
    r.tiles[d, s, 0:2, :] = jnp.where(c == 0, even, odd)
    r.tiles[d, s, 2:8, :] = jnp.zeros((6, LANES), WIDE)
    pl.semaphore_wait(barrier, len(group) + len(plane))

    def small_out(which, source):
        for peer in group:
            push(source, source, r.small_s.at[which, 0], r.small_r.at[which, 0], peer)

    def small_group(which, like):
        arrived(like, r.small_r.at[which, 0])
        sent(like, r.small_s.at[which, 0])

    def small_plane_out(which, source):
        for peer in plane:
            push(source, source, r.small_s.at[which, 1], r.small_r.at[which, 1], peer)

    def small_plane(which, like):
        arrived(like, r.small_r.at[which, 1])
        sent(like, r.small_s.at[which, 1])

    every = slice(None)

    def block(item, chip, section):
        if item < 4:
            return r.wa.at[item, chip, c, section]
        return r.wb.at[item - 4, chip, c, :, aligned(section * cols_b, cols_b)]

    def half_block(item, section, half):
        if item < 4:
            return r.wa.at[item, :, c, section, :, pl.ds(half * hidden // 2, hidden // 2)]
        rows = pl.ds(half * rows_b // 2, rows_b // 2)
        return r.wb.at[item - 4, :, c, rows, aligned(section * cols_b, cols_b)]

    def half_piece(item, section, half):
        rows = pl.ds(half * rows_b // 2, rows_b // 2)
        return r.wb.at[item - 4, z, c, rows, aligned(section * cols_b, cols_b)]

    def core_blocks(item, core):
        return r.wa.at[item, :, core] if item < 4 else r.wb.at[item - 4, :, core]

    def cut_out():
        for section, device in ((sd, {"section": sd}), (sx, to_x), (sy, to_y)):
            push(r.cut.at[section], r.wa.at[s, z, c, section], r.cut_s.at[0], r.cut_r.at[s], device)
        at_end(None, r.cut.at[pl.ds(0, SECTIONS - 1)], r.cut_s.at[0])

    def cut_in():
        for section in (sx, sy, sd):
            arrived(r.wa.at[section, z, c, s], r.cut_r.at[section])

    def line_out(item):
        if item in ROWS_FIRST:
            rows_out(item)
            return
        own = block(item, z, s)
        for step in range(1, chips):
            push(own, own, r.gz_s.at[item], r.gz_r.at[item, z], {"dp": 2 * lax.rem(z + step, chips) + c})
        several = block(item, pl.ds(0, chips - 1), s)
        at_end(None, several, r.gz_s.at[item])

    def plane_out(item, chip):
        own = block(item, chip, s)
        push(own, own, r.gx_s.at[item], r.gx_r.at[item], to_x)
        push(own, own, r.gy_s.at[item], r.gy_r.at[item], to_y)

    def rows_out(item):
        arrived(half_piece(item, sd, 0), r.rx_r.at[item])
        arrived(half_piece(item, sd, 1), r.ry_r.at[item])
        rows = r.wb.at[item - 4, z, c]
        for step in range(1, chips):
            push(rows, rows, r.gz_s.at[item], r.gz_r.at[item, z], {"dp": 2 * lax.rem(z + step, chips) + c})
        push(rows, rows, r.gs_s.at[item], r.gs_r.at[item], to_sibling)
        at_end(None, r.wb.at[item - 4, pl.ds(0, chips - 1), c], r.gz_s.at[item])

    def rows_in(item):
        for step in range(1, chips):
            chip = lax.rem(z + step, chips)
            rows = r.wb.at[item - 4, chip, c]
            arrived(rows, r.gz_r.at[item, chip])
            push(rows, rows, r.gs_s.at[item], r.gs_r.at[item], to_sibling)
        at_end(None, core_blocks(item, c), r.gs_s.at[item])

    def line_in(item):
        if item in ROWS_FIRST:
            rows_in(item)
            return
        for step in range(1, chips):
            chip = lax.rem(z + step, chips)
            arrived(block(item, chip, s), r.gz_r.at[item, chip])
            plane_out(item, chip)
        core_out(item, s)
        at_end(None, block(item, every, s), r.gx_s.at[item])
        at_end(None, block(item, every, s), r.gy_s.at[item])

    def core_out(item, section):
        blocks = block(item, every, section)
        push(blocks, blocks, r.gs_s.at[item], r.gs_r.at[item], to_sibling)

    def plane_in(item):
        over = z if item in ROWS_FIRST else every
        piece = half_piece if item in ROWS_FIRST else half_block
        arrived(block(item, over, sx), r.gx_r.at[item])
        part = piece(item, sx, 1)
        push(part, part, r.ry_s.at[item], r.ry_r.at[item], to_y)
        arrived(block(item, over, sy), r.gy_r.at[item])
        part = piece(item, sy, 0)
        push(part, part, r.rx_s.at[item], r.rx_r.at[item], to_x)
        if item in ROWS_FIRST:
            at_end(None, block(item, z, sx), r.gx_s.at[item])
            at_end(None, block(item, z, sx), r.gy_s.at[item])
        else:
            core_out(item, sx)
            core_out(item, sy)
        at_end(None, part, r.ry_s.at[item])
        at_end(None, part, r.rx_s.at[item])

    def far_in(item):
        arrived(half_block(item, sd, 0), r.rx_r.at[item])
        arrived(half_block(item, sd, 1), r.ry_r.at[item])
        core_out(item, sd)
        at_end(None, core_blocks(item, c), r.gs_s.at[item])

    def core_in(item):
        arrived(core_blocks(item, 1 - c), r.gs_r.at[item])

    mine, other = pl.ds(0, length), pl.ds(length, length)

    def give(slot, source, target):
        push(source, target, r.fac_s.at[slot], r.fac_r.at[slot], to_sibling)
        at_end(None, target, r.fac_s.at[slot])

    def taken(slot, target):
        arrived(target, r.fac_r.at[slot])

    def give_rows(layer):
        r.xt[layer] = r.x[layer].T.reshape(chips, 2, rows_a, length)
        r.xtc[layer, :, :, 0:length] = r.xt[layer, :, c]
        give(layer, r.xt.at[layer, :, 1 - c], r.xtc.at[layer, :, :, other])

    def product(left, right, dims):
        return lax.dot_general(left, right, (dims, ((), ())), preferred_element_type=WIDE)

    def loop(count, work):
        def one(index, carry):
            work(index)
            return carry

        lax.fori_loop(0, count, one, 0)

    def gain_row(layer, kind):
        parts = [
            r.tiles[2 * chip, layer, kind : kind + 1, :] + r.tiles[2 * chip + 1, layer, kind : kind + 1, :]
            for chip in range(chips)
        ]
        return jnp.concatenate(parts, axis=1)

    def stats(value):
        centre = value - jnp.mean(value, -1, keepdims=True)
        inverse = lax.rsqrt(jnp.mean(centre * centre, -1, keepdims=True) + EPSILON)
        return centre * inverse, inverse

    lane = lax.broadcasted_iota(jnp.int32, (1, 2 * head), 1)
    first_half = (lane < head).astype(WIDE)
    half_masks = (first_half.astype(LOW), (1.0 - first_half).astype(LOW))

    def prepare_masks():
        ends, total = [], jnp.int32(0)
        for slot in range(r.lengths.shape[1]):
            total = total + r.lengths[s, slot]
            ends.append(total)
        down_places = lax.broadcasted_iota(jnp.int32, (length, 1), 0)
        across_places = lax.broadcasted_iota(jnp.int32, (1, length), 1)
        down_segment = jnp.zeros((length, 1), jnp.int32)
        across_segment = jnp.zeros((1, length), jnp.int32)
        for end in ends:
            down_segment = down_segment + (end <= down_places).astype(jnp.int32)
            across_segment = across_segment + (end <= across_places).astype(jnp.int32)
        r.bias[...] = jnp.where(down_segment == across_segment, 0.0, NEGATIVE)
        r.live[...] = (down_places < total).astype(WIDE)

    def matrix(layer, place):
        value = r.wa[layer, :, :, :, :, place]
        return value.reshape(width, value.shape[-1])

    def attention_in(layer):
        at = layer // 2
        rows = r.x[layer]
        r.q[at] = product(rows, matrix(layer, pl.ds(0, width)), NN).astype(LOW) * jnp.asarray(scale, LOW)
        keys = product(rows, matrix(layer, pl.ds(width, width)), NN).astype(LOW)
        r.k[at] = keys
        values = product(rows, matrix(layer, pl.ds(2 * width, width)), NN).astype(LOW)
        r.v[at] = values
        r.vt[at] = values.T

    def attention_heads(layer, begin, count):
        at = layer // 2

        def pair(index):
            lanes = aligned(index * 2 * head, 2 * head)
            for which in range(2):
                scores = product(r.k[at, :, lanes], r.q[at, :, lanes] * half_masks[which], NT) + r.bias[...]
                weights = jnp.exp(scores - jnp.max(scores, 0, keepdims=True))
                probs = (weights * (1.0 / jnp.sum(weights, 0, keepdims=True))).astype(LOW)
                r.pt[at, 2 * index + which] = probs
                place = aligned((2 * index + which) * head, head)
                r.ot[at, index, which] = product(r.vt[at, place, :], probs, NN).astype(LOW)

        for index in range(begin, begin + count):
            pair(index)

    def attention_out(layer):
        at = layer // 2
        r.otc[at, :, :, 0:length] = r.ot[at, :, c]
        give(4 + at, r.ot.at[at, :, 1 - c], r.otc.at[at, :, :, other])
        r.f[...] = product(r.ot[at].reshape(width, length).T, matrix(layer, pl.ds(3 * width, width)), NN)

    def expand(layer, index):
        at = layer // 2
        place = pl.ds(index * width, width)
        pre = product(r.x[layer], matrix(layer, place), NN)
        squared = pre * pre
        slope = 0.7978845608 * (1.0 + 3 * 0.044715 * squared)
        bent = jnp.tanh(0.7978845608 * pre * (1.0 + 0.044715 * squared))
        r.g[at, :, place] = (0.5 * pre * (1.0 + bent)).astype(LOW)
        r.slope[at, :, place] = (0.5 * (1.0 + bent) + 0.5 * pre * (1.0 - bent * bent) * slope).astype(LOW)
        block = aligned((2 * index + c) * rows_b, rows_b)
        r.gc[at, index, 0:length, :] = r.g[at, :, block]
        block = aligned((2 * index + 1 - c) * rows_b, rows_b)
        give(6 + chips * at + index, r.g.at[at, :, block], r.gc.at[at, index, other, :])

    def contract(layer):
        r.f[...] = product(r.g[layer // 2], r.wb[layer // 2].reshape(hidden, width), NN)

    def by_rows(work):
        for index in range(length // BLOCK):
            work(pl.ds(index * BLOCK, BLOCK))

    def normalize(layer):
        gain, offset = gain_row(layer, 0), gain_row(layer, 1)

        def some(rows):
            branch = r.f[rows, :]
            normal, inverse = stats(r.x[layer, rows, :].astype(WIDE) + branch)
            r.n[layer, rows, :] = normal
            r.inv[layer, rows, :] = inverse
            out = normal * gain + offset
            dual = branch if layer == 0 else r.y[rows, :].astype(WIDE) + branch
            if layer < 3:
                r.x[layer + 1, rows, :] = out.astype(LOW)
                r.y[rows, :] = dual.astype(LOW)
            else:
                dual_normal, dual_inverse = stats(dual)
                r.output[rows, :] = (out + dual_normal).astype(LOW)
                pull = r.cot[rows, :].astype(WIDE) * r.live[rows, :]
                r.gx[rows, :] = pull
                r.gy[rows, :] = norm_back(dual_normal, dual_inverse, pull)

        by_rows(some)

    def back_normalize(layer):
        gain = gain_row(layer, 0)

        def some(index, sums):
            rows = pl.ds(index * BLOCK, BLOCK)
            upstream = r.gx[rows, :]
            normal = r.n[layer, rows, :]
            summed = norm_back(normal, r.inv[layer, rows, :], upstream * gain)
            dual = r.gy[rows, :]
            r.gx[rows, :] = summed
            r.df[layer // 2, rows, :] = (summed + dual).astype(LOW)
            if layer == 3:
                r.gy[rows, :] = dual.astype(LOW).astype(WIDE)
            return (
                sums[0] + jnp.sum(upstream * normal, 0, keepdims=True),
                sums[1] + jnp.sum(upstream, 0, keepdims=True),
            )

        zero = jnp.zeros((1, width), WIDE)
        gains, offsets = zero, zero
        for index in range(length // BLOCK):
            gains, offsets = some(index, (gains, offsets))
        r.ng[d, 2 * layer : 2 * layer + 1, :] = gains
        r.ng[d, 2 * layer + 1 : 2 * layer + 2, :] = offsets

    def pass_down(layer, inner):
        total = r.gx[...] + inner
        if layer > 0:
            r.gx[...] = total.astype(LOW).astype(WIDE)
        else:
            r.input_grad[...] = total

    base = 6 + 2 * chips

    def back_hidden(layer):
        at = layer // 2
        r.dft[at, :, 0:length] = r.df[at, 0:length, :].T
        give(base + at, r.dft.at[at, :, mine], r.dft.at[at, :, other])
        for index in range(hidden // width):
            place = pl.ds(index * width, width)
            pulled = product(r.df[at, 0:length, :], r.wb[at, index].reshape(width, width), NT)
            r.dh[at, 0:length, place] = (pulled * r.slope[at, :, place].astype(WIDE)).astype(LOW)
            give(base + 2 + chips * at + index, r.dh.at[at, mine, place], r.dh.at[at, other, place])

    def back_expand_end(layer):
        pass_down(layer, product(r.dh[layer // 2, 0:length, :], matrix(layer, pl.ds(0, hidden)), NT))

    def back_output(layer):
        at = layer // 2
        give(base + 2 + 2 * chips + at, r.df.at[at, mine], r.df.at[at, other])
        r.dm[...] = product(r.df[at, 0:length, :], matrix(layer, pl.ds(3 * width, width)), NT).astype(LOW)
        r.kt[at] = (r.k[at] * jnp.asarray(scale, LOW)).T

    def back_heads(layer, begin, count):
        at = layer // 2

        def pair(index):
            lanes = aligned(index * 2 * head, 2 * head)
            pulled = r.dm[:, lanes]
            keys, values = [], []
            for which in range(2):
                probs = r.pt[at, 2 * index + which]
                grad = product(r.v[at, :, lanes], pulled * half_masks[which], NT)
                full = probs.astype(WIDE)
                centre = jnp.sum(full * grad, 0, keepdims=True)
                scores = (full * (grad - centre)).astype(LOW)
                keys.append(product(scores, r.q[at, :, lanes], NN))
                values.append(product(probs, pulled, NN))
                place = aligned((2 * index + which) * head, head)
                r.dqt[place, :] = product(r.kt[at, place, :], scores, NN).astype(LOW)
            r.dp[at, 0:length, aligned(width + index * 2 * head, 2 * head)] = jnp.where(
                lane < head, keys[0], keys[1]
            ).astype(LOW)
            r.dp[at, 0:length, aligned(2 * width + index * 2 * head, 2 * head)] = jnp.where(
                lane < head, values[0], values[1]
            ).astype(LOW)

        def pairs(step):
            pair(begin + 2 * step)
            pair(begin + 2 * step + 1)

        loop(count // 2, pairs)

    def back_packed(layer):
        at = layer // 2
        slot = base + 4 + 2 * chips + 2 * at
        place = pl.ds(width, 2 * width)
        give(slot, r.dp.at[at, mine, place], r.dp.at[at, other, place])
        r.dp[at, 0:length, 0:width] = r.dqt[...].T
        place = pl.ds(0, width)
        give(slot + 1, r.dp.at[at, mine, place], r.dp.at[at, other, place])

    def back_packed_end(layer):
        pass_down(layer, product(r.dp[layer // 2, 0:length, :], matrix(layer, pl.ds(0, 3 * width)), NT))

    def keep(name, half, place, value):
        own = getattr(r, "own" + name)
        own[:, :, half, :, place] = value.astype(LOW).reshape(chips, SECTIONS, rows_a // SECTIONS, value.shape[1])

    def chip_rows(value):
        return value.reshape(chips * rows_a, 2 * length)

    def grad_down(at):
        own = getattr(r, "ownB%d" % at)
        taken(base + at, r.dft.at[at, :, other])
        for chip in range(chips):
            taken(6 + chips * at + chip, r.gc.at[at, chip, other, :])
            value = product(r.dft[at], r.gc[at, chip], NN)
            own[chip] = value.astype(LOW).reshape(SECTIONS, 2, half_b, rows_b)

    def grad_up(layer):
        at = layer // 2
        taken(layer, r.xtc.at[layer, :, :, other])
        for index in range(hidden // width):
            place = pl.ds(index * width, width)
            taken(base + 2 + chips * at + index, r.dh.at[at, other, place])
            value = product(chip_rows(r.xtc[layer]), r.dh[at, :, place], NN)
            keep("F%d" % layer, index // 2, pl.ds(index % 2 * width, width), value)

    def grad_output(layer):
        at = layer // 2
        taken(4 + at, r.otc.at[at, :, :, other])
        taken(base + 2 + 2 * chips + at, r.df.at[at, other])
        for half in range(2):
            place = pl.ds(half * width // 2, width // 2)
            value = product(chip_rows(r.otc[at]), r.df[at, :, place], NN)
            keep("O%d" % layer, half, pl.ds(0, width // 2), value)

    def grad_packed(layer):
        at = layer // 2
        slot = base + 4 + 2 * chips + 2 * at
        taken(layer, r.xtc.at[layer, :, :, other])
        taken(slot, r.dp.at[at, other, pl.ds(width, 2 * width)])
        taken(slot + 1, r.dp.at[at, other, pl.ds(0, width)])
        part = 3 * width // 2
        for half in range(2):
            value = product(chip_rows(r.xtc[layer]), r.dp[at, :, half * part : (half + 1) * part], NN)
            keep("K%d" % layer, half, pl.ds(0, part), value)

    def joined(target, others):
        return functools.reduce(
            lambda left, right: left + right, [ref[...].astype(WIDE) for ref in (target, *others)]
        )

    def add_into(target, others):
        if len(others) == 1:
            target[...] = target[...] + others[0][...]
        else:
            target[...] = joined(target, others).astype(LOW)

    places = {name: place for place, (name, _, _, _) in enumerate(grad_items)}

    def buffers(name):
        parts = ("own", "farx", "fary", "nearx", "neary", "line", "done")
        return types.SimpleNamespace(**{part: getattr(r, part + name) for part in parts})

    def to_plane(name):
        item, place = buffers(name), places[name]

        def over_x(section, half, target, slot):
            push(item.own.at[:, section, half], target, r.px_s.at[place, slot], r.px_r.at[place, slot], to_x)
            at_end(None, item.farx, r.px_s.at[place, slot])

        def over_y(section, half, target, slot):
            push(item.own.at[:, section, half], target, r.py_s.at[place, slot], r.py_r.at[place, slot], to_y)
            at_end(None, item.farx, r.py_s.at[place, slot])

        over_x(sd, 0, item.farx, 2)
        over_y(sd, 1, item.fary, 2)
        over_x(sx, 0, item.nearx.at[0], 0)
        over_y(sy, 1, item.neary.at[1], 1)

    def through_plane(name):
        item, place = buffers(name), places[name]
        own = item.own
        arrived(item.fary, r.py_r.at[place, 2])
        add_into(own.at[:, sx, 1], [item.fary])
        push(own.at[:, sx, 1], item.nearx.at[1], r.px_s.at[place, 1], r.px_r.at[place, 1], to_x)
        at_end(None, item.farx, r.px_s.at[place, 1])
        arrived(item.farx, r.px_r.at[place, 2])
        add_into(own.at[:, sy, 0], [item.farx])
        push(own.at[:, sy, 0], item.neary.at[0], r.py_s.at[place, 0], r.py_r.at[place, 0], to_y)
        at_end(None, item.farx, r.py_s.at[place, 0])

    def to_line(name):
        item, place = buffers(name), places[name]
        own = item.own.at[:, s]
        for half in range(2):
            arrived(item.nearx.at[half], r.px_r.at[place, half])
            arrived(item.neary.at[half], r.py_r.at[place, half])
            add_into(own.at[:, half], [item.nearx.at[half], item.neary.at[half]])
        for step in range(1, chips):
            chip = lax.rem(z + step, chips)
            push(
                own.at[chip],
                item.line.at[z],
                r.line_s.at[place, step],
                r.line_r.at[place, z],
                {"dp": 2 * chip + c},
            )
            at_end(None, item.line.at[0], r.line_s.at[place, step])

    def to_owner(name):
        item, place = buffers(name), places[name]
        others = [lax.rem(z + step, chips) for step in range(1, chips)]
        for chip in others:
            arrived(item.line.at[chip], r.line_r.at[place, chip])
        total = joined(item.own.at[z, s], [item.line.at[chip] for chip in others])
        square = total * total
        while square.ndim > 2:
            square = jnp.sum(square, 0)
        square = jnp.sum(jnp.sum(square, 0, keepdims=True), 1, keepdims=True)
        r.sum[...] = r.sum[...] + jnp.broadcast_to(square, (8, LANES))
        if name[0] == "B":
            item.done[...] = total
            return
        item.done[s] = total.astype(LOW)
        layer = grad_items[place][1]
        mine = item.done.at[s]
        away = s != layer
        when(
            away,
            lambda: push(mine, mine, r.done_s.at[place], r.done_r.at[place, s], {"section": jnp.int32(layer)}),
        )
        at_end(away, mine, r.done_s.at[place])

    def collect(name):
        item, place = buffers(name), places[name]
        layer = grad_items[place][1]

        def work():
            for section in range(SECTIONS):
                if section != layer:
                    arrived(item.done.at[section], r.done_r.at[place, section])
            columns = item.done.shape[-1]
            start = 3 * width if name[0] == "O" else 0
            for section in range(SECTIONS):
                for half in range(2):
                    rows = pl.ds(section * (rows_a // SECTIONS), rows_a // SECTIONS)
                    place_to = pl.ds(start + half * columns, columns)
                    r.grad_a[rows, place_to] = item.done[section, half].astype(WIDE)

        when(s == layer, work)

    def all_sent(count=None):
        for condition, source, sem in finish[:count]:
            when(condition, functools.partial(sent, source, sem))
        del finish[:count]

    cut_out()
    small_out(0, r.tiles.at[d, s])
    plane_out(5, z)
    line_out(4)
    plane_out(4, z)
    cut_in()
    plane_out(1, z)
    line_out(0)
    plane_out(0, z)
    line_out(1)
    line_out(2)
    plane_out(3, z)
    line_out(3)
    line_in(4)
    small_group(0, r.tiles.at[pl.ds(0, devices - 1), 0])
    for peer in plane:
        push(r.tiles.at[:, s], r.tiles.at[:, s], r.small_s.at[0, 1], r.small_r.at[0, 1], peer)
    line_in(0)
    plane_in(5)
    line_in(1)
    plane_in(0)
    plane_out(2, z)
    plane_in(1)
    far_in(0)
    line_in(2)
    plane_in(4)
    line_out(5)
    own_x.wait()
    own_cot.wait()
    prepare_masks()
    core_in(0)
    attention_in(0)
    far_in(1)
    attention_heads(0, 0, 2)
    attention_heads(0, 2, 2)
    plane_in(2)
    attention_out(0)
    small_plane(0, r.tiles.at[:, pl.ds(0, SECTIONS - 1)])
    normalize(0)
    far_in(4)
    core_in(1)
    line_in(3)
    expand(1, 0)
    expand(1, 1)
    early = len(finish)
    far_in(2)
    expand(1, 2)
    expand(1, 3)
    core_in(4)
    contract(1)
    normalize(1)
    core_in(2)
    plane_in(3)
    attention_in(2)
    attention_heads(2, 0, 2)
    attention_heads(2, 2, 2)
    far_in(3)
    attention_out(2)
    line_in(5)
    normalize(2)
    core_in(3)
    expand(3, 0)
    expand(3, 1)
    expand(3, 2)
    expand(3, 3)
    all_sent(early)
    core_in(5)
    contract(3)
    normalize(3)

    r.sum[...] = jnp.zeros((8, LANES), WIDE)
    back_normalize(3)
    back_hidden(3)
    give_rows(3)
    back_expand_end(3)
    back_normalize(2)
    grad_up(3)
    to_plane("F3")
    back_output(2)
    grad_down(1)
    to_plane("B1")
    back_heads(2, 0, 2)
    back_heads(2, 2, 2)
    back_packed(2)
    through_plane("B1")
    give_rows(2)
    grad_output(2)
    back_packed_end(2)
    give_rows(1)
    to_plane("O2")
    grad_packed(2)
    to_plane("K2")
    back_normalize(1)
    back_hidden(1)
    through_plane("K2")
    grad_down(0)
    to_plane("B0")
    back_expand_end(1)
    back_normalize(0)
    small_out(1, r.ng.at[d])
    to_line("K2")
    to_line("B1")
    back_output(0)
    grad_up(1)
    through_plane("B0")
    to_plane("F1")
    back_heads(0, 0, 2)
    back_heads(0, 2, 2)
    back_packed(0)
    to_line("B0")
    through_plane("O2")
    through_plane("F1")
    grad_output(0)
    to_plane("O0")
    give_rows(0)
    grad_packed(0)
    to_plane("K0")
    to_line("O2")
    to_line("F1")
    through_plane("O0")
    to_owner("B1")
    back_packed_end(0)
    to_owner("B0")
    all_sent()
    through_plane("K0")
    small_group(1, r.ng.at[pl.ds(0, devices - 1)])
    r.ns[s] = functools.reduce(lambda left, right: left + right, [r.ng[index] for index in range(devices)])
    small_plane_out(1, r.ns.at[s])
    through_plane("F3")
    to_line("O0")
    to_line("K0")
    to_owner("F1")
    to_line("F3")
    to_owner("O2")
    to_owner("K2")
    to_owner("F3")
    to_owner("O0")
    to_owner("K0")

    r.sq[d] = r.sum[...]
    small_out(2, r.sq.at[d])
    for name in ("F1", "O2", "K2", "F3"):
        collect(name)
    collect("O0")
    for layer in range(2):
        done = buffers("B%d" % layer).done
        r.grad_b[layer] = done[...].reshape(cols_b, rows_b).T
    small_plane(1, r.ns.at[pl.ds(0, SECTIONS - 1)])
    grads = functools.reduce(lambda left, right: left + right, [r.ns[index] for index in range(SECTIONS)])
    norm_square = jnp.sum(jnp.sum(grads * grads, 0, keepdims=True), 1, keepdims=True)
    chosen = jnp.zeros((2, width), WIDE)
    for layer in range(4):
        chosen = jnp.where(s == layer, grads[2 * layer : 2 * layer + 2, :], chosen)
    for chip in range(chips):
        pair_of = chosen[:, chip * LANES : (chip + 1) * LANES]
        r.grad_n[...] = jnp.where(
            z == chip, jnp.where(c == 0, pair_of[:, :rows_a], pair_of[:, rows_a:]), r.grad_n[...]
        )
    collect("K0")
    small_group(2, r.sq.at[pl.ds(0, devices - 1)])
    r.sqs[s] = functools.reduce(lambda left, right: left + right, [r.sq[index] for index in range(devices)])
    small_plane_out(2, r.sqs.at[s])
    all_sent()
    small_plane(2, r.sqs.at[pl.ds(0, SECTIONS - 1)])
    squares = functools.reduce(lambda left, right: left + right, [r.sqs[index] for index in range(SECTIONS)])
    r.square[...] = squares + norm_square


def step_call(tokens, cotangent, lengths, mat_a, mat_b, norms):
    rows_a, hidden = mat_a.shape[1:]
    rows_b, cols_b = mat_b.shape[1:]
    width = tokens.shape[1]
    length = tokens.shape[0] // lengths.shape[0]
    chips = width // rows_a // 2
    scratch = kernel_scratch(chips, rows_a, rows_b, cols_b, length, width, hidden)
    shapes = []
    for _, shape, kind in scratch:
        shapes.append(pltpu.SemaphoreType.DMA(shape) if kind is None else pltpu.VMEM(shape, kind))
    anywhere, vmem = pl.BlockSpec(memory_space=pl.ANY), pl.BlockSpec(memory_space=pltpu.VMEM)
    return pl.pallas_call(
        functools.partial(step_kernel, INPUTS + OUTPUTS + tuple(name for name, _, _ in scratch)),
        out_shape=(
            jax.ShapeDtypeStruct((rows_a, hidden), WIDE),
            jax.ShapeDtypeStruct(mat_b.shape, WIDE),
            jax.ShapeDtypeStruct((2, rows_a), WIDE),
            jax.ShapeDtypeStruct((8, LANES), WIDE),
            jax.ShapeDtypeStruct((length, width), LOW),
            jax.ShapeDtypeStruct((length, width), WIDE),
        ),
        in_specs=[anywhere, anywhere, pl.BlockSpec(memory_space=pltpu.SMEM), vmem, vmem, vmem],
        out_specs=[vmem] * len(OUTPUTS),
        scratch_shapes=shapes,
        compiler_params=pltpu.CompilerParams(
            collective_id=0, has_side_effects=True, vmem_limit_bytes=KERNEL_VMEM
        ),
    )(tokens, cotangent, lengths, mat_a, mat_b, norms)


def update_kernel(*refs):
    square, output, input_grad = (ref[...] for ref in refs[:3])
    grad_norm = jnp.sqrt(square[0:1, 0:1])
    factor = CLIP_NORM / jnp.maximum(grad_norm, CLIP_NORM)
    inputs, outputs = refs[3:15], refs[15:]
    outputs[0][...] = grad_norm
    outputs[1][0] = output
    outputs[2][0] = input_grad
    for group, (rate, decay) in enumerate(
        ((MATRIX_RATE, MATRIX_DECAY), (MATRIX_RATE, MATRIX_DECAY), (NORM_RATE, 0.0))
    ):
        grad, weight, one, two = inputs[4 * group : 4 * group + 4]
        clip = grad[...].reshape(weight.shape) * factor
        moment, square_new, master = adam_update(weight[...], one[...], two[...], clip, rate, decay)
        for ref, value in zip(
            outputs[3 + 5 * group : 8 + 5 * group], (clip, moment, square_new, master, master.astype(LOW))
        ):
            ref[...] = value


def kernel_body(
    tokens, cotangent, lengths, mat_a, mat_b, norms, first_a, second_a, first_b, second_b, first_n, second_n
):
    norms, first_n, second_n = (jnp.swapaxes(value, 1, 2) for value in (norms, first_n, second_n))
    grad_a, grad_b, grad_n, square, output, input_grad = step_call(
        tokens, cotangent, lengths, mat_a, mat_b, norms
    )
    steps = 4

    def cut(value, dim):
        shape = tuple(size // steps if at == dim else size for at, size in enumerate(value.shape))
        return pl.BlockSpec(shape, lambda step: tuple(step if at == dim else 0 for at in range(len(shape))))

    def whole(value):
        return pl.BlockSpec(value.shape, lambda step: (0,) * len(value.shape))

    def like(value, kind=WIDE):
        return jax.ShapeDtypeStruct(value.shape, kind)

    args = (square, output, input_grad, grad_a, mat_a, first_a, second_a, grad_b, mat_b, first_b, second_b)
    specs = [whole(square), cut(output, 0), cut(input_grad, 0)]
    specs += [cut(grad_a, 0)] + [cut(mat_a, 1)] * 3 + [cut(grad_b, 1)] * 4
    args += (grad_n, norms, first_n, second_n)
    specs += [whole(grad_n)] + [whole(norms)] * 3
    shapes = [jax.ShapeDtypeStruct((1, 1), WIDE), like(output[None], LOW), like(input_grad[None])]
    out_specs = [whole(shapes[0]), cut(shapes[1], 1), cut(shapes[2], 1)]
    for value, spec in ((mat_a, cut(mat_a, 1)), (mat_b, cut(mat_b, 1)), (norms, whole(norms))):
        shapes += [like(value)] * 4 + [like(value, LOW)]
        out_specs += [spec] * 5
    results = pl.pallas_call(
        update_kernel,
        grid=(steps,),
        out_shape=shapes,
        in_specs=specs,
        out_specs=out_specs,
        compiler_params=pltpu.CompilerParams(vmem_limit_bytes=KERNEL_VMEM),
    )(*args)
    results = [results[0][0, 0], *results[1:]]
    results[-5:] = [jnp.swapaxes(value, 1, 2) for value in results[-5:]]
    return tuple(results)


def chosen_body(*args):
    rows_a = args[3].shape[1]
    groups = lax.axis_size("dp")
    by_kernel = rows_a % 32 == 0 and 2 * rows_a == LANES and groups * rows_a == args[0].shape[1]
    return (kernel_body if by_kernel else body)(*args)


def solution(mesh):
    placed = (
        P("dp", None),
        P("dp", None),
        P("dp", None),
        P("section", "dp", None),
        P(None, "dp", "section"),
        P("section", "dp", None),
        P("section", "dp", None),
        P("section", "dp", None),
        P(None, "dp", "section"),
        P(None, "dp", "section"),
        P("section", "dp", None),
        P("section", "dp", None),
    )
    return jax.shard_map(
        chosen_body,
        mesh=mesh,
        in_specs=placed,
        out_specs=(
            P(),
            P("section", "dp", None),
            P("section", "dp", None),
            P("section", "dp", None),
            P("section", "dp", None),
            P("section", "dp", None),
            P("section", "dp", None),
            P("section", "dp", None),
            P(None, "dp", "section"),
            P(None, "dp", "section"),
            P(None, "dp", "section"),
            P(None, "dp", "section"),
            P(None, "dp", "section"),
            P("section", "dp", None),
            P("section", "dp", None),
            P("section", "dp", None),
            P("section", "dp", None),
            P("section", "dp", None),
        ),
        check_vma=False,
    )
```

```python
import functools
import types

import jax
import jax.numpy as jnp
from jax import lax
from jax.experimental import pallas as pl
from jax.experimental.pallas import tpu as pltpu
from jax.sharding import PartitionSpec as P

HEADS = 8
STEP = 5


EPSILON = 1e-05
NEGATIVE = -1e30
CLIP_NORM = 1.0
BETA_ONE = 0.5
BETA_TWO = 0.5
ADAM_EPSILON = 1e-08
MATRIX_RATE = 0.05
NORM_RATE = 0.5
MATRIX_DECAY = 0.01


def norm_stats(value):
    centre = value - jnp.mean(value, -1, keepdims=True)
    inverse = lax.rsqrt(jnp.mean(centre * centre, -1, keepdims=True) + EPSILON)
    return (centre * inverse, inverse)


def norm_back(normal, inverse, upstream):
    return inverse * (
        upstream
        - jnp.mean(upstream, -1, keepdims=True)
        - normal * jnp.mean(upstream * normal, -1, keepdims=True)
    )


def adam_update(weight, moment_one, moment_two, gradient, step_rate, decay_rate):
    first_new = BETA_ONE * moment_one + (1.0 - BETA_ONE) * gradient
    second_new = BETA_TWO * moment_two + (1.0 - BETA_TWO) * gradient * gradient
    first_hat = first_new / (1.0 - BETA_ONE**STEP)
    second_hat = second_new / (1.0 - BETA_TWO**STEP)
    weight_new = weight - step_rate * (
        first_hat / (jnp.sqrt(second_hat) + ADAM_EPSILON) + decay_rate * weight
    )
    return (first_new, second_new, weight_new)


def segments_of(lengths_row, length):
    ends = jnp.cumsum(lengths_row, dtype=jnp.int32)
    places = jnp.arange(length, dtype=jnp.int32)
    segment = jnp.sum((ends[None, :] <= places[:, None]).astype(jnp.int32), axis=1, dtype=jnp.int32)
    live = (places < ends[-1]).astype(jnp.float32)
    return segment, live


def matmul(left, right, dims):
    return lax.dot_general(left, right, (dims, ((), ())), preferred_element_type=jnp.float32)


NN = ((1,), (0,))
NT = ((1,), (1,))
TN = ((0,), (0,))


def attention_forward(stream, weight, mask):
    length, width = stream.shape
    size = width // HEADS
    packed = matmul(stream, weight[:, : 3 * width], NN).astype(jnp.bfloat16)
    heads = packed.reshape(length, 3, HEADS, size)
    scores = jnp.einsum("qhd,khd->hqk", heads[:, 0], heads[:, 1], preferred_element_type=jnp.float32)
    scores = jnp.where(mask[None], scores * size**-0.5, NEGATIVE)
    weights = jnp.exp(scores - jnp.max(scores, -1, keepdims=True))
    probs = weights / jnp.sum(weights, -1, keepdims=True)
    mixed = jnp.einsum("hqk,khd->qhd", probs.astype(jnp.bfloat16), heads[:, 2], preferred_element_type=jnp.float32)
    mixed = mixed.reshape(length, width).astype(jnp.bfloat16)
    branch = matmul(mixed, weight[:, 3 * width :], NN)
    return branch, (heads, probs, mixed)


def attention_backward(stream, weight, kept, grad_low):
    heads, probs, mixed = kept
    length, width = stream.shape
    size = width // HEADS
    grad_out = matmul(mixed, grad_low, TN)
    grad_mixed = matmul(grad_low, weight[:, 3 * width :], NT).astype(jnp.bfloat16)
    grad_mixed = grad_mixed.reshape(length, HEADS, size)
    grad_probs = jnp.einsum("qhd,khd->hqk", grad_mixed, heads[:, 2], preferred_element_type=jnp.float32)
    centre = jnp.sum(probs * grad_probs, -1, keepdims=True)
    grad_scores = (probs * (grad_probs - centre)).astype(jnp.bfloat16)
    low = probs.astype(jnp.bfloat16)
    scale = size**-0.5
    grad_q = jnp.einsum("hqk,khd->qhd", grad_scores, heads[:, 1], preferred_element_type=jnp.float32) * scale
    grad_k = jnp.einsum("hqk,qhd->khd", grad_scores, heads[:, 0], preferred_element_type=jnp.float32) * scale
    grad_v = jnp.einsum("hqk,qhd->khd", low, grad_mixed, preferred_element_type=jnp.float32)
    packed = jnp.concatenate([grad_q, grad_k, grad_v], axis=1).reshape(length, 3 * width)
    packed = packed.astype(jnp.bfloat16)
    grad_in = matmul(stream, packed, TN)
    grad_inputs = matmul(packed, weight[:, : 3 * width], NT)
    return grad_inputs, jnp.concatenate([grad_in, grad_out], axis=1)


def feed_forward(stream, weight, down):
    pre = matmul(stream, weight, NN)
    active = jax.nn.gelu(pre, approximate=True).astype(jnp.bfloat16)
    return matmul(active, down, NN), (pre, active)


def feed_backward(stream, weight, down, kept, grad_low):
    pre, active = kept
    grad_down = matmul(active, grad_low, TN)
    grad_active = matmul(grad_low, down, NT)
    pull = jax.vjp(lambda value: jax.nn.gelu(value, approximate=True), pre)[1]
    grad_pre = pull(grad_active)[0].astype(jnp.bfloat16)
    grad_up = matmul(stream, grad_pre, TN)
    return matmul(grad_pre, weight, NT), grad_up, grad_down


def micro_step(rows, pull, segment, mats, downs, gains, biases):
    low = jnp.bfloat16
    mask = segment[:, None] == segment[None, :]
    stream, dual = rows, jnp.zeros_like(rows)
    saved = []
    for sub in range(4):
        if sub % 2 == 0:
            branch, kept = attention_forward(stream, mats[sub], mask)
        else:
            branch, kept = feed_forward(stream, mats[sub], downs[sub // 2])
        normal, inverse = norm_stats(stream.astype(jnp.float32) + branch)
        out = normal * gains[sub] + biases[sub]
        total = dual.astype(jnp.float32) + branch
        saved.append((stream, kept, normal, inverse))
        if sub < 3:
            stream, dual = out.astype(low), total.astype(low)
    dual_normal, dual_inverse = norm_stats(total)
    output = (out + dual_normal).astype(low)
    grad_out, grad_dual = pull, norm_back(dual_normal, dual_inverse, pull)
    grads_a, grads_b, grads_n = [None] * 4, [None] * 2, [None] * 4
    for sub in (3, 2, 1, 0):
        stream, kept, normal, inverse = saved[sub]
        grads_n[sub] = jnp.stack([jnp.sum(grad_out * normal, 0), jnp.sum(grad_out, 0)], axis=1)
        summed = norm_back(normal, inverse, grad_out * gains[sub])
        branch_low = (summed + grad_dual).astype(low)
        if sub % 2 == 0:
            inner, grads_a[sub] = attention_backward(stream, mats[sub], kept, branch_low)
        else:
            inner, grads_a[sub], grads_b[sub // 2] = feed_backward(
                stream, mats[sub], downs[sub // 2], kept, branch_low
            )
        grad_in = summed + inner
        if sub > 0:
            grad_out = grad_in.astype(low).astype(jnp.float32)
            grad_dual = grad_dual.astype(low).astype(jnp.float32)
    return output, grad_in, jnp.stack(grads_a), jnp.stack(grads_b), jnp.stack(grads_n)


def finish_step(grad_norm, output, input_grad, *groups):
    factor = CLIP_NORM / jnp.maximum(grad_norm, CLIP_NORM)
    results = [grad_norm, output[None], input_grad[None]]
    for weight, one, two, grad, rate, decay in groups:
        clip = grad * factor
        moment, square_new, master = adam_update(weight, one, two, clip, rate, decay)
        results += [clip, moment, square_new, master, master.astype(jnp.bfloat16)]
    return tuple(results)


def body(
    tokens, cotangent, lengths, mat_a, mat_b, norms, first_a, second_a, first_b, second_b, first_n, second_n
):
    low = jnp.bfloat16
    own = lax.axis_index("section")
    length = tokens.shape[0] // lengths.shape[0]
    rows = lax.dynamic_slice_in_dim(tokens, own * length, length, 0)
    segment, live = segments_of(lax.dynamic_index_in_dim(lengths, own, 0, keepdims=False), length)
    pull = lax.dynamic_slice_in_dim(cotangent, own * length, length, 0).astype(jnp.float32) * live[:, None]

    def gathered(value):
        return lax.all_gather(lax.all_gather(value, "dp", axis=1, tiled=True), "section", axis=0, tiled=True)

    mats = gathered(mat_a.astype(low))
    scales = gathered(norms.astype(low)).astype(jnp.float32)
    downs = lax.all_gather(mat_b.astype(low), "section", axis=2, tiled=True)
    downs = lax.all_gather(downs, "dp", axis=1, tiled=True)
    output, input_grad, part_a, part_b, part_n = micro_step(
        rows, pull, segment, mats, downs, scales[:, :, 0], scales[:, :, 1]
    )

    def scattered(value, section_dim):
        value = lax.psum_scatter(value, "section", scatter_dimension=section_dim, tiled=True)
        return lax.psum_scatter(value, "dp", scatter_dimension=1, tiled=True).astype(jnp.float32)

    grad_a = scattered(part_a.astype(low), 0)
    grad_b = scattered(part_b.astype(low), 2)
    grad_n = scattered(part_n, 0)
    square = jnp.sum(grad_a * grad_a) + jnp.sum(grad_b * grad_b) + jnp.sum(grad_n * grad_n)
    grad_norm = jnp.sqrt(lax.psum(square, ("section", "dp")))
    return finish_step(
        grad_norm, output, input_grad,
        (mat_a, first_a, second_a, grad_a, MATRIX_RATE, MATRIX_DECAY),
        (mat_b, first_b, second_b, grad_b, MATRIX_RATE, MATRIX_DECAY),
        (norms, first_n, second_n, grad_n, NORM_RATE, 0.0),
    )


LOW = jnp.bfloat16
WIDE = jnp.float32
MESH = pl.DeviceIdType.MESH
SECTIONS = 4
LANES = 128
BLOCK = 64
ROWS_FIRST = ()
KERNEL_VMEM = 64 * 1024 * 1024 - 256 * 1024


def gradient_items(rows_a, rows_b, cols_b, width, hidden):
    part = rows_a // SECTIONS
    return (
        ("B1", 3, cols_b // 2, rows_b),
        ("F3", 3, part, hidden // 2),
        ("O2", 2, part, width // 2),
        ("K2", 2, part, 3 * width // 2),
        ("B0", 1, cols_b // 2, rows_b),
        ("F1", 1, part, hidden // 2),
        ("O0", 0, part, width // 2),
        ("K0", 0, part, 3 * width // 2),
    )


def item_scratch(name, chips, rows, columns):
    piece = (rows, columns)
    return (
        ("own" + name, (chips, SECTIONS, 2) + piece, LOW),
        ("farx" + name, (chips,) + piece, LOW),
        ("fary" + name, (chips,) + piece, LOW),
        ("nearx" + name, (2, chips) + piece, LOW),
        ("neary" + name, (2, chips) + piece, LOW),
        ("line" + name, (chips, 2) + piece, LOW),
        ("done" + name, (2,) + piece if name[0] == "B" else (SECTIONS, 2) + piece, WIDE if name[0] == "B" else LOW),
    )


def kernel_scratch(chips, rows_a, rows_b, cols_b, length, width, hidden):
    devices = 2 * chips
    items = gradient_items(rows_a, rows_b, cols_b, width, hidden)
    count = len(items)
    received = sum((item_scratch(name, chips, rows, columns) for name, _, rows, columns in items), ())
    return received + (
        ("fac_s", (32,), None),
        ("fac_r", (32,), None),
        ("px_s", (count, 3), None),
        ("px_r", (count, 3), None),
        ("py_s", (count, 3), None),
        ("py_r", (count, 3), None),
        ("line_s", (count, chips), None),
        ("line_r", (count, chips), None),
        ("done_s", (count,), None),
        ("done_r", (count, SECTIONS), None),
        ("wa", (4, chips, 2, SECTIONS, rows_a // SECTIONS, hidden), LOW),
        ("wb", (2, chips, 2, rows_b, width), LOW),
        ("cut", (SECTIONS, rows_a // SECTIONS, hidden), LOW),
        ("tiles", (devices, SECTIONS, 8, LANES), WIDE),
        ("x", (4, length, width), LOW),
        ("xt", (4, chips, 2, rows_a, length), LOW),
        ("xtc", (4, chips, rows_a, 2 * length), LOW),
        ("y", (length, width), LOW),
        ("cot", (length, width), LOW),
        ("bias", (length, length), WIDE),
        ("live", (length, 1), WIDE),
        ("f", (length, width), WIDE),
        ("n", (4, length, width), WIDE),
        ("inv", (4, length, 1), WIDE),
        ("q", (2, length, width), LOW),
        ("k", (2, length, width), LOW),
        ("v", (2, length, width), LOW),
        ("kt", (2, width, length), LOW),
        ("vt", (2, width, length), LOW),
        ("ot", (2, chips, 2, rows_a, length), LOW),
        ("otc", (2, chips, rows_a, 2 * length), LOW),
        ("pt", (2, HEADS, length, length), LOW),
        ("g", (2, length, hidden), LOW),
        ("gc", (2, chips, 2 * length, rows_b), LOW),
        ("slope", (2, length, hidden), LOW),
        ("gx", (length, width), WIDE),
        ("gy", (length, width), WIDE),
        ("df", (2, 2 * length, width), LOW),
        ("dft", (2, width, 2 * length), LOW),
        ("dm", (length, width), LOW),
        ("dqt", (width, length), LOW),
        ("dh", (2, 2 * length, hidden), LOW),
        ("dp", (2, 2 * length, 3 * width), LOW),
        ("ng", (devices, 8, width), WIDE),
        ("ns", (SECTIONS, 8, width), WIDE),
        ("sq", (devices, 8, LANES), WIDE),
        ("sqs", (SECTIONS, 8, LANES), WIDE),
        ("sum", (8, LANES), WIDE),
        ("in_s", (2,), None),
        ("cut_s", (1,), None),
        ("cut_r", (SECTIONS,), None),
        ("qz_s", (2, chips, 2), None),
        ("qz_r", (chips, 2), None),
        ("gz_s", (6,), None),
        ("gz_r", (6, chips), None),
        ("gx_s", (6,), None),
        ("gx_r", (6,), None),
        ("gy_s", (6,), None),
        ("gy_r", (6,), None),
        ("rx_s", (6,), None),
        ("rx_r", (6,), None),
        ("ry_s", (6,), None),
        ("ry_r", (6,), None),
        ("gs_s", (6,), None),
        ("gs_r", (6,), None),
        ("small_s", (3, 2), None),
        ("small_r", (3, 2), None),
    )


INPUTS = ("tokens", "cotangent", "lengths", "mat_a", "mat_b", "norms")
OUTPUTS = ("grad_a", "grad_b", "grad_n", "square", "output", "input_grad")


def step_kernel(names, *refs):
    r = types.SimpleNamespace(**dict(zip(names, refs)))
    length, width = r.x.shape[1:]
    hidden = r.wa.shape[-1]
    rows_a, (rows_b, cols_b) = r.mat_a.shape[1], r.mat_b.shape[1:]
    devices = r.tiles.shape[0]
    chips = devices // 2
    half_b = cols_b // 2
    grad_items = gradient_items(rows_a, rows_b, cols_b, width, hidden)
    head = width // HEADS
    scale = head**-0.5

    s, d = lax.axis_index("section"), lax.axis_index("dp")
    z, c = lax.div(d, 2), lax.rem(d, 2)
    sx = s + 1 - 2 * lax.rem(s, 2)
    sy = lax.rem(s + 2, SECTIONS)
    sd = SECTIONS - 1 - s
    to_sibling = {"dp": d + 1 - 2 * c}
    to_up, to_down = {"dp": d + 2}, {"dp": d - 2}
    to_x, to_y = {"section": sx}, {"section": sy}
    below, above = z > 0, z < chips - 1
    group = [{"dp": lax.rem(d + step, devices)} for step in range(1, devices)]
    plane = [{"section": lax.rem(s + step, SECTIONS)} for step in range(1, SECTIONS)]
    finish = []

    def when(condition, work):
        if condition is None:
            work()
        else:
            pl.when(condition)(work)

    def push(source, target, send_sem, recv_sem, device):
        pltpu.make_async_remote_copy(
            src_ref=source,
            dst_ref=target,
            send_sem=send_sem,
            recv_sem=recv_sem,
            device_id=device,
            device_id_type=MESH,
        ).start()

    def arrived(target, sem):
        pltpu.make_async_remote_copy(
            src_ref=target, dst_ref=target, send_sem=sem, recv_sem=sem, device_id=to_x, device_id_type=MESH
        ).wait_recv()

    def sent(source, sem):
        pltpu.make_async_remote_copy(
            src_ref=source, dst_ref=source, send_sem=sem, recv_sem=sem, device_id=to_x, device_id_type=MESH
        ).wait_send()

    def at_end(condition, source, sem):
        finish.append((condition, source, sem))

    def aligned(start, size):
        return pl.ds(pl.multiple_of(start, size), size)

    own_x = pltpu.make_async_copy(r.tokens.at[aligned(s * length, length)], r.x.at[0], r.in_s.at[0])
    own_cot = pltpu.make_async_copy(r.cotangent.at[aligned(s * length, length)], r.cot, r.in_s.at[1])
    own_x.start()
    own_cot.start()
    barrier = pltpu.get_barrier_semaphore()
    for peer in group + plane:
        pl.semaphore_signal(barrier, inc=1, device_id=peer, device_id_type=MESH)
    r.cut[...] = r.mat_a[0].astype(LOW).reshape(SECTIONS, rows_a // SECTIONS, hidden)
    r.wa[s, z, c, s] = r.cut[s]
    for layer in range(2):
        r.wb[layer, z, c, :, aligned(s * cols_b, cols_b)] = r.mat_b[layer].astype(LOW)
    norms = r.norms[0].astype(LOW).astype(WIDE)
    nothing = jnp.zeros((2, rows_a), WIDE)
    even = jnp.concatenate([norms, nothing], axis=1)
    odd = jnp.concatenate([nothing, norms], axis=1)
    r.tiles[d, s, 0:2, :] = jnp.where(c == 0, even, odd)
    r.tiles[d, s, 2:8, :] = jnp.zeros((6, LANES), WIDE)
    pl.semaphore_wait(barrier, len(group) + len(plane))

    def small_out(which, source):
        for peer in group:
            push(source, source, r.small_s.at[which, 0], r.small_r.at[which, 0], peer)

    def small_group(which, like):
        arrived(like, r.small_r.at[which, 0])
        sent(like, r.small_s.at[which, 0])

    def small_plane_out(which, source):
        for peer in plane:
            push(source, source, r.small_s.at[which, 1], r.small_r.at[which, 1], peer)

    def small_plane(which, like):
        arrived(like, r.small_r.at[which, 1])
        sent(like, r.small_s.at[which, 1])

    every = slice(None)

    def block(item, chip, section):
        if item < 4:
            return r.wa.at[item, chip, c, section]
        return r.wb.at[item - 4, chip, c, :, aligned(section * cols_b, cols_b)]

    def half_block(item, section, half):
        if item < 4:
            return r.wa.at[item, :, c, section, :, pl.ds(half * hidden // 2, hidden // 2)]
        rows = pl.ds(half * rows_b // 2, rows_b // 2)
        return r.wb.at[item - 4, :, c, rows, aligned(section * cols_b, cols_b)]

    def half_piece(item, section, half):
        rows = pl.ds(half * rows_b // 2, rows_b // 2)
        return r.wb.at[item - 4, z, c, rows, aligned(section * cols_b, cols_b)]

    def core_blocks(item, core):
        return r.wa.at[item, :, core] if item < 4 else r.wb.at[item - 4, :, core]

    def cut_out():
        for section, device in ((sd, {"section": sd}), (sx, to_x), (sy, to_y)):
            push(r.cut.at[section], r.wa.at[s, z, c, section], r.cut_s.at[0], r.cut_r.at[s], device)
        at_end(None, r.cut.at[pl.ds(0, SECTIONS - 1)], r.cut_s.at[0])

    def cut_in():
        for section in (sx, sy, sd):
            arrived(r.wa.at[section, z, c, s], r.cut_r.at[section])

    def line_out(item):
        if item in ROWS_FIRST:
            rows_out(item)
            return
        own = block(item, z, s)

        def to_chip(chip):
            push(own, own, r.gz_s.at[item], r.gz_r.at[item, z], {"dp": 2 * chip + c})

        for step in range(1, chips):
            when(z >= step, functools.partial(to_chip, z - step))
            when(z + step < chips, functools.partial(to_chip, z + step))
        several = block(item, pl.ds(0, chips - 1), s)
        at_end(None, several, r.gz_s.at[item])

    def plane_out(item, chip):
        own = block(item, chip, s)
        push(own, own, r.gx_s.at[item], r.gx_r.at[item], to_x)
        push(own, own, r.gy_s.at[item], r.gy_r.at[item], to_y)

    def row_half(item, chip, half):
        return r.wb.at[item - 4, chip, c, pl.ds(half * rows_b // 2, rows_b // 2), :]

    def rows_on(item, chip, half, way):
        rows = row_half(item, chip, half)
        when(
            below if way else above,
            lambda: push(
                rows, rows, r.qz_s.at[way, chip, half], r.qz_r.at[chip, half], to_down if way else to_up
            ),
        )

    def rows_out(item):
        for half, sem in ((0, r.rx_r), (1, r.ry_r)):
            arrived(half_piece(item, sd, half), sem.at[item])
            for way in range(2):
                rows_on(item, z, half, way)
        rows = r.wb.at[item - 4, z, c]
        push(rows, rows, r.gs_s.at[item], r.gs_r.at[item], to_sibling)
        for chip in range(chips):
            for half in range(2):
                at_end(above & (z >= chip), row_half(item, 0, half), r.qz_s.at[0, chip, half])
                at_end(below & (z <= chip), row_half(item, 0, half), r.qz_s.at[1, chip, half])

    def rows_step(item, step):
        def take(chip, way):
            for half in range(2):
                arrived(row_half(item, chip, half), r.qz_r.at[chip, half])
                rows_on(item, chip, half, way)
            rows = r.wb.at[item - 4, chip, c]
            push(rows, rows, r.gs_s.at[item], r.gs_r.at[item], to_sibling)

        when(z >= step, lambda: take(z - step, 0))
        when(z + step < chips, lambda: take(z + step, 1))
        if step == chips - 1:
            at_end(None, core_blocks(item, c), r.gs_s.at[item])

    def line_in(item):
        for step in range(1, chips):
            chip = lax.rem(z + step, chips)
            arrived(block(item, chip, s), r.gz_r.at[item, chip])
            plane_out(item, chip)
        core_out(item, s)
        at_end(None, block(item, every, s), r.gx_s.at[item])
        at_end(None, block(item, every, s), r.gy_s.at[item])

    def core_out(item, section):
        blocks = block(item, every, section)
        push(blocks, blocks, r.gs_s.at[item], r.gs_r.at[item], to_sibling)

    def plane_in(item):
        over = z if item in ROWS_FIRST else every
        piece = half_piece if item in ROWS_FIRST else half_block
        arrived(block(item, over, sx), r.gx_r.at[item])
        part = piece(item, sx, 1)
        push(part, part, r.ry_s.at[item], r.ry_r.at[item], to_y)
        arrived(block(item, over, sy), r.gy_r.at[item])
        part = piece(item, sy, 0)
        push(part, part, r.rx_s.at[item], r.rx_r.at[item], to_x)
        if item in ROWS_FIRST:
            at_end(None, block(item, z, sx), r.gx_s.at[item])
            at_end(None, block(item, z, sx), r.gy_s.at[item])
        else:
            core_out(item, sx)
            core_out(item, sy)
        at_end(None, part, r.ry_s.at[item])
        at_end(None, part, r.rx_s.at[item])

    def far_in(item):
        arrived(half_block(item, sd, 0), r.rx_r.at[item])
        arrived(half_block(item, sd, 1), r.ry_r.at[item])
        core_out(item, sd)
        at_end(None, core_blocks(item, c), r.gs_s.at[item])

    def core_in(item):
        arrived(core_blocks(item, 1 - c), r.gs_r.at[item])

    mine, other = pl.ds(0, length), pl.ds(length, length)

    def give(slot, source, target):
        push(source, target, r.fac_s.at[slot], r.fac_r.at[slot], to_sibling)
        at_end(None, target, r.fac_s.at[slot])

    def taken(slot, target):
        arrived(target, r.fac_r.at[slot])

    def give_rows(layer):
        r.xt[layer] = r.x[layer].T.reshape(chips, 2, rows_a, length)
        r.xtc[layer, :, :, 0:length] = r.xt[layer, :, c]
        give(layer, r.xt.at[layer, :, 1 - c], r.xtc.at[layer, :, :, other])

    def product(left, right, dims):
        return lax.dot_general(left, right, (dims, ((), ())), preferred_element_type=WIDE)

    def loop(count, work):
        def one(index, carry):
            work(index)
            return carry

        lax.fori_loop(0, count, one, 0)

    def gain_row(layer, kind):
        parts = [
            r.tiles[2 * chip, layer, kind : kind + 1, :] + r.tiles[2 * chip + 1, layer, kind : kind + 1, :]
            for chip in range(chips)
        ]
        return jnp.concatenate(parts, axis=1)

    def stats(value):
        centre = value - jnp.mean(value, -1, keepdims=True)
        inverse = lax.rsqrt(jnp.mean(centre * centre, -1, keepdims=True) + EPSILON)
        return centre * inverse, inverse

    lane = lax.broadcasted_iota(jnp.int32, (1, 2 * head), 1)
    first_half = (lane < head).astype(WIDE)
    half_masks = (first_half.astype(LOW), (1.0 - first_half).astype(LOW))

    def prepare_masks():
        ends, total = [], jnp.int32(0)
        for slot in range(r.lengths.shape[1]):
            total = total + r.lengths[s, slot]
            ends.append(total)
        down_places = lax.broadcasted_iota(jnp.int32, (length, 1), 0)
        across_places = lax.broadcasted_iota(jnp.int32, (1, length), 1)
        down_segment = jnp.zeros((length, 1), jnp.int32)
        across_segment = jnp.zeros((1, length), jnp.int32)
        for end in ends:
            down_segment = down_segment + (end <= down_places).astype(jnp.int32)
            across_segment = across_segment + (end <= across_places).astype(jnp.int32)
        r.bias[...] = jnp.where(down_segment == across_segment, 0.0, NEGATIVE)
        r.live[...] = (down_places < total).astype(WIDE)

    def matrix(layer, place):
        value = r.wa[layer, :, :, :, :, place]
        return value.reshape(width, value.shape[-1])

    def attention_in(layer):
        at = layer // 2
        rows = r.x[layer]
        r.q[at] = product(rows, matrix(layer, pl.ds(0, width)), NN).astype(LOW) * jnp.asarray(scale, LOW)
        keys = product(rows, matrix(layer, pl.ds(width, width)), NN).astype(LOW)
        r.k[at] = keys
        values = product(rows, matrix(layer, pl.ds(2 * width, width)), NN).astype(LOW)
        r.v[at] = values
        r.vt[at] = values.T

    def attention_heads(layer, begin, count):
        at = layer // 2

        def pair(index):
            lanes = aligned(index * 2 * head, 2 * head)
            for which in range(2):
                scores = product(r.k[at, :, lanes], r.q[at, :, lanes] * half_masks[which], NT) + r.bias[...]
                weights = jnp.exp(scores - jnp.max(scores, 0, keepdims=True))
                probs = (weights * (1.0 / jnp.sum(weights, 0, keepdims=True))).astype(LOW)
                r.pt[at, 2 * index + which] = probs
                place = aligned((2 * index + which) * head, head)
                r.ot[at, index, which] = product(r.vt[at, place, :], probs, NN).astype(LOW)

        for index in range(begin, begin + count):
            pair(index)

    def attention_out(layer):
        at = layer // 2
        r.otc[at, :, :, 0:length] = r.ot[at, :, c]
        give(4 + at, r.ot.at[at, :, 1 - c], r.otc.at[at, :, :, other])
        r.f[...] = product(r.ot[at].reshape(width, length).T, matrix(layer, pl.ds(3 * width, width)), NN)

    def expand(layer, index):
        at = layer // 2
        place = pl.ds(index * width, width)
        pre = product(r.x[layer], matrix(layer, place), NN)
        squared = pre * pre
        slope = 0.7978845608 * (1.0 + 3 * 0.044715 * squared)
        bent = jnp.tanh(0.7978845608 * pre * (1.0 + 0.044715 * squared))
        r.g[at, :, place] = (0.5 * pre * (1.0 + bent)).astype(LOW)
        r.slope[at, :, place] = (0.5 * (1.0 + bent) + 0.5 * pre * (1.0 - bent * bent) * slope).astype(LOW)
        block = aligned((2 * index + c) * rows_b, rows_b)
        r.gc[at, index, 0:length, :] = r.g[at, :, block]
        block = aligned((2 * index + 1 - c) * rows_b, rows_b)
        give(6 + chips * at + index, r.g.at[at, :, block], r.gc.at[at, index, other, :])

    def contract(layer):
        r.f[...] = product(r.g[layer // 2], r.wb[layer // 2].reshape(hidden, width), NN)

    def by_rows(work):
        for index in range(length // BLOCK):
            work(pl.ds(index * BLOCK, BLOCK))

    def normalize(layer):
        gain, offset = gain_row(layer, 0), gain_row(layer, 1)

        def some(rows):
            branch = r.f[rows, :]
            normal, inverse = stats(r.x[layer, rows, :].astype(WIDE) + branch)
            r.n[layer, rows, :] = normal
            r.inv[layer, rows, :] = inverse
            out = normal * gain + offset
            dual = branch if layer == 0 else r.y[rows, :].astype(WIDE) + branch
            if layer < 3:
                r.x[layer + 1, rows, :] = out.astype(LOW)
                r.y[rows, :] = dual.astype(LOW)
            else:
                dual_normal, dual_inverse = stats(dual)
                r.output[rows, :] = (out + dual_normal).astype(LOW)
                pull = r.cot[rows, :].astype(WIDE) * r.live[rows, :]
                r.gx[rows, :] = pull
                r.gy[rows, :] = norm_back(dual_normal, dual_inverse, pull)

        by_rows(some)

    def back_normalize(layer):
        gain = gain_row(layer, 0)

        def some(index, sums):
            rows = pl.ds(index * BLOCK, BLOCK)
            upstream = r.gx[rows, :]
            normal = r.n[layer, rows, :]
            summed = norm_back(normal, r.inv[layer, rows, :], upstream * gain)
            dual = r.gy[rows, :]
            r.gx[rows, :] = summed
            r.df[layer // 2, rows, :] = (summed + dual).astype(LOW)
            if layer == 3:
                r.gy[rows, :] = dual.astype(LOW).astype(WIDE)
            return (
                sums[0] + jnp.sum(upstream * normal, 0, keepdims=True),
                sums[1] + jnp.sum(upstream, 0, keepdims=True),
            )

        zero = jnp.zeros((1, width), WIDE)
        gains, offsets = zero, zero
        for index in range(length // BLOCK):
            gains, offsets = some(index, (gains, offsets))
        r.ng[d, 2 * layer : 2 * layer + 1, :] = gains
        r.ng[d, 2 * layer + 1 : 2 * layer + 2, :] = offsets

    def pass_down(layer, inner):
        total = r.gx[...] + inner
        if layer > 0:
            r.gx[...] = total.astype(LOW).astype(WIDE)
        else:
            r.input_grad[...] = total

    base = 6 + 2 * chips

    def back_hidden(layer):
        at = layer // 2
        r.dft[at, :, 0:length] = r.df[at, 0:length, :].T
        give(base + at, r.dft.at[at, :, mine], r.dft.at[at, :, other])
        for index in range(hidden // width):
            place = pl.ds(index * width, width)
            pulled = product(r.df[at, 0:length, :], r.wb[at, index].reshape(width, width), NT)
            r.dh[at, 0:length, place] = (pulled * r.slope[at, :, place].astype(WIDE)).astype(LOW)
            give(base + 2 + chips * at + index, r.dh.at[at, mine, place], r.dh.at[at, other, place])

    def back_expand_end(layer):
        pass_down(layer, product(r.dh[layer // 2, 0:length, :], matrix(layer, pl.ds(0, hidden)), NT))

    def back_output(layer):
        at = layer // 2
        give(base + 2 + 2 * chips + at, r.df.at[at, mine], r.df.at[at, other])
        r.dm[...] = product(r.df[at, 0:length, :], matrix(layer, pl.ds(3 * width, width)), NT).astype(LOW)
        r.kt[at] = (r.k[at] * jnp.asarray(scale, LOW)).T

    def back_heads(layer, begin, count):
        at = layer // 2

        def pair(index):
            lanes = aligned(index * 2 * head, 2 * head)
            pulled = r.dm[:, lanes]
            keys, values = [], []
            for which in range(2):
                probs = r.pt[at, 2 * index + which]
                grad = product(r.v[at, :, lanes], pulled * half_masks[which], NT)
                full = probs.astype(WIDE)
                centre = jnp.sum(full * grad, 0, keepdims=True)
                scores = (full * (grad - centre)).astype(LOW)
                keys.append(product(scores, r.q[at, :, lanes], NN))
                values.append(product(probs, pulled, NN))
                place = aligned((2 * index + which) * head, head)
                r.dqt[place, :] = product(r.kt[at, place, :], scores, NN).astype(LOW)
            r.dp[at, 0:length, aligned(width + index * 2 * head, 2 * head)] = jnp.where(
                lane < head, keys[0], keys[1]
            ).astype(LOW)
            r.dp[at, 0:length, aligned(2 * width + index * 2 * head, 2 * head)] = jnp.where(
                lane < head, values[0], values[1]
            ).astype(LOW)

        def pairs(step):
            pair(begin + 2 * step)
            pair(begin + 2 * step + 1)

        loop(count // 2, pairs)

    def back_packed(layer):
        at = layer // 2
        slot = base + 4 + 2 * chips + 2 * at
        place = pl.ds(width, 2 * width)
        give(slot, r.dp.at[at, mine, place], r.dp.at[at, other, place])
        r.dp[at, 0:length, 0:width] = r.dqt[...].T
        place = pl.ds(0, width)
        give(slot + 1, r.dp.at[at, mine, place], r.dp.at[at, other, place])

    def back_packed_end(layer):
        pass_down(layer, product(r.dp[layer // 2, 0:length, :], matrix(layer, pl.ds(0, 3 * width)), NT))

    def keep(name, half, place, value):
        own = getattr(r, "own" + name)
        own[:, :, half, :, place] = value.astype(LOW).reshape(chips, SECTIONS, rows_a // SECTIONS, value.shape[1])

    def chip_rows(value):
        return value.reshape(chips * rows_a, 2 * length)

    def grad_down(at):
        own = getattr(r, "ownB%d" % at)
        taken(base + at, r.dft.at[at, :, other])
        for chip in range(chips):
            taken(6 + chips * at + chip, r.gc.at[at, chip, other, :])
            value = product(r.dft[at], r.gc[at, chip], NN)
            own[chip] = value.astype(LOW).reshape(SECTIONS, 2, half_b, rows_b)

    def grad_up(layer):
        at = layer // 2
        taken(layer, r.xtc.at[layer, :, :, other])
        for index in range(hidden // width):
            place = pl.ds(index * width, width)
            taken(base + 2 + chips * at + index, r.dh.at[at, other, place])
            value = product(chip_rows(r.xtc[layer]), r.dh[at, :, place], NN)
            keep("F%d" % layer, index // 2, pl.ds(index % 2 * width, width), value)

    def grad_output(layer):
        at = layer // 2
        taken(4 + at, r.otc.at[at, :, :, other])
        taken(base + 2 + 2 * chips + at, r.df.at[at, other])
        for half in range(2):
            place = pl.ds(half * width // 2, width // 2)
            value = product(chip_rows(r.otc[at]), r.df[at, :, place], NN)
            keep("O%d" % layer, half, pl.ds(0, width // 2), value)

    def grad_packed(layer):
        at = layer // 2
        slot = base + 4 + 2 * chips + 2 * at
        taken(layer, r.xtc.at[layer, :, :, other])
        taken(slot, r.dp.at[at, other, pl.ds(width, 2 * width)])
        taken(slot + 1, r.dp.at[at, other, pl.ds(0, width)])
        part = 3 * width // 2
        for half in range(2):
            value = product(chip_rows(r.xtc[layer]), r.dp[at, :, half * part : (half + 1) * part], NN)
            keep("K%d" % layer, half, pl.ds(0, part), value)

    def joined(target, others):
        return functools.reduce(
            lambda left, right: left + right, [ref[...].astype(WIDE) for ref in (target, *others)]
        )

    def add_into(target, others):
        if len(others) == 1:
            target[...] = target[...] + others[0][...]
        else:
            target[...] = joined(target, others).astype(LOW)

    places = {name: place for place, (name, _, _, _) in enumerate(grad_items)}

    def buffers(name):
        parts = ("own", "farx", "fary", "nearx", "neary", "line", "done")
        return types.SimpleNamespace(**{part: getattr(r, part + name) for part in parts})

    def to_plane(name):
        item, place = buffers(name), places[name]

        def over_x(section, half, target, slot):
            push(item.own.at[:, section, half], target, r.px_s.at[place, slot], r.px_r.at[place, slot], to_x)
            at_end(None, item.farx, r.px_s.at[place, slot])

        def over_y(section, half, target, slot):
            push(item.own.at[:, section, half], target, r.py_s.at[place, slot], r.py_r.at[place, slot], to_y)
            at_end(None, item.farx, r.py_s.at[place, slot])

        over_x(sd, 0, item.farx, 2)
        over_y(sd, 1, item.fary, 2)
        over_x(sx, 0, item.nearx.at[0], 0)
        over_y(sy, 1, item.neary.at[1], 1)

    def through_plane(name):
        item, place = buffers(name), places[name]
        own = item.own
        arrived(item.fary, r.py_r.at[place, 2])
        add_into(own.at[:, sx, 1], [item.fary])
        push(own.at[:, sx, 1], item.nearx.at[1], r.px_s.at[place, 1], r.px_r.at[place, 1], to_x)
        at_end(None, item.farx, r.px_s.at[place, 1])
        arrived(item.farx, r.px_r.at[place, 2])
        add_into(own.at[:, sy, 0], [item.farx])
        push(own.at[:, sy, 0], item.neary.at[0], r.py_s.at[place, 0], r.py_r.at[place, 0], to_y)
        at_end(None, item.farx, r.py_s.at[place, 0])

    def to_line(name):
        item, place = buffers(name), places[name]
        own = item.own.at[:, s]
        for half in range(2):
            arrived(item.nearx.at[half], r.px_r.at[place, half])
            arrived(item.neary.at[half], r.py_r.at[place, half])
            add_into(own.at[:, half], [item.nearx.at[half], item.neary.at[half]])
        for step in range(1, chips):
            chip = lax.rem(z + step, chips)
            push(
                own.at[chip],
                item.line.at[z],
                r.line_s.at[place, step],
                r.line_r.at[place, z],
                {"dp": 2 * chip + c},
            )
            at_end(None, item.line.at[0], r.line_s.at[place, step])

    def to_owner(name):
        item, place = buffers(name), places[name]
        others = [lax.rem(z + step, chips) for step in range(1, chips)]
        for chip in others:
            arrived(item.line.at[chip], r.line_r.at[place, chip])
        total = joined(item.own.at[z, s], [item.line.at[chip] for chip in others])
        square = total * total
        while square.ndim > 2:
            square = jnp.sum(square, 0)
        square = jnp.sum(jnp.sum(square, 0, keepdims=True), 1, keepdims=True)
        r.sum[...] = r.sum[...] + jnp.broadcast_to(square, (8, LANES))
        if name[0] == "B":
            item.done[...] = total
            return
        item.done[s] = total.astype(LOW)
        layer = grad_items[place][1]
        mine = item.done.at[s]
        away = s != layer
        when(
            away,
            lambda: push(mine, mine, r.done_s.at[place], r.done_r.at[place, s], {"section": jnp.int32(layer)}),
        )
        at_end(away, mine, r.done_s.at[place])

    def collect(name):
        item, place = buffers(name), places[name]
        layer = grad_items[place][1]

        def work():
            for section in range(SECTIONS):
                if section != layer:
                    arrived(item.done.at[section], r.done_r.at[place, section])
            columns = item.done.shape[-1]
            start = 3 * width if name[0] == "O" else 0
            for section in range(SECTIONS):
                for half in range(2):
                    rows = pl.ds(section * (rows_a // SECTIONS), rows_a // SECTIONS)
                    place_to = pl.ds(start + half * columns, columns)
                    r.grad_a[rows, place_to] = item.done[section, half].astype(WIDE)

        when(s == layer, work)

    def all_sent(count=None):
        for condition, source, sem in finish[:count]:
            when(condition, functools.partial(sent, source, sem))
        del finish[:count]

    cut_out()
    small_out(0, r.tiles.at[d, s])
    line_out(4)
    plane_out(4, z)
    plane_out(5, z)
    cut_in()
    plane_out(1, z)
    line_out(0)
    line_out(1)
    plane_out(3, z)
    plane_out(0, z)
    line_in(4)
    small_group(0, r.tiles.at[pl.ds(0, devices - 1), 0])
    for peer in plane:
        push(r.tiles.at[:, s], r.tiles.at[:, s], r.small_s.at[0, 1], r.small_r.at[0, 1], peer)
    line_in(0)
    plane_out(2, z)
    line_out(2)
    line_out(3)
    line_in(1)
    plane_in(0)
    plane_in(4)
    far_in(0)
    line_out(5)
    plane_in(1)
    line_in(2)
    own_x.wait()
    own_cot.wait()
    prepare_masks()
    core_in(0)
    attention_in(0)
    attention_heads(0, 0, 2)
    attention_heads(0, 2, 2)
    far_in(1)
    line_in(3)
    attention_out(0)
    small_plane(0, r.tiles.at[:, pl.ds(0, SECTIONS - 1)])
    normalize(0)
    far_in(4)
    core_in(1)
    plane_in(2)
    expand(1, 0)
    expand(1, 1)
    line_in(5)
    expand(1, 2)
    expand(1, 3)
    early = len(finish)
    far_in(2)
    plane_in(3)
    core_in(4)
    contract(1)
    normalize(1)
    core_in(2)
    attention_in(2)
    plane_in(5)
    attention_heads(2, 0, 2)
    attention_heads(2, 2, 2)
    far_in(3)
    attention_out(2)
    normalize(2)
    core_in(3)
    expand(3, 0)
    far_in(5)
    expand(3, 1)
    expand(3, 2)
    expand(3, 3)
    all_sent(early)
    core_in(5)
    contract(3)
    normalize(3)

    r.sum[...] = jnp.zeros((8, LANES), WIDE)
    back_normalize(3)
    back_hidden(3)
    give_rows(3)
    back_expand_end(3)
    back_normalize(2)
    grad_up(3)
    to_plane("F3")
    back_output(2)
    grad_down(1)
    to_plane("B1")
    back_heads(2, 0, 2)
    back_heads(2, 2, 2)
    back_packed(2)
    through_plane("B1")
    give_rows(2)
    grad_output(2)
    back_packed_end(2)
    give_rows(1)
    to_plane("O2")
    grad_packed(2)
    to_plane("K2")
    back_normalize(1)
    back_hidden(1)
    through_plane("K2")
    grad_down(0)
    to_plane("B0")
    back_expand_end(1)
    back_normalize(0)
    small_out(1, r.ng.at[d])
    to_line("K2")
    to_line("B1")
    back_output(0)
    grad_up(1)
    through_plane("B0")
    to_plane("F1")
    back_heads(0, 0, 2)
    back_heads(0, 2, 2)
    back_packed(0)
    to_line("B0")
    through_plane("O2")
    through_plane("F1")
    grad_output(0)
    to_plane("O0")
    give_rows(0)
    grad_packed(0)
    to_plane("K0")
    to_line("O2")
    to_line("F1")
    through_plane("O0")
    to_owner("B1")
    back_packed_end(0)
    to_owner("B0")
    all_sent()
    through_plane("K0")
    small_group(1, r.ng.at[pl.ds(0, devices - 1)])
    r.ns[s] = functools.reduce(lambda left, right: left + right, [r.ng[index] for index in range(devices)])
    small_plane_out(1, r.ns.at[s])
    through_plane("F3")
    to_line("O0")
    to_line("K0")
    to_owner("F1")
    to_line("F3")
    to_owner("O2")
    to_owner("K2")
    to_owner("F3")
    to_owner("O0")
    to_owner("K0")

    r.sq[d] = r.sum[...]
    small_out(2, r.sq.at[d])
    for name in ("F1", "O2", "K2", "F3"):
        collect(name)
    collect("O0")
    for layer in range(2):
        done = buffers("B%d" % layer).done
        r.grad_b[layer] = done[...].reshape(cols_b, rows_b).T
    small_plane(1, r.ns.at[pl.ds(0, SECTIONS - 1)])
    grads = functools.reduce(lambda left, right: left + right, [r.ns[index] for index in range(SECTIONS)])
    norm_square = jnp.sum(jnp.sum(grads * grads, 0, keepdims=True), 1, keepdims=True)
    chosen = jnp.zeros((2, width), WIDE)
    for layer in range(4):
        chosen = jnp.where(s == layer, grads[2 * layer : 2 * layer + 2, :], chosen)
    for chip in range(chips):
        pair_of = chosen[:, chip * LANES : (chip + 1) * LANES]
        r.grad_n[...] = jnp.where(
            z == chip, jnp.where(c == 0, pair_of[:, :rows_a], pair_of[:, rows_a:]), r.grad_n[...]
        )
    collect("K0")
    small_group(2, r.sq.at[pl.ds(0, devices - 1)])
    r.sqs[s] = functools.reduce(lambda left, right: left + right, [r.sq[index] for index in range(devices)])
    small_plane_out(2, r.sqs.at[s])
    all_sent()
    small_plane(2, r.sqs.at[pl.ds(0, SECTIONS - 1)])
    squares = functools.reduce(lambda left, right: left + right, [r.sqs[index] for index in range(SECTIONS)])
    r.square[...] = squares + norm_square


def step_call(tokens, cotangent, lengths, mat_a, mat_b, norms):
    rows_a, hidden = mat_a.shape[1:]
    rows_b, cols_b = mat_b.shape[1:]
    width = tokens.shape[1]
    length = tokens.shape[0] // lengths.shape[0]
    chips = width // rows_a // 2
    scratch = kernel_scratch(chips, rows_a, rows_b, cols_b, length, width, hidden)
    shapes = []
    for _, shape, kind in scratch:
        shapes.append(pltpu.SemaphoreType.DMA(shape) if kind is None else pltpu.VMEM(shape, kind))
    anywhere, vmem = pl.BlockSpec(memory_space=pl.ANY), pl.BlockSpec(memory_space=pltpu.VMEM)
    return pl.pallas_call(
        functools.partial(step_kernel, INPUTS + OUTPUTS + tuple(name for name, _, _ in scratch)),
        out_shape=(
            jax.ShapeDtypeStruct((rows_a, hidden), WIDE),
            jax.ShapeDtypeStruct(mat_b.shape, WIDE),
            jax.ShapeDtypeStruct((2, rows_a), WIDE),
            jax.ShapeDtypeStruct((8, LANES), WIDE),
            jax.ShapeDtypeStruct((length, width), LOW),
            jax.ShapeDtypeStruct((length, width), WIDE),
        ),
        in_specs=[anywhere, anywhere, pl.BlockSpec(memory_space=pltpu.SMEM), vmem, vmem, vmem],
        out_specs=[vmem] * len(OUTPUTS),
        scratch_shapes=shapes,
        compiler_params=pltpu.CompilerParams(
            collective_id=0, has_side_effects=True, vmem_limit_bytes=KERNEL_VMEM
        ),
    )(tokens, cotangent, lengths, mat_a, mat_b, norms)


def update_kernel(*refs):
    square, output, input_grad = (ref[...] for ref in refs[:3])
    grad_norm = jnp.sqrt(square[0:1, 0:1])
    factor = CLIP_NORM / jnp.maximum(grad_norm, CLIP_NORM)
    inputs, outputs = refs[3:15], refs[15:]
    outputs[0][...] = grad_norm
    outputs[1][0] = output
    outputs[2][0] = input_grad
    for group, (rate, decay) in enumerate(
        ((MATRIX_RATE, MATRIX_DECAY), (MATRIX_RATE, MATRIX_DECAY), (NORM_RATE, 0.0))
    ):
        grad, weight, one, two = inputs[4 * group : 4 * group + 4]
        clip = grad[...].reshape(weight.shape) * factor
        moment, square_new, master = adam_update(weight[...], one[...], two[...], clip, rate, decay)
        for ref, value in zip(
            outputs[3 + 5 * group : 8 + 5 * group], (clip, moment, square_new, master, master.astype(LOW))
        ):
            ref[...] = value


def kernel_body(
    tokens, cotangent, lengths, mat_a, mat_b, norms, first_a, second_a, first_b, second_b, first_n, second_n
):
    norms, first_n, second_n = (jnp.swapaxes(value, 1, 2) for value in (norms, first_n, second_n))
    grad_a, grad_b, grad_n, square, output, input_grad = step_call(
        tokens, cotangent, lengths, mat_a, mat_b, norms
    )
    steps = 4

    def cut(value, dim):
        shape = tuple(size // steps if at == dim else size for at, size in enumerate(value.shape))
        return pl.BlockSpec(shape, lambda step: tuple(step if at == dim else 0 for at in range(len(shape))))

    def whole(value):
        return pl.BlockSpec(value.shape, lambda step: (0,) * len(value.shape))

    def like(value, kind=WIDE):
        return jax.ShapeDtypeStruct(value.shape, kind)

    args = (square, output, input_grad, grad_a, mat_a, first_a, second_a, grad_b, mat_b, first_b, second_b)
    specs = [whole(square), cut(output, 0), cut(input_grad, 0)]
    specs += [cut(grad_a, 0)] + [cut(mat_a, 1)] * 3 + [cut(grad_b, 1)] * 4
    args += (grad_n, norms, first_n, second_n)
    specs += [whole(grad_n)] + [whole(norms)] * 3
    shapes = [jax.ShapeDtypeStruct((1, 1), WIDE), like(output[None], LOW), like(input_grad[None])]
    out_specs = [whole(shapes[0]), cut(shapes[1], 1), cut(shapes[2], 1)]
    for value, spec in ((mat_a, cut(mat_a, 1)), (mat_b, cut(mat_b, 1)), (norms, whole(norms))):
        shapes += [like(value)] * 4 + [like(value, LOW)]
        out_specs += [spec] * 5
    results = pl.pallas_call(
        update_kernel,
        grid=(steps,),
        out_shape=shapes,
        in_specs=specs,
        out_specs=out_specs,
        compiler_params=pltpu.CompilerParams(vmem_limit_bytes=KERNEL_VMEM),
    )(*args)
    results = [results[0][0, 0], *results[1:]]
    results[-5:] = [jnp.swapaxes(value, 1, 2) for value in results[-5:]]
    return tuple(results)


def chosen_body(*args):
    rows_a = args[3].shape[1]
    groups = lax.axis_size("dp")
    by_kernel = rows_a % 32 == 0 and 2 * rows_a == LANES and groups * rows_a == args[0].shape[1]
    return (kernel_body if by_kernel else body)(*args)


def solution(mesh):
    placed = (
        P("dp", None),
        P("dp", None),
        P("dp", None),
        P("section", "dp", None),
        P(None, "dp", "section"),
        P("section", "dp", None),
        P("section", "dp", None),
        P("section", "dp", None),
        P(None, "dp", "section"),
        P(None, "dp", "section"),
        P("section", "dp", None),
        P("section", "dp", None),
    )
    return jax.shard_map(
        chosen_body,
        mesh=mesh,
        in_specs=placed,
        out_specs=(
            P(),
            P("section", "dp", None),
            P("section", "dp", None),
            P("section", "dp", None),
            P("section", "dp", None),
            P("section", "dp", None),
            P("section", "dp", None),
            P("section", "dp", None),
            P(None, "dp", "section"),
            P(None, "dp", "section"),
            P(None, "dp", "section"),
            P(None, "dp", "section"),
            P(None, "dp", "section"),
            P("section", "dp", None),
            P("section", "dp", None),
            P("section", "dp", None),
            P("section", "dp", None),
            P("section", "dp", None),
        ),
        check_vma=False,
    )
```

```python
import functools
import types

import jax
import jax.numpy as jnp
from jax import lax
from jax.experimental import pallas as pl
from jax.experimental.pallas import tpu as pltpu
from jax.sharding import PartitionSpec as P

HEADS = 8
STEP = 5


EPSILON = 1e-05
NEGATIVE = -1e30
CLIP_NORM = 1.0
BETA_ONE = 0.5
BETA_TWO = 0.5
ADAM_EPSILON = 1e-08
MATRIX_RATE = 0.05
NORM_RATE = 0.5
MATRIX_DECAY = 0.01


def norm_stats(value):
    centre = value - jnp.mean(value, -1, keepdims=True)
    inverse = lax.rsqrt(jnp.mean(centre * centre, -1, keepdims=True) + EPSILON)
    return (centre * inverse, inverse)


def norm_back(normal, inverse, upstream):
    return inverse * (
        upstream
        - jnp.mean(upstream, -1, keepdims=True)
        - normal * jnp.mean(upstream * normal, -1, keepdims=True)
    )


def adam_update(weight, moment_one, moment_two, gradient, step_rate, decay_rate):
    first_new = BETA_ONE * moment_one + (1.0 - BETA_ONE) * gradient
    second_new = BETA_TWO * moment_two + (1.0 - BETA_TWO) * gradient * gradient
    first_hat = first_new / (1.0 - BETA_ONE**STEP)
    second_hat = second_new / (1.0 - BETA_TWO**STEP)
    weight_new = weight - step_rate * (
        first_hat / (jnp.sqrt(second_hat) + ADAM_EPSILON) + decay_rate * weight
    )
    return (first_new, second_new, weight_new)


def segments_of(lengths_row, length):
    ends = jnp.cumsum(lengths_row, dtype=jnp.int32)
    places = jnp.arange(length, dtype=jnp.int32)
    segment = jnp.sum((ends[None, :] <= places[:, None]).astype(jnp.int32), axis=1, dtype=jnp.int32)
    live = (places < ends[-1]).astype(jnp.float32)
    return segment, live


def matmul(left, right, dims):
    return lax.dot_general(left, right, (dims, ((), ())), preferred_element_type=jnp.float32)


NN = ((1,), (0,))
NT = ((1,), (1,))
TN = ((0,), (0,))


def attention_forward(stream, weight, mask):
    length, width = stream.shape
    size = width // HEADS
    packed = matmul(stream, weight[:, : 3 * width], NN).astype(jnp.bfloat16)
    heads = packed.reshape(length, 3, HEADS, size)
    scores = jnp.einsum("qhd,khd->hqk", heads[:, 0], heads[:, 1], preferred_element_type=jnp.float32)
    scores = jnp.where(mask[None], scores * size**-0.5, NEGATIVE)
    weights = jnp.exp(scores - jnp.max(scores, -1, keepdims=True))
    probs = weights / jnp.sum(weights, -1, keepdims=True)
    mixed = jnp.einsum("hqk,khd->qhd", probs.astype(jnp.bfloat16), heads[:, 2], preferred_element_type=jnp.float32)
    mixed = mixed.reshape(length, width).astype(jnp.bfloat16)
    branch = matmul(mixed, weight[:, 3 * width :], NN)
    return branch, (heads, probs, mixed)


def attention_backward(stream, weight, kept, grad_low):
    heads, probs, mixed = kept
    length, width = stream.shape
    size = width // HEADS
    grad_out = matmul(mixed, grad_low, TN)
    grad_mixed = matmul(grad_low, weight[:, 3 * width :], NT).astype(jnp.bfloat16)
    grad_mixed = grad_mixed.reshape(length, HEADS, size)
    grad_probs = jnp.einsum("qhd,khd->hqk", grad_mixed, heads[:, 2], preferred_element_type=jnp.float32)
    centre = jnp.sum(probs * grad_probs, -1, keepdims=True)
    grad_scores = (probs * (grad_probs - centre)).astype(jnp.bfloat16)
    low = probs.astype(jnp.bfloat16)
    scale = size**-0.5
    grad_q = jnp.einsum("hqk,khd->qhd", grad_scores, heads[:, 1], preferred_element_type=jnp.float32) * scale
    grad_k = jnp.einsum("hqk,qhd->khd", grad_scores, heads[:, 0], preferred_element_type=jnp.float32) * scale
    grad_v = jnp.einsum("hqk,qhd->khd", low, grad_mixed, preferred_element_type=jnp.float32)
    packed = jnp.concatenate([grad_q, grad_k, grad_v], axis=1).reshape(length, 3 * width)
    packed = packed.astype(jnp.bfloat16)
    grad_in = matmul(stream, packed, TN)
    grad_inputs = matmul(packed, weight[:, : 3 * width], NT)
    return grad_inputs, jnp.concatenate([grad_in, grad_out], axis=1)


def feed_forward(stream, weight, down):
    pre = matmul(stream, weight, NN)
    active = jax.nn.gelu(pre, approximate=True).astype(jnp.bfloat16)
    return matmul(active, down, NN), (pre, active)


def feed_backward(stream, weight, down, kept, grad_low):
    pre, active = kept
    grad_down = matmul(active, grad_low, TN)
    grad_active = matmul(grad_low, down, NT)
    pull = jax.vjp(lambda value: jax.nn.gelu(value, approximate=True), pre)[1]
    grad_pre = pull(grad_active)[0].astype(jnp.bfloat16)
    grad_up = matmul(stream, grad_pre, TN)
    return matmul(grad_pre, weight, NT), grad_up, grad_down


def micro_step(rows, pull, segment, mats, downs, gains, biases):
    low = jnp.bfloat16
    mask = segment[:, None] == segment[None, :]
    stream, dual = rows, jnp.zeros_like(rows)
    saved = []
    for sub in range(4):
        if sub % 2 == 0:
            branch, kept = attention_forward(stream, mats[sub], mask)
        else:
            branch, kept = feed_forward(stream, mats[sub], downs[sub // 2])
        normal, inverse = norm_stats(stream.astype(jnp.float32) + branch)
        out = normal * gains[sub] + biases[sub]
        total = dual.astype(jnp.float32) + branch
        saved.append((stream, kept, normal, inverse))
        if sub < 3:
            stream, dual = out.astype(low), total.astype(low)
    dual_normal, dual_inverse = norm_stats(total)
    output = (out + dual_normal).astype(low)
    grad_out, grad_dual = pull, norm_back(dual_normal, dual_inverse, pull)
    grads_a, grads_b, grads_n = [None] * 4, [None] * 2, [None] * 4
    for sub in (3, 2, 1, 0):
        stream, kept, normal, inverse = saved[sub]
        grads_n[sub] = jnp.stack([jnp.sum(grad_out * normal, 0), jnp.sum(grad_out, 0)], axis=1)
        summed = norm_back(normal, inverse, grad_out * gains[sub])
        branch_low = (summed + grad_dual).astype(low)
        if sub % 2 == 0:
            inner, grads_a[sub] = attention_backward(stream, mats[sub], kept, branch_low)
        else:
            inner, grads_a[sub], grads_b[sub // 2] = feed_backward(
                stream, mats[sub], downs[sub // 2], kept, branch_low
            )
        grad_in = summed + inner
        if sub > 0:
            grad_out = grad_in.astype(low).astype(jnp.float32)
            grad_dual = grad_dual.astype(low).astype(jnp.float32)
    return output, grad_in, jnp.stack(grads_a), jnp.stack(grads_b), jnp.stack(grads_n)


def finish_step(grad_norm, output, input_grad, *groups):
    factor = CLIP_NORM / jnp.maximum(grad_norm, CLIP_NORM)
    results = [grad_norm, output[None], input_grad[None]]
    for weight, one, two, grad, rate, decay in groups:
        clip = grad * factor
        moment, square_new, master = adam_update(weight, one, two, clip, rate, decay)
        results += [clip, moment, square_new, master, master.astype(jnp.bfloat16)]
    return tuple(results)


def body(
    tokens, cotangent, lengths, mat_a, mat_b, norms, first_a, second_a, first_b, second_b, first_n, second_n
):
    low = jnp.bfloat16
    own = lax.axis_index("section")
    length = tokens.shape[0] // lengths.shape[0]
    rows = lax.dynamic_slice_in_dim(tokens, own * length, length, 0)
    segment, live = segments_of(lax.dynamic_index_in_dim(lengths, own, 0, keepdims=False), length)
    pull = lax.dynamic_slice_in_dim(cotangent, own * length, length, 0).astype(jnp.float32) * live[:, None]

    def gathered(value):
        return lax.all_gather(lax.all_gather(value, "dp", axis=1, tiled=True), "section", axis=0, tiled=True)

    mats = gathered(mat_a.astype(low))
    scales = gathered(norms.astype(low)).astype(jnp.float32)
    downs = lax.all_gather(mat_b.astype(low), "section", axis=2, tiled=True)
    downs = lax.all_gather(downs, "dp", axis=1, tiled=True)
    output, input_grad, part_a, part_b, part_n = micro_step(
        rows, pull, segment, mats, downs, scales[:, :, 0], scales[:, :, 1]
    )

    def scattered(value, section_dim):
        value = lax.psum_scatter(value, "section", scatter_dimension=section_dim, tiled=True)
        return lax.psum_scatter(value, "dp", scatter_dimension=1, tiled=True).astype(jnp.float32)

    grad_a = scattered(part_a.astype(low), 0)
    grad_b = scattered(part_b.astype(low), 2)
    grad_n = scattered(part_n, 0)
    square = jnp.sum(grad_a * grad_a) + jnp.sum(grad_b * grad_b) + jnp.sum(grad_n * grad_n)
    grad_norm = jnp.sqrt(lax.psum(square, ("section", "dp")))
    return finish_step(
        grad_norm, output, input_grad,
        (mat_a, first_a, second_a, grad_a, MATRIX_RATE, MATRIX_DECAY),
        (mat_b, first_b, second_b, grad_b, MATRIX_RATE, MATRIX_DECAY),
        (norms, first_n, second_n, grad_n, NORM_RATE, 0.0),
    )


LOW = jnp.bfloat16
WIDE = jnp.float32
MESH = pl.DeviceIdType.MESH
SECTIONS = 4
LANES = 128
BLOCK = 64
ROWS_FIRST = (5,)
KERNEL_VMEM = 64 * 1024 * 1024 - 256 * 1024


def gradient_items(rows_a, rows_b, cols_b, width, hidden):
    part = rows_a // SECTIONS
    return (
        ("B1", 3, cols_b // 2, rows_b),
        ("F3", 3, part, hidden // 2),
        ("O2", 2, part, width // 2),
        ("K2", 2, part, 3 * width // 2),
        ("B0", 1, cols_b // 2, rows_b),
        ("F1", 1, part, hidden // 2),
        ("O0", 0, part, width // 2),
        ("K0", 0, part, 3 * width // 2),
    )


def item_scratch(name, chips, rows, columns):
    piece = (rows, columns)
    return (
        ("own" + name, (chips, SECTIONS, 2) + piece, LOW),
        ("farx" + name, (chips,) + piece, LOW),
        ("fary" + name, (chips,) + piece, LOW),
        ("nearx" + name, (2, chips) + piece, LOW),
        ("neary" + name, (2, chips) + piece, LOW),
        ("line" + name, (chips, 2) + piece, LOW),
        ("done" + name, (2,) + piece if name[0] == "B" else (SECTIONS, 2) + piece, WIDE if name[0] == "B" else LOW),
    )


def kernel_scratch(chips, rows_a, rows_b, cols_b, length, width, hidden):
    devices = 2 * chips
    items = gradient_items(rows_a, rows_b, cols_b, width, hidden)
    count = len(items)
    received = sum((item_scratch(name, chips, rows, columns) for name, _, rows, columns in items), ())
    return received + (
        ("fac_s", (32,), None),
        ("fac_r", (32,), None),
        ("px_s", (count, 3), None),
        ("px_r", (count, 3), None),
        ("py_s", (count, 3), None),
        ("py_r", (count, 3), None),
        ("line_s", (count, chips), None),
        ("line_r", (count, chips), None),
        ("done_s", (count,), None),
        ("done_r", (count, SECTIONS), None),
        ("wa", (4, chips, 2, SECTIONS, rows_a // SECTIONS, hidden), LOW),
        ("wb", (2, chips, 2, SECTIONS, rows_b, cols_b), LOW),
        ("cut", (SECTIONS, rows_a // SECTIONS, hidden), LOW),
        ("tiles", (devices, SECTIONS, 8, LANES), WIDE),
        ("x", (4, length, width), LOW),
        ("xt", (4, chips, 2, rows_a, length), LOW),
        ("xtc", (4, chips, rows_a, 2 * length), LOW),
        ("y", (length, width), LOW),
        ("cot", (length, width), LOW),
        ("bias", (length, length), WIDE),
        ("live", (length, 1), WIDE),
        ("f", (length, width), WIDE),
        ("n", (4, length, width), WIDE),
        ("inv", (4, length, 1), WIDE),
        ("q", (2, length, width), LOW),
        ("k", (2, length, width), LOW),
        ("v", (2, length, width), LOW),
        ("kt", (2, width, length), LOW),
        ("vt", (2, width, length), LOW),
        ("ot", (2, chips, 2, rows_a, length), LOW),
        ("otc", (2, chips, rows_a, 2 * length), LOW),
        ("pt", (2, HEADS, length, length), LOW),
        ("g", (2, length, hidden), LOW),
        ("gc", (2, chips, 2 * length, rows_b), LOW),
        ("slope", (2, length, hidden), LOW),
        ("gx", (length, width), WIDE),
        ("gy", (length, width), WIDE),
        ("df", (2, 2 * length, width), LOW),
        ("dft", (2, width, 2 * length), LOW),
        ("dm", (length, width), LOW),
        ("dqt", (width, length), LOW),
        ("dh", (2, 2 * length, hidden), LOW),
        ("dp", (2, 2 * length, 3 * width), LOW),
        ("ng", (devices, 8, width), WIDE),
        ("ns", (SECTIONS, 8, width), WIDE),
        ("sq", (devices, 8, LANES), WIDE),
        ("sqs", (SECTIONS, 8, LANES), WIDE),
        ("sum", (8, LANES), WIDE),
        ("in_s", (2,), None),
        ("cut_s", (1,), None),
        ("cut_r", (SECTIONS,), None),
        ("gz_s", (6,), None),
        ("gz_r", (6, chips), None),
        ("gx_s", (6,), None),
        ("gx_r", (6,), None),
        ("gy_s", (6,), None),
        ("gy_r", (6,), None),
        ("rx_s", (6,), None),
        ("rx_r", (6,), None),
        ("ry_s", (6,), None),
        ("ry_r", (6,), None),
        ("gs_s", (6,), None),
        ("gs_r", (6,), None),
        ("small_s", (3, 2), None),
        ("small_r", (3, 2), None),
    )


INPUTS = ("tokens", "cotangent", "lengths", "mat_a", "mat_b", "norms")
OUTPUTS = ("grad_a", "grad_b", "grad_n", "square", "output", "input_grad")


def step_kernel(names, *refs):
    r = types.SimpleNamespace(**dict(zip(names, refs)))
    length, width = r.x.shape[1:]
    hidden = r.wa.shape[-1]
    rows_a, (rows_b, cols_b) = r.mat_a.shape[1], r.mat_b.shape[1:]
    devices = r.tiles.shape[0]
    chips = devices // 2
    half_b = cols_b // 2
    grad_items = gradient_items(rows_a, rows_b, cols_b, width, hidden)
    head = width // HEADS
    scale = head**-0.5

    s, d = lax.axis_index("section"), lax.axis_index("dp")
    z, c = lax.div(d, 2), lax.rem(d, 2)
    sx = s + 1 - 2 * lax.rem(s, 2)
    sy = lax.rem(s + 2, SECTIONS)
    sd = SECTIONS - 1 - s
    to_sibling = {"dp": d + 1 - 2 * c}
    to_up, to_down = {"dp": d + 2}, {"dp": d - 2}
    to_x, to_y = {"section": sx}, {"section": sy}
    below, above = z > 0, z < chips - 1
    group = [{"dp": lax.rem(d + step, devices)} for step in range(1, devices)]
    plane = [{"section": lax.rem(s + step, SECTIONS)} for step in range(1, SECTIONS)]
    finish = []

    def when(condition, work):
        if condition is None:
            work()
        else:
            pl.when(condition)(work)

    def push(source, target, send_sem, recv_sem, device):
        pltpu.make_async_remote_copy(
            src_ref=source,
            dst_ref=target,
            send_sem=send_sem,
            recv_sem=recv_sem,
            device_id=device,
            device_id_type=MESH,
        ).start()

    def arrived(target, sem):
        pltpu.make_async_remote_copy(
            src_ref=target, dst_ref=target, send_sem=sem, recv_sem=sem, device_id=to_x, device_id_type=MESH
        ).wait_recv()

    def sent(source, sem):
        pltpu.make_async_remote_copy(
            src_ref=source, dst_ref=source, send_sem=sem, recv_sem=sem, device_id=to_x, device_id_type=MESH
        ).wait_send()

    def at_end(condition, source, sem):
        finish.append((condition, source, sem))

    def aligned(start, size):
        return pl.ds(pl.multiple_of(start, size), size)

    own_x = pltpu.make_async_copy(r.tokens.at[aligned(s * length, length)], r.x.at[0], r.in_s.at[0])
    own_cot = pltpu.make_async_copy(r.cotangent.at[aligned(s * length, length)], r.cot, r.in_s.at[1])
    own_x.start()
    own_cot.start()
    barrier = pltpu.get_barrier_semaphore()
    for peer in group + plane:
        pl.semaphore_signal(barrier, inc=1, device_id=peer, device_id_type=MESH)
    r.cut[...] = r.mat_a[0].astype(LOW).reshape(SECTIONS, rows_a // SECTIONS, hidden)
    r.wa[s, z, c, s] = r.cut[s]
    for layer in range(2):
        r.wb[layer, z, c, s] = r.mat_b[layer].astype(LOW)
    norms = r.norms[0].astype(LOW).astype(WIDE)
    nothing = jnp.zeros((2, rows_a), WIDE)
    even = jnp.concatenate([norms, nothing], axis=1)
    odd = jnp.concatenate([nothing, norms], axis=1)
    r.tiles[d, s, 0:2, :] = jnp.where(c == 0, even, odd)
    r.tiles[d, s, 2:8, :] = jnp.zeros((6, LANES), WIDE)
    pl.semaphore_wait(barrier, len(group) + len(plane))

    def small_out(which, source):
        for peer in group:
            push(source, source, r.small_s.at[which, 0], r.small_r.at[which, 0], peer)

    def small_group(which, like):
        arrived(like, r.small_r.at[which, 0])
        sent(like, r.small_s.at[which, 0])

    def small_plane_out(which, source):
        for peer in plane:
            push(source, source, r.small_s.at[which, 1], r.small_r.at[which, 1], peer)

    def small_plane(which, like):
        arrived(like, r.small_r.at[which, 1])
        sent(like, r.small_s.at[which, 1])

    every = slice(None)

    def block(item, chip, section):
        if item < 4:
            return r.wa.at[item, chip, c, section]
        return r.wb.at[item - 4, chip, c, section]

    def half_block(item, section, half):
        if item < 4:
            return r.wa.at[item, :, c, section, :, pl.ds(half * hidden // 2, hidden // 2)]
        rows = pl.ds(half * rows_b // 2, rows_b // 2)
        return r.wb.at[item - 4, :, c, section, rows]

    def half_piece(item, section, half):
        rows = pl.ds(half * rows_b // 2, rows_b // 2)
        return r.wb.at[item - 4, z, c, section, rows]

    def core_blocks(item, core):
        return r.wa.at[item, :, core] if item < 4 else r.wb.at[item - 4, :, core]

    def cut_out():
        for section, device in ((sd, {"section": sd}), (sx, to_x), (sy, to_y)):
            push(r.cut.at[section], r.wa.at[s, z, c, section], r.cut_s.at[0], r.cut_r.at[s], device)
        at_end(None, r.cut.at[pl.ds(0, SECTIONS - 1)], r.cut_s.at[0])

    def cut_in():
        for section in (sx, sy, sd):
            arrived(r.wa.at[section, z, c, s], r.cut_r.at[section])

    def line_out(item):
        if item in ROWS_FIRST:
            rows_out(item)
            return
        own = block(item, z, s)
        for step in range(1, chips):
            push(own, own, r.gz_s.at[item], r.gz_r.at[item, z], {"dp": 2 * lax.rem(z + step, chips) + c})
        several = block(item, pl.ds(0, chips - 1), s)
        at_end(None, several, r.gz_s.at[item])

    def plane_out(item, chip):
        own = block(item, chip, s)
        push(own, own, r.gx_s.at[item], r.gx_r.at[item], to_x)
        push(own, own, r.gy_s.at[item], r.gy_r.at[item], to_y)

    def rows_out(item):
        arrived(half_piece(item, sd, 0), r.rx_r.at[item])
        arrived(half_piece(item, sd, 1), r.ry_r.at[item])
        rows = r.wb.at[item - 4, z, c]
        for step in range(1, chips):
            push(rows, rows, r.gz_s.at[item], r.gz_r.at[item, z], {"dp": 2 * lax.rem(z + step, chips) + c})
        push(rows, rows, r.gs_s.at[item], r.gs_r.at[item], to_sibling)
        at_end(None, r.wb.at[item - 4, pl.ds(0, chips - 1), c], r.gz_s.at[item])

    def rows_in(item):
        for step in range(1, chips):
            chip = lax.rem(z + step, chips)
            rows = r.wb.at[item - 4, chip, c]
            arrived(rows, r.gz_r.at[item, chip])
            push(rows, rows, r.gs_s.at[item], r.gs_r.at[item], to_sibling)
        at_end(None, core_blocks(item, c), r.gs_s.at[item])

    def line_in(item):
        if item in ROWS_FIRST:
            rows_in(item)
            return
        for step in range(1, chips):
            chip = lax.rem(z + step, chips)
            arrived(block(item, chip, s), r.gz_r.at[item, chip])
            plane_out(item, chip)
        core_out(item, s)
        at_end(None, block(item, every, s), r.gx_s.at[item])
        at_end(None, block(item, every, s), r.gy_s.at[item])

    def core_out(item, section):
        blocks = block(item, every, section)
        push(blocks, blocks, r.gs_s.at[item], r.gs_r.at[item], to_sibling)

    def plane_in(item):
        over = z if item in ROWS_FIRST else every
        piece = half_piece if item in ROWS_FIRST else half_block
        arrived(block(item, over, sx), r.gx_r.at[item])
        part = piece(item, sx, 1)
        push(part, part, r.ry_s.at[item], r.ry_r.at[item], to_y)
        arrived(block(item, over, sy), r.gy_r.at[item])
        part = piece(item, sy, 0)
        push(part, part, r.rx_s.at[item], r.rx_r.at[item], to_x)
        if item in ROWS_FIRST:
            at_end(None, block(item, z, sx), r.gx_s.at[item])
            at_end(None, block(item, z, sx), r.gy_s.at[item])
        else:
            core_out(item, sx)
            core_out(item, sy)
        at_end(None, part, r.ry_s.at[item])
        at_end(None, part, r.rx_s.at[item])

    def far_in(item):
        arrived(half_block(item, sd, 0), r.rx_r.at[item])
        arrived(half_block(item, sd, 1), r.ry_r.at[item])
        core_out(item, sd)
        at_end(None, core_blocks(item, c), r.gs_s.at[item])

    def core_in(item):
        arrived(core_blocks(item, 1 - c), r.gs_r.at[item])

    mine, other = pl.ds(0, length), pl.ds(length, length)

    def give(slot, source, target):
        push(source, target, r.fac_s.at[slot], r.fac_r.at[slot], to_sibling)
        at_end(None, target, r.fac_s.at[slot])

    def taken(slot, target):
        arrived(target, r.fac_r.at[slot])

    def give_rows(layer):
        r.xt[layer] = r.x[layer].T.reshape(chips, 2, rows_a, length)
        r.xtc[layer, :, :, 0:length] = r.xt[layer, :, c]
        give(layer, r.xt.at[layer, :, 1 - c], r.xtc.at[layer, :, :, other])

    def product(left, right, dims):
        return lax.dot_general(left, right, (dims, ((), ())), preferred_element_type=WIDE)

    def loop(count, work):
        def one(index, carry):
            work(index)
            return carry

        lax.fori_loop(0, count, one, 0)

    def gain_row(layer, kind):
        parts = [
            r.tiles[2 * chip, layer, kind : kind + 1, :] + r.tiles[2 * chip + 1, layer, kind : kind + 1, :]
            for chip in range(chips)
        ]
        return jnp.concatenate(parts, axis=1)

    def stats(value):
        centre = value - jnp.mean(value, -1, keepdims=True)
        inverse = lax.rsqrt(jnp.mean(centre * centre, -1, keepdims=True) + EPSILON)
        return centre * inverse, inverse

    lane = lax.broadcasted_iota(jnp.int32, (1, 2 * head), 1)
    first_half = (lane < head).astype(WIDE)
    half_masks = (first_half.astype(LOW), (1.0 - first_half).astype(LOW))

    def prepare_masks():
        ends, total = [], jnp.int32(0)
        for slot in range(r.lengths.shape[1]):
            total = total + r.lengths[s, slot]
            ends.append(total)
        down_places = lax.broadcasted_iota(jnp.int32, (length, 1), 0)
        across_places = lax.broadcasted_iota(jnp.int32, (1, length), 1)
        down_segment = jnp.zeros((length, 1), jnp.int32)
        across_segment = jnp.zeros((1, length), jnp.int32)
        for end in ends:
            down_segment = down_segment + (end <= down_places).astype(jnp.int32)
            across_segment = across_segment + (end <= across_places).astype(jnp.int32)
        r.bias[...] = jnp.where(down_segment == across_segment, 0.0, NEGATIVE)
        r.live[...] = (down_places < total).astype(WIDE)

    def matrix(layer, place):
        value = r.wa[layer, :, :, :, :, place]
        return value.reshape(width, value.shape[-1])

    def down(at, chip=slice(None)):
        blocks = [r.wb[at, chip, :, section] for section in range(SECTIONS)]
        return jnp.concatenate([block.reshape(-1, cols_b) for block in blocks], axis=1)

    def attention_in(layer):
        at = layer // 2
        rows = r.x[layer]
        r.q[at] = product(rows, matrix(layer, pl.ds(0, width)), NN).astype(LOW) * jnp.asarray(scale, LOW)
        keys = product(rows, matrix(layer, pl.ds(width, width)), NN).astype(LOW)
        r.k[at] = keys
        values = product(rows, matrix(layer, pl.ds(2 * width, width)), NN).astype(LOW)
        r.v[at] = values
        r.vt[at] = values.T

    def attention_heads(layer, begin, count):
        at = layer // 2

        def pair(index):
            lanes = aligned(index * 2 * head, 2 * head)
            for which in range(2):
                scores = product(r.k[at, :, lanes], r.q[at, :, lanes] * half_masks[which], NT) + r.bias[...]
                weights = jnp.exp(scores - jnp.max(scores, 0, keepdims=True))
                probs = (weights * (1.0 / jnp.sum(weights, 0, keepdims=True))).astype(LOW)
                r.pt[at, 2 * index + which] = probs
                place = aligned((2 * index + which) * head, head)
                r.ot[at, index, which] = product(r.vt[at, place, :], probs, NN).astype(LOW)

        for index in range(begin, begin + count):
            pair(index)

    def attention_out(layer):
        at = layer // 2
        r.otc[at, :, :, 0:length] = r.ot[at, :, c]
        give(4 + at, r.ot.at[at, :, 1 - c], r.otc.at[at, :, :, other])
        r.f[...] = product(r.ot[at].reshape(width, length).T, matrix(layer, pl.ds(3 * width, width)), NN)

    def expand(layer, index):
        at = layer // 2
        place = pl.ds(index * width, width)
        pre = product(r.x[layer], matrix(layer, place), NN)
        squared = pre * pre
        slope = 0.7978845608 * (1.0 + 3 * 0.044715 * squared)
        bent = jnp.tanh(0.7978845608 * pre * (1.0 + 0.044715 * squared))
        r.g[at, :, place] = (0.5 * pre * (1.0 + bent)).astype(LOW)
        r.slope[at, :, place] = (0.5 * (1.0 + bent) + 0.5 * pre * (1.0 - bent * bent) * slope).astype(LOW)
        block = aligned((2 * index + c) * rows_b, rows_b)
        r.gc[at, index, 0:length, :] = r.g[at, :, block]
        block = aligned((2 * index + 1 - c) * rows_b, rows_b)
        give(6 + chips * at + index, r.g.at[at, :, block], r.gc.at[at, index, other, :])

    def contract(layer):
        r.f[...] = product(r.g[layer // 2], down(layer // 2), NN)

    def by_rows(work):
        for index in range(length // BLOCK):
            work(pl.ds(index * BLOCK, BLOCK))

    def normalize(layer):
        gain, offset = gain_row(layer, 0), gain_row(layer, 1)

        def some(rows):
            branch = r.f[rows, :]
            normal, inverse = stats(r.x[layer, rows, :].astype(WIDE) + branch)
            r.n[layer, rows, :] = normal
            r.inv[layer, rows, :] = inverse
            out = normal * gain + offset
            dual = branch if layer == 0 else r.y[rows, :].astype(WIDE) + branch
            if layer < 3:
                r.x[layer + 1, rows, :] = out.astype(LOW)
                r.y[rows, :] = dual.astype(LOW)
            else:
                dual_normal, dual_inverse = stats(dual)
                r.output[rows, :] = (out + dual_normal).astype(LOW)
                pull = r.cot[rows, :].astype(WIDE) * r.live[rows, :]
                r.gx[rows, :] = pull
                r.gy[rows, :] = norm_back(dual_normal, dual_inverse, pull)

        by_rows(some)

    def back_normalize(layer):
        gain = gain_row(layer, 0)

        def some(index, sums):
            rows = pl.ds(index * BLOCK, BLOCK)
            upstream = r.gx[rows, :]
            normal = r.n[layer, rows, :]
            summed = norm_back(normal, r.inv[layer, rows, :], upstream * gain)
            dual = r.gy[rows, :]
            r.gx[rows, :] = summed
            r.df[layer // 2, rows, :] = (summed + dual).astype(LOW)
            if layer == 3:
                r.gy[rows, :] = dual.astype(LOW).astype(WIDE)
            return (
                sums[0] + jnp.sum(upstream * normal, 0, keepdims=True),
                sums[1] + jnp.sum(upstream, 0, keepdims=True),
            )

        zero = jnp.zeros((1, width), WIDE)
        gains, offsets = zero, zero
        for index in range(length // BLOCK):
            gains, offsets = some(index, (gains, offsets))
        r.ng[d, 2 * layer : 2 * layer + 1, :] = gains
        r.ng[d, 2 * layer + 1 : 2 * layer + 2, :] = offsets

    def pass_down(layer, inner):
        total = r.gx[...] + inner
        if layer > 0:
            r.gx[...] = total.astype(LOW).astype(WIDE)
        else:
            r.input_grad[...] = total

    base = 6 + 2 * chips

    def back_hidden(layer):
        at = layer // 2
        r.dft[at, :, 0:length] = r.df[at, 0:length, :].T
        give(base + at, r.dft.at[at, :, mine], r.dft.at[at, :, other])
        for index in range(hidden // width):
            place = pl.ds(index * width, width)
            pulled = product(r.df[at, 0:length, :], down(at, pl.ds(index, 1)), NT)
            r.dh[at, 0:length, place] = (pulled * r.slope[at, :, place].astype(WIDE)).astype(LOW)
            give(base + 2 + chips * at + index, r.dh.at[at, mine, place], r.dh.at[at, other, place])

    def back_expand_end(layer):
        pass_down(layer, product(r.dh[layer // 2, 0:length, :], matrix(layer, pl.ds(0, hidden)), NT))

    def back_output(layer):
        at = layer // 2
        give(base + 2 + 2 * chips + at, r.df.at[at, mine], r.df.at[at, other])
        r.dm[...] = product(r.df[at, 0:length, :], matrix(layer, pl.ds(3 * width, width)), NT).astype(LOW)
        r.kt[at] = (r.k[at] * jnp.asarray(scale, LOW)).T

    def back_heads(layer, begin, count):
        at = layer // 2

        def pair(index):
            lanes = aligned(index * 2 * head, 2 * head)
            pulled = r.dm[:, lanes]
            keys, values = [], []
            for which in range(2):
                probs = r.pt[at, 2 * index + which]
                grad = product(r.v[at, :, lanes], pulled * half_masks[which], NT)
                full = probs.astype(WIDE)
                centre = jnp.sum(full * grad, 0, keepdims=True)
                scores = (full * (grad - centre)).astype(LOW)
                keys.append(product(scores, r.q[at, :, lanes], NN))
                values.append(product(probs, pulled, NN))
                place = aligned((2 * index + which) * head, head)
                r.dqt[place, :] = product(r.kt[at, place, :], scores, NN).astype(LOW)
            r.dp[at, 0:length, aligned(width + index * 2 * head, 2 * head)] = jnp.where(
                lane < head, keys[0], keys[1]
            ).astype(LOW)
            r.dp[at, 0:length, aligned(2 * width + index * 2 * head, 2 * head)] = jnp.where(
                lane < head, values[0], values[1]
            ).astype(LOW)

        def pairs(step):
            pair(begin + 2 * step)
            pair(begin + 2 * step + 1)

        loop(count // 2, pairs)

    def back_packed(layer):
        at = layer // 2
        slot = base + 4 + 2 * chips + 2 * at
        place = pl.ds(width, 2 * width)
        give(slot, r.dp.at[at, mine, place], r.dp.at[at, other, place])
        r.dp[at, 0:length, 0:width] = r.dqt[...].T
        place = pl.ds(0, width)
        give(slot + 1, r.dp.at[at, mine, place], r.dp.at[at, other, place])

    def back_packed_end(layer):
        pass_down(layer, product(r.dp[layer // 2, 0:length, :], matrix(layer, pl.ds(0, 3 * width)), NT))

    def keep(name, half, place, value):
        own = getattr(r, "own" + name)
        own[:, :, half, :, place] = value.astype(LOW).reshape(chips, SECTIONS, rows_a // SECTIONS, value.shape[1])

    def chip_rows(value):
        return value.reshape(chips * rows_a, 2 * length)

    def grad_down(at):
        own = getattr(r, "ownB%d" % at)
        taken(base + at, r.dft.at[at, :, other])
        for chip in range(chips):
            taken(6 + chips * at + chip, r.gc.at[at, chip, other, :])
            value = product(r.dft[at], r.gc[at, chip], NN)
            own[chip] = value.astype(LOW).reshape(SECTIONS, 2, half_b, rows_b)

    def grad_up(layer):
        at = layer // 2
        taken(layer, r.xtc.at[layer, :, :, other])
        for index in range(hidden // width):
            place = pl.ds(index * width, width)
            taken(base + 2 + chips * at + index, r.dh.at[at, other, place])
            value = product(chip_rows(r.xtc[layer]), r.dh[at, :, place], NN)
            keep("F%d" % layer, index // 2, pl.ds(index % 2 * width, width), value)

    def grad_output(layer):
        at = layer // 2
        taken(4 + at, r.otc.at[at, :, :, other])
        taken(base + 2 + 2 * chips + at, r.df.at[at, other])
        for half in range(2):
            place = pl.ds(half * width // 2, width // 2)
            value = product(chip_rows(r.otc[at]), r.df[at, :, place], NN)
            keep("O%d" % layer, half, pl.ds(0, width // 2), value)

    def grad_packed(layer):
        at = layer // 2
        slot = base + 4 + 2 * chips + 2 * at
        taken(layer, r.xtc.at[layer, :, :, other])
        taken(slot, r.dp.at[at, other, pl.ds(width, 2 * width)])
        taken(slot + 1, r.dp.at[at, other, pl.ds(0, width)])
        part = 3 * width // 2
        for half in range(2):
            value = product(chip_rows(r.xtc[layer]), r.dp[at, :, half * part : (half + 1) * part], NN)
            keep("K%d" % layer, half, pl.ds(0, part), value)

    def joined(target, others):
        return functools.reduce(
            lambda left, right: left + right, [ref[...].astype(WIDE) for ref in (target, *others)]
        )

    def add_into(target, others):
        if len(others) == 1:
            target[...] = target[...] + others[0][...]
        else:
            target[...] = joined(target, others).astype(LOW)

    places = {name: place for place, (name, _, _, _) in enumerate(grad_items)}

    def buffers(name):
        parts = ("own", "farx", "fary", "nearx", "neary", "line", "done")
        return types.SimpleNamespace(**{part: getattr(r, part + name) for part in parts})

    def to_plane(name):
        item, place = buffers(name), places[name]

        def over_x(section, half, target, slot):
            push(item.own.at[:, section, half], target, r.px_s.at[place, slot], r.px_r.at[place, slot], to_x)
            at_end(None, item.farx, r.px_s.at[place, slot])

        def over_y(section, half, target, slot):
            push(item.own.at[:, section, half], target, r.py_s.at[place, slot], r.py_r.at[place, slot], to_y)
            at_end(None, item.farx, r.py_s.at[place, slot])

        over_x(sd, 0, item.farx, 2)
        over_y(sd, 1, item.fary, 2)
        over_x(sx, 0, item.nearx.at[0], 0)
        over_y(sy, 1, item.neary.at[1], 1)

    def through_plane(name):
        item, place = buffers(name), places[name]
        own = item.own
        arrived(item.fary, r.py_r.at[place, 2])
        add_into(own.at[:, sx, 1], [item.fary])
        push(own.at[:, sx, 1], item.nearx.at[1], r.px_s.at[place, 1], r.px_r.at[place, 1], to_x)
        at_end(None, item.farx, r.px_s.at[place, 1])
        arrived(item.farx, r.px_r.at[place, 2])
        add_into(own.at[:, sy, 0], [item.farx])
        push(own.at[:, sy, 0], item.neary.at[0], r.py_s.at[place, 0], r.py_r.at[place, 0], to_y)
        at_end(None, item.farx, r.py_s.at[place, 0])

    def to_line(name):
        item, place = buffers(name), places[name]
        own = item.own.at[:, s]
        for half in range(2):
            arrived(item.nearx.at[half], r.px_r.at[place, half])
            arrived(item.neary.at[half], r.py_r.at[place, half])
            add_into(own.at[:, half], [item.nearx.at[half], item.neary.at[half]])
        for step in range(1, chips):
            chip = lax.rem(z + step, chips)
            push(
                own.at[chip],
                item.line.at[z],
                r.line_s.at[place, step],
                r.line_r.at[place, z],
                {"dp": 2 * chip + c},
            )
            at_end(None, item.line.at[0], r.line_s.at[place, step])

    def to_owner(name):
        item, place = buffers(name), places[name]
        others = [lax.rem(z + step, chips) for step in range(1, chips)]
        for chip in others:
            arrived(item.line.at[chip], r.line_r.at[place, chip])
        total = joined(item.own.at[z, s], [item.line.at[chip] for chip in others])
        square = total * total
        while square.ndim > 2:
            square = jnp.sum(square, 0)
        square = jnp.sum(jnp.sum(square, 0, keepdims=True), 1, keepdims=True)
        r.sum[...] = r.sum[...] + jnp.broadcast_to(square, (8, LANES))
        if name[0] == "B":
            item.done[...] = total
            return
        item.done[s] = total.astype(LOW)
        layer = grad_items[place][1]
        mine = item.done.at[s]
        away = s != layer
        when(
            away,
            lambda: push(mine, mine, r.done_s.at[place], r.done_r.at[place, s], {"section": jnp.int32(layer)}),
        )
        at_end(away, mine, r.done_s.at[place])

    def collect(name):
        item, place = buffers(name), places[name]
        layer = grad_items[place][1]

        def work():
            for section in range(SECTIONS):
                if section != layer:
                    arrived(item.done.at[section], r.done_r.at[place, section])
            columns = item.done.shape[-1]
            start = 3 * width if name[0] == "O" else 0
            for section in range(SECTIONS):
                for half in range(2):
                    rows = pl.ds(section * (rows_a // SECTIONS), rows_a // SECTIONS)
                    place_to = pl.ds(start + half * columns, columns)
                    r.grad_a[rows, place_to] = item.done[section, half].astype(WIDE)

        when(s == layer, work)

    def all_sent(count=None):
        for condition, source, sem in finish[:count]:
            when(condition, functools.partial(sent, source, sem))
        del finish[:count]

    cut_out()
    small_out(0, r.tiles.at[d, s])
    plane_out(5, z)
    line_out(4)
    plane_out(4, z)
    cut_in()
    plane_out(1, z)
    line_out(0)
    plane_out(0, z)
    line_out(1)
    line_out(2)
    plane_out(3, z)
    line_out(3)
    line_in(4)
    small_group(0, r.tiles.at[pl.ds(0, devices - 1), 0])
    for peer in plane:
        push(r.tiles.at[:, s], r.tiles.at[:, s], r.small_s.at[0, 1], r.small_r.at[0, 1], peer)
    line_in(0)
    plane_in(5)
    line_in(1)
    plane_in(0)
    plane_out(2, z)
    plane_in(1)
    far_in(0)
    line_in(2)
    plane_in(4)
    line_out(5)
    own_x.wait()
    own_cot.wait()
    prepare_masks()
    core_in(0)
    attention_in(0)
    far_in(1)
    attention_heads(0, 0, 2)
    attention_heads(0, 2, 2)
    plane_in(2)
    attention_out(0)
    small_plane(0, r.tiles.at[:, pl.ds(0, SECTIONS - 1)])
    normalize(0)
    far_in(4)
    core_in(1)
    line_in(3)
    expand(1, 0)
    expand(1, 1)
    early = len(finish)
    far_in(2)
    expand(1, 2)
    expand(1, 3)
    core_in(4)
    contract(1)
    normalize(1)
    core_in(2)
    plane_in(3)
    attention_in(2)
    attention_heads(2, 0, 2)
    attention_heads(2, 2, 2)
    far_in(3)
    attention_out(2)
    line_in(5)
    normalize(2)
    core_in(3)
    expand(3, 0)
    expand(3, 1)
    expand(3, 2)
    expand(3, 3)
    all_sent(early)
    core_in(5)
    contract(3)
    normalize(3)

    r.sum[...] = jnp.zeros((8, LANES), WIDE)
    back_normalize(3)
    back_hidden(3)
    give_rows(3)
    back_expand_end(3)
    back_normalize(2)
    grad_up(3)
    to_plane("F3")
    back_output(2)
    grad_down(1)
    to_plane("B1")
    back_heads(2, 0, 2)
    back_heads(2, 2, 2)
    back_packed(2)
    through_plane("B1")
    give_rows(2)
    grad_output(2)
    back_packed_end(2)
    give_rows(1)
    to_plane("O2")
    grad_packed(2)
    to_plane("K2")
    back_normalize(1)
    back_hidden(1)
    through_plane("K2")
    grad_down(0)
    to_plane("B0")
    back_expand_end(1)
    back_normalize(0)
    small_out(1, r.ng.at[d])
    to_line("K2")
    to_line("B1")
    back_output(0)
    grad_up(1)
    through_plane("B0")
    to_plane("F1")
    back_heads(0, 0, 2)
    back_heads(0, 2, 2)
    back_packed(0)
    to_line("B0")
    through_plane("O2")
    through_plane("F1")
    grad_output(0)
    to_plane("O0")
    give_rows(0)
    grad_packed(0)
    to_plane("K0")
    to_line("O2")
    to_line("F1")
    through_plane("O0")
    to_owner("B1")
    back_packed_end(0)
    to_owner("B0")
    all_sent()
    through_plane("K0")
    small_group(1, r.ng.at[pl.ds(0, devices - 1)])
    r.ns[s] = functools.reduce(lambda left, right: left + right, [r.ng[index] for index in range(devices)])
    small_plane_out(1, r.ns.at[s])
    through_plane("F3")
    to_line("O0")
    to_line("K0")
    to_owner("F1")
    to_line("F3")
    to_owner("O2")
    to_owner("K2")
    to_owner("F3")
    to_owner("O0")
    to_owner("K0")

    r.sq[d] = r.sum[...]
    small_out(2, r.sq.at[d])
    for name in ("F1", "O2", "K2", "F3"):
        collect(name)
    collect("O0")
    for layer in range(2):
        done = buffers("B%d" % layer).done
        r.grad_b[layer] = done[...].reshape(cols_b, rows_b).T
    small_plane(1, r.ns.at[pl.ds(0, SECTIONS - 1)])
    grads = functools.reduce(lambda left, right: left + right, [r.ns[index] for index in range(SECTIONS)])
    norm_square = jnp.sum(jnp.sum(grads * grads, 0, keepdims=True), 1, keepdims=True)
    chosen = jnp.zeros((2, width), WIDE)
    for layer in range(4):
        chosen = jnp.where(s == layer, grads[2 * layer : 2 * layer + 2, :], chosen)
    for chip in range(chips):
        pair_of = chosen[:, chip * LANES : (chip + 1) * LANES]
        r.grad_n[...] = jnp.where(
            z == chip, jnp.where(c == 0, pair_of[:, :rows_a], pair_of[:, rows_a:]), r.grad_n[...]
        )
    collect("K0")
    small_group(2, r.sq.at[pl.ds(0, devices - 1)])
    r.sqs[s] = functools.reduce(lambda left, right: left + right, [r.sq[index] for index in range(devices)])
    small_plane_out(2, r.sqs.at[s])
    all_sent()
    small_plane(2, r.sqs.at[pl.ds(0, SECTIONS - 1)])
    squares = functools.reduce(lambda left, right: left + right, [r.sqs[index] for index in range(SECTIONS)])
    r.square[...] = squares + norm_square


def step_call(tokens, cotangent, lengths, mat_a, mat_b, norms):
    rows_a, hidden = mat_a.shape[1:]
    rows_b, cols_b = mat_b.shape[1:]
    width = tokens.shape[1]
    length = tokens.shape[0] // lengths.shape[0]
    chips = width // rows_a // 2
    scratch = kernel_scratch(chips, rows_a, rows_b, cols_b, length, width, hidden)
    shapes = []
    for _, shape, kind in scratch:
        shapes.append(pltpu.SemaphoreType.DMA(shape) if kind is None else pltpu.VMEM(shape, kind))
    anywhere, vmem = pl.BlockSpec(memory_space=pl.ANY), pl.BlockSpec(memory_space=pltpu.VMEM)
    return pl.pallas_call(
        functools.partial(step_kernel, INPUTS + OUTPUTS + tuple(name for name, _, _ in scratch)),
        out_shape=(
            jax.ShapeDtypeStruct((rows_a, hidden), WIDE),
            jax.ShapeDtypeStruct(mat_b.shape, WIDE),
            jax.ShapeDtypeStruct((2, rows_a), WIDE),
            jax.ShapeDtypeStruct((8, LANES), WIDE),
            jax.ShapeDtypeStruct((length, width), LOW),
            jax.ShapeDtypeStruct((length, width), WIDE),
        ),
        in_specs=[anywhere, anywhere, pl.BlockSpec(memory_space=pltpu.SMEM), vmem, vmem, vmem],
        out_specs=[vmem] * len(OUTPUTS),
        scratch_shapes=shapes,
        compiler_params=pltpu.CompilerParams(
            collective_id=0, has_side_effects=True, vmem_limit_bytes=KERNEL_VMEM
        ),
    )(tokens, cotangent, lengths, mat_a, mat_b, norms)


def update_kernel(*refs):
    square, output, input_grad = (ref[...] for ref in refs[:3])
    grad_norm = jnp.sqrt(square[0:1, 0:1])
    factor = CLIP_NORM / jnp.maximum(grad_norm, CLIP_NORM)
    inputs, outputs = refs[3:15], refs[15:]
    outputs[0][...] = grad_norm
    outputs[1][0] = output
    outputs[2][0] = input_grad
    for group, (rate, decay) in enumerate(
        ((MATRIX_RATE, MATRIX_DECAY), (MATRIX_RATE, MATRIX_DECAY), (NORM_RATE, 0.0))
    ):
        grad, weight, one, two = inputs[4 * group : 4 * group + 4]
        clip = grad[...].reshape(weight.shape) * factor
        moment, square_new, master = adam_update(weight[...], one[...], two[...], clip, rate, decay)
        for ref, value in zip(
            outputs[3 + 5 * group : 8 + 5 * group], (clip, moment, square_new, master, master.astype(LOW))
        ):
            ref[...] = value


def kernel_body(
    tokens, cotangent, lengths, mat_a, mat_b, norms, first_a, second_a, first_b, second_b, first_n, second_n
):
    norms, first_n, second_n = (jnp.swapaxes(value, 1, 2) for value in (norms, first_n, second_n))
    grad_a, grad_b, grad_n, square, output, input_grad = step_call(
        tokens, cotangent, lengths, mat_a, mat_b, norms
    )
    steps = 4

    def cut(value, dim):
        shape = tuple(size // steps if at == dim else size for at, size in enumerate(value.shape))
        return pl.BlockSpec(shape, lambda step: tuple(step if at == dim else 0 for at in range(len(shape))))

    def whole(value):
        return pl.BlockSpec(value.shape, lambda step: (0,) * len(value.shape))

    def like(value, kind=WIDE):
        return jax.ShapeDtypeStruct(value.shape, kind)

    args = (square, output, input_grad, grad_a, mat_a, first_a, second_a, grad_b, mat_b, first_b, second_b)
    specs = [whole(square), cut(output, 0), cut(input_grad, 0)]
    specs += [cut(grad_a, 0)] + [cut(mat_a, 1)] * 3 + [cut(grad_b, 1)] * 4
    args += (grad_n, norms, first_n, second_n)
    specs += [whole(grad_n)] + [whole(norms)] * 3
    shapes = [jax.ShapeDtypeStruct((1, 1), WIDE), like(output[None], LOW), like(input_grad[None])]
    out_specs = [whole(shapes[0]), cut(shapes[1], 1), cut(shapes[2], 1)]
    for value, spec in ((mat_a, cut(mat_a, 1)), (mat_b, cut(mat_b, 1)), (norms, whole(norms))):
        shapes += [like(value)] * 4 + [like(value, LOW)]
        out_specs += [spec] * 5
    results = pl.pallas_call(
        update_kernel,
        grid=(steps,),
        out_shape=shapes,
        in_specs=specs,
        out_specs=out_specs,
        compiler_params=pltpu.CompilerParams(vmem_limit_bytes=KERNEL_VMEM),
    )(*args)
    results = [results[0][0, 0], *results[1:]]
    results[-5:] = [jnp.swapaxes(value, 1, 2) for value in results[-5:]]
    return tuple(results)


def chosen_body(*args):
    rows_a = args[3].shape[1]
    groups = lax.axis_size("dp")
    by_kernel = rows_a % 32 == 0 and 2 * rows_a == LANES and groups * rows_a == args[0].shape[1]
    return (kernel_body if by_kernel else body)(*args)


def solution(mesh):
    placed = (
        P("dp", None),
        P("dp", None),
        P("dp", None),
        P("section", "dp", None),
        P(None, "dp", "section"),
        P("section", "dp", None),
        P("section", "dp", None),
        P("section", "dp", None),
        P(None, "dp", "section"),
        P(None, "dp", "section"),
        P("section", "dp", None),
        P("section", "dp", None),
    )
    return jax.shard_map(
        chosen_body,
        mesh=mesh,
        in_specs=placed,
        out_specs=(
            P(),
            P("section", "dp", None),
            P("section", "dp", None),
            P("section", "dp", None),
            P("section", "dp", None),
            P("section", "dp", None),
            P("section", "dp", None),
            P("section", "dp", None),
            P(None, "dp", "section"),
            P(None, "dp", "section"),
            P(None, "dp", "section"),
            P(None, "dp", "section"),
            P(None, "dp", "section"),
            P("section", "dp", None),
            P("section", "dp", None),
            P("section", "dp", None),
            P("section", "dp", None),
            P("section", "dp", None),
        ),
        check_vma=False,
    )
```

```python
import functools
import types

import jax
import jax.numpy as jnp
from jax import lax
from jax.experimental import pallas as pl
from jax.experimental.pallas import tpu as pltpu
from jax.sharding import PartitionSpec as P

HEADS = 8
STEP = 5


EPSILON = 1e-05
NEGATIVE = -1e30
CLIP_NORM = 1.0
BETA_ONE = 0.5
BETA_TWO = 0.5
ADAM_EPSILON = 1e-08
MATRIX_RATE = 0.05
NORM_RATE = 0.5
MATRIX_DECAY = 0.01


def norm_stats(value):
    centre = value - jnp.mean(value, -1, keepdims=True)
    inverse = lax.rsqrt(jnp.mean(centre * centre, -1, keepdims=True) + EPSILON)
    return (centre * inverse, inverse)


def norm_back(normal, inverse, upstream):
    return inverse * (
        upstream
        - jnp.mean(upstream, -1, keepdims=True)
        - normal * jnp.mean(upstream * normal, -1, keepdims=True)
    )


def adam_update(weight, moment_one, moment_two, gradient, step_rate, decay_rate):
    first_new = BETA_ONE * moment_one + (1.0 - BETA_ONE) * gradient
    second_new = BETA_TWO * moment_two + (1.0 - BETA_TWO) * gradient * gradient
    first_hat = first_new / (1.0 - BETA_ONE**STEP)
    second_hat = second_new / (1.0 - BETA_TWO**STEP)
    weight_new = weight - step_rate * (
        first_hat / (jnp.sqrt(second_hat) + ADAM_EPSILON) + decay_rate * weight
    )
    return (first_new, second_new, weight_new)


def segments_of(lengths_row, length):
    ends = jnp.cumsum(lengths_row, dtype=jnp.int32)
    places = jnp.arange(length, dtype=jnp.int32)
    segment = jnp.sum((ends[None, :] <= places[:, None]).astype(jnp.int32), axis=1, dtype=jnp.int32)
    live = (places < ends[-1]).astype(jnp.float32)
    return segment, live


def matmul(left, right, dims):
    return lax.dot_general(left, right, (dims, ((), ())), preferred_element_type=jnp.float32)


NN = ((1,), (0,))
NT = ((1,), (1,))
TN = ((0,), (0,))


def attention_forward(stream, weight, mask):
    length, width = stream.shape
    size = width // HEADS
    packed = matmul(stream, weight[:, : 3 * width], NN).astype(jnp.bfloat16)
    heads = packed.reshape(length, 3, HEADS, size)
    scores = jnp.einsum("qhd,khd->hqk", heads[:, 0], heads[:, 1], preferred_element_type=jnp.float32)
    scores = jnp.where(mask[None], scores * size**-0.5, NEGATIVE)
    weights = jnp.exp(scores - jnp.max(scores, -1, keepdims=True))
    probs = weights / jnp.sum(weights, -1, keepdims=True)
    mixed = jnp.einsum("hqk,khd->qhd", probs.astype(jnp.bfloat16), heads[:, 2], preferred_element_type=jnp.float32)
    mixed = mixed.reshape(length, width).astype(jnp.bfloat16)
    branch = matmul(mixed, weight[:, 3 * width :], NN)
    return branch, (heads, probs, mixed)


def attention_backward(stream, weight, kept, grad_low):
    heads, probs, mixed = kept
    length, width = stream.shape
    size = width // HEADS
    grad_out = matmul(mixed, grad_low, TN)
    grad_mixed = matmul(grad_low, weight[:, 3 * width :], NT).astype(jnp.bfloat16)
    grad_mixed = grad_mixed.reshape(length, HEADS, size)
    grad_probs = jnp.einsum("qhd,khd->hqk", grad_mixed, heads[:, 2], preferred_element_type=jnp.float32)
    centre = jnp.sum(probs * grad_probs, -1, keepdims=True)
    grad_scores = (probs * (grad_probs - centre)).astype(jnp.bfloat16)
    low = probs.astype(jnp.bfloat16)
    scale = size**-0.5
    grad_q = jnp.einsum("hqk,khd->qhd", grad_scores, heads[:, 1], preferred_element_type=jnp.float32) * scale
    grad_k = jnp.einsum("hqk,qhd->khd", grad_scores, heads[:, 0], preferred_element_type=jnp.float32) * scale
    grad_v = jnp.einsum("hqk,qhd->khd", low, grad_mixed, preferred_element_type=jnp.float32)
    packed = jnp.concatenate([grad_q, grad_k, grad_v], axis=1).reshape(length, 3 * width)
    packed = packed.astype(jnp.bfloat16)
    grad_in = matmul(stream, packed, TN)
    grad_inputs = matmul(packed, weight[:, : 3 * width], NT)
    return grad_inputs, jnp.concatenate([grad_in, grad_out], axis=1)


def feed_forward(stream, weight, down):
    pre = matmul(stream, weight, NN)
    active = jax.nn.gelu(pre, approximate=True).astype(jnp.bfloat16)
    return matmul(active, down, NN), (pre, active)


def feed_backward(stream, weight, down, kept, grad_low):
    pre, active = kept
    grad_down = matmul(active, grad_low, TN)
    grad_active = matmul(grad_low, down, NT)
    pull = jax.vjp(lambda value: jax.nn.gelu(value, approximate=True), pre)[1]
    grad_pre = pull(grad_active)[0].astype(jnp.bfloat16)
    grad_up = matmul(stream, grad_pre, TN)
    return matmul(grad_pre, weight, NT), grad_up, grad_down


def micro_step(rows, pull, segment, mats, downs, gains, biases):
    low = jnp.bfloat16
    mask = segment[:, None] == segment[None, :]
    stream, dual = rows, jnp.zeros_like(rows)
    saved = []
    for sub in range(4):
        if sub % 2 == 0:
            branch, kept = attention_forward(stream, mats[sub], mask)
        else:
            branch, kept = feed_forward(stream, mats[sub], downs[sub // 2])
        normal, inverse = norm_stats(stream.astype(jnp.float32) + branch)
        out = normal * gains[sub] + biases[sub]
        total = dual.astype(jnp.float32) + branch
        saved.append((stream, kept, normal, inverse))
        if sub < 3:
            stream, dual = out.astype(low), total.astype(low)
    dual_normal, dual_inverse = norm_stats(total)
    output = (out + dual_normal).astype(low)
    grad_out, grad_dual = pull, norm_back(dual_normal, dual_inverse, pull)
    grads_a, grads_b, grads_n = [None] * 4, [None] * 2, [None] * 4
    for sub in (3, 2, 1, 0):
        stream, kept, normal, inverse = saved[sub]
        grads_n[sub] = jnp.stack([jnp.sum(grad_out * normal, 0), jnp.sum(grad_out, 0)], axis=1)
        summed = norm_back(normal, inverse, grad_out * gains[sub])
        branch_low = (summed + grad_dual).astype(low)
        if sub % 2 == 0:
            inner, grads_a[sub] = attention_backward(stream, mats[sub], kept, branch_low)
        else:
            inner, grads_a[sub], grads_b[sub // 2] = feed_backward(
                stream, mats[sub], downs[sub // 2], kept, branch_low
            )
        grad_in = summed + inner
        if sub > 0:
            grad_out = grad_in.astype(low).astype(jnp.float32)
            grad_dual = grad_dual.astype(low).astype(jnp.float32)
    return output, grad_in, jnp.stack(grads_a), jnp.stack(grads_b), jnp.stack(grads_n)


def finish_step(grad_norm, output, input_grad, *groups):
    factor = CLIP_NORM / jnp.maximum(grad_norm, CLIP_NORM)
    results = [grad_norm, output[None], input_grad[None]]
    for weight, one, two, grad, rate, decay in groups:
        clip = grad * factor
        moment, square_new, master = adam_update(weight, one, two, clip, rate, decay)
        results += [clip, moment, square_new, master, master.astype(jnp.bfloat16)]
    return tuple(results)


def body(
    tokens, cotangent, lengths, mat_a, mat_b, norms, first_a, second_a, first_b, second_b, first_n, second_n
):
    low = jnp.bfloat16
    own = lax.axis_index("section")
    length = tokens.shape[0] // lengths.shape[0]
    rows = lax.dynamic_slice_in_dim(tokens, own * length, length, 0)
    segment, live = segments_of(lax.dynamic_index_in_dim(lengths, own, 0, keepdims=False), length)
    pull = lax.dynamic_slice_in_dim(cotangent, own * length, length, 0).astype(jnp.float32) * live[:, None]

    def gathered(value):
        return lax.all_gather(lax.all_gather(value, "dp", axis=1, tiled=True), "section", axis=0, tiled=True)

    mats = gathered(mat_a.astype(low))
    scales = gathered(norms.astype(low)).astype(jnp.float32)
    downs = lax.all_gather(mat_b.astype(low), "section", axis=2, tiled=True)
    downs = lax.all_gather(downs, "dp", axis=1, tiled=True)
    output, input_grad, part_a, part_b, part_n = micro_step(
        rows, pull, segment, mats, downs, scales[:, :, 0], scales[:, :, 1]
    )

    def scattered(value, section_dim):
        value = lax.psum_scatter(value, "section", scatter_dimension=section_dim, tiled=True)
        return lax.psum_scatter(value, "dp", scatter_dimension=1, tiled=True).astype(jnp.float32)

    grad_a = scattered(part_a.astype(low), 0)
    grad_b = scattered(part_b.astype(low), 2)
    grad_n = scattered(part_n, 0)
    square = jnp.sum(grad_a * grad_a) + jnp.sum(grad_b * grad_b) + jnp.sum(grad_n * grad_n)
    grad_norm = jnp.sqrt(lax.psum(square, ("section", "dp")))
    return finish_step(
        grad_norm, output, input_grad,
        (mat_a, first_a, second_a, grad_a, MATRIX_RATE, MATRIX_DECAY),
        (mat_b, first_b, second_b, grad_b, MATRIX_RATE, MATRIX_DECAY),
        (norms, first_n, second_n, grad_n, NORM_RATE, 0.0),
    )


LOW = jnp.bfloat16
WIDE = jnp.float32
MESH = pl.DeviceIdType.MESH
SECTIONS = 4
LANES = 128
BLOCK = 64
ROWS_FIRST = (5,)
KERNEL_VMEM = 64 * 1024 * 1024 - 256 * 1024


def gradient_items(rows_a, rows_b, cols_b, width, hidden):
    part = rows_a // SECTIONS
    return (
        ("B1", 3, cols_b // 2, rows_b),
        ("F3", 3, part, hidden // 2),
        ("O2", 2, part, width // 2),
        ("K2", 2, part, 3 * width // 2),
        ("B0", 1, cols_b // 2, rows_b),
        ("F1", 1, part, hidden // 2),
        ("O0", 0, part, width // 2),
        ("K0", 0, part, 3 * width // 2),
    )


def item_scratch(name, chips, rows, columns):
    piece = (rows, columns)
    return (
        ("own" + name, (chips, SECTIONS, 2) + piece, LOW),
        ("farx" + name, (chips,) + piece, LOW),
        ("fary" + name, (chips,) + piece, LOW),
        ("nearx" + name, (2, chips) + piece, LOW),
        ("neary" + name, (2, chips) + piece, LOW),
        ("line" + name, (chips, 2) + piece, LOW),
        ("done" + name, (2,) + piece if name[0] == "B" else (SECTIONS, 2) + piece, WIDE if name[0] == "B" else LOW),
    )


def kernel_scratch(chips, rows_a, rows_b, cols_b, length, width, hidden):
    devices = 2 * chips
    items = gradient_items(rows_a, rows_b, cols_b, width, hidden)
    count = len(items)
    received = sum((item_scratch(name, chips, rows, columns) for name, _, rows, columns in items), ())
    return received + (
        ("fac_s", (32,), None),
        ("fac_r", (32,), None),
        ("px_s", (count, 3), None),
        ("px_r", (count, 3), None),
        ("py_s", (count, 3), None),
        ("py_r", (count, 3), None),
        ("line_s", (count, chips), None),
        ("line_r", (count, chips), None),
        ("done_s", (count,), None),
        ("done_r", (count, SECTIONS), None),
        ("wa", (4, chips, 2, SECTIONS, rows_a // SECTIONS, hidden), LOW),
        ("wb", (2, chips, 2, SECTIONS, rows_b, cols_b), LOW),
        ("in_a", (1, rows_a, hidden), WIDE),
        ("in_b", (2, rows_b, cols_b), WIDE),
        ("in_n", (1, 2, rows_a), WIDE),
        ("out_a", (rows_a, hidden), WIDE),
        ("out_b", (2, rows_b, cols_b), WIDE),
        ("out_n", (2, rows_a), WIDE),
        ("out_square", (8, LANES), WIDE),
        ("out_output", (length, width), LOW),
        ("out_input", (length, width), WIDE),
        ("cut", (SECTIONS, rows_a // SECTIONS, hidden), LOW),
        ("tiles", (devices, SECTIONS, 8, LANES), WIDE),
        ("x", (4, length, width), LOW),
        ("xt", (4, chips, 2, rows_a, length), LOW),
        ("xtc", (4, chips, rows_a, 2 * length), LOW),
        ("y", (length, width), LOW),
        ("cot", (length, width), LOW),
        ("bias", (length, length), WIDE),
        ("live", (length, 1), WIDE),
        ("f", (length, width), WIDE),
        ("n", (4, length, width), WIDE),
        ("inv", (4, length, 1), WIDE),
        ("q", (2, length, width), LOW),
        ("k", (2, length, width), LOW),
        ("v", (2, length, width), LOW),
        ("kt", (2, width, length), LOW),
        ("vt", (2, width, length), LOW),
        ("ot", (2, chips, 2, rows_a, length), LOW),
        ("otc", (2, chips, rows_a, 2 * length), LOW),
        ("pt", (2, HEADS, length, length), LOW),
        ("g", (2, length, hidden), LOW),
        ("gc", (2, chips, 2 * length, rows_b), LOW),
        ("slope", (2, length, hidden), LOW),
        ("gx", (length, width), WIDE),
        ("gy", (length, width), WIDE),
        ("df", (2, 2 * length, width), LOW),
        ("dft", (2, width, 2 * length), LOW),
        ("dm", (length, width), LOW),
        ("dqt", (width, length), LOW),
        ("dh", (2, 2 * length, hidden), LOW),
        ("dp", (2, 2 * length, 3 * width), LOW),
        ("ng", (devices, 8, width), WIDE),
        ("ns", (SECTIONS, 8, width), WIDE),
        ("sq", (devices, 8, LANES), WIDE),
        ("sqs", (SECTIONS, 8, LANES), WIDE),
        ("sum", (8, LANES), WIDE),
        ("in_s", (5,), None),
        ("out_s", (6,), None),
        ("cut_s", (1,), None),
        ("cut_r", (SECTIONS,), None),
        ("gz_s", (6,), None),
        ("gz_r", (6, chips), None),
        ("gx_s", (6,), None),
        ("gx_r", (6,), None),
        ("gy_s", (6,), None),
        ("gy_r", (6,), None),
        ("rx_s", (6,), None),
        ("rx_r", (6,), None),
        ("ry_s", (6,), None),
        ("ry_r", (6,), None),
        ("gs_s", (6,), None),
        ("gs_r", (6,), None),
        ("small_s", (3, 2), None),
        ("small_r", (3, 2), None),
    )


INPUTS = ("tokens", "cotangent", "lengths", "mat_a", "mat_b", "norms")
OUTPUTS = ("grad_a", "grad_b", "grad_n", "square", "output", "input_grad")


def step_kernel(names, *refs):
    r = types.SimpleNamespace(**dict(zip(names, refs)))
    length, width = r.x.shape[1:]
    hidden = r.wa.shape[-1]
    rows_a, (rows_b, cols_b) = r.mat_a.shape[1], r.mat_b.shape[1:]
    devices = r.tiles.shape[0]
    chips = devices // 2
    half_b = cols_b // 2
    grad_items = gradient_items(rows_a, rows_b, cols_b, width, hidden)
    head = width // HEADS
    scale = head**-0.5

    s, d = lax.axis_index("section"), lax.axis_index("dp")
    z, c = lax.div(d, 2), lax.rem(d, 2)
    sx = s + 1 - 2 * lax.rem(s, 2)
    sy = lax.rem(s + 2, SECTIONS)
    sd = SECTIONS - 1 - s
    to_sibling = {"dp": d + 1 - 2 * c}
    to_up, to_down = {"dp": d + 2}, {"dp": d - 2}
    to_x, to_y = {"section": sx}, {"section": sy}
    below, above = z > 0, z < chips - 1
    group = [{"dp": lax.rem(d + step, devices)} for step in range(1, devices)]
    plane = [{"section": lax.rem(s + step, SECTIONS)} for step in range(1, SECTIONS)]
    finish = []

    def when(condition, work):
        if condition is None:
            work()
        else:
            pl.when(condition)(work)

    def push(source, target, send_sem, recv_sem, device):
        pltpu.make_async_remote_copy(
            src_ref=source,
            dst_ref=target,
            send_sem=send_sem,
            recv_sem=recv_sem,
            device_id=device,
            device_id_type=MESH,
        ).start()

    def arrived(target, sem):
        pltpu.make_async_remote_copy(
            src_ref=target, dst_ref=target, send_sem=sem, recv_sem=sem, device_id=to_x, device_id_type=MESH
        ).wait_recv()

    def sent(source, sem):
        pltpu.make_async_remote_copy(
            src_ref=source, dst_ref=source, send_sem=sem, recv_sem=sem, device_id=to_x, device_id_type=MESH
        ).wait_send()

    def at_end(condition, source, sem):
        finish.append((condition, source, sem))

    def aligned(start, size):
        return pl.ds(pl.multiple_of(start, size), size)

    own_x = pltpu.make_async_copy(r.tokens.at[aligned(s * length, length)], r.x.at[0], r.in_s.at[0])
    own_cot = pltpu.make_async_copy(r.cotangent.at[aligned(s * length, length)], r.cot, r.in_s.at[1])
    own_a = pltpu.make_async_copy(r.mat_a, r.in_a, r.in_s.at[2])
    own_b = pltpu.make_async_copy(r.mat_b, r.in_b, r.in_s.at[3])
    own_n = pltpu.make_async_copy(r.norms, r.in_n, r.in_s.at[4])
    own_a.start()
    own_n.start()
    own_b.start()
    own_x.start()
    own_cot.start()
    barrier = pltpu.get_barrier_semaphore()
    for peer in group + plane:
        pl.semaphore_signal(barrier, inc=1, device_id=peer, device_id_type=MESH)
    own_a.wait()
    r.cut[...] = r.in_a[0].astype(LOW).reshape(SECTIONS, rows_a // SECTIONS, hidden)
    r.wa[s, z, c, s] = r.cut[s]
    own_n.wait()
    norms = r.in_n[0].astype(LOW).astype(WIDE)
    nothing = jnp.zeros((2, rows_a), WIDE)
    even = jnp.concatenate([norms, nothing], axis=1)
    odd = jnp.concatenate([nothing, norms], axis=1)
    r.tiles[d, s, 0:2, :] = jnp.where(c == 0, even, odd)
    r.tiles[d, s, 2:8, :] = jnp.zeros((6, LANES), WIDE)
    own_b.wait()
    for layer in range(2):
        r.wb[layer, z, c, s] = r.in_b[layer].astype(LOW)
    pl.semaphore_wait(barrier, len(group) + len(plane))

    def put_out(slot, source, target):
        made = pltpu.make_async_copy(source, target, r.out_s.at[slot])
        made.start()
        return made

    def small_out(which, source):
        for peer in group:
            push(source, source, r.small_s.at[which, 0], r.small_r.at[which, 0], peer)

    def small_group(which, like):
        arrived(like, r.small_r.at[which, 0])
        sent(like, r.small_s.at[which, 0])

    def small_plane_out(which, source):
        for peer in plane:
            push(source, source, r.small_s.at[which, 1], r.small_r.at[which, 1], peer)

    def small_plane(which, like):
        arrived(like, r.small_r.at[which, 1])
        sent(like, r.small_s.at[which, 1])

    every = slice(None)

    def block(item, chip, section):
        if item < 4:
            return r.wa.at[item, chip, c, section]
        return r.wb.at[item - 4, chip, c, section]

    def half_block(item, section, half):
        if item < 4:
            return r.wa.at[item, :, c, section, :, pl.ds(half * hidden // 2, hidden // 2)]
        rows = pl.ds(half * rows_b // 2, rows_b // 2)
        return r.wb.at[item - 4, :, c, section, rows]

    def half_piece(item, section, half):
        rows = pl.ds(half * rows_b // 2, rows_b // 2)
        return r.wb.at[item - 4, z, c, section, rows]

    def core_blocks(item, core):
        return r.wa.at[item, :, core] if item < 4 else r.wb.at[item - 4, :, core]

    def cut_out():
        for section, device in ((sd, {"section": sd}), (sx, to_x), (sy, to_y)):
            push(r.cut.at[section], r.wa.at[s, z, c, section], r.cut_s.at[0], r.cut_r.at[s], device)
        at_end(None, r.cut.at[pl.ds(0, SECTIONS - 1)], r.cut_s.at[0])

    def cut_in():
        for section in (sx, sy, sd):
            arrived(r.wa.at[section, z, c, s], r.cut_r.at[section])

    def line_out(item):
        if item in ROWS_FIRST:
            rows_out(item)
            return
        own = block(item, z, s)
        for step in range(1, chips):
            push(own, own, r.gz_s.at[item], r.gz_r.at[item, z], {"dp": 2 * lax.rem(z + step, chips) + c})
        several = block(item, pl.ds(0, chips - 1), s)
        at_end(None, several, r.gz_s.at[item])

    def plane_out(item, chip):
        own = block(item, chip, s)
        push(own, own, r.gx_s.at[item], r.gx_r.at[item], to_x)
        push(own, own, r.gy_s.at[item], r.gy_r.at[item], to_y)

    def rows_out(item):
        arrived(half_piece(item, sd, 0), r.rx_r.at[item])
        arrived(half_piece(item, sd, 1), r.ry_r.at[item])
        rows = r.wb.at[item - 4, z, c]
        for step in range(1, chips):
            push(rows, rows, r.gz_s.at[item], r.gz_r.at[item, z], {"dp": 2 * lax.rem(z + step, chips) + c})
        push(rows, rows, r.gs_s.at[item], r.gs_r.at[item], to_sibling)
        at_end(None, r.wb.at[item - 4, pl.ds(0, chips - 1), c], r.gz_s.at[item])

    def rows_in(item):
        for step in range(1, chips):
            chip = lax.rem(z + step, chips)
            rows = r.wb.at[item - 4, chip, c]
            arrived(rows, r.gz_r.at[item, chip])
            push(rows, rows, r.gs_s.at[item], r.gs_r.at[item], to_sibling)
        at_end(None, core_blocks(item, c), r.gs_s.at[item])

    def line_in(item):
        if item in ROWS_FIRST:
            rows_in(item)
            return
        for step in range(1, chips):
            chip = lax.rem(z + step, chips)
            arrived(block(item, chip, s), r.gz_r.at[item, chip])
            plane_out(item, chip)
        core_out(item, s)
        at_end(None, block(item, every, s), r.gx_s.at[item])
        at_end(None, block(item, every, s), r.gy_s.at[item])

    def core_out(item, section):
        blocks = block(item, every, section)
        push(blocks, blocks, r.gs_s.at[item], r.gs_r.at[item], to_sibling)

    def plane_in(item):
        over = z if item in ROWS_FIRST else every
        piece = half_piece if item in ROWS_FIRST else half_block
        arrived(block(item, over, sx), r.gx_r.at[item])
        part = piece(item, sx, 1)
        push(part, part, r.ry_s.at[item], r.ry_r.at[item], to_y)
        arrived(block(item, over, sy), r.gy_r.at[item])
        part = piece(item, sy, 0)
        push(part, part, r.rx_s.at[item], r.rx_r.at[item], to_x)
        if item in ROWS_FIRST:
            at_end(None, block(item, z, sx), r.gx_s.at[item])
            at_end(None, block(item, z, sx), r.gy_s.at[item])
        else:
            core_out(item, sx)
            core_out(item, sy)
        at_end(None, part, r.ry_s.at[item])
        at_end(None, part, r.rx_s.at[item])

    def far_in(item):
        arrived(half_block(item, sd, 0), r.rx_r.at[item])
        arrived(half_block(item, sd, 1), r.ry_r.at[item])
        core_out(item, sd)
        at_end(None, core_blocks(item, c), r.gs_s.at[item])

    def core_in(item):
        arrived(core_blocks(item, 1 - c), r.gs_r.at[item])

    mine, other = pl.ds(0, length), pl.ds(length, length)

    def give(slot, source, target):
        push(source, target, r.fac_s.at[slot], r.fac_r.at[slot], to_sibling)
        at_end(None, target, r.fac_s.at[slot])

    def taken(slot, target):
        arrived(target, r.fac_r.at[slot])

    def give_rows(layer):
        r.xt[layer] = r.x[layer].T.reshape(chips, 2, rows_a, length)
        r.xtc[layer, :, :, 0:length] = r.xt[layer, :, c]
        give(layer, r.xt.at[layer, :, 1 - c], r.xtc.at[layer, :, :, other])

    def product(left, right, dims):
        return lax.dot_general(left, right, (dims, ((), ())), preferred_element_type=WIDE)

    def loop(count, work):
        def one(index, carry):
            work(index)
            return carry

        lax.fori_loop(0, count, one, 0)

    def gain_row(layer, kind):
        parts = [
            r.tiles[2 * chip, layer, kind : kind + 1, :] + r.tiles[2 * chip + 1, layer, kind : kind + 1, :]
            for chip in range(chips)
        ]
        return jnp.concatenate(parts, axis=1)

    def stats(value):
        centre = value - jnp.mean(value, -1, keepdims=True)
        inverse = lax.rsqrt(jnp.mean(centre * centre, -1, keepdims=True) + EPSILON)
        return centre * inverse, inverse

    lane = lax.broadcasted_iota(jnp.int32, (1, 2 * head), 1)
    first_half = (lane < head).astype(WIDE)
    half_masks = (first_half.astype(LOW), (1.0 - first_half).astype(LOW))

    def prepare_masks():
        ends, total = [], jnp.int32(0)
        for slot in range(r.lengths.shape[1]):
            total = total + r.lengths[s, slot]
            ends.append(total)
        down_places = lax.broadcasted_iota(jnp.int32, (length, 1), 0)
        across_places = lax.broadcasted_iota(jnp.int32, (1, length), 1)
        down_segment = jnp.zeros((length, 1), jnp.int32)
        across_segment = jnp.zeros((1, length), jnp.int32)
        for end in ends:
            down_segment = down_segment + (end <= down_places).astype(jnp.int32)
            across_segment = across_segment + (end <= across_places).astype(jnp.int32)
        r.bias[...] = jnp.where(down_segment == across_segment, 0.0, NEGATIVE)
        r.live[...] = (down_places < total).astype(WIDE)

    def matrix(layer, place):
        value = r.wa[layer, :, :, :, :, place]
        return value.reshape(width, value.shape[-1])

    def down(at, chip=slice(None)):
        blocks = [r.wb[at, chip, :, section] for section in range(SECTIONS)]
        return jnp.concatenate([block.reshape(-1, cols_b) for block in blocks], axis=1)

    def attention_in(layer):
        at = layer // 2
        rows = r.x[layer]
        r.q[at] = product(rows, matrix(layer, pl.ds(0, width)), NN).astype(LOW) * jnp.asarray(scale, LOW)
        keys = product(rows, matrix(layer, pl.ds(width, width)), NN).astype(LOW)
        r.k[at] = keys
        values = product(rows, matrix(layer, pl.ds(2 * width, width)), NN).astype(LOW)
        r.v[at] = values
        r.vt[at] = values.T

    def attention_heads(layer, begin, count):
        at = layer // 2

        def pair(index):
            lanes = aligned(index * 2 * head, 2 * head)
            for which in range(2):
                scores = product(r.k[at, :, lanes], r.q[at, :, lanes] * half_masks[which], NT) + r.bias[...]
                weights = jnp.exp(scores - jnp.max(scores, 0, keepdims=True))
                probs = (weights * (1.0 / jnp.sum(weights, 0, keepdims=True))).astype(LOW)
                r.pt[at, 2 * index + which] = probs
                place = aligned((2 * index + which) * head, head)
                r.ot[at, index, which] = product(r.vt[at, place, :], probs, NN).astype(LOW)

        for index in range(begin, begin + count):
            pair(index)

    def attention_out(layer):
        at = layer // 2
        r.otc[at, :, :, 0:length] = r.ot[at, :, c]
        give(4 + at, r.ot.at[at, :, 1 - c], r.otc.at[at, :, :, other])
        r.f[...] = product(r.ot[at].reshape(width, length).T, matrix(layer, pl.ds(3 * width, width)), NN)

    def expand(layer, index):
        at = layer // 2
        place = pl.ds(index * width, width)
        pre = product(r.x[layer], matrix(layer, place), NN)
        squared = pre * pre
        slope = 0.7978845608 * (1.0 + 3 * 0.044715 * squared)
        bent = jnp.tanh(0.7978845608 * pre * (1.0 + 0.044715 * squared))
        r.g[at, :, place] = (0.5 * pre * (1.0 + bent)).astype(LOW)
        r.slope[at, :, place] = (0.5 * (1.0 + bent) + 0.5 * pre * (1.0 - bent * bent) * slope).astype(LOW)
        block = aligned((2 * index + c) * rows_b, rows_b)
        r.gc[at, index, 0:length, :] = r.g[at, :, block]
        block = aligned((2 * index + 1 - c) * rows_b, rows_b)
        give(6 + chips * at + index, r.g.at[at, :, block], r.gc.at[at, index, other, :])

    def contract(layer):
        r.f[...] = product(r.g[layer // 2], down(layer // 2), NN)

    def by_rows(work):
        for index in range(length // BLOCK):
            work(pl.ds(index * BLOCK, BLOCK))

    def normalize(layer):
        gain, offset = gain_row(layer, 0), gain_row(layer, 1)

        def some(rows):
            branch = r.f[rows, :]
            normal, inverse = stats(r.x[layer, rows, :].astype(WIDE) + branch)
            r.n[layer, rows, :] = normal
            r.inv[layer, rows, :] = inverse
            out = normal * gain + offset
            dual = branch if layer == 0 else r.y[rows, :].astype(WIDE) + branch
            if layer < 3:
                r.x[layer + 1, rows, :] = out.astype(LOW)
                r.y[rows, :] = dual.astype(LOW)
            else:
                dual_normal, dual_inverse = stats(dual)
                r.out_output[rows, :] = (out + dual_normal).astype(LOW)
                pull = r.cot[rows, :].astype(WIDE) * r.live[rows, :]
                r.gx[rows, :] = pull
                r.gy[rows, :] = norm_back(dual_normal, dual_inverse, pull)

        by_rows(some)

    def back_normalize(layer):
        gain = gain_row(layer, 0)

        def some(index, sums):
            rows = pl.ds(index * BLOCK, BLOCK)
            upstream = r.gx[rows, :]
            normal = r.n[layer, rows, :]
            summed = norm_back(normal, r.inv[layer, rows, :], upstream * gain)
            dual = r.gy[rows, :]
            r.gx[rows, :] = summed
            r.df[layer // 2, rows, :] = (summed + dual).astype(LOW)
            if layer == 3:
                r.gy[rows, :] = dual.astype(LOW).astype(WIDE)
            return (
                sums[0] + jnp.sum(upstream * normal, 0, keepdims=True),
                sums[1] + jnp.sum(upstream, 0, keepdims=True),
            )

        zero = jnp.zeros((1, width), WIDE)
        gains, offsets = zero, zero
        for index in range(length // BLOCK):
            gains, offsets = some(index, (gains, offsets))
        r.ng[d, 2 * layer : 2 * layer + 1, :] = gains
        r.ng[d, 2 * layer + 1 : 2 * layer + 2, :] = offsets

    def pass_down(layer, inner):
        total = r.gx[...] + inner
        if layer > 0:
            r.gx[...] = total.astype(LOW).astype(WIDE)
        else:
            r.out_input[...] = total

    base = 6 + 2 * chips

    def back_hidden(layer):
        at = layer // 2
        r.dft[at, :, 0:length] = r.df[at, 0:length, :].T
        give(base + at, r.dft.at[at, :, mine], r.dft.at[at, :, other])
        for index in range(hidden // width):
            place = pl.ds(index * width, width)
            pulled = product(r.df[at, 0:length, :], down(at, pl.ds(index, 1)), NT)
            r.dh[at, 0:length, place] = (pulled * r.slope[at, :, place].astype(WIDE)).astype(LOW)
            give(base + 2 + chips * at + index, r.dh.at[at, mine, place], r.dh.at[at, other, place])

    def back_expand_end(layer):
        pass_down(layer, product(r.dh[layer // 2, 0:length, :], matrix(layer, pl.ds(0, hidden)), NT))

    def back_output(layer):
        at = layer // 2
        give(base + 2 + 2 * chips + at, r.df.at[at, mine], r.df.at[at, other])
        r.dm[...] = product(r.df[at, 0:length, :], matrix(layer, pl.ds(3 * width, width)), NT).astype(LOW)
        r.kt[at] = (r.k[at] * jnp.asarray(scale, LOW)).T

    def back_heads(layer, begin, count):
        at = layer // 2

        def pair(index):
            lanes = aligned(index * 2 * head, 2 * head)
            pulled = r.dm[:, lanes]
            keys, values = [], []
            for which in range(2):
                probs = r.pt[at, 2 * index + which]
                grad = product(r.v[at, :, lanes], pulled * half_masks[which], NT)
                full = probs.astype(WIDE)
                centre = jnp.sum(full * grad, 0, keepdims=True)
                scores = (full * (grad - centre)).astype(LOW)
                keys.append(product(scores, r.q[at, :, lanes], NN))
                values.append(product(probs, pulled, NN))
                place = aligned((2 * index + which) * head, head)
                r.dqt[place, :] = product(r.kt[at, place, :], scores, NN).astype(LOW)
            r.dp[at, 0:length, aligned(width + index * 2 * head, 2 * head)] = jnp.where(
                lane < head, keys[0], keys[1]
            ).astype(LOW)
            r.dp[at, 0:length, aligned(2 * width + index * 2 * head, 2 * head)] = jnp.where(
                lane < head, values[0], values[1]
            ).astype(LOW)

        def pairs(step):
            pair(begin + 2 * step)
            pair(begin + 2 * step + 1)

        loop(count // 2, pairs)

    def back_packed(layer):
        at = layer // 2
        slot = base + 4 + 2 * chips + 2 * at
        place = pl.ds(width, 2 * width)
        give(slot, r.dp.at[at, mine, place], r.dp.at[at, other, place])
        r.dp[at, 0:length, 0:width] = r.dqt[...].T
        place = pl.ds(0, width)
        give(slot + 1, r.dp.at[at, mine, place], r.dp.at[at, other, place])

    def back_packed_end(layer):
        pass_down(layer, product(r.dp[layer // 2, 0:length, :], matrix(layer, pl.ds(0, 3 * width)), NT))

    def keep(name, half, place, value):
        own = getattr(r, "own" + name)
        own[:, :, half, :, place] = value.astype(LOW).reshape(chips, SECTIONS, rows_a // SECTIONS, value.shape[1])

    def chip_rows(value):
        return value.reshape(chips * rows_a, 2 * length)

    def grad_down(at):
        own = getattr(r, "ownB%d" % at)
        taken(base + at, r.dft.at[at, :, other])
        for chip in range(chips):
            taken(6 + chips * at + chip, r.gc.at[at, chip, other, :])
            value = product(r.dft[at], r.gc[at, chip], NN)
            own[chip] = value.astype(LOW).reshape(SECTIONS, 2, half_b, rows_b)

    def grad_up(layer):
        at = layer // 2
        taken(layer, r.xtc.at[layer, :, :, other])
        for index in range(hidden // width):
            place = pl.ds(index * width, width)
            taken(base + 2 + chips * at + index, r.dh.at[at, other, place])
            value = product(chip_rows(r.xtc[layer]), r.dh[at, :, place], NN)
            keep("F%d" % layer, index // 2, pl.ds(index % 2 * width, width), value)

    def grad_output(layer):
        at = layer // 2
        taken(4 + at, r.otc.at[at, :, :, other])
        taken(base + 2 + 2 * chips + at, r.df.at[at, other])
        for half in range(2):
            place = pl.ds(half * width // 2, width // 2)
            value = product(chip_rows(r.otc[at]), r.df[at, :, place], NN)
            keep("O%d" % layer, half, pl.ds(0, width // 2), value)

    def grad_packed(layer):
        at = layer // 2
        slot = base + 4 + 2 * chips + 2 * at
        taken(layer, r.xtc.at[layer, :, :, other])
        taken(slot, r.dp.at[at, other, pl.ds(width, 2 * width)])
        taken(slot + 1, r.dp.at[at, other, pl.ds(0, width)])
        part = 3 * width // 2
        for half in range(2):
            value = product(chip_rows(r.xtc[layer]), r.dp[at, :, half * part : (half + 1) * part], NN)
            keep("K%d" % layer, half, pl.ds(0, part), value)

    def joined(target, others):
        return functools.reduce(
            lambda left, right: left + right, [ref[...].astype(WIDE) for ref in (target, *others)]
        )

    def add_into(target, others):
        if len(others) == 1:
            target[...] = target[...] + others[0][...]
        else:
            target[...] = joined(target, others).astype(LOW)

    places = {name: place for place, (name, _, _, _) in enumerate(grad_items)}

    def buffers(name):
        parts = ("own", "farx", "fary", "nearx", "neary", "line", "done")
        return types.SimpleNamespace(**{part: getattr(r, part + name) for part in parts})

    def to_plane(name):
        item, place = buffers(name), places[name]

        def over_x(section, half, target, slot):
            push(item.own.at[:, section, half], target, r.px_s.at[place, slot], r.px_r.at[place, slot], to_x)
            at_end(None, item.farx, r.px_s.at[place, slot])

        def over_y(section, half, target, slot):
            push(item.own.at[:, section, half], target, r.py_s.at[place, slot], r.py_r.at[place, slot], to_y)
            at_end(None, item.farx, r.py_s.at[place, slot])

        over_x(sd, 0, item.farx, 2)
        over_y(sd, 1, item.fary, 2)
        over_x(sx, 0, item.nearx.at[0], 0)
        over_y(sy, 1, item.neary.at[1], 1)

    def through_plane(name):
        item, place = buffers(name), places[name]
        own = item.own
        arrived(item.fary, r.py_r.at[place, 2])
        add_into(own.at[:, sx, 1], [item.fary])
        push(own.at[:, sx, 1], item.nearx.at[1], r.px_s.at[place, 1], r.px_r.at[place, 1], to_x)
        at_end(None, item.farx, r.px_s.at[place, 1])
        arrived(item.farx, r.px_r.at[place, 2])
        add_into(own.at[:, sy, 0], [item.farx])
        push(own.at[:, sy, 0], item.neary.at[0], r.py_s.at[place, 0], r.py_r.at[place, 0], to_y)
        at_end(None, item.farx, r.py_s.at[place, 0])

    def to_line(name):
        item, place = buffers(name), places[name]
        own = item.own.at[:, s]
        for half in range(2):
            arrived(item.nearx.at[half], r.px_r.at[place, half])
            arrived(item.neary.at[half], r.py_r.at[place, half])
            add_into(own.at[:, half], [item.nearx.at[half], item.neary.at[half]])
        for step in range(1, chips):
            chip = lax.rem(z + step, chips)
            push(
                own.at[chip],
                item.line.at[z],
                r.line_s.at[place, step],
                r.line_r.at[place, z],
                {"dp": 2 * chip + c},
            )
            at_end(None, item.line.at[0], r.line_s.at[place, step])

    def to_owner(name):
        item, place = buffers(name), places[name]
        others = [lax.rem(z + step, chips) for step in range(1, chips)]
        for chip in others:
            arrived(item.line.at[chip], r.line_r.at[place, chip])
        total = joined(item.own.at[z, s], [item.line.at[chip] for chip in others])
        square = total * total
        while square.ndim > 2:
            square = jnp.sum(square, 0)
        square = jnp.sum(jnp.sum(square, 0, keepdims=True), 1, keepdims=True)
        r.sum[...] = r.sum[...] + jnp.broadcast_to(square, (8, LANES))
        if name[0] == "B":
            item.done[...] = total
            return
        item.done[s] = total.astype(LOW)
        layer = grad_items[place][1]
        mine = item.done.at[s]
        away = s != layer
        when(
            away,
            lambda: push(mine, mine, r.done_s.at[place], r.done_r.at[place, s], {"section": jnp.int32(layer)}),
        )
        at_end(away, mine, r.done_s.at[place])

    def collect(name):
        item, place = buffers(name), places[name]
        layer = grad_items[place][1]

        def work():
            for section in range(SECTIONS):
                if section != layer:
                    arrived(item.done.at[section], r.done_r.at[place, section])
            columns = item.done.shape[-1]
            start = 3 * width if name[0] == "O" else 0
            for section in range(SECTIONS):
                for half in range(2):
                    rows = pl.ds(section * (rows_a // SECTIONS), rows_a // SECTIONS)
                    place_to = pl.ds(start + half * columns, columns)
                    r.out_a[rows, place_to] = item.done[section, half].astype(WIDE)

        when(s == layer, work)

    def all_sent(count=None):
        for condition, source, sem in finish[:count]:
            when(condition, functools.partial(sent, source, sem))
        del finish[:count]

    cut_out()
    small_out(0, r.tiles.at[d, s])
    plane_out(5, z)
    line_out(4)
    plane_out(4, z)
    cut_in()
    plane_out(1, z)
    line_out(0)
    plane_out(0, z)
    line_out(1)
    line_out(2)
    plane_out(3, z)
    line_out(3)
    line_in(4)
    small_group(0, r.tiles.at[pl.ds(0, devices - 1), 0])
    for peer in plane:
        push(r.tiles.at[:, s], r.tiles.at[:, s], r.small_s.at[0, 1], r.small_r.at[0, 1], peer)
    line_in(0)
    plane_in(5)
    line_in(1)
    plane_in(0)
    plane_out(2, z)
    plane_in(1)
    far_in(0)
    line_in(2)
    plane_in(4)
    line_out(5)
    own_x.wait()
    own_cot.wait()
    prepare_masks()
    core_in(0)
    attention_in(0)
    far_in(1)
    attention_heads(0, 0, 2)
    attention_heads(0, 2, 2)
    plane_in(2)
    attention_out(0)
    small_plane(0, r.tiles.at[:, pl.ds(0, SECTIONS - 1)])
    normalize(0)
    far_in(4)
    core_in(1)
    line_in(3)
    expand(1, 0)
    expand(1, 1)
    early = len(finish)
    far_in(2)
    expand(1, 2)
    expand(1, 3)
    core_in(4)
    contract(1)
    normalize(1)
    core_in(2)
    plane_in(3)
    attention_in(2)
    attention_heads(2, 0, 2)
    attention_heads(2, 2, 2)
    far_in(3)
    attention_out(2)
    line_in(5)
    normalize(2)
    core_in(3)
    expand(3, 0)
    expand(3, 1)
    expand(3, 2)
    expand(3, 3)
    all_sent(early)
    core_in(5)
    contract(3)
    normalize(3)
    leaving = [put_out(0, r.out_output, r.output)]

    r.sum[...] = jnp.zeros((8, LANES), WIDE)
    back_normalize(3)
    back_hidden(3)
    give_rows(3)
    back_expand_end(3)
    back_normalize(2)
    grad_up(3)
    to_plane("F3")
    back_output(2)
    grad_down(1)
    to_plane("B1")
    back_heads(2, 0, 2)
    back_heads(2, 2, 2)
    back_packed(2)
    through_plane("B1")
    give_rows(2)
    grad_output(2)
    back_packed_end(2)
    give_rows(1)
    to_plane("O2")
    grad_packed(2)
    to_plane("K2")
    back_normalize(1)
    back_hidden(1)
    through_plane("K2")
    grad_down(0)
    to_plane("B0")
    back_expand_end(1)
    back_normalize(0)
    small_out(1, r.ng.at[d])
    to_line("K2")
    to_line("B1")
    back_output(0)
    grad_up(1)
    through_plane("B0")
    to_plane("F1")
    back_heads(0, 0, 2)
    back_heads(0, 2, 2)
    back_packed(0)
    to_line("B0")
    through_plane("O2")
    through_plane("F1")
    grad_output(0)
    to_plane("O0")
    give_rows(0)
    grad_packed(0)
    to_plane("K0")
    to_line("O2")
    to_line("F1")
    through_plane("O0")
    to_owner("B1")
    back_packed_end(0)
    leaving.append(put_out(1, r.out_input, r.input_grad))
    to_owner("B0")
    all_sent()
    through_plane("K0")
    small_group(1, r.ng.at[pl.ds(0, devices - 1)])
    r.ns[s] = functools.reduce(lambda left, right: left + right, [r.ng[index] for index in range(devices)])
    small_plane_out(1, r.ns.at[s])
    through_plane("F3")
    to_line("O0")
    to_line("K0")
    to_owner("F1")
    to_line("F3")
    to_owner("O2")
    to_owner("K2")
    to_owner("F3")
    to_owner("O0")
    to_owner("K0")

    r.sq[d] = r.sum[...]
    small_out(2, r.sq.at[d])
    for name in ("F1", "O2", "K2", "F3"):
        collect(name)
    collect("O0")
    for layer in range(2):
        done = buffers("B%d" % layer).done
        r.out_b[layer] = done[...].reshape(cols_b, rows_b).T
    leaving.append(put_out(2, r.out_b, r.grad_b))
    small_plane(1, r.ns.at[pl.ds(0, SECTIONS - 1)])
    grads = functools.reduce(lambda left, right: left + right, [r.ns[index] for index in range(SECTIONS)])
    norm_square = jnp.sum(jnp.sum(grads * grads, 0, keepdims=True), 1, keepdims=True)
    chosen = jnp.zeros((2, width), WIDE)
    for layer in range(4):
        chosen = jnp.where(s == layer, grads[2 * layer : 2 * layer + 2, :], chosen)
    shard = jnp.zeros((2, rows_a), WIDE)
    for chip in range(chips):
        pair_of = chosen[:, chip * LANES : (chip + 1) * LANES]
        shard = jnp.where(z == chip, jnp.where(c == 0, pair_of[:, :rows_a], pair_of[:, rows_a:]), shard)
    r.out_n[...] = shard
    leaving.append(put_out(3, r.out_n, r.grad_n))
    collect("K0")
    leaving.append(put_out(4, r.out_a, r.grad_a))
    small_group(2, r.sq.at[pl.ds(0, devices - 1)])
    r.sqs[s] = functools.reduce(lambda left, right: left + right, [r.sq[index] for index in range(devices)])
    small_plane_out(2, r.sqs.at[s])
    all_sent()
    small_plane(2, r.sqs.at[pl.ds(0, SECTIONS - 1)])
    squares = functools.reduce(lambda left, right: left + right, [r.sqs[index] for index in range(SECTIONS)])
    r.out_square[...] = squares + norm_square
    leaving.append(put_out(5, r.out_square, r.square))
    for made in leaving:
        made.wait()


def step_call(tokens, cotangent, lengths, mat_a, mat_b, norms):
    rows_a, hidden = mat_a.shape[1:]
    rows_b, cols_b = mat_b.shape[1:]
    width = tokens.shape[1]
    length = tokens.shape[0] // lengths.shape[0]
    chips = width // rows_a // 2
    scratch = kernel_scratch(chips, rows_a, rows_b, cols_b, length, width, hidden)
    shapes = []
    for _, shape, kind in scratch:
        shapes.append(pltpu.SemaphoreType.DMA(shape) if kind is None else pltpu.VMEM(shape, kind))
    anywhere = pl.BlockSpec(memory_space=pl.ANY)
    return pl.pallas_call(
        functools.partial(step_kernel, INPUTS + OUTPUTS + tuple(name for name, _, _ in scratch)),
        out_shape=(
            jax.ShapeDtypeStruct((rows_a, hidden), WIDE),
            jax.ShapeDtypeStruct(mat_b.shape, WIDE),
            jax.ShapeDtypeStruct((2, rows_a), WIDE),
            jax.ShapeDtypeStruct((8, LANES), WIDE),
            jax.ShapeDtypeStruct((length, width), LOW),
            jax.ShapeDtypeStruct((length, width), WIDE),
        ),
        in_specs=[anywhere, anywhere, pl.BlockSpec(memory_space=pltpu.SMEM), anywhere, anywhere, anywhere],
        out_specs=[anywhere] * len(OUTPUTS),
        scratch_shapes=shapes,
        compiler_params=pltpu.CompilerParams(
            collective_id=0, has_side_effects=True, vmem_limit_bytes=KERNEL_VMEM
        ),
    )(tokens, cotangent, lengths, mat_a, mat_b, norms)


def update_kernel(names, *refs):
    r = types.SimpleNamespace(**dict(zip(names, refs)))
    started = []

    def copy(source, target):
        made = pltpu.make_async_copy(source, target, r.sems.at[len(started)])
        made.start()
        started.append(made)
        return made

    half = r.mat_a.shape[1] // 2
    parts = [("a", pl.ds(0, half), MATRIX_RATE, MATRIX_DECAY), ("a", pl.ds(half, half), MATRIX_RATE, MATRIX_DECAY)]
    parts += [("b", slice(None), MATRIX_RATE, MATRIX_DECAY), ("n", slice(None), NORM_RATE, 0.0)]
    coming = [copy(r.square, r.in_square)]
    waits = []
    for name, rows, _, _ in parts:
        coming_part = []
        for kind in ("grad", "mat", "first", "second"):
            source, target = getattr(r, kind + "_" + name), getattr(r, "in_%s_%s" % (kind, name))
            coming_part.append(copy(source.at[:, rows], target.at[:, rows]))
        waits.append(coming_part)
    leaving = [copy(r.output, r.new_output.at[0]), copy(r.input_grad, r.new_input_grad.at[0])]
    coming[0].wait()
    grad_norm = jnp.sqrt(r.in_square[0:1, 0:1])
    factor = CLIP_NORM / jnp.maximum(grad_norm, CLIP_NORM)
    r.grad_norm[...] = grad_norm
    for (name, rows, rate, decay), coming_part in zip(parts, waits):
        for one in coming_part:
            one.wait()
        grad, weight, one, two = (
            getattr(r, "in_%s_%s" % (kind, name))[:, rows] for kind in ("grad", "mat", "first", "second")
        )
        clip = grad * factor
        moment, square, master = adam_update(weight, one, two, clip, rate, decay)
        for kind, value in zip(RESULTS, (clip, moment, square, master, master.astype(LOW))):
            held = getattr(r, "out_%s_%s" % (kind, name))
            held[:, rows] = value
            leaving.append(copy(held.at[:, rows], getattr(r, "%s_%s" % (kind, name)).at[:, rows]))
    for one in leaving:
        one.wait()


RESULTS = ("clip", "moment", "square", "master", "copy")


def kernel_body(
    tokens, cotangent, lengths, mat_a, mat_b, norms, first_a, second_a, first_b, second_b, first_n, second_n
):
    norms, first_n, second_n = (jnp.swapaxes(value, 1, 2) for value in (norms, first_n, second_n))
    grad_a, grad_b, grad_n, square, output, input_grad = step_call(
        tokens, cotangent, lengths, mat_a, mat_b, norms
    )
    held = {"a": mat_a, "b": mat_b, "n": norms}
    args = {"square": square, "output": output, "input_grad": input_grad}
    args.update(grad_a=grad_a[None], mat_a=mat_a, first_a=first_a, second_a=second_a)
    args.update(grad_b=grad_b, mat_b=mat_b, first_b=first_b, second_b=second_b)
    args.update(grad_n=grad_n[None], mat_n=norms, first_n=first_n, second_n=second_n)
    anywhere, vmem = pl.BlockSpec(memory_space=pl.ANY), pl.BlockSpec(memory_space=pltpu.VMEM)
    shapes = {
        "grad_norm": jax.ShapeDtypeStruct((1, 1), WIDE),
        "new_output": jax.ShapeDtypeStruct((1,) + output.shape, LOW),
        "new_input_grad": jax.ShapeDtypeStruct((1,) + input_grad.shape, WIDE),
    }
    scratch = {"in_square": pltpu.VMEM(square.shape, WIDE)}
    for name, value in held.items():
        for kind in RESULTS:
            dtype = LOW if kind == "copy" else WIDE
            shapes["%s_%s" % (kind, name)] = jax.ShapeDtypeStruct(value.shape, dtype)
            scratch["out_%s_%s" % (kind, name)] = pltpu.VMEM(value.shape, dtype)
        for kind in ("grad", "mat", "first", "second"):
            scratch["in_%s_%s" % (kind, name)] = pltpu.VMEM(value.shape, WIDE)
    scratch["sems"] = pltpu.SemaphoreType.DMA((39,))
    results = pl.pallas_call(
        functools.partial(update_kernel, (*args, *shapes, *scratch)),
        out_shape=tuple(shapes.values()),
        in_specs=[anywhere] * len(args),
        out_specs=(vmem,) + (anywhere,) * (len(shapes) - 1),
        scratch_shapes=tuple(scratch.values()),
        compiler_params=pltpu.CompilerParams(vmem_limit_bytes=KERNEL_VMEM),
    )(*args.values())
    results = [results[0][0, 0], *results[1:]]
    results[-5:] = [jnp.swapaxes(value, 1, 2) for value in results[-5:]]
    return tuple(results)


def chosen_body(*args):
    rows_a = args[3].shape[1]
    groups = lax.axis_size("dp")
    by_kernel = rows_a % 32 == 0 and 2 * rows_a == LANES and groups * rows_a == args[0].shape[1]
    return (kernel_body if by_kernel else body)(*args)


def solution(mesh):
    placed = (
        P("dp", None),
        P("dp", None),
        P("dp", None),
        P("section", "dp", None),
        P(None, "dp", "section"),
        P("section", "dp", None),
        P("section", "dp", None),
        P("section", "dp", None),
        P(None, "dp", "section"),
        P(None, "dp", "section"),
        P("section", "dp", None),
        P("section", "dp", None),
    )
    return jax.shard_map(
        chosen_body,
        mesh=mesh,
        in_specs=placed,
        out_specs=(
            P(),
            P("section", "dp", None),
            P("section", "dp", None),
            P("section", "dp", None),
            P("section", "dp", None),
            P("section", "dp", None),
            P("section", "dp", None),
            P("section", "dp", None),
            P(None, "dp", "section"),
            P(None, "dp", "section"),
            P(None, "dp", "section"),
            P(None, "dp", "section"),
            P(None, "dp", "section"),
            P("section", "dp", None),
            P("section", "dp", None),
            P("section", "dp", None),
            P("section", "dp", None),
            P("section", "dp", None),
        ),
        check_vma=False,
    )
```

```python
import functools
import types

import jax
import jax.numpy as jnp
from jax import lax
from jax.experimental import pallas as pl
from jax.experimental.pallas import tpu as pltpu
from jax.sharding import PartitionSpec as P

HEADS = 8
STEP = 5


EPSILON = 1e-05
NEGATIVE = -1e30
CLIP_NORM = 1.0
BETA_ONE = 0.5
BETA_TWO = 0.5
ADAM_EPSILON = 1e-08
MATRIX_RATE = 0.05
NORM_RATE = 0.5
MATRIX_DECAY = 0.01


def norm_stats(value):
    centre = value - jnp.mean(value, -1, keepdims=True)
    inverse = lax.rsqrt(jnp.mean(centre * centre, -1, keepdims=True) + EPSILON)
    return (centre * inverse, inverse)


def norm_back(normal, inverse, upstream):
    return inverse * (
        upstream
        - jnp.mean(upstream, -1, keepdims=True)
        - normal * jnp.mean(upstream * normal, -1, keepdims=True)
    )


def adam_update(weight, moment_one, moment_two, gradient, step_rate, decay_rate):
    first_new = BETA_ONE * moment_one + (1.0 - BETA_ONE) * gradient
    second_new = BETA_TWO * moment_two + (1.0 - BETA_TWO) * gradient * gradient
    first_hat = first_new / (1.0 - BETA_ONE**STEP)
    second_hat = second_new / (1.0 - BETA_TWO**STEP)
    weight_new = weight - step_rate * (
        first_hat / (jnp.sqrt(second_hat) + ADAM_EPSILON) + decay_rate * weight
    )
    return (first_new, second_new, weight_new)


def segments_of(lengths_row, length):
    ends = jnp.cumsum(lengths_row, dtype=jnp.int32)
    places = jnp.arange(length, dtype=jnp.int32)
    segment = jnp.sum((ends[None, :] <= places[:, None]).astype(jnp.int32), axis=1, dtype=jnp.int32)
    live = (places < ends[-1]).astype(jnp.float32)
    return segment, live


def matmul(left, right, dims):
    return lax.dot_general(left, right, (dims, ((), ())), preferred_element_type=jnp.float32)


NN = ((1,), (0,))
NT = ((1,), (1,))
TN = ((0,), (0,))


def attention_forward(stream, weight, mask):
    length, width = stream.shape
    size = width // HEADS
    packed = matmul(stream, weight[:, : 3 * width], NN).astype(jnp.bfloat16)
    heads = packed.reshape(length, 3, HEADS, size)
    scores = jnp.einsum("qhd,khd->hqk", heads[:, 0], heads[:, 1], preferred_element_type=jnp.float32)
    scores = jnp.where(mask[None], scores * size**-0.5, NEGATIVE)
    weights = jnp.exp(scores - jnp.max(scores, -1, keepdims=True))
    probs = weights / jnp.sum(weights, -1, keepdims=True)
    mixed = jnp.einsum("hqk,khd->qhd", probs.astype(jnp.bfloat16), heads[:, 2], preferred_element_type=jnp.float32)
    mixed = mixed.reshape(length, width).astype(jnp.bfloat16)
    branch = matmul(mixed, weight[:, 3 * width :], NN)
    return branch, (heads, probs, mixed)


def attention_backward(stream, weight, kept, grad_low):
    heads, probs, mixed = kept
    length, width = stream.shape
    size = width // HEADS
    grad_out = matmul(mixed, grad_low, TN)
    grad_mixed = matmul(grad_low, weight[:, 3 * width :], NT).astype(jnp.bfloat16)
    grad_mixed = grad_mixed.reshape(length, HEADS, size)
    grad_probs = jnp.einsum("qhd,khd->hqk", grad_mixed, heads[:, 2], preferred_element_type=jnp.float32)
    centre = jnp.sum(probs * grad_probs, -1, keepdims=True)
    grad_scores = (probs * (grad_probs - centre)).astype(jnp.bfloat16)
    low = probs.astype(jnp.bfloat16)
    scale = size**-0.5
    grad_q = jnp.einsum("hqk,khd->qhd", grad_scores, heads[:, 1], preferred_element_type=jnp.float32) * scale
    grad_k = jnp.einsum("hqk,qhd->khd", grad_scores, heads[:, 0], preferred_element_type=jnp.float32) * scale
    grad_v = jnp.einsum("hqk,qhd->khd", low, grad_mixed, preferred_element_type=jnp.float32)
    packed = jnp.concatenate([grad_q, grad_k, grad_v], axis=1).reshape(length, 3 * width)
    packed = packed.astype(jnp.bfloat16)
    grad_in = matmul(stream, packed, TN)
    grad_inputs = matmul(packed, weight[:, : 3 * width], NT)
    return grad_inputs, jnp.concatenate([grad_in, grad_out], axis=1)


def feed_forward(stream, weight, down):
    pre = matmul(stream, weight, NN)
    active = jax.nn.gelu(pre, approximate=True).astype(jnp.bfloat16)
    return matmul(active, down, NN), (pre, active)


def feed_backward(stream, weight, down, kept, grad_low):
    pre, active = kept
    grad_down = matmul(active, grad_low, TN)
    grad_active = matmul(grad_low, down, NT)
    pull = jax.vjp(lambda value: jax.nn.gelu(value, approximate=True), pre)[1]
    grad_pre = pull(grad_active)[0].astype(jnp.bfloat16)
    grad_up = matmul(stream, grad_pre, TN)
    return matmul(grad_pre, weight, NT), grad_up, grad_down


def micro_step(rows, pull, segment, mats, downs, gains, biases):
    low = jnp.bfloat16
    mask = segment[:, None] == segment[None, :]
    stream, dual = rows, jnp.zeros_like(rows)
    saved = []
    for sub in range(4):
        if sub % 2 == 0:
            branch, kept = attention_forward(stream, mats[sub], mask)
        else:
            branch, kept = feed_forward(stream, mats[sub], downs[sub // 2])
        normal, inverse = norm_stats(stream.astype(jnp.float32) + branch)
        out = normal * gains[sub] + biases[sub]
        total = dual.astype(jnp.float32) + branch
        saved.append((stream, kept, normal, inverse))
        if sub < 3:
            stream, dual = out.astype(low), total.astype(low)
    dual_normal, dual_inverse = norm_stats(total)
    output = (out + dual_normal).astype(low)
    grad_out, grad_dual = pull, norm_back(dual_normal, dual_inverse, pull)
    grads_a, grads_b, grads_n = [None] * 4, [None] * 2, [None] * 4
    for sub in (3, 2, 1, 0):
        stream, kept, normal, inverse = saved[sub]
        grads_n[sub] = jnp.stack([jnp.sum(grad_out * normal, 0), jnp.sum(grad_out, 0)], axis=1)
        summed = norm_back(normal, inverse, grad_out * gains[sub])
        branch_low = (summed + grad_dual).astype(low)
        if sub % 2 == 0:
            inner, grads_a[sub] = attention_backward(stream, mats[sub], kept, branch_low)
        else:
            inner, grads_a[sub], grads_b[sub // 2] = feed_backward(
                stream, mats[sub], downs[sub // 2], kept, branch_low
            )
        grad_in = summed + inner
        if sub > 0:
            grad_out = grad_in.astype(low).astype(jnp.float32)
            grad_dual = grad_dual.astype(low).astype(jnp.float32)
    return output, grad_in, jnp.stack(grads_a), jnp.stack(grads_b), jnp.stack(grads_n)


def finish_step(grad_norm, output, input_grad, *groups):
    factor = CLIP_NORM / jnp.maximum(grad_norm, CLIP_NORM)
    results = [grad_norm, output[None], input_grad[None]]
    for weight, one, two, grad, rate, decay in groups:
        clip = grad * factor
        moment, square_new, master = adam_update(weight, one, two, clip, rate, decay)
        results += [clip, moment, square_new, master, master.astype(jnp.bfloat16)]
    return tuple(results)


def body(
    tokens, cotangent, lengths, mat_a, mat_b, norms, first_a, second_a, first_b, second_b, first_n, second_n
):
    low = jnp.bfloat16
    own = lax.axis_index("section")
    length = tokens.shape[0] // lengths.shape[0]
    rows = lax.dynamic_slice_in_dim(tokens, own * length, length, 0)
    segment, live = segments_of(lax.dynamic_index_in_dim(lengths, own, 0, keepdims=False), length)
    pull = lax.dynamic_slice_in_dim(cotangent, own * length, length, 0).astype(jnp.float32) * live[:, None]

    def gathered(value):
        return lax.all_gather(lax.all_gather(value, "dp", axis=1, tiled=True), "section", axis=0, tiled=True)

    mats = gathered(mat_a.astype(low))
    scales = gathered(norms.astype(low)).astype(jnp.float32)
    downs = lax.all_gather(mat_b.astype(low), "section", axis=2, tiled=True)
    downs = lax.all_gather(downs, "dp", axis=1, tiled=True)
    output, input_grad, part_a, part_b, part_n = micro_step(
        rows, pull, segment, mats, downs, scales[:, :, 0], scales[:, :, 1]
    )

    def scattered(value, section_dim):
        value = lax.psum_scatter(value, "section", scatter_dimension=section_dim, tiled=True)
        return lax.psum_scatter(value, "dp", scatter_dimension=1, tiled=True).astype(jnp.float32)

    grad_a = scattered(part_a.astype(low), 0)
    grad_b = scattered(part_b.astype(low), 2)
    grad_n = scattered(part_n, 0)
    square = jnp.sum(grad_a * grad_a) + jnp.sum(grad_b * grad_b) + jnp.sum(grad_n * grad_n)
    grad_norm = jnp.sqrt(lax.psum(square, ("section", "dp")))
    return finish_step(
        grad_norm, output, input_grad,
        (mat_a, first_a, second_a, grad_a, MATRIX_RATE, MATRIX_DECAY),
        (mat_b, first_b, second_b, grad_b, MATRIX_RATE, MATRIX_DECAY),
        (norms, first_n, second_n, grad_n, NORM_RATE, 0.0),
    )


LOW = jnp.bfloat16
WIDE = jnp.float32
MESH = pl.DeviceIdType.MESH
SECTIONS = 4
LANES = 128
BLOCK = 64
ROWS_FIRST = (5,)
KERNEL_VMEM = 64 * 1024 * 1024 - 256 * 1024


def gradient_items(rows_a, rows_b, cols_b, width, hidden):
    part = rows_a // SECTIONS
    return (
        ("B1", 3, cols_b // 2, rows_b),
        ("F3", 3, part, hidden // 2),
        ("O2", 2, part, width // 2),
        ("K2", 2, part, 3 * width // 2),
        ("B0", 1, cols_b // 2, rows_b),
        ("F1", 1, part, hidden // 2),
        ("O0", 0, part, width // 2),
        ("K0", 0, part, 3 * width // 2),
    )


def item_scratch(name, chips, rows, columns):
    piece = (rows, columns)
    return (
        ("own" + name, (chips, SECTIONS, 2) + piece, LOW),
        ("farx" + name, (chips,) + piece, LOW),
        ("fary" + name, (chips,) + piece, LOW),
        ("nearx" + name, (2, chips) + piece, LOW),
        ("neary" + name, (2, chips) + piece, LOW),
        ("line" + name, (chips, 2) + piece, LOW),
        ("done" + name, (2,) + piece if name[0] == "B" else (SECTIONS, 2) + piece, WIDE if name[0] == "B" else LOW),
    )


def kernel_scratch(chips, rows_a, rows_b, cols_b, length, width, hidden):
    devices = 2 * chips
    items = gradient_items(rows_a, rows_b, cols_b, width, hidden)
    count = len(items)
    received = sum((item_scratch(name, chips, rows, columns) for name, _, rows, columns in items), ())
    return received + (
        ("fac_s", (32,), None),
        ("fac_r", (32,), None),
        ("px_s", (count, 3), None),
        ("px_r", (count, 3), None),
        ("py_s", (count, 3), None),
        ("py_r", (count, 3), None),
        ("line_s", (count, chips), None),
        ("line_r", (count, chips), None),
        ("done_s", (count,), None),
        ("done_r", (count, SECTIONS), None),
        ("wa", (4, chips, 2, SECTIONS, rows_a // SECTIONS, hidden), LOW),
        ("wb", (2, chips, 2, SECTIONS, rows_b, cols_b), LOW),
        ("in_a", (1, rows_a, hidden), WIDE),
        ("in_b", (2, rows_b, cols_b), WIDE),
        ("in_n", (1, 2, rows_a), WIDE),
        ("out_a", (rows_a, hidden), WIDE),
        ("out_b", (2, rows_b, cols_b), WIDE),
        ("out_n", (2, rows_a), WIDE),
        ("out_square", (8, LANES), WIDE),
        ("out_output", (length, width), LOW),
        ("out_input", (length, width), WIDE),
        ("cut", (SECTIONS, rows_a // SECTIONS, hidden), LOW),
        ("tiles", (devices, SECTIONS, 8, LANES), WIDE),
        ("x", (4, length, width), LOW),
        ("xt", (4, chips, 2, rows_a, length), LOW),
        ("xtc", (4, chips, rows_a, 2 * length), LOW),
        ("y", (length, width), LOW),
        ("cot", (length, width), LOW),
        ("bias", (length, length), WIDE),
        ("live", (length, 1), WIDE),
        ("f", (length, width), WIDE),
        ("n", (4, length, width), WIDE),
        ("inv", (4, length, 1), WIDE),
        ("q", (2, length, width), LOW),
        ("k", (2, length, width), LOW),
        ("v", (2, length, width), LOW),
        ("kt", (2, width, length), LOW),
        ("vt", (2, width, length), LOW),
        ("ot", (2, chips, 2, rows_a, length), LOW),
        ("otc", (2, chips, rows_a, 2 * length), LOW),
        ("pt", (2, HEADS, length, length), LOW),
        ("g", (2, length, hidden), LOW),
        ("gc", (2, chips, 2 * length, rows_b), LOW),
        ("slope", (2, length, hidden), LOW),
        ("gx", (length, width), WIDE),
        ("gy", (length, width), WIDE),
        ("df", (2, 2 * length, width), LOW),
        ("dft", (2, width, 2 * length), LOW),
        ("dm", (length, width), LOW),
        ("dqt", (width, length), LOW),
        ("dh", (2, 2 * length, hidden), LOW),
        ("dp", (2, 2 * length, 3 * width), LOW),
        ("ng", (devices, 8, width), WIDE),
        ("ns", (SECTIONS, 8, width), WIDE),
        ("sq", (devices, 8, LANES), WIDE),
        ("sqs", (SECTIONS, 8, LANES), WIDE),
        ("sum", (8, LANES), WIDE),
        ("in_s", (5,), None),
        ("out_s", (6,), None),
        ("cut_s", (1,), None),
        ("cut_r", (SECTIONS,), None),
        ("gz_s", (6,), None),
        ("gz_r", (6, chips), None),
        ("gx_s", (6,), None),
        ("gx_r", (6,), None),
        ("gy_s", (6,), None),
        ("gy_r", (6,), None),
        ("rx_s", (6,), None),
        ("rx_r", (6,), None),
        ("ry_s", (6,), None),
        ("ry_r", (6,), None),
        ("gs_s", (6,), None),
        ("gs_r", (6,), None),
        ("small_s", (3, 2), None),
        ("small_r", (3, 2), None),
    )


INPUTS = ("tokens", "cotangent", "lengths", "mat_a", "mat_b", "norms")
OUTPUTS = ("grad_a", "grad_b", "grad_n", "square", "output", "input_grad")


def step_kernel(names, *refs):
    r = types.SimpleNamespace(**dict(zip(names, refs)))
    length, width = r.x.shape[1:]
    hidden = r.wa.shape[-1]
    rows_a, (rows_b, cols_b) = r.mat_a.shape[1], r.mat_b.shape[1:]
    devices = r.tiles.shape[0]
    chips = devices // 2
    half_b = cols_b // 2
    grad_items = gradient_items(rows_a, rows_b, cols_b, width, hidden)
    head = width // HEADS
    scale = head**-0.5

    s, d = lax.axis_index("section"), lax.axis_index("dp")
    z, c = lax.div(d, 2), lax.rem(d, 2)
    sx = s + 1 - 2 * lax.rem(s, 2)
    sy = lax.rem(s + 2, SECTIONS)
    sd = SECTIONS - 1 - s
    to_sibling = {"dp": d + 1 - 2 * c}
    to_up, to_down = {"dp": d + 2}, {"dp": d - 2}
    to_x, to_y = {"section": sx}, {"section": sy}
    below, above = z > 0, z < chips - 1
    group = [{"dp": lax.rem(d + step, devices)} for step in range(1, devices)]
    plane = [{"section": lax.rem(s + step, SECTIONS)} for step in range(1, SECTIONS)]
    finish = []

    def when(condition, work):
        if condition is None:
            work()
        else:
            pl.when(condition)(work)

    def push(source, target, send_sem, recv_sem, device):
        pltpu.make_async_remote_copy(
            src_ref=source,
            dst_ref=target,
            send_sem=send_sem,
            recv_sem=recv_sem,
            device_id=device,
            device_id_type=MESH,
        ).start()

    def arrived(target, sem):
        pltpu.make_async_remote_copy(
            src_ref=target, dst_ref=target, send_sem=sem, recv_sem=sem, device_id=to_x, device_id_type=MESH
        ).wait_recv()

    def sent(source, sem):
        pltpu.make_async_remote_copy(
            src_ref=source, dst_ref=source, send_sem=sem, recv_sem=sem, device_id=to_x, device_id_type=MESH
        ).wait_send()

    def at_end(condition, source, sem):
        finish.append((condition, source, sem))

    def aligned(start, size):
        return pl.ds(pl.multiple_of(start, size), size)

    own_x = pltpu.make_async_copy(r.tokens.at[aligned(s * length, length)], r.x.at[0], r.in_s.at[0])
    own_cot = pltpu.make_async_copy(r.cotangent.at[aligned(s * length, length)], r.cot, r.in_s.at[1])
    own_a = pltpu.make_async_copy(r.mat_a, r.in_a, r.in_s.at[2])
    own_b = pltpu.make_async_copy(r.mat_b, r.in_b, r.in_s.at[3])
    own_n = pltpu.make_async_copy(r.norms, r.in_n, r.in_s.at[4])
    own_a.start()
    own_n.start()
    own_b.start()
    own_x.start()
    own_cot.start()
    barrier = pltpu.get_barrier_semaphore()
    for peer in group + plane:
        pl.semaphore_signal(barrier, inc=1, device_id=peer, device_id_type=MESH)
    own_a.wait()
    r.cut[...] = r.in_a[0].astype(LOW).reshape(SECTIONS, rows_a // SECTIONS, hidden)
    r.wa[s, z, c, s] = r.cut[s]
    own_n.wait()
    norms = r.in_n[0].astype(LOW).astype(WIDE)
    nothing = jnp.zeros((2, rows_a), WIDE)
    even = jnp.concatenate([norms, nothing], axis=1)
    odd = jnp.concatenate([nothing, norms], axis=1)
    r.tiles[d, s, 0:2, :] = jnp.where(c == 0, even, odd)
    r.tiles[d, s, 2:8, :] = jnp.zeros((6, LANES), WIDE)
    own_b.wait()
    for layer in range(2):
        r.wb[layer, z, c, s] = r.in_b[layer].astype(LOW)
    pl.semaphore_wait(barrier, len(group) + len(plane))

    def put_out(slot, source, target):
        made = pltpu.make_async_copy(source, target, r.out_s.at[slot])
        made.start()
        return made

    def small_out(which, source):
        for peer in group:
            push(source, source, r.small_s.at[which, 0], r.small_r.at[which, 0], peer)

    def small_group(which, like):
        arrived(like, r.small_r.at[which, 0])
        sent(like, r.small_s.at[which, 0])

    def small_plane_out(which, source):
        for peer in plane:
            push(source, source, r.small_s.at[which, 1], r.small_r.at[which, 1], peer)

    def small_plane(which, like):
        arrived(like, r.small_r.at[which, 1])
        sent(like, r.small_s.at[which, 1])

    every = slice(None)

    def block(item, chip, section):
        if item < 4:
            return r.wa.at[item, chip, c, section]
        return r.wb.at[item - 4, chip, c, section]

    def half_block(item, section, half):
        if item < 4:
            return r.wa.at[item, :, c, section, :, pl.ds(half * hidden // 2, hidden // 2)]
        rows = pl.ds(half * rows_b // 2, rows_b // 2)
        return r.wb.at[item - 4, :, c, section, rows]

    def half_piece(item, section, half):
        rows = pl.ds(half * rows_b // 2, rows_b // 2)
        return r.wb.at[item - 4, z, c, section, rows]

    def core_blocks(item, core):
        return r.wa.at[item, :, core] if item < 4 else r.wb.at[item - 4, :, core]

    def cut_out():
        for section, device in ((sd, {"section": sd}), (sx, to_x), (sy, to_y)):
            push(r.cut.at[section], r.wa.at[s, z, c, section], r.cut_s.at[0], r.cut_r.at[s], device)
        at_end(None, r.cut.at[pl.ds(0, SECTIONS - 1)], r.cut_s.at[0])

    def cut_in():
        for section in (sx, sy, sd):
            arrived(r.wa.at[section, z, c, s], r.cut_r.at[section])

    def line_out(item):
        if item in ROWS_FIRST:
            rows_out(item)
            return
        own = block(item, z, s)
        for step in range(1, chips):
            push(own, own, r.gz_s.at[item], r.gz_r.at[item, z], {"dp": 2 * lax.rem(z + step, chips) + c})
        several = block(item, pl.ds(0, chips - 1), s)
        at_end(None, several, r.gz_s.at[item])

    def plane_out(item, chip):
        own = block(item, chip, s)
        push(own, own, r.gx_s.at[item], r.gx_r.at[item], to_x)
        push(own, own, r.gy_s.at[item], r.gy_r.at[item], to_y)

    def rows_out(item):
        arrived(half_piece(item, sd, 0), r.rx_r.at[item])
        arrived(half_piece(item, sd, 1), r.ry_r.at[item])
        rows = r.wb.at[item - 4, z, c]
        for step in range(1, chips):
            push(rows, rows, r.gz_s.at[item], r.gz_r.at[item, z], {"dp": 2 * lax.rem(z + step, chips) + c})
        push(rows, rows, r.gs_s.at[item], r.gs_r.at[item], to_sibling)
        at_end(None, r.wb.at[item - 4, pl.ds(0, chips - 1), c], r.gz_s.at[item])

    def rows_in(item):
        for step in range(1, chips):
            chip = lax.rem(z + step, chips)
            rows = r.wb.at[item - 4, chip, c]
            arrived(rows, r.gz_r.at[item, chip])
            push(rows, rows, r.gs_s.at[item], r.gs_r.at[item], to_sibling)
        at_end(None, core_blocks(item, c), r.gs_s.at[item])

    def line_in(item):
        if item in ROWS_FIRST:
            rows_in(item)
            return
        for step in range(1, chips):
            chip = lax.rem(z + step, chips)
            arrived(block(item, chip, s), r.gz_r.at[item, chip])
            plane_out(item, chip)
        core_out(item, s)
        at_end(None, block(item, every, s), r.gx_s.at[item])
        at_end(None, block(item, every, s), r.gy_s.at[item])

    def core_out(item, section):
        blocks = block(item, every, section)
        push(blocks, blocks, r.gs_s.at[item], r.gs_r.at[item], to_sibling)

    def plane_in(item):
        over = z if item in ROWS_FIRST else every
        piece = half_piece if item in ROWS_FIRST else half_block
        arrived(block(item, over, sx), r.gx_r.at[item])
        part = piece(item, sx, 1)
        push(part, part, r.ry_s.at[item], r.ry_r.at[item], to_y)
        arrived(block(item, over, sy), r.gy_r.at[item])
        part = piece(item, sy, 0)
        push(part, part, r.rx_s.at[item], r.rx_r.at[item], to_x)
        if item in ROWS_FIRST:
            at_end(None, block(item, z, sx), r.gx_s.at[item])
            at_end(None, block(item, z, sx), r.gy_s.at[item])
        else:
            core_out(item, sx)
            core_out(item, sy)
        at_end(None, part, r.ry_s.at[item])
        at_end(None, part, r.rx_s.at[item])

    def far_in(item):
        arrived(half_block(item, sd, 0), r.rx_r.at[item])
        arrived(half_block(item, sd, 1), r.ry_r.at[item])
        core_out(item, sd)
        at_end(None, core_blocks(item, c), r.gs_s.at[item])

    def core_in(item):
        arrived(core_blocks(item, 1 - c), r.gs_r.at[item])

    mine, other = pl.ds(0, length), pl.ds(length, length)

    def give(slot, source, target):
        push(source, target, r.fac_s.at[slot], r.fac_r.at[slot], to_sibling)
        at_end(None, target, r.fac_s.at[slot])

    def taken(slot, target):
        arrived(target, r.fac_r.at[slot])

    def give_rows(layer):
        r.xt[layer] = r.x[layer].T.reshape(chips, 2, rows_a, length)
        r.xtc[layer, :, :, 0:length] = r.xt[layer, :, c]
        give(layer, r.xt.at[layer, :, 1 - c], r.xtc.at[layer, :, :, other])

    def product(left, right, dims):
        return lax.dot_general(left, right, (dims, ((), ())), preferred_element_type=WIDE)

    def loop(count, work):
        def one(index, carry):
            work(index)
            return carry

        lax.fori_loop(0, count, one, 0)

    def gain_row(layer, kind):
        parts = [
            r.tiles[2 * chip, layer, kind : kind + 1, :] + r.tiles[2 * chip + 1, layer, kind : kind + 1, :]
            for chip in range(chips)
        ]
        return jnp.concatenate(parts, axis=1)

    def stats(value):
        centre = value - jnp.mean(value, -1, keepdims=True)
        inverse = lax.rsqrt(jnp.mean(centre * centre, -1, keepdims=True) + EPSILON)
        return centre * inverse, inverse

    lane = lax.broadcasted_iota(jnp.int32, (1, 2 * head), 1)
    first_half = (lane < head).astype(WIDE)
    half_masks = (first_half.astype(LOW), (1.0 - first_half).astype(LOW))

    def prepare_masks():
        ends, total = [], jnp.int32(0)
        for slot in range(r.lengths.shape[1]):
            total = total + r.lengths[s, slot]
            ends.append(total)
        down_places = lax.broadcasted_iota(jnp.int32, (length, 1), 0)
        across_places = lax.broadcasted_iota(jnp.int32, (1, length), 1)
        down_segment = jnp.zeros((length, 1), jnp.int32)
        across_segment = jnp.zeros((1, length), jnp.int32)
        for end in ends:
            down_segment = down_segment + (end <= down_places).astype(jnp.int32)
            across_segment = across_segment + (end <= across_places).astype(jnp.int32)
        r.bias[...] = jnp.where(down_segment == across_segment, 0.0, NEGATIVE)
        r.live[...] = (down_places < total).astype(WIDE)

    def matrix(layer, place):
        value = r.wa[layer, :, :, :, :, place]
        return value.reshape(width, value.shape[-1])

    def down(at, chip=slice(None)):
        blocks = [r.wb[at, chip, :, section] for section in range(SECTIONS)]
        return jnp.concatenate([block.reshape(-1, cols_b) for block in blocks], axis=1)

    def attention_in(layer):
        at = layer // 2
        rows = r.x[layer]
        r.q[at] = product(rows, matrix(layer, pl.ds(0, width)), NN).astype(LOW) * jnp.asarray(scale, LOW)
        keys = product(rows, matrix(layer, pl.ds(width, width)), NN).astype(LOW)
        r.k[at] = keys
        values = product(rows, matrix(layer, pl.ds(2 * width, width)), NN).astype(LOW)
        r.v[at] = values
        r.vt[at] = values.T

    def attention_heads(layer, begin, count):
        at = layer // 2

        def pair(index):
            lanes = aligned(index * 2 * head, 2 * head)
            for which in range(2):
                scores = product(r.k[at, :, lanes], r.q[at, :, lanes] * half_masks[which], NT) + r.bias[...]
                weights = jnp.exp(scores - jnp.max(scores, 0, keepdims=True))
                probs = (weights * (1.0 / jnp.sum(weights, 0, keepdims=True))).astype(LOW)
                r.pt[at, 2 * index + which] = probs
                place = aligned((2 * index + which) * head, head)
                r.ot[at, index, which] = product(r.vt[at, place, :], probs, NN).astype(LOW)

        for index in range(begin, begin + count):
            pair(index)

    def attention_out(layer):
        at = layer // 2
        r.otc[at, :, :, 0:length] = r.ot[at, :, c]
        give(4 + at, r.ot.at[at, :, 1 - c], r.otc.at[at, :, :, other])
        r.f[...] = product(r.ot[at].reshape(width, length).T, matrix(layer, pl.ds(3 * width, width)), NN)

    def expand(layer, index):
        at = layer // 2
        place = pl.ds(index * width, width)
        pre = product(r.x[layer], matrix(layer, place), NN)
        squared = pre * pre
        slope = 0.7978845608 * (1.0 + 3 * 0.044715 * squared)
        bent = jnp.tanh(0.7978845608 * pre * (1.0 + 0.044715 * squared))
        r.g[at, :, place] = (0.5 * pre * (1.0 + bent)).astype(LOW)
        r.slope[at, :, place] = (0.5 * (1.0 + bent) + 0.5 * pre * (1.0 - bent * bent) * slope).astype(LOW)
        block = aligned((2 * index + c) * rows_b, rows_b)
        r.gc[at, index, 0:length, :] = r.g[at, :, block]
        block = aligned((2 * index + 1 - c) * rows_b, rows_b)
        give(6 + chips * at + index, r.g.at[at, :, block], r.gc.at[at, index, other, :])

    def contract(layer):
        r.f[...] = product(r.g[layer // 2], down(layer // 2), NN)

    def by_rows(work):
        for index in range(length // BLOCK):
            work(pl.ds(index * BLOCK, BLOCK))

    def normalize(layer):
        gain, offset = gain_row(layer, 0), gain_row(layer, 1)

        def some(rows):
            branch = r.f[rows, :]
            normal, inverse = stats(r.x[layer, rows, :].astype(WIDE) + branch)
            r.n[layer, rows, :] = normal
            r.inv[layer, rows, :] = inverse
            out = normal * gain + offset
            dual = branch if layer == 0 else r.y[rows, :].astype(WIDE) + branch
            if layer < 3:
                r.x[layer + 1, rows, :] = out.astype(LOW)
                r.y[rows, :] = dual.astype(LOW)
            else:
                dual_normal, dual_inverse = stats(dual)
                r.out_output[rows, :] = (out + dual_normal).astype(LOW)
                pull = r.cot[rows, :].astype(WIDE) * r.live[rows, :]
                r.gx[rows, :] = pull
                r.gy[rows, :] = norm_back(dual_normal, dual_inverse, pull)

        by_rows(some)

    def back_normalize(layer):
        gain = gain_row(layer, 0)

        def some(index, sums):
            rows = pl.ds(index * BLOCK, BLOCK)
            upstream = r.gx[rows, :]
            normal = r.n[layer, rows, :]
            summed = norm_back(normal, r.inv[layer, rows, :], upstream * gain)
            dual = r.gy[rows, :]
            r.gx[rows, :] = summed
            r.df[layer // 2, rows, :] = (summed + dual).astype(LOW)
            if layer == 3:
                r.gy[rows, :] = dual.astype(LOW).astype(WIDE)
            return (
                sums[0] + jnp.sum(upstream * normal, 0, keepdims=True),
                sums[1] + jnp.sum(upstream, 0, keepdims=True),
            )

        zero = jnp.zeros((1, width), WIDE)
        gains, offsets = zero, zero
        for index in range(length // BLOCK):
            gains, offsets = some(index, (gains, offsets))
        r.ng[d, 2 * layer : 2 * layer + 1, :] = gains
        r.ng[d, 2 * layer + 1 : 2 * layer + 2, :] = offsets

    def pass_down(layer, inner):
        total = r.gx[...] + inner
        if layer > 0:
            r.gx[...] = total.astype(LOW).astype(WIDE)
        else:
            r.out_input[...] = total

    base = 6 + 2 * chips

    def back_hidden(layer):
        at = layer // 2
        r.dft[at, :, 0:length] = r.df[at, 0:length, :].T
        give(base + at, r.dft.at[at, :, mine], r.dft.at[at, :, other])
        for index in range(hidden // width):
            place = pl.ds(index * width, width)
            pulled = product(r.df[at, 0:length, :], down(at, pl.ds(index, 1)), NT)
            r.dh[at, 0:length, place] = (pulled * r.slope[at, :, place].astype(WIDE)).astype(LOW)
            give(base + 2 + chips * at + index, r.dh.at[at, mine, place], r.dh.at[at, other, place])

    def back_expand_end(layer):
        pass_down(layer, product(r.dh[layer // 2, 0:length, :], matrix(layer, pl.ds(0, hidden)), NT))

    def back_output(layer):
        at = layer // 2
        give(base + 2 + 2 * chips + at, r.df.at[at, mine], r.df.at[at, other])
        r.dm[...] = product(r.df[at, 0:length, :], matrix(layer, pl.ds(3 * width, width)), NT).astype(LOW)
        r.kt[at] = (r.k[at] * jnp.asarray(scale, LOW)).T

    def back_heads(layer, begin, count):
        at = layer // 2

        def pair(index):
            lanes = aligned(index * 2 * head, 2 * head)
            pulled = r.dm[:, lanes]
            keys, values = [], []
            for which in range(2):
                probs = r.pt[at, 2 * index + which]
                grad = product(r.v[at, :, lanes], pulled * half_masks[which], NT)
                full = probs.astype(WIDE)
                centre = jnp.sum(full * grad, 0, keepdims=True)
                scores = (full * (grad - centre)).astype(LOW)
                keys.append(product(scores, r.q[at, :, lanes], NN))
                values.append(product(probs, pulled, NN))
                place = aligned((2 * index + which) * head, head)
                r.dqt[place, :] = product(r.kt[at, place, :], scores, NN).astype(LOW)
            r.dp[at, 0:length, aligned(width + index * 2 * head, 2 * head)] = jnp.where(
                lane < head, keys[0], keys[1]
            ).astype(LOW)
            r.dp[at, 0:length, aligned(2 * width + index * 2 * head, 2 * head)] = jnp.where(
                lane < head, values[0], values[1]
            ).astype(LOW)

        def pairs(step):
            pair(begin + 2 * step)
            pair(begin + 2 * step + 1)

        loop(count // 2, pairs)

    def back_packed(layer):
        at = layer // 2
        slot = base + 4 + 2 * chips + 2 * at
        place = pl.ds(width, 2 * width)
        give(slot, r.dp.at[at, mine, place], r.dp.at[at, other, place])
        r.dp[at, 0:length, 0:width] = r.dqt[...].T
        place = pl.ds(0, width)
        give(slot + 1, r.dp.at[at, mine, place], r.dp.at[at, other, place])

    def back_packed_end(layer):
        pass_down(layer, product(r.dp[layer // 2, 0:length, :], matrix(layer, pl.ds(0, 3 * width)), NT))

    def keep(name, half, place, value):
        own = getattr(r, "own" + name)
        own[:, :, half, :, place] = value.astype(LOW).reshape(chips, SECTIONS, rows_a // SECTIONS, value.shape[1])

    def chip_rows(value):
        return value.reshape(chips * rows_a, 2 * length)

    def grad_down(at):
        own = getattr(r, "ownB%d" % at)
        taken(base + at, r.dft.at[at, :, other])
        for chip in range(chips):
            taken(6 + chips * at + chip, r.gc.at[at, chip, other, :])
            value = product(r.dft[at], r.gc[at, chip], NN)
            own[chip] = value.astype(LOW).reshape(SECTIONS, 2, half_b, rows_b)

    def grad_up(layer):
        at = layer // 2
        taken(layer, r.xtc.at[layer, :, :, other])
        for index in range(hidden // width):
            place = pl.ds(index * width, width)
            taken(base + 2 + chips * at + index, r.dh.at[at, other, place])
            value = product(chip_rows(r.xtc[layer]), r.dh[at, :, place], NN)
            keep("F%d" % layer, index // 2, pl.ds(index % 2 * width, width), value)

    def grad_output(layer):
        at = layer // 2
        taken(4 + at, r.otc.at[at, :, :, other])
        taken(base + 2 + 2 * chips + at, r.df.at[at, other])
        for half in range(2):
            place = pl.ds(half * width // 2, width // 2)
            value = product(chip_rows(r.otc[at]), r.df[at, :, place], NN)
            keep("O%d" % layer, half, pl.ds(0, width // 2), value)

    def grad_packed(layer):
        at = layer // 2
        slot = base + 4 + 2 * chips + 2 * at
        taken(layer, r.xtc.at[layer, :, :, other])
        taken(slot, r.dp.at[at, other, pl.ds(width, 2 * width)])
        taken(slot + 1, r.dp.at[at, other, pl.ds(0, width)])
        part = 3 * width // 2
        for half in range(2):
            value = product(chip_rows(r.xtc[layer]), r.dp[at, :, half * part : (half + 1) * part], NN)
            keep("K%d" % layer, half, pl.ds(0, part), value)

    def joined(target, others):
        return functools.reduce(
            lambda left, right: left + right, [ref[...].astype(WIDE) for ref in (target, *others)]
        )

    def add_into(target, others):
        if len(others) == 1:
            target[...] = target[...] + others[0][...]
        else:
            target[...] = joined(target, others).astype(LOW)

    places = {name: place for place, (name, _, _, _) in enumerate(grad_items)}

    def buffers(name):
        parts = ("own", "farx", "fary", "nearx", "neary", "line", "done")
        return types.SimpleNamespace(**{part: getattr(r, part + name) for part in parts})

    def to_plane(name):
        item, place = buffers(name), places[name]

        def over_x(section, half, target, slot):
            push(item.own.at[:, section, half], target, r.px_s.at[place, slot], r.px_r.at[place, slot], to_x)
            at_end(None, item.farx, r.px_s.at[place, slot])

        def over_y(section, half, target, slot):
            push(item.own.at[:, section, half], target, r.py_s.at[place, slot], r.py_r.at[place, slot], to_y)
            at_end(None, item.farx, r.py_s.at[place, slot])

        over_x(sd, 0, item.farx, 2)
        over_y(sd, 1, item.fary, 2)
        over_x(sx, 0, item.nearx.at[0], 0)
        over_y(sy, 1, item.neary.at[1], 1)

    def through_plane(name):
        item, place = buffers(name), places[name]
        own = item.own
        arrived(item.fary, r.py_r.at[place, 2])
        add_into(own.at[:, sx, 1], [item.fary])
        push(own.at[:, sx, 1], item.nearx.at[1], r.px_s.at[place, 1], r.px_r.at[place, 1], to_x)
        at_end(None, item.farx, r.px_s.at[place, 1])
        arrived(item.farx, r.px_r.at[place, 2])
        add_into(own.at[:, sy, 0], [item.farx])
        push(own.at[:, sy, 0], item.neary.at[0], r.py_s.at[place, 0], r.py_r.at[place, 0], to_y)
        at_end(None, item.farx, r.py_s.at[place, 0])

    def to_line(name):
        item, place = buffers(name), places[name]
        own = item.own.at[:, s]
        for half in range(2):
            arrived(item.nearx.at[half], r.px_r.at[place, half])
            arrived(item.neary.at[half], r.py_r.at[place, half])
            add_into(own.at[:, half], [item.nearx.at[half], item.neary.at[half]])
        for step in range(1, chips):
            chip = lax.rem(z + step, chips)
            push(
                own.at[chip],
                item.line.at[z],
                r.line_s.at[place, step],
                r.line_r.at[place, z],
                {"dp": 2 * chip + c},
            )
            at_end(None, item.line.at[0], r.line_s.at[place, step])

    def to_owner(name):
        item, place = buffers(name), places[name]
        others = [lax.rem(z + step, chips) for step in range(1, chips)]
        for chip in others:
            arrived(item.line.at[chip], r.line_r.at[place, chip])
        total = joined(item.own.at[z, s], [item.line.at[chip] for chip in others])
        square = total * total
        while square.ndim > 2:
            square = jnp.sum(square, 0)
        square = jnp.sum(jnp.sum(square, 0, keepdims=True), 1, keepdims=True)
        r.sum[...] = r.sum[...] + jnp.broadcast_to(square, (8, LANES))
        if name[0] == "B":
            item.done[...] = total
            return
        item.done[s] = total.astype(LOW)
        layer = grad_items[place][1]
        mine = item.done.at[s]
        away = s != layer
        when(
            away,
            lambda: push(mine, mine, r.done_s.at[place], r.done_r.at[place, s], {"section": jnp.int32(layer)}),
        )
        at_end(away, mine, r.done_s.at[place])

    def collect(name):
        item, place = buffers(name), places[name]
        layer = grad_items[place][1]

        def work():
            for section in range(SECTIONS):
                if section != layer:
                    arrived(item.done.at[section], r.done_r.at[place, section])
            columns = item.done.shape[-1]
            start = 3 * width if name[0] == "O" else 0
            for section in range(SECTIONS):
                for half in range(2):
                    rows = pl.ds(section * (rows_a // SECTIONS), rows_a // SECTIONS)
                    place_to = pl.ds(start + half * columns, columns)
                    r.out_a[rows, place_to] = item.done[section, half].astype(WIDE)

        when(s == layer, work)

    def all_sent(count=None):
        for condition, source, sem in finish[:count]:
            when(condition, functools.partial(sent, source, sem))
        del finish[:count]

    cut_out()
    small_out(0, r.tiles.at[d, s])
    plane_out(5, z)
    line_out(4)
    plane_out(4, z)
    cut_in()
    plane_out(1, z)
    line_out(0)
    plane_out(0, z)
    line_out(1)
    line_out(2)
    plane_out(3, z)
    line_out(3)
    line_in(4)
    small_group(0, r.tiles.at[pl.ds(0, devices - 1), 0])
    for peer in plane:
        push(r.tiles.at[:, s], r.tiles.at[:, s], r.small_s.at[0, 1], r.small_r.at[0, 1], peer)
    line_in(0)
    plane_in(5)
    line_in(1)
    plane_in(0)
    plane_out(2, z)
    plane_in(1)
    far_in(0)
    line_in(2)
    plane_in(4)
    line_out(5)
    own_x.wait()
    own_cot.wait()
    prepare_masks()
    core_in(0)
    attention_in(0)
    far_in(1)
    attention_heads(0, 0, 2)
    attention_heads(0, 2, 2)
    plane_in(2)
    attention_out(0)
    small_plane(0, r.tiles.at[:, pl.ds(0, SECTIONS - 1)])
    normalize(0)
    far_in(4)
    core_in(1)
    line_in(3)
    expand(1, 0)
    expand(1, 1)
    early = len(finish)
    far_in(2)
    expand(1, 2)
    expand(1, 3)
    core_in(4)
    contract(1)
    normalize(1)
    core_in(2)
    plane_in(3)
    attention_in(2)
    attention_heads(2, 0, 2)
    attention_heads(2, 2, 2)
    far_in(3)
    attention_out(2)
    line_in(5)
    normalize(2)
    core_in(3)
    expand(3, 0)
    expand(3, 1)
    expand(3, 2)
    expand(3, 3)
    all_sent(early)
    core_in(5)
    contract(3)
    normalize(3)
    leaving = [put_out(0, r.out_output, r.output)]

    r.sum[...] = jnp.zeros((8, LANES), WIDE)
    back_normalize(3)
    back_hidden(3)
    give_rows(3)
    back_expand_end(3)
    back_normalize(2)
    grad_up(3)
    to_plane("F3")
    back_output(2)
    grad_down(1)
    to_plane("B1")
    back_heads(2, 0, 2)
    back_heads(2, 2, 2)
    back_packed(2)
    through_plane("B1")
    give_rows(2)
    grad_output(2)
    back_packed_end(2)
    give_rows(1)
    to_plane("O2")
    grad_packed(2)
    to_plane("K2")
    back_normalize(1)
    back_hidden(1)
    through_plane("K2")
    grad_down(0)
    to_plane("B0")
    back_expand_end(1)
    back_normalize(0)
    small_out(1, r.ng.at[d])
    to_line("K2")
    to_line("B1")
    back_output(0)
    grad_up(1)
    through_plane("B0")
    to_plane("F1")
    back_heads(0, 0, 2)
    back_heads(0, 2, 2)
    back_packed(0)
    to_line("B0")
    through_plane("O2")
    through_plane("F1")
    grad_output(0)
    to_plane("O0")
    give_rows(0)
    grad_packed(0)
    to_plane("K0")
    to_line("O2")
    to_line("F1")
    through_plane("O0")
    to_owner("B1")
    back_packed_end(0)
    leaving.append(put_out(1, r.out_input, r.input_grad))
    to_owner("B0")
    all_sent()
    through_plane("K0")
    small_group(1, r.ng.at[pl.ds(0, devices - 1)])
    r.ns[s] = functools.reduce(lambda left, right: left + right, [r.ng[index] for index in range(devices)])
    small_plane_out(1, r.ns.at[s])
    through_plane("F3")
    to_line("O0")
    to_line("K0")
    to_owner("F1")
    to_line("F3")
    to_owner("O2")
    to_owner("K2")
    to_owner("F3")
    to_owner("O0")
    to_owner("K0")

    r.sq[d] = r.sum[...]
    small_out(2, r.sq.at[d])
    for name in ("F1", "O2", "K2", "F3"):
        collect(name)
    collect("O0")
    for layer in range(2):
        done = buffers("B%d" % layer).done
        r.out_b[layer] = done[...].reshape(cols_b, rows_b).T
    leaving.append(put_out(2, r.out_b, r.grad_b))
    small_plane(1, r.ns.at[pl.ds(0, SECTIONS - 1)])
    grads = functools.reduce(lambda left, right: left + right, [r.ns[index] for index in range(SECTIONS)])
    norm_square = jnp.sum(jnp.sum(grads * grads, 0, keepdims=True), 1, keepdims=True)
    chosen = jnp.zeros((2, width), WIDE)
    for layer in range(4):
        chosen = jnp.where(s == layer, grads[2 * layer : 2 * layer + 2, :], chosen)
    shard = jnp.zeros((2, rows_a), WIDE)
    for chip in range(chips):
        pair_of = chosen[:, chip * LANES : (chip + 1) * LANES]
        shard = jnp.where(z == chip, jnp.where(c == 0, pair_of[:, :rows_a], pair_of[:, rows_a:]), shard)
    r.out_n[...] = shard
    leaving.append(put_out(3, r.out_n, r.grad_n))
    collect("K0")
    leaving.append(put_out(4, r.out_a, r.grad_a))
    small_group(2, r.sq.at[pl.ds(0, devices - 1)])
    r.sqs[s] = functools.reduce(lambda left, right: left + right, [r.sq[index] for index in range(devices)])
    small_plane_out(2, r.sqs.at[s])
    all_sent()
    small_plane(2, r.sqs.at[pl.ds(0, SECTIONS - 1)])
    squares = functools.reduce(lambda left, right: left + right, [r.sqs[index] for index in range(SECTIONS)])
    r.out_square[...] = squares + norm_square
    leaving.append(put_out(5, r.out_square, r.square))
    for made in leaving:
        made.wait()


def step_call(tokens, cotangent, lengths, mat_a, mat_b, norms):
    rows_a, hidden = mat_a.shape[1:]
    rows_b, cols_b = mat_b.shape[1:]
    width = tokens.shape[1]
    length = tokens.shape[0] // lengths.shape[0]
    chips = width // rows_a // 2
    scratch = kernel_scratch(chips, rows_a, rows_b, cols_b, length, width, hidden)
    shapes = []
    for _, shape, kind in scratch:
        shapes.append(pltpu.SemaphoreType.DMA(shape) if kind is None else pltpu.VMEM(shape, kind))
    anywhere = pl.BlockSpec(memory_space=pl.ANY)
    return pl.pallas_call(
        functools.partial(step_kernel, INPUTS + OUTPUTS + tuple(name for name, _, _ in scratch)),
        out_shape=(
            jax.ShapeDtypeStruct((rows_a, hidden), WIDE),
            jax.ShapeDtypeStruct(mat_b.shape, WIDE),
            jax.ShapeDtypeStruct((2, rows_a), WIDE),
            jax.ShapeDtypeStruct((8, LANES), WIDE),
            jax.ShapeDtypeStruct((length, width), LOW),
            jax.ShapeDtypeStruct((length, width), WIDE),
        ),
        in_specs=[anywhere, anywhere, pl.BlockSpec(memory_space=pltpu.SMEM), anywhere, anywhere, anywhere],
        out_specs=[anywhere] * len(OUTPUTS),
        scratch_shapes=shapes,
        compiler_params=pltpu.CompilerParams(
            collective_id=0, has_side_effects=True, vmem_limit_bytes=KERNEL_VMEM
        ),
    )(tokens, cotangent, lengths, mat_a, mat_b, norms)


def update_kernel(*refs):
    inputs, outputs, held, made, sems = refs[:15], refs[15:33], refs[33:48], refs[48:63], refs[63]
    started = []

    def copy(source, target):
        one = pltpu.make_async_copy(source, target, sems.at[len(started)])
        one.start()
        started.append(one)
        return one

    half = inputs[4].shape[1] // 2
    parts = [(0, pl.ds(0, half)), (0, pl.ds(half, half)), (1, slice(None)), (2, slice(None))]
    rates = ((MATRIX_RATE, MATRIX_DECAY), (MATRIX_RATE, MATRIX_DECAY), (NORM_RATE, 0.0))
    norm_in = copy(inputs[0], held[0])
    coming = []
    for group, rows in parts:
        coming.append(
            [copy(inputs[at].at[:, rows], held[at].at[:, rows]) for at in range(3 + 4 * group, 7 + 4 * group)]
        )
    passing = [copy(inputs[at], held[at]) for at in (1, 2)]
    norm_in.wait()
    grad_norm = jnp.sqrt(held[0][0:1, 0:1])
    factor = CLIP_NORM / jnp.maximum(grad_norm, CLIP_NORM)
    outputs[0][...] = grad_norm
    leaving = []
    for (group, rows), waits in zip(parts, coming):
        for one in waits:
            one.wait()
        grad, weight, one, two = (held[at][:, rows] for at in range(3 + 4 * group, 7 + 4 * group))
        clip = grad * factor
        moment, square, master = adam_update(weight, one, two, clip, *rates[group])
        for kind, value in enumerate((clip, moment, square, master, master.astype(LOW))):
            buffer = made[5 * group + kind]
            buffer[:, rows] = value
            leaving.append(copy(buffer.at[:, rows], outputs[3 + 5 * group + kind].at[:, rows]))
        if passing:
            at = 3 - len(passing)
            passing.pop(0).wait()
            leaving.append(copy(held[at], outputs[at].at[0]))
    for one in leaving:
        one.wait()


def kernel_body(
    tokens, cotangent, lengths, mat_a, mat_b, norms, first_a, second_a, first_b, second_b, first_n, second_n
):
    norms, first_n, second_n = (jnp.swapaxes(value, 1, 2) for value in (norms, first_n, second_n))
    grad_a, grad_b, grad_n, square, output, input_grad = step_call(
        tokens, cotangent, lengths, mat_a, mat_b, norms
    )
    args = (square, output, input_grad, grad_a[None], mat_a, first_a, second_a, grad_b, mat_b, first_b, second_b)
    args += (grad_n[None], norms, first_n, second_n)
    anywhere, vmem = pl.BlockSpec(memory_space=pl.ANY), pl.BlockSpec(memory_space=pltpu.VMEM)
    shapes = [jax.ShapeDtypeStruct((1, 1), WIDE)]
    shapes += [jax.ShapeDtypeStruct((1,) + value.shape, value.dtype) for value in (output, input_grad)]
    for value in (mat_a, mat_b, norms):
        shapes += [jax.ShapeDtypeStruct(value.shape, kind) for kind in (WIDE, WIDE, WIDE, WIDE, LOW)]
    scratch = [pltpu.VMEM(value.shape, value.dtype) for value in (*args, *shapes[3:])]
    results = pl.pallas_call(
        update_kernel,
        out_shape=shapes,
        in_specs=[anywhere] * len(args),
        out_specs=[vmem] + [anywhere] * (len(shapes) - 1),
        scratch_shapes=scratch + [pltpu.SemaphoreType.DMA((48,))],
        compiler_params=pltpu.CompilerParams(vmem_limit_bytes=KERNEL_VMEM),
    )(*args)
    results = [results[0][0, 0], *results[1:]]
    results[-5:] = [jnp.swapaxes(value, 1, 2) for value in results[-5:]]
    return tuple(results)


def chosen_body(*args):
    rows_a = args[3].shape[1]
    groups = lax.axis_size("dp")
    by_kernel = rows_a % 32 == 0 and 2 * rows_a == LANES and groups * rows_a == args[0].shape[1]
    return (kernel_body if by_kernel else body)(*args)


def solution(mesh):
    placed = (
        P("dp", None),
        P("dp", None),
        P("dp", None),
        P("section", "dp", None),
        P(None, "dp", "section"),
        P("section", "dp", None),
        P("section", "dp", None),
        P("section", "dp", None),
        P(None, "dp", "section"),
        P(None, "dp", "section"),
        P("section", "dp", None),
        P("section", "dp", None),
    )
    return jax.shard_map(
        chosen_body,
        mesh=mesh,
        in_specs=placed,
        out_specs=(
            P(),
            P("section", "dp", None),
            P("section", "dp", None),
            P("section", "dp", None),
            P("section", "dp", None),
            P("section", "dp", None),
            P("section", "dp", None),
            P("section", "dp", None),
            P(None, "dp", "section"),
            P(None, "dp", "section"),
            P(None, "dp", "section"),
            P(None, "dp", "section"),
            P(None, "dp", "section"),
            P("section", "dp", None),
            P("section", "dp", None),
            P("section", "dp", None),
            P("section", "dp", None),
            P("section", "dp", None),
        ),
        check_vma=False,
    )
```

```python
import functools
import types

import jax
import jax.numpy as jnp
from jax import lax
from jax.experimental import pallas as pl
from jax.experimental.pallas import tpu as pltpu
from jax.sharding import PartitionSpec as P

HEADS = 8
STEP = 5


EPSILON = 1e-05
NEGATIVE = -1e30
CLIP_NORM = 1.0
BETA_ONE = 0.5
BETA_TWO = 0.5
ADAM_EPSILON = 1e-08
MATRIX_RATE = 0.05
NORM_RATE = 0.5
MATRIX_DECAY = 0.01


def norm_stats(value):
    centre = value - jnp.mean(value, -1, keepdims=True)
    inverse = lax.rsqrt(jnp.mean(centre * centre, -1, keepdims=True) + EPSILON)
    return (centre * inverse, inverse)


def norm_back(normal, inverse, upstream):
    return inverse * (
        upstream
        - jnp.mean(upstream, -1, keepdims=True)
        - normal * jnp.mean(upstream * normal, -1, keepdims=True)
    )


def adam_update(weight, moment_one, moment_two, gradient, step_rate, decay_rate):
    first_new = BETA_ONE * moment_one + (1.0 - BETA_ONE) * gradient
    second_new = BETA_TWO * moment_two + (1.0 - BETA_TWO) * gradient * gradient
    first_hat = first_new / (1.0 - BETA_ONE**STEP)
    second_hat = second_new / (1.0 - BETA_TWO**STEP)
    weight_new = weight - step_rate * (
        first_hat / (jnp.sqrt(second_hat) + ADAM_EPSILON) + decay_rate * weight
    )
    return (first_new, second_new, weight_new)


def segments_of(lengths_row, length):
    ends = jnp.cumsum(lengths_row, dtype=jnp.int32)
    places = jnp.arange(length, dtype=jnp.int32)
    segment = jnp.sum((ends[None, :] <= places[:, None]).astype(jnp.int32), axis=1, dtype=jnp.int32)
    live = (places < ends[-1]).astype(jnp.float32)
    return segment, live


def matmul(left, right, dims):
    return lax.dot_general(left, right, (dims, ((), ())), preferred_element_type=jnp.float32)


NN = ((1,), (0,))
NT = ((1,), (1,))
TN = ((0,), (0,))


def attention_forward(stream, weight, mask):
    length, width = stream.shape
    size = width // HEADS
    packed = matmul(stream, weight[:, : 3 * width], NN).astype(jnp.bfloat16)
    heads = packed.reshape(length, 3, HEADS, size)
    scores = jnp.einsum("qhd,khd->hqk", heads[:, 0], heads[:, 1], preferred_element_type=jnp.float32)
    scores = jnp.where(mask[None], scores * size**-0.5, NEGATIVE)
    weights = jnp.exp(scores - jnp.max(scores, -1, keepdims=True))
    probs = weights / jnp.sum(weights, -1, keepdims=True)
    mixed = jnp.einsum("hqk,khd->qhd", probs.astype(jnp.bfloat16), heads[:, 2], preferred_element_type=jnp.float32)
    mixed = mixed.reshape(length, width).astype(jnp.bfloat16)
    branch = matmul(mixed, weight[:, 3 * width :], NN)
    return branch, (heads, probs, mixed)


def attention_backward(stream, weight, kept, grad_low):
    heads, probs, mixed = kept
    length, width = stream.shape
    size = width // HEADS
    grad_out = matmul(mixed, grad_low, TN)
    grad_mixed = matmul(grad_low, weight[:, 3 * width :], NT).astype(jnp.bfloat16)
    grad_mixed = grad_mixed.reshape(length, HEADS, size)
    grad_probs = jnp.einsum("qhd,khd->hqk", grad_mixed, heads[:, 2], preferred_element_type=jnp.float32)
    centre = jnp.sum(probs * grad_probs, -1, keepdims=True)
    grad_scores = (probs * (grad_probs - centre)).astype(jnp.bfloat16)
    low = probs.astype(jnp.bfloat16)
    scale = size**-0.5
    grad_q = jnp.einsum("hqk,khd->qhd", grad_scores, heads[:, 1], preferred_element_type=jnp.float32) * scale
    grad_k = jnp.einsum("hqk,qhd->khd", grad_scores, heads[:, 0], preferred_element_type=jnp.float32) * scale
    grad_v = jnp.einsum("hqk,qhd->khd", low, grad_mixed, preferred_element_type=jnp.float32)
    packed = jnp.concatenate([grad_q, grad_k, grad_v], axis=1).reshape(length, 3 * width)
    packed = packed.astype(jnp.bfloat16)
    grad_in = matmul(stream, packed, TN)
    grad_inputs = matmul(packed, weight[:, : 3 * width], NT)
    return grad_inputs, jnp.concatenate([grad_in, grad_out], axis=1)


def feed_forward(stream, weight, down):
    pre = matmul(stream, weight, NN)
    active = jax.nn.gelu(pre, approximate=True).astype(jnp.bfloat16)
    return matmul(active, down, NN), (pre, active)


def feed_backward(stream, weight, down, kept, grad_low):
    pre, active = kept
    grad_down = matmul(active, grad_low, TN)
    grad_active = matmul(grad_low, down, NT)
    pull = jax.vjp(lambda value: jax.nn.gelu(value, approximate=True), pre)[1]
    grad_pre = pull(grad_active)[0].astype(jnp.bfloat16)
    grad_up = matmul(stream, grad_pre, TN)
    return matmul(grad_pre, weight, NT), grad_up, grad_down


def micro_step(rows, pull, segment, mats, downs, gains, biases):
    low = jnp.bfloat16
    mask = segment[:, None] == segment[None, :]
    stream, dual = rows, jnp.zeros_like(rows)
    saved = []
    for sub in range(4):
        if sub % 2 == 0:
            branch, kept = attention_forward(stream, mats[sub], mask)
        else:
            branch, kept = feed_forward(stream, mats[sub], downs[sub // 2])
        normal, inverse = norm_stats(stream.astype(jnp.float32) + branch)
        out = normal * gains[sub] + biases[sub]
        total = dual.astype(jnp.float32) + branch
        saved.append((stream, kept, normal, inverse))
        if sub < 3:
            stream, dual = out.astype(low), total.astype(low)
    dual_normal, dual_inverse = norm_stats(total)
    output = (out + dual_normal).astype(low)
    grad_out, grad_dual = pull, norm_back(dual_normal, dual_inverse, pull)
    grads_a, grads_b, grads_n = [None] * 4, [None] * 2, [None] * 4
    for sub in (3, 2, 1, 0):
        stream, kept, normal, inverse = saved[sub]
        grads_n[sub] = jnp.stack([jnp.sum(grad_out * normal, 0), jnp.sum(grad_out, 0)], axis=1)
        summed = norm_back(normal, inverse, grad_out * gains[sub])
        branch_low = (summed + grad_dual).astype(low)
        if sub % 2 == 0:
            inner, grads_a[sub] = attention_backward(stream, mats[sub], kept, branch_low)
        else:
            inner, grads_a[sub], grads_b[sub // 2] = feed_backward(
                stream, mats[sub], downs[sub // 2], kept, branch_low
            )
        grad_in = summed + inner
        if sub > 0:
            grad_out = grad_in.astype(low).astype(jnp.float32)
            grad_dual = grad_dual.astype(low).astype(jnp.float32)
    return output, grad_in, jnp.stack(grads_a), jnp.stack(grads_b), jnp.stack(grads_n)


def finish_step(grad_norm, output, input_grad, *groups):
    factor = CLIP_NORM / jnp.maximum(grad_norm, CLIP_NORM)
    results = [grad_norm, output[None], input_grad[None]]
    for weight, one, two, grad, rate, decay in groups:
        clip = grad * factor
        moment, square_new, master = adam_update(weight, one, two, clip, rate, decay)
        results += [clip, moment, square_new, master, master.astype(jnp.bfloat16)]
    return tuple(results)


def body(
    tokens, cotangent, lengths, mat_a, mat_b, norms, first_a, second_a, first_b, second_b, first_n, second_n
):
    low = jnp.bfloat16
    own = lax.axis_index("section")
    length = tokens.shape[0] // lengths.shape[0]
    rows = lax.dynamic_slice_in_dim(tokens, own * length, length, 0)
    segment, live = segments_of(lax.dynamic_index_in_dim(lengths, own, 0, keepdims=False), length)
    pull = lax.dynamic_slice_in_dim(cotangent, own * length, length, 0).astype(jnp.float32) * live[:, None]

    def gathered(value):
        return lax.all_gather(lax.all_gather(value, "dp", axis=1, tiled=True), "section", axis=0, tiled=True)

    mats = gathered(mat_a.astype(low))
    scales = gathered(norms.astype(low)).astype(jnp.float32)
    downs = lax.all_gather(mat_b.astype(low), "section", axis=2, tiled=True)
    downs = lax.all_gather(downs, "dp", axis=1, tiled=True)
    output, input_grad, part_a, part_b, part_n = micro_step(
        rows, pull, segment, mats, downs, scales[:, :, 0], scales[:, :, 1]
    )

    def scattered(value, section_dim):
        value = lax.psum_scatter(value, "section", scatter_dimension=section_dim, tiled=True)
        return lax.psum_scatter(value, "dp", scatter_dimension=1, tiled=True).astype(jnp.float32)

    grad_a = scattered(part_a.astype(low), 0)
    grad_b = scattered(part_b.astype(low), 2)
    grad_n = scattered(part_n, 0)
    square = jnp.sum(grad_a * grad_a) + jnp.sum(grad_b * grad_b) + jnp.sum(grad_n * grad_n)
    grad_norm = jnp.sqrt(lax.psum(square, ("section", "dp")))
    return finish_step(
        grad_norm, output, input_grad,
        (mat_a, first_a, second_a, grad_a, MATRIX_RATE, MATRIX_DECAY),
        (mat_b, first_b, second_b, grad_b, MATRIX_RATE, MATRIX_DECAY),
        (norms, first_n, second_n, grad_n, NORM_RATE, 0.0),
    )


LOW = jnp.bfloat16
WIDE = jnp.float32
MESH = pl.DeviceIdType.MESH
SECTIONS = 4
LANES = 128
BLOCK = 64
ROWS_FIRST = (4, 5)
KERNEL_VMEM = 64 * 1024 * 1024 - 256 * 1024


def gradient_items(rows_a, rows_b, cols_b, width, hidden):
    part = rows_a // SECTIONS
    return (
        ("B1", 3, cols_b // 2, rows_b),
        ("F3", 3, part, hidden // 2),
        ("O2", 2, part, width // 2),
        ("K2", 2, part, 3 * width // 2),
        ("B0", 1, cols_b // 2, rows_b),
        ("F1", 1, part, hidden // 2),
        ("O0", 0, part, width // 2),
        ("K0", 0, part, 3 * width // 2),
    )


def item_scratch(name, chips, rows, columns):
    piece = (rows, columns)
    return (
        ("own" + name, (chips, SECTIONS, 2) + piece, LOW),
        ("farx" + name, (chips,) + piece, LOW),
        ("fary" + name, (chips,) + piece, LOW),
        ("nearx" + name, (2, chips) + piece, LOW),
        ("neary" + name, (2, chips) + piece, LOW),
        ("line" + name, (chips, 2) + piece, LOW),
        ("done" + name, (2,) + piece if name[0] == "B" else (SECTIONS, 2) + piece, WIDE if name[0] == "B" else LOW),
    )


def kernel_scratch(chips, rows_a, rows_b, cols_b, length, width, hidden):
    devices = 2 * chips
    items = gradient_items(rows_a, rows_b, cols_b, width, hidden)
    count = len(items)
    received = sum((item_scratch(name, chips, rows, columns) for name, _, rows, columns in items), ())
    return received + (
        ("fac_s", (32,), None),
        ("fac_r", (32,), None),
        ("px_s", (count, 3), None),
        ("px_r", (count, 3), None),
        ("py_s", (count, 3), None),
        ("py_r", (count, 3), None),
        ("line_s", (count, chips), None),
        ("line_r", (count, chips), None),
        ("done_s", (count,), None),
        ("done_r", (count, SECTIONS), None),
        ("wa", (4, chips, 2, SECTIONS, rows_a // SECTIONS, hidden), LOW),
        ("wb", (2, chips, 2, SECTIONS, rows_b, cols_b), LOW),
        ("in_a", (1, rows_a, hidden), WIDE),
        ("in_b", (2, rows_b, cols_b), WIDE),
        ("in_n", (1, 2, rows_a), WIDE),
        ("out_a", (rows_a, hidden), WIDE),
        ("out_b", (2, rows_b, cols_b), WIDE),
        ("out_n", (2, rows_a), WIDE),
        ("out_square", (8, LANES), WIDE),
        ("out_output", (length, width), LOW),
        ("out_input", (length, width), WIDE),
        ("cut", (SECTIONS, rows_a // SECTIONS, hidden), LOW),
        ("tiles", (devices, SECTIONS, 8, LANES), WIDE),
        ("x", (4, length, width), LOW),
        ("xt", (4, chips, 2, rows_a, length), LOW),
        ("xtc", (4, chips, rows_a, 2 * length), LOW),
        ("y", (length, width), LOW),
        ("cot", (length, width), LOW),
        ("bias", (length, length), WIDE),
        ("live", (length, 1), WIDE),
        ("f", (length, width), WIDE),
        ("n", (4, length, width), WIDE),
        ("inv", (4, length, 1), WIDE),
        ("q", (2, length, width), LOW),
        ("k", (2, length, width), LOW),
        ("v", (2, length, width), LOW),
        ("kt", (2, width, length), LOW),
        ("vt", (2, width, length), LOW),
        ("ot", (2, chips, 2, rows_a, length), LOW),
        ("otc", (2, chips, rows_a, 2 * length), LOW),
        ("pt", (2, HEADS, length, length), LOW),
        ("g", (2, length, hidden), LOW),
        ("gc", (2, chips, 2 * length, rows_b), LOW),
        ("slope", (2, length, hidden), LOW),
        ("gx", (length, width), WIDE),
        ("gy", (length, width), WIDE),
        ("df", (2, 2 * length, width), LOW),
        ("dft", (2, width, 2 * length), LOW),
        ("dm", (length, width), LOW),
        ("dqt", (width, length), LOW),
        ("dh", (2, 2 * length, hidden), LOW),
        ("dp", (2, 2 * length, 3 * width), LOW),
        ("ng", (devices, 8, width), WIDE),
        ("ns", (SECTIONS, 8, width), WIDE),
        ("sq", (devices, 8, LANES), WIDE),
        ("sqs", (SECTIONS, 8, LANES), WIDE),
        ("sum", (8, LANES), WIDE),
        ("in_s", (5,), None),
        ("out_s", (6,), None),
        ("cut_s", (1,), None),
        ("cut_r", (SECTIONS,), None),
        ("qz_s", (2, 2, chips, 2), None),
        ("qz_r", (2, chips, 2), None),
        ("gz_s", (6,), None),
        ("gz_r", (6, chips), None),
        ("gx_s", (6,), None),
        ("gx_r", (6,), None),
        ("gy_s", (6,), None),
        ("gy_r", (6,), None),
        ("rx_s", (6,), None),
        ("rx_r", (6,), None),
        ("ry_s", (6,), None),
        ("ry_r", (6,), None),
        ("gs_s", (6,), None),
        ("gs_r", (6,), None),
        ("small_s", (3, 2), None),
        ("small_r", (3, 2), None),
    )


INPUTS = ("tokens", "cotangent", "lengths", "mat_a", "mat_b", "norms")
OUTPUTS = ("grad_a", "grad_b", "grad_n", "square", "output", "input_grad")


def step_kernel(names, *refs):
    r = types.SimpleNamespace(**dict(zip(names, refs)))
    length, width = r.x.shape[1:]
    hidden = r.wa.shape[-1]
    rows_a, (rows_b, cols_b) = r.mat_a.shape[1], r.mat_b.shape[1:]
    devices = r.tiles.shape[0]
    chips = devices // 2
    half_b = cols_b // 2
    grad_items = gradient_items(rows_a, rows_b, cols_b, width, hidden)
    head = width // HEADS
    scale = head**-0.5

    s, d = lax.axis_index("section"), lax.axis_index("dp")
    z, c = lax.div(d, 2), lax.rem(d, 2)
    sx = s + 1 - 2 * lax.rem(s, 2)
    sy = lax.rem(s + 2, SECTIONS)
    sd = SECTIONS - 1 - s
    to_sibling = {"dp": d + 1 - 2 * c}
    to_up, to_down = {"dp": d + 2}, {"dp": d - 2}
    to_x, to_y = {"section": sx}, {"section": sy}
    below, above = z > 0, z < chips - 1
    group = [{"dp": lax.rem(d + step, devices)} for step in range(1, devices)]
    plane = [{"section": lax.rem(s + step, SECTIONS)} for step in range(1, SECTIONS)]
    finish = []

    def when(condition, work):
        if condition is None:
            work()
        else:
            pl.when(condition)(work)

    def push(source, target, send_sem, recv_sem, device):
        pltpu.make_async_remote_copy(
            src_ref=source,
            dst_ref=target,
            send_sem=send_sem,
            recv_sem=recv_sem,
            device_id=device,
            device_id_type=MESH,
        ).start()

    def arrived(target, sem):
        pltpu.make_async_remote_copy(
            src_ref=target, dst_ref=target, send_sem=sem, recv_sem=sem, device_id=to_x, device_id_type=MESH
        ).wait_recv()

    def sent(source, sem):
        pltpu.make_async_remote_copy(
            src_ref=source, dst_ref=source, send_sem=sem, recv_sem=sem, device_id=to_x, device_id_type=MESH
        ).wait_send()

    def at_end(condition, source, sem):
        finish.append((condition, source, sem))

    def aligned(start, size):
        return pl.ds(pl.multiple_of(start, size), size)

    own_x = pltpu.make_async_copy(r.tokens.at[aligned(s * length, length)], r.x.at[0], r.in_s.at[0])
    own_cot = pltpu.make_async_copy(r.cotangent.at[aligned(s * length, length)], r.cot, r.in_s.at[1])
    own_a = pltpu.make_async_copy(r.mat_a, r.in_a, r.in_s.at[2])
    own_b = pltpu.make_async_copy(r.mat_b, r.in_b, r.in_s.at[3])
    own_n = pltpu.make_async_copy(r.norms, r.in_n, r.in_s.at[4])
    own_a.start()
    own_n.start()
    own_b.start()
    own_x.start()
    own_cot.start()
    barrier = pltpu.get_barrier_semaphore()
    for peer in group + plane:
        pl.semaphore_signal(barrier, inc=1, device_id=peer, device_id_type=MESH)
    own_a.wait()
    r.cut[...] = r.in_a[0].astype(LOW).reshape(SECTIONS, rows_a // SECTIONS, hidden)
    r.wa[s, z, c, s] = r.cut[s]
    own_n.wait()
    norms = r.in_n[0].astype(LOW).astype(WIDE)
    nothing = jnp.zeros((2, rows_a), WIDE)
    even = jnp.concatenate([norms, nothing], axis=1)
    odd = jnp.concatenate([nothing, norms], axis=1)
    r.tiles[d, s, 0:2, :] = jnp.where(c == 0, even, odd)
    r.tiles[d, s, 2:8, :] = jnp.zeros((6, LANES), WIDE)
    own_b.wait()
    for layer in range(2):
        r.wb[layer, z, c, s] = r.in_b[layer].astype(LOW)
    pl.semaphore_wait(barrier, len(group) + len(plane))

    def put_out(slot, source, target):
        made = pltpu.make_async_copy(source, target, r.out_s.at[slot])
        made.start()
        return made

    def small_out(which, source):
        for peer in group:
            push(source, source, r.small_s.at[which, 0], r.small_r.at[which, 0], peer)

    def small_group(which, like):
        arrived(like, r.small_r.at[which, 0])
        sent(like, r.small_s.at[which, 0])

    def small_plane_out(which, source):
        for peer in plane:
            push(source, source, r.small_s.at[which, 1], r.small_r.at[which, 1], peer)

    def small_plane(which, like):
        arrived(like, r.small_r.at[which, 1])
        sent(like, r.small_s.at[which, 1])

    every = slice(None)

    def block(item, chip, section):
        if item < 4:
            return r.wa.at[item, chip, c, section]
        return r.wb.at[item - 4, chip, c, section]

    def half_block(item, section, half):
        if item < 4:
            return r.wa.at[item, :, c, section, :, pl.ds(half * hidden // 2, hidden // 2)]
        rows = pl.ds(half * rows_b // 2, rows_b // 2)
        return r.wb.at[item - 4, :, c, section, rows]

    def half_piece(item, section, half):
        rows = pl.ds(half * rows_b // 2, rows_b // 2)
        return r.wb.at[item - 4, z, c, section, rows]

    def core_blocks(item, core):
        return r.wa.at[item, :, core] if item < 4 else r.wb.at[item - 4, :, core]

    def cut_out():
        for section, device in ((sd, {"section": sd}), (sx, to_x), (sy, to_y)):
            push(r.cut.at[section], r.wa.at[s, z, c, section], r.cut_s.at[0], r.cut_r.at[s], device)
        at_end(None, r.cut.at[pl.ds(0, SECTIONS - 1)], r.cut_s.at[0])

    def cut_in():
        for section in (sx, sy, sd):
            arrived(r.wa.at[section, z, c, s], r.cut_r.at[section])

    def line_out(item):
        if item in ROWS_FIRST:
            rows_out(item)
            return
        own = block(item, z, s)

        def to_chip(chip):
            push(own, own, r.gz_s.at[item], r.gz_r.at[item, z], {"dp": 2 * chip + c})

        for step in range(1, chips):
            when(z >= step, functools.partial(to_chip, z - step))
            when(z + step < chips, functools.partial(to_chip, z + step))
        several = block(item, pl.ds(0, chips - 1), s)
        at_end(None, several, r.gz_s.at[item])

    def plane_out(item, chip):
        own = block(item, chip, s)
        push(own, own, r.gx_s.at[item], r.gx_r.at[item], to_x)
        push(own, own, r.gy_s.at[item], r.gy_r.at[item], to_y)

    def row_half(item, chip, half):
        return r.wb.at[item - 4, chip, c, :, pl.ds(half * rows_b // 2, rows_b // 2)]

    def rows_on(item, chip, half, way):
        rows = row_half(item, chip, half)
        when(
            below if way else above,
            lambda: push(
                rows, rows, r.qz_s.at[item - 4, way, chip, half], r.qz_r.at[item - 4, chip, half], to_down if way else to_up
            ),
        )

    def rows_out(item):
        for half, sem in ((0, r.rx_r), (1, r.ry_r)):
            arrived(half_piece(item, sd, half), sem.at[item])
            for way in range(2):
                rows_on(item, z, half, way)
        rows = r.wb.at[item - 4, z, c]
        push(rows, rows, r.gs_s.at[item], r.gs_r.at[item], to_sibling)
        for chip in range(chips):
            for half in range(2):
                at_end(above & (z >= chip), row_half(item, 0, half), r.qz_s.at[item - 4, 0, chip, half])
                at_end(below & (z <= chip), row_half(item, 0, half), r.qz_s.at[item - 4, 1, chip, half])

    def rows_step(item, step):
        def take(chip, way):
            for half in range(2):
                arrived(row_half(item, chip, half), r.qz_r.at[item - 4, chip, half])
                rows_on(item, chip, half, way)
            rows = r.wb.at[item - 4, chip, c]
            push(rows, rows, r.gs_s.at[item], r.gs_r.at[item], to_sibling)

        when(z >= step, lambda: take(z - step, 0))
        when(z + step < chips, lambda: take(z + step, 1))
        if step == chips - 1:
            at_end(None, core_blocks(item, c), r.gs_s.at[item])

    def line_in(item):
        for step in range(1, chips):
            chip = lax.rem(z + step, chips)
            arrived(block(item, chip, s), r.gz_r.at[item, chip])
            plane_out(item, chip)
        core_out(item, s)
        at_end(None, block(item, every, s), r.gx_s.at[item])
        at_end(None, block(item, every, s), r.gy_s.at[item])

    def core_out(item, section):
        blocks = block(item, every, section)
        push(blocks, blocks, r.gs_s.at[item], r.gs_r.at[item], to_sibling)

    def plane_in(item):
        over = z if item in ROWS_FIRST else every
        piece = half_piece if item in ROWS_FIRST else half_block
        arrived(block(item, over, sx), r.gx_r.at[item])
        part = piece(item, sx, 1)
        push(part, part, r.ry_s.at[item], r.ry_r.at[item], to_y)
        arrived(block(item, over, sy), r.gy_r.at[item])
        part = piece(item, sy, 0)
        push(part, part, r.rx_s.at[item], r.rx_r.at[item], to_x)
        if item in ROWS_FIRST:
            at_end(None, block(item, z, sx), r.gx_s.at[item])
            at_end(None, block(item, z, sx), r.gy_s.at[item])
        else:
            core_out(item, sx)
            core_out(item, sy)
        at_end(None, part, r.ry_s.at[item])
        at_end(None, part, r.rx_s.at[item])

    def far_in(item):
        arrived(half_block(item, sd, 0), r.rx_r.at[item])
        arrived(half_block(item, sd, 1), r.ry_r.at[item])
        core_out(item, sd)
        at_end(None, core_blocks(item, c), r.gs_s.at[item])

    def core_in(item):
        arrived(core_blocks(item, 1 - c), r.gs_r.at[item])

    mine, other = pl.ds(0, length), pl.ds(length, length)

    def give(slot, source, target):
        push(source, target, r.fac_s.at[slot], r.fac_r.at[slot], to_sibling)
        at_end(None, target, r.fac_s.at[slot])

    def taken(slot, target):
        arrived(target, r.fac_r.at[slot])

    def give_rows(layer):
        r.xt[layer] = r.x[layer].T.reshape(chips, 2, rows_a, length)
        r.xtc[layer, :, :, 0:length] = r.xt[layer, :, c]
        give(layer, r.xt.at[layer, :, 1 - c], r.xtc.at[layer, :, :, other])

    def product(left, right, dims):
        return lax.dot_general(left, right, (dims, ((), ())), preferred_element_type=WIDE)

    def loop(count, work):
        def one(index, carry):
            work(index)
            return carry

        lax.fori_loop(0, count, one, 0)

    def gain_row(layer, kind):
        parts = [
            r.tiles[2 * chip, layer, kind : kind + 1, :] + r.tiles[2 * chip + 1, layer, kind : kind + 1, :]
            for chip in range(chips)
        ]
        return jnp.concatenate(parts, axis=1)

    def stats(value):
        centre = value - jnp.mean(value, -1, keepdims=True)
        inverse = lax.rsqrt(jnp.mean(centre * centre, -1, keepdims=True) + EPSILON)
        return centre * inverse, inverse

    lane = lax.broadcasted_iota(jnp.int32, (1, 2 * head), 1)
    first_half = (lane < head).astype(WIDE)
    half_masks = (first_half.astype(LOW), (1.0 - first_half).astype(LOW))

    def prepare_masks():
        ends, total = [], jnp.int32(0)
        for slot in range(r.lengths.shape[1]):
            total = total + r.lengths[s, slot]
            ends.append(total)
        down_places = lax.broadcasted_iota(jnp.int32, (length, 1), 0)
        across_places = lax.broadcasted_iota(jnp.int32, (1, length), 1)
        down_segment = jnp.zeros((length, 1), jnp.int32)
        across_segment = jnp.zeros((1, length), jnp.int32)
        for end in ends:
            down_segment = down_segment + (end <= down_places).astype(jnp.int32)
            across_segment = across_segment + (end <= across_places).astype(jnp.int32)
        r.bias[...] = jnp.where(down_segment == across_segment, 0.0, NEGATIVE)
        r.live[...] = (down_places < total).astype(WIDE)

    def matrix(layer, place):
        value = r.wa[layer, :, :, :, :, place]
        return value.reshape(width, value.shape[-1])

    def down(at, chip=slice(None)):
        blocks = [r.wb[at, chip, :, section] for section in range(SECTIONS)]
        return jnp.concatenate([block.reshape(-1, cols_b) for block in blocks], axis=1)

    def attention_in(layer):
        at = layer // 2
        rows = r.x[layer]
        r.q[at] = product(rows, matrix(layer, pl.ds(0, width)), NN).astype(LOW) * jnp.asarray(scale, LOW)
        keys = product(rows, matrix(layer, pl.ds(width, width)), NN).astype(LOW)
        r.k[at] = keys
        values = product(rows, matrix(layer, pl.ds(2 * width, width)), NN).astype(LOW)
        r.v[at] = values
        r.vt[at] = values.T

    def attention_heads(layer, begin, count):
        at = layer // 2

        def pair(index):
            lanes = aligned(index * 2 * head, 2 * head)
            for which in range(2):
                scores = product(r.k[at, :, lanes], r.q[at, :, lanes] * half_masks[which], NT) + r.bias[...]
                weights = jnp.exp(scores - jnp.max(scores, 0, keepdims=True))
                probs = (weights * (1.0 / jnp.sum(weights, 0, keepdims=True))).astype(LOW)
                r.pt[at, 2 * index + which] = probs
                place = aligned((2 * index + which) * head, head)
                r.ot[at, index, which] = product(r.vt[at, place, :], probs, NN).astype(LOW)

        for index in range(begin, begin + count):
            pair(index)

    def attention_out(layer):
        at = layer // 2
        r.otc[at, :, :, 0:length] = r.ot[at, :, c]
        give(4 + at, r.ot.at[at, :, 1 - c], r.otc.at[at, :, :, other])
        r.f[...] = product(r.ot[at].reshape(width, length).T, matrix(layer, pl.ds(3 * width, width)), NN)

    def expand(layer, index):
        at = layer // 2
        place = pl.ds(index * width, width)
        pre = product(r.x[layer], matrix(layer, place), NN)
        squared = pre * pre
        slope = 0.7978845608 * (1.0 + 3 * 0.044715 * squared)
        bent = jnp.tanh(0.7978845608 * pre * (1.0 + 0.044715 * squared))
        r.g[at, :, place] = (0.5 * pre * (1.0 + bent)).astype(LOW)
        r.slope[at, :, place] = (0.5 * (1.0 + bent) + 0.5 * pre * (1.0 - bent * bent) * slope).astype(LOW)
        block = aligned((2 * index + c) * rows_b, rows_b)
        r.gc[at, index, 0:length, :] = r.g[at, :, block]
        block = aligned((2 * index + 1 - c) * rows_b, rows_b)
        give(6 + chips * at + index, r.g.at[at, :, block], r.gc.at[at, index, other, :])

    def contract(layer):
        r.f[...] = product(r.g[layer // 2], down(layer // 2), NN)

    def by_rows(work):
        for index in range(length // BLOCK):
            work(pl.ds(index * BLOCK, BLOCK))

    def normalize(layer):
        gain, offset = gain_row(layer, 0), gain_row(layer, 1)

        def some(rows):
            branch = r.f[rows, :]
            normal, inverse = stats(r.x[layer, rows, :].astype(WIDE) + branch)
            r.n[layer, rows, :] = normal
            r.inv[layer, rows, :] = inverse
            out = normal * gain + offset
            dual = branch if layer == 0 else r.y[rows, :].astype(WIDE) + branch
            if layer < 3:
                r.x[layer + 1, rows, :] = out.astype(LOW)
                r.y[rows, :] = dual.astype(LOW)
            else:
                dual_normal, dual_inverse = stats(dual)
                r.out_output[rows, :] = (out + dual_normal).astype(LOW)
                pull = r.cot[rows, :].astype(WIDE) * r.live[rows, :]
                r.gx[rows, :] = pull
                r.gy[rows, :] = norm_back(dual_normal, dual_inverse, pull)

        by_rows(some)

    def back_normalize(layer):
        gain = gain_row(layer, 0)

        def some(index, sums):
            rows = pl.ds(index * BLOCK, BLOCK)
            upstream = r.gx[rows, :]
            normal = r.n[layer, rows, :]
            summed = norm_back(normal, r.inv[layer, rows, :], upstream * gain)
            dual = r.gy[rows, :]
            r.gx[rows, :] = summed
            r.df[layer // 2, rows, :] = (summed + dual).astype(LOW)
            if layer == 3:
                r.gy[rows, :] = dual.astype(LOW).astype(WIDE)
            return (
                sums[0] + jnp.sum(upstream * normal, 0, keepdims=True),
                sums[1] + jnp.sum(upstream, 0, keepdims=True),
            )

        zero = jnp.zeros((1, width), WIDE)
        gains, offsets = zero, zero
        for index in range(length // BLOCK):
            gains, offsets = some(index, (gains, offsets))
        r.ng[d, 2 * layer : 2 * layer + 1, :] = gains
        r.ng[d, 2 * layer + 1 : 2 * layer + 2, :] = offsets

    def pass_down(layer, inner):
        total = r.gx[...] + inner
        if layer > 0:
            r.gx[...] = total.astype(LOW).astype(WIDE)
        else:
            r.out_input[...] = total

    base = 6 + 2 * chips

    def back_hidden(layer):
        at = layer // 2
        r.dft[at, :, 0:length] = r.df[at, 0:length, :].T
        give(base + at, r.dft.at[at, :, mine], r.dft.at[at, :, other])
        for index in range(hidden // width):
            place = pl.ds(index * width, width)
            pulled = product(r.df[at, 0:length, :], down(at, pl.ds(index, 1)), NT)
            r.dh[at, 0:length, place] = (pulled * r.slope[at, :, place].astype(WIDE)).astype(LOW)
            give(base + 2 + chips * at + index, r.dh.at[at, mine, place], r.dh.at[at, other, place])

    def back_expand_end(layer):
        pass_down(layer, product(r.dh[layer // 2, 0:length, :], matrix(layer, pl.ds(0, hidden)), NT))

    def back_output(layer):
        at = layer // 2
        give(base + 2 + 2 * chips + at, r.df.at[at, mine], r.df.at[at, other])
        r.dm[...] = product(r.df[at, 0:length, :], matrix(layer, pl.ds(3 * width, width)), NT).astype(LOW)
        r.kt[at] = (r.k[at] * jnp.asarray(scale, LOW)).T

    def back_heads(layer, begin, count):
        at = layer // 2

        def pair(index):
            lanes = aligned(index * 2 * head, 2 * head)
            pulled = r.dm[:, lanes]
            keys, values = [], []
            for which in range(2):
                probs = r.pt[at, 2 * index + which]
                grad = product(r.v[at, :, lanes], pulled * half_masks[which], NT)
                full = probs.astype(WIDE)
                centre = jnp.sum(full * grad, 0, keepdims=True)
                scores = (full * (grad - centre)).astype(LOW)
                keys.append(product(scores, r.q[at, :, lanes], NN))
                values.append(product(probs, pulled, NN))
                place = aligned((2 * index + which) * head, head)
                r.dqt[place, :] = product(r.kt[at, place, :], scores, NN).astype(LOW)
            r.dp[at, 0:length, aligned(width + index * 2 * head, 2 * head)] = jnp.where(
                lane < head, keys[0], keys[1]
            ).astype(LOW)
            r.dp[at, 0:length, aligned(2 * width + index * 2 * head, 2 * head)] = jnp.where(
                lane < head, values[0], values[1]
            ).astype(LOW)

        def pairs(step):
            pair(begin + 2 * step)
            pair(begin + 2 * step + 1)

        loop(count // 2, pairs)

    def back_packed(layer):
        at = layer // 2
        slot = base + 4 + 2 * chips + 2 * at
        place = pl.ds(width, 2 * width)
        give(slot, r.dp.at[at, mine, place], r.dp.at[at, other, place])
        r.dp[at, 0:length, 0:width] = r.dqt[...].T
        place = pl.ds(0, width)
        give(slot + 1, r.dp.at[at, mine, place], r.dp.at[at, other, place])

    def back_packed_end(layer):
        pass_down(layer, product(r.dp[layer // 2, 0:length, :], matrix(layer, pl.ds(0, 3 * width)), NT))

    def keep(name, half, place, value):
        own = getattr(r, "own" + name)
        own[:, :, half, :, place] = value.astype(LOW).reshape(chips, SECTIONS, rows_a // SECTIONS, value.shape[1])

    def chip_rows(value):
        return value.reshape(chips * rows_a, 2 * length)

    def grad_down(at):
        own = getattr(r, "ownB%d" % at)
        taken(base + at, r.dft.at[at, :, other])
        for chip in range(chips):
            taken(6 + chips * at + chip, r.gc.at[at, chip, other, :])
            value = product(r.dft[at], r.gc[at, chip], NN)
            own[chip] = value.astype(LOW).reshape(SECTIONS, 2, half_b, rows_b)

    def grad_up(layer):
        at = layer // 2
        taken(layer, r.xtc.at[layer, :, :, other])
        for index in range(hidden // width):
            place = pl.ds(index * width, width)
            taken(base + 2 + chips * at + index, r.dh.at[at, other, place])
            value = product(chip_rows(r.xtc[layer]), r.dh[at, :, place], NN)
            keep("F%d" % layer, index // 2, pl.ds(index % 2 * width, width), value)

    def grad_output(layer):
        at = layer // 2
        taken(4 + at, r.otc.at[at, :, :, other])
        taken(base + 2 + 2 * chips + at, r.df.at[at, other])
        for half in range(2):
            place = pl.ds(half * width // 2, width // 2)
            value = product(chip_rows(r.otc[at]), r.df[at, :, place], NN)
            keep("O%d" % layer, half, pl.ds(0, width // 2), value)

    def grad_packed(layer):
        at = layer // 2
        slot = base + 4 + 2 * chips + 2 * at
        taken(layer, r.xtc.at[layer, :, :, other])
        taken(slot, r.dp.at[at, other, pl.ds(width, 2 * width)])
        taken(slot + 1, r.dp.at[at, other, pl.ds(0, width)])
        part = 3 * width // 2
        for half in range(2):
            value = product(chip_rows(r.xtc[layer]), r.dp[at, :, half * part : (half + 1) * part], NN)
            keep("K%d" % layer, half, pl.ds(0, part), value)

    def joined(target, others):
        return functools.reduce(
            lambda left, right: left + right, [ref[...].astype(WIDE) for ref in (target, *others)]
        )

    def add_into(target, others):
        if len(others) == 1:
            target[...] = target[...] + others[0][...]
        else:
            target[...] = joined(target, others).astype(LOW)

    places = {name: place for place, (name, _, _, _) in enumerate(grad_items)}

    def buffers(name):
        parts = ("own", "farx", "fary", "nearx", "neary", "line", "done")
        return types.SimpleNamespace(**{part: getattr(r, part + name) for part in parts})

    def to_plane(name):
        item, place = buffers(name), places[name]

        def over_x(section, half, target, slot):
            push(item.own.at[:, section, half], target, r.px_s.at[place, slot], r.px_r.at[place, slot], to_x)
            at_end(None, item.farx, r.px_s.at[place, slot])

        def over_y(section, half, target, slot):
            push(item.own.at[:, section, half], target, r.py_s.at[place, slot], r.py_r.at[place, slot], to_y)
            at_end(None, item.farx, r.py_s.at[place, slot])

        over_x(sd, 0, item.farx, 2)
        over_y(sd, 1, item.fary, 2)
        over_x(sx, 0, item.nearx.at[0], 0)
        over_y(sy, 1, item.neary.at[1], 1)

    def through_plane(name):
        item, place = buffers(name), places[name]
        own = item.own
        arrived(item.fary, r.py_r.at[place, 2])
        add_into(own.at[:, sx, 1], [item.fary])
        push(own.at[:, sx, 1], item.nearx.at[1], r.px_s.at[place, 1], r.px_r.at[place, 1], to_x)
        at_end(None, item.farx, r.px_s.at[place, 1])
        arrived(item.farx, r.px_r.at[place, 2])
        add_into(own.at[:, sy, 0], [item.farx])
        push(own.at[:, sy, 0], item.neary.at[0], r.py_s.at[place, 0], r.py_r.at[place, 0], to_y)
        at_end(None, item.farx, r.py_s.at[place, 0])

    def to_line(name):
        item, place = buffers(name), places[name]
        own = item.own.at[:, s]
        for half in range(2):
            arrived(item.nearx.at[half], r.px_r.at[place, half])
            arrived(item.neary.at[half], r.py_r.at[place, half])
            add_into(own.at[:, half], [item.nearx.at[half], item.neary.at[half]])
        for step in range(1, chips):
            chip = lax.rem(z + step, chips)
            push(
                own.at[chip],
                item.line.at[z],
                r.line_s.at[place, step],
                r.line_r.at[place, z],
                {"dp": 2 * chip + c},
            )
            at_end(None, item.line.at[0], r.line_s.at[place, step])

    def to_owner(name):
        item, place = buffers(name), places[name]
        others = [lax.rem(z + step, chips) for step in range(1, chips)]
        for chip in others:
            arrived(item.line.at[chip], r.line_r.at[place, chip])
        total = joined(item.own.at[z, s], [item.line.at[chip] for chip in others])
        square = total * total
        while square.ndim > 2:
            square = jnp.sum(square, 0)
        square = jnp.sum(jnp.sum(square, 0, keepdims=True), 1, keepdims=True)
        r.sum[...] = r.sum[...] + jnp.broadcast_to(square, (8, LANES))
        if name[0] == "B":
            item.done[...] = total
            return
        item.done[s] = total.astype(LOW)
        layer = grad_items[place][1]
        mine = item.done.at[s]
        away = s != layer
        when(
            away,
            lambda: push(mine, mine, r.done_s.at[place], r.done_r.at[place, s], {"section": jnp.int32(layer)}),
        )
        at_end(away, mine, r.done_s.at[place])

    def collect(name):
        item, place = buffers(name), places[name]
        layer = grad_items[place][1]

        def work():
            for section in range(SECTIONS):
                if section != layer:
                    arrived(item.done.at[section], r.done_r.at[place, section])
            columns = item.done.shape[-1]
            start = 3 * width if name[0] == "O" else 0
            for section in range(SECTIONS):
                for half in range(2):
                    rows = pl.ds(section * (rows_a // SECTIONS), rows_a // SECTIONS)
                    place_to = pl.ds(start + half * columns, columns)
                    r.out_a[rows, place_to] = item.done[section, half].astype(WIDE)

        when(s == layer, work)

    def all_sent(count=None):
        for condition, source, sem in finish[:count]:
            when(condition, functools.partial(sent, source, sem))
        del finish[:count]

    cut_out()
    small_out(0, r.tiles.at[d, s])
    plane_out(5, z)
    plane_out(4, z)
    cut_in()
    line_out(0)
    plane_out(2, z)
    plane_in(4)
    plane_out(0, z)
    plane_out(1, z)
    line_out(4)
    line_out(1)
    plane_in(5)
    line_in(0)
    small_group(0, r.tiles.at[pl.ds(0, devices - 1), 0])
    for peer in plane:
        push(r.tiles.at[:, s], r.tiles.at[:, s], r.small_s.at[0, 1], r.small_r.at[0, 1], peer)
    plane_out(3, z)
    plane_in(0)
    line_out(2)
    line_in(1)
    rows_step(4, 1)
    far_in(0)
    line_in(2)
    own_x.wait()
    own_cot.wait()
    prepare_masks()
    core_in(0)
    line_out(3)
    attention_in(0)
    plane_in(1)
    attention_heads(0, 0, 2)
    plane_in(2)
    attention_heads(0, 2, 2)
    attention_out(0)
    rows_step(4, 2)
    small_plane(0, r.tiles.at[:, pl.ds(0, SECTIONS - 1)])
    normalize(0)
    far_in(1)
    line_in(3)
    line_out(5)
    core_in(1)
    expand(1, 0)
    expand(1, 1)
    early = len(finish)
    far_in(2)
    expand(1, 2)
    expand(1, 3)
    rows_step(4, 3)
    core_in(4)
    contract(1)
    plane_in(3)
    rows_step(5, 1)
    normalize(1)
    core_in(2)
    attention_in(2)
    attention_heads(2, 0, 2)
    far_in(3)
    attention_heads(2, 2, 2)
    rows_step(5, 2)
    attention_out(2)
    normalize(2)
    core_in(3)
    expand(3, 0)
    expand(3, 1)
    rows_step(5, 3)
    expand(3, 2)
    expand(3, 3)
    all_sent(early)
    core_in(5)
    contract(3)
    normalize(3)
    leaving = [put_out(0, r.out_output, r.output)]

    r.sum[...] = jnp.zeros((8, LANES), WIDE)
    back_normalize(3)
    back_hidden(3)
    give_rows(3)
    back_expand_end(3)
    back_normalize(2)
    grad_up(3)
    to_plane("F3")
    back_output(2)
    grad_down(1)
    to_plane("B1")
    back_heads(2, 0, 2)
    back_heads(2, 2, 2)
    back_packed(2)
    through_plane("B1")
    give_rows(2)
    grad_output(2)
    back_packed_end(2)
    give_rows(1)
    to_plane("O2")
    grad_packed(2)
    to_plane("K2")
    back_normalize(1)
    back_hidden(1)
    through_plane("K2")
    grad_down(0)
    to_plane("B0")
    back_expand_end(1)
    back_normalize(0)
    small_out(1, r.ng.at[d])
    to_line("K2")
    to_line("B1")
    back_output(0)
    grad_up(1)
    through_plane("B0")
    to_plane("F1")
    back_heads(0, 0, 2)
    back_heads(0, 2, 2)
    back_packed(0)
    to_line("B0")
    through_plane("O2")
    through_plane("F1")
    grad_output(0)
    to_plane("O0")
    give_rows(0)
    grad_packed(0)
    to_plane("K0")
    to_line("O2")
    to_line("F1")
    through_plane("O0")
    to_owner("B1")
    back_packed_end(0)
    leaving.append(put_out(1, r.out_input, r.input_grad))
    to_owner("B0")
    all_sent()
    through_plane("K0")
    small_group(1, r.ng.at[pl.ds(0, devices - 1)])
    r.ns[s] = functools.reduce(lambda left, right: left + right, [r.ng[index] for index in range(devices)])
    small_plane_out(1, r.ns.at[s])
    through_plane("F3")
    to_line("O0")
    to_line("K0")
    to_owner("F1")
    to_line("F3")
    to_owner("O2")
    to_owner("K2")
    to_owner("F3")
    to_owner("O0")
    to_owner("K0")

    r.sq[d] = r.sum[...]
    small_out(2, r.sq.at[d])
    for name in ("F1", "O2", "K2", "F3"):
        collect(name)
    collect("O0")
    for layer in range(2):
        done = buffers("B%d" % layer).done
        r.out_b[layer] = done[...].reshape(cols_b, rows_b).T
    leaving.append(put_out(2, r.out_b, r.grad_b))
    small_plane(1, r.ns.at[pl.ds(0, SECTIONS - 1)])
    grads = functools.reduce(lambda left, right: left + right, [r.ns[index] for index in range(SECTIONS)])
    norm_square = jnp.sum(jnp.sum(grads * grads, 0, keepdims=True), 1, keepdims=True)
    chosen = jnp.zeros((2, width), WIDE)
    for layer in range(4):
        chosen = jnp.where(s == layer, grads[2 * layer : 2 * layer + 2, :], chosen)
    shard = jnp.zeros((2, rows_a), WIDE)
    for chip in range(chips):
        pair_of = chosen[:, chip * LANES : (chip + 1) * LANES]
        shard = jnp.where(z == chip, jnp.where(c == 0, pair_of[:, :rows_a], pair_of[:, rows_a:]), shard)
    r.out_n[...] = shard
    leaving.append(put_out(3, r.out_n, r.grad_n))
    collect("K0")
    leaving.append(put_out(4, r.out_a, r.grad_a))
    small_group(2, r.sq.at[pl.ds(0, devices - 1)])
    r.sqs[s] = functools.reduce(lambda left, right: left + right, [r.sq[index] for index in range(devices)])
    small_plane_out(2, r.sqs.at[s])
    all_sent()
    small_plane(2, r.sqs.at[pl.ds(0, SECTIONS - 1)])
    squares = functools.reduce(lambda left, right: left + right, [r.sqs[index] for index in range(SECTIONS)])
    r.out_square[...] = squares + norm_square
    leaving.append(put_out(5, r.out_square, r.square))
    for made in leaving:
        made.wait()


def step_call(tokens, cotangent, lengths, mat_a, mat_b, norms):
    rows_a, hidden = mat_a.shape[1:]
    rows_b, cols_b = mat_b.shape[1:]
    width = tokens.shape[1]
    length = tokens.shape[0] // lengths.shape[0]
    chips = width // rows_a // 2
    scratch = kernel_scratch(chips, rows_a, rows_b, cols_b, length, width, hidden)
    shapes = []
    for _, shape, kind in scratch:
        shapes.append(pltpu.SemaphoreType.DMA(shape) if kind is None else pltpu.VMEM(shape, kind))
    anywhere = pl.BlockSpec(memory_space=pl.ANY)
    return pl.pallas_call(
        functools.partial(step_kernel, INPUTS + OUTPUTS + tuple(name for name, _, _ in scratch)),
        out_shape=(
            jax.ShapeDtypeStruct((rows_a, hidden), WIDE),
            jax.ShapeDtypeStruct(mat_b.shape, WIDE),
            jax.ShapeDtypeStruct((2, rows_a), WIDE),
            jax.ShapeDtypeStruct((8, LANES), WIDE),
            jax.ShapeDtypeStruct((length, width), LOW),
            jax.ShapeDtypeStruct((length, width), WIDE),
        ),
        in_specs=[anywhere, anywhere, pl.BlockSpec(memory_space=pltpu.SMEM), anywhere, anywhere, anywhere],
        out_specs=[anywhere] * len(OUTPUTS),
        scratch_shapes=shapes,
        compiler_params=pltpu.CompilerParams(
            collective_id=0, has_side_effects=True, vmem_limit_bytes=KERNEL_VMEM
        ),
    )(tokens, cotangent, lengths, mat_a, mat_b, norms)


def update_kernel(*refs):
    inputs, outputs, held, made, sems = refs[:15], refs[15:33], refs[33:48], refs[48:63], refs[63]
    started = []

    def copy(source, target):
        one = pltpu.make_async_copy(source, target, sems.at[len(started)])
        one.start()
        started.append(one)
        return one

    half = inputs[4].shape[1] // 2
    parts = [(0, pl.ds(0, half)), (0, pl.ds(half, half)), (1, slice(None)), (2, slice(None))]
    rates = ((MATRIX_RATE, MATRIX_DECAY), (MATRIX_RATE, MATRIX_DECAY), (NORM_RATE, 0.0))
    norm_in = copy(inputs[0], held[0])
    coming = []
    for group, rows in parts:
        coming.append(
            [copy(inputs[at].at[:, rows], held[at].at[:, rows]) for at in range(3 + 4 * group, 7 + 4 * group)]
        )
    passing = [copy(inputs[at], held[at]) for at in (1, 2)]
    norm_in.wait()
    grad_norm = jnp.sqrt(held[0][0:1, 0:1])
    factor = CLIP_NORM / jnp.maximum(grad_norm, CLIP_NORM)
    outputs[0][...] = grad_norm
    leaving = []
    for (group, rows), waits in zip(parts, coming):
        for one in waits:
            one.wait()
        grad, weight, one, two = (held[at][:, rows] for at in range(3 + 4 * group, 7 + 4 * group))
        clip = grad * factor
        moment, square, master = adam_update(weight, one, two, clip, *rates[group])
        for kind, value in enumerate((clip, moment, square, master, master.astype(LOW))):
            buffer = made[5 * group + kind]
            buffer[:, rows] = value
            leaving.append(copy(buffer.at[:, rows], outputs[3 + 5 * group + kind].at[:, rows]))
        if passing:
            at = 3 - len(passing)
            passing.pop(0).wait()
            leaving.append(copy(held[at], outputs[at].at[0]))
    for one in leaving:
        one.wait()


def kernel_body(
    tokens, cotangent, lengths, mat_a, mat_b, norms, first_a, second_a, first_b, second_b, first_n, second_n
):
    norms, first_n, second_n = (jnp.swapaxes(value, 1, 2) for value in (norms, first_n, second_n))
    grad_a, grad_b, grad_n, square, output, input_grad = step_call(
        tokens, cotangent, lengths, mat_a, mat_b, norms
    )
    args = (square, output, input_grad, grad_a[None], mat_a, first_a, second_a, grad_b, mat_b, first_b, second_b)
    args += (grad_n[None], norms, first_n, second_n)
    anywhere, vmem = pl.BlockSpec(memory_space=pl.ANY), pl.BlockSpec(memory_space=pltpu.VMEM)
    shapes = [jax.ShapeDtypeStruct((1, 1), WIDE)]
    shapes += [jax.ShapeDtypeStruct((1,) + value.shape, value.dtype) for value in (output, input_grad)]
    for value in (mat_a, mat_b, norms):
        shapes += [jax.ShapeDtypeStruct(value.shape, kind) for kind in (WIDE, WIDE, WIDE, WIDE, LOW)]
    scratch = [pltpu.VMEM(value.shape, value.dtype) for value in (*args, *shapes[3:])]
    results = pl.pallas_call(
        update_kernel,
        out_shape=shapes,
        in_specs=[anywhere] * len(args),
        out_specs=[vmem] + [anywhere] * (len(shapes) - 1),
        scratch_shapes=scratch + [pltpu.SemaphoreType.DMA((48,))],
        compiler_params=pltpu.CompilerParams(vmem_limit_bytes=KERNEL_VMEM),
    )(*args)
    results = [results[0][0, 0], *results[1:]]
    results[-5:] = [jnp.swapaxes(value, 1, 2) for value in results[-5:]]
    return tuple(results)


def chosen_body(*args):
    rows_a = args[3].shape[1]
    groups = lax.axis_size("dp")
    by_kernel = rows_a % 32 == 0 and 2 * rows_a == LANES and groups * rows_a == args[0].shape[1]
    return (kernel_body if by_kernel else body)(*args)


def solution(mesh):
    placed = (
        P("dp", None),
        P("dp", None),
        P("dp", None),
        P("section", "dp", None),
        P(None, "dp", "section"),
        P("section", "dp", None),
        P("section", "dp", None),
        P("section", "dp", None),
        P(None, "dp", "section"),
        P(None, "dp", "section"),
        P("section", "dp", None),
        P("section", "dp", None),
    )
    return jax.shard_map(
        chosen_body,
        mesh=mesh,
        in_specs=placed,
        out_specs=(
            P(),
            P("section", "dp", None),
            P("section", "dp", None),
            P("section", "dp", None),
            P("section", "dp", None),
            P("section", "dp", None),
            P("section", "dp", None),
            P("section", "dp", None),
            P(None, "dp", "section"),
            P(None, "dp", "section"),
            P(None, "dp", "section"),
            P(None, "dp", "section"),
            P(None, "dp", "section"),
            P("section", "dp", None),
            P("section", "dp", None),
            P("section", "dp", None),
            P("section", "dp", None),
            P("section", "dp", None),
        ),
        check_vma=False,
    )
```

```python
import functools
import types

import jax
import jax.numpy as jnp
from jax import lax
from jax.experimental import pallas as pl
from jax.experimental.pallas import tpu as pltpu
from jax.sharding import PartitionSpec as P

HEADS = 8
STEP = 5


EPSILON = 1e-05
NEGATIVE = -1e30
CLIP_NORM = 1.0
BETA_ONE = 0.5
BETA_TWO = 0.5
ADAM_EPSILON = 1e-08
MATRIX_RATE = 0.05
NORM_RATE = 0.5
MATRIX_DECAY = 0.01


def norm_stats(value):
    centre = value - jnp.mean(value, -1, keepdims=True)
    inverse = lax.rsqrt(jnp.mean(centre * centre, -1, keepdims=True) + EPSILON)
    return (centre * inverse, inverse)


def norm_back(normal, inverse, upstream):
    return inverse * (
        upstream
        - jnp.mean(upstream, -1, keepdims=True)
        - normal * jnp.mean(upstream * normal, -1, keepdims=True)
    )


def adam_update(weight, moment_one, moment_two, gradient, step_rate, decay_rate):
    first_new = BETA_ONE * moment_one + (1.0 - BETA_ONE) * gradient
    second_new = BETA_TWO * moment_two + (1.0 - BETA_TWO) * gradient * gradient
    first_hat = first_new / (1.0 - BETA_ONE**STEP)
    second_hat = second_new / (1.0 - BETA_TWO**STEP)
    weight_new = weight - step_rate * (
        first_hat / (jnp.sqrt(second_hat) + ADAM_EPSILON) + decay_rate * weight
    )
    return (first_new, second_new, weight_new)


def segments_of(lengths_row, length):
    ends = jnp.cumsum(lengths_row, dtype=jnp.int32)
    places = jnp.arange(length, dtype=jnp.int32)
    segment = jnp.sum((ends[None, :] <= places[:, None]).astype(jnp.int32), axis=1, dtype=jnp.int32)
    live = (places < ends[-1]).astype(jnp.float32)
    return segment, live


def matmul(left, right, dims):
    return lax.dot_general(left, right, (dims, ((), ())), preferred_element_type=jnp.float32)


NN = ((1,), (0,))
NT = ((1,), (1,))
TN = ((0,), (0,))


def attention_forward(stream, weight, mask):
    length, width = stream.shape
    size = width // HEADS
    packed = matmul(stream, weight[:, : 3 * width], NN).astype(jnp.bfloat16)
    heads = packed.reshape(length, 3, HEADS, size)
    scores = jnp.einsum("qhd,khd->hqk", heads[:, 0], heads[:, 1], preferred_element_type=jnp.float32)
    scores = jnp.where(mask[None], scores * size**-0.5, NEGATIVE)
    weights = jnp.exp(scores - jnp.max(scores, -1, keepdims=True))
    probs = weights / jnp.sum(weights, -1, keepdims=True)
    mixed = jnp.einsum("hqk,khd->qhd", probs.astype(jnp.bfloat16), heads[:, 2], preferred_element_type=jnp.float32)
    mixed = mixed.reshape(length, width).astype(jnp.bfloat16)
    branch = matmul(mixed, weight[:, 3 * width :], NN)
    return branch, (heads, probs, mixed)


def attention_backward(stream, weight, kept, grad_low):
    heads, probs, mixed = kept
    length, width = stream.shape
    size = width // HEADS
    grad_out = matmul(mixed, grad_low, TN)
    grad_mixed = matmul(grad_low, weight[:, 3 * width :], NT).astype(jnp.bfloat16)
    grad_mixed = grad_mixed.reshape(length, HEADS, size)
    grad_probs = jnp.einsum("qhd,khd->hqk", grad_mixed, heads[:, 2], preferred_element_type=jnp.float32)
    centre = jnp.sum(probs * grad_probs, -1, keepdims=True)
    grad_scores = (probs * (grad_probs - centre)).astype(jnp.bfloat16)
    low = probs.astype(jnp.bfloat16)
    scale = size**-0.5
    grad_q = jnp.einsum("hqk,khd->qhd", grad_scores, heads[:, 1], preferred_element_type=jnp.float32) * scale
    grad_k = jnp.einsum("hqk,qhd->khd", grad_scores, heads[:, 0], preferred_element_type=jnp.float32) * scale
    grad_v = jnp.einsum("hqk,qhd->khd", low, grad_mixed, preferred_element_type=jnp.float32)
    packed = jnp.concatenate([grad_q, grad_k, grad_v], axis=1).reshape(length, 3 * width)
    packed = packed.astype(jnp.bfloat16)
    grad_in = matmul(stream, packed, TN)
    grad_inputs = matmul(packed, weight[:, : 3 * width], NT)
    return grad_inputs, jnp.concatenate([grad_in, grad_out], axis=1)


def feed_forward(stream, weight, down):
    pre = matmul(stream, weight, NN)
    active = jax.nn.gelu(pre, approximate=True).astype(jnp.bfloat16)
    return matmul(active, down, NN), (pre, active)


def feed_backward(stream, weight, down, kept, grad_low):
    pre, active = kept
    grad_down = matmul(active, grad_low, TN)
    grad_active = matmul(grad_low, down, NT)
    pull = jax.vjp(lambda value: jax.nn.gelu(value, approximate=True), pre)[1]
    grad_pre = pull(grad_active)[0].astype(jnp.bfloat16)
    grad_up = matmul(stream, grad_pre, TN)
    return matmul(grad_pre, weight, NT), grad_up, grad_down


def micro_step(rows, pull, segment, mats, downs, gains, biases):
    low = jnp.bfloat16
    mask = segment[:, None] == segment[None, :]
    stream, dual = rows, jnp.zeros_like(rows)
    saved = []
    for sub in range(4):
        if sub % 2 == 0:
            branch, kept = attention_forward(stream, mats[sub], mask)
        else:
            branch, kept = feed_forward(stream, mats[sub], downs[sub // 2])
        normal, inverse = norm_stats(stream.astype(jnp.float32) + branch)
        out = normal * gains[sub] + biases[sub]
        total = dual.astype(jnp.float32) + branch
        saved.append((stream, kept, normal, inverse))
        if sub < 3:
            stream, dual = out.astype(low), total.astype(low)
    dual_normal, dual_inverse = norm_stats(total)
    output = (out + dual_normal).astype(low)
    grad_out, grad_dual = pull, norm_back(dual_normal, dual_inverse, pull)
    grads_a, grads_b, grads_n = [None] * 4, [None] * 2, [None] * 4
    for sub in (3, 2, 1, 0):
        stream, kept, normal, inverse = saved[sub]
        grads_n[sub] = jnp.stack([jnp.sum(grad_out * normal, 0), jnp.sum(grad_out, 0)], axis=1)
        summed = norm_back(normal, inverse, grad_out * gains[sub])
        branch_low = (summed + grad_dual).astype(low)
        if sub % 2 == 0:
            inner, grads_a[sub] = attention_backward(stream, mats[sub], kept, branch_low)
        else:
            inner, grads_a[sub], grads_b[sub // 2] = feed_backward(
                stream, mats[sub], downs[sub // 2], kept, branch_low
            )
        grad_in = summed + inner
        if sub > 0:
            grad_out = grad_in.astype(low).astype(jnp.float32)
            grad_dual = grad_dual.astype(low).astype(jnp.float32)
    return output, grad_in, jnp.stack(grads_a), jnp.stack(grads_b), jnp.stack(grads_n)


def finish_step(grad_norm, output, input_grad, *groups):
    factor = CLIP_NORM / jnp.maximum(grad_norm, CLIP_NORM)
    results = [grad_norm, output[None], input_grad[None]]
    for weight, one, two, grad, rate, decay in groups:
        clip = grad * factor
        moment, square_new, master = adam_update(weight, one, two, clip, rate, decay)
        results += [clip, moment, square_new, master, master.astype(jnp.bfloat16)]
    return tuple(results)


def body(
    tokens, cotangent, lengths, mat_a, mat_b, norms, first_a, second_a, first_b, second_b, first_n, second_n
):
    low = jnp.bfloat16
    own = lax.axis_index("section")
    length = tokens.shape[0] // lengths.shape[0]
    rows = lax.dynamic_slice_in_dim(tokens, own * length, length, 0)
    segment, live = segments_of(lax.dynamic_index_in_dim(lengths, own, 0, keepdims=False), length)
    pull = lax.dynamic_slice_in_dim(cotangent, own * length, length, 0).astype(jnp.float32) * live[:, None]

    def gathered(value):
        return lax.all_gather(lax.all_gather(value, "dp", axis=1, tiled=True), "section", axis=0, tiled=True)

    mats = gathered(mat_a.astype(low))
    scales = gathered(norms.astype(low)).astype(jnp.float32)
    downs = lax.all_gather(mat_b.astype(low), "section", axis=2, tiled=True)
    downs = lax.all_gather(downs, "dp", axis=1, tiled=True)
    output, input_grad, part_a, part_b, part_n = micro_step(
        rows, pull, segment, mats, downs, scales[:, :, 0], scales[:, :, 1]
    )

    def scattered(value, section_dim):
        value = lax.psum_scatter(value, "section", scatter_dimension=section_dim, tiled=True)
        return lax.psum_scatter(value, "dp", scatter_dimension=1, tiled=True).astype(jnp.float32)

    grad_a = scattered(part_a.astype(low), 0)
    grad_b = scattered(part_b.astype(low), 2)
    grad_n = scattered(part_n, 0)
    square = jnp.sum(grad_a * grad_a) + jnp.sum(grad_b * grad_b) + jnp.sum(grad_n * grad_n)
    grad_norm = jnp.sqrt(lax.psum(square, ("section", "dp")))
    return finish_step(
        grad_norm, output, input_grad,
        (mat_a, first_a, second_a, grad_a, MATRIX_RATE, MATRIX_DECAY),
        (mat_b, first_b, second_b, grad_b, MATRIX_RATE, MATRIX_DECAY),
        (norms, first_n, second_n, grad_n, NORM_RATE, 0.0),
    )


LOW = jnp.bfloat16
WIDE = jnp.float32
MESH = pl.DeviceIdType.MESH
SECTIONS = 4
LANES = 128
BLOCK = 64
BY_BOTH = (4, 5)
KERNEL_VMEM = 64 * 1024 * 1024 - 256 * 1024


def gradient_items(rows_a, rows_b, cols_b, width, hidden):
    part = rows_a // SECTIONS
    return (
        ("B1", 3, cols_b // 2, rows_b),
        ("F3", 3, part, hidden // 2),
        ("O2", 2, part, width // 2),
        ("K2", 2, part, 3 * width // 2),
        ("B0", 1, cols_b // 2, rows_b),
        ("F1", 1, part, hidden // 2),
        ("O0", 0, part, width // 2),
        ("K0", 0, part, 3 * width // 2),
    )


def item_scratch(name, chips, rows, columns):
    piece = (rows, columns)
    return (
        ("own" + name, (chips, SECTIONS, 2) + piece, LOW),
        ("farx" + name, (chips,) + piece, LOW),
        ("fary" + name, (chips,) + piece, LOW),
        ("nearx" + name, (2, chips) + piece, LOW),
        ("neary" + name, (2, chips) + piece, LOW),
        ("line" + name, (chips, 2) + piece, LOW),
        ("done" + name, (2,) + piece if name[0] == "B" else (SECTIONS, 2) + piece, WIDE if name[0] == "B" else LOW),
    )


def kernel_scratch(chips, rows_a, rows_b, cols_b, length, width, hidden):
    devices = 2 * chips
    items = gradient_items(rows_a, rows_b, cols_b, width, hidden)
    count = len(items)
    received = sum((item_scratch(name, chips, rows, columns) for name, _, rows, columns in items), ())
    return received + (
        ("fac_s", (32,), None),
        ("fac_r", (32,), None),
        ("px_s", (count, 3), None),
        ("px_r", (count, 3), None),
        ("py_s", (count, 3), None),
        ("py_r", (count, 3), None),
        ("line_s", (count, chips), None),
        ("line_r", (count, chips), None),
        ("done_s", (count,), None),
        ("done_r", (count, SECTIONS), None),
        ("wa", (4, chips, 2, SECTIONS, rows_a // SECTIONS, hidden), LOW),
        ("wb", (2, chips, 2, SECTIONS, rows_b, cols_b), LOW),
        ("in_a", (1, rows_a, hidden), WIDE),
        ("in_b", (2, rows_b, cols_b), WIDE),
        ("in_n", (1, 2, rows_a), WIDE),
        ("out_a", (rows_a, hidden), WIDE),
        ("out_b", (2, rows_b, cols_b), WIDE),
        ("out_n", (2, rows_a), WIDE),
        ("out_square", (8, LANES), WIDE),
        ("out_output", (length, width), LOW),
        ("out_input", (length, width), WIDE),
        ("cut", (SECTIONS, rows_a // SECTIONS, hidden), LOW),
        ("tiles", (devices, SECTIONS, 8, LANES), WIDE),
        ("x", (4, length, width), LOW),
        ("xt", (4, chips, 2, rows_a, length), LOW),
        ("xtc", (4, chips, rows_a, 2 * length), LOW),
        ("y", (length, width), LOW),
        ("cot", (length, width), LOW),
        ("bias", (length, length), WIDE),
        ("live", (length, 1), WIDE),
        ("f", (length, width), WIDE),
        ("n", (4, length, width), WIDE),
        ("inv", (4, length, 1), WIDE),
        ("q", (2, length, width), LOW),
        ("k", (2, length, width), LOW),
        ("v", (2, length, width), LOW),
        ("kt", (2, width, length), LOW),
        ("vt", (2, width, length), LOW),
        ("ot", (2, chips, 2, rows_a, length), LOW),
        ("otc", (2, chips, rows_a, 2 * length), LOW),
        ("pt", (2, HEADS, length, length), LOW),
        ("g", (2, length, hidden), LOW),
        ("gc", (2, chips, 2 * length, rows_b), LOW),
        ("slope", (2, length, hidden), LOW),
        ("gx", (length, width), WIDE),
        ("gy", (length, width), WIDE),
        ("df", (2, 2 * length, width), LOW),
        ("dft", (2, width, 2 * length), LOW),
        ("dm", (length, width), LOW),
        ("dqt", (width, length), LOW),
        ("dh", (2, 2 * length, hidden), LOW),
        ("dp", (2, 2 * length, 3 * width), LOW),
        ("ng", (devices, 8, width), WIDE),
        ("ns", (SECTIONS, 8, width), WIDE),
        ("sq", (devices, 8, LANES), WIDE),
        ("sqs", (SECTIONS, 8, LANES), WIDE),
        ("sum", (8, LANES), WIDE),
        ("in_s", (5,), None),
        ("out_s", (6,), None),
        ("cut_s", (1,), None),
        ("cut_r", (SECTIONS,), None),
        ("gz_s", (6,), None),
        ("gz_r", (6, chips), None),
        ("gx_s", (6,), None),
        ("gx_r", (6,), None),
        ("gy_s", (6,), None),
        ("gy_r", (6,), None),
        ("rx_s", (6,), None),
        ("rx_r", (6,), None),
        ("ry_s", (6,), None),
        ("ry_r", (6,), None),
        ("gs_s", (6,), None),
        ("gs_r", (6,), None),
        ("small_s", (3, 2), None),
        ("small_r", (3, 2), None),
    )


INPUTS = ("tokens", "cotangent", "lengths", "mat_a", "mat_b", "norms")
OUTPUTS = ("grad_a", "grad_b", "grad_n", "square", "output", "input_grad")


def step_kernel(names, *refs):
    r = types.SimpleNamespace(**dict(zip(names, refs)))
    length, width = r.x.shape[1:]
    hidden = r.wa.shape[-1]
    rows_a, (rows_b, cols_b) = r.mat_a.shape[1], r.mat_b.shape[1:]
    devices = r.tiles.shape[0]
    chips = devices // 2
    half_b = cols_b // 2
    grad_items = gradient_items(rows_a, rows_b, cols_b, width, hidden)
    head = width // HEADS
    scale = head**-0.5

    s, d = lax.axis_index("section"), lax.axis_index("dp")
    z, c = lax.div(d, 2), lax.rem(d, 2)
    sx = s + 1 - 2 * lax.rem(s, 2)
    sy = lax.rem(s + 2, SECTIONS)
    sd = SECTIONS - 1 - s
    to_sibling = {"dp": d + 1 - 2 * c}
    to_up, to_down = {"dp": d + 2}, {"dp": d - 2}
    to_x, to_y = {"section": sx}, {"section": sy}
    below, above = z > 0, z < chips - 1
    group = [{"dp": lax.rem(d + step, devices)} for step in range(1, devices)]
    plane = [{"section": lax.rem(s + step, SECTIONS)} for step in range(1, SECTIONS)]
    finish = []

    def when(condition, work):
        if condition is None:
            work()
        else:
            pl.when(condition)(work)

    def push(source, target, send_sem, recv_sem, device):
        pltpu.make_async_remote_copy(
            src_ref=source,
            dst_ref=target,
            send_sem=send_sem,
            recv_sem=recv_sem,
            device_id=device,
            device_id_type=MESH,
        ).start()

    def arrived(target, sem):
        pltpu.make_async_remote_copy(
            src_ref=target, dst_ref=target, send_sem=sem, recv_sem=sem, device_id=to_x, device_id_type=MESH
        ).wait_recv()

    def sent(source, sem):
        pltpu.make_async_remote_copy(
            src_ref=source, dst_ref=source, send_sem=sem, recv_sem=sem, device_id=to_x, device_id_type=MESH
        ).wait_send()

    def at_end(condition, source, sem):
        finish.append((condition, source, sem))

    def aligned(start, size):
        return pl.ds(pl.multiple_of(start, size), size)

    own_x = pltpu.make_async_copy(r.tokens.at[aligned(s * length, length)], r.x.at[0], r.in_s.at[0])
    own_cot = pltpu.make_async_copy(r.cotangent.at[aligned(s * length, length)], r.cot, r.in_s.at[1])
    own_a = pltpu.make_async_copy(r.mat_a, r.in_a, r.in_s.at[2])
    own_b = pltpu.make_async_copy(r.mat_b, r.in_b, r.in_s.at[3])
    own_n = pltpu.make_async_copy(r.norms, r.in_n, r.in_s.at[4])
    own_a.start()
    own_n.start()
    own_b.start()
    own_x.start()
    own_cot.start()
    barrier = pltpu.get_barrier_semaphore()
    for peer in group + plane:
        pl.semaphore_signal(barrier, inc=1, device_id=peer, device_id_type=MESH)
    own_a.wait()
    r.cut[...] = r.in_a[0].astype(LOW).reshape(SECTIONS, rows_a // SECTIONS, hidden)
    r.wa[s, z, c, s] = r.cut[s]
    own_n.wait()
    norms = r.in_n[0].astype(LOW).astype(WIDE)
    nothing = jnp.zeros((2, rows_a), WIDE)
    even = jnp.concatenate([norms, nothing], axis=1)
    odd = jnp.concatenate([nothing, norms], axis=1)
    r.tiles[d, s, 0:2, :] = jnp.where(c == 0, even, odd)
    r.tiles[d, s, 2:8, :] = jnp.zeros((6, LANES), WIDE)
    own_b.wait()
    for layer in range(2):
        r.wb[layer, z, c, s] = r.in_b[layer].astype(LOW)
    pl.semaphore_wait(barrier, len(group) + len(plane))

    def put_out(slot, source, target):
        made = pltpu.make_async_copy(source, target, r.out_s.at[slot])
        made.start()
        return made

    def small_out(which, source):
        for peer in group:
            push(source, source, r.small_s.at[which, 0], r.small_r.at[which, 0], peer)

    def small_group(which, like):
        arrived(like, r.small_r.at[which, 0])
        sent(like, r.small_s.at[which, 0])

    def small_plane_out(which, source):
        for peer in plane:
            push(source, source, r.small_s.at[which, 1], r.small_r.at[which, 1], peer)

    def small_plane(which, like):
        arrived(like, r.small_r.at[which, 1])
        sent(like, r.small_s.at[which, 1])

    every = slice(None)

    def cores(item):
        return every if item in BY_BOTH else c

    def swap_out(item):
        own = r.wb.at[item - 4, z, c, s]
        push(own, own, r.gs_s.at[item], r.gs_r.at[item], to_sibling)
        at_end(None, own, r.gs_s.at[item])

    def swap_in(item):
        arrived(r.wb.at[item - 4, z, 1 - c, s], r.gs_r.at[item])

    def block(item, chip, section):
        if item < 4:
            return r.wa.at[item, chip, c, section]
        return r.wb.at[item - 4, chip, cores(item), section]

    def half_block(item, section, half):
        if item < 4:
            return r.wa.at[item, :, c, section, :, pl.ds(half * hidden // 2, hidden // 2)]
        rows = pl.ds(half * rows_b // 2, rows_b // 2)
        return r.wb.at[item - 4, :, cores(item), section, rows]

    def core_blocks(item, core):
        return r.wa.at[item, :, core] if item < 4 else r.wb.at[item - 4, :, core]

    def cut_out():
        for section, device in ((sd, {"section": sd}), (sx, to_x), (sy, to_y)):
            push(r.cut.at[section], r.wa.at[s, z, c, section], r.cut_s.at[0], r.cut_r.at[s], device)
        at_end(None, r.cut.at[pl.ds(0, SECTIONS - 1)], r.cut_s.at[0])

    def cut_in():
        for section in (sx, sy, sd):
            arrived(r.wa.at[section, z, c, s], r.cut_r.at[section])

    def line_out(item):
        own = block(item, z, s)

        def to_chip(chip):
            push(own, own, r.gz_s.at[item], r.gz_r.at[item, z], {"dp": 2 * chip + c})

        for step in range(1, chips):
            when(z >= step, functools.partial(to_chip, z - step))
            when(z + step < chips, functools.partial(to_chip, z + step))
        several = block(item, pl.ds(0, chips - 1), s)
        at_end(None, several, r.gz_s.at[item])

    def plane_out(item, chip):
        own = block(item, chip, s)
        push(own, own, r.gx_s.at[item], r.gx_r.at[item], to_x)
        push(own, own, r.gy_s.at[item], r.gy_r.at[item], to_y)

    def line_in(item):
        for step in range(1, chips):
            chip = lax.rem(z + step, chips)
            arrived(block(item, chip, s), r.gz_r.at[item, chip])
            plane_out(item, chip)
        core_out(item, s)
        at_end(None, block(item, every, s), r.gx_s.at[item])
        at_end(None, block(item, every, s), r.gy_s.at[item])

    def core_out(item, section):
        if item in BY_BOTH:
            return
        blocks = block(item, every, section)
        push(blocks, blocks, r.gs_s.at[item], r.gs_r.at[item], to_sibling)

    def plane_in(item):
        arrived(block(item, every, sx), r.gx_r.at[item])
        part = half_block(item, sx, 1)
        push(part, part, r.ry_s.at[item], r.ry_r.at[item], to_y)
        arrived(block(item, every, sy), r.gy_r.at[item])
        part = half_block(item, sy, 0)
        push(part, part, r.rx_s.at[item], r.rx_r.at[item], to_x)
        core_out(item, sx)
        core_out(item, sy)
        at_end(None, part, r.ry_s.at[item])
        at_end(None, part, r.rx_s.at[item])

    def far_in(item):
        arrived(half_block(item, sd, 0), r.rx_r.at[item])
        arrived(half_block(item, sd, 1), r.ry_r.at[item])
        core_out(item, sd)
        if item not in BY_BOTH:
            at_end(None, core_blocks(item, c), r.gs_s.at[item])

    def core_in(item):
        if item not in BY_BOTH:
            arrived(core_blocks(item, 1 - c), r.gs_r.at[item])

    mine, other = pl.ds(0, length), pl.ds(length, length)

    def give(slot, source, target):
        push(source, target, r.fac_s.at[slot], r.fac_r.at[slot], to_sibling)
        at_end(None, target, r.fac_s.at[slot])

    def taken(slot, target):
        arrived(target, r.fac_r.at[slot])

    def give_rows(layer):
        r.xt[layer] = r.x[layer].T.reshape(chips, 2, rows_a, length)
        r.xtc[layer, :, :, 0:length] = r.xt[layer, :, c]
        give(layer, r.xt.at[layer, :, 1 - c], r.xtc.at[layer, :, :, other])

    def product(left, right, dims):
        return lax.dot_general(left, right, (dims, ((), ())), preferred_element_type=WIDE)

    def loop(count, work):
        def one(index, carry):
            work(index)
            return carry

        lax.fori_loop(0, count, one, 0)

    def gain_row(layer, kind):
        parts = [
            r.tiles[2 * chip, layer, kind : kind + 1, :] + r.tiles[2 * chip + 1, layer, kind : kind + 1, :]
            for chip in range(chips)
        ]
        return jnp.concatenate(parts, axis=1)

    def stats(value):
        centre = value - jnp.mean(value, -1, keepdims=True)
        inverse = lax.rsqrt(jnp.mean(centre * centre, -1, keepdims=True) + EPSILON)
        return centre * inverse, inverse

    lane = lax.broadcasted_iota(jnp.int32, (1, 2 * head), 1)
    first_half = (lane < head).astype(WIDE)
    half_masks = (first_half.astype(LOW), (1.0 - first_half).astype(LOW))

    def prepare_masks():
        ends, total = [], jnp.int32(0)
        for slot in range(r.lengths.shape[1]):
            total = total + r.lengths[s, slot]
            ends.append(total)
        down_places = lax.broadcasted_iota(jnp.int32, (length, 1), 0)
        across_places = lax.broadcasted_iota(jnp.int32, (1, length), 1)
        down_segment = jnp.zeros((length, 1), jnp.int32)
        across_segment = jnp.zeros((1, length), jnp.int32)
        for end in ends:
            down_segment = down_segment + (end <= down_places).astype(jnp.int32)
            across_segment = across_segment + (end <= across_places).astype(jnp.int32)
        r.bias[...] = jnp.where(down_segment == across_segment, 0.0, NEGATIVE)
        r.live[...] = (down_places < total).astype(WIDE)

    def matrix(layer, place):
        value = r.wa[layer, :, :, :, :, place]
        return value.reshape(width, value.shape[-1])

    def down(at, chip=slice(None)):
        blocks = [r.wb[at, chip, :, section] for section in range(SECTIONS)]
        return jnp.concatenate([block.reshape(-1, cols_b) for block in blocks], axis=1)

    def attention_in(layer):
        at = layer // 2
        rows = r.x[layer]
        r.q[at] = product(rows, matrix(layer, pl.ds(0, width)), NN).astype(LOW) * jnp.asarray(scale, LOW)
        keys = product(rows, matrix(layer, pl.ds(width, width)), NN).astype(LOW)
        r.k[at] = keys
        values = product(rows, matrix(layer, pl.ds(2 * width, width)), NN).astype(LOW)
        r.v[at] = values
        r.vt[at] = values.T

    def attention_heads(layer, begin, count):
        at = layer // 2

        def pair(index):
            lanes = aligned(index * 2 * head, 2 * head)
            for which in range(2):
                scores = product(r.k[at, :, lanes], r.q[at, :, lanes] * half_masks[which], NT) + r.bias[...]
                weights = jnp.exp(scores - jnp.max(scores, 0, keepdims=True))
                probs = (weights * (1.0 / jnp.sum(weights, 0, keepdims=True))).astype(LOW)
                r.pt[at, 2 * index + which] = probs
                place = aligned((2 * index + which) * head, head)
                r.ot[at, index, which] = product(r.vt[at, place, :], probs, NN).astype(LOW)

        for index in range(begin, begin + count):
            pair(index)

    def attention_out(layer):
        at = layer // 2
        r.otc[at, :, :, 0:length] = r.ot[at, :, c]
        give(4 + at, r.ot.at[at, :, 1 - c], r.otc.at[at, :, :, other])
        r.f[...] = product(r.ot[at].reshape(width, length).T, matrix(layer, pl.ds(3 * width, width)), NN)

    def expand(layer, index):
        at = layer // 2
        place = pl.ds(index * width, width)
        pre = product(r.x[layer], matrix(layer, place), NN)
        squared = pre * pre
        slope = 0.7978845608 * (1.0 + 3 * 0.044715 * squared)
        bent = jnp.tanh(0.7978845608 * pre * (1.0 + 0.044715 * squared))
        r.g[at, :, place] = (0.5 * pre * (1.0 + bent)).astype(LOW)
        r.slope[at, :, place] = (0.5 * (1.0 + bent) + 0.5 * pre * (1.0 - bent * bent) * slope).astype(LOW)
        block = aligned((2 * index + c) * rows_b, rows_b)
        r.gc[at, index, 0:length, :] = r.g[at, :, block]
        block = aligned((2 * index + 1 - c) * rows_b, rows_b)
        give(6 + chips * at + index, r.g.at[at, :, block], r.gc.at[at, index, other, :])

    def contract(layer):
        r.f[...] = product(r.g[layer // 2], down(layer // 2), NN)

    def by_rows(work):
        for index in range(length // BLOCK):
            work(pl.ds(index * BLOCK, BLOCK))

    def normalize(layer):
        gain, offset = gain_row(layer, 0), gain_row(layer, 1)

        def some(rows):
            branch = r.f[rows, :]
            normal, inverse = stats(r.x[layer, rows, :].astype(WIDE) + branch)
            r.n[layer, rows, :] = normal
            r.inv[layer, rows, :] = inverse
            out = normal * gain + offset
            dual = branch if layer == 0 else r.y[rows, :].astype(WIDE) + branch
            if layer < 3:
                r.x[layer + 1, rows, :] = out.astype(LOW)
                r.y[rows, :] = dual.astype(LOW)
            else:
                dual_normal, dual_inverse = stats(dual)
                r.out_output[rows, :] = (out + dual_normal).astype(LOW)
                pull = r.cot[rows, :].astype(WIDE) * r.live[rows, :]
                r.gx[rows, :] = pull
                r.gy[rows, :] = norm_back(dual_normal, dual_inverse, pull)

        by_rows(some)

    def back_normalize(layer):
        gain = gain_row(layer, 0)

        def some(index, sums):
            rows = pl.ds(index * BLOCK, BLOCK)
            upstream = r.gx[rows, :]
            normal = r.n[layer, rows, :]
            summed = norm_back(normal, r.inv[layer, rows, :], upstream * gain)
            dual = r.gy[rows, :]
            r.gx[rows, :] = summed
            r.df[layer // 2, rows, :] = (summed + dual).astype(LOW)
            if layer == 3:
                r.gy[rows, :] = dual.astype(LOW).astype(WIDE)
            return (
                sums[0] + jnp.sum(upstream * normal, 0, keepdims=True),
                sums[1] + jnp.sum(upstream, 0, keepdims=True),
            )

        zero = jnp.zeros((1, width), WIDE)
        gains, offsets = zero, zero
        for index in range(length // BLOCK):
            gains, offsets = some(index, (gains, offsets))
        r.ng[d, 2 * layer : 2 * layer + 1, :] = gains
        r.ng[d, 2 * layer + 1 : 2 * layer + 2, :] = offsets

    def pass_down(layer, inner):
        total = r.gx[...] + inner
        if layer > 0:
            r.gx[...] = total.astype(LOW).astype(WIDE)
        else:
            r.out_input[...] = total

    base = 6 + 2 * chips

    def back_hidden(layer):
        at = layer // 2
        r.dft[at, :, 0:length] = r.df[at, 0:length, :].T
        give(base + at, r.dft.at[at, :, mine], r.dft.at[at, :, other])
        for index in range(hidden // width):
            place = pl.ds(index * width, width)
            pulled = product(r.df[at, 0:length, :], down(at, pl.ds(index, 1)), NT)
            r.dh[at, 0:length, place] = (pulled * r.slope[at, :, place].astype(WIDE)).astype(LOW)
            give(base + 2 + chips * at + index, r.dh.at[at, mine, place], r.dh.at[at, other, place])

    def back_expand_end(layer):
        pass_down(layer, product(r.dh[layer // 2, 0:length, :], matrix(layer, pl.ds(0, hidden)), NT))

    def back_output(layer):
        at = layer // 2
        give(base + 2 + 2 * chips + at, r.df.at[at, mine], r.df.at[at, other])
        r.dm[...] = product(r.df[at, 0:length, :], matrix(layer, pl.ds(3 * width, width)), NT).astype(LOW)
        r.kt[at] = (r.k[at] * jnp.asarray(scale, LOW)).T

    def back_heads(layer, begin, count):
        at = layer // 2

        def pair(index):
            lanes = aligned(index * 2 * head, 2 * head)
            pulled = r.dm[:, lanes]
            keys, values = [], []
            for which in range(2):
                probs = r.pt[at, 2 * index + which]
                grad = product(r.v[at, :, lanes], pulled * half_masks[which], NT)
                full = probs.astype(WIDE)
                centre = jnp.sum(full * grad, 0, keepdims=True)
                scores = (full * (grad - centre)).astype(LOW)
                keys.append(product(scores, r.q[at, :, lanes], NN))
                values.append(product(probs, pulled, NN))
                place = aligned((2 * index + which) * head, head)
                r.dqt[place, :] = product(r.kt[at, place, :], scores, NN).astype(LOW)
            r.dp[at, 0:length, aligned(width + index * 2 * head, 2 * head)] = jnp.where(
                lane < head, keys[0], keys[1]
            ).astype(LOW)
            r.dp[at, 0:length, aligned(2 * width + index * 2 * head, 2 * head)] = jnp.where(
                lane < head, values[0], values[1]
            ).astype(LOW)

        def pairs(step):
            pair(begin + 2 * step)
            pair(begin + 2 * step + 1)

        loop(count // 2, pairs)

    def back_packed(layer):
        at = layer // 2
        slot = base + 4 + 2 * chips + 2 * at
        place = pl.ds(width, 2 * width)
        give(slot, r.dp.at[at, mine, place], r.dp.at[at, other, place])
        r.dp[at, 0:length, 0:width] = r.dqt[...].T
        place = pl.ds(0, width)
        give(slot + 1, r.dp.at[at, mine, place], r.dp.at[at, other, place])

    def back_packed_end(layer):
        pass_down(layer, product(r.dp[layer // 2, 0:length, :], matrix(layer, pl.ds(0, 3 * width)), NT))

    def keep(name, half, place, value):
        own = getattr(r, "own" + name)
        own[:, :, half, :, place] = value.astype(LOW).reshape(chips, SECTIONS, rows_a // SECTIONS, value.shape[1])

    def chip_rows(value):
        return value.reshape(chips * rows_a, 2 * length)

    def grad_down(at):
        own = getattr(r, "ownB%d" % at)
        taken(base + at, r.dft.at[at, :, other])
        for chip in range(chips):
            taken(6 + chips * at + chip, r.gc.at[at, chip, other, :])
            value = product(r.dft[at], r.gc[at, chip], NN)
            own[chip] = value.astype(LOW).reshape(SECTIONS, 2, half_b, rows_b)

    def grad_up(layer):
        at = layer // 2
        taken(layer, r.xtc.at[layer, :, :, other])
        for index in range(hidden // width):
            place = pl.ds(index * width, width)
            taken(base + 2 + chips * at + index, r.dh.at[at, other, place])
            value = product(chip_rows(r.xtc[layer]), r.dh[at, :, place], NN)
            keep("F%d" % layer, index // 2, pl.ds(index % 2 * width, width), value)

    def grad_output(layer):
        at = layer // 2
        taken(4 + at, r.otc.at[at, :, :, other])
        taken(base + 2 + 2 * chips + at, r.df.at[at, other])
        for half in range(2):
            place = pl.ds(half * width // 2, width // 2)
            value = product(chip_rows(r.otc[at]), r.df[at, :, place], NN)
            keep("O%d" % layer, half, pl.ds(0, width // 2), value)

    def grad_packed(layer):
        at = layer // 2
        slot = base + 4 + 2 * chips + 2 * at
        taken(layer, r.xtc.at[layer, :, :, other])
        taken(slot, r.dp.at[at, other, pl.ds(width, 2 * width)])
        taken(slot + 1, r.dp.at[at, other, pl.ds(0, width)])
        part = 3 * width // 2
        for half in range(2):
            value = product(chip_rows(r.xtc[layer]), r.dp[at, :, half * part : (half + 1) * part], NN)
            keep("K%d" % layer, half, pl.ds(0, part), value)

    def joined(target, others):
        return functools.reduce(
            lambda left, right: left + right, [ref[...].astype(WIDE) for ref in (target, *others)]
        )

    def add_into(target, others):
        if len(others) == 1:
            target[...] = target[...] + others[0][...]
        else:
            target[...] = joined(target, others).astype(LOW)

    places = {name: place for place, (name, _, _, _) in enumerate(grad_items)}

    def buffers(name):
        parts = ("own", "farx", "fary", "nearx", "neary", "line", "done")
        return types.SimpleNamespace(**{part: getattr(r, part + name) for part in parts})

    def to_plane(name):
        item, place = buffers(name), places[name]

        def over_x(section, half, target, slot):
            push(item.own.at[:, section, half], target, r.px_s.at[place, slot], r.px_r.at[place, slot], to_x)
            at_end(None, item.farx, r.px_s.at[place, slot])

        def over_y(section, half, target, slot):
            push(item.own.at[:, section, half], target, r.py_s.at[place, slot], r.py_r.at[place, slot], to_y)
            at_end(None, item.farx, r.py_s.at[place, slot])

        over_x(sd, 0, item.farx, 2)
        over_y(sd, 1, item.fary, 2)
        over_x(sx, 0, item.nearx.at[0], 0)
        over_y(sy, 1, item.neary.at[1], 1)

    def through_plane(name):
        item, place = buffers(name), places[name]
        own = item.own
        arrived(item.fary, r.py_r.at[place, 2])
        add_into(own.at[:, sx, 1], [item.fary])
        push(own.at[:, sx, 1], item.nearx.at[1], r.px_s.at[place, 1], r.px_r.at[place, 1], to_x)
        at_end(None, item.farx, r.px_s.at[place, 1])
        arrived(item.farx, r.px_r.at[place, 2])
        add_into(own.at[:, sy, 0], [item.farx])
        push(own.at[:, sy, 0], item.neary.at[0], r.py_s.at[place, 0], r.py_r.at[place, 0], to_y)
        at_end(None, item.farx, r.py_s.at[place, 0])

    def to_line(name):
        item, place = buffers(name), places[name]
        own = item.own.at[:, s]
        for half in range(2):
            arrived(item.nearx.at[half], r.px_r.at[place, half])
            arrived(item.neary.at[half], r.py_r.at[place, half])
            add_into(own.at[:, half], [item.nearx.at[half], item.neary.at[half]])
        for step in range(1, chips):
            chip = lax.rem(z + step, chips)
            push(
                own.at[chip],
                item.line.at[z],
                r.line_s.at[place, step],
                r.line_r.at[place, z],
                {"dp": 2 * chip + c},
            )
            at_end(None, item.line.at[0], r.line_s.at[place, step])

    def to_owner(name):
        item, place = buffers(name), places[name]
        others = [lax.rem(z + step, chips) for step in range(1, chips)]
        for chip in others:
            arrived(item.line.at[chip], r.line_r.at[place, chip])
        total = joined(item.own.at[z, s], [item.line.at[chip] for chip in others])
        square = total * total
        while square.ndim > 2:
            square = jnp.sum(square, 0)
        square = jnp.sum(jnp.sum(square, 0, keepdims=True), 1, keepdims=True)
        r.sum[...] = r.sum[...] + jnp.broadcast_to(square, (8, LANES))
        if name[0] == "B":
            item.done[...] = total
            return
        item.done[s] = total.astype(LOW)
        layer = grad_items[place][1]
        mine = item.done.at[s]
        away = s != layer
        when(
            away,
            lambda: push(mine, mine, r.done_s.at[place], r.done_r.at[place, s], {"section": jnp.int32(layer)}),
        )
        at_end(away, mine, r.done_s.at[place])

    def collect(name):
        item, place = buffers(name), places[name]
        layer = grad_items[place][1]

        def work():
            for section in range(SECTIONS):
                if section != layer:
                    arrived(item.done.at[section], r.done_r.at[place, section])
            columns = item.done.shape[-1]
            start = 3 * width if name[0] == "O" else 0
            for section in range(SECTIONS):
                for half in range(2):
                    rows = pl.ds(section * (rows_a // SECTIONS), rows_a // SECTIONS)
                    place_to = pl.ds(start + half * columns, columns)
                    r.out_a[rows, place_to] = item.done[section, half].astype(WIDE)

        when(s == layer, work)

    def all_sent(count=None):
        for condition, source, sem in finish[:count]:
            when(condition, functools.partial(sent, source, sem))
        del finish[:count]

    cut_out()
    swap_out(4)
    swap_out(5)
    small_out(0, r.tiles.at[d, s])
    swap_in(4)
    line_out(4)
    plane_out(4, z)
    swap_in(5)
    plane_out(5, z)
    cut_in()
    plane_out(1, z)
    line_out(0)
    line_out(1)
    plane_out(3, z)
    plane_out(0, z)
    line_in(4)
    small_group(0, r.tiles.at[pl.ds(0, devices - 1), 0])
    for peer in plane:
        push(r.tiles.at[:, s], r.tiles.at[:, s], r.small_s.at[0, 1], r.small_r.at[0, 1], peer)
    line_in(0)
    plane_out(2, z)
    line_out(2)
    line_out(3)
    line_in(1)
    plane_in(0)
    plane_in(4)
    far_in(0)
    line_out(5)
    plane_in(1)
    line_in(2)
    own_x.wait()
    own_cot.wait()
    prepare_masks()
    core_in(0)
    attention_in(0)
    attention_heads(0, 0, 2)
    attention_heads(0, 2, 2)
    far_in(1)
    line_in(3)
    attention_out(0)
    small_plane(0, r.tiles.at[:, pl.ds(0, SECTIONS - 1)])
    normalize(0)
    far_in(4)
    core_in(1)
    plane_in(2)
    expand(1, 0)
    expand(1, 1)
    line_in(5)
    expand(1, 2)
    expand(1, 3)
    early = len(finish)
    far_in(2)
    plane_in(3)
    core_in(4)
    contract(1)
    normalize(1)
    core_in(2)
    attention_in(2)
    plane_in(5)
    attention_heads(2, 0, 2)
    attention_heads(2, 2, 2)
    far_in(3)
    attention_out(2)
    normalize(2)
    core_in(3)
    expand(3, 0)
    far_in(5)
    expand(3, 1)
    expand(3, 2)
    expand(3, 3)
    all_sent(early)
    core_in(5)
    contract(3)
    normalize(3)
    leaving = [put_out(0, r.out_output, r.output)]

    r.sum[...] = jnp.zeros((8, LANES), WIDE)
    back_normalize(3)
    back_hidden(3)
    give_rows(3)
    back_expand_end(3)
    back_normalize(2)
    grad_up(3)
    to_plane("F3")
    back_output(2)
    grad_down(1)
    to_plane("B1")
    back_heads(2, 0, 2)
    back_heads(2, 2, 2)
    back_packed(2)
    through_plane("B1")
    give_rows(2)
    grad_output(2)
    back_packed_end(2)
    give_rows(1)
    to_plane("O2")
    grad_packed(2)
    to_plane("K2")
    back_normalize(1)
    back_hidden(1)
    through_plane("K2")
    grad_down(0)
    to_plane("B0")
    back_expand_end(1)
    back_normalize(0)
    small_out(1, r.ng.at[d])
    to_line("K2")
    to_line("B1")
    back_output(0)
    grad_up(1)
    through_plane("B0")
    to_plane("F1")
    back_heads(0, 0, 2)
    back_heads(0, 2, 2)
    back_packed(0)
    to_line("B0")
    through_plane("O2")
    through_plane("F1")
    grad_output(0)
    to_plane("O0")
    give_rows(0)
    grad_packed(0)
    to_plane("K0")
    to_line("O2")
    to_line("F1")
    through_plane("O0")
    to_owner("B1")
    back_packed_end(0)
    leaving.append(put_out(1, r.out_input, r.input_grad))
    to_owner("B0")
    all_sent()
    through_plane("K0")
    small_group(1, r.ng.at[pl.ds(0, devices - 1)])
    r.ns[s] = functools.reduce(lambda left, right: left + right, [r.ng[index] for index in range(devices)])
    small_plane_out(1, r.ns.at[s])
    through_plane("F3")
    to_line("O0")
    to_line("K0")
    to_owner("F1")
    to_line("F3")
    to_owner("O2")
    to_owner("K2")
    to_owner("F3")
    to_owner("O0")
    to_owner("K0")

    r.sq[d] = r.sum[...]
    small_out(2, r.sq.at[d])
    for name in ("F1", "O2", "K2", "F3"):
        collect(name)
    collect("O0")
    for layer in range(2):
        done = buffers("B%d" % layer).done
        r.out_b[layer] = done[...].reshape(cols_b, rows_b).T
    leaving.append(put_out(2, r.out_b, r.grad_b))
    small_plane(1, r.ns.at[pl.ds(0, SECTIONS - 1)])
    grads = functools.reduce(lambda left, right: left + right, [r.ns[index] for index in range(SECTIONS)])
    norm_square = jnp.sum(jnp.sum(grads * grads, 0, keepdims=True), 1, keepdims=True)
    chosen = jnp.zeros((2, width), WIDE)
    for layer in range(4):
        chosen = jnp.where(s == layer, grads[2 * layer : 2 * layer + 2, :], chosen)
    shard = jnp.zeros((2, rows_a), WIDE)
    for chip in range(chips):
        pair_of = chosen[:, chip * LANES : (chip + 1) * LANES]
        shard = jnp.where(z == chip, jnp.where(c == 0, pair_of[:, :rows_a], pair_of[:, rows_a:]), shard)
    r.out_n[...] = shard
    leaving.append(put_out(3, r.out_n, r.grad_n))
    collect("K0")
    leaving.append(put_out(4, r.out_a, r.grad_a))
    small_group(2, r.sq.at[pl.ds(0, devices - 1)])
    r.sqs[s] = functools.reduce(lambda left, right: left + right, [r.sq[index] for index in range(devices)])
    small_plane_out(2, r.sqs.at[s])
    all_sent()
    small_plane(2, r.sqs.at[pl.ds(0, SECTIONS - 1)])
    squares = functools.reduce(lambda left, right: left + right, [r.sqs[index] for index in range(SECTIONS)])
    r.out_square[...] = squares + norm_square
    leaving.append(put_out(5, r.out_square, r.square))
    for made in leaving:
        made.wait()


def step_call(tokens, cotangent, lengths, mat_a, mat_b, norms):
    rows_a, hidden = mat_a.shape[1:]
    rows_b, cols_b = mat_b.shape[1:]
    width = tokens.shape[1]
    length = tokens.shape[0] // lengths.shape[0]
    chips = width // rows_a // 2
    scratch = kernel_scratch(chips, rows_a, rows_b, cols_b, length, width, hidden)
    shapes = []
    for _, shape, kind in scratch:
        shapes.append(pltpu.SemaphoreType.DMA(shape) if kind is None else pltpu.VMEM(shape, kind))
    anywhere = pl.BlockSpec(memory_space=pl.ANY)
    return pl.pallas_call(
        functools.partial(step_kernel, INPUTS + OUTPUTS + tuple(name for name, _, _ in scratch)),
        out_shape=(
            jax.ShapeDtypeStruct((rows_a, hidden), WIDE),
            jax.ShapeDtypeStruct(mat_b.shape, WIDE),
            jax.ShapeDtypeStruct((2, rows_a), WIDE),
            jax.ShapeDtypeStruct((8, LANES), WIDE),
            jax.ShapeDtypeStruct((length, width), LOW),
            jax.ShapeDtypeStruct((length, width), WIDE),
        ),
        in_specs=[anywhere, anywhere, pl.BlockSpec(memory_space=pltpu.SMEM), anywhere, anywhere, anywhere],
        out_specs=[anywhere] * len(OUTPUTS),
        scratch_shapes=shapes,
        compiler_params=pltpu.CompilerParams(
            collective_id=0, has_side_effects=True, vmem_limit_bytes=KERNEL_VMEM
        ),
    )(tokens, cotangent, lengths, mat_a, mat_b, norms)


def update_kernel(*refs):
    inputs, outputs, held, made, sems = refs[:15], refs[15:33], refs[33:48], refs[48:63], refs[63]
    started = []

    def copy(source, target):
        one = pltpu.make_async_copy(source, target, sems.at[len(started)])
        one.start()
        started.append(one)
        return one

    half = inputs[4].shape[1] // 2
    parts = [(0, pl.ds(0, half)), (0, pl.ds(half, half)), (1, slice(None)), (2, slice(None))]
    rates = ((MATRIX_RATE, MATRIX_DECAY), (MATRIX_RATE, MATRIX_DECAY), (NORM_RATE, 0.0))
    norm_in = copy(inputs[0], held[0])
    coming = []
    for group, rows in parts:
        coming.append(
            [copy(inputs[at].at[:, rows], held[at].at[:, rows]) for at in range(3 + 4 * group, 7 + 4 * group)]
        )
    passing = [copy(inputs[at], held[at]) for at in (1, 2)]
    norm_in.wait()
    grad_norm = jnp.sqrt(held[0][0:1, 0:1])
    factor = CLIP_NORM / jnp.maximum(grad_norm, CLIP_NORM)
    outputs[0][...] = grad_norm
    leaving = []
    for (group, rows), waits in zip(parts, coming):
        for one in waits:
            one.wait()
        grad, weight, one, two = (held[at][:, rows] for at in range(3 + 4 * group, 7 + 4 * group))
        clip = grad * factor
        moment, square, master = adam_update(weight, one, two, clip, *rates[group])
        for kind, value in enumerate((clip, moment, square, master, master.astype(LOW))):
            buffer = made[5 * group + kind]
            buffer[:, rows] = value
            leaving.append(copy(buffer.at[:, rows], outputs[3 + 5 * group + kind].at[:, rows]))
        if passing:
            at = 3 - len(passing)
            passing.pop(0).wait()
            leaving.append(copy(held[at], outputs[at].at[0]))
    for one in leaving:
        one.wait()


def kernel_body(
    tokens, cotangent, lengths, mat_a, mat_b, norms, first_a, second_a, first_b, second_b, first_n, second_n
):
    norms, first_n, second_n = (jnp.swapaxes(value, 1, 2) for value in (norms, first_n, second_n))
    grad_a, grad_b, grad_n, square, output, input_grad = step_call(
        tokens, cotangent, lengths, mat_a, mat_b, norms
    )
    args = (square, output, input_grad, grad_a[None], mat_a, first_a, second_a, grad_b, mat_b, first_b, second_b)
    args += (grad_n[None], norms, first_n, second_n)
    anywhere, vmem = pl.BlockSpec(memory_space=pl.ANY), pl.BlockSpec(memory_space=pltpu.VMEM)
    shapes = [jax.ShapeDtypeStruct((1, 1), WIDE)]
    shapes += [jax.ShapeDtypeStruct((1,) + value.shape, value.dtype) for value in (output, input_grad)]
    for value in (mat_a, mat_b, norms):
        shapes += [jax.ShapeDtypeStruct(value.shape, kind) for kind in (WIDE, WIDE, WIDE, WIDE, LOW)]
    scratch = [pltpu.VMEM(value.shape, value.dtype) for value in (*args, *shapes[3:])]
    results = pl.pallas_call(
        update_kernel,
        out_shape=shapes,
        in_specs=[anywhere] * len(args),
        out_specs=[vmem] + [anywhere] * (len(shapes) - 1),
        scratch_shapes=scratch + [pltpu.SemaphoreType.DMA((48,))],
        compiler_params=pltpu.CompilerParams(vmem_limit_bytes=KERNEL_VMEM),
    )(*args)
    results = [results[0][0, 0], *results[1:]]
    results[-5:] = [jnp.swapaxes(value, 1, 2) for value in results[-5:]]
    return tuple(results)


def chosen_body(*args):
    rows_a = args[3].shape[1]
    groups = lax.axis_size("dp")
    by_kernel = rows_a % 32 == 0 and 2 * rows_a == LANES and groups * rows_a == args[0].shape[1]
    return (kernel_body if by_kernel else body)(*args)


def solution(mesh):
    placed = (
        P("dp", None),
        P("dp", None),
        P("dp", None),
        P("section", "dp", None),
        P(None, "dp", "section"),
        P("section", "dp", None),
        P("section", "dp", None),
        P("section", "dp", None),
        P(None, "dp", "section"),
        P(None, "dp", "section"),
        P("section", "dp", None),
        P("section", "dp", None),
    )
    return jax.shard_map(
        chosen_body,
        mesh=mesh,
        in_specs=placed,
        out_specs=(
            P(),
            P("section", "dp", None),
            P("section", "dp", None),
            P("section", "dp", None),
            P("section", "dp", None),
            P("section", "dp", None),
            P("section", "dp", None),
            P("section", "dp", None),
            P(None, "dp", "section"),
            P(None, "dp", "section"),
            P(None, "dp", "section"),
            P(None, "dp", "section"),
            P(None, "dp", "section"),
            P("section", "dp", None),
            P("section", "dp", None),
            P("section", "dp", None),
            P("section", "dp", None),
            P("section", "dp", None),
        ),
        check_vma=False,
    )
```

```python
import functools
import types

import jax
import jax.numpy as jnp
from jax import lax
from jax.experimental import pallas as pl
from jax.experimental.pallas import tpu as pltpu
from jax.sharding import PartitionSpec as P

HEADS = 8
STEP = 5


EPSILON = 1e-05
NEGATIVE = -1e30
CLIP_NORM = 1.0
BETA_ONE = 0.5
BETA_TWO = 0.5
ADAM_EPSILON = 1e-08
MATRIX_RATE = 0.05
NORM_RATE = 0.5
MATRIX_DECAY = 0.01


def norm_stats(value):
    centre = value - jnp.mean(value, -1, keepdims=True)
    inverse = lax.rsqrt(jnp.mean(centre * centre, -1, keepdims=True) + EPSILON)
    return (centre * inverse, inverse)


def norm_back(normal, inverse, upstream):
    return inverse * (
        upstream
        - jnp.mean(upstream, -1, keepdims=True)
        - normal * jnp.mean(upstream * normal, -1, keepdims=True)
    )


def adam_update(weight, moment_one, moment_two, gradient, step_rate, decay_rate):
    first_new = BETA_ONE * moment_one + (1.0 - BETA_ONE) * gradient
    second_new = BETA_TWO * moment_two + (1.0 - BETA_TWO) * gradient * gradient
    first_hat = first_new / (1.0 - BETA_ONE**STEP)
    second_hat = second_new / (1.0 - BETA_TWO**STEP)
    weight_new = weight - step_rate * (
        first_hat / (jnp.sqrt(second_hat) + ADAM_EPSILON) + decay_rate * weight
    )
    return (first_new, second_new, weight_new)


def segments_of(lengths_row, length):
    ends = jnp.cumsum(lengths_row, dtype=jnp.int32)
    places = jnp.arange(length, dtype=jnp.int32)
    segment = jnp.sum((ends[None, :] <= places[:, None]).astype(jnp.int32), axis=1, dtype=jnp.int32)
    live = (places < ends[-1]).astype(jnp.float32)
    return segment, live


def matmul(left, right, dims):
    return lax.dot_general(left, right, (dims, ((), ())), preferred_element_type=jnp.float32)


NN = ((1,), (0,))
NT = ((1,), (1,))
TN = ((0,), (0,))


def attention_forward(stream, weight, mask):
    length, width = stream.shape
    size = width // HEADS
    packed = matmul(stream, weight[:, : 3 * width], NN).astype(jnp.bfloat16)
    heads = packed.reshape(length, 3, HEADS, size)
    scores = jnp.einsum("qhd,khd->hqk", heads[:, 0], heads[:, 1], preferred_element_type=jnp.float32)
    scores = jnp.where(mask[None], scores * size**-0.5, NEGATIVE)
    weights = jnp.exp(scores - jnp.max(scores, -1, keepdims=True))
    probs = weights / jnp.sum(weights, -1, keepdims=True)
    mixed = jnp.einsum("hqk,khd->qhd", probs.astype(jnp.bfloat16), heads[:, 2], preferred_element_type=jnp.float32)
    mixed = mixed.reshape(length, width).astype(jnp.bfloat16)
    branch = matmul(mixed, weight[:, 3 * width :], NN)
    return branch, (heads, probs, mixed)


def attention_backward(stream, weight, kept, grad_low):
    heads, probs, mixed = kept
    length, width = stream.shape
    size = width // HEADS
    grad_out = matmul(mixed, grad_low, TN)
    grad_mixed = matmul(grad_low, weight[:, 3 * width :], NT).astype(jnp.bfloat16)
    grad_mixed = grad_mixed.reshape(length, HEADS, size)
    grad_probs = jnp.einsum("qhd,khd->hqk", grad_mixed, heads[:, 2], preferred_element_type=jnp.float32)
    centre = jnp.sum(probs * grad_probs, -1, keepdims=True)
    grad_scores = (probs * (grad_probs - centre)).astype(jnp.bfloat16)
    low = probs.astype(jnp.bfloat16)
    scale = size**-0.5
    grad_q = jnp.einsum("hqk,khd->qhd", grad_scores, heads[:, 1], preferred_element_type=jnp.float32) * scale
    grad_k = jnp.einsum("hqk,qhd->khd", grad_scores, heads[:, 0], preferred_element_type=jnp.float32) * scale
    grad_v = jnp.einsum("hqk,qhd->khd", low, grad_mixed, preferred_element_type=jnp.float32)
    packed = jnp.concatenate([grad_q, grad_k, grad_v], axis=1).reshape(length, 3 * width)
    packed = packed.astype(jnp.bfloat16)
    grad_in = matmul(stream, packed, TN)
    grad_inputs = matmul(packed, weight[:, : 3 * width], NT)
    return grad_inputs, jnp.concatenate([grad_in, grad_out], axis=1)


def feed_forward(stream, weight, down):
    pre = matmul(stream, weight, NN)
    active = jax.nn.gelu(pre, approximate=True).astype(jnp.bfloat16)
    return matmul(active, down, NN), (pre, active)


def feed_backward(stream, weight, down, kept, grad_low):
    pre, active = kept
    grad_down = matmul(active, grad_low, TN)
    grad_active = matmul(grad_low, down, NT)
    pull = jax.vjp(lambda value: jax.nn.gelu(value, approximate=True), pre)[1]
    grad_pre = pull(grad_active)[0].astype(jnp.bfloat16)
    grad_up = matmul(stream, grad_pre, TN)
    return matmul(grad_pre, weight, NT), grad_up, grad_down


def micro_step(rows, pull, segment, mats, downs, gains, biases):
    low = jnp.bfloat16
    mask = segment[:, None] == segment[None, :]
    stream, dual = rows, jnp.zeros_like(rows)
    saved = []
    for sub in range(4):
        if sub % 2 == 0:
            branch, kept = attention_forward(stream, mats[sub], mask)
        else:
            branch, kept = feed_forward(stream, mats[sub], downs[sub // 2])
        normal, inverse = norm_stats(stream.astype(jnp.float32) + branch)
        out = normal * gains[sub] + biases[sub]
        total = dual.astype(jnp.float32) + branch
        saved.append((stream, kept, normal, inverse))
        if sub < 3:
            stream, dual = out.astype(low), total.astype(low)
    dual_normal, dual_inverse = norm_stats(total)
    output = (out + dual_normal).astype(low)
    grad_out, grad_dual = pull, norm_back(dual_normal, dual_inverse, pull)
    grads_a, grads_b, grads_n = [None] * 4, [None] * 2, [None] * 4
    for sub in (3, 2, 1, 0):
        stream, kept, normal, inverse = saved[sub]
        grads_n[sub] = jnp.stack([jnp.sum(grad_out * normal, 0), jnp.sum(grad_out, 0)], axis=1)
        summed = norm_back(normal, inverse, grad_out * gains[sub])
        branch_low = (summed + grad_dual).astype(low)
        if sub % 2 == 0:
            inner, grads_a[sub] = attention_backward(stream, mats[sub], kept, branch_low)
        else:
            inner, grads_a[sub], grads_b[sub // 2] = feed_backward(
                stream, mats[sub], downs[sub // 2], kept, branch_low
            )
        grad_in = summed + inner
        if sub > 0:
            grad_out = grad_in.astype(low).astype(jnp.float32)
            grad_dual = grad_dual.astype(low).astype(jnp.float32)
    return output, grad_in, jnp.stack(grads_a), jnp.stack(grads_b), jnp.stack(grads_n)


def finish_step(grad_norm, output, input_grad, *groups):
    factor = CLIP_NORM / jnp.maximum(grad_norm, CLIP_NORM)
    results = [grad_norm, output[None], input_grad[None]]
    for weight, one, two, grad, rate, decay in groups:
        clip = grad * factor
        moment, square_new, master = adam_update(weight, one, two, clip, rate, decay)
        results += [clip, moment, square_new, master, master.astype(jnp.bfloat16)]
    return tuple(results)


def body(
    tokens, cotangent, lengths, mat_a, mat_b, norms, first_a, second_a, first_b, second_b, first_n, second_n
):
    low = jnp.bfloat16
    own = lax.axis_index("section")
    length = tokens.shape[0] // lengths.shape[0]
    rows = lax.dynamic_slice_in_dim(tokens, own * length, length, 0)
    segment, live = segments_of(lax.dynamic_index_in_dim(lengths, own, 0, keepdims=False), length)
    pull = lax.dynamic_slice_in_dim(cotangent, own * length, length, 0).astype(jnp.float32) * live[:, None]

    def gathered(value):
        return lax.all_gather(lax.all_gather(value, "dp", axis=1, tiled=True), "section", axis=0, tiled=True)

    mats = gathered(mat_a.astype(low))
    scales = gathered(norms.astype(low)).astype(jnp.float32)
    downs = lax.all_gather(mat_b.astype(low), "section", axis=2, tiled=True)
    downs = lax.all_gather(downs, "dp", axis=1, tiled=True)
    output, input_grad, part_a, part_b, part_n = micro_step(
        rows, pull, segment, mats, downs, scales[:, :, 0], scales[:, :, 1]
    )

    def scattered(value, section_dim):
        value = lax.psum_scatter(value, "section", scatter_dimension=section_dim, tiled=True)
        return lax.psum_scatter(value, "dp", scatter_dimension=1, tiled=True).astype(jnp.float32)

    grad_a = scattered(part_a.astype(low), 0)
    grad_b = scattered(part_b.astype(low), 2)
    grad_n = scattered(part_n, 0)
    square = jnp.sum(grad_a * grad_a) + jnp.sum(grad_b * grad_b) + jnp.sum(grad_n * grad_n)
    grad_norm = jnp.sqrt(lax.psum(square, ("section", "dp")))
    return finish_step(
        grad_norm, output, input_grad,
        (mat_a, first_a, second_a, grad_a, MATRIX_RATE, MATRIX_DECAY),
        (mat_b, first_b, second_b, grad_b, MATRIX_RATE, MATRIX_DECAY),
        (norms, first_n, second_n, grad_n, NORM_RATE, 0.0),
    )


LOW = jnp.bfloat16
WIDE = jnp.float32
MESH = pl.DeviceIdType.MESH
SECTIONS = 4
LANES = 128
BLOCK = 64
ROWS_FIRST = (5,)
KERNEL_VMEM = 64 * 1024 * 1024 - 256 * 1024


def gradient_items(rows_a, rows_b, cols_b, width, hidden):
    part = rows_a // SECTIONS
    return (
        ("B1", 3, cols_b // 2, rows_b),
        ("F3", 3, part, hidden // 2),
        ("O2", 2, part, width // 2),
        ("K2", 2, part, 3 * width // 2),
        ("B0", 1, cols_b // 2, rows_b),
        ("F1", 1, part, hidden // 2),
        ("O0", 0, part, width // 2),
        ("K0", 0, part, 3 * width // 2),
    )


def item_scratch(name, chips, rows, columns):
    piece = (rows, columns)
    return (
        ("own" + name, (chips, SECTIONS, 2) + piece, LOW),
        ("farx" + name, (chips,) + piece, LOW),
        ("fary" + name, (chips,) + piece, LOW),
        ("nearx" + name, (2, chips) + piece, LOW),
        ("neary" + name, (2, chips) + piece, LOW),
        ("line" + name, (chips, 2) + piece, LOW),
        ("done" + name, (2,) + piece if name[0] == "B" else (SECTIONS, 2) + piece, WIDE if name[0] == "B" else LOW),
    )


def kernel_scratch(chips, rows_a, rows_b, cols_b, length, width, hidden):
    devices = 2 * chips
    items = gradient_items(rows_a, rows_b, cols_b, width, hidden)
    count = len(items)
    received = sum((item_scratch(name, chips, rows, columns) for name, _, rows, columns in items), ())
    return received + (
        ("fac_s", (32,), None),
        ("fac_r", (32,), None),
        ("px_s", (count, 3), None),
        ("px_r", (count, 3), None),
        ("py_s", (count, 3), None),
        ("py_r", (count, 3), None),
        ("line_s", (count, chips), None),
        ("line_r", (count, chips), None),
        ("done_s", (count,), None),
        ("done_r", (count, SECTIONS), None),
        ("wa", (4, chips, 2, SECTIONS, rows_a // SECTIONS, hidden), LOW),
        ("wb", (2, chips, 2, SECTIONS, rows_b, cols_b), LOW),
        ("in_a", (1, rows_a, hidden), WIDE),
        ("in_b", (2, rows_b, cols_b), WIDE),
        ("in_n", (1, 2, rows_a), WIDE),
        ("out_a", (rows_a, hidden), WIDE),
        ("out_b", (2, rows_b, cols_b), WIDE),
        ("out_n", (2, rows_a), WIDE),
        ("out_square", (8, LANES), WIDE),
        ("out_output", (length, width), LOW),
        ("out_input", (length, width), WIDE),
        ("cut", (SECTIONS, rows_a // SECTIONS, hidden), LOW),
        ("tiles", (devices, SECTIONS, 8, LANES), WIDE),
        ("x", (4, length, width), LOW),
        ("xt", (4, chips, 2, rows_a, length), LOW),
        ("xtc", (4, chips, rows_a, 2 * length), LOW),
        ("y", (length, width), LOW),
        ("cot", (length, width), LOW),
        ("bias", (length, length), WIDE),
        ("live", (length, 1), WIDE),
        ("f", (length, width), WIDE),
        ("n", (4, length, width), WIDE),
        ("inv", (4, length, 1), WIDE),
        ("q", (2, length, width), LOW),
        ("k", (2, length, width), LOW),
        ("v", (2, length, width), LOW),
        ("kt", (2, width, length), LOW),
        ("vt", (2, width, length), LOW),
        ("ot", (2, chips, 2, rows_a, length), LOW),
        ("otc", (2, chips, rows_a, 2 * length), LOW),
        ("pt", (2, HEADS, length, length), LOW),
        ("g", (2, length, hidden), LOW),
        ("gc", (2, chips, 2 * length, rows_b), LOW),
        ("slope", (2, length, hidden), LOW),
        ("gx", (length, width), WIDE),
        ("gy", (length, width), WIDE),
        ("df", (2, 2 * length, width), LOW),
        ("dft", (2, width, 2 * length), LOW),
        ("dm", (length, width), LOW),
        ("dqt", (width, length), LOW),
        ("dh", (2, 2 * length, hidden), LOW),
        ("dp", (2, 2 * length, 3 * width), LOW),
        ("ng", (devices, 8, width), WIDE),
        ("ns", (SECTIONS, 8, width), WIDE),
        ("sq", (devices, 8, LANES), WIDE),
        ("sqs", (SECTIONS, 8, LANES), WIDE),
        ("sum", (8, LANES), WIDE),
        ("in_s", (5,), None),
        ("out_s", (6,), None),
        ("cut_s", (1,), None),
        ("cut_r", (SECTIONS,), None),
        ("gz_s", (6,), None),
        ("gz_r", (6, chips), None),
        ("gx_s", (6,), None),
        ("gx_r", (6,), None),
        ("gy_s", (6,), None),
        ("gy_r", (6,), None),
        ("rx_s", (6,), None),
        ("rx_r", (6,), None),
        ("ry_s", (6,), None),
        ("ry_r", (6,), None),
        ("gs_s", (6,), None),
        ("gs_r", (6,), None),
        ("small_s", (3, 2), None),
        ("small_r", (3, 2), None),
    )


INPUTS = ("tokens", "cotangent", "lengths", "mat_a", "mat_b", "norms")
OUTPUTS = ("grad_a", "grad_b", "grad_n", "square", "output", "input_grad")


def step_kernel(names, *refs):
    r = types.SimpleNamespace(**dict(zip(names, refs)))
    length, width = r.x.shape[1:]
    hidden = r.wa.shape[-1]
    rows_a, (rows_b, cols_b) = r.mat_a.shape[1], r.mat_b.shape[1:]
    devices = r.tiles.shape[0]
    chips = devices // 2
    half_b = cols_b // 2
    grad_items = gradient_items(rows_a, rows_b, cols_b, width, hidden)
    head = width // HEADS
    scale = head**-0.5

    s, d = lax.axis_index("section"), lax.axis_index("dp")
    z, c = lax.div(d, 2), lax.rem(d, 2)
    sx = s + 1 - 2 * lax.rem(s, 2)
    sy = lax.rem(s + 2, SECTIONS)
    sd = SECTIONS - 1 - s
    to_sibling = {"dp": d + 1 - 2 * c}
    to_up, to_down = {"dp": d + 2}, {"dp": d - 2}
    to_x, to_y = {"section": sx}, {"section": sy}
    below, above = z > 0, z < chips - 1
    group = [{"dp": lax.rem(d + step, devices)} for step in range(1, devices)]
    plane = [{"section": lax.rem(s + step, SECTIONS)} for step in range(1, SECTIONS)]
    finish = []

    def when(condition, work):
        if condition is None:
            work()
        else:
            pl.when(condition)(work)

    def push(source, target, send_sem, recv_sem, device):
        pltpu.make_async_remote_copy(
            src_ref=source,
            dst_ref=target,
            send_sem=send_sem,
            recv_sem=recv_sem,
            device_id=device,
            device_id_type=MESH,
        ).start()

    def arrived(target, sem):
        pltpu.make_async_remote_copy(
            src_ref=target, dst_ref=target, send_sem=sem, recv_sem=sem, device_id=to_x, device_id_type=MESH
        ).wait_recv()

    def sent(source, sem):
        pltpu.make_async_remote_copy(
            src_ref=source, dst_ref=source, send_sem=sem, recv_sem=sem, device_id=to_x, device_id_type=MESH
        ).wait_send()

    def at_end(condition, source, sem):
        finish.append((condition, source, sem))

    def aligned(start, size):
        return pl.ds(pl.multiple_of(start, size), size)

    own_x = pltpu.make_async_copy(r.tokens.at[aligned(s * length, length)], r.x.at[0], r.in_s.at[0])
    own_cot = pltpu.make_async_copy(r.cotangent.at[aligned(s * length, length)], r.cot, r.in_s.at[1])
    own_a = pltpu.make_async_copy(r.mat_a, r.in_a, r.in_s.at[2])
    own_b = pltpu.make_async_copy(r.mat_b, r.in_b, r.in_s.at[3])
    own_n = pltpu.make_async_copy(r.norms, r.in_n, r.in_s.at[4])
    own_a.start()
    own_n.start()
    own_b.start()
    own_x.start()
    own_cot.start()
    barrier = pltpu.get_barrier_semaphore()
    for peer in group + plane:
        pl.semaphore_signal(barrier, inc=1, device_id=peer, device_id_type=MESH)
    own_a.wait()
    r.cut[...] = r.in_a[0].astype(LOW).reshape(SECTIONS, rows_a // SECTIONS, hidden)
    r.wa[s, z, c, s] = r.cut[s]
    own_n.wait()
    norms = r.in_n[0].astype(LOW).astype(WIDE)
    nothing = jnp.zeros((2, rows_a), WIDE)
    even = jnp.concatenate([norms, nothing], axis=1)
    odd = jnp.concatenate([nothing, norms], axis=1)
    r.tiles[d, s, 0:2, :] = jnp.where(c == 0, even, odd)
    r.tiles[d, s, 2:8, :] = jnp.zeros((6, LANES), WIDE)
    own_b.wait()
    for layer in range(2):
        r.wb[layer, z, c, s] = r.in_b[layer].astype(LOW)
    pl.semaphore_wait(barrier, len(group) + len(plane))

    def put_out(slot, source, target):
        made = pltpu.make_async_copy(source, target, r.out_s.at[slot])
        made.start()
        return made

    def small_out(which, source):
        for peer in group:
            push(source, source, r.small_s.at[which, 0], r.small_r.at[which, 0], peer)

    def small_group(which, like):
        arrived(like, r.small_r.at[which, 0])
        sent(like, r.small_s.at[which, 0])

    def small_plane_out(which, source):
        for peer in plane:
            push(source, source, r.small_s.at[which, 1], r.small_r.at[which, 1], peer)

    def small_plane(which, like):
        arrived(like, r.small_r.at[which, 1])
        sent(like, r.small_s.at[which, 1])

    every = slice(None)

    def block(item, chip, section):
        if item < 4:
            return r.wa.at[item, chip, c, section]
        return r.wb.at[item - 4, chip, c, section]

    def half_block(item, section, half):
        if item < 4:
            return r.wa.at[item, :, c, section, :, pl.ds(half * hidden // 2, hidden // 2)]
        rows = pl.ds(half * rows_b // 2, rows_b // 2)
        return r.wb.at[item - 4, :, c, section, rows]

    def half_piece(item, section, half):
        rows = pl.ds(half * rows_b // 2, rows_b // 2)
        return r.wb.at[item - 4, z, c, section, rows]

    def core_blocks(item, core):
        return r.wa.at[item, :, core] if item < 4 else r.wb.at[item - 4, :, core]

    def cut_out():
        for section, device in ((sd, {"section": sd}), (sx, to_x), (sy, to_y)):
            push(r.cut.at[section], r.wa.at[s, z, c, section], r.cut_s.at[0], r.cut_r.at[s], device)
        at_end(None, r.cut.at[pl.ds(0, SECTIONS - 1)], r.cut_s.at[0])

    def cut_in():
        for section in (sx, sy, sd):
            arrived(r.wa.at[section, z, c, s], r.cut_r.at[section])

    def line_out(item):
        if item in ROWS_FIRST:
            rows_out(item)
            return
        own = block(item, z, s)
        for step in range(1, chips):
            push(own, own, r.gz_s.at[item], r.gz_r.at[item, z], {"dp": 2 * lax.rem(z + step, chips) + c})
        several = block(item, pl.ds(0, chips - 1), s)
        at_end(None, several, r.gz_s.at[item])

    def plane_out(item, chip):
        own = block(item, chip, s)
        push(own, own, r.gx_s.at[item], r.gx_r.at[item], to_x)
        push(own, own, r.gy_s.at[item], r.gy_r.at[item], to_y)

    def rows_out(item):
        arrived(half_piece(item, sd, 0), r.rx_r.at[item])
        arrived(half_piece(item, sd, 1), r.ry_r.at[item])
        rows = r.wb.at[item - 4, z, c]
        for step in range(1, chips):
            push(rows, rows, r.gz_s.at[item], r.gz_r.at[item, z], {"dp": 2 * lax.rem(z + step, chips) + c})
        push(rows, rows, r.gs_s.at[item], r.gs_r.at[item], to_sibling)
        at_end(None, r.wb.at[item - 4, pl.ds(0, chips - 1), c], r.gz_s.at[item])

    def rows_in(item):
        for step in range(1, chips):
            chip = lax.rem(z + step, chips)
            rows = r.wb.at[item - 4, chip, c]
            arrived(rows, r.gz_r.at[item, chip])
            push(rows, rows, r.gs_s.at[item], r.gs_r.at[item], to_sibling)
        at_end(None, core_blocks(item, c), r.gs_s.at[item])

    def line_in(item):
        if item in ROWS_FIRST:
            rows_in(item)
            return
        for step in range(1, chips):
            chip = lax.rem(z + step, chips)
            arrived(block(item, chip, s), r.gz_r.at[item, chip])
            plane_out(item, chip)
        core_out(item, s)
        at_end(None, block(item, every, s), r.gx_s.at[item])
        at_end(None, block(item, every, s), r.gy_s.at[item])

    def core_out(item, section):
        blocks = block(item, every, section)
        push(blocks, blocks, r.gs_s.at[item], r.gs_r.at[item], to_sibling)

    def plane_in(item):
        over = z if item in ROWS_FIRST else every
        piece = half_piece if item in ROWS_FIRST else half_block
        arrived(block(item, over, sx), r.gx_r.at[item])
        part = piece(item, sx, 1)
        push(part, part, r.ry_s.at[item], r.ry_r.at[item], to_y)
        arrived(block(item, over, sy), r.gy_r.at[item])
        part = piece(item, sy, 0)
        push(part, part, r.rx_s.at[item], r.rx_r.at[item], to_x)
        if item in ROWS_FIRST:
            at_end(None, block(item, z, sx), r.gx_s.at[item])
            at_end(None, block(item, z, sx), r.gy_s.at[item])
        else:
            core_out(item, sx)
            core_out(item, sy)
        at_end(None, part, r.ry_s.at[item])
        at_end(None, part, r.rx_s.at[item])

    def far_in(item):
        arrived(half_block(item, sd, 0), r.rx_r.at[item])
        arrived(half_block(item, sd, 1), r.ry_r.at[item])
        core_out(item, sd)
        at_end(None, core_blocks(item, c), r.gs_s.at[item])

    def core_in(item):
        arrived(core_blocks(item, 1 - c), r.gs_r.at[item])

    mine, other = pl.ds(0, length), pl.ds(length, length)

    def give(slot, source, target):
        push(source, target, r.fac_s.at[slot], r.fac_r.at[slot], to_sibling)
        at_end(None, target, r.fac_s.at[slot])

    def taken(slot, target):
        arrived(target, r.fac_r.at[slot])

    def give_rows(layer):
        r.xt[layer] = r.x[layer].T.reshape(chips, 2, rows_a, length)
        r.xtc[layer, :, :, 0:length] = r.xt[layer, :, c]
        give(layer, r.xt.at[layer, :, 1 - c], r.xtc.at[layer, :, :, other])

    def product(left, right, dims):
        return lax.dot_general(left, right, (dims, ((), ())), preferred_element_type=WIDE)

    def loop(count, work):
        def one(index, carry):
            work(index)
            return carry

        lax.fori_loop(0, count, one, 0)

    def gain_row(layer, kind):
        parts = [
            r.tiles[2 * chip, layer, kind : kind + 1, :] + r.tiles[2 * chip + 1, layer, kind : kind + 1, :]
            for chip in range(chips)
        ]
        return jnp.concatenate(parts, axis=1)

    def stats(value):
        centre = value - jnp.mean(value, -1, keepdims=True)
        inverse = lax.rsqrt(jnp.mean(centre * centre, -1, keepdims=True) + EPSILON)
        return centre * inverse, inverse

    lane = lax.broadcasted_iota(jnp.int32, (1, 2 * head), 1)
    first_half = (lane < head).astype(WIDE)
    half_masks = (first_half.astype(LOW), (1.0 - first_half).astype(LOW))

    def prepare_masks():
        ends, total = [], jnp.int32(0)
        for slot in range(r.lengths.shape[1]):
            total = total + r.lengths[s, slot]
            ends.append(total)
        down_places = lax.broadcasted_iota(jnp.int32, (length, 1), 0)
        across_places = lax.broadcasted_iota(jnp.int32, (1, length), 1)
        down_segment = jnp.zeros((length, 1), jnp.int32)
        across_segment = jnp.zeros((1, length), jnp.int32)
        for end in ends:
            down_segment = down_segment + (end <= down_places).astype(jnp.int32)
            across_segment = across_segment + (end <= across_places).astype(jnp.int32)
        r.bias[...] = jnp.where(down_segment == across_segment, 0.0, NEGATIVE)
        r.live[...] = (down_places < total).astype(WIDE)

    def matrix(layer, place):
        value = r.wa[layer, :, :, :, :, place]
        return value.reshape(width, value.shape[-1])

    def down(at, chip=slice(None)):
        blocks = [r.wb[at, chip, :, section] for section in range(SECTIONS)]
        return jnp.concatenate([block.reshape(-1, cols_b) for block in blocks], axis=1)

    def attention_in(layer):
        at = layer // 2
        rows = r.x[layer]
        r.q[at] = product(rows, matrix(layer, pl.ds(0, width)), NN).astype(LOW) * jnp.asarray(scale, LOW)
        keys = product(rows, matrix(layer, pl.ds(width, width)), NN).astype(LOW)
        r.k[at] = keys
        values = product(rows, matrix(layer, pl.ds(2 * width, width)), NN).astype(LOW)
        r.v[at] = values
        r.vt[at] = values.T

    def attention_heads(layer, begin, count):
        at = layer // 2

        def pair(index):
            lanes = aligned(index * 2 * head, 2 * head)
            for which in range(2):
                scores = product(r.k[at, :, lanes], r.q[at, :, lanes] * half_masks[which], NT) + r.bias[...]
                weights = jnp.exp(scores - jnp.max(scores, 0, keepdims=True))
                probs = (weights * (1.0 / jnp.sum(weights, 0, keepdims=True))).astype(LOW)
                r.pt[at, 2 * index + which] = probs
                place = aligned((2 * index + which) * head, head)
                r.ot[at, index, which] = product(r.vt[at, place, :], probs, NN).astype(LOW)

        for index in range(begin, begin + count):
            pair(index)

    def attention_out(layer):
        at = layer // 2
        r.otc[at, :, :, 0:length] = r.ot[at, :, c]
        give(4 + at, r.ot.at[at, :, 1 - c], r.otc.at[at, :, :, other])
        r.f[...] = product(r.ot[at].reshape(width, length).T, matrix(layer, pl.ds(3 * width, width)), NN)

    def expand(layer, index):
        at = layer // 2
        place = pl.ds(index * width, width)
        pre = product(r.x[layer], matrix(layer, place), NN)
        squared = pre * pre
        slope = 0.7978845608 * (1.0 + 3 * 0.044715 * squared)
        bent = jnp.tanh(0.7978845608 * pre * (1.0 + 0.044715 * squared))
        r.g[at, :, place] = (0.5 * pre * (1.0 + bent)).astype(LOW)
        r.slope[at, :, place] = (0.5 * (1.0 + bent) + 0.5 * pre * (1.0 - bent * bent) * slope).astype(LOW)
        block = aligned((2 * index + c) * rows_b, rows_b)
        r.gc[at, index, 0:length, :] = r.g[at, :, block]
        block = aligned((2 * index + 1 - c) * rows_b, rows_b)
        give(6 + chips * at + index, r.g.at[at, :, block], r.gc.at[at, index, other, :])

    def contract(layer):
        r.f[...] = product(r.g[layer // 2], down(layer // 2), NN)

    def by_rows(work):
        for index in range(length // BLOCK):
            work(pl.ds(index * BLOCK, BLOCK))

    def normalize(layer):
        gain, offset = gain_row(layer, 0), gain_row(layer, 1)

        def some(rows):
            branch = r.f[rows, :]
            normal, inverse = stats(r.x[layer, rows, :].astype(WIDE) + branch)
            r.n[layer, rows, :] = normal
            r.inv[layer, rows, :] = inverse
            out = normal * gain + offset
            dual = branch if layer == 0 else r.y[rows, :].astype(WIDE) + branch
            if layer < 3:
                r.x[layer + 1, rows, :] = out.astype(LOW)
                r.y[rows, :] = dual.astype(LOW)
            else:
                dual_normal, dual_inverse = stats(dual)
                r.out_output[rows, :] = (out + dual_normal).astype(LOW)
                pull = r.cot[rows, :].astype(WIDE) * r.live[rows, :]
                r.gx[rows, :] = pull
                r.gy[rows, :] = norm_back(dual_normal, dual_inverse, pull)

        by_rows(some)

    def back_normalize(layer):
        gain = gain_row(layer, 0)

        def some(index, sums):
            rows = pl.ds(index * BLOCK, BLOCK)
            upstream = r.gx[rows, :]
            normal = r.n[layer, rows, :]
            summed = norm_back(normal, r.inv[layer, rows, :], upstream * gain)
            dual = r.gy[rows, :]
            r.gx[rows, :] = summed
            r.df[layer // 2, rows, :] = (summed + dual).astype(LOW)
            if layer == 3:
                r.gy[rows, :] = dual.astype(LOW).astype(WIDE)
            return (
                sums[0] + jnp.sum(upstream * normal, 0, keepdims=True),
                sums[1] + jnp.sum(upstream, 0, keepdims=True),
            )

        zero = jnp.zeros((1, width), WIDE)
        gains, offsets = zero, zero
        for index in range(length // BLOCK):
            gains, offsets = some(index, (gains, offsets))
        r.ng[d, 2 * layer : 2 * layer + 1, :] = gains
        r.ng[d, 2 * layer + 1 : 2 * layer + 2, :] = offsets

    def pass_down(layer, inner):
        total = r.gx[...] + inner
        if layer > 0:
            r.gx[...] = total.astype(LOW).astype(WIDE)
        else:
            r.out_input[...] = total

    base = 6 + 2 * chips

    def back_hidden(layer):
        at = layer // 2
        r.dft[at, :, 0:length] = r.df[at, 0:length, :].T
        give(base + at, r.dft.at[at, :, mine], r.dft.at[at, :, other])
        for index in range(hidden // width):
            place = pl.ds(index * width, width)
            pulled = product(r.df[at, 0:length, :], down(at, pl.ds(index, 1)), NT)
            r.dh[at, 0:length, place] = (pulled * r.slope[at, :, place].astype(WIDE)).astype(LOW)
            give(base + 2 + chips * at + index, r.dh.at[at, mine, place], r.dh.at[at, other, place])

    def back_expand_end(layer):
        pass_down(layer, product(r.dh[layer // 2, 0:length, :], matrix(layer, pl.ds(0, hidden)), NT))

    def back_output(layer):
        at = layer // 2
        give(base + 2 + 2 * chips + at, r.df.at[at, mine], r.df.at[at, other])
        r.dm[...] = product(r.df[at, 0:length, :], matrix(layer, pl.ds(3 * width, width)), NT).astype(LOW)
        r.kt[at] = (r.k[at] * jnp.asarray(scale, LOW)).T

    def back_heads(layer, begin, count):
        at = layer // 2

        def pair(index):
            lanes = aligned(index * 2 * head, 2 * head)
            pulled = r.dm[:, lanes]
            keys, values = [], []
            for which in range(2):
                probs = r.pt[at, 2 * index + which]
                grad = product(r.v[at, :, lanes], pulled * half_masks[which], NT)
                full = probs.astype(WIDE)
                centre = jnp.sum(full * grad, 0, keepdims=True)
                scores = (full * (grad - centre)).astype(LOW)
                keys.append(product(scores, r.q[at, :, lanes], NN))
                values.append(product(probs, pulled, NN))
                place = aligned((2 * index + which) * head, head)
                r.dqt[place, :] = product(r.kt[at, place, :], scores, NN).astype(LOW)
            r.dp[at, 0:length, aligned(width + index * 2 * head, 2 * head)] = jnp.where(
                lane < head, keys[0], keys[1]
            ).astype(LOW)
            r.dp[at, 0:length, aligned(2 * width + index * 2 * head, 2 * head)] = jnp.where(
                lane < head, values[0], values[1]
            ).astype(LOW)

        def pairs(step):
            pair(begin + 2 * step)
            pair(begin + 2 * step + 1)

        loop(count // 2, pairs)

    def back_packed(layer):
        at = layer // 2
        slot = base + 4 + 2 * chips + 2 * at
        place = pl.ds(width, 2 * width)
        give(slot, r.dp.at[at, mine, place], r.dp.at[at, other, place])
        r.dp[at, 0:length, 0:width] = r.dqt[...].T
        place = pl.ds(0, width)
        give(slot + 1, r.dp.at[at, mine, place], r.dp.at[at, other, place])

    def back_packed_end(layer):
        pass_down(layer, product(r.dp[layer // 2, 0:length, :], matrix(layer, pl.ds(0, 3 * width)), NT))

    def keep(name, half, place, value):
        own = getattr(r, "own" + name)
        own[:, :, half, :, place] = value.astype(LOW).reshape(chips, SECTIONS, rows_a // SECTIONS, value.shape[1])

    def chip_rows(value):
        return value.reshape(chips * rows_a, 2 * length)

    def grad_down(at):
        own = getattr(r, "ownB%d" % at)
        taken(base + at, r.dft.at[at, :, other])
        for chip in range(chips):
            taken(6 + chips * at + chip, r.gc.at[at, chip, other, :])
            value = product(r.dft[at], r.gc[at, chip], NN)
            own[chip] = value.astype(LOW).reshape(SECTIONS, 2, half_b, rows_b)

    def grad_up(layer):
        at = layer // 2
        taken(layer, r.xtc.at[layer, :, :, other])
        for index in range(hidden // width):
            place = pl.ds(index * width, width)
            taken(base + 2 + chips * at + index, r.dh.at[at, other, place])
            value = product(chip_rows(r.xtc[layer]), r.dh[at, :, place], NN)
            keep("F%d" % layer, index // 2, pl.ds(index % 2 * width, width), value)

    def grad_output(layer):
        at = layer // 2
        taken(4 + at, r.otc.at[at, :, :, other])
        taken(base + 2 + 2 * chips + at, r.df.at[at, other])
        for half in range(2):
            place = pl.ds(half * width // 2, width // 2)
            value = product(chip_rows(r.otc[at]), r.df[at, :, place], NN)
            keep("O%d" % layer, half, pl.ds(0, width // 2), value)

    def grad_packed(layer):
        at = layer // 2
        slot = base + 4 + 2 * chips + 2 * at
        taken(layer, r.xtc.at[layer, :, :, other])
        taken(slot, r.dp.at[at, other, pl.ds(width, 2 * width)])
        taken(slot + 1, r.dp.at[at, other, pl.ds(0, width)])
        part = 3 * width // 2
        for half in range(2):
            value = product(chip_rows(r.xtc[layer]), r.dp[at, :, half * part : (half + 1) * part], NN)
            keep("K%d" % layer, half, pl.ds(0, part), value)

    def joined(target, others):
        return functools.reduce(
            lambda left, right: left + right, [ref[...].astype(WIDE) for ref in (target, *others)]
        )

    def add_into(target, others):
        if len(others) < 3:
            target[...] = functools.reduce(lambda left, right: left + right, [ref[...] for ref in (target, *others)])
        else:
            target[...] = joined(target, others).astype(LOW)

    places = {name: place for place, (name, _, _, _) in enumerate(grad_items)}

    def buffers(name):
        parts = ("own", "farx", "fary", "nearx", "neary", "line", "done")
        return types.SimpleNamespace(**{part: getattr(r, part + name) for part in parts})

    def to_plane(name):
        item, place = buffers(name), places[name]

        def over_x(section, half, target, slot):
            push(item.own.at[:, section, half], target, r.px_s.at[place, slot], r.px_r.at[place, slot], to_x)
            at_end(None, item.farx, r.px_s.at[place, slot])

        def over_y(section, half, target, slot):
            push(item.own.at[:, section, half], target, r.py_s.at[place, slot], r.py_r.at[place, slot], to_y)
            at_end(None, item.farx, r.py_s.at[place, slot])

        over_x(sd, 0, item.farx, 2)
        over_y(sd, 1, item.fary, 2)
        over_x(sx, 0, item.nearx.at[0], 0)
        over_y(sy, 1, item.neary.at[1], 1)

    def through_plane(name):
        item, place = buffers(name), places[name]
        own = item.own
        arrived(item.fary, r.py_r.at[place, 2])
        add_into(own.at[:, sx, 1], [item.fary])
        push(own.at[:, sx, 1], item.nearx.at[1], r.px_s.at[place, 1], r.px_r.at[place, 1], to_x)
        at_end(None, item.farx, r.px_s.at[place, 1])
        arrived(item.farx, r.px_r.at[place, 2])
        add_into(own.at[:, sy, 0], [item.farx])
        push(own.at[:, sy, 0], item.neary.at[0], r.py_s.at[place, 0], r.py_r.at[place, 0], to_y)
        at_end(None, item.farx, r.py_s.at[place, 0])

    def to_line(name):
        item, place = buffers(name), places[name]
        own = item.own.at[:, s]
        for half in range(2):
            arrived(item.nearx.at[half], r.px_r.at[place, half])
            arrived(item.neary.at[half], r.py_r.at[place, half])
            add_into(own.at[:, half], [item.nearx.at[half], item.neary.at[half]])
        for step in range(1, chips):
            chip = lax.rem(z + step, chips)
            push(
                own.at[chip],
                item.line.at[z],
                r.line_s.at[place, step],
                r.line_r.at[place, z],
                {"dp": 2 * chip + c},
            )
            at_end(None, item.line.at[0], r.line_s.at[place, step])

    def to_owner(name):
        item, place = buffers(name), places[name]
        others = [lax.rem(z + step, chips) for step in range(1, chips)]
        for chip in others:
            arrived(item.line.at[chip], r.line_r.at[place, chip])
        total = joined(item.own.at[z, s], [item.line.at[chip] for chip in others])
        square = total * total
        while square.ndim > 2:
            square = jnp.sum(square, 0)
        square = jnp.sum(jnp.sum(square, 0, keepdims=True), 1, keepdims=True)
        r.sum[...] = r.sum[...] + jnp.broadcast_to(square, (8, LANES))
        if name[0] == "B":
            item.done[...] = total
            return
        item.done[s] = total.astype(LOW)
        layer = grad_items[place][1]
        mine = item.done.at[s]
        away = s != layer
        when(
            away,
            lambda: push(mine, mine, r.done_s.at[place], r.done_r.at[place, s], {"section": jnp.int32(layer)}),
        )
        at_end(away, mine, r.done_s.at[place])

    def collect(name):
        item, place = buffers(name), places[name]
        layer = grad_items[place][1]

        def work():
            for section in range(SECTIONS):
                if section != layer:
                    arrived(item.done.at[section], r.done_r.at[place, section])
            columns = item.done.shape[-1]
            start = 3 * width if name[0] == "O" else 0
            for section in range(SECTIONS):
                for half in range(2):
                    rows = pl.ds(section * (rows_a // SECTIONS), rows_a // SECTIONS)
                    place_to = pl.ds(start + half * columns, columns)
                    r.out_a[rows, place_to] = item.done[section, half].astype(WIDE)

        when(s == layer, work)

    def all_sent(count=None):
        for condition, source, sem in finish[:count]:
            when(condition, functools.partial(sent, source, sem))
        del finish[:count]

    cut_out()
    small_out(0, r.tiles.at[d, s])
    plane_out(5, z)
    line_out(4)
    plane_out(4, z)
    cut_in()
    plane_out(1, z)
    line_out(0)
    plane_out(0, z)
    line_out(1)
    line_out(2)
    plane_out(3, z)
    line_out(3)
    line_in(4)
    small_group(0, r.tiles.at[pl.ds(0, devices - 1), 0])
    for peer in plane:
        push(r.tiles.at[:, s], r.tiles.at[:, s], r.small_s.at[0, 1], r.small_r.at[0, 1], peer)
    line_in(0)
    plane_in(5)
    line_in(1)
    plane_in(0)
    plane_out(2, z)
    plane_in(1)
    far_in(0)
    line_in(2)
    plane_in(4)
    line_out(5)
    own_x.wait()
    own_cot.wait()
    prepare_masks()
    give_rows(0)
    core_in(0)
    attention_in(0)
    far_in(1)
    attention_heads(0, 0, 2)
    attention_heads(0, 2, 2)
    plane_in(2)
    attention_out(0)
    small_plane(0, r.tiles.at[:, pl.ds(0, SECTIONS - 1)])
    normalize(0)
    far_in(4)
    core_in(1)
    line_in(3)
    expand(1, 0)
    expand(1, 1)
    early = len(finish)
    far_in(2)
    expand(1, 2)
    expand(1, 3)
    core_in(4)
    contract(1)
    normalize(1)
    core_in(2)
    plane_in(3)
    attention_in(2)
    attention_heads(2, 0, 2)
    attention_heads(2, 2, 2)
    far_in(3)
    attention_out(2)
    line_in(5)
    normalize(2)
    core_in(3)
    expand(3, 0)
    expand(3, 1)
    expand(3, 2)
    expand(3, 3)
    all_sent(early)
    core_in(5)
    contract(3)
    normalize(3)
    leaving = [put_out(0, r.out_output, r.output)]

    r.sum[...] = jnp.zeros((8, LANES), WIDE)
    back_normalize(3)
    back_hidden(3)
    give_rows(3)
    back_expand_end(3)
    back_normalize(2)
    grad_up(3)
    to_plane("F3")
    back_output(2)
    grad_down(1)
    to_plane("B1")
    back_heads(2, 0, 2)
    back_heads(2, 2, 2)
    back_packed(2)
    through_plane("B1")
    give_rows(2)
    grad_output(2)
    back_packed_end(2)
    give_rows(1)
    to_plane("O2")
    grad_packed(2)
    to_plane("K2")
    back_normalize(1)
    back_hidden(1)
    through_plane("K2")
    grad_down(0)
    to_plane("B0")
    back_expand_end(1)
    back_normalize(0)
    small_out(1, r.ng.at[d])
    to_line("K2")
    to_line("B1")
    back_output(0)
    grad_up(1)
    through_plane("B0")
    to_plane("F1")
    back_heads(0, 0, 2)
    back_heads(0, 2, 2)
    back_packed(0)
    to_line("B0")
    through_plane("O2")
    through_plane("F1")
    grad_output(0)
    to_plane("O0")
    grad_packed(0)
    to_plane("K0")
    to_line("O2")
    to_line("F1")
    through_plane("O0")
    to_owner("B1")
    back_packed_end(0)
    leaving.append(put_out(1, r.out_input, r.input_grad))
    to_owner("B0")
    all_sent(len(finish) // 3)
    through_plane("K0")
    small_group(1, r.ng.at[pl.ds(0, devices - 1)])
    r.ns[s] = functools.reduce(lambda left, right: left + right, [r.ng[index] for index in range(devices)])
    small_plane_out(1, r.ns.at[s])
    through_plane("F3")
    to_line("O0")
    all_sent(len(finish) // 3)
    to_line("K0")
    to_owner("F1")
    to_line("F3")
    to_owner("O2")
    to_owner("K2")
    to_owner("F3")
    to_owner("O0")
    all_sent(len(finish) // 3)
    to_owner("K0")

    r.sq[d] = r.sum[...]
    small_out(2, r.sq.at[d])
    for name in ("F1", "O2", "K2", "F3"):
        collect(name)
    collect("O0")
    for layer in range(2):
        done = buffers("B%d" % layer).done
        r.out_b[layer] = done[...].reshape(cols_b, rows_b).T
    leaving.append(put_out(2, r.out_b, r.grad_b))
    small_plane(1, r.ns.at[pl.ds(0, SECTIONS - 1)])
    grads = functools.reduce(lambda left, right: left + right, [r.ns[index] for index in range(SECTIONS)])
    norm_square = jnp.sum(jnp.sum(grads * grads, 0, keepdims=True), 1, keepdims=True)
    chosen = jnp.zeros((2, width), WIDE)
    for layer in range(4):
        chosen = jnp.where(s == layer, grads[2 * layer : 2 * layer + 2, :], chosen)
    shard = jnp.zeros((2, rows_a), WIDE)
    for chip in range(chips):
        pair_of = chosen[:, chip * LANES : (chip + 1) * LANES]
        shard = jnp.where(z == chip, jnp.where(c == 0, pair_of[:, :rows_a], pair_of[:, rows_a:]), shard)
    r.out_n[...] = shard
    leaving.append(put_out(3, r.out_n, r.grad_n))
    collect("K0")
    leaving.append(put_out(4, r.out_a, r.grad_a))
    small_group(2, r.sq.at[pl.ds(0, devices - 1)])
    r.sqs[s] = functools.reduce(lambda left, right: left + right, [r.sq[index] for index in range(devices)])
    small_plane_out(2, r.sqs.at[s])
    all_sent()
    small_plane(2, r.sqs.at[pl.ds(0, SECTIONS - 1)])
    squares = functools.reduce(lambda left, right: left + right, [r.sqs[index] for index in range(SECTIONS)])
    r.out_square[...] = squares + norm_square
    leaving.append(put_out(5, r.out_square, r.square))
    for made in leaving:
        made.wait()


def step_call(tokens, cotangent, lengths, mat_a, mat_b, norms):
    rows_a, hidden = mat_a.shape[1:]
    rows_b, cols_b = mat_b.shape[1:]
    width = tokens.shape[1]
    length = tokens.shape[0] // lengths.shape[0]
    chips = width // rows_a // 2
    scratch = kernel_scratch(chips, rows_a, rows_b, cols_b, length, width, hidden)
    shapes = []
    for _, shape, kind in scratch:
        shapes.append(pltpu.SemaphoreType.DMA(shape) if kind is None else pltpu.VMEM(shape, kind))
    anywhere = pl.BlockSpec(memory_space=pl.ANY)
    return pl.pallas_call(
        functools.partial(step_kernel, INPUTS + OUTPUTS + tuple(name for name, _, _ in scratch)),
        out_shape=(
            jax.ShapeDtypeStruct((rows_a, hidden), WIDE),
            jax.ShapeDtypeStruct(mat_b.shape, WIDE),
            jax.ShapeDtypeStruct((2, rows_a), WIDE),
            jax.ShapeDtypeStruct((8, LANES), WIDE),
            jax.ShapeDtypeStruct((length, width), LOW),
            jax.ShapeDtypeStruct((length, width), WIDE),
        ),
        in_specs=[anywhere, anywhere, pl.BlockSpec(memory_space=pltpu.SMEM), anywhere, anywhere, anywhere],
        out_specs=[anywhere] * len(OUTPUTS),
        scratch_shapes=shapes,
        compiler_params=pltpu.CompilerParams(
            collective_id=0, has_side_effects=True, vmem_limit_bytes=KERNEL_VMEM
        ),
    )(tokens, cotangent, lengths, mat_a, mat_b, norms)


def update_kernel(*refs):
    inputs, outputs, held, made, sems = refs[:15], refs[15:33], refs[33:48], refs[48:63], refs[63]
    started = []

    def copy(source, target):
        one = pltpu.make_async_copy(source, target, sems.at[len(started)])
        one.start()
        started.append(one)
        return one

    half = inputs[4].shape[1] // 2
    parts = [(0, pl.ds(0, half)), (0, pl.ds(half, half)), (1, slice(None)), (2, slice(None))]
    rates = ((MATRIX_RATE, MATRIX_DECAY), (MATRIX_RATE, MATRIX_DECAY), (NORM_RATE, 0.0))
    norm_in = copy(inputs[0], held[0])
    coming = []
    for group, rows in parts:
        coming.append(
            [copy(inputs[at].at[:, rows], held[at].at[:, rows]) for at in range(3 + 4 * group, 7 + 4 * group)]
        )
    passing = [copy(inputs[at], held[at]) for at in (1, 2)]
    norm_in.wait()
    grad_norm = jnp.sqrt(held[0][0:1, 0:1])
    factor = CLIP_NORM / jnp.maximum(grad_norm, CLIP_NORM)
    outputs[0][...] = grad_norm
    leaving = []
    for (group, rows), waits in zip(parts, coming):
        for one in waits:
            one.wait()
        grad, weight, one, two = (held[at][:, rows] for at in range(3 + 4 * group, 7 + 4 * group))
        clip = grad * factor
        moment, square, master = adam_update(weight, one, two, clip, *rates[group])
        for kind, value in enumerate((clip, moment, square, master, master.astype(LOW))):
            buffer = made[5 * group + kind]
            buffer[:, rows] = value
            leaving.append(copy(buffer.at[:, rows], outputs[3 + 5 * group + kind].at[:, rows]))
        if passing:
            at = 3 - len(passing)
            passing.pop(0).wait()
            leaving.append(copy(held[at], outputs[at].at[0]))
    for one in leaving:
        one.wait()


def kernel_body(
    tokens, cotangent, lengths, mat_a, mat_b, norms, first_a, second_a, first_b, second_b, first_n, second_n
):
    norms, first_n, second_n = (jnp.swapaxes(value, 1, 2) for value in (norms, first_n, second_n))
    grad_a, grad_b, grad_n, square, output, input_grad = step_call(
        tokens, cotangent, lengths, mat_a, mat_b, norms
    )
    args = (square, output, input_grad, grad_a[None], mat_a, first_a, second_a, grad_b, mat_b, first_b, second_b)
    args += (grad_n[None], norms, first_n, second_n)
    anywhere, vmem = pl.BlockSpec(memory_space=pl.ANY), pl.BlockSpec(memory_space=pltpu.VMEM)
    shapes = [jax.ShapeDtypeStruct((1, 1), WIDE)]
    shapes += [jax.ShapeDtypeStruct((1,) + value.shape, value.dtype) for value in (output, input_grad)]
    for value in (mat_a, mat_b, norms):
        shapes += [jax.ShapeDtypeStruct(value.shape, kind) for kind in (WIDE, WIDE, WIDE, WIDE, LOW)]
    scratch = [pltpu.VMEM(value.shape, value.dtype) for value in (*args, *shapes[3:])]
    results = pl.pallas_call(
        update_kernel,
        out_shape=shapes,
        in_specs=[anywhere] * len(args),
        out_specs=[vmem] + [anywhere] * (len(shapes) - 1),
        scratch_shapes=scratch + [pltpu.SemaphoreType.DMA((48,))],
        compiler_params=pltpu.CompilerParams(vmem_limit_bytes=KERNEL_VMEM),
    )(*args)
    results = [results[0][0, 0], *results[1:]]
    results[-5:] = [jnp.swapaxes(value, 1, 2) for value in results[-5:]]
    return tuple(results)


def chosen_body(*args):
    rows_a = args[3].shape[1]
    groups = lax.axis_size("dp")
    by_kernel = rows_a % 32 == 0 and 2 * rows_a == LANES and groups * rows_a == args[0].shape[1]
    return (kernel_body if by_kernel else body)(*args)


def solution(mesh):
    placed = (
        P("dp", None),
        P("dp", None),
        P("dp", None),
        P("section", "dp", None),
        P(None, "dp", "section"),
        P("section", "dp", None),
        P("section", "dp", None),
        P("section", "dp", None),
        P(None, "dp", "section"),
        P(None, "dp", "section"),
        P("section", "dp", None),
        P("section", "dp", None),
    )
    return jax.shard_map(
        chosen_body,
        mesh=mesh,
        in_specs=placed,
        out_specs=(
            P(),
            P("section", "dp", None),
            P("section", "dp", None),
            P("section", "dp", None),
            P("section", "dp", None),
            P("section", "dp", None),
            P("section", "dp", None),
            P("section", "dp", None),
            P(None, "dp", "section"),
            P(None, "dp", "section"),
            P(None, "dp", "section"),
            P(None, "dp", "section"),
            P(None, "dp", "section"),
            P("section", "dp", None),
            P("section", "dp", None),
            P("section", "dp", None),
            P("section", "dp", None),
            P("section", "dp", None),
        ),
        check_vma=False,
    )
```

```python
import functools
import types

import jax
import jax.numpy as jnp
from jax import lax
from jax.experimental import pallas as pl
from jax.experimental.pallas import tpu as pltpu
from jax.sharding import PartitionSpec as P

HEADS = 8
STEP = 5


EPSILON = 1e-05
NEGATIVE = -1e30
CLIP_NORM = 1.0
BETA_ONE = 0.5
BETA_TWO = 0.5
ADAM_EPSILON = 1e-08
MATRIX_RATE = 0.05
NORM_RATE = 0.5
MATRIX_DECAY = 0.01


def norm_stats(value):
    centre = value - jnp.mean(value, -1, keepdims=True)
    inverse = lax.rsqrt(jnp.mean(centre * centre, -1, keepdims=True) + EPSILON)
    return (centre * inverse, inverse)


def norm_back(normal, inverse, upstream):
    return inverse * (
        upstream
        - jnp.mean(upstream, -1, keepdims=True)
        - normal * jnp.mean(upstream * normal, -1, keepdims=True)
    )


def adam_update(weight, moment_one, moment_two, gradient, step_rate, decay_rate):
    first_new = BETA_ONE * moment_one + (1.0 - BETA_ONE) * gradient
    second_new = BETA_TWO * moment_two + (1.0 - BETA_TWO) * gradient * gradient
    first_hat = first_new / (1.0 - BETA_ONE**STEP)
    second_hat = second_new / (1.0 - BETA_TWO**STEP)
    weight_new = weight - step_rate * (
        first_hat / (jnp.sqrt(second_hat) + ADAM_EPSILON) + decay_rate * weight
    )
    return (first_new, second_new, weight_new)


def segments_of(lengths_row, length):
    ends = jnp.cumsum(lengths_row, dtype=jnp.int32)
    places = jnp.arange(length, dtype=jnp.int32)
    segment = jnp.sum((ends[None, :] <= places[:, None]).astype(jnp.int32), axis=1, dtype=jnp.int32)
    live = (places < ends[-1]).astype(jnp.float32)
    return segment, live


def matmul(left, right, dims):
    return lax.dot_general(left, right, (dims, ((), ())), preferred_element_type=jnp.float32)


NN = ((1,), (0,))
NT = ((1,), (1,))
TN = ((0,), (0,))


def attention_forward(stream, weight, mask):
    length, width = stream.shape
    size = width // HEADS
    packed = matmul(stream, weight[:, : 3 * width], NN).astype(jnp.bfloat16)
    heads = packed.reshape(length, 3, HEADS, size)
    scores = jnp.einsum("qhd,khd->hqk", heads[:, 0], heads[:, 1], preferred_element_type=jnp.float32)
    scores = jnp.where(mask[None], scores * size**-0.5, NEGATIVE)
    weights = jnp.exp(scores - jnp.max(scores, -1, keepdims=True))
    probs = weights / jnp.sum(weights, -1, keepdims=True)
    mixed = jnp.einsum("hqk,khd->qhd", probs.astype(jnp.bfloat16), heads[:, 2], preferred_element_type=jnp.float32)
    mixed = mixed.reshape(length, width).astype(jnp.bfloat16)
    branch = matmul(mixed, weight[:, 3 * width :], NN)
    return branch, (heads, probs, mixed)


def attention_backward(stream, weight, kept, grad_low):
    heads, probs, mixed = kept
    length, width = stream.shape
    size = width // HEADS
    grad_out = matmul(mixed, grad_low, TN)
    grad_mixed = matmul(grad_low, weight[:, 3 * width :], NT).astype(jnp.bfloat16)
    grad_mixed = grad_mixed.reshape(length, HEADS, size)
    grad_probs = jnp.einsum("qhd,khd->hqk", grad_mixed, heads[:, 2], preferred_element_type=jnp.float32)
    centre = jnp.sum(probs * grad_probs, -1, keepdims=True)
    grad_scores = (probs * (grad_probs - centre)).astype(jnp.bfloat16)
    low = probs.astype(jnp.bfloat16)
    scale = size**-0.5
    grad_q = jnp.einsum("hqk,khd->qhd", grad_scores, heads[:, 1], preferred_element_type=jnp.float32) * scale
    grad_k = jnp.einsum("hqk,qhd->khd", grad_scores, heads[:, 0], preferred_element_type=jnp.float32) * scale
    grad_v = jnp.einsum("hqk,qhd->khd", low, grad_mixed, preferred_element_type=jnp.float32)
    packed = jnp.concatenate([grad_q, grad_k, grad_v], axis=1).reshape(length, 3 * width)
    packed = packed.astype(jnp.bfloat16)
    grad_in = matmul(stream, packed, TN)
    grad_inputs = matmul(packed, weight[:, : 3 * width], NT)
    return grad_inputs, jnp.concatenate([grad_in, grad_out], axis=1)


def feed_forward(stream, weight, down):
    pre = matmul(stream, weight, NN)
    active = jax.nn.gelu(pre, approximate=True).astype(jnp.bfloat16)
    return matmul(active, down, NN), (pre, active)


def feed_backward(stream, weight, down, kept, grad_low):
    pre, active = kept
    grad_down = matmul(active, grad_low, TN)
    grad_active = matmul(grad_low, down, NT)
    pull = jax.vjp(lambda value: jax.nn.gelu(value, approximate=True), pre)[1]
    grad_pre = pull(grad_active)[0].astype(jnp.bfloat16)
    grad_up = matmul(stream, grad_pre, TN)
    return matmul(grad_pre, weight, NT), grad_up, grad_down


def micro_step(rows, pull, segment, mats, downs, gains, biases):
    low = jnp.bfloat16
    mask = segment[:, None] == segment[None, :]
    stream, dual = rows, jnp.zeros_like(rows)
    saved = []
    for sub in range(4):
        if sub % 2 == 0:
            branch, kept = attention_forward(stream, mats[sub], mask)
        else:
            branch, kept = feed_forward(stream, mats[sub], downs[sub // 2])
        normal, inverse = norm_stats(stream.astype(jnp.float32) + branch)
        out = normal * gains[sub] + biases[sub]
        total = dual.astype(jnp.float32) + branch
        saved.append((stream, kept, normal, inverse))
        if sub < 3:
            stream, dual = out.astype(low), total.astype(low)
    dual_normal, dual_inverse = norm_stats(total)
    output = (out + dual_normal).astype(low)
    grad_out, grad_dual = pull, norm_back(dual_normal, dual_inverse, pull)
    grads_a, grads_b, grads_n = [None] * 4, [None] * 2, [None] * 4
    for sub in (3, 2, 1, 0):
        stream, kept, normal, inverse = saved[sub]
        grads_n[sub] = jnp.stack([jnp.sum(grad_out * normal, 0), jnp.sum(grad_out, 0)], axis=1)
        summed = norm_back(normal, inverse, grad_out * gains[sub])
        branch_low = (summed + grad_dual).astype(low)
        if sub % 2 == 0:
            inner, grads_a[sub] = attention_backward(stream, mats[sub], kept, branch_low)
        else:
            inner, grads_a[sub], grads_b[sub // 2] = feed_backward(
                stream, mats[sub], downs[sub // 2], kept, branch_low
            )
        grad_in = summed + inner
        if sub > 0:
            grad_out = grad_in.astype(low).astype(jnp.float32)
            grad_dual = grad_dual.astype(low).astype(jnp.float32)
    return output, grad_in, jnp.stack(grads_a), jnp.stack(grads_b), jnp.stack(grads_n)


def finish_step(grad_norm, output, input_grad, *groups):
    factor = CLIP_NORM / jnp.maximum(grad_norm, CLIP_NORM)
    results = [grad_norm, output[None], input_grad[None]]
    for weight, one, two, grad, rate, decay in groups:
        clip = grad * factor
        moment, square_new, master = adam_update(weight, one, two, clip, rate, decay)
        results += [clip, moment, square_new, master, master.astype(jnp.bfloat16)]
    return tuple(results)


def body(
    tokens, cotangent, lengths, mat_a, mat_b, norms, first_a, second_a, first_b, second_b, first_n, second_n
):
    low = jnp.bfloat16
    own = lax.axis_index("section")
    length = tokens.shape[0] // lengths.shape[0]
    rows = lax.dynamic_slice_in_dim(tokens, own * length, length, 0)
    segment, live = segments_of(lax.dynamic_index_in_dim(lengths, own, 0, keepdims=False), length)
    pull = lax.dynamic_slice_in_dim(cotangent, own * length, length, 0).astype(jnp.float32) * live[:, None]

    def gathered(value):
        return lax.all_gather(lax.all_gather(value, "dp", axis=1, tiled=True), "section", axis=0, tiled=True)

    mats = gathered(mat_a.astype(low))
    scales = gathered(norms.astype(low)).astype(jnp.float32)
    downs = lax.all_gather(mat_b.astype(low), "section", axis=2, tiled=True)
    downs = lax.all_gather(downs, "dp", axis=1, tiled=True)
    output, input_grad, part_a, part_b, part_n = micro_step(
        rows, pull, segment, mats, downs, scales[:, :, 0], scales[:, :, 1]
    )

    def scattered(value, section_dim):
        value = lax.psum_scatter(value, "section", scatter_dimension=section_dim, tiled=True)
        return lax.psum_scatter(value, "dp", scatter_dimension=1, tiled=True).astype(jnp.float32)

    grad_a = scattered(part_a.astype(low), 0)
    grad_b = scattered(part_b.astype(low), 2)
    grad_n = scattered(part_n, 0)
    square = jnp.sum(grad_a * grad_a) + jnp.sum(grad_b * grad_b) + jnp.sum(grad_n * grad_n)
    grad_norm = jnp.sqrt(lax.psum(square, ("section", "dp")))
    return finish_step(
        grad_norm, output, input_grad,
        (mat_a, first_a, second_a, grad_a, MATRIX_RATE, MATRIX_DECAY),
        (mat_b, first_b, second_b, grad_b, MATRIX_RATE, MATRIX_DECAY),
        (norms, first_n, second_n, grad_n, NORM_RATE, 0.0),
    )


LOW = jnp.bfloat16
WIDE = jnp.float32
MESH = pl.DeviceIdType.MESH
SECTIONS = 4
LANES = 128
BLOCK = 64
ROWS_FIRST = (5,)
KERNEL_VMEM = 64 * 1024 * 1024 - 256 * 1024


def gradient_items(rows_a, rows_b, cols_b, width, hidden):
    part = rows_a // SECTIONS
    return (
        ("B1", 3, cols_b // 2, rows_b),
        ("F3", 3, part, hidden // 2),
        ("O2", 2, part, width // 2),
        ("K2", 2, part, 3 * width // 2),
        ("B0", 1, cols_b // 2, rows_b),
        ("F1", 1, part, hidden // 2),
        ("O0", 0, part, width // 2),
        ("K0", 0, part, 3 * width // 2),
    )


def item_scratch(name, chips, rows, columns):
    piece = (rows, columns)
    return (
        ("own" + name, (chips, SECTIONS, 2) + piece, LOW),
        ("farx" + name, (chips,) + piece, LOW),
        ("fary" + name, (chips,) + piece, LOW),
        ("nearx" + name, (2, chips) + piece, LOW),
        ("neary" + name, (2, chips) + piece, LOW),
        ("line" + name, (chips, 2) + piece, LOW),
        ("done" + name, (2,) + piece if name[0] == "B" else (SECTIONS, 2) + piece, WIDE if name[0] == "B" else LOW),
    )


def kernel_scratch(chips, rows_a, rows_b, cols_b, length, width, hidden):
    devices = 2 * chips
    items = gradient_items(rows_a, rows_b, cols_b, width, hidden)
    count = len(items)
    received = sum((item_scratch(name, chips, rows, columns) for name, _, rows, columns in items), ())
    return received + (
        ("fac_s", (32,), None),
        ("fac_r", (32,), None),
        ("px_s", (count, 3), None),
        ("px_r", (count, 3), None),
        ("py_s", (count, 3), None),
        ("py_r", (count, 3), None),
        ("line_s", (count, chips), None),
        ("line_r", (count, chips), None),
        ("done_s", (count,), None),
        ("done_r", (count, SECTIONS), None),
        ("wa", (4, chips, 2, SECTIONS, rows_a // SECTIONS, hidden), LOW),
        ("wb", (2, chips, 2, SECTIONS, rows_b, cols_b), LOW),
        ("in_a", (1, rows_a, hidden), WIDE),
        ("in_b", (2, rows_b, cols_b), WIDE),
        ("in_n", (1, 2, rows_a), WIDE),
        ("out_a", (rows_a, hidden), WIDE),
        ("out_b", (2, rows_b, cols_b), WIDE),
        ("out_n", (2, rows_a), WIDE),
        ("out_square", (8, LANES), WIDE),
        ("out_output", (length, width), LOW),
        ("out_input", (length, width), WIDE),
        ("cut", (SECTIONS, rows_a // SECTIONS, hidden), LOW),
        ("tiles", (devices, SECTIONS, 8, LANES), WIDE),
        ("x", (4, length, width), LOW),
        ("xt", (4, chips, 2, rows_a, length), LOW),
        ("xtc", (4, chips, rows_a, 2 * length), LOW),
        ("y", (length, width), LOW),
        ("cot", (length, width), LOW),
        ("bias", (length, length), WIDE),
        ("live", (length, 1), WIDE),
        ("f", (length, width), WIDE),
        ("n", (4, length, width), WIDE),
        ("inv", (4, length, 1), WIDE),
        ("q", (2, length, width), LOW),
        ("k", (2, length, width), LOW),
        ("v", (2, length, width), LOW),
        ("kt", (2, width, length), LOW),
        ("vt", (2, width, length), LOW),
        ("ot", (2, chips, 2, rows_a, length), LOW),
        ("otc", (2, chips, rows_a, 2 * length), LOW),
        ("pt", (2, HEADS, length, length), LOW),
        ("g", (2, length, hidden), LOW),
        ("gc", (2, chips, 2 * length, rows_b), LOW),
        ("slope", (2, length, hidden), LOW),
        ("gx", (length, width), WIDE),
        ("gy", (length, width), WIDE),
        ("df", (2, 2 * length, width), LOW),
        ("dft", (2, width, 2 * length), LOW),
        ("dm", (length, width), LOW),
        ("dqt", (width, length), LOW),
        ("dh", (2, 2 * length, hidden), LOW),
        ("dp", (2, 2 * length, 3 * width), LOW),
        ("ng", (devices, 8, width), WIDE),
        ("ns", (SECTIONS, 8, width), WIDE),
        ("sq", (devices, 8, LANES), WIDE),
        ("sqs", (SECTIONS, 8, LANES), WIDE),
        ("sum", (8, LANES), WIDE),
        ("in_s", (5,), None),
        ("out_s", (6,), None),
        ("cut_s", (1,), None),
        ("cut_r", (SECTIONS,), None),
        ("gz_s", (6,), None),
        ("gz_r", (6, chips), None),
        ("gx_s", (6,), None),
        ("gx_r", (6,), None),
        ("gy_s", (6,), None),
        ("gy_r", (6,), None),
        ("rx_s", (6,), None),
        ("rx_r", (6,), None),
        ("ry_s", (6,), None),
        ("ry_r", (6,), None),
        ("gs_s", (6,), None),
        ("gs_r", (6,), None),
        ("small_s", (3, 2), None),
        ("small_r", (3, 2), None),
    )


INPUTS = ("tokens", "cotangent", "lengths", "mat_a", "mat_b", "norms")
OUTPUTS = ("grad_a", "grad_b", "grad_n", "square", "output", "input_grad")


def step_kernel(names, *refs):
    r = types.SimpleNamespace(**dict(zip(names, refs)))
    length, width = r.x.shape[1:]
    hidden = r.wa.shape[-1]
    rows_a, (rows_b, cols_b) = r.mat_a.shape[1], r.mat_b.shape[1:]
    devices = r.tiles.shape[0]
    chips = devices // 2
    half_b = cols_b // 2
    grad_items = gradient_items(rows_a, rows_b, cols_b, width, hidden)
    head = width // HEADS
    scale = head**-0.5

    s, d = lax.axis_index("section"), lax.axis_index("dp")
    z, c = lax.div(d, 2), lax.rem(d, 2)
    sx = s + 1 - 2 * lax.rem(s, 2)
    sy = lax.rem(s + 2, SECTIONS)
    sd = SECTIONS - 1 - s
    to_sibling = {"dp": d + 1 - 2 * c}
    to_up, to_down = {"dp": d + 2}, {"dp": d - 2}
    to_x, to_y = {"section": sx}, {"section": sy}
    below, above = z > 0, z < chips - 1
    group = [{"dp": lax.rem(d + step, devices)} for step in range(1, devices)]
    plane = [{"section": lax.rem(s + step, SECTIONS)} for step in range(1, SECTIONS)]
    finish = []

    def when(condition, work):
        if condition is None:
            work()
        else:
            pl.when(condition)(work)

    def push(source, target, send_sem, recv_sem, device):
        pltpu.make_async_remote_copy(
            src_ref=source,
            dst_ref=target,
            send_sem=send_sem,
            recv_sem=recv_sem,
            device_id=device,
            device_id_type=MESH,
        ).start()

    def arrived(target, sem):
        pltpu.make_async_remote_copy(
            src_ref=target, dst_ref=target, send_sem=sem, recv_sem=sem, device_id=to_x, device_id_type=MESH
        ).wait_recv()

    def sent(source, sem):
        pltpu.make_async_remote_copy(
            src_ref=source, dst_ref=source, send_sem=sem, recv_sem=sem, device_id=to_x, device_id_type=MESH
        ).wait_send()

    def at_end(condition, source, sem):
        finish.append((condition, source, sem))

    def aligned(start, size):
        return pl.ds(pl.multiple_of(start, size), size)

    own_x = pltpu.make_async_copy(r.tokens.at[aligned(s * length, length)], r.x.at[0], r.in_s.at[0])
    own_cot = pltpu.make_async_copy(r.cotangent.at[aligned(s * length, length)], r.cot, r.in_s.at[1])
    own_a = pltpu.make_async_copy(r.mat_a, r.in_a, r.in_s.at[2])
    own_b = pltpu.make_async_copy(r.mat_b, r.in_b, r.in_s.at[3])
    own_n = pltpu.make_async_copy(r.norms, r.in_n, r.in_s.at[4])
    own_a.start()
    own_n.start()
    own_b.start()
    own_x.start()
    own_cot.start()
    barrier = pltpu.get_barrier_semaphore()
    for peer in group + plane:
        pl.semaphore_signal(barrier, inc=1, device_id=peer, device_id_type=MESH)
    own_a.wait()
    r.cut[...] = r.in_a[0].astype(LOW).reshape(SECTIONS, rows_a // SECTIONS, hidden)
    r.wa[s, z, c, s] = r.cut[s]
    own_n.wait()
    norms = r.in_n[0].astype(LOW).astype(WIDE)
    nothing = jnp.zeros((2, rows_a), WIDE)
    even = jnp.concatenate([norms, nothing], axis=1)
    odd = jnp.concatenate([nothing, norms], axis=1)
    r.tiles[d, s, 0:2, :] = jnp.where(c == 0, even, odd)
    r.tiles[d, s, 2:8, :] = jnp.zeros((6, LANES), WIDE)
    own_b.wait()
    for layer in range(2):
        r.wb[layer, z, c, s] = r.in_b[layer].astype(LOW)
    pl.semaphore_wait(barrier, len(group) + len(plane))

    def put_out(slot, source, target):
        made = pltpu.make_async_copy(source, target, r.out_s.at[slot])
        made.start()
        return made

    def small_out(which, source):
        for peer in group:
            push(source, source, r.small_s.at[which, 0], r.small_r.at[which, 0], peer)

    def small_group(which, like):
        arrived(like, r.small_r.at[which, 0])
        sent(like, r.small_s.at[which, 0])

    def small_plane_out(which, source):
        for peer in plane:
            push(source, source, r.small_s.at[which, 1], r.small_r.at[which, 1], peer)

    def small_plane(which, like):
        arrived(like, r.small_r.at[which, 1])
        sent(like, r.small_s.at[which, 1])

    every = slice(None)

    def block(item, chip, section):
        if item < 4:
            return r.wa.at[item, chip, c, section]
        return r.wb.at[item - 4, chip, c, section]

    def half_block(item, section, half):
        if item < 4:
            return r.wa.at[item, :, c, section, :, pl.ds(half * hidden // 2, hidden // 2)]
        rows = pl.ds(half * rows_b // 2, rows_b // 2)
        return r.wb.at[item - 4, :, c, section, rows]

    def half_piece(item, section, half):
        rows = pl.ds(half * rows_b // 2, rows_b // 2)
        return r.wb.at[item - 4, z, c, section, rows]

    def core_blocks(item, core):
        return r.wa.at[item, :, core] if item < 4 else r.wb.at[item - 4, :, core]

    def cut_out():
        for section, device in ((sd, {"section": sd}), (sx, to_x), (sy, to_y)):
            push(r.cut.at[section], r.wa.at[s, z, c, section], r.cut_s.at[0], r.cut_r.at[s], device)
        at_end(None, r.cut.at[pl.ds(0, SECTIONS - 1)], r.cut_s.at[0])

    def cut_in():
        for section in (sx, sy, sd):
            arrived(r.wa.at[section, z, c, s], r.cut_r.at[section])

    def line_out(item):
        if item in ROWS_FIRST:
            rows_out(item)
            return
        own = block(item, z, s)
        for step in range(1, chips):
            push(own, own, r.gz_s.at[item], r.gz_r.at[item, z], {"dp": 2 * lax.rem(z + step, chips) + c})
        several = block(item, pl.ds(0, chips - 1), s)
        at_end(None, several, r.gz_s.at[item])

    def plane_out(item, chip):
        own = block(item, chip, s)
        push(own, own, r.gx_s.at[item], r.gx_r.at[item], to_x)
        push(own, own, r.gy_s.at[item], r.gy_r.at[item], to_y)

    def rows_out(item):
        arrived(half_piece(item, sd, 0), r.rx_r.at[item])
        arrived(half_piece(item, sd, 1), r.ry_r.at[item])
        rows = r.wb.at[item - 4, z, c]
        for step in range(1, chips):
            push(rows, rows, r.gz_s.at[item], r.gz_r.at[item, z], {"dp": 2 * lax.rem(z + step, chips) + c})
        push(rows, rows, r.gs_s.at[item], r.gs_r.at[item], to_sibling)
        at_end(None, r.wb.at[item - 4, pl.ds(0, chips - 1), c], r.gz_s.at[item])

    def rows_in(item):
        for step in range(1, chips):
            chip = lax.rem(z + step, chips)
            rows = r.wb.at[item - 4, chip, c]
            arrived(rows, r.gz_r.at[item, chip])
            push(rows, rows, r.gs_s.at[item], r.gs_r.at[item], to_sibling)
        at_end(None, core_blocks(item, c), r.gs_s.at[item])

    def line_in(item):
        if item in ROWS_FIRST:
            rows_in(item)
            return
        for step in range(1, chips):
            chip = lax.rem(z + step, chips)
            arrived(block(item, chip, s), r.gz_r.at[item, chip])
            plane_out(item, chip)
        core_out(item, s)
        at_end(None, block(item, every, s), r.gx_s.at[item])
        at_end(None, block(item, every, s), r.gy_s.at[item])

    def core_out(item, section):
        blocks = block(item, every, section)
        push(blocks, blocks, r.gs_s.at[item], r.gs_r.at[item], to_sibling)

    def plane_in(item):
        over = z if item in ROWS_FIRST else every
        piece = half_piece if item in ROWS_FIRST else half_block
        arrived(block(item, over, sx), r.gx_r.at[item])
        part = piece(item, sx, 1)
        push(part, part, r.ry_s.at[item], r.ry_r.at[item], to_y)
        arrived(block(item, over, sy), r.gy_r.at[item])
        part = piece(item, sy, 0)
        push(part, part, r.rx_s.at[item], r.rx_r.at[item], to_x)
        if item in ROWS_FIRST:
            at_end(None, block(item, z, sx), r.gx_s.at[item])
            at_end(None, block(item, z, sx), r.gy_s.at[item])
        else:
            core_out(item, sx)
            core_out(item, sy)
        at_end(None, part, r.ry_s.at[item])
        at_end(None, part, r.rx_s.at[item])

    def far_in(item):
        arrived(half_block(item, sd, 0), r.rx_r.at[item])
        arrived(half_block(item, sd, 1), r.ry_r.at[item])
        core_out(item, sd)
        at_end(None, core_blocks(item, c), r.gs_s.at[item])

    def core_in(item):
        arrived(core_blocks(item, 1 - c), r.gs_r.at[item])

    mine, other = pl.ds(0, length), pl.ds(length, length)

    def give(slot, source, target):
        push(source, target, r.fac_s.at[slot], r.fac_r.at[slot], to_sibling)
        at_end(None, target, r.fac_s.at[slot])

    def taken(slot, target):
        arrived(target, r.fac_r.at[slot])

    def give_rows(layer):
        r.xt[layer] = r.x[layer].T.reshape(chips, 2, rows_a, length)
        r.xtc[layer, :, :, 0:length] = r.xt[layer, :, c]
        give(layer, r.xt.at[layer, :, 1 - c], r.xtc.at[layer, :, :, other])

    def product(left, right, dims):
        return lax.dot_general(left, right, (dims, ((), ())), preferred_element_type=WIDE)

    def gain_row(layer, kind):
        parts = [
            r.tiles[2 * chip, layer, kind : kind + 1, :] + r.tiles[2 * chip + 1, layer, kind : kind + 1, :]
            for chip in range(chips)
        ]
        return jnp.concatenate(parts, axis=1)

    def stats(value):
        centre = value - jnp.mean(value, -1, keepdims=True)
        inverse = lax.rsqrt(jnp.mean(centre * centre, -1, keepdims=True) + EPSILON)
        return centre * inverse, inverse

    lane = lax.broadcasted_iota(jnp.int32, (1, 2 * head), 1)
    first_half = (lane < head).astype(WIDE)
    half_masks = (first_half.astype(LOW), (1.0 - first_half).astype(LOW))

    def prepare_masks():
        ends, total = [], jnp.int32(0)
        for slot in range(r.lengths.shape[1]):
            total = total + r.lengths[s, slot]
            ends.append(total)
        down_places = lax.broadcasted_iota(jnp.int32, (length, 1), 0)
        across_places = lax.broadcasted_iota(jnp.int32, (1, length), 1)
        down_segment = jnp.zeros((length, 1), jnp.int32)
        across_segment = jnp.zeros((1, length), jnp.int32)
        for end in ends:
            down_segment = down_segment + (end <= down_places).astype(jnp.int32)
            across_segment = across_segment + (end <= across_places).astype(jnp.int32)
        r.bias[...] = jnp.where(down_segment == across_segment, 0.0, NEGATIVE)
        r.live[...] = (down_places < total).astype(WIDE)

    def matrix(layer, place):
        value = r.wa[layer, :, :, :, :, place]
        return value.reshape(width, value.shape[-1])

    def down(at, chip=slice(None)):
        blocks = [r.wb[at, chip, :, section] for section in range(SECTIONS)]
        return jnp.concatenate([block.reshape(-1, cols_b) for block in blocks], axis=1)

    def attention_in(layer):
        at = layer // 2
        rows = r.x[layer]
        r.q[at] = product(rows, matrix(layer, pl.ds(0, width)), NN).astype(LOW) * jnp.asarray(scale, LOW)
        keys = product(rows, matrix(layer, pl.ds(width, width)), NN).astype(LOW)
        r.k[at] = keys
        values = product(rows, matrix(layer, pl.ds(2 * width, width)), NN).astype(LOW)
        r.v[at] = values
        r.vt[at] = values.T

    def attention_heads(layer, begin, count):
        at = layer // 2

        def pair(index):
            lanes = pl.ds(index * 2 * head, 2 * head)
            for which in range(2):
                scores = product(r.k[at, :, lanes], r.q[at, :, lanes] * half_masks[which], NT) + r.bias[...]
                weights = jnp.exp(scores - jnp.max(scores, 0, keepdims=True))
                probs = (weights * (1.0 / jnp.sum(weights, 0, keepdims=True))).astype(LOW)
                r.pt[at, 2 * index + which] = probs
                place = pl.ds((2 * index + which) * head, head)
                r.ot[at, index, which] = product(r.vt[at, place, :], probs, NN).astype(LOW)

        for index in range(begin, begin + count):
            pair(index)

    def attention_out(layer):
        at = layer // 2
        r.otc[at, :, :, 0:length] = r.ot[at, :, c]
        give(4 + at, r.ot.at[at, :, 1 - c], r.otc.at[at, :, :, other])
        r.f[...] = product(r.ot[at].reshape(width, length).T, matrix(layer, pl.ds(3 * width, width)), NN)

    def expand(layer, index):
        at = layer // 2
        place = pl.ds(index * width, width)
        pre = product(r.x[layer], matrix(layer, place), NN)
        squared = pre * pre
        slope = 0.7978845608 * (1.0 + 3 * 0.044715 * squared)
        bent = jnp.tanh(0.7978845608 * pre * (1.0 + 0.044715 * squared))
        r.g[at, :, place] = (0.5 * pre * (1.0 + bent)).astype(LOW)
        r.slope[at, :, place] = (0.5 * (1.0 + bent) + 0.5 * pre * (1.0 - bent * bent) * slope).astype(LOW)
        block = aligned((2 * index + c) * rows_b, rows_b)
        r.gc[at, index, 0:length, :] = r.g[at, :, block]
        block = aligned((2 * index + 1 - c) * rows_b, rows_b)
        give(6 + chips * at + index, r.g.at[at, :, block], r.gc.at[at, index, other, :])

    def contract(layer):
        r.f[...] = product(r.g[layer // 2], down(layer // 2), NN)

    def by_rows(work):
        for index in range(length // BLOCK):
            work(pl.ds(index * BLOCK, BLOCK))

    def normalize(layer):
        gain, offset = gain_row(layer, 0), gain_row(layer, 1)

        def some(rows):
            branch = r.f[rows, :]
            normal, inverse = stats(r.x[layer, rows, :].astype(WIDE) + branch)
            r.n[layer, rows, :] = normal
            r.inv[layer, rows, :] = inverse
            out = normal * gain + offset
            dual = branch if layer == 0 else r.y[rows, :].astype(WIDE) + branch
            if layer < 3:
                r.x[layer + 1, rows, :] = out.astype(LOW)
                r.y[rows, :] = dual.astype(LOW)
            else:
                dual_normal, dual_inverse = stats(dual)
                r.out_output[rows, :] = (out + dual_normal).astype(LOW)
                pull = r.cot[rows, :].astype(WIDE) * r.live[rows, :]
                r.gx[rows, :] = pull
                r.gy[rows, :] = norm_back(dual_normal, dual_inverse, pull)

        by_rows(some)

    def back_normalize(layer):
        gain = gain_row(layer, 0)

        def some(index, sums):
            rows = pl.ds(index * BLOCK, BLOCK)
            upstream = r.gx[rows, :]
            normal = r.n[layer, rows, :]
            summed = norm_back(normal, r.inv[layer, rows, :], upstream * gain)
            dual = r.gy[rows, :]
            r.gx[rows, :] = summed
            r.df[layer // 2, rows, :] = (summed + dual).astype(LOW)
            if layer == 3:
                r.gy[rows, :] = dual.astype(LOW).astype(WIDE)
            return (
                sums[0] + jnp.sum(upstream * normal, 0, keepdims=True),
                sums[1] + jnp.sum(upstream, 0, keepdims=True),
            )

        zero = jnp.zeros((1, width), WIDE)
        gains, offsets = zero, zero
        for index in range(length // BLOCK):
            gains, offsets = some(index, (gains, offsets))
        r.ng[d, 2 * layer : 2 * layer + 1, :] = gains
        r.ng[d, 2 * layer + 1 : 2 * layer + 2, :] = offsets

    def pass_down(layer, inner):
        total = r.gx[...] + inner
        if layer > 0:
            r.gx[...] = total.astype(LOW).astype(WIDE)
        else:
            r.out_input[...] = total

    base = 6 + 2 * chips

    def back_hidden(layer):
        at = layer // 2
        r.dft[at, :, 0:length] = r.df[at, 0:length, :].T
        give(base + at, r.dft.at[at, :, mine], r.dft.at[at, :, other])
        for index in range(hidden // width):
            place = pl.ds(index * width, width)
            pulled = product(r.df[at, 0:length, :], down(at, pl.ds(index, 1)), NT)
            r.dh[at, 0:length, place] = (pulled * r.slope[at, :, place].astype(WIDE)).astype(LOW)
            give(base + 2 + chips * at + index, r.dh.at[at, mine, place], r.dh.at[at, other, place])

    def back_expand_end(layer):
        pass_down(layer, product(r.dh[layer // 2, 0:length, :], matrix(layer, pl.ds(0, hidden)), NT))

    def back_output(layer):
        at = layer // 2
        give(base + 2 + 2 * chips + at, r.df.at[at, mine], r.df.at[at, other])
        r.dm[...] = product(r.df[at, 0:length, :], matrix(layer, pl.ds(3 * width, width)), NT).astype(LOW)
        r.kt[at] = (r.k[at] * jnp.asarray(scale, LOW)).T

    def back_heads(layer, begin, count):
        at = layer // 2

        def pair(index):
            lanes = pl.ds(index * 2 * head, 2 * head)
            pulled = r.dm[:, lanes]
            keys, values = [], []
            for which in range(2):
                probs = r.pt[at, 2 * index + which]
                grad = product(r.v[at, :, lanes], pulled * half_masks[which], NT)
                full = probs.astype(WIDE)
                centre = jnp.sum(full * grad, 0, keepdims=True)
                scores = (full * (grad - centre)).astype(LOW)
                keys.append(product(scores, r.q[at, :, lanes], NN))
                values.append(product(probs, pulled, NN))
                place = pl.ds((2 * index + which) * head, head)
                r.dqt[place, :] = product(r.kt[at, place, :], scores, NN).astype(LOW)
            r.dp[at, 0:length, pl.ds(width + index * 2 * head, 2 * head)] = jnp.where(
                lane < head, keys[0], keys[1]
            ).astype(LOW)
            r.dp[at, 0:length, pl.ds(2 * width + index * 2 * head, 2 * head)] = jnp.where(
                lane < head, values[0], values[1]
            ).astype(LOW)

        for index in range(begin, begin + count):
            pair(index)

    def back_packed(layer):
        at = layer // 2
        slot = base + 4 + 2 * chips + 2 * at
        place = pl.ds(width, 2 * width)
        give(slot, r.dp.at[at, mine, place], r.dp.at[at, other, place])
        r.dp[at, 0:length, 0:width] = r.dqt[...].T
        place = pl.ds(0, width)
        give(slot + 1, r.dp.at[at, mine, place], r.dp.at[at, other, place])

    def back_packed_end(layer):
        pass_down(layer, product(r.dp[layer // 2, 0:length, :], matrix(layer, pl.ds(0, 3 * width)), NT))

    def keep(name, half, place, value):
        own = getattr(r, "own" + name)
        own[:, :, half, :, place] = value.astype(LOW).reshape(chips, SECTIONS, rows_a // SECTIONS, value.shape[1])

    def chip_rows(value):
        return value.reshape(chips * rows_a, 2 * length)

    def grad_down(at):
        own = getattr(r, "ownB%d" % at)
        taken(base + at, r.dft.at[at, :, other])
        for chip in range(chips):
            taken(6 + chips * at + chip, r.gc.at[at, chip, other, :])
            value = product(r.dft[at], r.gc[at, chip], NN)
            own[chip] = value.astype(LOW).reshape(SECTIONS, 2, half_b, rows_b)

    def grad_up(layer):
        at = layer // 2
        taken(layer, r.xtc.at[layer, :, :, other])
        for index in range(hidden // width):
            place = pl.ds(index * width, width)
            taken(base + 2 + chips * at + index, r.dh.at[at, other, place])
            value = product(chip_rows(r.xtc[layer]), r.dh[at, :, place], NN)
            keep("F%d" % layer, index // 2, pl.ds(index % 2 * width, width), value)

    def grad_output(layer):
        at = layer // 2
        taken(4 + at, r.otc.at[at, :, :, other])
        taken(base + 2 + 2 * chips + at, r.df.at[at, other])
        for half in range(2):
            place = pl.ds(half * width // 2, width // 2)
            value = product(chip_rows(r.otc[at]), r.df[at, :, place], NN)
            keep("O%d" % layer, half, pl.ds(0, width // 2), value)

    def grad_packed(layer):
        at = layer // 2
        slot = base + 4 + 2 * chips + 2 * at
        taken(layer, r.xtc.at[layer, :, :, other])
        taken(slot, r.dp.at[at, other, pl.ds(width, 2 * width)])
        taken(slot + 1, r.dp.at[at, other, pl.ds(0, width)])
        part = 3 * width // 2
        for half in range(2):
            value = product(chip_rows(r.xtc[layer]), r.dp[at, :, half * part : (half + 1) * part], NN)
            keep("K%d" % layer, half, pl.ds(0, part), value)

    def joined(target, others):
        return functools.reduce(
            lambda left, right: left + right, [ref[...].astype(WIDE) for ref in (target, *others)]
        )

    def add_into(target, others):
        if len(others) < 3:
            target[...] = functools.reduce(lambda left, right: left + right, [ref[...] for ref in (target, *others)])
        else:
            target[...] = joined(target, others).astype(LOW)

    places = {name: place for place, (name, _, _, _) in enumerate(grad_items)}

    def buffers(name):
        parts = ("own", "farx", "fary", "nearx", "neary", "line", "done")
        return types.SimpleNamespace(**{part: getattr(r, part + name) for part in parts})

    def to_plane(name):
        item, place = buffers(name), places[name]

        def over_x(section, half, target, slot):
            push(item.own.at[:, section, half], target, r.px_s.at[place, slot], r.px_r.at[place, slot], to_x)
            at_end(None, item.farx, r.px_s.at[place, slot])

        def over_y(section, half, target, slot):
            push(item.own.at[:, section, half], target, r.py_s.at[place, slot], r.py_r.at[place, slot], to_y)
            at_end(None, item.farx, r.py_s.at[place, slot])

        over_x(sd, 0, item.farx, 2)
        over_y(sd, 1, item.fary, 2)
        over_x(sx, 0, item.nearx.at[0], 0)
        over_y(sy, 1, item.neary.at[1], 1)

    def through_plane(name):
        item, place = buffers(name), places[name]
        own = item.own
        arrived(item.fary, r.py_r.at[place, 2])
        add_into(own.at[:, sx, 1], [item.fary])
        push(own.at[:, sx, 1], item.nearx.at[1], r.px_s.at[place, 1], r.px_r.at[place, 1], to_x)
        at_end(None, item.farx, r.px_s.at[place, 1])
        arrived(item.farx, r.px_r.at[place, 2])
        add_into(own.at[:, sy, 0], [item.farx])
        push(own.at[:, sy, 0], item.neary.at[0], r.py_s.at[place, 0], r.py_r.at[place, 0], to_y)
        at_end(None, item.farx, r.py_s.at[place, 0])

    def to_line(name):
        item, place = buffers(name), places[name]
        own = item.own.at[:, s]
        for half in range(2):
            arrived(item.nearx.at[half], r.px_r.at[place, half])
            arrived(item.neary.at[half], r.py_r.at[place, half])
            add_into(own.at[:, half], [item.nearx.at[half], item.neary.at[half]])
        for step in range(1, chips):
            chip = lax.rem(z + step, chips)
            push(
                own.at[chip],
                item.line.at[z],
                r.line_s.at[place, step],
                r.line_r.at[place, z],
                {"dp": 2 * chip + c},
            )
            at_end(None, item.line.at[0], r.line_s.at[place, step])

    def to_owner(name):
        item, place = buffers(name), places[name]
        others = [lax.rem(z + step, chips) for step in range(1, chips)]
        for chip in others:
            arrived(item.line.at[chip], r.line_r.at[place, chip])
        total = joined(item.own.at[z, s], [item.line.at[chip] for chip in others])
        square = total * total
        while square.ndim > 2:
            square = jnp.sum(square, 0)
        square = jnp.sum(jnp.sum(square, 0, keepdims=True), 1, keepdims=True)
        r.sum[...] = r.sum[...] + jnp.broadcast_to(square, (8, LANES))
        if name[0] == "B":
            item.done[...] = total
            return
        item.done[s] = total.astype(LOW)
        layer = grad_items[place][1]
        mine = item.done.at[s]
        away = s != layer
        when(
            away,
            lambda: push(mine, mine, r.done_s.at[place], r.done_r.at[place, s], {"section": jnp.int32(layer)}),
        )
        at_end(away, mine, r.done_s.at[place])

    def collect(name):
        item, place = buffers(name), places[name]
        layer = grad_items[place][1]

        def work():
            for section in range(SECTIONS):
                if section != layer:
                    arrived(item.done.at[section], r.done_r.at[place, section])
            columns = item.done.shape[-1]
            start = 3 * width if name[0] == "O" else 0
            for section in range(SECTIONS):
                for half in range(2):
                    rows = pl.ds(section * (rows_a // SECTIONS), rows_a // SECTIONS)
                    place_to = pl.ds(start + half * columns, columns)
                    r.out_a[rows, place_to] = item.done[section, half].astype(WIDE)

        when(s == layer, work)

    def all_sent(count=None):
        for condition, source, sem in finish[:count]:
            when(condition, functools.partial(sent, source, sem))
        del finish[:count]

    cut_out()
    plane_out(5, z)
    line_out(4)
    plane_out(4, z)
    small_out(0, r.tiles.at[d, s])
    cut_in()
    plane_out(1, z)
    line_out(0)
    plane_out(0, z)
    line_out(1)
    line_out(2)
    plane_out(3, z)
    line_out(3)
    line_in(4)
    small_group(0, r.tiles.at[pl.ds(0, devices - 1), 0])
    for peer in plane:
        push(r.tiles.at[:, s], r.tiles.at[:, s], r.small_s.at[0, 1], r.small_r.at[0, 1], peer)
    line_in(0)
    plane_in(5)
    line_in(1)
    plane_in(0)
    plane_out(2, z)
    plane_in(1)
    far_in(0)
    line_in(2)
    plane_in(4)
    line_out(5)
    own_x.wait()
    own_cot.wait()
    prepare_masks()
    give_rows(0)
    core_in(0)
    attention_in(0)
    far_in(1)
    attention_heads(0, 0, 2)
    attention_heads(0, 2, 2)
    plane_in(2)
    attention_out(0)
    small_plane(0, r.tiles.at[:, pl.ds(0, SECTIONS - 1)])
    normalize(0)
    far_in(4)
    core_in(1)
    line_in(3)
    expand(1, 0)
    expand(1, 1)
    early = len(finish)
    far_in(2)
    expand(1, 2)
    expand(1, 3)
    core_in(4)
    contract(1)
    normalize(1)
    core_in(2)
    plane_in(3)
    attention_in(2)
    attention_heads(2, 0, 2)
    attention_heads(2, 2, 2)
    far_in(3)
    attention_out(2)
    line_in(5)
    normalize(2)
    core_in(3)
    expand(3, 0)
    expand(3, 1)
    expand(3, 2)
    expand(3, 3)
    all_sent(early)
    core_in(5)
    contract(3)
    normalize(3)
    leaving = [put_out(0, r.out_output, r.output)]

    r.sum[...] = jnp.zeros((8, LANES), WIDE)
    back_normalize(3)
    back_hidden(3)
    give_rows(3)
    back_expand_end(3)
    back_normalize(2)
    grad_up(3)
    to_plane("F3")
    back_output(2)
    grad_down(1)
    to_plane("B1")
    back_heads(2, 0, 2)
    back_heads(2, 2, 2)
    back_packed(2)
    through_plane("B1")
    give_rows(2)
    grad_output(2)
    back_packed_end(2)
    give_rows(1)
    to_plane("O2")
    grad_packed(2)
    to_plane("K2")
    back_normalize(1)
    back_hidden(1)
    through_plane("K2")
    grad_down(0)
    to_plane("B0")
    back_expand_end(1)
    back_normalize(0)
    small_out(1, r.ng.at[d])
    to_line("K2")
    to_line("B1")
    back_output(0)
    grad_up(1)
    through_plane("B0")
    to_plane("F1")
    back_heads(0, 0, 2)
    back_heads(0, 2, 2)
    back_packed(0)
    to_line("B0")
    through_plane("O2")
    through_plane("F1")
    grad_output(0)
    to_plane("O0")
    grad_packed(0)
    to_plane("K0")
    to_line("O2")
    to_line("F1")
    through_plane("O0")
    to_owner("B1")
    back_packed_end(0)
    leaving.append(put_out(1, r.out_input, r.input_grad))
    to_owner("B0")
    all_sent(len(finish) // 3)
    through_plane("K0")
    small_group(1, r.ng.at[pl.ds(0, devices - 1)])
    r.ns[s] = functools.reduce(lambda left, right: left + right, [r.ng[index] for index in range(devices)])
    small_plane_out(1, r.ns.at[s])
    through_plane("F3")
    to_line("O0")
    all_sent(len(finish) // 3)
    to_line("K0")
    to_owner("F1")
    to_line("F3")
    to_owner("O2")
    to_owner("K2")
    to_owner("F3")
    to_owner("O0")
    all_sent(len(finish) // 3)
    to_owner("K0")

    r.sq[d] = r.sum[...]
    small_out(2, r.sq.at[d])
    for name in ("F1", "O2", "K2", "F3"):
        collect(name)
    collect("O0")
    for layer in range(2):
        done = buffers("B%d" % layer).done
        r.out_b[layer] = done[...].reshape(cols_b, rows_b).T
    leaving.append(put_out(2, r.out_b, r.grad_b))
    small_plane(1, r.ns.at[pl.ds(0, SECTIONS - 1)])
    grads = functools.reduce(lambda left, right: left + right, [r.ns[index] for index in range(SECTIONS)])
    norm_square = jnp.sum(jnp.sum(grads * grads, 0, keepdims=True), 1, keepdims=True)
    chosen = jnp.zeros((2, width), WIDE)
    for layer in range(4):
        chosen = jnp.where(s == layer, grads[2 * layer : 2 * layer + 2, :], chosen)
    shard = jnp.zeros((2, rows_a), WIDE)
    for chip in range(chips):
        pair_of = chosen[:, chip * LANES : (chip + 1) * LANES]
        shard = jnp.where(z == chip, jnp.where(c == 0, pair_of[:, :rows_a], pair_of[:, rows_a:]), shard)
    r.out_n[...] = shard
    leaving.append(put_out(3, r.out_n, r.grad_n))
    collect("K0")
    leaving.append(put_out(4, r.out_a, r.grad_a))
    small_group(2, r.sq.at[pl.ds(0, devices - 1)])
    r.sqs[s] = functools.reduce(lambda left, right: left + right, [r.sq[index] for index in range(devices)])
    small_plane_out(2, r.sqs.at[s])
    all_sent()
    small_plane(2, r.sqs.at[pl.ds(0, SECTIONS - 1)])
    squares = functools.reduce(lambda left, right: left + right, [r.sqs[index] for index in range(SECTIONS)])
    r.out_square[...] = squares + norm_square
    leaving.append(put_out(5, r.out_square, r.square))
    for made in leaving:
        made.wait()


def step_call(tokens, cotangent, lengths, mat_a, mat_b, norms):
    rows_a, hidden = mat_a.shape[1:]
    rows_b, cols_b = mat_b.shape[1:]
    width = tokens.shape[1]
    length = tokens.shape[0] // lengths.shape[0]
    chips = width // rows_a // 2
    scratch = kernel_scratch(chips, rows_a, rows_b, cols_b, length, width, hidden)
    shapes = []
    for _, shape, kind in scratch:
        shapes.append(pltpu.SemaphoreType.DMA(shape) if kind is None else pltpu.VMEM(shape, kind))
    anywhere = pl.BlockSpec(memory_space=pl.ANY)
    return pl.pallas_call(
        functools.partial(step_kernel, INPUTS + OUTPUTS + tuple(name for name, _, _ in scratch)),
        out_shape=(
            jax.ShapeDtypeStruct((rows_a, hidden), WIDE),
            jax.ShapeDtypeStruct(mat_b.shape, WIDE),
            jax.ShapeDtypeStruct((2, rows_a), WIDE),
            jax.ShapeDtypeStruct((8, LANES), WIDE),
            jax.ShapeDtypeStruct((length, width), LOW),
            jax.ShapeDtypeStruct((length, width), WIDE),
        ),
        in_specs=[anywhere, anywhere, pl.BlockSpec(memory_space=pltpu.SMEM), anywhere, anywhere, anywhere],
        out_specs=[anywhere] * len(OUTPUTS),
        scratch_shapes=shapes,
        compiler_params=pltpu.CompilerParams(
            collective_id=0, has_side_effects=True, vmem_limit_bytes=KERNEL_VMEM
        ),
    )(tokens, cotangent, lengths, mat_a, mat_b, norms)


def update_kernel(*refs):
    inputs, outputs, held, made, sems = refs[:15], refs[15:33], refs[33:48], refs[48:63], refs[63]
    started = []

    def copy(source, target):
        one = pltpu.make_async_copy(source, target, sems.at[len(started)])
        one.start()
        started.append(one)
        return one

    half = inputs[4].shape[1] // 2
    parts = [(0, pl.ds(0, half)), (0, pl.ds(half, half)), (1, slice(None)), (2, slice(None))]
    rates = ((MATRIX_RATE, MATRIX_DECAY), (MATRIX_RATE, MATRIX_DECAY), (NORM_RATE, 0.0))
    norm_in = copy(inputs[0], held[0])
    coming = []
    for group, rows in parts:
        coming.append(
            [copy(inputs[at].at[:, rows], held[at].at[:, rows]) for at in range(3 + 4 * group, 7 + 4 * group)]
        )
    passing = [copy(inputs[at], held[at]) for at in (1, 2)]
    norm_in.wait()
    grad_norm = jnp.sqrt(held[0][0:1, 0:1])
    factor = CLIP_NORM / jnp.maximum(grad_norm, CLIP_NORM)
    outputs[0][...] = grad_norm
    leaving = []
    for (group, rows), waits in zip(parts, coming):
        for one in waits:
            one.wait()
        grad, weight, one, two = (held[at][:, rows] for at in range(3 + 4 * group, 7 + 4 * group))
        clip = grad * factor
        moment, square, master = adam_update(weight, one, two, clip, *rates[group])
        for kind, value in enumerate((clip, moment, square, master, master.astype(LOW))):
            buffer = made[5 * group + kind]
            buffer[:, rows] = value
            leaving.append(copy(buffer.at[:, rows], outputs[3 + 5 * group + kind].at[:, rows]))
        if passing:
            at = 3 - len(passing)
            passing.pop(0).wait()
            leaving.append(copy(held[at], outputs[at].at[0]))
    for one in leaving:
        one.wait()


def kernel_body(
    tokens, cotangent, lengths, mat_a, mat_b, norms, first_a, second_a, first_b, second_b, first_n, second_n
):
    norms, first_n, second_n = (jnp.swapaxes(value, 1, 2) for value in (norms, first_n, second_n))
    grad_a, grad_b, grad_n, square, output, input_grad = step_call(
        tokens, cotangent, lengths, mat_a, mat_b, norms
    )
    args = (square, output, input_grad, grad_a[None], mat_a, first_a, second_a, grad_b, mat_b, first_b, second_b)
    args += (grad_n[None], norms, first_n, second_n)
    anywhere, vmem = pl.BlockSpec(memory_space=pl.ANY), pl.BlockSpec(memory_space=pltpu.VMEM)
    shapes = [jax.ShapeDtypeStruct((1, 1), WIDE)]
    shapes += [jax.ShapeDtypeStruct((1,) + value.shape, value.dtype) for value in (output, input_grad)]
    for value in (mat_a, mat_b, norms):
        shapes += [jax.ShapeDtypeStruct(value.shape, kind) for kind in (WIDE, WIDE, WIDE, WIDE, LOW)]
    scratch = [pltpu.VMEM(value.shape, value.dtype) for value in (*args, *shapes[3:])]
    results = pl.pallas_call(
        update_kernel,
        out_shape=shapes,
        in_specs=[anywhere] * len(args),
        out_specs=[vmem] + [anywhere] * (len(shapes) - 1),
        scratch_shapes=scratch + [pltpu.SemaphoreType.DMA((48,))],
        compiler_params=pltpu.CompilerParams(vmem_limit_bytes=KERNEL_VMEM),
    )(*args)
    results = [results[0][0, 0], *results[1:]]
    results[-5:] = [jnp.swapaxes(value, 1, 2) for value in results[-5:]]
    return tuple(results)


def chosen_body(*args):
    rows_a = args[3].shape[1]
    groups = lax.axis_size("dp")
    by_kernel = rows_a % 32 == 0 and 2 * rows_a == LANES and groups * rows_a == args[0].shape[1]
    return (kernel_body if by_kernel else body)(*args)


def solution(mesh):
    placed = (
        P("dp", None),
        P("dp", None),
        P("dp", None),
        P("section", "dp", None),
        P(None, "dp", "section"),
        P("section", "dp", None),
        P("section", "dp", None),
        P("section", "dp", None),
        P(None, "dp", "section"),
        P(None, "dp", "section"),
        P("section", "dp", None),
        P("section", "dp", None),
    )
    return jax.shard_map(
        chosen_body,
        mesh=mesh,
        in_specs=placed,
        out_specs=(
            P(),
            P("section", "dp", None),
            P("section", "dp", None),
            P("section", "dp", None),
            P("section", "dp", None),
            P("section", "dp", None),
            P("section", "dp", None),
            P("section", "dp", None),
            P(None, "dp", "section"),
            P(None, "dp", "section"),
            P(None, "dp", "section"),
            P(None, "dp", "section"),
            P(None, "dp", "section"),
            P("section", "dp", None),
            P("section", "dp", None),
            P("section", "dp", None),
            P("section", "dp", None),
            P("section", "dp", None),
        ),
        check_vma=False,
    )
```

```python
import functools
import types

import jax
import jax.numpy as jnp
from jax import lax
from jax.experimental import pallas as pl
from jax.experimental.pallas import tpu as pltpu
from jax.sharding import PartitionSpec as P

HEADS = 8
STEP = 5


EPSILON = 1e-05
NEGATIVE = -1e30
CLIP_NORM = 1.0
BETA_ONE = 0.5
BETA_TWO = 0.5
ADAM_EPSILON = 1e-08
MATRIX_RATE = 0.05
NORM_RATE = 0.5
MATRIX_DECAY = 0.01


def norm_stats(value):
    centre = value - jnp.mean(value, -1, keepdims=True)
    inverse = lax.rsqrt(jnp.mean(centre * centre, -1, keepdims=True) + EPSILON)
    return (centre * inverse, inverse)


def norm_back(normal, inverse, upstream):
    return inverse * (
        upstream
        - jnp.mean(upstream, -1, keepdims=True)
        - normal * jnp.mean(upstream * normal, -1, keepdims=True)
    )


def adam_update(weight, moment_one, moment_two, gradient, step_rate, decay_rate):
    first_new = BETA_ONE * moment_one + (1.0 - BETA_ONE) * gradient
    second_new = BETA_TWO * moment_two + (1.0 - BETA_TWO) * gradient * gradient
    first_hat = first_new / (1.0 - BETA_ONE**STEP)
    second_hat = second_new / (1.0 - BETA_TWO**STEP)
    weight_new = weight - step_rate * (
        first_hat / (jnp.sqrt(second_hat) + ADAM_EPSILON) + decay_rate * weight
    )
    return (first_new, second_new, weight_new)


def segments_of(lengths_row, length):
    ends = jnp.cumsum(lengths_row, dtype=jnp.int32)
    places = jnp.arange(length, dtype=jnp.int32)
    segment = jnp.sum((ends[None, :] <= places[:, None]).astype(jnp.int32), axis=1, dtype=jnp.int32)
    live = (places < ends[-1]).astype(jnp.float32)
    return segment, live


def matmul(left, right, dims):
    return lax.dot_general(left, right, (dims, ((), ())), preferred_element_type=jnp.float32)


NN = ((1,), (0,))
NT = ((1,), (1,))
TN = ((0,), (0,))


def attention_forward(stream, weight, mask):
    length, width = stream.shape
    size = width // HEADS
    packed = matmul(stream, weight[:, : 3 * width], NN).astype(jnp.bfloat16)
    heads = packed.reshape(length, 3, HEADS, size)
    scores = jnp.einsum("qhd,khd->hqk", heads[:, 0], heads[:, 1], preferred_element_type=jnp.float32)
    scores = jnp.where(mask[None], scores * size**-0.5, NEGATIVE)
    weights = jnp.exp(scores - jnp.max(scores, -1, keepdims=True))
    probs = weights / jnp.sum(weights, -1, keepdims=True)
    mixed = jnp.einsum("hqk,khd->qhd", probs.astype(jnp.bfloat16), heads[:, 2], preferred_element_type=jnp.float32)
    mixed = mixed.reshape(length, width).astype(jnp.bfloat16)
    branch = matmul(mixed, weight[:, 3 * width :], NN)
    return branch, (heads, probs, mixed)


def attention_backward(stream, weight, kept, grad_low):
    heads, probs, mixed = kept
    length, width = stream.shape
    size = width // HEADS
    grad_out = matmul(mixed, grad_low, TN)
    grad_mixed = matmul(grad_low, weight[:, 3 * width :], NT).astype(jnp.bfloat16)
    grad_mixed = grad_mixed.reshape(length, HEADS, size)
    grad_probs = jnp.einsum("qhd,khd->hqk", grad_mixed, heads[:, 2], preferred_element_type=jnp.float32)
    centre = jnp.sum(probs * grad_probs, -1, keepdims=True)
    grad_scores = (probs * (grad_probs - centre)).astype(jnp.bfloat16)
    low = probs.astype(jnp.bfloat16)
    scale = size**-0.5
    grad_q = jnp.einsum("hqk,khd->qhd", grad_scores, heads[:, 1], preferred_element_type=jnp.float32) * scale
    grad_k = jnp.einsum("hqk,qhd->khd", grad_scores, heads[:, 0], preferred_element_type=jnp.float32) * scale
    grad_v = jnp.einsum("hqk,qhd->khd", low, grad_mixed, preferred_element_type=jnp.float32)
    packed = jnp.concatenate([grad_q, grad_k, grad_v], axis=1).reshape(length, 3 * width)
    packed = packed.astype(jnp.bfloat16)
    grad_in = matmul(stream, packed, TN)
    grad_inputs = matmul(packed, weight[:, : 3 * width], NT)
    return grad_inputs, jnp.concatenate([grad_in, grad_out], axis=1)


def feed_forward(stream, weight, down):
    pre = matmul(stream, weight, NN)
    active = jax.nn.gelu(pre, approximate=True).astype(jnp.bfloat16)
    return matmul(active, down, NN), (pre, active)


def feed_backward(stream, weight, down, kept, grad_low):
    pre, active = kept
    grad_down = matmul(active, grad_low, TN)
    grad_active = matmul(grad_low, down, NT)
    pull = jax.vjp(lambda value: jax.nn.gelu(value, approximate=True), pre)[1]
    grad_pre = pull(grad_active)[0].astype(jnp.bfloat16)
    grad_up = matmul(stream, grad_pre, TN)
    return matmul(grad_pre, weight, NT), grad_up, grad_down


def micro_step(rows, pull, segment, mats, downs, gains, biases):
    low = jnp.bfloat16
    mask = segment[:, None] == segment[None, :]
    stream, dual = rows, jnp.zeros_like(rows)
    saved = []
    for sub in range(4):
        if sub % 2 == 0:
            branch, kept = attention_forward(stream, mats[sub], mask)
        else:
            branch, kept = feed_forward(stream, mats[sub], downs[sub // 2])
        normal, inverse = norm_stats(stream.astype(jnp.float32) + branch)
        out = normal * gains[sub] + biases[sub]
        total = dual.astype(jnp.float32) + branch
        saved.append((stream, kept, normal, inverse))
        if sub < 3:
            stream, dual = out.astype(low), total.astype(low)
    dual_normal, dual_inverse = norm_stats(total)
    output = (out + dual_normal).astype(low)
    grad_out, grad_dual = pull, norm_back(dual_normal, dual_inverse, pull)
    grads_a, grads_b, grads_n = [None] * 4, [None] * 2, [None] * 4
    for sub in (3, 2, 1, 0):
        stream, kept, normal, inverse = saved[sub]
        grads_n[sub] = jnp.stack([jnp.sum(grad_out * normal, 0), jnp.sum(grad_out, 0)], axis=1)
        summed = norm_back(normal, inverse, grad_out * gains[sub])
        branch_low = (summed + grad_dual).astype(low)
        if sub % 2 == 0:
            inner, grads_a[sub] = attention_backward(stream, mats[sub], kept, branch_low)
        else:
            inner, grads_a[sub], grads_b[sub // 2] = feed_backward(
                stream, mats[sub], downs[sub // 2], kept, branch_low
            )
        grad_in = summed + inner
        if sub > 0:
            grad_out = grad_in.astype(low).astype(jnp.float32)
            grad_dual = grad_dual.astype(low).astype(jnp.float32)
    return output, grad_in, jnp.stack(grads_a), jnp.stack(grads_b), jnp.stack(grads_n)


def finish_step(grad_norm, output, input_grad, *groups):
    factor = CLIP_NORM / jnp.maximum(grad_norm, CLIP_NORM)
    results = [grad_norm, output[None], input_grad[None]]
    for weight, one, two, grad, rate, decay in groups:
        clip = grad * factor
        moment, square_new, master = adam_update(weight, one, two, clip, rate, decay)
        results += [clip, moment, square_new, master, master.astype(jnp.bfloat16)]
    return tuple(results)


def body(
    tokens, cotangent, lengths, mat_a, mat_b, norms, first_a, second_a, first_b, second_b, first_n, second_n
):
    low = jnp.bfloat16
    own = lax.axis_index("section")
    length = tokens.shape[0] // lengths.shape[0]
    rows = lax.dynamic_slice_in_dim(tokens, own * length, length, 0)
    segment, live = segments_of(lax.dynamic_index_in_dim(lengths, own, 0, keepdims=False), length)
    pull = lax.dynamic_slice_in_dim(cotangent, own * length, length, 0).astype(jnp.float32) * live[:, None]

    def gathered(value):
        return lax.all_gather(lax.all_gather(value, "dp", axis=1, tiled=True), "section", axis=0, tiled=True)

    mats = gathered(mat_a.astype(low))
    scales = gathered(norms.astype(low)).astype(jnp.float32)
    downs = lax.all_gather(mat_b.astype(low), "section", axis=2, tiled=True)
    downs = lax.all_gather(downs, "dp", axis=1, tiled=True)
    output, input_grad, part_a, part_b, part_n = micro_step(
        rows, pull, segment, mats, downs, scales[:, :, 0], scales[:, :, 1]
    )

    def scattered(value, section_dim):
        value = lax.psum_scatter(value, "section", scatter_dimension=section_dim, tiled=True)
        return lax.psum_scatter(value, "dp", scatter_dimension=1, tiled=True).astype(jnp.float32)

    grad_a = scattered(part_a.astype(low), 0)
    grad_b = scattered(part_b.astype(low), 2)
    grad_n = scattered(part_n, 0)
    square = jnp.sum(grad_a * grad_a) + jnp.sum(grad_b * grad_b) + jnp.sum(grad_n * grad_n)
    grad_norm = jnp.sqrt(lax.psum(square, ("section", "dp")))
    return finish_step(
        grad_norm, output, input_grad,
        (mat_a, first_a, second_a, grad_a, MATRIX_RATE, MATRIX_DECAY),
        (mat_b, first_b, second_b, grad_b, MATRIX_RATE, MATRIX_DECAY),
        (norms, first_n, second_n, grad_n, NORM_RATE, 0.0),
    )


LOW = jnp.bfloat16
WIDE = jnp.float32
MESH = pl.DeviceIdType.MESH
SECTIONS = 4
LANES = 128
BLOCK = 64
ROWS_FIRST = (5,)
KERNEL_VMEM = 64 * 1024 * 1024 - 256 * 1024


def gradient_items(rows_a, rows_b, cols_b, width, hidden):
    part = rows_a // SECTIONS
    return (
        ("B1", 3, cols_b // 2, rows_b),
        ("F3", 3, part, hidden // 2),
        ("O2", 2, part, width // 2),
        ("K2", 2, part, 3 * width // 2),
        ("B0", 1, cols_b // 2, rows_b),
        ("F1", 1, part, hidden // 2),
        ("O0", 0, part, width // 2),
        ("K0", 0, part, 3 * width // 2),
    )


def item_scratch(name, chips, rows, columns):
    piece = (rows, columns)
    return (
        ("own" + name, (chips, SECTIONS, 2) + piece, LOW),
        ("farx" + name, (chips,) + piece, LOW),
        ("fary" + name, (chips,) + piece, LOW),
        ("nearx" + name, (2, chips) + piece, LOW),
        ("neary" + name, (2, chips) + piece, LOW),
        ("line" + name, (chips, 2) + piece, LOW),
        ("done" + name, (2,) + piece if name[0] == "B" else (SECTIONS, 2) + piece, WIDE if name[0] == "B" else LOW),
    )


def kernel_scratch(chips, rows_a, rows_b, cols_b, length, width, hidden):
    devices = 2 * chips
    items = gradient_items(rows_a, rows_b, cols_b, width, hidden)
    count = len(items)
    received = sum((item_scratch(name, chips, rows, columns) for name, _, rows, columns in items), ())
    return received + (
        ("fac_s", (32,), None),
        ("fac_r", (32,), None),
        ("px_s", (count, 3), None),
        ("px_r", (count, 3), None),
        ("py_s", (count, 3), None),
        ("py_r", (count, 3), None),
        ("line_s", (count, chips), None),
        ("line_r", (count, chips), None),
        ("done_s", (count,), None),
        ("done_r", (count, SECTIONS), None),
        ("wa", (4, chips, 2, SECTIONS, rows_a // SECTIONS, hidden), LOW),
        ("wb", (2, chips, 2, SECTIONS, rows_b, cols_b), LOW),
        ("in_a", (1, rows_a, hidden), WIDE),
        ("in_b", (2, rows_b, cols_b), WIDE),
        ("in_n", (1, 2, rows_a), WIDE),
        ("out_a", (rows_a, hidden), WIDE),
        ("out_b", (2, rows_b, cols_b), WIDE),
        ("out_n", (2, rows_a), WIDE),
        ("out_square", (8, LANES), WIDE),
        ("out_output", (length, width), LOW),
        ("out_input", (length, width), WIDE),
        ("cut", (SECTIONS, rows_a // SECTIONS, hidden), LOW),
        ("tiles", (devices, SECTIONS, 8, LANES), WIDE),
        ("x", (4, length, width), LOW),
        ("xt", (4, chips, 2, rows_a, length), LOW),
        ("xtc", (4, chips, rows_a, 2 * length), LOW),
        ("y", (length, width), LOW),
        ("cot", (length, width), LOW),
        ("bias", (length, length), WIDE),
        ("live", (length, 1), WIDE),
        ("f", (length, width), WIDE),
        ("n", (4, length, width), WIDE),
        ("inv", (4, length, 1), WIDE),
        ("q", (2, length, width), LOW),
        ("k", (2, length, width), LOW),
        ("v", (2, length, width), LOW),
        ("kt", (2, width, length), LOW),
        ("vt", (2, width, length), LOW),
        ("ot", (2, chips, 2, rows_a, length), LOW),
        ("otc", (2, chips, rows_a, 2 * length), LOW),
        ("pt", (2, HEADS, length, length), LOW),
        ("g", (2, length, hidden), LOW),
        ("gc", (2, chips, 2 * length, rows_b), LOW),
        ("slope", (2, length, hidden), LOW),
        ("gx", (length, width), WIDE),
        ("gy", (length, width), WIDE),
        ("df", (2, 2 * length, width), LOW),
        ("dft", (2, width, 2 * length), LOW),
        ("dm", (length, width), LOW),
        ("dqt", (width, length), LOW),
        ("dh", (2, 2 * length, hidden), LOW),
        ("dp", (2, 2 * length, 3 * width), LOW),
        ("ng", (devices, 8, width), WIDE),
        ("ns", (SECTIONS, 8, width), WIDE),
        ("sq", (devices, 8, LANES), WIDE),
        ("sqs", (SECTIONS, 8, LANES), WIDE),
        ("sum", (8, LANES), WIDE),
        ("in_s", (5,), None),
        ("out_s", (6,), None),
        ("cut_s", (1,), None),
        ("cut_r", (SECTIONS,), None),
        ("gz_s", (6,), None),
        ("gz_r", (6, chips), None),
        ("gx_s", (6,), None),
        ("gx_r", (6,), None),
        ("gy_s", (6,), None),
        ("gy_r", (6,), None),
        ("rx_s", (6,), None),
        ("rx_r", (6,), None),
        ("ry_s", (6,), None),
        ("ry_r", (6,), None),
        ("gs_s", (6,), None),
        ("gs_r", (6,), None),
        ("small_s", (3, 2), None),
        ("small_r", (3, 2), None),
    )


INPUTS = ("tokens", "cotangent", "lengths", "mat_a", "mat_b", "norms")
OUTPUTS = ("grad_a", "grad_b", "grad_n", "square", "output", "input_grad")


def step_kernel(names, *refs):
    r = types.SimpleNamespace(**dict(zip(names, refs)))
    length, width = r.x.shape[1:]
    hidden = r.wa.shape[-1]
    rows_a, (rows_b, cols_b) = r.mat_a.shape[1], r.mat_b.shape[1:]
    devices = r.tiles.shape[0]
    chips = devices // 2
    half_b = cols_b // 2
    grad_items = gradient_items(rows_a, rows_b, cols_b, width, hidden)
    head = width // HEADS
    scale = head**-0.5

    s, d = lax.axis_index("section"), lax.axis_index("dp")
    z, c = lax.div(d, 2), lax.rem(d, 2)
    sx = s + 1 - 2 * lax.rem(s, 2)
    sy = lax.rem(s + 2, SECTIONS)
    sd = SECTIONS - 1 - s
    to_sibling = {"dp": d + 1 - 2 * c}
    to_up, to_down = {"dp": d + 2}, {"dp": d - 2}
    to_x, to_y = {"section": sx}, {"section": sy}
    below, above = z > 0, z < chips - 1
    group = [{"dp": lax.rem(d + step, devices)} for step in range(1, devices)]
    plane = [{"section": lax.rem(s + step, SECTIONS)} for step in range(1, SECTIONS)]
    finish = []

    def when(condition, work):
        if condition is None:
            work()
        else:
            pl.when(condition)(work)

    def push(source, target, send_sem, recv_sem, device):
        pltpu.make_async_remote_copy(
            src_ref=source,
            dst_ref=target,
            send_sem=send_sem,
            recv_sem=recv_sem,
            device_id=device,
            device_id_type=MESH,
        ).start()

    def arrived(target, sem):
        pltpu.make_async_remote_copy(
            src_ref=target, dst_ref=target, send_sem=sem, recv_sem=sem, device_id=to_x, device_id_type=MESH
        ).wait_recv()

    def sent(source, sem):
        pltpu.make_async_remote_copy(
            src_ref=source, dst_ref=source, send_sem=sem, recv_sem=sem, device_id=to_x, device_id_type=MESH
        ).wait_send()

    def at_end(condition, source, sem):
        finish.append((condition, source, sem))

    def aligned(start, size):
        return pl.ds(pl.multiple_of(start, size), size)

    own_x = pltpu.make_async_copy(r.tokens.at[aligned(s * length, length)], r.x.at[0], r.in_s.at[0])
    own_cot = pltpu.make_async_copy(r.cotangent.at[aligned(s * length, length)], r.cot, r.in_s.at[1])
    own_a = pltpu.make_async_copy(r.mat_a, r.in_a, r.in_s.at[2])
    own_b = pltpu.make_async_copy(r.mat_b, r.in_b, r.in_s.at[3])
    own_n = pltpu.make_async_copy(r.norms, r.in_n, r.in_s.at[4])
    own_a.start()
    own_n.start()
    own_b.start()
    own_x.start()
    own_cot.start()
    barrier = pltpu.get_barrier_semaphore()
    for peer in group + plane:
        pl.semaphore_signal(barrier, inc=1, device_id=peer, device_id_type=MESH)
    own_a.wait()
    r.cut[...] = r.in_a[0].astype(LOW).reshape(SECTIONS, rows_a // SECTIONS, hidden)
    r.wa[s, z, c, s] = r.cut[s]
    own_n.wait()
    norms = r.in_n[0].astype(LOW).astype(WIDE)
    nothing = jnp.zeros((2, rows_a), WIDE)
    even = jnp.concatenate([norms, nothing], axis=1)
    odd = jnp.concatenate([nothing, norms], axis=1)
    r.tiles[d, s, 0:2, :] = jnp.where(c == 0, even, odd)
    r.tiles[d, s, 2:8, :] = jnp.zeros((6, LANES), WIDE)
    own_b.wait()
    for layer in range(2):
        r.wb[layer, z, c, s] = r.in_b[layer].astype(LOW)
    pl.semaphore_wait(barrier, len(group) + len(plane))

    def put_out(slot, source, target):
        made = pltpu.make_async_copy(source, target, r.out_s.at[slot])
        made.start()
        return made

    def small_out(which, source):
        for peer in group:
            push(source, source, r.small_s.at[which, 0], r.small_r.at[which, 0], peer)

    def small_group(which, like):
        arrived(like, r.small_r.at[which, 0])
        sent(like, r.small_s.at[which, 0])

    def small_plane_out(which, source):
        for peer in plane:
            push(source, source, r.small_s.at[which, 1], r.small_r.at[which, 1], peer)

    def small_plane(which, like):
        arrived(like, r.small_r.at[which, 1])
        sent(like, r.small_s.at[which, 1])

    every = slice(None)

    def block(item, chip, section):
        if item < 4:
            return r.wa.at[item, chip, c, section]
        return r.wb.at[item - 4, chip, c, section]

    def half_block(item, section, half):
        if item < 4:
            return r.wa.at[item, :, c, section, :, pl.ds(half * hidden // 2, hidden // 2)]
        rows = pl.ds(half * rows_b // 2, rows_b // 2)
        return r.wb.at[item - 4, :, c, section, rows]

    def half_piece(item, section, half):
        rows = pl.ds(half * rows_b // 2, rows_b // 2)
        return r.wb.at[item - 4, z, c, section, rows]

    def core_blocks(item, core):
        return r.wa.at[item, :, core] if item < 4 else r.wb.at[item - 4, :, core]

    def cut_out():
        for section, device in ((sd, {"section": sd}), (sx, to_x), (sy, to_y)):
            push(r.cut.at[section], r.wa.at[s, z, c, section], r.cut_s.at[0], r.cut_r.at[s], device)
        at_end(None, r.cut.at[pl.ds(0, SECTIONS - 1)], r.cut_s.at[0])

    def cut_in():
        for section in (sx, sy, sd):
            arrived(r.wa.at[section, z, c, s], r.cut_r.at[section])

    def line_out(item):
        if item in ROWS_FIRST:
            rows_out(item)
            return
        own = block(item, z, s)
        for step in range(1, chips):
            push(own, own, r.gz_s.at[item], r.gz_r.at[item, z], {"dp": 2 * lax.rem(z + step, chips) + c})
        several = block(item, pl.ds(0, chips - 1), s)
        at_end(None, several, r.gz_s.at[item])

    def plane_out(item, chip):
        own = block(item, chip, s)
        push(own, own, r.gx_s.at[item], r.gx_r.at[item], to_x)
        push(own, own, r.gy_s.at[item], r.gy_r.at[item], to_y)

    def rows_out(item):
        arrived(half_piece(item, sd, 0), r.rx_r.at[item])
        arrived(half_piece(item, sd, 1), r.ry_r.at[item])
        rows = r.wb.at[item - 4, z, c]
        for step in range(1, chips):
            push(rows, rows, r.gz_s.at[item], r.gz_r.at[item, z], {"dp": 2 * lax.rem(z + step, chips) + c})
        push(rows, rows, r.gs_s.at[item], r.gs_r.at[item], to_sibling)
        at_end(None, r.wb.at[item - 4, pl.ds(0, chips - 1), c], r.gz_s.at[item])

    def rows_in(item):
        for step in range(1, chips):
            chip = lax.rem(z + step, chips)
            rows = r.wb.at[item - 4, chip, c]
            arrived(rows, r.gz_r.at[item, chip])
            push(rows, rows, r.gs_s.at[item], r.gs_r.at[item], to_sibling)
        at_end(None, core_blocks(item, c), r.gs_s.at[item])

    def line_in(item):
        if item in ROWS_FIRST:
            rows_in(item)
            return
        for step in range(1, chips):
            chip = lax.rem(z + step, chips)
            arrived(block(item, chip, s), r.gz_r.at[item, chip])
            plane_out(item, chip)
        core_out(item, s)
        at_end(None, block(item, every, s), r.gx_s.at[item])
        at_end(None, block(item, every, s), r.gy_s.at[item])

    def core_out(item, section):
        blocks = block(item, every, section)
        push(blocks, blocks, r.gs_s.at[item], r.gs_r.at[item], to_sibling)

    def plane_in(item):
        over = z if item in ROWS_FIRST else every
        piece = half_piece if item in ROWS_FIRST else half_block
        arrived(block(item, over, sx), r.gx_r.at[item])
        part = piece(item, sx, 1)
        push(part, part, r.ry_s.at[item], r.ry_r.at[item], to_y)
        arrived(block(item, over, sy), r.gy_r.at[item])
        part = piece(item, sy, 0)
        push(part, part, r.rx_s.at[item], r.rx_r.at[item], to_x)
        if item in ROWS_FIRST:
            at_end(None, block(item, z, sx), r.gx_s.at[item])
            at_end(None, block(item, z, sx), r.gy_s.at[item])
        else:
            core_out(item, sx)
            core_out(item, sy)
        at_end(None, part, r.ry_s.at[item])
        at_end(None, part, r.rx_s.at[item])

    def far_in(item):
        arrived(half_block(item, sd, 0), r.rx_r.at[item])
        arrived(half_block(item, sd, 1), r.ry_r.at[item])
        core_out(item, sd)
        at_end(None, core_blocks(item, c), r.gs_s.at[item])

    def core_in(item):
        arrived(core_blocks(item, 1 - c), r.gs_r.at[item])

    mine, other = pl.ds(0, length), pl.ds(length, length)

    def give(slot, source, target):
        push(source, target, r.fac_s.at[slot], r.fac_r.at[slot], to_sibling)
        at_end(None, target, r.fac_s.at[slot])

    def taken(slot, target):
        arrived(target, r.fac_r.at[slot])

    def give_rows(layer):
        r.xt[layer] = r.x[layer].T.reshape(chips, 2, rows_a, length)
        r.xtc[layer, :, :, 0:length] = r.xt[layer, :, c]
        give(layer, r.xt.at[layer, :, 1 - c], r.xtc.at[layer, :, :, other])

    def product(left, right, dims):
        return lax.dot_general(left, right, (dims, ((), ())), preferred_element_type=WIDE)

    def gain_row(layer, kind):
        parts = [
            r.tiles[2 * chip, layer, kind : kind + 1, :] + r.tiles[2 * chip + 1, layer, kind : kind + 1, :]
            for chip in range(chips)
        ]
        return jnp.concatenate(parts, axis=1)

    def stats(value):
        centre = value - jnp.mean(value, -1, keepdims=True)
        inverse = lax.rsqrt(jnp.mean(centre * centre, -1, keepdims=True) + EPSILON)
        return centre * inverse, inverse

    lane = lax.broadcasted_iota(jnp.int32, (1, 2 * head), 1)
    first_half = (lane < head).astype(WIDE)
    half_masks = (first_half.astype(LOW), (1.0 - first_half).astype(LOW))

    def prepare_masks():
        ends, total = [], jnp.int32(0)
        for slot in range(r.lengths.shape[1]):
            total = total + r.lengths[s, slot]
            ends.append(total)
        down_places = lax.broadcasted_iota(jnp.int32, (length, 1), 0)
        across_places = lax.broadcasted_iota(jnp.int32, (1, length), 1)
        down_segment = jnp.zeros((length, 1), jnp.int32)
        across_segment = jnp.zeros((1, length), jnp.int32)
        for end in ends:
            down_segment = down_segment + (end <= down_places).astype(jnp.int32)
            across_segment = across_segment + (end <= across_places).astype(jnp.int32)
        r.bias[...] = jnp.where(down_segment == across_segment, 0.0, NEGATIVE)
        r.live[...] = (down_places < total).astype(WIDE)

    def matrix(layer, place):
        value = r.wa[layer, :, :, :, :, place]
        return value.reshape(width, value.shape[-1])

    def down(at, chip=slice(None)):
        blocks = [r.wb[at, chip, :, section] for section in range(SECTIONS)]
        return jnp.concatenate([block.reshape(-1, cols_b) for block in blocks], axis=1)

    def turn_keys(at):
        r.kt[at] = (r.k[at] * jnp.asarray(scale, LOW)).T

    def attention_in(layer):
        at = layer // 2
        rows = r.x[layer]
        r.q[at] = product(rows, matrix(layer, pl.ds(0, width)), NN).astype(LOW) * jnp.asarray(scale, LOW)
        keys = product(rows, matrix(layer, pl.ds(width, width)), NN).astype(LOW)
        r.k[at] = keys
        values = product(rows, matrix(layer, pl.ds(2 * width, width)), NN).astype(LOW)
        r.v[at] = values
        r.vt[at] = values.T

    def attention_heads(layer, begin, count):
        at = layer // 2

        def pair(index):
            lanes = pl.ds(index * 2 * head, 2 * head)
            for which in range(2):
                scores = product(r.k[at, :, lanes], r.q[at, :, lanes] * half_masks[which], NT) + r.bias[...]
                weights = jnp.exp(scores - jnp.max(scores, 0, keepdims=True))
                probs = (weights * (1.0 / jnp.sum(weights, 0, keepdims=True))).astype(LOW)
                r.pt[at, 2 * index + which] = probs
                place = pl.ds((2 * index + which) * head, head)
                r.ot[at, index, which] = product(r.vt[at, place, :], probs, NN).astype(LOW)

        for index in range(begin, begin + count):
            pair(index)

    def attention_out(layer):
        at = layer // 2
        r.otc[at, :, :, 0:length] = r.ot[at, :, c]
        give(4 + at, r.ot.at[at, :, 1 - c], r.otc.at[at, :, :, other])
        r.f[...] = product(r.ot[at].reshape(width, length).T, matrix(layer, pl.ds(3 * width, width)), NN)

    def expand(layer, index):
        at = layer // 2
        place = pl.ds(index * width, width)
        pre = product(r.x[layer], matrix(layer, place), NN)
        squared = pre * pre
        slope = 0.7978845608 * (1.0 + 3 * 0.044715 * squared)
        bent = jnp.tanh(0.7978845608 * pre * (1.0 + 0.044715 * squared))
        r.g[at, :, place] = (0.5 * pre * (1.0 + bent)).astype(LOW)
        r.slope[at, :, place] = (0.5 * (1.0 + bent) + 0.5 * pre * (1.0 - bent * bent) * slope).astype(LOW)
        block = aligned((2 * index + c) * rows_b, rows_b)
        r.gc[at, index, 0:length, :] = r.g[at, :, block]
        block = aligned((2 * index + 1 - c) * rows_b, rows_b)
        give(6 + chips * at + index, r.g.at[at, :, block], r.gc.at[at, index, other, :])

    def contract(layer):
        r.f[...] = product(r.g[layer // 2], down(layer // 2), NN)

    def by_rows(work):
        for index in range(length // BLOCK):
            work(pl.ds(index * BLOCK, BLOCK))

    def normalize(layer):
        gain, offset = gain_row(layer, 0), gain_row(layer, 1)

        def some(rows):
            branch = r.f[rows, :]
            normal, inverse = stats(r.x[layer, rows, :].astype(WIDE) + branch)
            r.n[layer, rows, :] = normal
            r.inv[layer, rows, :] = inverse
            out = normal * gain + offset
            dual = branch if layer == 0 else r.y[rows, :].astype(WIDE) + branch
            if layer < 3:
                r.x[layer + 1, rows, :] = out.astype(LOW)
                r.y[rows, :] = dual.astype(LOW)
            else:
                dual_normal, dual_inverse = stats(dual)
                r.out_output[rows, :] = (out + dual_normal).astype(LOW)
                pull = r.cot[rows, :].astype(WIDE) * r.live[rows, :]
                r.gx[rows, :] = pull
                r.gy[rows, :] = norm_back(dual_normal, dual_inverse, pull)

        by_rows(some)

    def back_normalize(layer):
        gain = gain_row(layer, 0)

        def some(index, sums):
            rows = pl.ds(index * BLOCK, BLOCK)
            upstream = r.gx[rows, :]
            normal = r.n[layer, rows, :]
            summed = norm_back(normal, r.inv[layer, rows, :], upstream * gain)
            dual = r.gy[rows, :]
            r.gx[rows, :] = summed
            r.df[layer // 2, rows, :] = (summed + dual).astype(LOW)
            if layer == 3:
                r.gy[rows, :] = dual.astype(LOW).astype(WIDE)
            return (
                sums[0] + jnp.sum(upstream * normal, 0, keepdims=True),
                sums[1] + jnp.sum(upstream, 0, keepdims=True),
            )

        zero = jnp.zeros((1, width), WIDE)
        gains, offsets = zero, zero
        for index in range(length // BLOCK):
            gains, offsets = some(index, (gains, offsets))
        r.ng[d, 2 * layer : 2 * layer + 1, :] = gains
        r.ng[d, 2 * layer + 1 : 2 * layer + 2, :] = offsets

    def pass_down(layer, inner):
        total = r.gx[...] + inner
        if layer > 0:
            r.gx[...] = total.astype(LOW).astype(WIDE)
        else:
            r.out_input[...] = total

    base = 6 + 2 * chips

    def back_hidden(layer):
        at = layer // 2
        r.dft[at, :, 0:length] = r.df[at, 0:length, :].T
        give(base + at, r.dft.at[at, :, mine], r.dft.at[at, :, other])
        for index in range(hidden // width):
            place = pl.ds(index * width, width)
            pulled = product(r.df[at, 0:length, :], down(at, pl.ds(index, 1)), NT)
            r.dh[at, 0:length, place] = (pulled * r.slope[at, :, place].astype(WIDE)).astype(LOW)
            give(base + 2 + chips * at + index, r.dh.at[at, mine, place], r.dh.at[at, other, place])

    def back_expand_end(layer):
        pass_down(layer, product(r.dh[layer // 2, 0:length, :], matrix(layer, pl.ds(0, hidden)), NT))

    def back_output(layer):
        at = layer // 2
        give(base + 2 + 2 * chips + at, r.df.at[at, mine], r.df.at[at, other])
        r.dm[...] = product(r.df[at, 0:length, :], matrix(layer, pl.ds(3 * width, width)), NT).astype(LOW)

    def back_heads(layer, begin, count):
        at = layer // 2

        def pair(index):
            lanes = pl.ds(index * 2 * head, 2 * head)
            pulled = r.dm[:, lanes]
            keys, values = [], []
            for which in range(2):
                probs = r.pt[at, 2 * index + which]
                grad = product(r.v[at, :, lanes], pulled * half_masks[which], NT)
                full = probs.astype(WIDE)
                centre = jnp.sum(full * grad, 0, keepdims=True)
                scores = (full * (grad - centre)).astype(LOW)
                keys.append(product(scores, r.q[at, :, lanes], NN))
                values.append(product(probs, pulled, NN))
                place = pl.ds((2 * index + which) * head, head)
                r.dqt[place, :] = product(r.kt[at, place, :], scores, NN).astype(LOW)
            r.dp[at, 0:length, pl.ds(width + index * 2 * head, 2 * head)] = jnp.where(
                lane < head, keys[0], keys[1]
            ).astype(LOW)
            r.dp[at, 0:length, pl.ds(2 * width + index * 2 * head, 2 * head)] = jnp.where(
                lane < head, values[0], values[1]
            ).astype(LOW)

        for index in range(begin, begin + count):
            pair(index)

    def back_packed(layer):
        at = layer // 2
        slot = base + 4 + 2 * chips + 2 * at
        place = pl.ds(width, 2 * width)
        give(slot, r.dp.at[at, mine, place], r.dp.at[at, other, place])
        r.dp[at, 0:length, 0:width] = r.dqt[...].T
        place = pl.ds(0, width)
        give(slot + 1, r.dp.at[at, mine, place], r.dp.at[at, other, place])

    def back_packed_end(layer):
        pass_down(layer, product(r.dp[layer // 2, 0:length, :], matrix(layer, pl.ds(0, 3 * width)), NT))

    def keep(name, half, place, value):
        own = getattr(r, "own" + name)
        own[:, :, half, :, place] = value.astype(LOW).reshape(chips, SECTIONS, rows_a // SECTIONS, value.shape[1])

    def chip_rows(value):
        return value.reshape(chips * rows_a, 2 * length)

    def grad_down(at):
        own = getattr(r, "ownB%d" % at)
        taken(base + at, r.dft.at[at, :, other])
        for chip in range(chips):
            taken(6 + chips * at + chip, r.gc.at[at, chip, other, :])
            value = product(r.dft[at], r.gc[at, chip], NN)
            own[chip] = value.astype(LOW).reshape(SECTIONS, 2, half_b, rows_b)

    def grad_up(layer):
        at = layer // 2
        taken(layer, r.xtc.at[layer, :, :, other])
        for index in range(hidden // width):
            place = pl.ds(index * width, width)
            taken(base + 2 + chips * at + index, r.dh.at[at, other, place])
            value = product(chip_rows(r.xtc[layer]), r.dh[at, :, place], NN)
            keep("F%d" % layer, index // 2, pl.ds(index % 2 * width, width), value)

    def grad_output(layer):
        at = layer // 2
        taken(4 + at, r.otc.at[at, :, :, other])
        taken(base + 2 + 2 * chips + at, r.df.at[at, other])
        for half in range(2):
            place = pl.ds(half * width // 2, width // 2)
            value = product(chip_rows(r.otc[at]), r.df[at, :, place], NN)
            keep("O%d" % layer, half, pl.ds(0, width // 2), value)

    def grad_packed(layer):
        at = layer // 2
        slot = base + 4 + 2 * chips + 2 * at
        taken(layer, r.xtc.at[layer, :, :, other])
        taken(slot, r.dp.at[at, other, pl.ds(width, 2 * width)])
        taken(slot + 1, r.dp.at[at, other, pl.ds(0, width)])
        part = 3 * width // 2
        for half in range(2):
            value = product(chip_rows(r.xtc[layer]), r.dp[at, :, half * part : (half + 1) * part], NN)
            keep("K%d" % layer, half, pl.ds(0, part), value)

    def joined(target, others):
        return functools.reduce(
            lambda left, right: left + right, [ref[...].astype(WIDE) for ref in (target, *others)]
        )

    def add_into(target, others):
        if len(others) < 3:
            target[...] = functools.reduce(lambda left, right: left + right, [ref[...] for ref in (target, *others)])
        else:
            target[...] = joined(target, others).astype(LOW)

    places = {name: place for place, (name, _, _, _) in enumerate(grad_items)}

    def buffers(name):
        parts = ("own", "farx", "fary", "nearx", "neary", "line", "done")
        return types.SimpleNamespace(**{part: getattr(r, part + name) for part in parts})

    def to_plane(name):
        item, place = buffers(name), places[name]

        def over_x(section, half, target, slot):
            push(item.own.at[:, section, half], target, r.px_s.at[place, slot], r.px_r.at[place, slot], to_x)
            at_end(None, item.farx, r.px_s.at[place, slot])

        def over_y(section, half, target, slot):
            push(item.own.at[:, section, half], target, r.py_s.at[place, slot], r.py_r.at[place, slot], to_y)
            at_end(None, item.farx, r.py_s.at[place, slot])

        over_x(sd, 0, item.farx, 2)
        over_y(sd, 1, item.fary, 2)
        over_x(sx, 0, item.nearx.at[0], 0)
        over_y(sy, 1, item.neary.at[1], 1)

    def through_plane(name):
        item, place = buffers(name), places[name]
        own = item.own
        arrived(item.fary, r.py_r.at[place, 2])
        add_into(own.at[:, sx, 1], [item.fary])
        push(own.at[:, sx, 1], item.nearx.at[1], r.px_s.at[place, 1], r.px_r.at[place, 1], to_x)
        at_end(None, item.farx, r.px_s.at[place, 1])
        arrived(item.farx, r.px_r.at[place, 2])
        add_into(own.at[:, sy, 0], [item.farx])
        push(own.at[:, sy, 0], item.neary.at[0], r.py_s.at[place, 0], r.py_r.at[place, 0], to_y)
        at_end(None, item.farx, r.py_s.at[place, 0])

    def to_line(name):
        item, place = buffers(name), places[name]
        own = item.own.at[:, s]
        for half in range(2):
            arrived(item.nearx.at[half], r.px_r.at[place, half])
            arrived(item.neary.at[half], r.py_r.at[place, half])
            add_into(own.at[:, half], [item.nearx.at[half], item.neary.at[half]])
        for step in range(1, chips):
            chip = lax.rem(z + step, chips)
            push(
                own.at[chip],
                item.line.at[z],
                r.line_s.at[place, step],
                r.line_r.at[place, z],
                {"dp": 2 * chip + c},
            )
            at_end(None, item.line.at[0], r.line_s.at[place, step])

    def to_owner(name):
        item, place = buffers(name), places[name]
        others = [lax.rem(z + step, chips) for step in range(1, chips)]
        for chip in others:
            arrived(item.line.at[chip], r.line_r.at[place, chip])
        total = joined(item.own.at[z, s], [item.line.at[chip] for chip in others])
        square = total * total
        while square.ndim > 2:
            square = jnp.sum(square, 0)
        square = jnp.sum(jnp.sum(square, 0, keepdims=True), 1, keepdims=True)
        r.sum[...] = r.sum[...] + jnp.broadcast_to(square, (8, LANES))
        if name[0] == "B":
            item.done[...] = total
            return
        item.done[s] = total.astype(LOW)
        layer = grad_items[place][1]
        mine = item.done.at[s]
        away = s != layer
        when(
            away,
            lambda: push(mine, mine, r.done_s.at[place], r.done_r.at[place, s], {"section": jnp.int32(layer)}),
        )
        at_end(away, mine, r.done_s.at[place])

    def collect(name):
        item, place = buffers(name), places[name]
        layer = grad_items[place][1]

        def work():
            for section in range(SECTIONS):
                if section != layer:
                    arrived(item.done.at[section], r.done_r.at[place, section])
            columns = item.done.shape[-1]
            start = 3 * width if name[0] == "O" else 0
            for section in range(SECTIONS):
                for half in range(2):
                    rows = pl.ds(section * (rows_a // SECTIONS), rows_a // SECTIONS)
                    place_to = pl.ds(start + half * columns, columns)
                    r.out_a[rows, place_to] = item.done[section, half].astype(WIDE)

        when(s == layer, work)

    def all_sent(count=None):
        for condition, source, sem in finish[:count]:
            when(condition, functools.partial(sent, source, sem))
        del finish[:count]

    cut_out()
    plane_out(5, z)
    line_out(4)
    plane_out(4, z)
    small_out(0, r.tiles.at[d, s])
    cut_in()
    plane_out(1, z)
    line_out(0)
    plane_out(0, z)
    line_out(1)
    line_out(2)
    plane_out(3, z)
    line_out(3)
    line_in(4)
    small_group(0, r.tiles.at[pl.ds(0, devices - 1), 0])
    for peer in plane:
        push(r.tiles.at[:, s], r.tiles.at[:, s], r.small_s.at[0, 1], r.small_r.at[0, 1], peer)
    line_in(0)
    plane_in(5)
    line_in(1)
    plane_in(0)
    plane_out(2, z)
    plane_in(1)
    far_in(0)
    line_in(2)
    plane_in(4)
    line_out(5)
    own_x.wait()
    own_cot.wait()
    prepare_masks()
    give_rows(0)
    core_in(0)
    attention_in(0)
    far_in(1)
    attention_heads(0, 0, 2)
    attention_heads(0, 2, 2)
    plane_in(2)
    attention_out(0)
    small_plane(0, r.tiles.at[:, pl.ds(0, SECTIONS - 1)])
    normalize(0)
    far_in(4)
    core_in(1)
    line_in(3)
    expand(1, 0)
    expand(1, 1)
    early = len(finish)
    far_in(2)
    expand(1, 2)
    expand(1, 3)
    core_in(4)
    contract(1)
    normalize(1)
    core_in(2)
    plane_in(3)
    attention_in(2)
    attention_heads(2, 0, 2)
    attention_heads(2, 2, 2)
    far_in(3)
    attention_out(2)
    line_in(5)
    normalize(2)
    core_in(3)
    expand(3, 0)
    expand(3, 1)
    expand(3, 2)
    expand(3, 3)
    for layer in (3, 2, 1):
        give_rows(layer)
    for at in (1, 0):
        turn_keys(at)
    all_sent(early)
    core_in(5)
    contract(3)
    normalize(3)
    leaving = [put_out(0, r.out_output, r.output)]

    r.sum[...] = jnp.zeros((8, LANES), WIDE)
    back_normalize(3)
    back_hidden(3)
    back_expand_end(3)
    back_normalize(2)
    grad_up(3)
    to_plane("F3")
    back_output(2)
    grad_down(1)
    to_plane("B1")
    back_heads(2, 0, 2)
    back_heads(2, 2, 2)
    back_packed(2)
    through_plane("B1")
    grad_output(2)
    back_packed_end(2)
    to_plane("O2")
    grad_packed(2)
    to_plane("K2")
    back_normalize(1)
    back_hidden(1)
    through_plane("K2")
    grad_down(0)
    to_plane("B0")
    back_expand_end(1)
    back_normalize(0)
    small_out(1, r.ng.at[d])
    to_line("K2")
    to_line("B1")
    back_output(0)
    grad_up(1)
    through_plane("B0")
    to_plane("F1")
    back_heads(0, 0, 2)
    back_heads(0, 2, 2)
    back_packed(0)
    to_line("B0")
    through_plane("O2")
    through_plane("F1")
    grad_output(0)
    to_plane("O0")
    grad_packed(0)
    to_plane("K0")
    to_line("O2")
    to_line("F1")
    through_plane("O0")
    to_owner("B1")
    back_packed_end(0)
    leaving.append(put_out(1, r.out_input, r.input_grad))
    to_owner("B0")
    all_sent(len(finish) // 3)
    through_plane("K0")
    small_group(1, r.ng.at[pl.ds(0, devices - 1)])
    r.ns[s] = functools.reduce(lambda left, right: left + right, [r.ng[index] for index in range(devices)])
    small_plane_out(1, r.ns.at[s])
    through_plane("F3")
    to_line("O0")
    all_sent(len(finish) // 3)
    to_line("K0")
    to_owner("F1")
    to_line("F3")
    to_owner("O2")
    to_owner("K2")
    to_owner("F3")
    to_owner("O0")
    all_sent(len(finish) // 3)
    to_owner("K0")

    r.sq[d] = r.sum[...]
    small_out(2, r.sq.at[d])
    for name in ("F1", "O2", "K2", "F3"):
        collect(name)
    collect("O0")
    for layer in range(2):
        done = buffers("B%d" % layer).done
        r.out_b[layer] = done[...].reshape(cols_b, rows_b).T
    leaving.append(put_out(2, r.out_b, r.grad_b))
    small_plane(1, r.ns.at[pl.ds(0, SECTIONS - 1)])
    grads = functools.reduce(lambda left, right: left + right, [r.ns[index] for index in range(SECTIONS)])
    norm_square = jnp.sum(jnp.sum(grads * grads, 0, keepdims=True), 1, keepdims=True)
    chosen = jnp.zeros((2, width), WIDE)
    for layer in range(4):
        chosen = jnp.where(s == layer, grads[2 * layer : 2 * layer + 2, :], chosen)
    shard = jnp.zeros((2, rows_a), WIDE)
    for chip in range(chips):
        pair_of = chosen[:, chip * LANES : (chip + 1) * LANES]
        shard = jnp.where(z == chip, jnp.where(c == 0, pair_of[:, :rows_a], pair_of[:, rows_a:]), shard)
    r.out_n[...] = shard
    leaving.append(put_out(3, r.out_n, r.grad_n))
    collect("K0")
    leaving.append(put_out(4, r.out_a, r.grad_a))
    small_group(2, r.sq.at[pl.ds(0, devices - 1)])
    r.sqs[s] = functools.reduce(lambda left, right: left + right, [r.sq[index] for index in range(devices)])
    small_plane_out(2, r.sqs.at[s])
    all_sent()
    small_plane(2, r.sqs.at[pl.ds(0, SECTIONS - 1)])
    squares = functools.reduce(lambda left, right: left + right, [r.sqs[index] for index in range(SECTIONS)])
    r.out_square[...] = squares + norm_square
    leaving.append(put_out(5, r.out_square, r.square))
    for made in leaving:
        made.wait()


def step_call(tokens, cotangent, lengths, mat_a, mat_b, norms):
    rows_a, hidden = mat_a.shape[1:]
    rows_b, cols_b = mat_b.shape[1:]
    width = tokens.shape[1]
    length = tokens.shape[0] // lengths.shape[0]
    chips = width // rows_a // 2
    scratch = kernel_scratch(chips, rows_a, rows_b, cols_b, length, width, hidden)
    shapes = []
    for _, shape, kind in scratch:
        shapes.append(pltpu.SemaphoreType.DMA(shape) if kind is None else pltpu.VMEM(shape, kind))
    anywhere = pl.BlockSpec(memory_space=pl.ANY)
    return pl.pallas_call(
        functools.partial(step_kernel, INPUTS + OUTPUTS + tuple(name for name, _, _ in scratch)),
        out_shape=(
            jax.ShapeDtypeStruct((rows_a, hidden), WIDE),
            jax.ShapeDtypeStruct(mat_b.shape, WIDE),
            jax.ShapeDtypeStruct((2, rows_a), WIDE),
            jax.ShapeDtypeStruct((8, LANES), WIDE),
            jax.ShapeDtypeStruct((length, width), LOW),
            jax.ShapeDtypeStruct((length, width), WIDE),
        ),
        in_specs=[anywhere, anywhere, pl.BlockSpec(memory_space=pltpu.SMEM), anywhere, anywhere, anywhere],
        out_specs=[anywhere] * len(OUTPUTS),
        scratch_shapes=shapes,
        compiler_params=pltpu.CompilerParams(
            collective_id=0, has_side_effects=True, vmem_limit_bytes=KERNEL_VMEM
        ),
    )(tokens, cotangent, lengths, mat_a, mat_b, norms)


def update_kernel(*refs):
    inputs, outputs, held, made, sems = refs[:15], refs[15:33], refs[33:48], refs[48:63], refs[63]
    started = []

    def copy(source, target):
        one = pltpu.make_async_copy(source, target, sems.at[len(started)])
        one.start()
        started.append(one)
        return one

    half = inputs[4].shape[1] // 2
    parts = [(0, pl.ds(0, half)), (0, pl.ds(half, half)), (1, slice(None)), (2, slice(None))]
    rates = ((MATRIX_RATE, MATRIX_DECAY), (MATRIX_RATE, MATRIX_DECAY), (NORM_RATE, 0.0))
    norm_in = copy(inputs[0], held[0])
    coming = []
    for group, rows in parts:
        coming.append(
            [copy(inputs[at].at[:, rows], held[at].at[:, rows]) for at in range(3 + 4 * group, 7 + 4 * group)]
        )
    passing = [copy(inputs[at], held[at]) for at in (1, 2)]
    norm_in.wait()
    grad_norm = jnp.sqrt(held[0][0:1, 0:1])
    factor = CLIP_NORM / jnp.maximum(grad_norm, CLIP_NORM)
    outputs[0][...] = grad_norm
    leaving = []
    for (group, rows), waits in zip(parts, coming):
        for one in waits:
            one.wait()
        grad, weight, one, two = (held[at][:, rows] for at in range(3 + 4 * group, 7 + 4 * group))
        clip = grad * factor
        moment, square, master = adam_update(weight, one, two, clip, *rates[group])
        for kind, value in enumerate((clip, moment, square, master, master.astype(LOW))):
            buffer = made[5 * group + kind]
            buffer[:, rows] = value
            leaving.append(copy(buffer.at[:, rows], outputs[3 + 5 * group + kind].at[:, rows]))
        if passing:
            at = 3 - len(passing)
            passing.pop(0).wait()
            leaving.append(copy(held[at], outputs[at].at[0]))
    for one in leaving:
        one.wait()


def kernel_body(
    tokens, cotangent, lengths, mat_a, mat_b, norms, first_a, second_a, first_b, second_b, first_n, second_n
):
    norms, first_n, second_n = (jnp.swapaxes(value, 1, 2) for value in (norms, first_n, second_n))
    grad_a, grad_b, grad_n, square, output, input_grad = step_call(
        tokens, cotangent, lengths, mat_a, mat_b, norms
    )
    args = (square, output, input_grad, grad_a[None], mat_a, first_a, second_a, grad_b, mat_b, first_b, second_b)
    args += (grad_n[None], norms, first_n, second_n)
    anywhere, vmem = pl.BlockSpec(memory_space=pl.ANY), pl.BlockSpec(memory_space=pltpu.VMEM)
    shapes = [jax.ShapeDtypeStruct((1, 1), WIDE)]
    shapes += [jax.ShapeDtypeStruct((1,) + value.shape, value.dtype) for value in (output, input_grad)]
    for value in (mat_a, mat_b, norms):
        shapes += [jax.ShapeDtypeStruct(value.shape, kind) for kind in (WIDE, WIDE, WIDE, WIDE, LOW)]
    scratch = [pltpu.VMEM(value.shape, value.dtype) for value in (*args, *shapes[3:])]
    results = pl.pallas_call(
        update_kernel,
        out_shape=shapes,
        in_specs=[anywhere] * len(args),
        out_specs=[vmem] + [anywhere] * (len(shapes) - 1),
        scratch_shapes=scratch + [pltpu.SemaphoreType.DMA((48,))],
        compiler_params=pltpu.CompilerParams(vmem_limit_bytes=KERNEL_VMEM),
    )(*args)
    results = [results[0][0, 0], *results[1:]]
    results[-5:] = [jnp.swapaxes(value, 1, 2) for value in results[-5:]]
    return tuple(results)


def chosen_body(*args):
    rows_a = args[3].shape[1]
    groups = lax.axis_size("dp")
    by_kernel = rows_a % 32 == 0 and 2 * rows_a == LANES and groups * rows_a == args[0].shape[1]
    return (kernel_body if by_kernel else body)(*args)


def solution(mesh):
    placed = (
        P("dp", None),
        P("dp", None),
        P("dp", None),
        P("section", "dp", None),
        P(None, "dp", "section"),
        P("section", "dp", None),
        P("section", "dp", None),
        P("section", "dp", None),
        P(None, "dp", "section"),
        P(None, "dp", "section"),
        P("section", "dp", None),
        P("section", "dp", None),
    )
    return jax.shard_map(
        chosen_body,
        mesh=mesh,
        in_specs=placed,
        out_specs=(
            P(),
            P("section", "dp", None),
            P("section", "dp", None),
            P("section", "dp", None),
            P("section", "dp", None),
            P("section", "dp", None),
            P("section", "dp", None),
            P("section", "dp", None),
            P(None, "dp", "section"),
            P(None, "dp", "section"),
            P(None, "dp", "section"),
            P(None, "dp", "section"),
            P(None, "dp", "section"),
            P("section", "dp", None),
            P("section", "dp", None),
            P("section", "dp", None),
            P("section", "dp", None),
            P("section", "dp", None),
        ),
        check_vma=False,
    )
```
